32 devices in a mesh: dp: 2 (over y), expert: 16 (over z, x, core).
Axes of the slice: x: 2, y: 2, z: 4, core: 2. Of those that a mesh axis runs over, the one named last changes fastest.
Arguments:
- layer_input: bfloat16 [2, 2, 1024, 2048], P(None, 'dp', 'expert'), may hold values from -6 to 6
- out_cotangent: bfloat16 [2, 2, 1024, 2048], P(None, 'dp', 'expert'), may hold values from -6 to 6
- lengths: int32 [2, 2], P(None, 'dp'), may hold values from 256 to 1024, as said below
- routes: int32 [2, 2, 1024, 6], P(None, 'dp', 'expert'), may hold values from 0 to 15, all different within a row; in each aligned block of 64 rows (0 to 63, 64 to 127, ..., all dimensions but the last counted through in order) at most 30 rows name the same one
- attn_gain: bfloat16 [2048], P(('dp', 'expert')), may hold values from 0.5 to 1.5
- query_weight: bfloat16 [2048, 3072], P(('dp', 'expert')), may hold values from -0.125 to 0.125
- latent_weight: bfloat16 [2048, 576], P(('dp', 'expert')), may hold values from -0.125 to 0.125
- latent_gain: bfloat16 [512], P(('dp', 'expert')), may hold values from 0.5 to 1.5
- expand_weight: bfloat16 [512, 4096], P(('dp', 'expert')), may hold values from -0.25 to 0.25
- output_weight: bfloat16 [2048, 2048], P(('dp', 'expert')), may hold values from -2 to 2
- mixer_gain: bfloat16 [2048], P(('dp', 'expert')), may hold values from 0.5 to 1.5
- router_weight: bfloat16 [2048, 16], P(('dp', 'expert')), may hold values from -0.0625 to 0.0625
- gate_weight: bfloat16 [16, 2048, 1408], P('expert', 'dp'), may hold values from -0.125 to 0.125
- up_weight: bfloat16 [16, 2048, 1408], P('expert', 'dp'), may hold values from -0.125 to 0.125
- down_weight: bfloat16 [16, 1408, 2048], P('expert', 'dp'), may hold values from -0.15625 to 0.15625
- shared_gate: bfloat16 [2048, 2816], P('dp', 'expert'), may hold values from -0.125 to 0.125
- shared_up: bfloat16 [2048, 2816], P('dp', 'expert'), may hold values from -0.125 to 0.125
- shared_down: bfloat16 [2816, 2048], P('expert', 'dp'), may hold values from -0.109375 to 0.109375
Outputs:
- layer_output: float32 [2, 2, 1024, 2048], P(None, 'dp', 'expert')
- grad_input: float32 [2, 2, 1024, 2048], P(None, 'dp', 'expert')
- grad_attn_gain: float32 [2048], P(('dp', 'expert'))
- grad_query_weight: float32 [2048, 3072], P(('dp', 'expert'))
- grad_latent_weight: float32 [2048, 576], P(('dp', 'expert'))
- grad_latent_gain: float32 [512], P(('dp', 'expert'))
- grad_expand_weight: float32 [512, 4096], P(('dp', 'expert'))
- grad_output_weight: float32 [2048, 2048], P(('dp', 'expert'))
- grad_mixer_gain: float32 [2048], P(('dp', 'expert'))
- grad_router_weight: float32 [2048, 16], P(('dp', 'expert'))
- grad_gate_weight: float32 [16, 2048, 1408], P('expert', 'dp')
- grad_up_weight: float32 [16, 2048, 1408], P('expert', 'dp')
- grad_down_weight: float32 [16, 1408, 2048], P('expert', 'dp')
- grad_shared_gate: float32 [2048, 2816], P('dp', 'expert')
- grad_shared_up: float32 [2048, 2816], P('dp', 'expert')
- grad_shared_down: float32 [2816, 2048], P('expert', 'dp')
The draws below stay inside these ranges and needn't reach their ends.
Inputs may be any that keep to these rules, and one draw needn't show every extreme that they name: `lengths`: for every index of dp, one of the 2 micro-batches holds a sequence of full length 1024. `routes`: in each micro-batch the 64 positions of one device name any one expert at most 30 times, a bound that some block reaches.
All inputs are finite; a program needn't handle non-finite values.
Results may differ from the reference program's by a relative error of at most 0.019.
Values may be sent and summed in bfloat16 or wider, within the bound.
A program may use at most 320 MiB of HBM per device.

```python
import math
import jax
import jax.numpy as jnp
import numpy as np
from jax import lax

D = 2048
H = 16
QK_NOPE = 128
ROPE = 64
V_DIM = 128
KV_RANK = 512
FF = 1408
FS = 2816
TOP = 6
SEQ = 1024
MB = 2
SEQS = 2
EXPERTS = 16
TOK_DEV = 64
CAP = 30


def draw_lengths(key, part):
    key = jax.random.fold_in(key, 7)
    first_key, second_key = jax.random.split(key)
    drawn = jax.random.randint(first_key, (MB, SEQS), SEQ // 4, SEQ + 1)
    longest = jax.random.randint(second_key, (SEQS,), 0, MB)
    chosen = jnp.arange(MB)[:, None] == longest[None, :]
    return jnp.where(chosen, SEQ, drawn).astype(jnp.int32)


def block_scale(rng, shape, cuts, smallest, high):
    def one(dim, blocks):
        steps = jax.random.uniform(jax.random.fold_in(jax.random.fold_in(rng, 6), dim), (blocks,), jnp.float32, smallest / len(cuts), high / len(cuts))
        return jnp.repeat(jnp.exp(steps), shape[dim] // blocks).reshape((-1,) + (1,) * (len(shape) - dim - 1))

    level = one(*cuts[0])
    for cut in cuts[1:]:
        level = level * one(*cut)
    return level


def assign_block(key, own, number, rows, count, top, limit, slope):
    order = jax.random.permutation(key, count)
    heavy_load, ordinary = load_shares(count, rows * top, limit, slope, True), load_shares(count, rows * top, limit, slope, False)
    places = jnp.arange(count)

    def named(sizes, turn):
        used = int((sizes > 0).sum())
        fixed = max(1, used // 4)
        shifted = fixed + (places - fixed + turn * (used - fixed)) % max(1, count - fixed)
        return jnp.zeros((count,), jnp.int32).at[order[jnp.where(places < fixed, places, shifted)]].set(jnp.asarray(sizes, jnp.int32))

    sizes = jnp.where(number % 4 == 0, named(heavy_load, number // 4), named(ordinary, number - number // 4 - 1))
    mixed = jax.random.permutation(jax.random.fold_in(own, 3), count)
    donor, sink = mixed[0:count // 2 * 2:2], mixed[1:count // 2 * 2:2]
    slack = jnp.minimum(sizes[donor] - 1, limit - sizes[sink]) // 2
    slack = jnp.where((donor == order[0]) | (sink == order[0]) | (sizes[sink] == 0), 0, jnp.maximum(slack, 0))
    shifted = jax.random.randint(jax.random.fold_in(own, 4), (count // 2,), 0, 1 << 20) % (slack + 1)
    sizes = sizes.at[donor].add(-shifted).at[sink].add(shifted)
    items = jnp.searchsorted(jnp.cumsum(sizes), jnp.arange(rows * top), side="right").astype(jnp.int32)
    table = items.reshape(top, rows).T
    table = table[jax.random.permutation(jax.random.fold_in(own, 1), rows)]
    turn = jax.random.randint(jax.random.fold_in(own, 2), (rows, 1), 0, top)
    return jnp.take_along_axis(table, (jnp.arange(top)[None, :] + turn) % top, axis=1)


def load_shares(count, total, bound, slope, full):
    weights = [(1 << 20) // math.isqrt(rank ** slope) + 1 for rank in range(1, count + 1)]
    largest = bound if full else min(bound, max(-(-total // count), total * weights[0] // sum(weights)))
    least = 1 if total - largest >= count - 1 else 0
    holding, rest = [largest] + [least] * (count - 1), total - largest - least * (count - 1)
    while rest > 0:
        free = [i for i in range(1, count) if holding[i] < largest] or [i for i in range(1, count) if holding[i] < bound]
        whole, remaining = sum([weights[i] for i in free]), rest
        for i in free:
            extra = min(bound - holding[i], max(1, remaining * weights[i] // whole), rest)
            holding[i] = holding[i] + extra
            rest = rest - extra
    return np.array(holding)


def centred(stream_key, extent, deviation, reach, shards=(), kind=jnp.bfloat16):
    array = jax.random.normal(stream_key, extent, jnp.float32) * deviation
    if len(shards) > 0:
        array = block_scale(stream_key, extent, shards, -0.22, 0.18) * array
    return jnp.clip(array, min=-reach, max=reach).astype(kind)


def setup_inputs(seed: int = 0) -> dict:
    keys = jax.random.split(jax.random.key(seed), 19)
    layer_input = centred(keys[0], (MB, SEQS, SEQ, D), 1.0, 6.0, ((1, 2), (2, 16)))
    out_cotangent = centred(keys[1], (MB, SEQS, SEQ, D), 1.0, 6.0, ((1, 2), (2, 16)))
    lengths = draw_lengths(jax.random.fold_in(keys[18], 71), 0)
    routes_keys = jax.random.split(jax.random.fold_in(keys[3], 1), MB * SEQS * SEQ // TOK_DEV)
    routes_turns = jax.random.permutation(jax.random.fold_in(keys[3], 3), MB * SEQS * SEQ // TOK_DEV)
    routes = jax.vmap(lambda own, number: assign_block(jax.random.fold_in(keys[3], 2), own, number, TOK_DEV, EXPERTS, TOP, CAP, 1))(routes_keys, routes_turns).reshape((MB, SEQS, SEQ, TOP))
    attn_gain = jnp.clip(1.0 + 0.1 * jax.random.normal(keys[4], (D,), jnp.float32), 0.5, 1.5).astype(jnp.bfloat16)
    query_weight = centred(keys[5], (D, H * (QK_NOPE + ROPE)), D ** -0.5, 0.125, ((0, 32),))
    latent_weight = centred(keys[6], (D, KV_RANK + ROPE), D ** -0.5, 0.125, ((0, 32),))
    latent_gain = jnp.clip(1.0 + 0.1 * jax.random.normal(keys[7], (KV_RANK,), jnp.float32), 0.5, 1.5).astype(jnp.bfloat16)
    expand_weight = centred(keys[8], (KV_RANK, H * (QK_NOPE + V_DIM)), KV_RANK ** -0.5, 0.25, ((0, 32),))
    output_weight = centred(keys[9], (H * V_DIM, D), (max(1, H * V_DIM // 256)) ** -0.5, 2.0, ((0, 32),))
    mixer_gain = jnp.clip(1.0 + 0.1 * jax.random.normal(keys[10], (D,), jnp.float32), 0.5, 1.5).astype(jnp.bfloat16)
    router_weight = centred(keys[11], (D, EXPERTS), (4 * D) ** -0.5, 0.0625, ((0, 32),))
    gate_weight = centred(keys[12], (EXPERTS, D, FF), D ** -0.5, 0.125, ((0, 16), (1, 2)))
    up_weight = centred(keys[13], (EXPERTS, D, FF), D ** -0.5, 0.125, ((0, 16), (1, 2)))
    down_weight = centred(keys[14], (EXPERTS, FF, D), FF ** -0.5, 0.15625, ((0, 16), (1, 2)))
    shared_gate = centred(keys[15], (D, FS), D ** -0.5, 0.125, ((0, 2), (1, 16)))
    shared_up = centred(keys[16], (D, FS), D ** -0.5, 0.125, ((0, 2), (1, 16)))
    shared_down = centred(keys[17], (FS, D), FS ** -0.5, 0.109375, ((0, 16), (1, 2)))
    return {"layer_input": layer_input, "out_cotangent": out_cotangent, "lengths": lengths, "routes": routes, "attn_gain": attn_gain, "query_weight": query_weight, "latent_weight": latent_weight, "latent_gain": latent_gain, "expand_weight": expand_weight, "output_weight": output_weight, "mixer_gain": mixer_gain, "router_weight": router_weight, "gate_weight": gate_weight, "up_weight": up_weight, "down_weight": down_weight, "shared_gate": shared_gate, "shared_up": shared_up, "shared_down": shared_down}


EPSILON = 1e-06
ROTARY_BASE = 10000.0

@jax.custom_vjp
def low(v):
    return lax.optimization_barrier(v.astype(jnp.bfloat16)).astype(jnp.float32)

@jax.custom_vjp
def low_back(v):
    return v

def low_keep(v):
    return (low(v), None)

def low_pass(kept, grad):
    return (grad,)

def back_keep(v):
    return (v, None)

def back_low(kept, grad):
    return (low(grad),)
low.defvjp(low_keep, low_pass)
low_back.defvjp(back_keep, back_low)

def product_high(left_side, right_side):
    return jnp.matmul(left_side, right_side, precision=lax.Precision.HIGHEST)

def root_norm(values, gains):
    return values * lax.rsqrt(lax.optimization_barrier(jnp.mean(values * values, axis=-1, keepdims=True)) + EPSILON) * gains

def rotary_tables(positions, rotary_width):
    half_width = rotary_width // 2
    frequency = ROTARY_BASE ** (-jnp.arange(half_width, dtype=jnp.float32) * 2.0 / rotary_width)
    angles = positions[:, None] * frequency[None, :]
    return (jnp.cos(angles), jnp.sin(angles))

def rotate(values, cosine, sine_table):
    half_width = values.shape[-1] // 2
    first_half = values[..., :half_width]
    second_half = values[..., half_width:]
    return jnp.concatenate([first_half * cosine - second_half * sine_table, second_half * cosine + first_half * sine_table], axis=-1)

def slot_index(route_rows, experts_total, capacity):
    flat_routes = route_rows.reshape(-1).astype(jnp.int32)
    onehot = (flat_routes[:, None] == jnp.arange(experts_total, dtype=jnp.int32)[None, :]).astype(jnp.int32)
    earlier = jnp.cumsum(onehot, axis=0) - onehot
    position = lax.optimization_barrier(jnp.sum(earlier * onehot, axis=1))
    return (flat_routes * capacity + position).reshape(route_rows.shape).astype(jnp.int32)

def attend(normed_seq, seq_length, query_mat, latent_mat, gain_latent, expand_mat, output_mat):
    positions = jnp.arange(SEQ, dtype=jnp.int32)
    cosine, sine_table = rotary_tables(positions.astype(jnp.float32), ROPE)
    scale_factor = float(QK_NOPE + ROPE) ** (-0.5)
    query_raw = low_back(product_high(normed_seq, query_mat)).reshape(SEQ, H, QK_NOPE + ROPE)
    query_nope = low(query_raw[..., :QK_NOPE])
    query_rope = low(rotate(query_raw[..., QK_NOPE:], cosine[:, None, :], sine_table[:, None, :]))
    latent_raw = low_back(product_high(normed_seq, latent_mat))
    latent = low(root_norm(latent_raw[:, :KV_RANK], gain_latent))
    key_rope = low(rotate(latent_raw[:, KV_RANK:], cosine, sine_table))
    expanded = low(product_high(latent, expand_mat)).reshape(SEQ, H, QK_NOPE + V_DIM)
    key_nope = expanded[..., :QK_NOPE]
    key_values = expanded[..., QK_NOPE:]
    scores = jnp.einsum('thd,shd->hts', query_nope, key_nope, precision=lax.Precision.HIGHEST)
    scores = scores + jnp.einsum('thd,sd->hts', query_rope, key_rope, precision=lax.Precision.HIGHEST)
    scores = low_back(scores * scale_factor)
    allowed = (positions[None, :] <= positions[:, None]) & (positions[None, :] < seq_length)
    scores = jnp.where(allowed[None, :, :], scores, -1e+30)
    weights = low(jax.nn.softmax(scores, axis=-1))
    attended = low(low_back(jnp.einsum('hts,shd->thd', weights, key_values, precision=lax.Precision.HIGHEST)))
    return low_back(product_high(attended.reshape(SEQ, H * V_DIM), output_mat))

def mixture(hidden_mix, valid, route_rows, slot_rows, blocks, router_mat, gate_mats, up_mats, down_mats, share_gate, share_up, share_down):
    count = hidden_mix.shape[0]
    logits = low_back(product_high(hidden_mix, router_mat))
    picker = (route_rows[..., None] == jnp.arange(EXPERTS, dtype=jnp.int32)).astype(jnp.float32)
    chosen = lax.optimization_barrier(jnp.sum(picker * logits[:, None, :], axis=-1))
    gates = jax.nn.softmax(chosen, axis=-1) * valid[:, None]
    shared_gate_in = low_back(product_high(hidden_mix, share_gate))
    shared_up_in = low_back(product_high(hidden_mix, share_up))
    shared_out = low_back(product_high(low(jax.nn.silu(shared_gate_in) * shared_up_in), share_down))
    copies = low_back(jnp.broadcast_to((hidden_mix * valid[:, None])[:, None, :], (count, TOP, D)))
    buffer = jnp.zeros((blocks * EXPERTS * CAP, D), jnp.float32).at[slot_rows.reshape(-1)].set(copies.reshape(count * TOP, D))
    buffer = buffer.reshape(blocks, EXPERTS, CAP, D).transpose(1, 0, 2, 3).reshape(EXPERTS, blocks * CAP, D)

    def one_expert(item):
        expert_rows, gate_mat, up_mat, down_mat = item
        gate_in = low_back(product_high(expert_rows, gate_mat))
        up_in = low_back(product_high(expert_rows, up_mat))
        return low_back(low(product_high(low(jax.nn.silu(gate_in) * up_in), down_mat)))
    results = lax.map(jax.checkpoint(one_expert), (buffer, gate_mats, up_mats, down_mats))
    results = results.reshape(EXPERTS, blocks, CAP, D).transpose(1, 0, 2, 3).reshape(blocks * EXPERTS * CAP, D)
    picked = results[slot_rows]
    return shared_out + lax.optimization_barrier(jnp.sum(gates[..., None] * picked, axis=1))

def reference(layer_input, out_cotangent, lengths, routes, attn_gain, query_weight, latent_weight, latent_gain, expand_weight, output_weight, mixer_gain, router_weight, gate_weight, up_weight, down_weight, shared_gate, shared_up, shared_down):
    sequences = MB * SEQS
    count = sequences * SEQ
    blocks = count // TOK_DEV
    seq_lengths = lengths.reshape(sequences).astype(jnp.int32)
    positions = jnp.arange(SEQ, dtype=jnp.int32)
    valid = (positions[None, :] < seq_lengths[:, None]).astype(jnp.float32).reshape(count)
    route_rows = routes.reshape(count, TOP).astype(jnp.int32)
    local_slots = jax.vmap(lambda part_routes: slot_index(part_routes, EXPERTS, CAP))(route_rows.reshape(blocks, TOK_DEV, TOP))
    offsets = jnp.arange(blocks, dtype=jnp.int32)[:, None, None] * (EXPERTS * CAP)
    slot_rows = (local_slots + offsets).reshape(count, TOP).astype(jnp.int32)
    params = tuple((item.astype(jnp.float32) for item in (layer_input, attn_gain, query_weight, latent_weight, latent_gain, expand_weight, output_weight, mixer_gain, router_weight, gate_weight, up_weight, down_weight, shared_gate, shared_up, shared_down)))

    def forward(inputs, gain_attn, query_mat, latent_mat, gain_latent, expand_mat, output_mat, gain_mix, router_mat, gate_all, up_all, down_all, share_gate, share_up, share_down):
        seq_inputs = inputs.reshape(sequences, SEQ, D)
        normed = low(root_norm(seq_inputs, gain_attn))

        def one_seq(item):
            return attend(item[0], item[1], query_mat, latent_mat, gain_latent, expand_mat, output_mat)
        attended = lax.map(jax.checkpoint(one_seq), (normed, seq_lengths))
        middle = (seq_inputs + attended).reshape(count, D)
        hidden_mix = low(root_norm(middle, gain_mix))
        branch = mixture(hidden_mix, valid, route_rows, slot_rows, blocks, router_mat, gate_all, up_all, down_all, share_gate, share_up, share_down)
        return valid[:, None] * (middle + branch)
    result, pullback = jax.vjp(forward, *params)
    grads = pullback(out_cotangent.astype(jnp.float32).reshape(count, D))
    shape_full = (MB, SEQS, SEQ, D)
    return (result.reshape(shape_full), grads[0].reshape(shape_full), grads[1], grads[2], grads[3], grads[4], grads[5], grads[6], grads[7], grads[8], grads[9], grads[10], grads[11], grads[12], grads[13], grads[14])
```

```python
import functools
import jax
import jax.numpy as jnp
from jax import lax
from jax.experimental import pallas as pl
from jax.experimental.pallas import tpu as pltpu
from jax.sharding import PartitionSpec as P

MESH = pl.DeviceIdType.MESH
NZ = 4


def place():
    me = lax.axis_index("expert")
    z = me // 4
    x = (me // 2) % 2
    c = me % 2
    return me, z, x, c, me + 1 - 2 * c, me + 2 - 4 * x


def enter(me, z, core, side):
    barrier = pltpu.get_barrier_semaphore()
    for other in (core, side):
        pl.semaphore_signal(barrier, inc=1, device_id={"expert": other}, device_id_type=MESH)

    @pl.when(z < NZ - 1)
    def _():
        pl.semaphore_signal(barrier, inc=1, device_id={"expert": me + 4}, device_id_type=MESH)

    @pl.when(z > 0)
    def _():
        pl.semaphore_signal(barrier, inc=1, device_id={"expert": me - 4}, device_id_type=MESH)

    pl.semaphore_wait(barrier, 2 + (z < NZ - 1).astype(jnp.int32) + (z > 0).astype(jnp.int32))


def gather_kernel(chunks, x_ref, o_ref, own_sem, up_s, up_r, dn_s, dn_r, xs, xr, cs, cr):
    me, z, x, c, core, side = place()
    rows = x_ref.shape[0] // chunks

    def part(ref, k):
        return ref.at[pl.ds(k * rows, rows)]

    def copy(block, k, src, send, recv, to):
        return pltpu.make_async_remote_copy(
            src_ref=part(x_ref if src is None else o_ref.at[src], k),
            dst_ref=part(o_ref.at[block], k),
            send_sem=send, recv_sem=recv,
            device_id={"expert": to}, device_id_type=MESH,
        )

    def up(k, s, src=None):
        b = me - 4 * s
        return copy(b, k, src, up_s.at[s, k], up_r.at[s, k], me + 4)

    def down(k, s, src=None):
        b = me + 4 * s
        return copy(b, k, src, dn_s.at[s, k], dn_r.at[s, k], me - 4)

    def across(k, slot, block, src=None):
        return copy(block, k, src, xs.at[slot, k], xr.at[slot, k], side)

    def over(k, slot, block, src=None):
        return copy(block, k, src, cs.at[slot, k], cr.at[slot, k], core)

    enter(me, z, core, side)
    own = pltpu.make_async_copy(x_ref, o_ref.at[me], own_sem)
    own.start()
    for k in range(chunks):
        across(k, 0, me).start()

        @pl.when(z < NZ - 1)
        def _():
            up(k, 0).start()

        @pl.when(z > 0)
        def _():
            down(k, 0).start()

        over(k, 0, me).start()

    def line(k, s):
        @pl.when(z >= s)
        def _():
            b = me - 4 * s
            up_in(k, s).wait_recv()
            across(k, s, b, b).start()

            @pl.when(z < NZ - 1)
            def _():
                up(k, s, b).start()

            over(k, s, b, b).start()

        @pl.when(z + s <= NZ - 1)
        def _():
            b = me + 4 * s
            dn_in(k, s).wait_recv()
            across(k, 3 + s, b, b).start()

            @pl.when(z > 0)
            def _():
                down(k, s, b).start()

            over(k, 3 + s, b, b).start()

    def up_in(k, s):
        b = me - 4 * s
        return copy(b, k, b, up_s.at[s - 1, k], up_r.at[s - 1, k], side)

    def dn_in(k, s):
        b = me + 4 * s
        return copy(b, k, b, dn_s.at[s - 1, k], dn_r.at[s - 1, k], side)

    def side_block(slot):
        return side - 4 * slot if slot <= 3 else side + 4 * (slot - 3)

    def core_block(slot):
        if slot < 7:
            return core - 4 * slot if slot <= 3 else core + 4 * (slot - 3)
        other = core + 2 - 4 * x
        slot = slot - 7
        return other - 4 * slot if slot <= 3 else other + 4 * (slot - 3)

    def has(slot):
        slot = slot % 7
        if slot == 0:
            return z >= 0
        return z >= slot if slot <= 3 else z + (slot - 3) <= NZ - 1

    def from_side(k, slot):
        @pl.when(has(slot))
        def _():
            b = side_block(slot)
            across(k, slot, b, b).wait_recv()
            over(k, 7 + slot, b, b).start()

    for s in range(1, NZ):
        for k in range(chunks):
            line(k, s)
        for k in range(chunks):
            for slot in ((0,) if s == 1 else (s - 1, s + 2)):
                from_side(k, slot)
    for k in range(chunks):
        for slot in (NZ - 1, NZ + 2):
            from_side(k, slot)
    own.wait()
    for k in range(chunks):
        for slot in range(14):
            @pl.when(has(slot))
            def _():
                b = core_block(slot)
                over(k, slot, b, b).wait_recv()
                over(k, slot, b, b).wait_send()
        for slot in range(7):
            @pl.when(has(slot))
            def _():
                across(k, slot, me).wait_send()
        for s in range(NZ - 1):
            @pl.when((z >= s) & (z < NZ - 1))
            def _():
                up(k, s).wait_send()

            @pl.when((z + s <= NZ - 1) & (z > 0))
            def _():
                down(k, s).wait_send()


def gather16(v, cid, chunks=2):
    rows, width = v.shape
    dma = pltpu.SemaphoreType.DMA
    return pl.pallas_call(
        functools.partial(gather_kernel, chunks),
        out_shape=jax.ShapeDtypeStruct((16, rows, width), v.dtype),
        in_specs=[pl.BlockSpec(memory_space=pl.ANY)],
        out_specs=pl.BlockSpec(memory_space=pl.ANY),
        scratch_shapes=[
            dma, dma((4, chunks)), dma((4, chunks)), dma((4, chunks)), dma((4, chunks)),
            dma((7, chunks)), dma((7, chunks)), dma((14, chunks)), dma((14, chunks)),
        ],
        compiler_params=pltpu.CompilerParams(collective_id=cid, has_side_effects=True),
        cost_estimate=pl.CostEstimate(flops=0, bytes_accessed=150_000_000, transcendentals=0),
        name="gather16",
    )(v)


def order(z, i):
    a, b = (3, 2, 1, 0)[i], (3, 2, 0, 1)[i]
    return jnp.where(z == 0, a, jnp.where(z == 1, b, jnp.where(z == 2, 3 - b, 3 - a)))


def scatter_kernel(chunks, p_ref, o_ref, cbuf, own, xbuf, ubuf, dbuf,
                   ld, cs, cr, xs, xr, us, ur, ds_, dr):
    me, z, x, c, core, side = place()
    rows = o_ref.shape[0] // chunks
    f32 = jnp.float32

    def rng(k):
        return pl.ds(k * rows, rows)

    def over(i, j, k):
        b = 4 * order(z, i) + 2 * jnp.where(j == 0, 1 - x, x)
        return pltpu.make_async_remote_copy(
            src_ref=p_ref.at[b + 1 - c, rng(k)], dst_ref=cbuf.at[2 * i + j, rng(k)],
            send_sem=cs.at[2 * i + j, k], recv_sem=cr.at[2 * i + j, k],
            device_id={"expert": core}, device_id_type=MESH)

    def load(i, j):
        b = 4 * order(z, i) + 2 * jnp.where(j == 0, 1 - x, x)
        return pltpu.make_async_copy(p_ref.at[b + c], own.at[2 * i + j], ld.at[2 * i + j])

    def across(i, k):
        return pltpu.make_async_remote_copy(
            src_ref=own.at[2 * i, rng(k)], dst_ref=xbuf.at[i, rng(k)],
            send_sem=xs.at[i, k], recv_sem=xr.at[i, k],
            device_id={"expert": side}, device_id_type=MESH)

    def up(t, i, k):
        return pltpu.make_async_remote_copy(
            src_ref=own.at[2 * i + 1, rng(k)], dst_ref=ubuf.at[t, rng(k)],
            send_sem=us.at[t, k], recv_sem=ur.at[t, k],
            device_id={"expert": me + 4}, device_id_type=MESH)

    def down(t, i, k):
        return pltpu.make_async_remote_copy(
            src_ref=own.at[2 * i + 1, rng(k)], dst_ref=dbuf.at[t, rng(k)],
            send_sem=ds_.at[t, k], recv_sem=dr.at[t, k],
            device_id={"expert": me - 4}, device_id_type=MESH)

    enter(me, z, core, side)
    for i in range(NZ):
        for j in range(2):
            load(i, j).start()
            for k in range(chunks):
                over(i, j, k).start()

    def first(i):
        load(i, 0).wait()
        for k in range(chunks):
            over(i, 0, k).wait_recv()
            s = rng(k)
            own[2 * i, s] = (own[2 * i, s].astype(f32) + cbuf[2 * i, s].astype(f32)).astype(own.dtype)
            across(i, k).start()

    def second(i):
        t = order(z, i)
        load(i, 1).wait()
        for k in range(chunks):
            s = rng(k)
            over(i, 1, k).wait_recv()
            across(i, k).wait_recv()

            def base():
                return (own[2 * i + 1, s].astype(f32) + cbuf[2 * i + 1, s].astype(f32)
                        + xbuf[i, s].astype(f32))

            if i < NZ - 1:
                @pl.when(t > z)
                def _():
                    @pl.when(z > 0)
                    def _():
                        up(t, i, k).wait_recv()
                        own[2 * i + 1, s] = (base() + ubuf[t, s].astype(f32)).astype(own.dtype)

                    @pl.when(z == 0)
                    def _():
                        own[2 * i + 1, s] = base().astype(own.dtype)

                    up(t, i, k).start()

                @pl.when(t < z)
                def _():
                    @pl.when(z < NZ - 1)
                    def _():
                        down(t, i, k).wait_recv()
                        own[2 * i + 1, s] = (base() + dbuf[t, s].astype(f32)).astype(own.dtype)

                    @pl.when(z == NZ - 1)
                    def _():
                        own[2 * i + 1, s] = base().astype(own.dtype)

                    down(t, i, k).start()
            else:
                @pl.when(z > 0)
                def _():
                    up(t, i, k).wait_recv()

                @pl.when(z < NZ - 1)
                def _():
                    down(t, i, k).wait_recv()

                @pl.when((z > 0) & (z < NZ - 1))
                def _():
                    o_ref[s] = (base() + ubuf[t, s].astype(f32) + dbuf[t, s].astype(f32)).astype(o_ref.dtype)

                @pl.when(z == 0)
                def _():
                    o_ref[s] = (base() + dbuf[t, s].astype(f32)).astype(o_ref.dtype)

                @pl.when(z == NZ - 1)
                def _():
                    o_ref[s] = (base() + ubuf[t, s].astype(f32)).astype(o_ref.dtype)

    first(0)
    for i in range(NZ):
        if i + 1 < NZ:
            first(i + 1)
        second(i)

    for k in range(chunks):
        for i in range(NZ):
            across(i, k).wait_send()
            for j in range(2):
                over(i, j, k).wait_send()
            if i < NZ - 1:
                t = order(z, i)

                @pl.when(t > z)
                def _():
                    up(t, i, k).wait_send()

                @pl.when(t < z)
                def _():
                    down(t, i, k).wait_send()


def scatter16(p, cid, chunks=2, out_dtype=jnp.float32):
    _, rows, width = p.shape
    dma = pltpu.SemaphoreType.DMA
    bf = p.dtype
    return pl.pallas_call(
        functools.partial(scatter_kernel, chunks),
        out_shape=jax.ShapeDtypeStruct((rows, width), out_dtype),
        in_specs=[pl.BlockSpec(memory_space=pl.ANY)],
        out_specs=pl.BlockSpec(memory_space=pltpu.VMEM),
        scratch_shapes=[
            pltpu.VMEM((8, rows, width), bf), pltpu.VMEM((8, rows, width), bf),
            pltpu.VMEM((4, rows, width), bf), pltpu.VMEM((4, rows, width), bf), pltpu.VMEM((4, rows, width), bf),
            dma((8,)), dma((8, chunks)), dma((8, chunks)), dma((4, chunks)), dma((4, chunks)),
            dma((4, chunks)), dma((4, chunks)), dma((4, chunks)), dma((4, chunks)),
        ],
        compiler_params=pltpu.CompilerParams(collective_id=cid, has_side_effects=True,
                                             vmem_limit_bytes=32 * 1024 * 1024),
        cost_estimate=pl.CostEstimate(flops=0, bytes_accessed=150_000_000, transcendentals=0),
        name="scatter16",
    )(p)


H = 16
QK_NOPE = 128
ROPE = 64
V_DIM = 128
KV_RANK = 512
GROUPS = 16
EPSILON = 1e-06
ROTARY_BASE = 10000.0
BF = jnp.bfloat16
F32 = jnp.float32


def product(left_side, right_side):
    return jnp.dot(left_side, right_side, preferred_element_type=F32)


def product_lead(left_side, right_side):
    return lax.dot_general(
        left_side, right_side, (((0,), (0,)), ((), ())), preferred_element_type=F32
    )


def product_trail(left_side, right_side):
    return lax.dot_general(
        left_side, right_side, (((1,), (1,)), ((), ())), preferred_element_type=F32
    )


def rotary_tables(positions):
    half_width = ROPE // 2
    frequency = ROTARY_BASE ** (-jnp.arange(half_width, dtype=F32) * 2.0 / ROPE)
    angles = positions[:, None] * frequency[None, :]
    return (jnp.cos(angles), jnp.sin(angles))


def rotate(values, cosine, sine_table):
    first_half, second_half = jnp.split(values, 2, axis=-1)
    return jnp.concatenate(
        [
            first_half * cosine - second_half * sine_table,
            second_half * cosine + first_half * sine_table,
        ],
        axis=-1,
    )


def norm_forward(values, gains):
    factor = lax.rsqrt(jnp.mean(values * values, axis=-1, keepdims=True) + EPSILON)
    normed = values * factor
    return (normed * gains, normed, factor)


def norm_backward(gradient, normed, factor, gains):
    gain_grad = jnp.sum(gradient * normed, axis=0)
    scaled = gradient * gains
    return (
        factor * (scaled - normed * jnp.mean(scaled * normed, axis=-1, keepdims=True)),
        gain_grad,
    )


def silu_pair(gate_in):
    sigmoid = jax.nn.sigmoid(gate_in)
    return (gate_in * sigmoid, sigmoid * (1.0 + gate_in * (1.0 - sigmoid)))


def selected_experts(routes):
    chosen = routes[:, :, None] == jnp.arange(GROUPS, dtype=routes.dtype)
    return jnp.any(chosen, axis=1)


def masked_softmax(logits, mask):
    held = jnp.where(mask, logits, -1e30)
    peak = jnp.max(held, axis=-1, keepdims=True)
    raised = jnp.where(mask, jnp.exp(held - peak), 0.0)
    return raised / jnp.sum(raised, axis=-1, keepdims=True)


def head_blocks(dp):
    rounds = []
    for i in range(dp):
        sources, blocks = [], []
        for head in range(H):
            j = (i + head * dp // GROUPS) % dp
            blocks.append((dp * head + j) // GROUPS)
            sources.append((dp * head + j) % GROUPS)
        rounds.append((sources, blocks))
    return rounds


def per_device(
    layer_input,
    out_cotangent,
    lengths,
    routes,
    attn_gain,
    query_weight,
    latent_weight,
    latent_gain,
    expand_weight,
    output_weight,
    mixer_gain,
    router_weight,
    gate_weight,
    up_weight,
    down_weight,
    shared_gate,
    shared_up,
    shared_down,
):
    dp = lax.axis_size("dp")
    me = lax.axis_index("expert")
    plane = lax.axis_index("dp")
    batches, _, here, width = layer_input.shape
    own = batches * here
    total = own * GROUPS
    seq_total = here * GROUPS
    rows_w = query_weight.shape[0]
    rows_l = expand_weight.shape[0]
    scale_factor = float(QK_NOPE + ROPE) ** (-0.5)

    x_own = layer_input.reshape(own, width)
    x_all = gather16(x_own, 1).reshape(total, width)

    latent_column = jnp.zeros((rows_w,), BF).at[:rows_l].set(latent_gain)
    small = jnp.concatenate(
        [
            latent_weight,
            router_weight,
            attn_gain[:, None],
            mixer_gain[:, None],
            latent_column[:, None],
            jnp.zeros((rows_w, 640 - 595), BF),
        ],
        axis=1,
    )
    small = lax.all_gather(small, ("dp", "expert"), axis=0, tiled=True)
    latent_full = small[:, :576]
    router_full = small[:, 576:592]
    gain_attn = small[:, 592].astype(F32)
    gain_mixer = small[:, 593].astype(F32)
    gain_latent = small[:, 594].reshape(dp * GROUPS, rows_w)[:, :rows_l].reshape(-1).astype(F32)

    query_parts = query_weight.reshape(rows_w, H, QK_NOPE + ROPE).transpose(1, 0, 2)
    expand_parts = expand_weight.reshape(rows_l, H, QK_NOPE + V_DIM).transpose(1, 0, 2)
    query_head = lax.all_to_all(query_parts, "expert", 0, 0, tiled=True)
    expand_head = lax.all_to_all(expand_parts, "expert", 0, 0, tiled=True)
    query_head = lax.all_gather(query_head, "dp", axis=0, tiled=True).reshape(width, QK_NOPE + ROPE)
    expand_head = lax.all_gather(expand_head, "dp", axis=0, tiled=True).reshape(KV_RANK, QK_NOPE + V_DIM)
    output_rows = lax.all_gather(output_weight, "dp", axis=0)
    received = []
    shift = (me * dp) // GROUPS
    for sources, blocks in head_blocks(dp):
        table = [0] * GROUPS
        for source, block in zip(sources, blocks):
            table[source] = block
        block = lax.dynamic_index_in_dim(output_rows, jnp.array(table, jnp.int32)[me], 0, False)
        received.append(lax.ppermute(block, "expert", [(s, h) for h, s in enumerate(sources)]))
    received = jnp.stack(received)
    output_head = jnp.stack(
        [lax.dynamic_index_in_dim(received, (j - shift) % dp, 0, False) for j in range(dp)]
    ).reshape(V_DIM, width)

    gate_full = lax.all_gather(gate_weight[0], "dp", axis=0, tiled=True)
    up_full = lax.all_gather(up_weight[0], "dp", axis=0, tiled=True)
    down_full = lax.all_gather(down_weight[0], "dp", axis=0, tiled=True)
    share_gate = lax.all_gather(shared_gate, "dp", axis=0, tiled=True)
    share_up = lax.all_gather(shared_up, "dp", axis=0, tiled=True)
    share_down = lax.all_gather(shared_down, "dp", axis=1, tiled=True)

    seq_lengths = lengths.reshape(batches)
    own_positions = me * here + jnp.arange(here, dtype=jnp.int32)
    valid_own = (own_positions[None, :] < seq_lengths[:, None]).reshape(own).astype(F32)
    all_positions = jnp.arange(seq_total, dtype=jnp.int32).reshape(GROUPS, 1, here)
    valid_all = jnp.broadcast_to(
        all_positions < seq_lengths[None, :, None], (GROUPS, batches, here)
    ).reshape(total)
    key_positions = jnp.arange(seq_total, dtype=jnp.int32)
    cosine, sine_table = rotary_tables(key_positions.astype(F32))
    cosine_own = lax.dynamic_slice_in_dim(cosine, me * here, here)
    sine_own = lax.dynamic_slice_in_dim(sine_table, me * here, here)

    def by_sequence(v):
        return v.reshape(GROUPS, batches, here, v.shape[-1]).swapaxes(0, 1).reshape(batches, seq_total, -1)

    def by_device(v):
        return v.reshape(batches, GROUPS, here, v.shape[-1]).swapaxes(0, 1).reshape(total, -1)

    grad_own = out_cotangent.reshape(own, width) * valid_own[:, None].astype(BF)
    routes_own = routes.reshape(own, -1)
    packed = jnp.concatenate(
        [grad_own, routes_own.astype(BF), jnp.zeros((own, 128 - routes_own.shape[1]), BF)], axis=1
    )
    packed = lax.all_gather(packed, "expert", axis=0, tiled=True)
    grad_all = packed[:, :width]
    routes_all = packed[:, width : width + routes_own.shape[1]].astype(jnp.int32)

    hidden_all = norm_forward(x_all.astype(F32), gain_attn)[0].astype(BF)
    raw = product(hidden_all, jnp.concatenate([query_head, latent_full], axis=1))
    raw = by_sequence(raw)
    query_nope = raw[..., :QK_NOPE].astype(BF)
    query_rope = rotate(raw[..., QK_NOPE : QK_NOPE + ROPE], cosine, sine_table).astype(BF)
    query = jnp.concatenate([query_nope, query_rope], axis=-1)
    latent_raw = raw[..., QK_NOPE + ROPE :]
    latent = norm_forward(latent_raw[..., :KV_RANK], gain_latent)[0].astype(BF)
    key_rope = rotate(latent_raw[..., KV_RANK:], cosine, sine_table).astype(BF)
    expanded = product(latent, expand_head).astype(BF)
    key = jnp.concatenate([expanded[..., :QK_NOPE], key_rope], axis=-1)
    values = expanded[..., QK_NOPE:]
    allowed = (key_positions[None, None, :] <= key_positions[None, :, None]) & (
        key_positions[None, None, :] < seq_lengths[:, None, None]
    )

    def score(query, key):
        raw_scores = jnp.einsum("btd,bsd->bts", query, key, preferred_element_type=F32)
        return jnp.where(allowed, raw_scores * scale_factor, -1e30)

    scores = score(query, key)
    peak = jnp.max(scores, axis=-1, keepdims=True)
    log_total = peak + jnp.log(jnp.sum(jnp.exp(scores - peak), axis=-1, keepdims=True))
    probs_low = jnp.exp(scores - log_total).astype(BF)
    attended = jnp.einsum("bts,bsd->btd", probs_low, values, preferred_element_type=F32).astype(BF)
    attended_rows = by_device(attended)
    attn_part = product(attended_rows, output_head).astype(BF).reshape(GROUPS, own, width)
    attn_out = scatter16(attn_part, 2)

    x_wide = x_own.astype(F32)
    middle = x_wide + attn_out
    normed_mix, unit_mix, factor_mix = norm_forward(middle, gain_mixer)
    hidden_mix = normed_mix.astype(BF)
    mix_all = gather16(hidden_mix, 3).reshape(total, width)

    shared_width = share_gate.shape[1]
    fan = jnp.concatenate(
        [share_gate, router_full, jnp.zeros((width, 256 - shared_width - GROUPS), BF),
         share_up, jnp.zeros((width, 256 - shared_width), BF)], axis=1)
    fanned = product(mix_all, fan)
    shared_gate_in = fanned[:, :shared_width]
    logits_all = fanned[:, shared_width : shared_width + GROUPS]
    shared_up_in = fanned[:, 256 : 256 + shared_width]
    shared_act, shared_slope = silu_pair(shared_gate_in)
    shared_hidden = (shared_act * shared_up_in).astype(BF)

    blocks = GROUPS * batches
    mask_all = selected_experts(routes_all)
    gates_all = masked_softmax(logits_all, mask_all)
    mine = jnp.arange(GROUPS) == me
    taken = (jnp.any(mask_all & mine, axis=1) & valid_all).reshape(blocks, here)
    gates_mine = jnp.sum(jnp.where(mine, gates_all, 0.0), axis=1).reshape(blocks, here)
    place_in = jnp.cumsum(taken.astype(jnp.int32), axis=1) - 1
    slots = 32
    spread = (place_in[:, None, :] == jnp.arange(slots)[None, :, None]) & taken[:, None, :]
    spread_low = spread.astype(BF)
    gates_rows = jnp.sum(jnp.where(spread, gates_mine[:, None, :], 0.0), axis=2).reshape(blocks * slots, 1)

    def to_slots(v):
        return jnp.einsum(
            "bst,btd->bsd", spread_low, v.reshape(blocks, here, width), preferred_element_type=F32
        ).astype(BF).reshape(blocks * slots, width)

    def to_tokens(v):
        return jnp.einsum(
            "bst,bsd->btd", spread_low, v.reshape(blocks, slots, width), preferred_element_type=F32
        ).reshape(total, width)

    rows = to_slots(mix_all)
    grad_rows = to_slots(grad_all)
    gate_in = product(rows, gate_full)
    up_in = product(rows, up_full)
    activated, slope = silu_pair(gate_in)
    hidden = (activated * up_in).astype(BF)
    result = product(hidden, down_full).astype(BF)
    out_part = product(shared_hidden, share_down) + gates_mine.reshape(total, 1) * to_tokens(result)
    out_part = out_part.astype(BF).reshape(GROUPS, own, width)
    mixed = scatter16(out_part, 4)
    layer_output = valid_own[:, None] * (middle + mixed)

    grad_wide = grad_rows.astype(F32)
    grad_gates = jnp.sum(grad_wide * result.astype(F32), axis=1).reshape(blocks, slots)
    grad_gates = jnp.sum(jnp.where(spread, grad_gates[:, :, None], 0.0), axis=1).reshape(total, 1)
    grad_result = (gates_rows * grad_wide).astype(BF)
    grad_down = product_lead(hidden, grad_result).astype(BF)
    grad_hidden = product_trail(grad_result, down_full)
    grad_gate_in = (grad_hidden * up_in * slope).astype(BF)
    grad_up_in = (grad_hidden * activated).astype(BF)
    grad_gate = product_lead(rows, grad_gate_in).astype(BF)
    grad_up = product_lead(rows, grad_up_in).astype(BF)
    grad_taken = (product_trail(grad_gate_in, gate_full) + product_trail(grad_up_in, up_full)).astype(BF)

    grad_shared_down = product_lead(shared_hidden, grad_all).astype(BF)
    grad_shared_hidden = product_trail(grad_all, share_down)
    grad_shared_gate_in = (grad_shared_hidden * shared_up_in * shared_slope).astype(BF)
    grad_shared_up_in = (grad_shared_hidden * shared_act).astype(BF)
    grad_shared_gate = product_lead(mix_all, grad_shared_gate_in).astype(BF)
    grad_shared_up = product_lead(mix_all, grad_shared_up_in).astype(BF)
    mix_part = (
        product_trail(grad_shared_gate_in, share_gate)
        + product_trail(grad_shared_up_in, share_up)
        + to_tokens(grad_taken)
    ).astype(BF)
    gates_high = grad_gates.astype(BF)
    gates_low = (grad_gates - gates_high.astype(F32)).astype(BF)
    lane = jnp.arange(128)
    gates_part = jnp.where(lane == me, gates_high, jnp.where(lane == me + GROUPS, gates_low, 0))
    mix_part = jnp.concatenate([mix_part, gates_part], axis=1).reshape(GROUPS, own, width + 128)
    mix_part, grad_gate, grad_up, grad_down = lax.optimization_barrier(
        (mix_part, grad_gate, grad_up, grad_down))
    mix_sum = scatter16(mix_part, 5)

    out_gate = lax.psum_scatter(grad_gate, "dp", scatter_dimension=0, tiled=True)
    out_up = lax.psum_scatter(grad_up, "dp", scatter_dimension=0, tiled=True)
    out_down = lax.psum_scatter(grad_down, "dp", scatter_dimension=0, tiled=True)
    out_shared_gate = lax.psum_scatter(grad_shared_gate, "dp", scatter_dimension=0, tiled=True)
    out_shared_up = lax.psum_scatter(grad_shared_up, "dp", scatter_dimension=0, tiled=True)
    out_shared_down = lax.psum_scatter(grad_shared_down, "dp", scatter_dimension=1, tiled=True)

    mask_own = selected_experts(routes_own)
    soft_own = masked_softmax(product(hidden_mix, router_full), mask_own)
    grad_masked = (mix_sum[:, width : width + GROUPS] + mix_sum[:, width + GROUPS : width + 2 * GROUPS])
    grad_masked = grad_masked * valid_own[:, None]
    grad_logits = soft_own * (grad_masked - jnp.sum(grad_masked * soft_own, axis=1, keepdims=True))
    grad_logits = grad_logits.astype(BF)
    grad_mix = mix_sum[:, :width] + product_trail(grad_logits, router_full)
    grad_middle_norm, grad_gain_mixer = norm_backward(grad_mix, unit_mix, factor_mix, gain_mixer)
    grad_middle = grad_own.astype(F32) + grad_middle_norm

    grad_attn_all = gather16(grad_middle.astype(BF), 6).reshape(total, width)
    grad_output = product_lead(attended_rows, grad_attn_all)
    grad_attended = by_sequence(product_trail(grad_attn_all, output_head).astype(BF))
    probs = jnp.exp(score(query, key) - log_total)
    probs_low = probs.astype(BF)
    grad_probs = jnp.einsum("btd,bsd->bts", grad_attended, values, preferred_element_type=F32)
    inner_sum = jnp.sum(grad_probs * probs, axis=-1, keepdims=True)
    grad_scores = (probs * (grad_probs - inner_sum)).astype(BF)
    grad_query = jnp.einsum("bts,bsd->btd", grad_scores, key, preferred_element_type=F32) * scale_factor
    grad_key = jnp.einsum("bts,btd->bsd", grad_scores, query, preferred_element_type=F32) * scale_factor
    grad_values = jnp.einsum("bts,btd->bsd", probs_low, grad_attended, preferred_element_type=F32)
    grad_expanded = jnp.concatenate([grad_key[..., :QK_NOPE], grad_values], axis=-1).astype(BF)
    grad_expanded = grad_expanded.reshape(total, -1)
    grad_expand = product_lead(latent.reshape(total, -1), grad_expanded)
    grad_latent = product_trail(grad_expanded, expand_head)
    grad_query = jnp.concatenate(
        [grad_query[..., :QK_NOPE], rotate(grad_query[..., QK_NOPE:], cosine, -sine_table)], axis=-1
    ).astype(BF)
    grad_query = by_device(grad_query)
    grad_query_w = product_lead(hidden_all, grad_query)
    back_part = product_trail(grad_query, query_head).astype(BF)
    latent_part = jnp.concatenate(
        [grad_latent.astype(BF).reshape(batches, seq_total, -1), grad_key[..., QK_NOPE:].astype(BF),
         jnp.zeros((batches, seq_total, 64), BF)], axis=-1)
    back_part = jnp.concatenate([back_part, by_device(latent_part)], axis=1)
    back_sum = scatter16(back_part.reshape(GROUPS, own, back_part.shape[1]), 7)

    x_normed, unit_attn, factor_attn = norm_forward(x_wide, gain_attn)
    hidden_own = x_normed.astype(BF)
    latent_own = product(hidden_own, latent_full)
    _, unit_latent, factor_latent = norm_forward(latent_own[:, :KV_RANK], gain_latent)
    grad_latent_in, grad_gain_latent = norm_backward(
        back_sum[:, width : width + KV_RANK], unit_latent, factor_latent, gain_latent
    )
    grad_rope = back_sum[:, width + KV_RANK : width + KV_RANK + ROPE].reshape(batches, here, ROPE)
    grad_rope = rotate(grad_rope, cosine_own, -sine_own).reshape(own, ROPE)
    grad_latent_raw = jnp.concatenate([grad_latent_in, grad_rope], axis=1).astype(BF)
    grad_hidden_attn = back_sum[:, :width] + product_trail(grad_latent_raw, latent_full)
    grad_input_norm, grad_gain_attn = norm_backward(grad_hidden_attn, unit_attn, factor_attn, gain_attn)
    grad_input = grad_middle + grad_input_norm

    latent_rows = grad_gain_latent.reshape(dp * GROUPS, rows_l)
    latent_rows = jnp.pad(latent_rows, ((0, 0), (0, rows_w - rows_l))).reshape(width, 1)
    tokens_side = jnp.concatenate([hidden_own, hidden_mix], axis=0)
    grads_side = jnp.concatenate(
        [jnp.pad(grad_latent_raw, ((0, 0), (0, 64))), jnp.pad(grad_logits, ((0, 0), (576, 640 - 592)))], axis=0)
    lane = jnp.arange(640)[None, :]
    small_grad = product_lead(tokens_side, grads_side)
    small_grad = small_grad + jnp.where(lane == 592, grad_gain_attn[:, None], 0.0)
    small_grad = small_grad + jnp.where(lane == 593, grad_gain_mixer[:, None], 0.0)
    small_grad = (small_grad + jnp.where(lane == 594, latent_rows, 0.0)).astype(BF)
    small_sum = lax.psum_scatter(small_grad, ("dp", "expert"), scatter_dimension=0, tiled=True).astype(F32)

    def home(v, rows):
        v = v.reshape(dp, GROUPS, rows, v.shape[-1])
        v = lax.psum_scatter(v.astype(BF), "dp", scatter_dimension=0, tiled=False)
        v = lax.all_to_all(v, "expert", 0, 0, tiled=True)
        return v.transpose(1, 0, 2).reshape(rows, -1).astype(F32)

    out_query = home(grad_query_w, rows_w)
    out_expand = home(grad_expand, rows_l)
    grad_output = lax.psum(grad_output, "dp").reshape(dp, rows_w, width)
    out_output = jnp.zeros((rows_w, width), F32)
    for i, (sources, blocks) in enumerate(head_blocks(dp)):
        block = lax.dynamic_index_in_dim(grad_output, (i + shift) % dp, 0, False)
        block = lax.ppermute(block, "expert", [(h, s) for h, s in enumerate(sources)])
        table = [0] * GROUPS
        for source, at in zip(sources, blocks):
            table[source] = at
        out_output = jnp.where(jnp.array(table, jnp.int32)[me] == plane, block, out_output)

    def as_input(v):
        return v.reshape(batches, 1, here, width)

    return (
        as_input(layer_output),
        as_input(grad_input),
        small_sum[:, 592],
        out_query,
        small_sum[:, :576],
        small_sum[:rows_l, 594],
        out_expand,
        out_output,
        small_sum[:, 593],
        small_sum[:, 576:592],
        out_gate.astype(F32)[None],
        out_up.astype(F32)[None],
        out_down.astype(F32)[None],
        out_shared_gate.astype(F32),
        out_shared_up.astype(F32),
        out_shared_down.astype(F32),
    )


def solution(mesh):
    split = P(("dp", "expert"), None)
    line = P(("dp", "expert"))
    tokens = P(None, "dp", "expert", None)
    expert = P("expert", "dp", None)
    return jax.shard_map(
        per_device,
        mesh=mesh,
        in_specs=(
            tokens, tokens, P(None, "dp"), tokens, line, split, split, line, split, split, line, split,
            expert, expert, expert, P("dp", "expert"), P("dp", "expert"), P("expert", "dp"),
        ),
        out_specs=(
            tokens, tokens, line, split, split, line, split, split, line, split,
            expert, expert, expert, P("dp", "expert"), P("dp", "expert"), P("expert", "dp"),
        ),
        check_vma=False,
    )
```

```python
import functools
import jax
import jax.numpy as jnp
from jax import lax
from jax.experimental import pallas as pl
from jax.experimental.pallas import tpu as pltpu
from jax.sharding import PartitionSpec as P

MESH = pl.DeviceIdType.MESH
NZ = 4
NE = 16


def place():
    me = lax.axis_index("expert")
    z = me // 4
    x = (me // 2) % 2
    c = me % 2
    return me, z, x, c, me + 1 - 2 * c, me + 2 - 4 * x


def enter(me, z, core, side):
    barrier = pltpu.get_barrier_semaphore()
    for other in (core, side):
        pl.semaphore_signal(barrier, inc=1, device_id={"expert": other}, device_id_type=MESH)

    @pl.when(z < NZ - 1)
    def _():
        pl.semaphore_signal(barrier, inc=1, device_id={"expert": me + 4}, device_id_type=MESH)

    @pl.when(z > 0)
    def _():
        pl.semaphore_signal(barrier, inc=1, device_id={"expert": me - 4}, device_id_type=MESH)

    pl.semaphore_wait(barrier, 2 + (z < NZ - 1).astype(jnp.int32) + (z > 0).astype(jnp.int32))


def enter_all(me, plane, dp):
    barrier = pltpu.get_barrier_semaphore()
    for r in range(1, NE):
        pl.semaphore_signal(
            barrier, inc=1, device_id={"expert": (me + r) % NE}, device_id_type=MESH)
    for r in range(1, dp):
        pl.semaphore_signal(
            barrier, inc=1, device_id={"dp": (plane + r) % dp}, device_id_type=MESH)
    pl.semaphore_wait(barrier, NE - 1 + dp - 1)


class Gather:
    def __init__(self, src, out, chunks, sems):
        self.src, self.out, self.chunks = src, out, chunks
        self.rows = src.shape[0] // chunks
        self.own_sem, self.us, self.ur, self.ds, self.dr, self.xs, self.xr, self.cs, self.cr = sems
        self.me, self.z, self.x, self.c, self.core, self.side = place()

    @staticmethod
    def scratch(chunks):
        dma = pltpu.SemaphoreType.DMA
        return [dma] + [dma((4, chunks))] * 4 + [dma((7, chunks))] * 2 + [dma((14, chunks))] * 2

    def copy(self, block, k, src, send, recv, to):
        part = pl.ds(k * self.rows, self.rows)
        return pltpu.make_async_remote_copy(
            src_ref=(self.src if src is None else self.out.at[src]).at[part],
            dst_ref=self.out.at[block].at[part],
            send_sem=send, recv_sem=recv,
            device_id={"expert": to}, device_id_type=MESH,
        )

    def up(self, k, s, src=None):
        return self.copy(self.me - 4 * s, k, src, self.us.at[s, k], self.ur.at[s, k], self.me + 4)

    def down(self, k, s, src=None):
        return self.copy(self.me + 4 * s, k, src, self.ds.at[s, k], self.dr.at[s, k], self.me - 4)

    def across(self, k, slot, block, src=None):
        return self.copy(block, k, src, self.xs.at[slot, k], self.xr.at[slot, k], self.side)

    def over(self, k, slot, block, src=None):
        return self.copy(block, k, src, self.cs.at[slot, k], self.cr.at[slot, k], self.core)

    def up_in(self, k, s):
        b = self.me - 4 * s
        return self.copy(b, k, b, self.us.at[s - 1, k], self.ur.at[s - 1, k], self.side)

    def dn_in(self, k, s):
        b = self.me + 4 * s
        return self.copy(b, k, b, self.ds.at[s - 1, k], self.dr.at[s - 1, k], self.side)

    def shift(self, base, slot):
        return base - 4 * slot if slot <= 3 else base + 4 * (slot - 3)

    def core_block(self, slot):
        if slot < 7:
            return self.shift(self.core, slot)
        return self.shift(self.core + 2 - 4 * self.x, slot - 7)

    def has(self, slot):
        slot = slot % 7
        if slot == 0:
            return self.z >= 0
        return self.z >= slot if slot <= 3 else self.z + (slot - 3) <= NZ - 1

    def start(self):
        z, me = self.z, self.me
        self.own = pltpu.make_async_copy(self.src, self.out.at[me], self.own_sem)
        self.own.start()
        for k in range(self.chunks):
            self.across(k, 0, me).start()

            @pl.when(z < NZ - 1)
            def _():
                self.up(k, 0).start()

            @pl.when(z > 0)
            def _():
                self.down(k, 0).start()

            self.over(k, 0, me).start()

    def line(self, k, s):
        z, me = self.z, self.me

        @pl.when(z >= s)
        def _():
            b = me - 4 * s
            self.up_in(k, s).wait_recv()
            self.across(k, s, b, b).start()

            @pl.when(z < NZ - 1)
            def _():
                self.up(k, s, b).start()

            self.over(k, s, b, b).start()

        @pl.when(z + s <= NZ - 1)
        def _():
            b = me + 4 * s
            self.dn_in(k, s).wait_recv()
            self.across(k, 3 + s, b, b).start()

            @pl.when(z > 0)
            def _():
                self.down(k, s, b).start()

            self.over(k, 3 + s, b, b).start()

    def from_side(self, k, slot):
        @pl.when(self.has(slot))
        def _():
            b = self.shift(self.side, slot)
            self.across(k, slot, b, b).wait_recv()
            self.over(k, 7 + slot, b, b).start()

    def round(self, s):
        if s < NZ:
            for k in range(self.chunks):
                self.line(k, s)
        for k in range(self.chunks):
            for slot in ((0,) if s == 1 else (s - 1, s + 2)):
                self.from_side(k, slot)

    def finish(self):
        z = self.z
        self.own.wait()
        for k in range(self.chunks):
            for slot in range(14):
                @pl.when(self.has(slot))
                def _():
                    b = self.core_block(slot)
                    self.over(k, slot, b, b).wait_recv()
                    self.over(k, slot, b, b).wait_send()
            for slot in range(7):
                @pl.when(self.has(slot))
                def _():
                    self.across(k, slot, self.me).wait_send()
            for s in range(NZ - 1):
                @pl.when((z >= s) & (z < NZ - 1))
                def _():
                    self.up(k, s).wait_send()

                @pl.when((z + s <= NZ - 1) & (z > 0))
                def _():
                    self.down(k, s).wait_send()


def gather_kernel(chunks, x_ref, o_ref, *sems):
    g = Gather(x_ref, o_ref, chunks, sems)
    enter(g.me, g.z, g.core, g.side)
    g.start()
    for s in range(1, NZ + 1):
        g.round(s)
    g.finish()


COST = pl.CostEstimate(flops=0, bytes_accessed=4_000_000, transcendentals=0)
ANY = pl.BlockSpec(memory_space=pl.ANY)


def gather16(v, cid, chunks=4):
    rows, width = v.shape
    return pl.pallas_call(
        functools.partial(gather_kernel, chunks),
        out_shape=jax.ShapeDtypeStruct((NE, rows, width), v.dtype),
        in_specs=[ANY],
        out_specs=ANY,
        scratch_shapes=Gather.scratch(chunks),
        compiler_params=pltpu.CompilerParams(collective_id=cid, has_side_effects=True),
        cost_estimate=COST,
        name="gather16",
    )(v)


def opening_kernel(dp, chunks, x_ref, small_ref, parts_ref, out_ref,
                   x_all, small_all, parts_head, out_head, small_dp, parts_dp, out_dp, *sems):
    ng = 9
    gx = Gather(x_ref, x_all, chunks, sems[:ng])
    gs = Gather(small_dp, small_all, 1, sems[ng:2 * ng])
    loc, ys, yr, ps, pr, os_, or_, pl_sem, ol_sem = sems[2 * ng:]
    me = gx.me
    plane = lax.axis_index("dp")
    rows = parts_ref.shape[1]
    enter_all(me, plane, dp)
    pairs = ((small_ref, small_dp.at[pl.ds(plane * rows, rows)]), (parts_ref, parts_dp.at[plane]),
             (out_ref, out_dp.at[plane]))

    def lift(i, r):
        src, dst = pairs[i]
        return pltpu.make_async_remote_copy(
            src_ref=src, dst_ref=dst, send_sem=ys.at[i, r], recv_sem=yr.at[i, r],
            device_id={"dp": (plane + r) % dp}, device_id_type=MESH)

    def landed(i, r):
        p = (plane - r + dp) % dp
        dst = (small_dp.at[pl.ds(p * rows, rows)], parts_dp.at[p], out_dp.at[p])[i]
        return pltpu.make_async_remote_copy(
            src_ref=dst, dst_ref=dst, send_sem=ys.at[i, r], recv_sem=yr.at[i, r],
            device_id={"dp": p}, device_id_type=MESH)

    def kept(i):
        src, dst = pairs[i]
        return pltpu.make_async_copy(src, dst, loc.at[i])

    for i in range(3):
        for r in range(1, dp):
            lift(i, r).start()
        kept(i).start()
    gx.start()
    gx.round(1)

    kept(0).wait()
    for r in range(1, dp):
        landed(0, r).wait_recv()
    gs.start()

    def part(r):
        h = (me + r) % NE
        return pltpu.make_async_remote_copy(
            src_ref=parts_dp.at[:, h], dst_ref=parts_head.at[:, me],
            send_sem=ps.at[r], recv_sem=pr.at[r],
            device_id={"expert": h}, device_id_type=MESH)

    def part_in(r):
        e = (me - r + NE) % NE
        return pltpu.make_async_remote_copy(
            src_ref=parts_head.at[:, e], dst_ref=parts_head.at[:, e],
            send_sem=ps.at[r], recv_sem=pr.at[r],
            device_id={"expert": e}, device_id_type=MESH)

    def part_kept():
        return pltpu.make_async_copy(parts_dp.at[:, me], parts_head.at[:, me], pl_sem)

    kept(1).wait()
    for r in range(1, dp):
        landed(1, r).wait_recv()
    for r in range(1, NE):
        part(r).start()
    part_kept().start()
    gx.round(2)

    def row(d):
        b = NE * d + me
        return pltpu.make_async_remote_copy(
            src_ref=out_dp.at[d], dst_ref=out_head.at[b % dp],
            send_sem=os_.at[d], recv_sem=or_.at[b % dp],
            device_id={"expert": b // dp}, device_id_type=MESH)

    def row_kept(d):
        b = NE * d + me
        return pltpu.make_async_copy(out_dp.at[d], out_head.at[b % dp], ol_sem.at[d])

    kept(2).wait()
    for r in range(1, dp):
        landed(2, r).wait_recv()
    for d in range(dp):
        home = (NE * d + me) // dp

        @pl.when(home != me)
        def _():
            row(d).start()

        @pl.when(home == me)
        def _():
            row_kept(d).start()

    gs.round(1)
    gx.round(3)
    gs.round(2)
    gx.round(4)
    gs.round(3)
    gs.round(4)

    def row_in(j):
        return pltpu.make_async_remote_copy(
            src_ref=out_head.at[j], dst_ref=out_head.at[j], send_sem=os_.at[j], recv_sem=or_.at[j],
            device_id={"expert": gx.core}, device_id_type=MESH)

    for r in range(1, NE):
        part_in(r).wait_recv()
        part(r).wait_send()
    part_kept().wait()
    for j in range(dp):
        @pl.when((dp * me + j) % NE != me)
        def _():
            row_in(j).wait_recv()
    for d in range(dp):
        home = (NE * d + me) // dp

        @pl.when(home != me)
        def _():
            row(d).wait_send()

        @pl.when(home == me)
        def _():
            row_kept(d).wait()
    for i in range(3):
        for r in range(1, dp):
            lift(i, r).wait_send()
    gx.finish()
    gs.finish()


def opening(dp, x, small, parts, out, cid, chunks=4):
    dma = pltpu.SemaphoreType.DMA
    rows, ws = small.shape
    bf = x.dtype
    wo = out.shape[1]
    shape = jax.ShapeDtypeStruct
    res = pl.pallas_call(
        functools.partial(opening_kernel, dp, chunks),
        out_shape=(
            shape((NE,) + x.shape, bf), shape((NE, dp * rows, ws), bf), shape((dp, NE) + parts.shape[1:], bf),
            shape((dp, rows, wo), bf),
            shape((dp * rows, ws), bf), shape((dp,) + parts.shape, bf), shape((dp, rows, wo), bf),
        ),
        in_specs=[ANY] * 4,
        out_specs=[ANY] * 7,
        scratch_shapes=Gather.scratch(chunks) + Gather.scratch(1) + [
            dma((3,)), dma((3, dp)), dma((3, dp)), dma((NE,)), dma((NE,)), dma((dp,)), dma((dp,)), dma, dma((dp,))],
        compiler_params=pltpu.CompilerParams(collective_id=cid, has_side_effects=True),
        cost_estimate=COST,
        name="opening",
    )(x, small, parts, out)
    return res[:4]


def order(z, i):
    a, b = (3, 2, 1, 0)[i], (3, 2, 0, 1)[i]
    return jnp.where(z == 0, a, jnp.where(z == 1, b, jnp.where(z == 2, 3 - b, 3 - a)))


class Scatter:
    def __init__(self, p_ref, o_ref, chunks, scratch):
        self.p, self.o, self.chunks = p_ref, o_ref, chunks
        (self.cbuf, self.own, self.xbuf, self.ubuf, self.dbuf, self.ld, self.cs, self.cr, self.xs, self.xr,
         self.us, self.ur, self.ds, self.dr) = scratch
        self.rows = o_ref.shape[0] // chunks
        self.me, self.z, self.x, self.c, self.core, self.side = place()

    @staticmethod
    def scratch(rows, width, chunks, bf):
        dma = pltpu.SemaphoreType.DMA
        return [pltpu.VMEM((n, rows, width), bf) for n in (8, 8, 4, 4, 4)] + [
            dma((8,)), dma((8, chunks)), dma((8, chunks))] + [dma((4, chunks))] * 6

    def rng(self, k):
        return pl.ds(k * self.rows, self.rows)

    def column(self, i, j):
        return 4 * order(self.z, i) + 2 * jnp.where(j == 0, 1 - self.x, self.x)

    def remote(self, src, dst, send, recv, to):
        return pltpu.make_async_remote_copy(
            src_ref=src, dst_ref=dst, send_sem=send, recv_sem=recv,
            device_id={"expert": to}, device_id_type=MESH)

    def over(self, i, j, k):
        n = 2 * i + j
        return self.remote(
            self.p.at[self.column(i, j) + 1 - self.c, self.rng(k)], self.cbuf.at[n, self.rng(k)],
            self.cs.at[n, k], self.cr.at[n, k], self.core)

    def load(self, i, j):
        n = 2 * i + j
        return pltpu.make_async_copy(self.p.at[self.column(i, j) + self.c], self.own.at[n], self.ld.at[n])

    def across(self, i, k):
        return self.remote(self.own.at[2 * i, self.rng(k)], self.xbuf.at[i, self.rng(k)],
                           self.xs.at[i, k], self.xr.at[i, k], self.side)

    def up(self, t, i, k):
        return self.remote(self.own.at[2 * i + 1, self.rng(k)], self.ubuf.at[t, self.rng(k)],
                           self.us.at[t, k], self.ur.at[t, k], self.me + 4)

    def down(self, t, i, k):
        return self.remote(self.own.at[2 * i + 1, self.rng(k)], self.dbuf.at[t, self.rng(k)],
                           self.ds.at[t, k], self.dr.at[t, k], self.me - 4)

    def start(self):
        for i in range(NZ):
            for j in range(2):
                self.load(i, j).start()
                for k in range(self.chunks):
                    self.over(i, j, k).start()

    def first(self, i):
        f32 = jnp.float32
        self.load(i, 0).wait()
        for k in range(self.chunks):
            self.over(i, 0, k).wait_recv()
            s = self.rng(k)
            self.own[2 * i, s] = (
                self.own[2 * i, s].astype(f32) + self.cbuf[2 * i, s].astype(f32)).astype(self.own.dtype)
            self.across(i, k).start()

    def second(self, i):
        f32 = jnp.float32
        z, own, o = self.z, self.own, self.o
        t = order(z, i)
        self.load(i, 1).wait()
        for k in range(self.chunks):
            s = self.rng(k)
            self.over(i, 1, k).wait_recv()
            self.across(i, k).wait_recv()

            def base():
                return (own[2 * i + 1, s].astype(f32) + self.cbuf[2 * i + 1, s].astype(f32)
                        + self.xbuf[i, s].astype(f32))

            if i < NZ - 1:
                @pl.when(t > z)
                def _():
                    @pl.when(z > 0)
                    def _():
                        self.up(t, i, k).wait_recv()
                        own[2 * i + 1, s] = (base() + self.ubuf[t, s].astype(f32)).astype(own.dtype)

                    @pl.when(z == 0)
                    def _():
                        own[2 * i + 1, s] = base().astype(own.dtype)

                    self.up(t, i, k).start()

                @pl.when(t < z)
                def _():
                    @pl.when(z < NZ - 1)
                    def _():
                        self.down(t, i, k).wait_recv()
                        own[2 * i + 1, s] = (base() + self.dbuf[t, s].astype(f32)).astype(own.dtype)

                    @pl.when(z == NZ - 1)
                    def _():
                        own[2 * i + 1, s] = base().astype(own.dtype)

                    self.down(t, i, k).start()
            else:
                @pl.when(z > 0)
                def _():
                    self.up(t, i, k).wait_recv()

                @pl.when(z < NZ - 1)
                def _():
                    self.down(t, i, k).wait_recv()

                @pl.when((z > 0) & (z < NZ - 1))
                def _():
                    o[s] = (base() + self.ubuf[t, s].astype(f32) + self.dbuf[t, s].astype(f32)).astype(o.dtype)

                @pl.when(z == 0)
                def _():
                    o[s] = (base() + self.dbuf[t, s].astype(f32)).astype(o.dtype)

                @pl.when(z == NZ - 1)
                def _():
                    o[s] = (base() + self.ubuf[t, s].astype(f32)).astype(o.dtype)

    def run(self):
        self.first(0)
        for i in range(NZ):
            if i + 1 < NZ:
                self.first(i + 1)
            self.second(i)

    def finish(self):
        z = self.z
        for k in range(self.chunks):
            for i in range(NZ):
                self.across(i, k).wait_send()
                for j in range(2):
                    self.over(i, j, k).wait_send()
                if i < NZ - 1:
                    t = order(z, i)

                    @pl.when(t > z)
                    def _():
                        self.up(t, i, k).wait_send()

                    @pl.when(t < z)
                    def _():
                        self.down(t, i, k).wait_send()


def scatter_kernel(chunks, p_ref, o_ref, *scratch):
    s = Scatter(p_ref, o_ref, chunks, scratch)
    enter(s.me, s.z, s.core, s.side)
    s.start()
    s.run()
    s.finish()


VMEM = pl.BlockSpec(memory_space=pltpu.VMEM)


def scatter16(p, cid, chunks=2, out_dtype=jnp.float32):
    _, rows, width = p.shape
    return pl.pallas_call(
        functools.partial(scatter_kernel, chunks),
        out_shape=jax.ShapeDtypeStruct((rows, width), out_dtype),
        in_specs=[ANY],
        out_specs=VMEM,
        scratch_shapes=Scatter.scratch(rows, width, chunks, p.dtype),
        compiler_params=pltpu.CompilerParams(
            collective_id=cid, has_side_effects=True, vmem_limit_bytes=32 * 1024 * 1024),
        cost_estimate=COST,
        name="scatter16",
    )(p)


def return_kernel(dp, chunks, p_ref, parts_ref, rows_ref, o_ref, parts_in, rows_in, parts_far, rows_far, *scratch):
    ns = 14
    s = Scatter(p_ref, o_ref, chunks, scratch[:ns])
    ps, pr, os_, or_, pl_sem, ol_sem, ys, yr = scratch[ns:]
    me = s.me
    plane = lax.axis_index("dp")
    enter_all(me, plane, dp)

    def part(r):
        e = (me + r) % NE
        return pltpu.make_async_remote_copy(
            src_ref=parts_ref.at[:, e], dst_ref=parts_in.at[:, me],
            send_sem=ps.at[r], recv_sem=pr.at[r],
            device_id={"expert": e}, device_id_type=MESH)

    def part_in(r):
        h = (me - r + NE) % NE
        return pltpu.make_async_remote_copy(
            src_ref=parts_in.at[:, h], dst_ref=parts_in.at[:, h],
            send_sem=ps.at[r], recv_sem=pr.at[r],
            device_id={"expert": h}, device_id_type=MESH)

    def part_kept():
        return pltpu.make_async_copy(parts_ref.at[:, me], parts_in.at[:, me], pl_sem)

    def row(j):
        b = dp * me + j
        return pltpu.make_async_remote_copy(
            src_ref=rows_ref.at[j], dst_ref=rows_in.at[b // NE],
            send_sem=os_.at[j], recv_sem=or_.at[b // NE],
            device_id={"expert": b % NE}, device_id_type=MESH)

    def row_kept(j):
        b = dp * me + j
        return pltpu.make_async_copy(rows_ref.at[j], rows_in.at[b // NE], ol_sem.at[j])

    def row_in(d):
        return pltpu.make_async_remote_copy(
            src_ref=rows_in.at[d], dst_ref=rows_in.at[d], send_sem=os_.at[d], recv_sem=or_.at[d],
            device_id={"expert": s.core}, device_id_type=MESH)

    def lift(i, r):
        to = (plane + r) % dp
        src, dst = ((parts_in.at[to], parts_far.at[r - 1]), (rows_in.at[to], rows_far.at[r - 1]))[i]
        return pltpu.make_async_remote_copy(
            src_ref=src, dst_ref=dst, send_sem=ys.at[i, r], recv_sem=yr.at[i, r],
            device_id={"dp": to}, device_id_type=MESH)

    s.start()
    for r in range(1, NE):
        part(r).start()
    part_kept().start()
    for j in range(dp):
        @pl.when((dp * me + j) % NE != me)
        def _():
            row(j).start()

        @pl.when((dp * me + j) % NE == me)
        def _():
            row_kept(j).start()
    s.first(0)
    s.first(1)
    s.second(0)
    for r in range(1, NE):
        part_in(r).wait_recv()
    part_kept().wait()
    for j in range(dp):
        @pl.when((dp * me + j) % NE == me)
        def _():
            row_kept(j).wait()
    for d in range(dp):
        @pl.when((NE * d + me) // dp != me)
        def _():
            row_in(d).wait_recv()
    for i in range(2):
        for r in range(1, dp):
            lift(i, r).start()
    s.first(2)
    s.second(1)
    s.first(3)
    s.second(2)
    s.second(3)
    for i in range(2):
        for r in range(1, dp):
            lift(i, r).wait_recv()
            lift(i, r).wait_send()
    for r in range(1, NE):
        part(r).wait_send()
    for j in range(dp):
        @pl.when((dp * me + j) % NE != me)
        def _():
            row(j).wait_send()
    s.finish()


def returning(dp, p, parts, rows, cid, chunks=2):
    dma = pltpu.SemaphoreType.DMA
    _, n, width = p.shape
    shape = jax.ShapeDtypeStruct
    out, parts_in, rows_in, parts_far, rows_far = pl.pallas_call(
        functools.partial(return_kernel, dp, chunks),
        out_shape=(
            shape((n, width), jnp.float32), shape(parts.shape, parts.dtype), shape(rows.shape, rows.dtype),
            shape((dp - 1,) + parts.shape[1:], parts.dtype), shape((dp - 1,) + rows.shape[1:], rows.dtype)),
        in_specs=[ANY] * 3,
        out_specs=[VMEM] + [ANY] * 4,
        scratch_shapes=Scatter.scratch(n, width, chunks, p.dtype) + [
            dma((NE,)), dma((NE,)), dma((dp,)), dma((dp,)), dma, dma((dp,)), dma((2, dp)), dma((2, dp))],
        compiler_params=pltpu.CompilerParams(
            collective_id=cid, has_side_effects=True, vmem_limit_bytes=48 * 1024 * 1024),
        cost_estimate=COST,
        name="returning",
    )(p, parts, rows)
    plane = lax.axis_index("dp")

    def total(near, far):
        own = lax.dynamic_index_in_dim(near, plane, 0, False).astype(jnp.float32)
        return own + jnp.sum(far.astype(jnp.float32), axis=0)

    return out, total(parts_in, parts_far), total(rows_in, rows_far)


def closing_kernel(dp, chunks, p_ref, o_ref, far_ref, *scratch):
    ns = 14
    s = Scatter(p_ref, o_ref, chunks, scratch[:ns])
    ys, yr = scratch[ns:]
    plane = lax.axis_index("dp")
    rows = o_ref.shape[0] // dp
    barrier = pltpu.get_barrier_semaphore()
    for r in range(1, dp):
        pl.semaphore_signal(barrier, inc=1, device_id={"dp": (plane + r) % dp}, device_id_type=MESH)
    z = s.z
    for other in (s.core, s.side):
        pl.semaphore_signal(barrier, inc=1, device_id={"expert": other}, device_id_type=MESH)

    @pl.when(z < NZ - 1)
    def _():
        pl.semaphore_signal(barrier, inc=1, device_id={"expert": s.me + 4}, device_id_type=MESH)

    @pl.when(z > 0)
    def _():
        pl.semaphore_signal(barrier, inc=1, device_id={"expert": s.me - 4}, device_id_type=MESH)

    pl.semaphore_wait(barrier, dp + 1 + (z < NZ - 1).astype(jnp.int32) + (z > 0).astype(jnp.int32))

    def lift(r):
        to = (plane + r) % dp
        return pltpu.make_async_remote_copy(
            src_ref=o_ref.at[pl.ds(pl.multiple_of(to * rows, 16), rows)], dst_ref=far_ref.at[r - 1],
            send_sem=ys.at[r], recv_sem=yr.at[r],
            device_id={"dp": to}, device_id_type=MESH)

    s.start()
    s.run()
    for r in range(1, dp):
        lift(r).start()
    s.finish()
    for r in range(1, dp):
        lift(r).wait_recv()
        lift(r).wait_send()


def closing(dp, p, cid):
    dma = pltpu.SemaphoreType.DMA
    _, n, width = p.shape
    shape = jax.ShapeDtypeStruct
    near, far = pl.pallas_call(
        functools.partial(closing_kernel, dp, 1),
        out_shape=(shape((n, width), p.dtype), shape((dp - 1, n // dp, width), p.dtype)),
        in_specs=[ANY],
        out_specs=[VMEM, VMEM],
        scratch_shapes=Scatter.scratch(n, width, 1, p.dtype) + [dma((dp,)), dma((dp,))],
        compiler_params=pltpu.CompilerParams(
            collective_id=cid, has_side_effects=True, vmem_limit_bytes=32 * 1024 * 1024),
        cost_estimate=COST,
        name="closing",
    )(p)
    own = lax.dynamic_slice_in_dim(near, lax.axis_index("dp") * (n // dp), n // dp).astype(jnp.float32)
    return own + jnp.sum(far.astype(jnp.float32), axis=0)
BF = jnp.bfloat16
F32 = jnp.float32


def mm(a, b):
    return jnp.dot(a, b, preferred_element_type=F32)


def mm_t(a, b):
    return lax.dot_general(a, b, (((1,), (1,)), ((), ())), preferred_element_type=F32)


def silu_pair(gate_in):
    sigmoid = 1.0 / (1.0 + jnp.exp(-gate_in))
    return (gate_in * sigmoid, sigmoid * (1.0 + gate_in * (1.0 - sigmoid)))


TILE = 256
WIDE = 512
SHARE = 176


def mixture_kernel(pick_ref, mix_ref, dy_ref, slot_row, slot_col, valid_ref, gu_ref, wd_ref, fan_ref, sd_ref,
                   out_ref, dh_ref, rows_ref, deo_ref, hid_ref, dgu_ref, sh_ref, ds_ref,
                   act_buf, slo_buf):
    tokens, width = mix_ref.shape
    groups = tokens // 256
    slots = 128
    ff = hid_ref.shape[1]

    def lanes(j):
        return pl.ds(pl.multiple_of(j * WIDE, WIDE), WIDE)

    mix = mix_ref[...]
    fanned = mm_t(mix, fan_ref[:TILE, :])
    s_up = mm_t(mix, fan_ref[TILE:, :])
    s_act, s_slope = silu_pair(fanned)
    s_hidden = (s_act * s_up).astype(BF)
    sh_ref[...] = s_hidden
    logits = fanned[:, SHARE:SHARE + 16]
    lane16 = lax.broadcasted_iota(jnp.int32, (tokens, 16), 1).astype(F32)
    routes = dy_ref[:, width:width + 16].astype(F32)
    mask = lane16 < 0
    for k in range(6):
        mask = mask | (lane16 == routes[:, k:k + 1])
    held = jnp.where(mask, logits, -1e30)
    raised = jnp.where(mask, jnp.exp(held - jnp.max(held, axis=1, keepdims=True)), 0.0)
    soft = raised / jnp.sum(raised, axis=1, keepdims=True)
    gate = jnp.sum(soft * pick_ref[:, :16], axis=1, keepdims=True) * valid_ref[...]
    dy = dy_ref[:, :width]
    d_sh = mm_t(dy, sd_ref[...])
    ds_ref[:, :TILE] = (d_sh * s_up * s_slope).astype(BF)
    ds_ref[:, TILE:] = (d_sh * s_act).astype(BF)

    to_slot, to_token = [], []
    for g in range(groups):
        row = slot_row[:, g * 256:(g + 1) * 256]
        col = slot_col[g * 256:(g + 1) * 256, :]
        to_slot.append((lax.broadcasted_iota(jnp.int32, (slots, 256), 0) == row).astype(BF))
        to_token.append((lax.broadcasted_iota(jnp.int32, (256, slots), 1) == col).astype(BF))

    def dispatch(j, _):
        for g in range(groups):
            t = pl.ds(g * 256, 256)
            s = pl.ds(g * slots, slots)
            rows_ref[s, lanes(j)] = mm(to_slot[g], mix_ref[t, lanes(j)]).astype(BF)
            gated = (gate[g * 256:(g + 1) * 256] * dy_ref[t, lanes(j)].astype(F32)).astype(BF)
            deo_ref[s, lanes(j)] = mm(to_slot[g], gated).astype(BF)
        return 0

    lax.fori_loop(0, width // WIDE, dispatch, 0)

    def fan_in(start, size):
        both = mm(rows_ref[...], gu_ref[:, pl.ds(start, size)])
        for i in range(size // TILE):
            gate_in, up_in = both[:, i * TILE:i * TILE + 128], both[:, i * TILE + 128:(i + 1) * TILE]
            act, slope = silu_pair(gate_in)
            half = pl.ds(pl.multiple_of(start // 2 + i * 128, 128), 128)
            hid_ref[:, half] = (act * up_in).astype(BF)
            act_buf[:, half] = act
            slo_buf[:, half] = up_in * slope

    def fan_loop(j, _):
        fan_in(pl.multiple_of(j * WIDE, WIDE), WIDE)
        return 0

    lax.fori_loop(0, 2 * ff // WIDE, fan_loop, 0)
    if 2 * ff % WIDE:
        fan_in(2 * ff // WIDE * WIDE, 2 * ff % WIDE)

    def fan_out(j, d_gates):
        eo = mm(hid_ref[...], wd_ref[:, lanes(j)]).astype(BF)
        shared = mm(s_hidden, sd_ref[:, lanes(j)])
        picked = jnp.concatenate(
            [mm(to_token[g], eo[g * slots:(g + 1) * slots]) for g in range(groups)], axis=0)
        out_ref[:, lanes(j)] = (shared + gate * picked).astype(BF)
        return d_gates + jnp.sum(dy_ref[:, lanes(j)].astype(F32) * picked, axis=1, keepdims=True)

    d_gates = lax.fori_loop(0, width // WIDE, fan_out, jnp.zeros((tokens, 1), F32))

    def back_out(start, size):
        cols = pl.ds(start, size)
        d_eh = mm_t(deo_ref[...], wd_ref[cols, :])
        dg = (d_eh * slo_buf[:, cols]).astype(BF)
        du = (d_eh * act_buf[:, cols]).astype(BF)
        for i in range(size // 128):
            at = pl.multiple_of(2 * start + i * TILE, TILE)
            dgu_ref[:, pl.ds(at, 128)] = dg[:, i * 128:(i + 1) * 128]
            dgu_ref[:, pl.ds(at + 128, 128)] = du[:, i * 128:(i + 1) * 128]

    def back_loop(j, _):
        back_out(pl.multiple_of(j * WIDE, WIDE), WIDE)
        return 0

    lax.fori_loop(0, ff // WIDE, back_loop, 0)
    if ff % WIDE:
        back_out(ff // WIDE * WIDE, ff % WIDE)

    d_s = ds_ref[...]

    def back_in(j, _):
        d_rows = mm_t(dgu_ref[...], gu_ref[lanes(j), :]).astype(BF)
        shared = mm(d_s, fan_ref[:, lanes(j)])
        taken = jnp.concatenate(
            [mm(to_token[g], d_rows[g * slots:(g + 1) * slots]) for g in range(groups)], axis=0)
        dh_ref[:, lanes(j)] = (shared + taken).astype(BF)
        return 0

    lax.fori_loop(0, width // WIDE, back_in, 0)
    high = d_gates.astype(BF).astype(F32)
    tail = high * pick_ref[:, :128] + (d_gates - high) * pick_ref[:, 128:]
    dh_ref[:, width:] = tail.astype(BF)


def mixture(pick, mix, packed, slot_row, slot_col, valid, gu, wd, fan, sd, step=512):
    total, width = mix.shape
    steps = total // step
    ff = wd.shape[0]
    rows = total // 2
    shape = jax.ShapeDtypeStruct
    once = pl.Buffered(buffer_count=1)

    def whole(v):
        return pl.BlockSpec(v.shape, lambda i: (0, 0), pipeline_mode=once)

    def tokens(w):
        return pl.BlockSpec((step, w), lambda i: (i, 0))

    def slots(w):
        return pl.BlockSpec((step // 2, w), lambda i: (i, 0))

    return pl.pallas_call(
        mixture_kernel,
        grid=(steps,),
        out_shape=(
            shape((total, width), BF), shape((total, width + 128), BF), shape((rows, width), BF),
            shape((rows, width), BF), shape((rows, ff), BF), shape((rows, 2 * ff), BF),
            shape((total, TILE), BF), shape((total, 2 * TILE), BF)),
        in_specs=[whole(pick), tokens(width), tokens(width + 128), pl.BlockSpec((1, step), lambda i: (0, i)),
                  tokens(1), tokens(1), whole(gu), whole(wd), whole(fan), whole(sd)],
        out_specs=[tokens(width), tokens(width + 128), slots(width), slots(width), slots(ff), slots(2 * ff),
                   tokens(TILE), tokens(2 * TILE)],
        scratch_shapes=[pltpu.VMEM((step // 2, ff), F32), pltpu.VMEM((step // 2, ff), F32)],
        compiler_params=pltpu.CompilerParams(vmem_limit_bytes=60 * 1024 * 1024),
        cost_estimate=pl.CostEstimate(flops=60_000_000_000, bytes_accessed=60_000_000, transcendentals=0),
        name="mixture",
    )(pick, mix, packed, slot_row, slot_col, valid, gu, wd, fan, sd)


H = 16
QK_NOPE = 128
ROPE = 64
V_DIM = 128
KV_RANK = 512
GROUPS = 16
EPSILON = 1e-06
ROTARY_BASE = 10000.0


def product(left_side, right_side):
    return jnp.dot(left_side, right_side, preferred_element_type=F32)


def product_lead(left_side, right_side):
    return lax.dot_general(
        left_side, right_side, (((0,), (0,)), ((), ())), preferred_element_type=F32
    )


def product_trail(left_side, right_side):
    return lax.dot_general(
        left_side, right_side, (((1,), (1,)), ((), ())), preferred_element_type=F32
    )


def rotary_tables(positions):
    half_width = ROPE // 2
    frequency = ROTARY_BASE ** (-jnp.arange(half_width, dtype=F32) * 2.0 / ROPE)
    angles = positions[:, None] * frequency[None, :]
    return (jnp.cos(angles), jnp.sin(angles))


def rotate(values, cosine, sine_table):
    first_half, second_half = jnp.split(values, 2, axis=-1)
    return jnp.concatenate(
        [
            first_half * cosine - second_half * sine_table,
            second_half * cosine + first_half * sine_table,
        ],
        axis=-1,
    )


def norm_forward(values, gains):
    factor = lax.rsqrt(jnp.mean(values * values, axis=-1, keepdims=True) + EPSILON)
    normed = values * factor
    return (normed * gains, normed, factor)


def norm_backward(gradient, normed, factor, gains):
    gain_grad = jnp.sum(gradient * normed, axis=0)
    scaled = gradient * gains
    return (
        factor * (scaled - normed * jnp.mean(scaled * normed, axis=-1, keepdims=True)),
        gain_grad,
    )


def selected_experts(routes):
    chosen = routes[:, :, None] == jnp.arange(GROUPS, dtype=routes.dtype)
    return jnp.any(chosen, axis=1)


def masked_softmax(logits, mask):
    held = jnp.where(mask, logits, -1e30)
    peak = jnp.max(held, axis=-1, keepdims=True)
    raised = jnp.where(mask, jnp.exp(held - peak), 0.0)
    return raised / jnp.sum(raised, axis=-1, keepdims=True)


def per_device(
    layer_input,
    out_cotangent,
    lengths,
    routes,
    attn_gain,
    query_weight,
    latent_weight,
    latent_gain,
    expand_weight,
    output_weight,
    mixer_gain,
    router_weight,
    gate_weight,
    up_weight,
    down_weight,
    shared_gate,
    shared_up,
    shared_down,
):
    dp = lax.axis_size("dp")
    me = lax.axis_index("expert")
    plane = lax.axis_index("dp")
    batches, _, here, width = layer_input.shape
    own = batches * here
    total = own * GROUPS
    seq_total = here * GROUPS
    rows_w = query_weight.shape[0]
    rows_l = expand_weight.shape[0]
    scale_factor = float(QK_NOPE + ROPE) ** (-0.5)

    x_own = layer_input.reshape(own, width)
    latent_column = jnp.zeros((rows_w,), BF).at[:rows_l].set(latent_gain)
    small = jnp.concatenate(
        [
            latent_weight,
            router_weight,
            attn_gain[:, None],
            mixer_gain[:, None],
            latent_column[:, None],
            jnp.zeros((rows_w, 640 - 595), BF),
        ],
        axis=1,
    )
    query_parts = query_weight.reshape(rows_w, H, QK_NOPE + ROPE).transpose(1, 0, 2)
    expand_parts = expand_weight.reshape(rows_l, H, QK_NOPE + V_DIM).transpose(1, 0, 2)
    parts = jnp.concatenate([query_parts, expand_parts.reshape(H, rows_w, ROPE)], axis=2)
    x_all, small, parts_head, output_head = opening(dp, x_own, small, parts, output_weight, 1)
    x_all = x_all.reshape(total, width)
    small = small.reshape(GROUPS, dp, rows_w, 640).swapaxes(0, 1).reshape(width, 640)
    latent_full = small[:, :576]
    router_full = small[:, 576:592]
    gain_attn = small[:, 592].astype(F32)
    gain_mixer = small[:, 593].astype(F32)
    gain_latent = small[:, 594].reshape(dp * GROUPS, rows_w)[:, :rows_l].reshape(-1).astype(F32)
    query_head = parts_head[..., : QK_NOPE + ROPE].reshape(width, QK_NOPE + ROPE)
    expand_head = parts_head[..., QK_NOPE + ROPE :].reshape(KV_RANK, QK_NOPE + V_DIM)
    output_head = output_head.reshape(V_DIM, width)

    ff = gate_weight.shape[2]
    fan_own = jnp.stack(
        [gate_weight[0].reshape(-1, ff // 128, 128), up_weight[0].reshape(-1, ff // 128, 128)], axis=2
    ).reshape(-1, 2 * ff)
    share_own = jnp.concatenate([shared_gate.T, shared_up.T, shared_down], axis=0)
    share_width = shared_down.shape[0]
    fan_full = lax.all_gather(fan_own, "dp", axis=0, tiled=True)
    down_full = lax.all_gather(down_weight[0], "dp", axis=0, tiled=True)
    share_full = lax.all_gather(share_own, "dp", axis=0)
    share_full = share_full.transpose(1, 0, 2).reshape(3 * share_width, width)

    seq_lengths = lengths.reshape(batches)
    own_positions = me * here + jnp.arange(here, dtype=jnp.int32)
    valid_own = (own_positions[None, :] < seq_lengths[:, None]).reshape(own).astype(F32)
    all_positions = jnp.arange(seq_total, dtype=jnp.int32).reshape(GROUPS, 1, here)
    valid_all = jnp.broadcast_to(
        all_positions < seq_lengths[None, :, None], (GROUPS, batches, here)
    ).reshape(total)
    key_positions = jnp.arange(seq_total, dtype=jnp.int32)
    cosine, sine_table = rotary_tables(key_positions.astype(F32))
    cosine_own = lax.dynamic_slice_in_dim(cosine, me * here, here)
    sine_own = lax.dynamic_slice_in_dim(sine_table, me * here, here)

    def by_sequence(v):
        return v.reshape(GROUPS, batches, here, v.shape[-1]).swapaxes(0, 1).reshape(batches, seq_total, -1)

    def by_device(v):
        return v.reshape(batches, GROUPS, here, v.shape[-1]).swapaxes(0, 1).reshape(total, -1)

    grad_own = out_cotangent.reshape(own, width) * valid_own[:, None].astype(BF)
    routes_own = routes.reshape(own, -1)
    packed = jnp.concatenate(
        [grad_own, routes_own.astype(BF), jnp.zeros((own, 128 - routes_own.shape[1]), BF)], axis=1
    )
    packed = lax.all_gather(packed, "expert", axis=0, tiled=True)
    routes_all = packed[:, width : width + routes_own.shape[1]].astype(jnp.int32)
    taken = jnp.any(routes_all == me, axis=1) & valid_all
    places = jnp.cumsum(taken.reshape(-1, here).astype(jnp.int32), axis=1) - 1
    places = places + 32 * (jnp.arange(places.shape[0], dtype=jnp.int32) % 4)[:, None]
    slot = jnp.where(taken, places.reshape(total), -1)

    hidden_all = norm_forward(x_all.astype(F32), gain_attn)[0].astype(BF)
    raw = product(hidden_all, jnp.concatenate([query_head, latent_full], axis=1))
    raw = by_sequence(raw)
    query_nope = raw[..., :QK_NOPE].astype(BF)
    query_rope = rotate(raw[..., QK_NOPE : QK_NOPE + ROPE], cosine, sine_table).astype(BF)
    query = jnp.concatenate([query_nope, query_rope], axis=-1)
    latent_raw = raw[..., QK_NOPE + ROPE :]
    latent = norm_forward(latent_raw[..., :KV_RANK], gain_latent)[0].astype(BF)
    key_rope = rotate(latent_raw[..., KV_RANK:], cosine, sine_table).astype(BF)
    expanded = product(latent, expand_head).astype(BF)
    key = jnp.concatenate([expanded[..., :QK_NOPE], key_rope], axis=-1)
    values = expanded[..., QK_NOPE:]
    allowed = (key_positions[None, None, :] <= key_positions[None, :, None]) & (
        key_positions[None, None, :] < seq_lengths[:, None, None]
    )

    def score(query, key):
        raw_scores = jnp.einsum("btd,bsd->bts", query, key, preferred_element_type=F32)
        return jnp.where(allowed, raw_scores * scale_factor, -1e30)

    scores = score(query, key)
    peak = jnp.max(scores, axis=-1, keepdims=True)
    log_total = peak + jnp.log(jnp.sum(jnp.exp(scores - peak), axis=-1, keepdims=True))
    probs_low = jnp.exp(scores - log_total).astype(BF)
    attended = jnp.einsum("bts,bsd->btd", probs_low, values, preferred_element_type=F32).astype(BF)
    attended_rows = by_device(attended)
    attn_part = product(attended_rows, output_head).astype(BF).reshape(GROUPS, own, width)
    attn_out = scatter16(attn_part, 2)

    x_wide = x_own.astype(F32)
    middle = x_wide + attn_out
    normed_mix, unit_mix, factor_mix = norm_forward(middle, gain_mixer)
    hidden_mix = normed_mix.astype(BF)
    mix_all = gather16(hidden_mix, 3).reshape(total, width)

    pad = TILE - share_width
    fan_share = jnp.concatenate(
        [share_full[:share_width], router_full.T, jnp.zeros((pad - GROUPS, width), BF),
         share_full[share_width : 2 * share_width], jnp.zeros((pad, width), BF)], axis=0)
    down_share = jnp.concatenate([share_full[2 * share_width :], jnp.zeros((pad, width), BF)], axis=0)
    lane = jnp.arange(128)[None, :]
    pick = jnp.concatenate([lane == me, lane == me + GROUPS], axis=1).astype(F32)
    out_part, mix_part, rows, grad_result, hidden, grad_fan_in, share_hidden, grad_share_in = mixture(
        pick, mix_all, packed, slot[None, :], slot[:, None], valid_all.astype(F32)[:, None],
        fan_full, down_full, fan_share, down_share)
    grad_down = product_lead(hidden, grad_result).astype(BF)
    grad_fan = product_lead(rows, grad_fan_in).astype(BF)
    grad_share_fan = product_lead(grad_share_in, mix_all).astype(BF)
    grad_share_down = product_lead(share_hidden, packed[:, :width]).astype(BF)
    mix_part, grad_down, grad_fan = lax.optimization_barrier((mix_part, grad_down, grad_fan))
    mix_sum = scatter16(mix_part.reshape(GROUPS, own, width + 128), 5)
    mixed = scatter16(out_part.reshape(GROUPS, own, width), 4)
    layer_output = valid_own[:, None] * (middle + mixed)

    out_down = lax.psum_scatter(grad_down, "dp", scatter_dimension=0, tiled=True)
    out_fan = lax.psum_scatter(grad_fan, "dp", scatter_dimension=0, tiled=True)
    out_fan = out_fan.reshape(-1, ff // 128, 2, 128)
    grad_share = jnp.concatenate(
        [grad_share_fan[:share_width], grad_share_fan[TILE : TILE + share_width], grad_share_down[:share_width]],
        axis=0)
    grad_share = grad_share.reshape(3 * share_width, dp, width // dp).swapaxes(0, 1)
    out_share = lax.psum_scatter(grad_share, "dp", scatter_dimension=0, tiled=False).astype(F32)

    mask_own = selected_experts(routes_own)
    soft_own = masked_softmax(product(hidden_mix, router_full), mask_own)
    grad_masked = (mix_sum[:, width : width + GROUPS] + mix_sum[:, width + GROUPS : width + 2 * GROUPS])
    grad_masked = grad_masked * valid_own[:, None]
    grad_logits = soft_own * (grad_masked - jnp.sum(grad_masked * soft_own, axis=1, keepdims=True))
    grad_logits = grad_logits.astype(BF)
    grad_mix = mix_sum[:, :width] + product_trail(grad_logits, router_full)
    grad_middle_norm, grad_gain_mixer = norm_backward(grad_mix, unit_mix, factor_mix, gain_mixer)
    grad_middle = grad_own.astype(F32) + grad_middle_norm

    grad_attn_all = gather16(grad_middle.astype(BF), 6).reshape(total, width)
    grad_output = product_lead(attended_rows, grad_attn_all)
    grad_attended = by_sequence(product_trail(grad_attn_all, output_head).astype(BF))
    probs = jnp.exp(score(query, key) - log_total)
    probs_low = probs.astype(BF)
    grad_probs = jnp.einsum("btd,bsd->bts", grad_attended, values, preferred_element_type=F32)
    inner_sum = jnp.sum(grad_probs * probs, axis=-1, keepdims=True)
    grad_scores = (probs * (grad_probs - inner_sum)).astype(BF)
    grad_query = jnp.einsum("bts,bsd->btd", grad_scores, key, preferred_element_type=F32) * scale_factor
    grad_key = jnp.einsum("bts,btd->bsd", grad_scores, query, preferred_element_type=F32) * scale_factor
    grad_values = jnp.einsum("bts,btd->bsd", probs_low, grad_attended, preferred_element_type=F32)
    grad_expanded = jnp.concatenate([grad_key[..., :QK_NOPE], grad_values], axis=-1).astype(BF)
    grad_expanded = grad_expanded.reshape(total, -1)
    grad_expand = product_lead(latent.reshape(total, -1), grad_expanded)
    grad_latent = product_trail(grad_expanded, expand_head)
    grad_query = jnp.concatenate(
        [grad_query[..., :QK_NOPE], rotate(grad_query[..., QK_NOPE:], cosine, -sine_table)], axis=-1
    ).astype(BF)
    grad_query = by_device(grad_query)
    grad_query_w = product_lead(hidden_all, grad_query)
    back_part = product_trail(grad_query, query_head).astype(BF)
    latent_part = jnp.concatenate(
        [grad_latent.astype(BF).reshape(batches, seq_total, -1), grad_key[..., QK_NOPE:].astype(BF),
         jnp.zeros((batches, seq_total, 64), BF)], axis=-1)
    back_part = jnp.concatenate([back_part, by_device(latent_part)], axis=1)
    parts_grad = jnp.concatenate(
        [grad_query_w.astype(BF), grad_expand.astype(BF).reshape(width, ROPE)], axis=1)
    back_sum, out_parts, out_output = returning(
        dp, back_part.reshape(GROUPS, own, back_part.shape[1]),
        parts_grad.reshape(dp, GROUPS, rows_w, TILE), grad_output.astype(BF).reshape(dp, rows_w, width), 7)
    out_query = out_parts[..., : QK_NOPE + ROPE].transpose(1, 0, 2).reshape(rows_w, -1)
    out_expand = out_parts[..., QK_NOPE + ROPE :].reshape(H, rows_l, QK_NOPE + V_DIM)
    out_expand = out_expand.transpose(1, 0, 2).reshape(rows_l, -1)

    x_normed, unit_attn, factor_attn = norm_forward(x_wide, gain_attn)
    hidden_own = x_normed.astype(BF)
    latent_own = product(hidden_own, latent_full)
    _, unit_latent, factor_latent = norm_forward(latent_own[:, :KV_RANK], gain_latent)
    grad_latent_in, grad_gain_latent = norm_backward(
        back_sum[:, width : width + KV_RANK], unit_latent, factor_latent, gain_latent
    )
    grad_rope = back_sum[:, width + KV_RANK : width + KV_RANK + ROPE].reshape(batches, here, ROPE)
    grad_rope = rotate(grad_rope, cosine_own, -sine_own).reshape(own, ROPE)
    grad_latent_raw = jnp.concatenate([grad_latent_in, grad_rope], axis=1).astype(BF)
    grad_hidden_attn = back_sum[:, :width] + product_trail(grad_latent_raw, latent_full)
    grad_input_norm, grad_gain_attn = norm_backward(grad_hidden_attn, unit_attn, factor_attn, gain_attn)
    grad_input = grad_middle + grad_input_norm

    latent_rows = grad_gain_latent.reshape(dp * GROUPS, rows_l)
    latent_rows = jnp.pad(latent_rows, ((0, 0), (0, rows_w - rows_l))).reshape(width, 1)
    tokens_side = jnp.concatenate([hidden_own, hidden_mix], axis=0)
    grads_side = jnp.concatenate(
        [jnp.pad(grad_latent_raw, ((0, 0), (0, 64))), jnp.pad(grad_logits, ((0, 0), (576, 640 - 592)))], axis=0)
    lane = jnp.arange(640)[None, :]
    small_grad = product_lead(tokens_side, grads_side)
    small_grad = small_grad + jnp.where(lane == 592, grad_gain_attn[:, None], 0.0)
    small_grad = small_grad + jnp.where(lane == 593, grad_gain_mixer[:, None], 0.0)
    small_grad = (small_grad + jnp.where(lane == 594, latent_rows, 0.0)).astype(BF)
    small_grad = small_grad.reshape(dp, GROUPS, rows_w, 640).swapaxes(0, 1).reshape(GROUPS, dp * rows_w, 640)
    small_sum = closing(dp, small_grad, 9)

    def as_input(v):
        return v.reshape(batches, 1, here, width)

    return (
        as_input(layer_output),
        as_input(grad_input),
        small_sum[:, 592],
        out_query,
        small_sum[:, :576],
        small_sum[:rows_l, 594],
        out_expand,
        out_output,
        small_sum[:, 593],
        small_sum[:, 576:592],
        out_fan[:, :, 0].reshape(-1, ff).astype(F32)[None],
        out_fan[:, :, 1].reshape(-1, ff).astype(F32)[None],
        out_down.astype(F32)[None],
        out_share[:share_width].T,
        out_share[share_width : 2 * share_width].T,
        out_share[2 * share_width :],
    )


def solution(mesh):
    split = P(("dp", "expert"), None)
    line = P(("dp", "expert"))
    tokens = P(None, "dp", "expert", None)
    expert = P("expert", "dp", None)
    return jax.shard_map(
        per_device,
        mesh=mesh,
        in_specs=(
            tokens, tokens, P(None, "dp"), tokens, line, split, split, line, split, split, line, split,
            expert, expert, expert, P("dp", "expert"), P("dp", "expert"), P("expert", "dp"),
        ),
        out_specs=(
            tokens, tokens, line, split, split, line, split, split, line, split,
            expert, expert, expert, P("dp", "expert"), P("dp", "expert"), P("expert", "dp"),
        ),
        check_vma=False,
    )
```

```python
import functools
import jax
import jax.numpy as jnp
from jax import lax
from jax.experimental import pallas as pl
from jax.experimental.pallas import tpu as pltpu
from jax.sharding import PartitionSpec as P

MESH = pl.DeviceIdType.MESH
NZ = 4
NE = 16


def place():
    me = lax.axis_index("expert")
    z = me // 4
    x = (me // 2) % 2
    c = me % 2
    return me, z, x, c, me + 1 - 2 * c, me + 2 - 4 * x


def enter(me, z, core, side):
    barrier = pltpu.get_barrier_semaphore()
    for other in (core, side):
        pl.semaphore_signal(barrier, inc=1, device_id={"expert": other}, device_id_type=MESH)

    @pl.when(z < NZ - 1)
    def _():
        pl.semaphore_signal(barrier, inc=1, device_id={"expert": me + 4}, device_id_type=MESH)

    @pl.when(z > 0)
    def _():
        pl.semaphore_signal(barrier, inc=1, device_id={"expert": me - 4}, device_id_type=MESH)

    pl.semaphore_wait(barrier, 2 + (z < NZ - 1).astype(jnp.int32) + (z > 0).astype(jnp.int32))


def enter_all(me, plane, dp):
    barrier = pltpu.get_barrier_semaphore()
    for r in range(1, NE):
        pl.semaphore_signal(
            barrier, inc=1, device_id={"expert": (me + r) % NE}, device_id_type=MESH)
    for r in range(1, dp):
        pl.semaphore_signal(
            barrier, inc=1, device_id={"dp": (plane + r) % dp}, device_id_type=MESH)
    pl.semaphore_wait(barrier, NE - 1 + dp - 1)


class Gather:
    def __init__(self, src, out, chunks, sems, view=lambda ref, b: ref.at[b]):
        self.src, self.out, self.chunks, self.view = src, out, chunks, view
        self.rows = src.shape[0] // chunks
        self.own_sem, self.us, self.ur, self.ds, self.dr, self.xs, self.xr, self.cs, self.cr = sems
        self.me, self.z, self.x, self.c, self.core, self.side = place()

    @staticmethod
    def scratch(chunks):
        dma = pltpu.SemaphoreType.DMA
        return [dma] + [dma((4, chunks))] * 4 + [dma((7, chunks))] * 2 + [dma((14, chunks))] * 2

    def copy(self, block, k, src, send, recv, to):
        src_ref = self.src if src is None else self.view(self.out, src)
        dst_ref = self.view(self.out, block)
        if self.chunks > 1:
            part = pl.ds(k * self.rows, self.rows)
            src_ref, dst_ref = src_ref.at[part], dst_ref.at[part]
        return pltpu.make_async_remote_copy(
            src_ref=src_ref,
            dst_ref=dst_ref,
            send_sem=send, recv_sem=recv,
            device_id={"expert": to}, device_id_type=MESH,
        )

    def up(self, k, s, src=None):
        return self.copy(self.me - 4 * s, k, src, self.us.at[s, k], self.ur.at[s, k], self.me + 4)

    def down(self, k, s, src=None):
        return self.copy(self.me + 4 * s, k, src, self.ds.at[s, k], self.dr.at[s, k], self.me - 4)

    def across(self, k, slot, block, src=None):
        return self.copy(block, k, src, self.xs.at[slot, k], self.xr.at[slot, k], self.side)

    def over(self, k, slot, block, src=None):
        return self.copy(block, k, src, self.cs.at[slot, k], self.cr.at[slot, k], self.core)

    def up_in(self, k, s):
        b = self.me - 4 * s
        return self.copy(b, k, b, self.us.at[s - 1, k], self.ur.at[s - 1, k], self.side)

    def dn_in(self, k, s):
        b = self.me + 4 * s
        return self.copy(b, k, b, self.ds.at[s - 1, k], self.dr.at[s - 1, k], self.side)

    def shift(self, base, slot):
        return base - 4 * slot if slot <= 3 else base + 4 * (slot - 3)

    def core_block(self, slot):
        if slot < 7:
            return self.shift(self.core, slot)
        return self.shift(self.core + 2 - 4 * self.x, slot - 7)

    def has(self, slot):
        slot = slot % 7
        if slot == 0:
            return self.z >= 0
        return self.z >= slot if slot <= 3 else self.z + (slot - 3) <= NZ - 1

    def start(self):
        z, me = self.z, self.me
        self.own = pltpu.make_async_copy(self.src, self.view(self.out, me), self.own_sem)
        self.own.start()
        for k in range(self.chunks):
            self.across(k, 0, me).start()

            @pl.when(z < NZ - 1)
            def _():
                self.up(k, 0).start()

            @pl.when(z > 0)
            def _():
                self.down(k, 0).start()

            self.over(k, 0, me).start()

    def line(self, k, s):
        z, me = self.z, self.me

        @pl.when(z >= s)
        def _():
            b = me - 4 * s
            self.up_in(k, s).wait_recv()
            self.across(k, s, b, b).start()

            @pl.when(z < NZ - 1)
            def _():
                self.up(k, s, b).start()

            self.over(k, s, b, b).start()

        @pl.when(z + s <= NZ - 1)
        def _():
            b = me + 4 * s
            self.dn_in(k, s).wait_recv()
            self.across(k, 3 + s, b, b).start()

            @pl.when(z > 0)
            def _():
                self.down(k, s, b).start()

            self.over(k, 3 + s, b, b).start()

    def from_side(self, k, slot):
        @pl.when(self.has(slot))
        def _():
            b = self.shift(self.side, slot)
            self.across(k, slot, b, b).wait_recv()
            self.over(k, 7 + slot, b, b).start()

    def round(self, s):
        if s < NZ:
            for k in range(self.chunks):
                self.line(k, s)
        for k in range(self.chunks):
            for slot in ((0,) if s == 1 else (s - 1, s + 2)):
                self.from_side(k, slot)

    def finish(self):
        z = self.z
        self.own.wait()
        for k in range(self.chunks):
            for slot in range(14):
                @pl.when(self.has(slot))
                def _():
                    b = self.core_block(slot)
                    self.over(k, slot, b, b).wait_recv()
                    self.over(k, slot, b, b).wait_send()
            for slot in range(7):
                @pl.when(self.has(slot))
                def _():
                    self.across(k, slot, self.me).wait_send()
            for s in range(NZ - 1):
                @pl.when((z >= s) & (z < NZ - 1))
                def _():
                    self.up(k, s).wait_send()

                @pl.when((z + s <= NZ - 1) & (z > 0))
                def _():
                    self.down(k, s).wait_send()


def gather_kernel(chunks, x_ref, o_ref, *sems):
    g = Gather(x_ref, o_ref, chunks, sems)
    enter(g.me, g.z, g.core, g.side)
    g.start()
    for s in range(1, NZ + 1):
        g.round(s)
    g.finish()


COST = pl.CostEstimate(flops=0, bytes_accessed=4_000_000, transcendentals=0)
ANY = pl.BlockSpec(memory_space=pl.ANY)


def gather16(v, cid, chunks=4):
    rows, width = v.shape
    return pl.pallas_call(
        functools.partial(gather_kernel, chunks),
        out_shape=jax.ShapeDtypeStruct((NE, rows, width), v.dtype),
        in_specs=[ANY],
        out_specs=ANY,
        scratch_shapes=Gather.scratch(chunks),
        compiler_params=pltpu.CompilerParams(collective_id=cid, has_side_effects=True),
        cost_estimate=COST,
        name="gather16",
    )(v)


def opening_kernel(dp, chunks, x_ref, small_ref, parts_ref, out_ref,
                   x_all, small_all, parts_head, out_head, small_dp, parts_dp, out_dp, *sems):
    ng = 9
    gx = Gather(x_ref, x_all, chunks, sems[:ng])
    gs = Gather(small_dp, small_all, 1, sems[ng:2 * ng], lambda ref, b: ref.at[:, b])
    loc, ys, yr, ps, pr, os_, or_, pl_sem, ol_sem = sems[2 * ng:]
    me = gx.me
    plane = lax.axis_index("dp")
    enter_all(me, plane, dp)
    pairs = ((small_ref, small_dp.at[plane]), (parts_ref, parts_dp.at[plane]),
             (out_ref, out_dp.at[plane]))

    def lift(i, r):
        src, dst = pairs[i]
        return pltpu.make_async_remote_copy(
            src_ref=src, dst_ref=dst, send_sem=ys.at[i, r], recv_sem=yr.at[i, r],
            device_id={"dp": (plane + r) % dp}, device_id_type=MESH)

    def landed(i, r):
        p = (plane - r + dp) % dp
        dst = (small_dp.at[p], parts_dp.at[p], out_dp.at[p])[i]
        return pltpu.make_async_remote_copy(
            src_ref=dst, dst_ref=dst, send_sem=ys.at[i, r], recv_sem=yr.at[i, r],
            device_id={"dp": p}, device_id_type=MESH)

    def kept(i):
        src, dst = pairs[i]
        return pltpu.make_async_copy(src, dst, loc.at[i])

    for i in range(3):
        for r in range(1, dp):
            lift(i, r).start()
        kept(i).start()
    gx.start()
    gx.round(1)

    kept(0).wait()
    for r in range(1, dp):
        landed(0, r).wait_recv()
    gs.start()

    def part(r):
        h = (me + r) % NE
        return pltpu.make_async_remote_copy(
            src_ref=parts_dp.at[:, h], dst_ref=parts_head.at[:, me],
            send_sem=ps.at[r], recv_sem=pr.at[r],
            device_id={"expert": h}, device_id_type=MESH)

    def part_in(r):
        e = (me - r + NE) % NE
        return pltpu.make_async_remote_copy(
            src_ref=parts_head.at[:, e], dst_ref=parts_head.at[:, e],
            send_sem=ps.at[r], recv_sem=pr.at[r],
            device_id={"expert": e}, device_id_type=MESH)

    def part_kept():
        return pltpu.make_async_copy(parts_dp.at[:, me], parts_head.at[:, me], pl_sem)

    kept(1).wait()
    for r in range(1, dp):
        landed(1, r).wait_recv()
    for r in range(1, NE):
        part(r).start()
    part_kept().start()
    gx.round(2)

    def row(d):
        b = NE * d + me
        return pltpu.make_async_remote_copy(
            src_ref=out_dp.at[d], dst_ref=out_head.at[b % dp],
            send_sem=os_.at[d], recv_sem=or_.at[b % dp],
            device_id={"expert": b // dp}, device_id_type=MESH)

    def row_kept(d):
        b = NE * d + me
        return pltpu.make_async_copy(out_dp.at[d], out_head.at[b % dp], ol_sem.at[d])

    kept(2).wait()
    for r in range(1, dp):
        landed(2, r).wait_recv()
    for d in range(dp):
        home = (NE * d + me) // dp

        @pl.when(home != me)
        def _():
            row(d).start()

        @pl.when(home == me)
        def _():
            row_kept(d).start()

    gs.round(1)
    gx.round(3)
    gs.round(2)
    gx.round(4)
    gs.round(3)
    gs.round(4)

    def row_in(j):
        return pltpu.make_async_remote_copy(
            src_ref=out_head.at[j], dst_ref=out_head.at[j], send_sem=os_.at[j], recv_sem=or_.at[j],
            device_id={"expert": gx.core}, device_id_type=MESH)

    for r in range(1, NE):
        part_in(r).wait_recv()
        part(r).wait_send()
    part_kept().wait()
    for j in range(dp):
        @pl.when((dp * me + j) % NE != me)
        def _():
            row_in(j).wait_recv()
    for d in range(dp):
        home = (NE * d + me) // dp

        @pl.when(home != me)
        def _():
            row(d).wait_send()

        @pl.when(home == me)
        def _():
            row_kept(d).wait()
    for i in range(3):
        for r in range(1, dp):
            lift(i, r).wait_send()
    gx.finish()
    gs.finish()


def opening(dp, x, small, parts, out, cid, chunks=4):
    dma = pltpu.SemaphoreType.DMA
    rows, ws = small.shape
    bf = x.dtype
    wo = out.shape[1]
    shape = jax.ShapeDtypeStruct
    res = pl.pallas_call(
        functools.partial(opening_kernel, dp, chunks),
        out_shape=(
            shape((NE,) + x.shape, bf), shape((dp, NE, rows, ws), bf), shape((dp, NE) + parts.shape[1:], bf),
            shape((dp, rows, wo), bf),
            shape((dp, rows, ws), bf), shape((dp,) + parts.shape, bf), shape((dp, rows, wo), bf),
        ),
        in_specs=[ANY] * 4,
        out_specs=[ANY] * 7,
        scratch_shapes=Gather.scratch(chunks) + Gather.scratch(1) + [
            dma((3,)), dma((3, dp)), dma((3, dp)), dma((NE,)), dma((NE,)), dma((dp,)), dma((dp,)), dma, dma((dp,))],
        compiler_params=pltpu.CompilerParams(collective_id=cid, has_side_effects=True),
        cost_estimate=COST,
        name="opening",
    )(x, small, parts, out)
    return res[:4]


def order(z, i):
    a, b = (3, 2, 1, 0)[i], (3, 2, 0, 1)[i]
    return jnp.where(z == 0, a, jnp.where(z == 1, b, jnp.where(z == 2, 3 - b, 3 - a)))


class Scatter:
    def __init__(self, p_ref, o_ref, chunks, scratch):
        self.p, self.o, self.chunks = p_ref, o_ref, chunks
        (self.cbuf, self.own, self.xbuf, self.ubuf, self.dbuf, self.ld, self.cs, self.cr, self.xs, self.xr,
         self.us, self.ur, self.ds, self.dr) = scratch
        self.rows = o_ref.shape[0] // chunks
        self.me, self.z, self.x, self.c, self.core, self.side = place()

    @staticmethod
    def scratch(rows, width, chunks, bf):
        dma = pltpu.SemaphoreType.DMA
        return [pltpu.VMEM((n, rows, width), bf) for n in (8, 8, 4, 4, 4)] + [
            dma((8,)), dma((8, chunks)), dma((8, chunks))] + [dma((4, chunks))] * 6

    def rng(self, k):
        return pl.ds(k * self.rows, self.rows)

    def column(self, i, j):
        return 4 * order(self.z, i) + 2 * jnp.where(j == 0, 1 - self.x, self.x)

    def remote(self, src, dst, send, recv, to):
        return pltpu.make_async_remote_copy(
            src_ref=src, dst_ref=dst, send_sem=send, recv_sem=recv,
            device_id={"expert": to}, device_id_type=MESH)

    def over(self, i, j, k):
        n = 2 * i + j
        return self.remote(
            self.p.at[self.column(i, j) + 1 - self.c, self.rng(k)], self.cbuf.at[n, self.rng(k)],
            self.cs.at[n, k], self.cr.at[n, k], self.core)

    def load(self, i, j):
        n = 2 * i + j
        return pltpu.make_async_copy(self.p.at[self.column(i, j) + self.c], self.own.at[n], self.ld.at[n])

    def across(self, i, k):
        return self.remote(self.own.at[2 * i, self.rng(k)], self.xbuf.at[i, self.rng(k)],
                           self.xs.at[i, k], self.xr.at[i, k], self.side)

    def up(self, t, i, k):
        return self.remote(self.own.at[2 * i + 1, self.rng(k)], self.ubuf.at[t, self.rng(k)],
                           self.us.at[t, k], self.ur.at[t, k], self.me + 4)

    def down(self, t, i, k):
        return self.remote(self.own.at[2 * i + 1, self.rng(k)], self.dbuf.at[t, self.rng(k)],
                           self.ds.at[t, k], self.dr.at[t, k], self.me - 4)

    def start(self):
        for i in range(NZ):
            for j in range(2):
                self.load(i, j).start()
                for k in range(self.chunks):
                    self.over(i, j, k).start()

    def first(self, i):
        f32 = jnp.float32
        self.load(i, 0).wait()
        for k in range(self.chunks):
            self.over(i, 0, k).wait_recv()
            s = self.rng(k)
            self.own[2 * i, s] = (
                self.own[2 * i, s].astype(f32) + self.cbuf[2 * i, s].astype(f32)).astype(self.own.dtype)
            self.across(i, k).start()

    def second(self, i):
        f32 = jnp.float32
        z, own, o = self.z, self.own, self.o
        t = order(z, i)
        self.load(i, 1).wait()
        for k in range(self.chunks):
            s = self.rng(k)
            self.over(i, 1, k).wait_recv()
            self.across(i, k).wait_recv()

            def base():
                return (own[2 * i + 1, s].astype(f32) + self.cbuf[2 * i + 1, s].astype(f32)
                        + self.xbuf[i, s].astype(f32))

            if i < NZ - 1:
                @pl.when(t > z)
                def _():
                    @pl.when(z > 0)
                    def _():
                        self.up(t, i, k).wait_recv()
                        own[2 * i + 1, s] = (base() + self.ubuf[t, s].astype(f32)).astype(own.dtype)

                    @pl.when(z == 0)
                    def _():
                        own[2 * i + 1, s] = base().astype(own.dtype)

                    self.up(t, i, k).start()

                @pl.when(t < z)
                def _():
                    @pl.when(z < NZ - 1)
                    def _():
                        self.down(t, i, k).wait_recv()
                        own[2 * i + 1, s] = (base() + self.dbuf[t, s].astype(f32)).astype(own.dtype)

                    @pl.when(z == NZ - 1)
                    def _():
                        own[2 * i + 1, s] = base().astype(own.dtype)

                    self.down(t, i, k).start()
            else:
                @pl.when(z > 0)
                def _():
                    self.up(t, i, k).wait_recv()

                @pl.when(z < NZ - 1)
                def _():
                    self.down(t, i, k).wait_recv()

                @pl.when((z > 0) & (z < NZ - 1))
                def _():
                    o[s] = (base() + self.ubuf[t, s].astype(f32) + self.dbuf[t, s].astype(f32)).astype(o.dtype)

                @pl.when(z == 0)
                def _():
                    o[s] = (base() + self.dbuf[t, s].astype(f32)).astype(o.dtype)

                @pl.when(z == NZ - 1)
                def _():
                    o[s] = (base() + self.ubuf[t, s].astype(f32)).astype(o.dtype)

    def run(self):
        self.first(0)
        for i in range(NZ):
            if i + 1 < NZ:
                self.first(i + 1)
            self.second(i)

    def finish(self):
        z = self.z
        for k in range(self.chunks):
            for i in range(NZ):
                self.across(i, k).wait_send()
                for j in range(2):
                    self.over(i, j, k).wait_send()
                if i < NZ - 1:
                    t = order(z, i)

                    @pl.when(t > z)
                    def _():
                        self.up(t, i, k).wait_send()

                    @pl.when(t < z)
                    def _():
                        self.down(t, i, k).wait_send()


def scatter_kernel(chunks, p_ref, o_ref, *scratch):
    s = Scatter(p_ref, o_ref, chunks, scratch)
    enter(s.me, s.z, s.core, s.side)
    s.start()
    s.run()
    s.finish()


VMEM = pl.BlockSpec(memory_space=pltpu.VMEM)


def scatter16(p, cid, chunks=2, out_dtype=jnp.float32):
    _, rows, width = p.shape
    return pl.pallas_call(
        functools.partial(scatter_kernel, chunks),
        out_shape=jax.ShapeDtypeStruct((rows, width), out_dtype),
        in_specs=[ANY],
        out_specs=VMEM,
        scratch_shapes=Scatter.scratch(rows, width, chunks, p.dtype),
        compiler_params=pltpu.CompilerParams(
            collective_id=cid, has_side_effects=True, vmem_limit_bytes=32 * 1024 * 1024),
        cost_estimate=COST,
        name="scatter16",
    )(p)


def return_kernel(dp, chunks, p_ref, parts_ref, rows_ref, o_ref, parts_in, rows_in, parts_far, rows_far, *scratch):
    ns = 14
    s = Scatter(p_ref, o_ref, chunks, scratch[:ns])
    ps, pr, os_, or_, pl_sem, ol_sem, ys, yr = scratch[ns:]
    me = s.me
    plane = lax.axis_index("dp")
    enter_all(me, plane, dp)

    def part(r):
        e = (me + r) % NE
        return pltpu.make_async_remote_copy(
            src_ref=parts_ref.at[:, e], dst_ref=parts_in.at[:, me],
            send_sem=ps.at[r], recv_sem=pr.at[r],
            device_id={"expert": e}, device_id_type=MESH)

    def part_in(r):
        h = (me - r + NE) % NE
        return pltpu.make_async_remote_copy(
            src_ref=parts_in.at[:, h], dst_ref=parts_in.at[:, h],
            send_sem=ps.at[r], recv_sem=pr.at[r],
            device_id={"expert": h}, device_id_type=MESH)

    def part_kept():
        return pltpu.make_async_copy(parts_ref.at[:, me], parts_in.at[:, me], pl_sem)

    def row(j):
        b = dp * me + j
        return pltpu.make_async_remote_copy(
            src_ref=rows_ref.at[j], dst_ref=rows_in.at[b // NE],
            send_sem=os_.at[j], recv_sem=or_.at[b // NE],
            device_id={"expert": b % NE}, device_id_type=MESH)

    def row_kept(j):
        b = dp * me + j
        return pltpu.make_async_copy(rows_ref.at[j], rows_in.at[b // NE], ol_sem.at[j])

    def row_in(d):
        return pltpu.make_async_remote_copy(
            src_ref=rows_in.at[d], dst_ref=rows_in.at[d], send_sem=os_.at[d], recv_sem=or_.at[d],
            device_id={"expert": s.core}, device_id_type=MESH)

    def lift(i, r):
        to = (plane + r) % dp
        src, dst = ((parts_in.at[to], parts_far.at[r - 1]), (rows_in.at[to], rows_far.at[r - 1]))[i]
        return pltpu.make_async_remote_copy(
            src_ref=src, dst_ref=dst, send_sem=ys.at[i, r], recv_sem=yr.at[i, r],
            device_id={"dp": to}, device_id_type=MESH)

    s.start()
    for r in range(1, NE):
        part(r).start()
    part_kept().start()
    for j in range(dp):
        @pl.when((dp * me + j) % NE != me)
        def _():
            row(j).start()

        @pl.when((dp * me + j) % NE == me)
        def _():
            row_kept(j).start()
    s.first(0)
    s.first(1)
    s.second(0)
    for r in range(1, NE):
        part_in(r).wait_recv()
    part_kept().wait()
    for j in range(dp):
        @pl.when((dp * me + j) % NE == me)
        def _():
            row_kept(j).wait()
    for d in range(dp):
        @pl.when((NE * d + me) // dp != me)
        def _():
            row_in(d).wait_recv()
    for i in range(2):
        for r in range(1, dp):
            lift(i, r).start()
    s.first(2)
    s.second(1)
    s.first(3)
    s.second(2)
    s.second(3)
    for i in range(2):
        for r in range(1, dp):
            lift(i, r).wait_recv()
            lift(i, r).wait_send()
    for r in range(1, NE):
        part(r).wait_send()
    for j in range(dp):
        @pl.when((dp * me + j) % NE != me)
        def _():
            row(j).wait_send()
    s.finish()


def returning(dp, p, parts, rows, cid, chunks=2):
    dma = pltpu.SemaphoreType.DMA
    _, n, width = p.shape
    shape = jax.ShapeDtypeStruct
    out, parts_in, rows_in, parts_far, rows_far = pl.pallas_call(
        functools.partial(return_kernel, dp, chunks),
        out_shape=(
            shape((n, width), jnp.float32), shape(parts.shape, parts.dtype), shape(rows.shape, rows.dtype),
            shape((dp - 1,) + parts.shape[1:], parts.dtype), shape((dp - 1,) + rows.shape[1:], rows.dtype)),
        in_specs=[ANY] * 3,
        out_specs=[VMEM] + [ANY] * 4,
        scratch_shapes=Scatter.scratch(n, width, chunks, p.dtype) + [
            dma((NE,)), dma((NE,)), dma((dp,)), dma((dp,)), dma, dma((dp,)), dma((2, dp)), dma((2, dp))],
        compiler_params=pltpu.CompilerParams(
            collective_id=cid, has_side_effects=True, vmem_limit_bytes=48 * 1024 * 1024),
        cost_estimate=COST,
        name="returning",
    )(p, parts, rows)
    plane = lax.axis_index("dp")

    def total(near, far):
        own = lax.dynamic_index_in_dim(near, plane, 0, False).astype(jnp.float32)
        return own + jnp.sum(far.astype(jnp.float32), axis=0)

    return out, total(parts_in, parts_far), total(rows_in, rows_far)


def closing_kernel(dp, chunks, p_ref, o_ref, far_ref, *scratch):
    ns = 14
    s = Scatter(p_ref, o_ref, chunks, scratch[:ns])
    ys, yr = scratch[ns:]
    plane = lax.axis_index("dp")
    rows = o_ref.shape[0] // dp
    barrier = pltpu.get_barrier_semaphore()
    for r in range(1, dp):
        pl.semaphore_signal(barrier, inc=1, device_id={"dp": (plane + r) % dp}, device_id_type=MESH)
    z = s.z
    for other in (s.core, s.side):
        pl.semaphore_signal(barrier, inc=1, device_id={"expert": other}, device_id_type=MESH)

    @pl.when(z < NZ - 1)
    def _():
        pl.semaphore_signal(barrier, inc=1, device_id={"expert": s.me + 4}, device_id_type=MESH)

    @pl.when(z > 0)
    def _():
        pl.semaphore_signal(barrier, inc=1, device_id={"expert": s.me - 4}, device_id_type=MESH)

    pl.semaphore_wait(barrier, dp + 1 + (z < NZ - 1).astype(jnp.int32) + (z > 0).astype(jnp.int32))

    def lift(r):
        to = (plane + r) % dp
        return pltpu.make_async_remote_copy(
            src_ref=o_ref.at[pl.ds(pl.multiple_of(to * rows, 16), rows)], dst_ref=far_ref.at[r - 1],
            send_sem=ys.at[r], recv_sem=yr.at[r],
            device_id={"dp": to}, device_id_type=MESH)

    s.start()
    s.run()
    for r in range(1, dp):
        lift(r).start()
    s.finish()
    for r in range(1, dp):
        lift(r).wait_recv()
        lift(r).wait_send()


def closing(dp, p, cid):
    dma = pltpu.SemaphoreType.DMA
    _, n, width = p.shape
    shape = jax.ShapeDtypeStruct
    near, far = pl.pallas_call(
        functools.partial(closing_kernel, dp, 1),
        out_shape=(shape((n, width), p.dtype), shape((dp - 1, n // dp, width), p.dtype)),
        in_specs=[ANY],
        out_specs=[VMEM, VMEM],
        scratch_shapes=Scatter.scratch(n, width, 1, p.dtype) + [dma((dp,)), dma((dp,))],
        compiler_params=pltpu.CompilerParams(
            collective_id=cid, has_side_effects=True, vmem_limit_bytes=32 * 1024 * 1024),
        cost_estimate=COST,
        name="closing",
    )(p)
    own = lax.dynamic_slice_in_dim(near, lax.axis_index("dp") * (n // dp), n // dp).astype(jnp.float32)
    return own + jnp.sum(far.astype(jnp.float32), axis=0)
BF = jnp.bfloat16
F32 = jnp.float32


def mm(a, b):
    return jnp.dot(a, b, preferred_element_type=F32)


def mm_t(a, b):
    return lax.dot_general(a, b, (((1,), (1,)), ((), ())), preferred_element_type=F32)


def silu_pair(gate_in):
    sigmoid = 1.0 / (1.0 + jnp.exp(-gate_in))
    return (gate_in * sigmoid, sigmoid * (1.0 + gate_in * (1.0 - sigmoid)))


TILE = 256
WIDE = 512
SHARE = 176


def mixture_kernel(pick_ref, mix_ref, dy_ref, slot_row, slot_col, valid_ref, wg_ref, wu_ref, wd_ref, fan_ref, sd_ref,
                   out_ref, dh_ref, rows_ref, deo_ref, hid_ref, dg_ref, du_ref, sh_ref, ds_ref,
                   act_buf, slo_buf):
    tokens, width = mix_ref.shape
    groups = tokens // 256
    slots = 128
    ff = hid_ref.shape[1]

    def lanes(j):
        return pl.ds(pl.multiple_of(j * WIDE, WIDE), WIDE)

    mix = mix_ref[...]
    fanned = mm_t(mix, fan_ref[:TILE, :])
    s_up = mm_t(mix, fan_ref[TILE:, :])
    s_act, s_slope = silu_pair(fanned)
    s_hidden = (s_act * s_up).astype(BF)
    sh_ref[...] = s_hidden
    logits = fanned[:, SHARE:SHARE + 16]
    lane16 = lax.broadcasted_iota(jnp.int32, (tokens, 16), 1).astype(F32)
    routes = dy_ref[:, width:width + 16].astype(F32)
    mask = lane16 < 0
    for k in range(6):
        mask = mask | (lane16 == routes[:, k:k + 1])
    held = jnp.where(mask, logits, -1e30)
    raised = jnp.where(mask, jnp.exp(held - jnp.max(held, axis=1, keepdims=True)), 0.0)
    soft = raised / jnp.sum(raised, axis=1, keepdims=True)
    gate = jnp.sum(soft * pick_ref[:, :16], axis=1, keepdims=True) * valid_ref[...]
    dy = dy_ref[:, :width]
    d_sh = mm_t(dy, sd_ref[...])
    ds_ref[:, :TILE] = (d_sh * s_up * s_slope).astype(BF)
    ds_ref[:, TILE:] = (d_sh * s_act).astype(BF)

    to_slot, to_token = [], []
    for g in range(groups):
        row = slot_row[:, g * 256:(g + 1) * 256]
        col = slot_col[g * 256:(g + 1) * 256, :]
        to_slot.append((lax.broadcasted_iota(jnp.int32, (slots, 256), 0) == row).astype(BF))
        to_token.append((lax.broadcasted_iota(jnp.int32, (256, slots), 1) == col).astype(BF))

    def dispatch(j, _):
        for g in range(groups):
            t = pl.ds(g * 256, 256)
            s = pl.ds(g * slots, slots)
            rows_ref[s, lanes(j)] = mm(to_slot[g], mix_ref[t, lanes(j)]).astype(BF)
            gated = (gate[g * 256:(g + 1) * 256] * dy_ref[t, lanes(j)].astype(F32)).astype(BF)
            deo_ref[s, lanes(j)] = mm(to_slot[g], gated).astype(BF)
        return 0

    lax.fori_loop(0, width // WIDE, dispatch, 0)

    def fan_in(start, size):
        cols = pl.ds(start, size)
        gate_in = mm(rows_ref[...], wg_ref[:, cols])
        up_in = mm(rows_ref[...], wu_ref[:, cols])
        act, slope = silu_pair(gate_in)
        hid_ref[:, cols] = (act * up_in).astype(BF)
        act_buf[:, cols] = act
        slo_buf[:, cols] = up_in * slope

    def fan_loop(j, _):
        fan_in(pl.multiple_of(j * WIDE, WIDE), WIDE)
        return 0

    lax.fori_loop(0, ff // WIDE, fan_loop, 0)
    if ff % WIDE:
        fan_in(ff // WIDE * WIDE, ff % WIDE)

    def fan_out(j, d_gates):
        eo = mm(hid_ref[...], wd_ref[:, lanes(j)]).astype(BF)
        shared = mm(s_hidden, sd_ref[:, lanes(j)])
        picked = jnp.concatenate(
            [mm(to_token[g], eo[g * slots:(g + 1) * slots]) for g in range(groups)], axis=0)
        out_ref[:, lanes(j)] = (shared + gate * picked).astype(BF)
        return d_gates + jnp.sum(dy_ref[:, lanes(j)].astype(F32) * picked, axis=1, keepdims=True)

    d_gates = lax.fori_loop(0, width // WIDE, fan_out, jnp.zeros((tokens, 1), F32))

    def back_out(start, size):
        cols = pl.ds(start, size)
        d_eh = mm_t(deo_ref[...], wd_ref[cols, :])
        dg_ref[:, cols] = (d_eh * slo_buf[:, cols]).astype(BF)
        du_ref[:, cols] = (d_eh * act_buf[:, cols]).astype(BF)

    def back_loop(j, _):
        back_out(pl.multiple_of(j * WIDE, WIDE), WIDE)
        return 0

    lax.fori_loop(0, ff // WIDE, back_loop, 0)
    if ff % WIDE:
        back_out(ff // WIDE * WIDE, ff % WIDE)

    d_s = ds_ref[...]

    def back_in(j, _):
        d_rows = (mm_t(dg_ref[...], wg_ref[lanes(j), :]) + mm_t(du_ref[...], wu_ref[lanes(j), :])).astype(BF)
        shared = mm(d_s, fan_ref[:, lanes(j)])
        taken = jnp.concatenate(
            [mm(to_token[g], d_rows[g * slots:(g + 1) * slots]) for g in range(groups)], axis=0)
        dh_ref[:, lanes(j)] = (shared + taken).astype(BF)
        return 0

    lax.fori_loop(0, width // WIDE, back_in, 0)
    high = d_gates.astype(BF).astype(F32)
    tail = high * pick_ref[:, :128] + (d_gates - high) * pick_ref[:, 128:]
    dh_ref[:, width:] = tail.astype(BF)


def mixture(pick, mix, packed, slot_row, slot_col, valid, wg, wu, wd, fan, sd, step=512):
    total, width = mix.shape
    steps = total // step
    ff = wd.shape[0]
    rows = total // 2
    shape = jax.ShapeDtypeStruct
    once = pl.Buffered(buffer_count=1)

    def whole(v):
        return pl.BlockSpec(v.shape, lambda i: (0, 0), pipeline_mode=once)

    def tokens(w):
        return pl.BlockSpec((step, w), lambda i: (i, 0))

    def slots(w):
        return pl.BlockSpec((step // 2, w), lambda i: (i, 0))

    return pl.pallas_call(
        mixture_kernel,
        grid=(steps,),
        out_shape=(
            shape((total, width), BF), shape((total, width + 128), BF), shape((rows, width), BF),
            shape((rows, width), BF), shape((rows, ff), BF), shape((rows, ff), BF), shape((rows, ff), BF),
            shape((total, TILE), BF), shape((total, 2 * TILE), BF)),
        in_specs=[whole(pick), tokens(width), tokens(width + 128), pl.BlockSpec((1, step), lambda i: (0, i)),
                  tokens(1), tokens(1), whole(wg), whole(wu), whole(wd), whole(fan), whole(sd)],
        out_specs=[tokens(width), tokens(width + 128), slots(width), slots(width), slots(ff), slots(ff), slots(ff),
                   tokens(TILE), tokens(2 * TILE)],
        scratch_shapes=[pltpu.VMEM((step // 2, ff), F32), pltpu.VMEM((step // 2, ff), F32)],
        compiler_params=pltpu.CompilerParams(vmem_limit_bytes=60 * 1024 * 1024),
        cost_estimate=pl.CostEstimate(flops=60_000_000_000, bytes_accessed=60_000_000, transcendentals=0),
        name="mixture",
    )(pick, mix, packed, slot_row, slot_col, valid, wg, wu, wd, fan, sd)


def mm_lead(a, b):
    return lax.dot_general(a, b, (((0,), (0,)), ((), ())), preferred_element_type=F32)


def turn(v, cosine, sine):
    half = v.shape[1] // 2
    a, b = v[:, :half], v[:, half:]
    return jnp.concatenate([a * cosine - b * sine, b * cosine + a * sine], axis=1)


def project_kernel(x_ref, gain_ref, lgain_ref, wq_ref, wl_ref, we_ref, cos_ref, sin_ref,
                   h_ref, q_ref, k_ref, v_ref, lat_ref):
    blocks = x_ref.shape[0]
    batches, rows, _ = q_ref.shape
    here = rows // blocks
    x = x_ref[...].reshape(blocks * batches * here, x_ref.shape[2]).astype(F32)
    h = x * lax.rsqrt(jnp.mean(x * x, axis=1, keepdims=True) + 1e-6) * gain_ref[...]
    h = h.astype(BF)
    h_ref[...] = h
    raw = mm(h, wq_ref[...])
    raw_lat = mm(h, wl_ref[...])
    cosine, sine = cos_ref[...], sin_ref[...]
    zeros = jnp.zeros((raw.shape[0], 64), BF)
    q = jnp.concatenate([raw[:, :128].astype(BF), turn(raw[:, 128:192], cosine, sine).astype(BF), zeros], axis=1)
    k_rope = turn(raw_lat[:, 512:576], cosine, sine).astype(BF)
    lat = raw_lat[:, :512]
    lat = (lat * lax.rsqrt(jnp.mean(lat * lat, axis=1, keepdims=True) + 1e-6) * lgain_ref[...]).astype(BF)
    expanded = mm(lat, we_ref[...]).astype(BF)
    k = jnp.concatenate([expanded[:, :128], k_rope, zeros], axis=1)
    for e in range(blocks):
        for m in range(batches):
            src = slice((e * batches + m) * here, (e * batches + m + 1) * here)
            dst = slice(e * here, (e + 1) * here)
            q_ref[m, dst] = q[src]
            k_ref[m, dst] = k[src]
            v_ref[m, dst] = expanded[src, 128:]
            lat_ref[m, dst] = lat[src]


def project(x_all, gain, lgain, wq, wl, we, cosine, sine, batches):
    groups, rows, width = x_all.shape
    here = rows // batches
    per = 4
    seq = groups * here
    shape = jax.ShapeDtypeStruct

    def whole(v):
        return pl.BlockSpec(v.shape, lambda i: (0, 0))

    def by_seq(w):
        return pl.BlockSpec((batches, per * here, w), lambda i: (0, i, 0))

    table = pl.BlockSpec((per * rows, 32), lambda i: (i, 0))
    return pl.pallas_call(
        project_kernel,
        grid=(groups // per,),
        out_shape=(shape((groups * rows, width), BF), shape((batches, seq, 256), BF), shape((batches, seq, 256), BF),
                   shape((batches, seq, 128), BF), shape((batches, seq, 512), BF)),
        in_specs=[pl.BlockSpec((per, rows, width), lambda i: (i, 0, 0)), whole(gain), whole(lgain), whole(wq), whole(wl), whole(we),
                  table, table],
        out_specs=[pl.BlockSpec((per * rows, width), lambda i: (i, 0)), by_seq(256), by_seq(256), by_seq(128), by_seq(512)],
        compiler_params=pltpu.CompilerParams(vmem_limit_bytes=48 * 1024 * 1024),
        cost_estimate=pl.CostEstimate(flops=7_000_000_000, bytes_accessed=20_000_000, transcendentals=0),
        name="project",
    )(x_all, gain, lgain, wq, wl, we, cosine, sine)


ROWS = 256
SCALE = 192.0 ** -0.5


def held_scores(q, k, first, length):
    s = mm_t(q, k) * SCALE
    t = lax.broadcasted_iota(jnp.int32, s.shape, 0) + first
    u = lax.broadcasted_iota(jnp.int32, s.shape, 1)
    return jnp.where((u <= t) & (u < length), s, -1e30)


def attend_kernel(len_ref, q_ref, k_ref, v_ref, wo_ref, part_ref, att_ref, lse_ref):
    length = len_ref[pl.program_id(0)]
    seq = q_ref.shape[1]
    groups, _, here, width = part_ref.shape
    for i in range(seq // ROWS):
        tile = slice(i * ROWS, (i + 1) * ROWS)
        ext = (i + 1) * ROWS
        s = held_scores(q_ref[0, tile], k_ref[0, :ext], i * ROWS, length)
        peak = jnp.max(s, axis=1, keepdims=True)
        raised = jnp.exp(s - peak)
        total = jnp.sum(raised, axis=1, keepdims=True)
        lse_ref[0, tile] = peak + jnp.log(total)
        p = (raised / total).astype(BF)
        att = mm(p, v_ref[0, :ext]).astype(BF)
        per = ROWS // here
        att_ref[i * per:(i + 1) * per, 0] = att.reshape(per, here, att.shape[1])
        for j in range(width // 512):
            cols = slice(j * 512, (j + 1) * 512)
            part_ref[i * per:(i + 1) * per, 0, :, cols] = mm(att, wo_ref[:, cols]).astype(BF).reshape(per, here, 512)


def attend(lengths, q, k, v, wo, groups):
    batches, seq, _ = q.shape
    here = seq // groups
    width = wo.shape[1]
    shape = jax.ShapeDtypeStruct

    def by_seq(w):
        return pl.BlockSpec((1, seq, w), lambda m: (m, 0, 0))

    def by_dev(w):
        return pl.BlockSpec((groups, 1, here, w), lambda m: (0, m, 0, 0))

    return pl.pallas_call(
        attend_kernel,
        grid=(batches,),
        out_shape=(shape((groups, batches, here, width), BF), shape((groups, batches, here, 128), BF),
                   shape((batches, seq, 1), F32)),
        in_specs=[pl.BlockSpec(memory_space=pltpu.SMEM), by_seq(256), by_seq(256), by_seq(128),
                  pl.BlockSpec(wo.shape, lambda m: (0, 0))],
        out_specs=[by_dev(width), by_dev(128), by_seq(1)],
        compiler_params=pltpu.CompilerParams(vmem_limit_bytes=48 * 1024 * 1024),
        cost_estimate=pl.CostEstimate(flops=4_000_000_000, bytes_accessed=15_000_000, transcendentals=2_000_000),
        name="attend",
    )(lengths, q, k, v, wo)


def attend_back_kernel(len_ref, dout_ref, q_ref, k_ref, v_ref, lat_ref, att_ref, lse_ref, wo_ref, wq_ref, we_ref,
                       cos_ref, sin_ref, part_ref, dq_ref, gwo_ref, gwe_ref, dk, dv, datt):
    m = pl.program_id(0)
    length = len_ref[m]
    seq = q_ref.shape[1]
    groups, _, here, width = dout_ref.shape
    per = ROWS // here

    @pl.when(m == 0)
    def _():
        gwo_ref[...] = jnp.zeros_like(gwo_ref)
        gwe_ref[...] = jnp.zeros_like(gwe_ref)

    for j in range(4):
        blocks = slice(j * groups // 4, (j + 1) * groups // 4)
        dout = dout_ref[blocks].reshape(seq // 4, width)
        rows = slice(j * seq // 4, (j + 1) * seq // 4)
        datt[rows] = mm_t(dout, wo_ref[...]).astype(BF)
        gwo_ref[...] += mm_lead(att_ref[blocks].reshape(seq // 4, 128), dout)
    dk[...] = jnp.zeros_like(dk)
    dv[...] = jnp.zeros_like(dv)
    for i in range(seq // ROWS):
        tile = slice(i * ROWS, (i + 1) * ROWS)
        ext = (i + 1) * ROWS
        q = q_ref[0, tile]
        p = jnp.exp(held_scores(q, k_ref[0, :ext], i * ROWS, length) - lse_ref[0, tile])
        da = datt[tile]
        dp = mm_t(da, v_ref[0, :ext])
        inner = jnp.sum(dp * p, axis=1, keepdims=True)
        ds = (p * (dp - inner)).astype(BF)
        dq = mm(ds, k_ref[0, :ext]) * SCALE
        dk[:ext] += mm_lead(ds, q)
        dv[:ext] += mm_lead(p.astype(BF), da)
        rope = turn(dq[:, 128:192], cos_ref[tile], -sin_ref[tile])
        dq = jnp.concatenate([dq[:, :128].astype(BF), rope.astype(BF), jnp.zeros((ROWS, 64), BF)], axis=1)
        dq_ref[i * per:(i + 1) * per, 0] = dq.reshape(per, here, 256)
        for j in range(width // 512):
            cols = slice(j * 512, (j + 1) * 512)
            part_ref[i * per:(i + 1) * per, 0, :, cols] = mm_t(dq, wq_ref[cols]).astype(BF).reshape(per, here, 512)
    for i in range(seq // ROWS):
        tile = slice(i * ROWS, (i + 1) * ROWS)
        d_k = dk[tile] * SCALE
        d_exp = jnp.concatenate([d_k[:, :128].astype(BF), dv[tile].astype(BF)], axis=1)
        gwe_ref[...] += mm_lead(lat_ref[0, tile], d_exp)
        d_lat = mm_t(d_exp, we_ref[...]).astype(BF)
        tail = jnp.concatenate([d_lat, d_k[:, 128:].astype(BF)], axis=1)
        pad = part_ref.shape[3] - width - tail.shape[1]
        if pad > 0:
            tail = jnp.concatenate([tail, jnp.zeros((ROWS, pad), BF)], axis=1)
        part_ref[i * per:(i + 1) * per, 0, :, width:] = tail[:, :part_ref.shape[3] - width].reshape(per, here, -1)


def attend_back(lengths, dout, q, k, v, lat, att, lse, wo, wq, we, cosine, sine, tail):
    groups, batches, here, width = dout.shape
    seq = groups * here
    shape = jax.ShapeDtypeStruct

    def by_seq(w):
        return pl.BlockSpec((1, seq, w), lambda m: (m, 0, 0))

    def by_dev(w):
        return pl.BlockSpec((groups, 1, here, w), lambda m: (0, m, 0, 0))

    def whole(v):
        return pl.BlockSpec(v.shape, lambda m: (0, 0))

    return pl.pallas_call(
        attend_back_kernel,
        grid=(batches,),
        out_shape=(shape((groups, batches, here, width + tail), BF), shape((groups, batches, here, 256), BF),
                   shape(wo.shape, F32), shape(we.shape, F32)),
        in_specs=[pl.BlockSpec(memory_space=pltpu.SMEM), by_dev(width), by_seq(256), by_seq(256), by_seq(128),
                  by_seq(512), by_dev(128), by_seq(1), whole(wo), whole(wq), whole(we), whole(cosine), whole(sine)],
        out_specs=[by_dev(width + tail), by_dev(256), whole(wo), whole(we)],
        scratch_shapes=[pltpu.VMEM((seq, 256), F32), pltpu.VMEM((seq, 128), F32), pltpu.VMEM((seq, 128), BF)],
        compiler_params=pltpu.CompilerParams(vmem_limit_bytes=56 * 1024 * 1024),
        cost_estimate=pl.CostEstimate(flops=14_000_000_000, bytes_accessed=25_000_000, transcendentals=2_000_000),
        name="attend_back",
    )(lengths, dout, q, k, v, lat, att, lse, wo, wq, we, cosine, sine)


H = 16
QK_NOPE = 128
ROPE = 64
V_DIM = 128
KV_RANK = 512
GROUPS = 16
EPSILON = 1e-06
ROTARY_BASE = 10000.0


def product(left_side, right_side):
    return jnp.dot(left_side, right_side, preferred_element_type=F32)


def product_lead(left_side, right_side):
    return lax.dot_general(
        left_side, right_side, (((0,), (0,)), ((), ())), preferred_element_type=F32
    )


def product_trail(left_side, right_side):
    return lax.dot_general(
        left_side, right_side, (((1,), (1,)), ((), ())), preferred_element_type=F32
    )


def rotary_tables(positions):
    half_width = ROPE // 2
    frequency = ROTARY_BASE ** (-jnp.arange(half_width, dtype=F32) * 2.0 / ROPE)
    angles = positions[:, None] * frequency[None, :]
    return (jnp.cos(angles), jnp.sin(angles))


def rotate(values, cosine, sine_table):
    first_half, second_half = jnp.split(values, 2, axis=-1)
    return jnp.concatenate(
        [
            first_half * cosine - second_half * sine_table,
            second_half * cosine + first_half * sine_table,
        ],
        axis=-1,
    )


def norm_forward(values, gains):
    factor = lax.rsqrt(jnp.mean(values * values, axis=-1, keepdims=True) + EPSILON)
    normed = values * factor
    return (normed * gains, normed, factor)


def norm_backward(gradient, normed, factor, gains):
    gain_grad = jnp.sum(gradient * normed, axis=0)
    scaled = gradient * gains
    return (
        factor * (scaled - normed * jnp.mean(scaled * normed, axis=-1, keepdims=True)),
        gain_grad,
    )


def selected_experts(routes):
    chosen = routes[:, :, None] == jnp.arange(GROUPS, dtype=routes.dtype)
    return jnp.any(chosen, axis=1)


def masked_softmax(logits, mask):
    held = jnp.where(mask, logits, -1e30)
    peak = jnp.max(held, axis=-1, keepdims=True)
    raised = jnp.where(mask, jnp.exp(held - peak), 0.0)
    return raised / jnp.sum(raised, axis=-1, keepdims=True)


def per_device(
    layer_input,
    out_cotangent,
    lengths,
    routes,
    attn_gain,
    query_weight,
    latent_weight,
    latent_gain,
    expand_weight,
    output_weight,
    mixer_gain,
    router_weight,
    gate_weight,
    up_weight,
    down_weight,
    shared_gate,
    shared_up,
    shared_down,
):
    dp = lax.axis_size("dp")
    me = lax.axis_index("expert")
    plane = lax.axis_index("dp")
    batches, _, here, width = layer_input.shape
    own = batches * here
    total = own * GROUPS
    seq_total = here * GROUPS
    rows_w = query_weight.shape[0]
    rows_l = expand_weight.shape[0]

    x_own = layer_input.reshape(own, width)
    latent_column = jnp.zeros((rows_w,), BF).at[:rows_l].set(latent_gain)
    small = jnp.concatenate(
        [
            latent_weight,
            router_weight,
            attn_gain[:, None],
            mixer_gain[:, None],
            latent_column[:, None],
            jnp.zeros((rows_w, 640 - 595), BF),
        ],
        axis=1,
    )
    query_parts = query_weight.reshape(rows_w, H, QK_NOPE + ROPE).transpose(1, 0, 2)
    expand_parts = expand_weight.reshape(rows_l, H, QK_NOPE + V_DIM).transpose(1, 0, 2)
    parts = jnp.concatenate([query_parts, expand_parts.reshape(H, rows_w, ROPE)], axis=2)
    x_all, small, parts_head, output_head = opening(dp, x_own, small, parts, output_weight, 1)
    x_all = x_all.reshape(total, width)
    small = small.reshape(width, 640)
    parts_head = parts_head.reshape(width, TILE)
    latent_full = small[:, :576]
    router_full = small[:, 576:592]
    gain_attn = small[:, 592].astype(F32)
    gain_mixer = small[:, 593].astype(F32)
    gain_latent = small[:, 594].reshape(dp * GROUPS, rows_w)[:, :rows_l].reshape(-1).astype(F32)
    expand_head = parts_head[:, QK_NOPE + ROPE :].reshape(KV_RANK, QK_NOPE + V_DIM)
    output_head = output_head.reshape(V_DIM, width)

    share_own = jnp.concatenate([shared_gate.T, shared_up.T, shared_down], axis=0)
    share_width = shared_down.shape[0]
    gate_full = lax.all_gather(gate_weight[0], "dp", axis=0, tiled=True)
    up_full = lax.all_gather(up_weight[0], "dp", axis=0, tiled=True)
    down_full = lax.all_gather(down_weight[0], "dp", axis=0, tiled=True)
    share_full = lax.all_gather(share_own, "dp", axis=0)
    share_full = share_full.transpose(1, 0, 2).reshape(3 * share_width, width)

    seq_lengths = lengths.reshape(batches)
    own_positions = me * here + jnp.arange(here, dtype=jnp.int32)
    valid_own = (own_positions[None, :] < seq_lengths[:, None]).reshape(own).astype(F32)
    all_positions = jnp.arange(seq_total, dtype=jnp.int32).reshape(GROUPS, 1, here)
    valid_all = jnp.broadcast_to(
        all_positions < seq_lengths[None, :, None], (GROUPS, batches, here)
    ).reshape(total)
    key_positions = jnp.arange(seq_total, dtype=jnp.int32)
    cosine, sine_table = rotary_tables(key_positions.astype(F32))
    cosine_own = lax.dynamic_slice_in_dim(cosine, me * here, here)
    sine_own = lax.dynamic_slice_in_dim(sine_table, me * here, here)

    def by_sequence(v):
        return v.reshape(GROUPS, batches, here, v.shape[-1]).swapaxes(0, 1).reshape(batches, seq_total, -1)

    def by_device(v):
        return v.reshape(batches, GROUPS, here, v.shape[-1]).swapaxes(0, 1).reshape(total, -1)

    grad_own = out_cotangent.reshape(own, width) * valid_own[:, None].astype(BF)
    routes_own = routes.reshape(own, -1)
    packed = jnp.concatenate(
        [grad_own, routes_own.astype(BF), jnp.zeros((own, 128 - routes_own.shape[1]), BF)], axis=1
    )
    packed, x_all = lax.optimization_barrier((packed, x_all))
    packed = lax.all_gather(packed, "expert", axis=0, tiled=True)
    routes_all = packed[:, width : width + routes_own.shape[1]].astype(jnp.int32)
    taken = jnp.any(routes_all == me, axis=1) & valid_all
    places = jnp.cumsum(taken.reshape(-1, here).astype(jnp.int32), axis=1) - 1
    places = places + 32 * (jnp.arange(places.shape[0], dtype=jnp.int32) % 4)[:, None]
    slot = jnp.where(taken, places.reshape(total), -1)

    def by_token(table):
        return jnp.broadcast_to(
            table.reshape(GROUPS, 1, here, -1), (GROUPS, batches, here, table.shape[1])).reshape(total, -1)

    hidden_all, query, key, values, latent = project(
        x_all.reshape(GROUPS, own, width), gain_attn[None], gain_latent[None], parts_head, small, expand_head,
        by_token(cosine), by_token(sine_table), batches)
    attn_part, attended, log_total = attend(seq_lengths, query, key, values, output_head, GROUPS)
    attn_part = attn_part.reshape(GROUPS, own, width)
    attn_out = scatter16(attn_part, 2)

    x_wide = x_own.astype(F32)
    middle = x_wide + attn_out
    normed_mix, unit_mix, factor_mix = norm_forward(middle, gain_mixer)
    hidden_mix = normed_mix.astype(BF)
    mix_all = gather16(hidden_mix, 3).reshape(total, width)

    pad = TILE - share_width
    fan_share = jnp.concatenate(
        [share_full[:share_width], router_full.T, jnp.zeros((pad - GROUPS, width), BF),
         share_full[share_width : 2 * share_width], jnp.zeros((pad, width), BF)], axis=0)
    down_share = jnp.concatenate([share_full[2 * share_width :], jnp.zeros((pad, width), BF)], axis=0)
    lane = jnp.arange(128)[None, :]
    pick = jnp.concatenate([lane == me, lane == me + GROUPS], axis=1).astype(F32)
    out_part, mix_part, rows, grad_result, hidden, grad_gate_in, grad_up_in, share_hidden, grad_share_in = mixture(
        pick, mix_all, packed, slot[None, :], slot[:, None], valid_all.astype(F32)[:, None],
        gate_full, up_full, down_full, fan_share, down_share)
    grad_down = product_lead(hidden, grad_result).astype(BF)
    grad_gate = product_lead(rows, grad_gate_in).astype(BF)
    grad_up = product_lead(rows, grad_up_in).astype(BF)
    grad_share_fan = product_lead(grad_share_in, mix_all).astype(BF)
    grad_share_down = product_lead(share_hidden, packed[:, :width]).astype(BF)
    mix_part, grad_down, grad_gate, grad_up = lax.optimization_barrier((mix_part, grad_down, grad_gate, grad_up))
    mix_sum = scatter16(mix_part.reshape(GROUPS, own, width + 128), 5)
    mixed = scatter16(out_part.reshape(GROUPS, own, width), 4)
    layer_output = valid_own[:, None] * (middle + mixed)

    out_down = lax.psum_scatter(grad_down, "dp", scatter_dimension=0, tiled=True)
    out_gate = lax.psum_scatter(grad_gate, "dp", scatter_dimension=0, tiled=True)
    out_up = lax.psum_scatter(grad_up, "dp", scatter_dimension=0, tiled=True)
    grad_share = jnp.concatenate(
        [grad_share_fan[:share_width], grad_share_fan[TILE : TILE + share_width], grad_share_down[:share_width]],
        axis=0)
    grad_share = grad_share.reshape(3 * share_width, dp, width // dp).swapaxes(0, 1)
    out_share = lax.psum_scatter(grad_share, "dp", scatter_dimension=0, tiled=False).astype(F32)

    mask_own = selected_experts(routes_own)
    soft_own = masked_softmax(product(hidden_mix, router_full), mask_own)
    grad_masked = (mix_sum[:, width : width + GROUPS] + mix_sum[:, width + GROUPS : width + 2 * GROUPS])
    grad_masked = grad_masked * valid_own[:, None]
    grad_logits = soft_own * (grad_masked - jnp.sum(grad_masked * soft_own, axis=1, keepdims=True))
    grad_logits = grad_logits.astype(BF)
    grad_mix = mix_sum[:, :width] + product_trail(grad_logits, router_full)
    grad_middle_norm, grad_gain_mixer = norm_backward(grad_mix, unit_mix, factor_mix, gain_mixer)
    grad_middle = grad_own.astype(F32) + grad_middle_norm

    grad_attn_all = gather16(grad_middle.astype(BF), 6).reshape(GROUPS, batches, here, width)
    back_part, grad_query, grad_output, grad_expand = attend_back(
        seq_lengths, grad_attn_all, query, key, values, latent, attended, log_total, output_head, parts_head,
        expand_head, cosine, sine_table, 640)
    grad_query_w = product_lead(hidden_all, grad_query.reshape(total, TILE)).astype(BF)
    parts_grad = jnp.concatenate(
        [grad_query_w[:, : QK_NOPE + ROPE], grad_expand.astype(BF).reshape(width, ROPE)], axis=1)
    back_sum, out_parts, out_output = returning(
        dp, back_part.reshape(GROUPS, own, back_part.shape[3]),
        parts_grad.reshape(dp, GROUPS, rows_w, TILE), grad_output.astype(BF).reshape(dp, rows_w, width), 7)
    out_query = out_parts[..., : QK_NOPE + ROPE].transpose(1, 0, 2).reshape(rows_w, -1)
    out_expand = out_parts[..., QK_NOPE + ROPE :].reshape(H, rows_l, QK_NOPE + V_DIM)
    out_expand = out_expand.transpose(1, 0, 2).reshape(rows_l, -1)

    x_normed, unit_attn, factor_attn = norm_forward(x_wide, gain_attn)
    hidden_own = x_normed.astype(BF)
    latent_own = product(hidden_own, latent_full)
    _, unit_latent, factor_latent = norm_forward(latent_own[:, :KV_RANK], gain_latent)
    grad_latent_in, grad_gain_latent = norm_backward(
        back_sum[:, width : width + KV_RANK], unit_latent, factor_latent, gain_latent
    )
    grad_rope = back_sum[:, width + KV_RANK : width + KV_RANK + ROPE].reshape(batches, here, ROPE)
    grad_rope = rotate(grad_rope, cosine_own, -sine_own).reshape(own, ROPE)
    grad_latent_raw = jnp.concatenate([grad_latent_in, grad_rope], axis=1).astype(BF)
    grad_hidden_attn = back_sum[:, :width] + product_trail(grad_latent_raw, latent_full)
    grad_input_norm, grad_gain_attn = norm_backward(grad_hidden_attn, unit_attn, factor_attn, gain_attn)
    grad_input = grad_middle + grad_input_norm

    latent_rows = grad_gain_latent.reshape(dp * GROUPS, rows_l)
    latent_rows = jnp.pad(latent_rows, ((0, 0), (0, rows_w - rows_l))).reshape(width, 1)
    tokens_side = jnp.concatenate([hidden_own, hidden_mix], axis=0)
    grads_side = jnp.concatenate(
        [jnp.pad(grad_latent_raw, ((0, 0), (0, 64))), jnp.pad(grad_logits, ((0, 0), (576, 640 - 592)))], axis=0)
    lane = jnp.arange(640)[None, :]
    small_grad = product_lead(tokens_side, grads_side)
    small_grad = small_grad + jnp.where(lane == 592, grad_gain_attn[:, None], 0.0)
    small_grad = small_grad + jnp.where(lane == 593, grad_gain_mixer[:, None], 0.0)
    small_grad = (small_grad + jnp.where(lane == 594, latent_rows, 0.0)).astype(BF)
    small_grad = small_grad.reshape(dp, GROUPS, rows_w, 640).swapaxes(0, 1).reshape(GROUPS, dp * rows_w, 640)
    small_sum = closing(dp, small_grad, 9)

    def as_input(v):
        return v.reshape(batches, 1, here, width)

    return (
        as_input(layer_output),
        as_input(grad_input),
        small_sum[:, 592],
        out_query,
        small_sum[:, :576],
        small_sum[:rows_l, 594],
        out_expand,
        out_output,
        small_sum[:, 593],
        small_sum[:, 576:592],
        out_gate.astype(F32)[None],
        out_up.astype(F32)[None],
        out_down.astype(F32)[None],
        out_share[:share_width].T,
        out_share[share_width : 2 * share_width].T,
        out_share[2 * share_width :],
    )


def solution(mesh):
    split = P(("dp", "expert"), None)
    line = P(("dp", "expert"))
    tokens = P(None, "dp", "expert", None)
    expert = P("expert", "dp", None)
    return jax.shard_map(
        per_device,
        mesh=mesh,
        in_specs=(
            tokens, tokens, P(None, "dp"), tokens, line, split, split, line, split, split, line, split,
            expert, expert, expert, P("dp", "expert"), P("dp", "expert"), P("expert", "dp"),
        ),
        out_specs=(
            tokens, tokens, line, split, split, line, split, split, line, split,
            expert, expert, expert, P("dp", "expert"), P("dp", "expert"), P("expert", "dp"),
        ),
        check_vma=False,
    )
```

```python
import functools
import jax
import jax.numpy as jnp
from jax import lax
from jax.experimental import pallas as pl
from jax.experimental.pallas import tpu as pltpu
from jax.sharding import PartitionSpec as P

MESH = pl.DeviceIdType.MESH
NZ = 4
NE = 16


def place():
    me = lax.axis_index("expert")
    z = me // 4
    x = (me // 2) % 2
    c = me % 2
    return me, z, x, c, me + 1 - 2 * c, me + 2 - 4 * x


def enter(me, z, core, side):
    barrier = pltpu.get_barrier_semaphore()
    for other in (core, side):
        pl.semaphore_signal(barrier, inc=1, device_id={"expert": other}, device_id_type=MESH)

    @pl.when(z < NZ - 1)
    def _():
        pl.semaphore_signal(barrier, inc=1, device_id={"expert": me + 4}, device_id_type=MESH)

    @pl.when(z > 0)
    def _():
        pl.semaphore_signal(barrier, inc=1, device_id={"expert": me - 4}, device_id_type=MESH)

    pl.semaphore_wait(barrier, 2 + (z < NZ - 1).astype(jnp.int32) + (z > 0).astype(jnp.int32))


def enter_all(me, plane, dp):
    barrier = pltpu.get_barrier_semaphore()
    for r in range(1, NE):
        pl.semaphore_signal(
            barrier, inc=1, device_id={"expert": (me + r) % NE}, device_id_type=MESH)
    for r in range(1, dp):
        pl.semaphore_signal(
            barrier, inc=1, device_id={"dp": (plane + r) % dp}, device_id_type=MESH)
    pl.semaphore_wait(barrier, NE - 1 + dp - 1)


class Gather:
    def __init__(self, src, out, chunks, sems, view=lambda ref, b: ref.at[b]):
        self.src, self.out, self.chunks, self.view = src, out, chunks, view
        self.rows = src.shape[0] // chunks
        self.own_sem, self.us, self.ur, self.ds, self.dr, self.xs, self.xr, self.cs, self.cr = sems
        self.me, self.z, self.x, self.c, self.core, self.side = place()

    @staticmethod
    def scratch(chunks):
        dma = pltpu.SemaphoreType.DMA
        return [dma] + [dma((4, chunks))] * 4 + [dma((7, chunks))] * 2 + [dma((14, chunks))] * 2

    def copy(self, block, k, src, send, recv, to):
        src_ref = self.src if src is None else self.view(self.out, src)
        dst_ref = self.view(self.out, block)
        if self.chunks > 1:
            part = pl.ds(k * self.rows, self.rows)
            src_ref, dst_ref = src_ref.at[part], dst_ref.at[part]
        return pltpu.make_async_remote_copy(
            src_ref=src_ref,
            dst_ref=dst_ref,
            send_sem=send, recv_sem=recv,
            device_id={"expert": to}, device_id_type=MESH,
        )

    def up(self, k, s, src=None):
        return self.copy(self.me - 4 * s, k, src, self.us.at[s, k], self.ur.at[s, k], self.me + 4)

    def down(self, k, s, src=None):
        return self.copy(self.me + 4 * s, k, src, self.ds.at[s, k], self.dr.at[s, k], self.me - 4)

    def across(self, k, slot, block, src=None):
        return self.copy(block, k, src, self.xs.at[slot, k], self.xr.at[slot, k], self.side)

    def over(self, k, slot, block, src=None):
        return self.copy(block, k, src, self.cs.at[slot, k], self.cr.at[slot, k], self.core)

    def up_in(self, k, s):
        b = self.me - 4 * s
        return self.copy(b, k, b, self.us.at[s - 1, k], self.ur.at[s - 1, k], self.side)

    def dn_in(self, k, s):
        b = self.me + 4 * s
        return self.copy(b, k, b, self.ds.at[s - 1, k], self.dr.at[s - 1, k], self.side)

    def shift(self, base, slot):
        return base - 4 * slot if slot <= 3 else base + 4 * (slot - 3)

    def core_block(self, slot):
        if slot < 7:
            return self.shift(self.core, slot)
        return self.shift(self.core + 2 - 4 * self.x, slot - 7)

    def has(self, slot):
        slot = slot % 7
        if slot == 0:
            return self.z >= 0
        return self.z >= slot if slot <= 3 else self.z + (slot - 3) <= NZ - 1

    def start(self):
        z, me = self.z, self.me
        self.own = pltpu.make_async_copy(self.src, self.view(self.out, me), self.own_sem)
        self.own.start()
        for k in range(self.chunks):
            self.across(k, 0, me).start()

            @pl.when(z < NZ - 1)
            def _():
                self.up(k, 0).start()

            @pl.when(z > 0)
            def _():
                self.down(k, 0).start()

            self.over(k, 0, me).start()

    def line(self, k, s):
        z, me = self.z, self.me

        @pl.when(z >= s)
        def _():
            b = me - 4 * s
            self.up_in(k, s).wait_recv()
            self.across(k, s, b, b).start()

            @pl.when(z < NZ - 1)
            def _():
                self.up(k, s, b).start()

            self.over(k, s, b, b).start()

        @pl.when(z + s <= NZ - 1)
        def _():
            b = me + 4 * s
            self.dn_in(k, s).wait_recv()
            self.across(k, 3 + s, b, b).start()

            @pl.when(z > 0)
            def _():
                self.down(k, s, b).start()

            self.over(k, 3 + s, b, b).start()

    def from_side(self, k, slot):
        @pl.when(self.has(slot))
        def _():
            b = self.shift(self.side, slot)
            self.across(k, slot, b, b).wait_recv()
            self.over(k, 7 + slot, b, b).start()

    def round(self, s):
        if s < NZ:
            for k in range(self.chunks):
                self.line(k, s)
        for k in range(self.chunks):
            for slot in ((0,) if s == 1 else (s - 1, s + 2)):
                self.from_side(k, slot)

    def finish(self):
        z = self.z
        self.own.wait()
        for k in range(self.chunks):
            for slot in range(14):
                @pl.when(self.has(slot))
                def _():
                    b = self.core_block(slot)
                    self.over(k, slot, b, b).wait_recv()
                    self.over(k, slot, b, b).wait_send()
            for slot in range(7):
                @pl.when(self.has(slot))
                def _():
                    self.across(k, slot, self.me).wait_send()
            for s in range(NZ - 1):
                @pl.when((z >= s) & (z < NZ - 1))
                def _():
                    self.up(k, s).wait_send()

                @pl.when((z + s <= NZ - 1) & (z > 0))
                def _():
                    self.down(k, s).wait_send()


def gather_kernel(chunks, x_ref, o_ref, *sems):
    g = Gather(x_ref, o_ref, chunks, sems)
    enter(g.me, g.z, g.core, g.side)
    g.start()
    for s in range(1, NZ + 1):
        g.round(s)
    g.finish()


COST = pl.CostEstimate(flops=0, bytes_accessed=4_000_000, transcendentals=0)
ANY = pl.BlockSpec(memory_space=pl.ANY)


def gather16(v, cid, chunks=4):
    rows, width = v.shape
    return pl.pallas_call(
        functools.partial(gather_kernel, chunks),
        out_shape=jax.ShapeDtypeStruct((NE, rows, width), v.dtype),
        in_specs=[ANY],
        out_specs=ANY,
        scratch_shapes=Gather.scratch(chunks),
        compiler_params=pltpu.CompilerParams(collective_id=cid, has_side_effects=True),
        cost_estimate=COST,
        name="gather16",
    )(v)


def opening_kernel(dp, chunks, x_ref, small_ref, parts_ref, out_ref,
                   x_all, small_all, parts_head, out_head, small_dp, parts_dp, out_dp, *sems):
    ng = 9
    gx = Gather(x_ref, x_all, chunks, sems[:ng])
    gs = Gather(small_dp, small_all, 1, sems[ng:2 * ng], lambda ref, b: ref.at[:, b])
    loc, ys, yr, ps, pr, os_, or_, pl_sem, ol_sem = sems[2 * ng:]
    me = gx.me
    plane = lax.axis_index("dp")
    enter_all(me, plane, dp)
    pairs = ((small_ref, small_dp.at[plane]), (parts_ref, parts_dp.at[plane]),
             (out_ref, out_dp.at[plane]))

    def lift(i, r):
        src, dst = pairs[i]
        return pltpu.make_async_remote_copy(
            src_ref=src, dst_ref=dst, send_sem=ys.at[i, r], recv_sem=yr.at[i, r],
            device_id={"dp": (plane + r) % dp}, device_id_type=MESH)

    def landed(i, r):
        p = (plane - r + dp) % dp
        dst = (small_dp.at[p], parts_dp.at[p], out_dp.at[p])[i]
        return pltpu.make_async_remote_copy(
            src_ref=dst, dst_ref=dst, send_sem=ys.at[i, r], recv_sem=yr.at[i, r],
            device_id={"dp": p}, device_id_type=MESH)

    def kept(i):
        src, dst = pairs[i]
        return pltpu.make_async_copy(src, dst, loc.at[i])

    for i in range(3):
        for r in range(1, dp):
            lift(i, r).start()
        kept(i).start()
    gx.start()
    gx.round(1)

    kept(0).wait()
    for r in range(1, dp):
        landed(0, r).wait_recv()
    gs.start()

    def part(r):
        h = (me + r) % NE
        return pltpu.make_async_remote_copy(
            src_ref=parts_dp.at[:, h], dst_ref=parts_head.at[:, me],
            send_sem=ps.at[r], recv_sem=pr.at[r],
            device_id={"expert": h}, device_id_type=MESH)

    def part_in(r):
        e = (me - r + NE) % NE
        return pltpu.make_async_remote_copy(
            src_ref=parts_head.at[:, e], dst_ref=parts_head.at[:, e],
            send_sem=ps.at[r], recv_sem=pr.at[r],
            device_id={"expert": e}, device_id_type=MESH)

    def part_kept():
        return pltpu.make_async_copy(parts_dp.at[:, me], parts_head.at[:, me], pl_sem)

    kept(1).wait()
    for r in range(1, dp):
        landed(1, r).wait_recv()
    for r in range(1, NE):
        part(r).start()
    part_kept().start()
    gx.round(2)

    def row(d):
        b = NE * d + me
        return pltpu.make_async_remote_copy(
            src_ref=out_dp.at[d], dst_ref=out_head.at[b % dp],
            send_sem=os_.at[d], recv_sem=or_.at[b % dp],
            device_id={"expert": b // dp}, device_id_type=MESH)

    def row_kept(d):
        b = NE * d + me
        return pltpu.make_async_copy(out_dp.at[d], out_head.at[b % dp], ol_sem.at[d])

    kept(2).wait()
    for r in range(1, dp):
        landed(2, r).wait_recv()
    for d in range(dp):
        home = (NE * d + me) // dp

        @pl.when(home != me)
        def _():
            row(d).start()

        @pl.when(home == me)
        def _():
            row_kept(d).start()

    gs.round(1)
    gx.round(3)
    gs.round(2)
    gx.round(4)
    gs.round(3)
    gs.round(4)

    def row_in(j):
        return pltpu.make_async_remote_copy(
            src_ref=out_head.at[j], dst_ref=out_head.at[j], send_sem=os_.at[j], recv_sem=or_.at[j],
            device_id={"expert": gx.core}, device_id_type=MESH)

    for r in range(1, NE):
        part_in(r).wait_recv()
        part(r).wait_send()
    part_kept().wait()
    for j in range(dp):
        @pl.when((dp * me + j) % NE != me)
        def _():
            row_in(j).wait_recv()
    for d in range(dp):
        home = (NE * d + me) // dp

        @pl.when(home != me)
        def _():
            row(d).wait_send()

        @pl.when(home == me)
        def _():
            row_kept(d).wait()
    for i in range(3):
        for r in range(1, dp):
            lift(i, r).wait_send()
    gx.finish()
    gs.finish()


def opening(dp, x, small, parts, out, cid, chunks=4):
    dma = pltpu.SemaphoreType.DMA
    rows, ws = small.shape
    bf = x.dtype
    wo = out.shape[1]
    shape = jax.ShapeDtypeStruct
    res = pl.pallas_call(
        functools.partial(opening_kernel, dp, chunks),
        out_shape=(
            shape((NE,) + x.shape, bf), shape((dp, NE, rows, ws), bf), shape((dp, NE) + parts.shape[1:], bf),
            shape((dp, rows, wo), bf),
            shape((dp, rows, ws), bf), shape((dp,) + parts.shape, bf), shape((dp, rows, wo), bf),
        ),
        in_specs=[ANY] * 4,
        out_specs=[ANY] * 7,
        scratch_shapes=Gather.scratch(chunks) + Gather.scratch(1) + [
            dma((3,)), dma((3, dp)), dma((3, dp)), dma((NE,)), dma((NE,)), dma((dp,)), dma((dp,)), dma, dma((dp,))],
        compiler_params=pltpu.CompilerParams(collective_id=cid, has_side_effects=True),
        cost_estimate=COST,
        name="opening",
    )(x, small, parts, out)
    return res[:4]


def order(z, i):
    a, b = (3, 2, 1, 0)[i], (3, 2, 0, 1)[i]
    return jnp.where(z == 0, a, jnp.where(z == 1, b, jnp.where(z == 2, 3 - b, 3 - a)))


class Scatter:
    def __init__(self, p_ref, o_ref, chunks, scratch):
        self.p, self.o, self.chunks = p_ref, o_ref, chunks
        (self.cbuf, self.own, self.xbuf, self.ubuf, self.dbuf, self.ld, self.cs, self.cr, self.xs, self.xr,
         self.us, self.ur, self.ds, self.dr) = scratch
        self.rows = o_ref.shape[0] // chunks
        self.me, self.z, self.x, self.c, self.core, self.side = place()

    @staticmethod
    def scratch(rows, width, chunks, bf):
        dma = pltpu.SemaphoreType.DMA
        return [pltpu.VMEM((n, rows, width), bf) for n in (8, 8, 4, 4, 4)] + [
            dma((8,)), dma((8, chunks)), dma((8, chunks))] + [dma((4, chunks))] * 6

    def rng(self, k):
        return pl.ds(k * self.rows, self.rows)

    def column(self, i, j):
        return 4 * order(self.z, i) + 2 * jnp.where(j == 0, 1 - self.x, self.x)

    def remote(self, src, dst, send, recv, to):
        return pltpu.make_async_remote_copy(
            src_ref=src, dst_ref=dst, send_sem=send, recv_sem=recv,
            device_id={"expert": to}, device_id_type=MESH)

    def over(self, i, j, k):
        n = 2 * i + j
        return self.remote(
            self.p.at[self.column(i, j) + 1 - self.c, self.rng(k)], self.cbuf.at[n, self.rng(k)],
            self.cs.at[n, k], self.cr.at[n, k], self.core)

    def load(self, i, j):
        n = 2 * i + j
        return pltpu.make_async_copy(self.p.at[self.column(i, j) + self.c], self.own.at[n], self.ld.at[n])

    def across(self, i, k):
        return self.remote(self.own.at[2 * i, self.rng(k)], self.xbuf.at[i, self.rng(k)],
                           self.xs.at[i, k], self.xr.at[i, k], self.side)

    def up(self, t, i, k):
        return self.remote(self.own.at[2 * i + 1, self.rng(k)], self.ubuf.at[t, self.rng(k)],
                           self.us.at[t, k], self.ur.at[t, k], self.me + 4)

    def down(self, t, i, k):
        return self.remote(self.own.at[2 * i + 1, self.rng(k)], self.dbuf.at[t, self.rng(k)],
                           self.ds.at[t, k], self.dr.at[t, k], self.me - 4)

    def start(self):
        for i in range(NZ):
            for j in range(2):
                self.load(i, j).start()
                for k in range(self.chunks):
                    self.over(i, j, k).start()

    def first(self, i):
        f32 = jnp.float32
        self.load(i, 0).wait()
        for k in range(self.chunks):
            self.over(i, 0, k).wait_recv()
            s = self.rng(k)
            self.own[2 * i, s] = (
                self.own[2 * i, s].astype(f32) + self.cbuf[2 * i, s].astype(f32)).astype(self.own.dtype)
            self.across(i, k).start()

    def second(self, i):
        f32 = jnp.float32
        z, own, o = self.z, self.own, self.o
        t = order(z, i)
        self.load(i, 1).wait()
        for k in range(self.chunks):
            s = self.rng(k)
            self.over(i, 1, k).wait_recv()
            self.across(i, k).wait_recv()

            def base():
                return (own[2 * i + 1, s].astype(f32) + self.cbuf[2 * i + 1, s].astype(f32)
                        + self.xbuf[i, s].astype(f32))

            if i < NZ - 1:
                @pl.when(t > z)
                def _():
                    @pl.when(z > 0)
                    def _():
                        self.up(t, i, k).wait_recv()
                        own[2 * i + 1, s] = (base() + self.ubuf[t, s].astype(f32)).astype(own.dtype)

                    @pl.when(z == 0)
                    def _():
                        own[2 * i + 1, s] = base().astype(own.dtype)

                    self.up(t, i, k).start()

                @pl.when(t < z)
                def _():
                    @pl.when(z < NZ - 1)
                    def _():
                        self.down(t, i, k).wait_recv()
                        own[2 * i + 1, s] = (base() + self.dbuf[t, s].astype(f32)).astype(own.dtype)

                    @pl.when(z == NZ - 1)
                    def _():
                        own[2 * i + 1, s] = base().astype(own.dtype)

                    self.down(t, i, k).start()
            else:
                @pl.when(z > 0)
                def _():
                    self.up(t, i, k).wait_recv()

                @pl.when(z < NZ - 1)
                def _():
                    self.down(t, i, k).wait_recv()

                @pl.when((z > 0) & (z < NZ - 1))
                def _():
                    o[s] = (base() + self.ubuf[t, s].astype(f32) + self.dbuf[t, s].astype(f32)).astype(o.dtype)

                @pl.when(z == 0)
                def _():
                    o[s] = (base() + self.dbuf[t, s].astype(f32)).astype(o.dtype)

                @pl.when(z == NZ - 1)
                def _():
                    o[s] = (base() + self.ubuf[t, s].astype(f32)).astype(o.dtype)

    def run(self):
        self.first(0)
        for i in range(NZ):
            if i + 1 < NZ:
                self.first(i + 1)
            self.second(i)

    def finish(self):
        z = self.z
        for k in range(self.chunks):
            for i in range(NZ):
                self.across(i, k).wait_send()
                for j in range(2):
                    self.over(i, j, k).wait_send()
                if i < NZ - 1:
                    t = order(z, i)

                    @pl.when(t > z)
                    def _():
                        self.up(t, i, k).wait_send()

                    @pl.when(t < z)
                    def _():
                        self.down(t, i, k).wait_send()


def scatter_kernel(chunks, p_ref, o_ref, *scratch):
    s = Scatter(p_ref, o_ref, chunks, scratch)
    enter(s.me, s.z, s.core, s.side)
    s.start()
    s.run()
    s.finish()


VMEM = pl.BlockSpec(memory_space=pltpu.VMEM)


def scatter16(p, cid, chunks=2, out_dtype=jnp.float32):
    _, rows, width = p.shape
    return pl.pallas_call(
        functools.partial(scatter_kernel, chunks),
        out_shape=jax.ShapeDtypeStruct((rows, width), out_dtype),
        in_specs=[ANY],
        out_specs=VMEM,
        scratch_shapes=Scatter.scratch(rows, width, chunks, p.dtype),
        compiler_params=pltpu.CompilerParams(
            collective_id=cid, has_side_effects=True, vmem_limit_bytes=32 * 1024 * 1024),
        cost_estimate=COST,
        name="scatter16",
    )(p)


def return_kernel(dp, chunks, p_ref, parts_ref, rows_ref, o_ref, parts_in, rows_in, parts_far, rows_far, *scratch):
    ns = 14
    s = Scatter(p_ref, o_ref, chunks, scratch[:ns])
    ps, pr, os_, or_, pl_sem, ol_sem, ys, yr = scratch[ns:]
    me = s.me
    plane = lax.axis_index("dp")
    enter_all(me, plane, dp)

    def part(r):
        e = (me + r) % NE
        return pltpu.make_async_remote_copy(
            src_ref=parts_ref.at[:, e], dst_ref=parts_in.at[:, me],
            send_sem=ps.at[r], recv_sem=pr.at[r],
            device_id={"expert": e}, device_id_type=MESH)

    def part_in(r):
        h = (me - r + NE) % NE
        return pltpu.make_async_remote_copy(
            src_ref=parts_in.at[:, h], dst_ref=parts_in.at[:, h],
            send_sem=ps.at[r], recv_sem=pr.at[r],
            device_id={"expert": h}, device_id_type=MESH)

    def part_kept():
        return pltpu.make_async_copy(parts_ref.at[:, me], parts_in.at[:, me], pl_sem)

    def row(j):
        b = dp * me + j
        return pltpu.make_async_remote_copy(
            src_ref=rows_ref.at[j], dst_ref=rows_in.at[b // NE],
            send_sem=os_.at[j], recv_sem=or_.at[b // NE],
            device_id={"expert": b % NE}, device_id_type=MESH)

    def row_kept(j):
        b = dp * me + j
        return pltpu.make_async_copy(rows_ref.at[j], rows_in.at[b // NE], ol_sem.at[j])

    def row_in(d):
        return pltpu.make_async_remote_copy(
            src_ref=rows_in.at[d], dst_ref=rows_in.at[d], send_sem=os_.at[d], recv_sem=or_.at[d],
            device_id={"expert": s.core}, device_id_type=MESH)

    def lift(i, r):
        to = (plane + r) % dp
        src, dst = ((parts_in.at[to], parts_far.at[r - 1]), (rows_in.at[to], rows_far.at[r - 1]))[i]
        return pltpu.make_async_remote_copy(
            src_ref=src, dst_ref=dst, send_sem=ys.at[i, r], recv_sem=yr.at[i, r],
            device_id={"dp": to}, device_id_type=MESH)

    s.start()
    for r in range(1, NE):
        part(r).start()
    part_kept().start()
    for j in range(dp):
        @pl.when((dp * me + j) % NE != me)
        def _():
            row(j).start()

        @pl.when((dp * me + j) % NE == me)
        def _():
            row_kept(j).start()
    s.first(0)
    s.first(1)
    s.second(0)
    for r in range(1, NE):
        part_in(r).wait_recv()
    part_kept().wait()
    for j in range(dp):
        @pl.when((dp * me + j) % NE == me)
        def _():
            row_kept(j).wait()
    for d in range(dp):
        @pl.when((NE * d + me) // dp != me)
        def _():
            row_in(d).wait_recv()
    for i in range(2):
        for r in range(1, dp):
            lift(i, r).start()
    s.first(2)
    s.second(1)
    s.first(3)
    s.second(2)
    s.second(3)
    for i in range(2):
        for r in range(1, dp):
            lift(i, r).wait_recv()
            lift(i, r).wait_send()
    for r in range(1, NE):
        part(r).wait_send()
    for j in range(dp):
        @pl.when((dp * me + j) % NE != me)
        def _():
            row(j).wait_send()
    s.finish()


def returning(dp, p, parts, rows, cid, chunks=2):
    dma = pltpu.SemaphoreType.DMA
    _, n, width = p.shape
    shape = jax.ShapeDtypeStruct
    out, parts_in, rows_in, parts_far, rows_far = pl.pallas_call(
        functools.partial(return_kernel, dp, chunks),
        out_shape=(
            shape((n, width), jnp.float32), shape(parts.shape, parts.dtype), shape(rows.shape, rows.dtype),
            shape((dp - 1,) + parts.shape[1:], parts.dtype), shape((dp - 1,) + rows.shape[1:], rows.dtype)),
        in_specs=[ANY] * 3,
        out_specs=[VMEM] + [ANY] * 4,
        scratch_shapes=Scatter.scratch(n, width, chunks, p.dtype) + [
            dma((NE,)), dma((NE,)), dma((dp,)), dma((dp,)), dma, dma((dp,)), dma((2, dp)), dma((2, dp))],
        compiler_params=pltpu.CompilerParams(
            collective_id=cid, has_side_effects=True, vmem_limit_bytes=48 * 1024 * 1024),
        cost_estimate=COST,
        name="returning",
    )(p, parts, rows)
    plane = lax.axis_index("dp")

    def total(near, far):
        own = lax.dynamic_index_in_dim(near, plane, 0, False).astype(jnp.float32)
        return own + jnp.sum(far.astype(jnp.float32), axis=0)

    return out, total(parts_in, parts_far), total(rows_in, rows_far)


def closing_kernel(dp, chunks, p_ref, o_ref, far_ref, *scratch):
    ns = 14
    s = Scatter(p_ref, o_ref, chunks, scratch[:ns])
    ys, yr = scratch[ns:]
    plane = lax.axis_index("dp")
    rows = o_ref.shape[0] // dp
    barrier = pltpu.get_barrier_semaphore()
    for r in range(1, dp):
        pl.semaphore_signal(barrier, inc=1, device_id={"dp": (plane + r) % dp}, device_id_type=MESH)
    z = s.z
    for other in (s.core, s.side):
        pl.semaphore_signal(barrier, inc=1, device_id={"expert": other}, device_id_type=MESH)

    @pl.when(z < NZ - 1)
    def _():
        pl.semaphore_signal(barrier, inc=1, device_id={"expert": s.me + 4}, device_id_type=MESH)

    @pl.when(z > 0)
    def _():
        pl.semaphore_signal(barrier, inc=1, device_id={"expert": s.me - 4}, device_id_type=MESH)

    pl.semaphore_wait(barrier, dp + 1 + (z < NZ - 1).astype(jnp.int32) + (z > 0).astype(jnp.int32))

    def lift(r):
        to = (plane + r) % dp
        return pltpu.make_async_remote_copy(
            src_ref=o_ref.at[pl.ds(pl.multiple_of(to * rows, 16), rows)], dst_ref=far_ref.at[r - 1],
            send_sem=ys.at[r], recv_sem=yr.at[r],
            device_id={"dp": to}, device_id_type=MESH)

    s.start()
    s.run()
    for r in range(1, dp):
        lift(r).start()
    s.finish()
    for r in range(1, dp):
        lift(r).wait_recv()
        lift(r).wait_send()


def closing(dp, p, cid):
    dma = pltpu.SemaphoreType.DMA
    _, n, width = p.shape
    shape = jax.ShapeDtypeStruct
    near, far = pl.pallas_call(
        functools.partial(closing_kernel, dp, 1),
        out_shape=(shape((n, width), p.dtype), shape((dp - 1, n // dp, width), p.dtype)),
        in_specs=[ANY],
        out_specs=[VMEM, VMEM],
        scratch_shapes=Scatter.scratch(n, width, 1, p.dtype) + [dma((dp,)), dma((dp,))],
        compiler_params=pltpu.CompilerParams(
            collective_id=cid, has_side_effects=True, vmem_limit_bytes=32 * 1024 * 1024),
        cost_estimate=COST,
        name="closing",
    )(p)
    own = lax.dynamic_slice_in_dim(near, lax.axis_index("dp") * (n // dp), n // dp).astype(jnp.float32)
    return own + jnp.sum(far.astype(jnp.float32), axis=0)
BF = jnp.bfloat16
F32 = jnp.float32


def mm(a, b):
    return jnp.dot(a, b, preferred_element_type=F32)


def mm_t(a, b):
    return lax.dot_general(a, b, (((1,), (1,)), ((), ())), preferred_element_type=F32)


def silu_pair(gate_in):
    sigmoid = 1.0 / (1.0 + jnp.exp(-gate_in))
    return (gate_in * sigmoid, sigmoid * (1.0 + gate_in * (1.0 - sigmoid)))


TILE = 256
WIDE = 512
SHARE = 176


def one_hots(slot_row, slot_col, groups, slots):
    to_slot, to_token = [], []
    for g in range(groups):
        row = slot_row[:, g * 256:(g + 1) * 256]
        col = slot_col[g * 256:(g + 1) * 256, :]
        to_slot.append((lax.broadcasted_iota(jnp.int32, (slots, 256), 0) == row).astype(BF))
        to_token.append((lax.broadcasted_iota(jnp.int32, (256, slots), 1) == col).astype(BF))
    return to_slot, to_token


def lanes(j):
    return pl.ds(pl.multiple_of(j * WIDE, WIDE), WIDE)


def over_columns(total, body):
    def step(j, _):
        body(pl.multiple_of(j * WIDE, WIDE), WIDE)
        return 0

    lax.fori_loop(0, total // WIDE, step, 0)
    if total % WIDE:
        body(total // WIDE * WIDE, total % WIDE)


def forward_kernel(chunks, pick_ref, mix_ref, routes_ref, slot_row, slot_col, valid_ref, wg_ref, wu_ref, wd_ref,
                   fan_ref, sd_ref, dy_ref,
                   out_ref, rows_ref, hid_ref, act_ref, slo_ref, eo_ref, sh_ref, sact_ref, sslo_ref, gate_ref,
                   dy_all, *sems):
    step = pl.program_id(0)
    tokens, width = mix_ref.shape
    groups, slots = tokens // 256, 128
    ff = hid_ref.shape[1]
    g = Gather(dy_ref, dy_all, chunks, sems)

    @pl.when(step == 0)
    def _():
        enter(g.me, g.z, g.core, g.side)
        g.start()

    mix = mix_ref[...]
    fanned = mm_t(mix, fan_ref[:TILE, :])
    s_up = mm_t(mix, fan_ref[TILE:, :])
    s_act, s_slope = silu_pair(fanned)
    s_hidden = (s_act * s_up).astype(BF)
    sh_ref[...] = s_hidden
    sact_ref[...] = s_act.astype(BF)
    sslo_ref[...] = (s_up * s_slope).astype(BF)
    logits = fanned[:, SHARE:SHARE + 16]
    lane16 = lax.broadcasted_iota(jnp.int32, (tokens, 16), 1)
    mask = lane16 < 0
    for k in range(routes_ref.shape[1]):
        mask = mask | (lane16 == routes_ref[:, k:k + 1])
    held = jnp.where(mask, logits, -1e30)
    raised = jnp.where(mask, jnp.exp(held - jnp.max(held, axis=1, keepdims=True)), 0.0)
    soft = raised / jnp.sum(raised, axis=1, keepdims=True)
    gate = jnp.sum(soft * pick_ref[:, :16], axis=1, keepdims=True) * valid_ref[...]
    gate_ref[...] = gate
    to_slot, to_token = one_hots(slot_row, slot_col, groups, slots)

    def dispatch(j, _):
        for n in range(groups):
            rows_ref[n * slots:(n + 1) * slots, lanes(j)] = mm(
                to_slot[n], mix_ref[n * 256:(n + 1) * 256, lanes(j)]).astype(BF)
        return 0

    lax.fori_loop(0, width // WIDE, dispatch, 0)

    def fan_in(start, size):
        cols = pl.ds(start, size)
        gate_in = mm(rows_ref[...], wg_ref[:, cols])
        up_in = mm(rows_ref[...], wu_ref[:, cols])
        act, slope = silu_pair(gate_in)
        hid_ref[:, cols] = (act * up_in).astype(BF)
        act_ref[:, cols] = act.astype(BF)
        slo_ref[:, cols] = (up_in * slope).astype(BF)

    over_columns(ff, fan_in)

    def fan_out(j, _):
        eo = mm(hid_ref[...], wd_ref[:, lanes(j)]).astype(BF)
        eo_ref[:, lanes(j)] = eo
        shared = mm(s_hidden, sd_ref[:, lanes(j)])
        picked = jnp.concatenate(
            [mm(to_token[n], eo[n * slots:(n + 1) * slots]) for n in range(groups)], axis=0)
        out_ref[:, lanes(j)] = (shared + gate * picked).astype(BF)
        return 0

    lax.fori_loop(0, width // WIDE, fan_out, 0)
    steps = pl.num_programs(0)
    for r in range(1, NZ + 1):
        @pl.when(step == r - 1)
        def _():
            g.round(r)

    @pl.when(step == steps - 1)
    def _():
        g.finish()


def backward_kernel(chunks, pick_ref, dy_ref, slot_row, slot_col, wg_ref, wu_ref, wd_ref, fan_ref, sd_ref,
                    act_ref, slo_ref, eo_ref, sact_ref, sslo_ref, gate_ref, part_ref,
                    dh_ref, deo_ref, dg_ref, du_ref, ds_ref, sum_ref, *scratch):
    step = pl.program_id(0)
    tokens, width = dy_ref.shape
    groups, slots = tokens // 256, 128
    ff = dg_ref.shape[1]
    sc = Scatter(part_ref, sum_ref, chunks, scratch)

    @pl.when(step == 0)
    def _():
        enter(sc.me, sc.z, sc.core, sc.side)
        sc.start()

    d_sh = mm_t(dy_ref[...], sd_ref[...])
    ds_ref[:, :TILE] = (d_sh * sslo_ref[...].astype(F32)).astype(BF)
    ds_ref[:, TILE:] = (d_sh * sact_ref[...].astype(F32)).astype(BF)
    to_slot, to_token = one_hots(slot_row, slot_col, groups, slots)
    gate = gate_ref[...]

    def dispatch(j, total):
        dy = dy_ref[:, lanes(j)].astype(F32)
        gated = (gate * dy).astype(BF)
        for n in range(groups):
            deo_ref[n * slots:(n + 1) * slots, lanes(j)] = mm(to_slot[n], gated[n * 256:(n + 1) * 256]).astype(BF)
        picked = jnp.concatenate(
            [mm(to_token[n], eo_ref[n * slots:(n + 1) * slots, lanes(j)]) for n in range(groups)], axis=0)
        return total + jnp.sum(dy * picked, axis=1, keepdims=True)

    d_gates = lax.fori_loop(0, width // WIDE, dispatch, jnp.zeros((tokens, 1), F32))

    @pl.when(step == 0)
    def _():
        sc.first(0)
        sc.first(1)

    def back_out(start, size):
        cols = pl.ds(start, size)
        d_eh = mm_t(deo_ref[...], wd_ref[cols, :])
        dg_ref[:, cols] = (d_eh * slo_ref[:, cols].astype(F32)).astype(BF)
        du_ref[:, cols] = (d_eh * act_ref[:, cols].astype(F32)).astype(BF)

    over_columns(ff, back_out)

    @pl.when(step == 1)
    def _():
        sc.second(0)
        sc.first(2)

    @pl.when(step == 2)
    def _():
        sc.second(1)
        sc.first(3)

    @pl.when(step == 3)
    def _():
        sc.second(2)

    d_s = ds_ref[...]

    def back_in(j, _):
        d_rows = (mm_t(dg_ref[...], wg_ref[lanes(j), :]) + mm_t(du_ref[...], wu_ref[lanes(j), :])).astype(BF)
        shared = mm(d_s, fan_ref[:, lanes(j)])
        taken = jnp.concatenate(
            [mm(to_token[n], d_rows[n * slots:(n + 1) * slots]) for n in range(groups)], axis=0)
        dh_ref[:, lanes(j)] = (shared + taken).astype(BF)
        return 0

    lax.fori_loop(0, width // WIDE, back_in, 0)
    high = d_gates.astype(BF).astype(F32)
    dh_ref[:, width:] = (high * pick_ref[:, :128] + (d_gates - high) * pick_ref[:, 128:]).astype(BF)

    @pl.when(step == 3)
    def _():
        sc.second(3)
        sc.finish()


def whole(v):
    return pl.BlockSpec(v.shape, lambda i: (0, 0), pipeline_mode=pl.Buffered(buffer_count=1))


def tiles(rows, w):
    return pl.BlockSpec((rows, w), lambda i: (i, 0))


def mixture_forward(pick, mix, routes, slot, valid, wg, wu, wd, fan, sd, dy, cid, chunks=2):
    total, width = mix.shape
    step, half = total // 4, total // 8
    ff = wd.shape[0]
    shape = jax.ShapeDtypeStruct
    rows = total // 2
    return pl.pallas_call(
        functools.partial(forward_kernel, chunks),
        grid=(4,),
        out_shape=(
            shape((total, width), BF), shape((rows, width), BF), shape((rows, ff), BF), shape((rows, ff), BF),
            shape((rows, ff), BF), shape((rows, width), BF), shape((total, TILE), BF), shape((total, TILE), BF),
            shape((total, TILE), BF), shape((total, 1), F32), shape((NE,) + dy.shape, BF)),
        in_specs=[whole(pick), tiles(step, width), tiles(step, routes.shape[1]), pl.BlockSpec((1, step), lambda i: (0, i)),
                  tiles(step, 1), tiles(step, 1), whole(wg), whole(wu), whole(wd), whole(fan), whole(sd), ANY],
        out_specs=[tiles(step, width), tiles(half, width), tiles(half, ff), tiles(half, ff), tiles(half, ff),
                   tiles(half, width), tiles(step, TILE), tiles(step, TILE), tiles(step, TILE), tiles(step, 1), ANY],
        scratch_shapes=Gather.scratch(chunks),
        compiler_params=pltpu.CompilerParams(
            collective_id=cid, has_side_effects=True, vmem_limit_bytes=60 * 1024 * 1024),
        cost_estimate=COST,
        name="mixture_forward",
    )(pick, mix, routes, slot[None, :], slot[:, None], valid, wg, wu, wd, fan, sd, dy)


def mixture_backward(pick, dy, slot, wg, wu, wd, fan, sd, act, slo, eo, sact, sslo, gate, part, cid, chunks=2):
    total, width = dy.shape
    step, half = total // 4, total // 8
    ff = wd.shape[0]
    shape = jax.ShapeDtypeStruct
    rows = total // 2
    _, own, _ = part.shape
    return pl.pallas_call(
        functools.partial(backward_kernel, chunks),
        grid=(4,),
        out_shape=(
            shape((total, width + 128), BF), shape((rows, width), BF), shape((rows, ff), BF), shape((rows, ff), BF),
            shape((total, 2 * TILE), BF), shape((own, width), F32)),
        in_specs=[whole(pick), tiles(step, width), pl.BlockSpec((1, step), lambda i: (0, i)), tiles(step, 1),
                  whole(wg), whole(wu), whole(wd), whole(fan), whole(sd),
                  tiles(half, ff), tiles(half, ff), tiles(half, width), tiles(step, TILE), tiles(step, TILE),
                  tiles(step, 1), ANY],
        out_specs=[tiles(step, width + 128), tiles(half, width), tiles(half, ff), tiles(half, ff),
                   tiles(step, 2 * TILE), pl.BlockSpec((own, width), lambda i: (0, 0))],
        scratch_shapes=Scatter.scratch(own, width, chunks, BF),
        compiler_params=pltpu.CompilerParams(
            collective_id=cid, has_side_effects=True, vmem_limit_bytes=60 * 1024 * 1024),
        cost_estimate=COST,
        name="mixture_backward",
    )(pick, dy, slot[None, :], slot[:, None], wg, wu, wd, fan, sd, act, slo, eo, sact, sslo, gate, part)


def mm_lead(a, b):
    return lax.dot_general(a, b, (((0,), (0,)), ((), ())), preferred_element_type=F32)


def turn(v, cosine, sine):
    half = v.shape[1] // 2
    a, b = v[:, :half], v[:, half:]
    return jnp.concatenate([a * cosine - b * sine, b * cosine + a * sine], axis=1)


def project_kernel(x_ref, gain_ref, lgain_ref, wq_ref, wl_ref, we_ref, cos_ref, sin_ref,
                   h_ref, q_ref, k_ref, v_ref, lat_ref):
    blocks = x_ref.shape[0]
    batches, rows, _ = q_ref.shape
    here = rows // blocks
    x = x_ref[...].reshape(blocks * batches * here, x_ref.shape[2]).astype(F32)
    h = x * lax.rsqrt(jnp.mean(x * x, axis=1, keepdims=True) + 1e-6) * gain_ref[...]
    h = h.astype(BF)
    h_ref[...] = h
    raw = mm(h, wq_ref[...])
    raw_lat = mm(h, wl_ref[...])
    cosine, sine = cos_ref[...], sin_ref[...]
    zeros = jnp.zeros((raw.shape[0], 64), BF)
    q = jnp.concatenate([raw[:, :128].astype(BF), turn(raw[:, 128:192], cosine, sine).astype(BF), zeros], axis=1)
    k_rope = turn(raw_lat[:, 512:576], cosine, sine).astype(BF)
    lat = raw_lat[:, :512]
    lat = (lat * lax.rsqrt(jnp.mean(lat * lat, axis=1, keepdims=True) + 1e-6) * lgain_ref[...]).astype(BF)
    expanded = mm(lat, we_ref[...]).astype(BF)
    k = jnp.concatenate([expanded[:, :128], k_rope, zeros], axis=1)
    for e in range(blocks):
        for m in range(batches):
            src = slice((e * batches + m) * here, (e * batches + m + 1) * here)
            dst = slice(e * here, (e + 1) * here)
            q_ref[m, dst] = q[src]
            k_ref[m, dst] = k[src]
            v_ref[m, dst] = expanded[src, 128:]
            lat_ref[m, dst] = lat[src]


def project(x_all, gain, lgain, wq, wl, we, cosine, sine, batches):
    groups, rows, width = x_all.shape
    here = rows // batches
    per = 4
    seq = groups * here
    shape = jax.ShapeDtypeStruct

    def whole(v):
        return pl.BlockSpec(v.shape, lambda i: (0, 0))

    def by_seq(w):
        return pl.BlockSpec((batches, per * here, w), lambda i: (0, i, 0))

    table = pl.BlockSpec((per * rows, 32), lambda i: (i, 0))
    return pl.pallas_call(
        project_kernel,
        grid=(groups // per,),
        out_shape=(shape((groups * rows, width), BF), shape((batches, seq, 256), BF), shape((batches, seq, 256), BF),
                   shape((batches, seq, 128), BF), shape((batches, seq, 512), BF)),
        in_specs=[pl.BlockSpec((per, rows, width), lambda i: (i, 0, 0)), whole(gain), whole(lgain), whole(wq), whole(wl), whole(we),
                  table, table],
        out_specs=[pl.BlockSpec((per * rows, width), lambda i: (i, 0)), by_seq(256), by_seq(256), by_seq(128), by_seq(512)],
        compiler_params=pltpu.CompilerParams(vmem_limit_bytes=48 * 1024 * 1024),
        cost_estimate=pl.CostEstimate(flops=7_000_000_000, bytes_accessed=20_000_000, transcendentals=0),
        name="project",
    )(x_all, gain, lgain, wq, wl, we, cosine, sine)


ROWS = 256
SCALE = 192.0 ** -0.5


def held_scores(q, k, first, length):
    s = mm_t(q, k) * SCALE
    t = lax.broadcasted_iota(jnp.int32, s.shape, 0) + first
    u = lax.broadcasted_iota(jnp.int32, s.shape, 1)
    return jnp.where((u <= t) & (u < length), s, -1e30)


def attend_kernel(len_ref, q_ref, k_ref, v_ref, wo_ref, part_ref, att_ref, lse_ref):
    length = len_ref[pl.program_id(0)]
    seq = q_ref.shape[1]
    groups, _, here, width = part_ref.shape
    for i in range(seq // ROWS):
        tile = slice(i * ROWS, (i + 1) * ROWS)
        ext = (i + 1) * ROWS
        s = held_scores(q_ref[0, tile], k_ref[0, :ext], i * ROWS, length)
        peak = jnp.max(s, axis=1, keepdims=True)
        raised = jnp.exp(s - peak)
        total = jnp.sum(raised, axis=1, keepdims=True)
        lse_ref[0, tile] = peak + jnp.log(total)
        p = (raised / total).astype(BF)
        att = mm(p, v_ref[0, :ext]).astype(BF)
        per = ROWS // here
        att_ref[i * per:(i + 1) * per, 0] = att.reshape(per, here, att.shape[1])
        for j in range(width // 512):
            cols = slice(j * 512, (j + 1) * 512)
            part_ref[i * per:(i + 1) * per, 0, :, cols] = mm(att, wo_ref[:, cols]).astype(BF).reshape(per, here, 512)


def attend(lengths, q, k, v, wo, groups):
    batches, seq, _ = q.shape
    here = seq // groups
    width = wo.shape[1]
    shape = jax.ShapeDtypeStruct

    def by_seq(w):
        return pl.BlockSpec((1, seq, w), lambda m: (m, 0, 0))

    def by_dev(w):
        return pl.BlockSpec((groups, 1, here, w), lambda m: (0, m, 0, 0))

    return pl.pallas_call(
        attend_kernel,
        grid=(batches,),
        out_shape=(shape((groups, batches, here, width), BF), shape((groups, batches, here, 128), BF),
                   shape((batches, seq, 1), F32)),
        in_specs=[pl.BlockSpec(memory_space=pltpu.SMEM), by_seq(256), by_seq(256), by_seq(128),
                  pl.BlockSpec(wo.shape, lambda m: (0, 0))],
        out_specs=[by_dev(width), by_dev(128), by_seq(1)],
        compiler_params=pltpu.CompilerParams(vmem_limit_bytes=48 * 1024 * 1024),
        cost_estimate=pl.CostEstimate(flops=4_000_000_000, bytes_accessed=15_000_000, transcendentals=2_000_000),
        name="attend",
    )(lengths, q, k, v, wo)


def attend_back_kernel(len_ref, dout_ref, q_ref, k_ref, v_ref, lat_ref, att_ref, lse_ref, wo_ref, wq_ref, we_ref,
                       cos_ref, sin_ref, part_ref, dq_ref, gwo_ref, gwe_ref, dk, dv, datt):
    m = pl.program_id(0)
    length = len_ref[m]
    seq = q_ref.shape[1]
    groups, _, here, width = dout_ref.shape
    per = ROWS // here

    @pl.when(m == 0)
    def _():
        gwo_ref[...] = jnp.zeros_like(gwo_ref)
        gwe_ref[...] = jnp.zeros_like(gwe_ref)

    for j in range(4):
        blocks = slice(j * groups // 4, (j + 1) * groups // 4)
        dout = dout_ref[blocks].reshape(seq // 4, width)
        rows = slice(j * seq // 4, (j + 1) * seq // 4)
        datt[rows] = mm_t(dout, wo_ref[...]).astype(BF)
        gwo_ref[...] += mm_lead(att_ref[blocks].reshape(seq // 4, 128), dout)
    dk[...] = jnp.zeros_like(dk)
    dv[...] = jnp.zeros_like(dv)
    for i in range(seq // ROWS):
        tile = slice(i * ROWS, (i + 1) * ROWS)
        ext = (i + 1) * ROWS
        q = q_ref[0, tile]
        p = jnp.exp(held_scores(q, k_ref[0, :ext], i * ROWS, length) - lse_ref[0, tile])
        da = datt[tile]
        dp = mm_t(da, v_ref[0, :ext])
        inner = jnp.sum(dp * p, axis=1, keepdims=True)
        ds = (p * (dp - inner)).astype(BF)
        dq = mm(ds, k_ref[0, :ext]) * SCALE
        dk[:ext] += mm_lead(ds, q)
        dv[:ext] += mm_lead(p.astype(BF), da)
        rope = turn(dq[:, 128:192], cos_ref[tile], -sin_ref[tile])
        dq = jnp.concatenate([dq[:, :128].astype(BF), rope.astype(BF), jnp.zeros((ROWS, 64), BF)], axis=1)
        dq_ref[i * per:(i + 1) * per, 0] = dq.reshape(per, here, 256)
        for j in range(width // 512):
            cols = slice(j * 512, (j + 1) * 512)
            part_ref[i * per:(i + 1) * per, 0, :, cols] = mm_t(dq, wq_ref[cols]).astype(BF).reshape(per, here, 512)
    for i in range(seq // ROWS):
        tile = slice(i * ROWS, (i + 1) * ROWS)
        d_k = dk[tile] * SCALE
        d_exp = jnp.concatenate([d_k[:, :128].astype(BF), dv[tile].astype(BF)], axis=1)
        gwe_ref[...] += mm_lead(lat_ref[0, tile], d_exp)
        d_lat = mm_t(d_exp, we_ref[...]).astype(BF)
        tail = jnp.concatenate([d_lat, d_k[:, 128:].astype(BF)], axis=1)
        pad = part_ref.shape[3] - width - tail.shape[1]
        if pad > 0:
            tail = jnp.concatenate([tail, jnp.zeros((ROWS, pad), BF)], axis=1)
        part_ref[i * per:(i + 1) * per, 0, :, width:] = tail[:, :part_ref.shape[3] - width].reshape(per, here, -1)


def attend_back(lengths, dout, q, k, v, lat, att, lse, wo, wq, we, cosine, sine, tail):
    groups, batches, here, width = dout.shape
    seq = groups * here
    shape = jax.ShapeDtypeStruct

    def by_seq(w):
        return pl.BlockSpec((1, seq, w), lambda m: (m, 0, 0))

    def by_dev(w):
        return pl.BlockSpec((groups, 1, here, w), lambda m: (0, m, 0, 0))

    def whole(v):
        return pl.BlockSpec(v.shape, lambda m: (0, 0))

    return pl.pallas_call(
        attend_back_kernel,
        grid=(batches,),
        out_shape=(shape((groups, batches, here, width + tail), BF), shape((groups, batches, here, 256), BF),
                   shape(wo.shape, F32), shape(we.shape, F32)),
        in_specs=[pl.BlockSpec(memory_space=pltpu.SMEM), by_dev(width), by_seq(256), by_seq(256), by_seq(128),
                  by_seq(512), by_dev(128), by_seq(1), whole(wo), whole(wq), whole(we), whole(cosine), whole(sine)],
        out_specs=[by_dev(width + tail), by_dev(256), whole(wo), whole(we)],
        scratch_shapes=[pltpu.VMEM((seq, 256), F32), pltpu.VMEM((seq, 128), F32), pltpu.VMEM((seq, 128), BF)],
        compiler_params=pltpu.CompilerParams(vmem_limit_bytes=56 * 1024 * 1024),
        cost_estimate=pl.CostEstimate(flops=14_000_000_000, bytes_accessed=25_000_000, transcendentals=2_000_000),
        name="attend_back",
    )(lengths, dout, q, k, v, lat, att, lse, wo, wq, we, cosine, sine)


H = 16
QK_NOPE = 128
ROPE = 64
V_DIM = 128
KV_RANK = 512
GROUPS = 16
EPSILON = 1e-06
ROTARY_BASE = 10000.0


def product(left_side, right_side):
    return jnp.dot(left_side, right_side, preferred_element_type=F32)


def product_lead(left_side, right_side):
    return lax.dot_general(
        left_side, right_side, (((0,), (0,)), ((), ())), preferred_element_type=F32
    )


def product_trail(left_side, right_side):
    return lax.dot_general(
        left_side, right_side, (((1,), (1,)), ((), ())), preferred_element_type=F32
    )


def rotary_tables(positions):
    half_width = ROPE // 2
    frequency = ROTARY_BASE ** (-jnp.arange(half_width, dtype=F32) * 2.0 / ROPE)
    angles = positions[:, None] * frequency[None, :]
    return (jnp.cos(angles), jnp.sin(angles))


def rotate(values, cosine, sine_table):
    first_half, second_half = jnp.split(values, 2, axis=-1)
    return jnp.concatenate(
        [
            first_half * cosine - second_half * sine_table,
            second_half * cosine + first_half * sine_table,
        ],
        axis=-1,
    )


def norm_forward(values, gains):
    factor = lax.rsqrt(jnp.mean(values * values, axis=-1, keepdims=True) + EPSILON)
    normed = values * factor
    return (normed * gains, normed, factor)


def norm_backward(gradient, normed, factor, gains):
    gain_grad = jnp.sum(gradient * normed, axis=0)
    scaled = gradient * gains
    return (
        factor * (scaled - normed * jnp.mean(scaled * normed, axis=-1, keepdims=True)),
        gain_grad,
    )


def selected_experts(routes):
    chosen = routes[:, :, None] == jnp.arange(GROUPS, dtype=routes.dtype)
    return jnp.any(chosen, axis=1)


def masked_softmax(logits, mask):
    held = jnp.where(mask, logits, -1e30)
    peak = jnp.max(held, axis=-1, keepdims=True)
    raised = jnp.where(mask, jnp.exp(held - peak), 0.0)
    return raised / jnp.sum(raised, axis=-1, keepdims=True)


def per_device(
    layer_input,
    out_cotangent,
    lengths,
    routes,
    attn_gain,
    query_weight,
    latent_weight,
    latent_gain,
    expand_weight,
    output_weight,
    mixer_gain,
    router_weight,
    gate_weight,
    up_weight,
    down_weight,
    shared_gate,
    shared_up,
    shared_down,
):
    dp = lax.axis_size("dp")
    me = lax.axis_index("expert")
    plane = lax.axis_index("dp")
    batches, _, here, width = layer_input.shape
    own = batches * here
    total = own * GROUPS
    seq_total = here * GROUPS
    rows_w = query_weight.shape[0]
    rows_l = expand_weight.shape[0]

    x_own = layer_input.reshape(own, width)
    routes_own = routes.reshape(own, -1)
    choices = routes_own.shape[1]
    route_columns = routes_own.astype(BF).reshape(rows_w, -1)
    small_width = -(-(595 + route_columns.shape[1]) // 128) * 128
    latent_column = jnp.zeros((rows_w,), BF).at[:rows_l].set(latent_gain)
    small = jnp.concatenate(
        [
            latent_weight,
            router_weight,
            attn_gain[:, None],
            mixer_gain[:, None],
            latent_column[:, None],
            route_columns,
            jnp.zeros((rows_w, small_width - 595 - route_columns.shape[1]), BF),
        ],
        axis=1,
    )
    query_parts = query_weight.reshape(rows_w, H, QK_NOPE + ROPE).transpose(1, 0, 2)
    expand_parts = expand_weight.reshape(rows_l, H, QK_NOPE + V_DIM).transpose(1, 0, 2)
    parts = jnp.concatenate([query_parts, expand_parts.reshape(H, rows_w, ROPE)], axis=2)
    x_all, small, parts_head, output_head = opening(dp, x_own, small, parts, output_weight, 1)
    x_all = x_all.reshape(total, width)
    routes_all = lax.dynamic_index_in_dim(small, plane, 0, False)[..., 595 : 595 + route_columns.shape[1]]
    routes_all = routes_all.reshape(total, choices).astype(jnp.int32)
    small = small.reshape(width, small_width)
    parts_head = parts_head.reshape(width, TILE)
    latent_full = small[:, :576]
    router_full = small[:, 576:592]
    gain_attn = small[:, 592].astype(F32)
    gain_mixer = small[:, 593].astype(F32)
    gain_latent = small[:, 594].reshape(dp * GROUPS, rows_w)[:, :rows_l].reshape(-1).astype(F32)
    expand_head = parts_head[:, QK_NOPE + ROPE :].reshape(KV_RANK, QK_NOPE + V_DIM)
    output_head = output_head.reshape(V_DIM, width)

    share_own = jnp.concatenate([shared_gate.T, shared_up.T, shared_down], axis=0)
    share_width = shared_down.shape[0]
    gate_full = lax.all_gather(gate_weight[0], "dp", axis=0, tiled=True)
    up_full = lax.all_gather(up_weight[0], "dp", axis=0, tiled=True)
    down_full = lax.all_gather(down_weight[0], "dp", axis=0, tiled=True)
    share_full = lax.all_gather(share_own, "dp", axis=0)
    share_full = share_full.transpose(1, 0, 2).reshape(3 * share_width, width)

    seq_lengths = lengths.reshape(batches)
    own_positions = me * here + jnp.arange(here, dtype=jnp.int32)
    valid_own = (own_positions[None, :] < seq_lengths[:, None]).reshape(own).astype(F32)
    all_positions = jnp.arange(seq_total, dtype=jnp.int32).reshape(GROUPS, 1, here)
    valid_all = jnp.broadcast_to(
        all_positions < seq_lengths[None, :, None], (GROUPS, batches, here)
    ).reshape(total)
    key_positions = jnp.arange(seq_total, dtype=jnp.int32)
    cosine, sine_table = rotary_tables(key_positions.astype(F32))
    cosine_own = lax.dynamic_slice_in_dim(cosine, me * here, here)
    sine_own = lax.dynamic_slice_in_dim(sine_table, me * here, here)

    def by_sequence(v):
        return v.reshape(GROUPS, batches, here, v.shape[-1]).swapaxes(0, 1).reshape(batches, seq_total, -1)

    def by_device(v):
        return v.reshape(batches, GROUPS, here, v.shape[-1]).swapaxes(0, 1).reshape(total, -1)

    grad_own = out_cotangent.reshape(own, width) * valid_own[:, None].astype(BF)
    taken = jnp.any(routes_all == me, axis=1) & valid_all
    places = jnp.cumsum(taken.reshape(-1, here).astype(jnp.int32), axis=1) - 1
    places = places + 32 * (jnp.arange(places.shape[0], dtype=jnp.int32) % 4)[:, None]
    slot = jnp.where(taken, places.reshape(total), -1)

    def by_token(table):
        return jnp.broadcast_to(
            table.reshape(GROUPS, 1, here, -1), (GROUPS, batches, here, table.shape[1])).reshape(total, -1)

    hidden_all, query, key, values, latent = project(
        x_all.reshape(GROUPS, own, width), gain_attn[None], gain_latent[None], parts_head, small, expand_head,
        by_token(cosine), by_token(sine_table), batches)
    attn_part, attended, log_total = attend(seq_lengths, query, key, values, output_head, GROUPS)
    attn_part = attn_part.reshape(GROUPS, own, width)
    attn_out = scatter16(attn_part, 2)

    x_wide = x_own.astype(F32)
    middle = x_wide + attn_out
    normed_mix, unit_mix, factor_mix = norm_forward(middle, gain_mixer)
    hidden_mix = normed_mix.astype(BF)
    mix_all = gather16(hidden_mix, 3).reshape(total, width)

    pad = TILE - share_width
    fan_share = jnp.concatenate(
        [share_full[:share_width], router_full.T, jnp.zeros((pad - GROUPS, width), BF),
         share_full[share_width : 2 * share_width], jnp.zeros((pad, width), BF)], axis=0)
    down_share = jnp.concatenate([share_full[2 * share_width :], jnp.zeros((pad, width), BF)], axis=0)
    lane = jnp.arange(128)[None, :]
    pick = jnp.concatenate([lane == me, lane == me + GROUPS], axis=1).astype(F32)
    out_part, rows, hidden, act, slope, result, share_hidden, share_act, share_slope, gates, grad_all = mixture_forward(
        pick, mix_all, routes_all, slot, valid_all.astype(F32)[:, None],
        gate_full, up_full, down_full, fan_share, down_share, grad_own, 4)
    grad_all = grad_all.reshape(total, width)
    mix_part, grad_result, grad_gate_in, grad_up_in, grad_share_in, mixed = mixture_backward(
        pick, grad_all, slot, gate_full, up_full, down_full, fan_share, down_share, act, slope, result,
        share_act, share_slope, gates, out_part.reshape(GROUPS, own, width), 8)
    grad_down = product_lead(hidden, grad_result).astype(BF)
    grad_gate = product_lead(rows, grad_gate_in).astype(BF)
    grad_up = product_lead(rows, grad_up_in).astype(BF)
    grad_share_fan = product_lead(grad_share_in, mix_all).astype(BF)
    grad_share_down = product_lead(share_hidden, grad_all).astype(BF)
    mix_part, grad_down, grad_gate, grad_up = lax.optimization_barrier((mix_part, grad_down, grad_gate, grad_up))
    mix_sum = scatter16(mix_part.reshape(GROUPS, own, width + 128), 5)
    layer_output = valid_own[:, None] * (middle + mixed)

    out_down = lax.psum_scatter(grad_down, "dp", scatter_dimension=0, tiled=True)
    out_gate = lax.psum_scatter(grad_gate, "dp", scatter_dimension=0, tiled=True)
    out_up = lax.psum_scatter(grad_up, "dp", scatter_dimension=0, tiled=True)
    grad_share = jnp.concatenate(
        [grad_share_fan[:share_width], grad_share_fan[TILE : TILE + share_width], grad_share_down[:share_width]],
        axis=0)
    grad_share = grad_share.reshape(3 * share_width, dp, width // dp).swapaxes(0, 1)
    out_share = lax.psum_scatter(grad_share, "dp", scatter_dimension=0, tiled=False).astype(F32)

    mask_own = selected_experts(routes_own)
    soft_own = masked_softmax(product(hidden_mix, router_full), mask_own)
    grad_masked = (mix_sum[:, width : width + GROUPS] + mix_sum[:, width + GROUPS : width + 2 * GROUPS])
    grad_masked = grad_masked * valid_own[:, None]
    grad_logits = soft_own * (grad_masked - jnp.sum(grad_masked * soft_own, axis=1, keepdims=True))
    grad_logits = grad_logits.astype(BF)
    grad_mix = mix_sum[:, :width] + product_trail(grad_logits, router_full)
    grad_middle_norm, grad_gain_mixer = norm_backward(grad_mix, unit_mix, factor_mix, gain_mixer)
    grad_middle = grad_own.astype(F32) + grad_middle_norm

    grad_attn_all = gather16(grad_middle.astype(BF), 6).reshape(GROUPS, batches, here, width)
    back_part, grad_query, grad_output, grad_expand = attend_back(
        seq_lengths, grad_attn_all, query, key, values, latent, attended, log_total, output_head, parts_head,
        expand_head, cosine, sine_table, 640)
    grad_query_w = product_lead(hidden_all, grad_query.reshape(total, TILE)).astype(BF)
    parts_grad = jnp.concatenate(
        [grad_query_w[:, : QK_NOPE + ROPE], grad_expand.astype(BF).reshape(width, ROPE)], axis=1)
    back_sum, out_parts, out_output = returning(
        dp, back_part.reshape(GROUPS, own, back_part.shape[3]),
        parts_grad.reshape(dp, GROUPS, rows_w, TILE), grad_output.astype(BF).reshape(dp, rows_w, width), 7)
    out_query = out_parts[..., : QK_NOPE + ROPE].transpose(1, 0, 2).reshape(rows_w, -1)
    out_expand = out_parts[..., QK_NOPE + ROPE :].reshape(H, rows_l, QK_NOPE + V_DIM)
    out_expand = out_expand.transpose(1, 0, 2).reshape(rows_l, -1)

    x_normed, unit_attn, factor_attn = norm_forward(x_wide, gain_attn)
    hidden_own = x_normed.astype(BF)
    latent_own = product(hidden_own, latent_full)
    _, unit_latent, factor_latent = norm_forward(latent_own[:, :KV_RANK], gain_latent)
    grad_latent_in, grad_gain_latent = norm_backward(
        back_sum[:, width : width + KV_RANK], unit_latent, factor_latent, gain_latent
    )
    grad_rope = back_sum[:, width + KV_RANK : width + KV_RANK + ROPE].reshape(batches, here, ROPE)
    grad_rope = rotate(grad_rope, cosine_own, -sine_own).reshape(own, ROPE)
    grad_latent_raw = jnp.concatenate([grad_latent_in, grad_rope], axis=1).astype(BF)
    grad_hidden_attn = back_sum[:, :width] + product_trail(grad_latent_raw, latent_full)
    grad_input_norm, grad_gain_attn = norm_backward(grad_hidden_attn, unit_attn, factor_attn, gain_attn)
    grad_input = grad_middle + grad_input_norm

    latent_rows = grad_gain_latent.reshape(dp * GROUPS, rows_l)
    latent_rows = jnp.pad(latent_rows, ((0, 0), (0, rows_w - rows_l))).reshape(width, 1)
    tokens_side = jnp.concatenate([hidden_own, hidden_mix], axis=0)
    grads_side = jnp.concatenate(
        [jnp.pad(grad_latent_raw, ((0, 0), (0, 64))), jnp.pad(grad_logits, ((0, 0), (576, 640 - 592)))], axis=0)
    lane = jnp.arange(640)[None, :]
    small_grad = product_lead(tokens_side, grads_side)
    small_grad = small_grad + jnp.where(lane == 592, grad_gain_attn[:, None], 0.0)
    small_grad = small_grad + jnp.where(lane == 593, grad_gain_mixer[:, None], 0.0)
    small_grad = (small_grad + jnp.where(lane == 594, latent_rows, 0.0)).astype(BF)
    small_grad = small_grad.reshape(dp, GROUPS, rows_w, 640).swapaxes(0, 1).reshape(GROUPS, dp * rows_w, 640)
    small_sum = closing(dp, small_grad, 9)

    def as_input(v):
        return v.reshape(batches, 1, here, width)

    return (
        as_input(layer_output),
        as_input(grad_input),
        small_sum[:, 592],
        out_query,
        small_sum[:, :576],
        small_sum[:rows_l, 594],
        out_expand,
        out_output,
        small_sum[:, 593],
        small_sum[:, 576:592],
        out_gate.astype(F32)[None],
        out_up.astype(F32)[None],
        out_down.astype(F32)[None],
        out_share[:share_width].T,
        out_share[share_width : 2 * share_width].T,
        out_share[2 * share_width :],
    )


def solution(mesh):
    split = P(("dp", "expert"), None)
    line = P(("dp", "expert"))
    tokens = P(None, "dp", "expert", None)
    expert = P("expert", "dp", None)
    return jax.shard_map(
        per_device,
        mesh=mesh,
        in_specs=(
            tokens, tokens, P(None, "dp"), tokens, line, split, split, line, split, split, line, split,
            expert, expert, expert, P("dp", "expert"), P("dp", "expert"), P("expert", "dp"),
        ),
        out_specs=(
            tokens, tokens, line, split, split, line, split, split, line, split,
            expert, expert, expert, P("dp", "expert"), P("dp", "expert"), P("expert", "dp"),
        ),
        check_vma=False,
    )
```

```python
import functools
import jax
import jax.numpy as jnp
import numpy as np
from jax import lax
from jax.experimental import pallas as pl
from jax.experimental.pallas import tpu as pltpu
from jax.sharding import PartitionSpec as P

MESH = pl.DeviceIdType.MESH
NZ = 4
NE = 16


def place():
    me = lax.axis_index("expert")
    z = me // 4
    x = (me // 2) % 2
    c = me % 2
    return me, z, x, c, me + 1 - 2 * c, me + 2 - 4 * x


def enter(me, z, core, side, dp=1):
    barrier = pltpu.get_barrier_semaphore()
    plane = lax.axis_index("dp")
    for r in range(1, dp):
        pl.semaphore_signal(barrier, inc=1, device_id={"dp": (plane + r) % dp}, device_id_type=MESH)
    for other in (core, side):
        pl.semaphore_signal(barrier, inc=1, device_id={"expert": other}, device_id_type=MESH)

    @pl.when(z < NZ - 1)
    def _():
        pl.semaphore_signal(barrier, inc=1, device_id={"expert": me + 4}, device_id_type=MESH)

    @pl.when(z > 0)
    def _():
        pl.semaphore_signal(barrier, inc=1, device_id={"expert": me - 4}, device_id_type=MESH)

    pl.semaphore_wait(barrier, dp + 1 + (z < NZ - 1).astype(jnp.int32) + (z > 0).astype(jnp.int32))


class Spread:
    def __init__(self, dp, src, out, sems):
        self.dp, self.src, self.out = dp, src, out
        self.own, self.send, self.recv = sems
        self.plane = lax.axis_index("dp")

    @staticmethod
    def scratch(dp):
        dma = pltpu.SemaphoreType.DMA
        return [dma, dma((dp,)), dma((dp,))]

    def out_shape(dp, rows, v):
        return jax.ShapeDtypeStruct((dp, rows, v.shape[1]), v.dtype)

    def copy(self, r):
        return pltpu.make_async_remote_copy(
            src_ref=self.src, dst_ref=self.out.at[self.plane], send_sem=self.send.at[r], recv_sem=self.recv.at[r],
            device_id={"dp": (self.plane + r) % self.dp}, device_id_type=MESH)

    def arrival(self, r):
        p = (self.plane - r + self.dp) % self.dp
        return pltpu.make_async_remote_copy(
            src_ref=self.src, dst_ref=self.out.at[p], send_sem=self.send.at[r], recv_sem=self.recv.at[r],
            device_id={"dp": p}, device_id_type=MESH)

    def start(self):
        for r in range(1, self.dp):
            self.copy(r).start()
        self.kept = pltpu.make_async_copy(self.src, self.out.at[self.plane], self.own)
        self.kept.start()

    def finish(self):
        self.kept.wait()
        for r in range(1, self.dp):
            self.arrival(r).wait_recv()
            self.copy(r).wait_send()


class Swap:
    def __init__(self, dp, src, out, sems):
        self.dp, self.src, self.out = dp, src, out
        self.send, self.recv = sems
        self.plane = lax.axis_index("dp")

    @staticmethod
    def scratch(dp):
        dma = pltpu.SemaphoreType.DMA
        return [dma((dp,)), dma((dp,))]

    def out_shape(dp, rows, v):
        return jax.ShapeDtypeStruct((dp - 1, rows, v.shape[2]), v.dtype)

    def copy(self, r):
        to = (self.plane + r) % self.dp
        return pltpu.make_async_remote_copy(
            src_ref=self.src.at[to], dst_ref=self.out.at[r - 1], send_sem=self.send.at[r], recv_sem=self.recv.at[r],
            device_id={"dp": to}, device_id_type=MESH)

    def start(self):
        for r in range(1, self.dp):
            self.copy(r).start()

    def finish(self):
        for r in range(1, self.dp):
            self.copy(r).wait_recv()
            self.copy(r).wait_send()


def side_job(kind, dp, span, src, out, sems):
    first, rows = span
    part = pl.ds(first, rows)
    return kind(dp, src.at[part] if kind is Spread else src.at[:, part], out, sems)


def enter_all(me, plane, dp):
    barrier = pltpu.get_barrier_semaphore()
    for r in range(1, NE):
        pl.semaphore_signal(
            barrier, inc=1, device_id={"expert": (me + r) % NE}, device_id_type=MESH)
    for r in range(1, dp):
        pl.semaphore_signal(
            barrier, inc=1, device_id={"dp": (plane + r) % dp}, device_id_type=MESH)
    pl.semaphore_wait(barrier, NE - 1 + dp - 1)


class Gather:
    def __init__(self, src, out, chunks, sems, view=lambda ref, b: ref.at[b]):
        self.src, self.out, self.chunks, self.view = src, out, chunks, view
        self.rows = src.shape[0] // chunks
        self.own_sem, self.us, self.ur, self.ds, self.dr, self.xs, self.xr, self.cs, self.cr = sems
        self.me, self.z, self.x, self.c, self.core, self.side = place()

    @staticmethod
    def scratch(chunks):
        dma = pltpu.SemaphoreType.DMA
        return [dma] + [dma((4, chunks))] * 4 + [dma((7, chunks))] * 2 + [dma((14, chunks))] * 2

    def copy(self, block, k, src, send, recv, to):
        src_ref = self.src if src is None else self.view(self.out, src)
        dst_ref = self.view(self.out, block)
        if self.chunks > 1:
            part = pl.ds(k * self.rows, self.rows)
            src_ref, dst_ref = src_ref.at[part], dst_ref.at[part]
        return pltpu.make_async_remote_copy(
            src_ref=src_ref,
            dst_ref=dst_ref,
            send_sem=send, recv_sem=recv,
            device_id={"expert": to}, device_id_type=MESH,
        )

    def up(self, k, s, src=None):
        return self.copy(self.me - 4 * s, k, src, self.us.at[s, k], self.ur.at[s, k], self.me + 4)

    def down(self, k, s, src=None):
        return self.copy(self.me + 4 * s, k, src, self.ds.at[s, k], self.dr.at[s, k], self.me - 4)

    def across(self, k, slot, block, src=None):
        return self.copy(block, k, src, self.xs.at[slot, k], self.xr.at[slot, k], self.side)

    def over(self, k, slot, block, src=None):
        return self.copy(block, k, src, self.cs.at[slot, k], self.cr.at[slot, k], self.core)

    def up_in(self, k, s):
        b = self.me - 4 * s
        return self.copy(b, k, b, self.us.at[s - 1, k], self.ur.at[s - 1, k], self.side)

    def dn_in(self, k, s):
        b = self.me + 4 * s
        return self.copy(b, k, b, self.ds.at[s - 1, k], self.dr.at[s - 1, k], self.side)

    def shift(self, base, slot):
        return base - 4 * slot if slot <= 3 else base + 4 * (slot - 3)

    def core_block(self, slot):
        if slot < 7:
            return self.shift(self.core, slot)
        return self.shift(self.core + 2 - 4 * self.x, slot - 7)

    def has(self, slot):
        slot = slot % 7
        if slot == 0:
            return self.z >= 0
        return self.z >= slot if slot <= 3 else self.z + (slot - 3) <= NZ - 1

    def start(self):
        z, me = self.z, self.me
        self.own = pltpu.make_async_copy(self.src, self.view(self.out, me), self.own_sem)
        self.own.start()
        for k in range(self.chunks):
            self.across(k, 0, me).start()

            @pl.when(z < NZ - 1)
            def _():
                self.up(k, 0).start()

            @pl.when(z > 0)
            def _():
                self.down(k, 0).start()

            self.over(k, 0, me).start()

    def line(self, k, s):
        z, me = self.z, self.me

        @pl.when(z >= s)
        def _():
            b = me - 4 * s
            self.up_in(k, s).wait_recv()
            self.across(k, s, b, b).start()

            @pl.when(z < NZ - 1)
            def _():
                self.up(k, s, b).start()

            self.over(k, s, b, b).start()

        @pl.when(z + s <= NZ - 1)
        def _():
            b = me + 4 * s
            self.dn_in(k, s).wait_recv()
            self.across(k, 3 + s, b, b).start()

            @pl.when(z > 0)
            def _():
                self.down(k, s, b).start()

            self.over(k, 3 + s, b, b).start()

    def from_side(self, k, slot):
        @pl.when(self.has(slot))
        def _():
            b = self.shift(self.side, slot)
            self.across(k, slot, b, b).wait_recv()
            self.over(k, 7 + slot, b, b).start()

    def round(self, s):
        if s < NZ:
            for k in range(self.chunks):
                self.line(k, s)
        for k in range(self.chunks):
            for slot in ((0,) if s == 1 else (s - 1, s + 2)):
                self.from_side(k, slot)

    def finish(self):
        z = self.z
        self.own.wait()
        for k in range(self.chunks):
            for slot in range(14):
                @pl.when(self.has(slot))
                def _():
                    b = self.core_block(slot)
                    self.over(k, slot, b, b).wait_recv()
                    self.over(k, slot, b, b).wait_send()
            for slot in range(7):
                @pl.when(self.has(slot))
                def _():
                    self.across(k, slot, self.me).wait_send()
            for s in range(NZ - 1):
                @pl.when((z >= s) & (z < NZ - 1))
                def _():
                    self.up(k, s).wait_send()

                @pl.when((z + s <= NZ - 1) & (z > 0))
                def _():
                    self.down(k, s).wait_send()


def gather_kernel(chunks, dp, kind, span, x_ref, *refs):
    job = None
    ng = 9
    if kind is None:
        o_ref, *sems = refs
    else:
        src, o_ref, out, *sems = refs
        job = side_job(kind, dp, span, src, out, sems[ng:])
    g = Gather(x_ref, o_ref, chunks, sems[:ng])
    enter(g.me, g.z, g.core, g.side, 1 if job is None else dp)
    g.start()
    if job is not None:
        job.start()
    for s in range(1, NZ + 1):
        g.round(s)
    g.finish()
    if job is not None:
        job.finish()


COST = pl.CostEstimate(flops=0, bytes_accessed=4_000_000, transcendentals=0)
ANY = pl.BlockSpec(memory_space=pl.ANY)


def gather16(v, cid, chunks=4, dp=1, kind=None, span=None, side=None):
    rows, width = v.shape
    extra = kind is not None
    out = pl.pallas_call(
        functools.partial(gather_kernel, chunks, dp, kind, span),
        out_shape=(jax.ShapeDtypeStruct((NE, rows, width), v.dtype),)
        + ((kind.out_shape(dp, span[1], side),) if extra else ()),
        in_specs=[ANY] * (2 if extra else 1),
        out_specs=(ANY,) * (2 if extra else 1),
        scratch_shapes=Gather.scratch(chunks) + (kind.scratch(dp) if extra else []),
        compiler_params=pltpu.CompilerParams(collective_id=cid, has_side_effects=True),
        cost_estimate=COST,
        name="gather16",
    )(*((v, side) if extra else (v,)))
    return out if extra else out[0]


def opening_kernel(dp, chunks, x_ref, small_ref, parts_ref, out_ref,
                   x_all, small_all, parts_head, out_head, small_dp, parts_dp, out_dp, *sems):
    ng = 9
    gx = Gather(x_ref, x_all, chunks, sems[:ng])
    gs = Gather(small_dp, small_all, 1, sems[ng:2 * ng], lambda ref, b: ref.at[:, b])
    loc, ys, yr, ps, pr, os_, or_, pl_sem, ol_sem = sems[2 * ng:]
    me = gx.me
    plane = lax.axis_index("dp")
    enter_all(me, plane, dp)
    pairs = ((small_ref, small_dp.at[plane]), (parts_ref, parts_dp.at[plane]),
             (out_ref, out_dp.at[plane]))

    def lift(i, r):
        src, dst = pairs[i]
        return pltpu.make_async_remote_copy(
            src_ref=src, dst_ref=dst, send_sem=ys.at[i, r], recv_sem=yr.at[i, r],
            device_id={"dp": (plane + r) % dp}, device_id_type=MESH)

    def landed(i, r):
        p = (plane - r + dp) % dp
        dst = (small_dp.at[p], parts_dp.at[p], out_dp.at[p])[i]
        return pltpu.make_async_remote_copy(
            src_ref=dst, dst_ref=dst, send_sem=ys.at[i, r], recv_sem=yr.at[i, r],
            device_id={"dp": p}, device_id_type=MESH)

    def kept(i):
        src, dst = pairs[i]
        return pltpu.make_async_copy(src, dst, loc.at[i])

    for i in range(3):
        for r in range(1, dp):
            lift(i, r).start()
        kept(i).start()
    gx.start()
    gx.round(1)

    kept(0).wait()
    for r in range(1, dp):
        landed(0, r).wait_recv()
    gs.start()

    def part(r):
        h = (me + r) % NE
        return pltpu.make_async_remote_copy(
            src_ref=parts_dp.at[:, h], dst_ref=parts_head.at[:, me],
            send_sem=ps.at[r], recv_sem=pr.at[r],
            device_id={"expert": h}, device_id_type=MESH)

    def part_in(r):
        e = (me - r + NE) % NE
        return pltpu.make_async_remote_copy(
            src_ref=parts_head.at[:, e], dst_ref=parts_head.at[:, e],
            send_sem=ps.at[r], recv_sem=pr.at[r],
            device_id={"expert": e}, device_id_type=MESH)

    def part_kept():
        return pltpu.make_async_copy(parts_dp.at[:, me], parts_head.at[:, me], pl_sem)

    kept(1).wait()
    for r in range(1, dp):
        landed(1, r).wait_recv()
    for r in range(1, NE):
        part(r).start()
    part_kept().start()
    gx.round(2)

    def row(d):
        b = NE * d + me
        return pltpu.make_async_remote_copy(
            src_ref=out_dp.at[d], dst_ref=out_head.at[b % dp],
            send_sem=os_.at[d], recv_sem=or_.at[b % dp],
            device_id={"expert": b // dp}, device_id_type=MESH)

    def row_kept(d):
        b = NE * d + me
        return pltpu.make_async_copy(out_dp.at[d], out_head.at[b % dp], ol_sem.at[d])

    kept(2).wait()
    for r in range(1, dp):
        landed(2, r).wait_recv()
    for d in range(dp):
        home = (NE * d + me) // dp

        @pl.when(home != me)
        def _():
            row(d).start()

        @pl.when(home == me)
        def _():
            row_kept(d).start()

    gs.round(1)
    gx.round(3)
    gs.round(2)
    gx.round(4)
    gs.round(3)
    gs.round(4)

    def row_in(j):
        return pltpu.make_async_remote_copy(
            src_ref=out_head.at[j], dst_ref=out_head.at[j], send_sem=os_.at[j], recv_sem=or_.at[j],
            device_id={"expert": gx.core}, device_id_type=MESH)

    for r in range(1, NE):
        part_in(r).wait_recv()
        part(r).wait_send()
    part_kept().wait()
    for j in range(dp):
        @pl.when((dp * me + j) % NE != me)
        def _():
            row_in(j).wait_recv()
    for d in range(dp):
        home = (NE * d + me) // dp

        @pl.when(home != me)
        def _():
            row(d).wait_send()

        @pl.when(home == me)
        def _():
            row_kept(d).wait()
    for i in range(3):
        for r in range(1, dp):
            lift(i, r).wait_send()
    gx.finish()
    gs.finish()


def opening(dp, x, small, parts, out, cid, chunks=4):
    dma = pltpu.SemaphoreType.DMA
    rows, ws = small.shape
    bf = x.dtype
    wo = out.shape[1]
    shape = jax.ShapeDtypeStruct
    res = pl.pallas_call(
        functools.partial(opening_kernel, dp, chunks),
        out_shape=(
            shape((NE,) + x.shape, bf), shape((dp, NE, rows, ws), bf), shape((dp, NE) + parts.shape[1:], bf),
            shape((dp, rows, wo), bf),
            shape((dp, rows, ws), bf), shape((dp,) + parts.shape, bf), shape((dp, rows, wo), bf),
        ),
        in_specs=[ANY] * 4,
        out_specs=[ANY] * 7,
        scratch_shapes=Gather.scratch(chunks) + Gather.scratch(1) + [
            dma((3,)), dma((3, dp)), dma((3, dp)), dma((NE,)), dma((NE,)), dma((dp,)), dma((dp,)), dma, dma((dp,))],
        compiler_params=pltpu.CompilerParams(collective_id=cid, has_side_effects=True),
        cost_estimate=COST,
        name="opening",
    )(x, small, parts, out)
    return res[:4]


def order(z, i):
    a, b = (3, 2, 1, 0)[i], (3, 2, 0, 1)[i]
    return jnp.where(z == 0, a, jnp.where(z == 1, b, jnp.where(z == 2, 3 - b, 3 - a)))


class Scatter:
    def __init__(self, p_ref, o_ref, chunks, scratch):
        self.p, self.o, self.chunks = p_ref, o_ref, chunks
        (self.cbuf, self.own, self.xbuf, self.ubuf, self.dbuf, self.ld, self.cs, self.cr, self.xs, self.xr,
         self.us, self.ur, self.ds, self.dr) = scratch
        self.rows = o_ref.shape[0] // chunks
        self.me, self.z, self.x, self.c, self.core, self.side = place()

    @staticmethod
    def scratch(rows, width, chunks, bf):
        dma = pltpu.SemaphoreType.DMA
        return [pltpu.VMEM((n, rows, width), bf) for n in (8, 8, 4, 4, 4)] + [
            dma((8,)), dma((8, chunks)), dma((8, chunks))] + [dma((4, chunks))] * 6

    def rng(self, k):
        return pl.ds(k * self.rows, self.rows)

    def column(self, i, j):
        return 4 * order(self.z, i) + 2 * jnp.where(j == 0, 1 - self.x, self.x)

    def remote(self, src, dst, send, recv, to):
        return pltpu.make_async_remote_copy(
            src_ref=src, dst_ref=dst, send_sem=send, recv_sem=recv,
            device_id={"expert": to}, device_id_type=MESH)

    def over(self, i, j, k):
        n = 2 * i + j
        return self.remote(
            self.p.at[self.column(i, j) + 1 - self.c, self.rng(k)], self.cbuf.at[n, self.rng(k)],
            self.cs.at[n, k], self.cr.at[n, k], self.core)

    def load(self, i, j):
        n = 2 * i + j
        return pltpu.make_async_copy(self.p.at[self.column(i, j) + self.c], self.own.at[n], self.ld.at[n])

    def across(self, i, k):
        return self.remote(self.own.at[2 * i, self.rng(k)], self.xbuf.at[i, self.rng(k)],
                           self.xs.at[i, k], self.xr.at[i, k], self.side)

    def up(self, t, i, k):
        return self.remote(self.own.at[2 * i + 1, self.rng(k)], self.ubuf.at[t, self.rng(k)],
                           self.us.at[t, k], self.ur.at[t, k], self.me + 4)

    def down(self, t, i, k):
        return self.remote(self.own.at[2 * i + 1, self.rng(k)], self.dbuf.at[t, self.rng(k)],
                           self.ds.at[t, k], self.dr.at[t, k], self.me - 4)

    def start(self):
        for i in range(NZ):
            for j in range(2):
                self.load(i, j).start()
                for k in range(self.chunks):
                    self.over(i, j, k).start()

    def first(self, i):
        f32 = jnp.float32
        self.load(i, 0).wait()
        for k in range(self.chunks):
            self.over(i, 0, k).wait_recv()
            s = self.rng(k)
            self.own[2 * i, s] = (
                self.own[2 * i, s].astype(f32) + self.cbuf[2 * i, s].astype(f32)).astype(self.own.dtype)
            self.across(i, k).start()

    def second(self, i):
        f32 = jnp.float32
        z, own, o = self.z, self.own, self.o
        t = order(z, i)
        self.load(i, 1).wait()
        for k in range(self.chunks):
            s = self.rng(k)
            self.over(i, 1, k).wait_recv()
            self.across(i, k).wait_recv()

            def base():
                return (own[2 * i + 1, s].astype(f32) + self.cbuf[2 * i + 1, s].astype(f32)
                        + self.xbuf[i, s].astype(f32))

            if i < NZ - 1:
                @pl.when(t > z)
                def _():
                    @pl.when(z > 0)
                    def _():
                        self.up(t, i, k).wait_recv()
                        own[2 * i + 1, s] = (base() + self.ubuf[t, s].astype(f32)).astype(own.dtype)

                    @pl.when(z == 0)
                    def _():
                        own[2 * i + 1, s] = base().astype(own.dtype)

                    self.up(t, i, k).start()

                @pl.when(t < z)
                def _():
                    @pl.when(z < NZ - 1)
                    def _():
                        self.down(t, i, k).wait_recv()
                        own[2 * i + 1, s] = (base() + self.dbuf[t, s].astype(f32)).astype(own.dtype)

                    @pl.when(z == NZ - 1)
                    def _():
                        own[2 * i + 1, s] = base().astype(own.dtype)

                    self.down(t, i, k).start()
            else:
                @pl.when(z > 0)
                def _():
                    self.up(t, i, k).wait_recv()

                @pl.when(z < NZ - 1)
                def _():
                    self.down(t, i, k).wait_recv()

                @pl.when((z > 0) & (z < NZ - 1))
                def _():
                    o[s] = (base() + self.ubuf[t, s].astype(f32) + self.dbuf[t, s].astype(f32)).astype(o.dtype)

                @pl.when(z == 0)
                def _():
                    o[s] = (base() + self.dbuf[t, s].astype(f32)).astype(o.dtype)

                @pl.when(z == NZ - 1)
                def _():
                    o[s] = (base() + self.ubuf[t, s].astype(f32)).astype(o.dtype)

    def run(self):
        self.first(0)
        for i in range(NZ):
            if i + 1 < NZ:
                self.first(i + 1)
            self.second(i)

    def finish(self):
        z = self.z
        for k in range(self.chunks):
            for i in range(NZ):
                self.across(i, k).wait_send()
                for j in range(2):
                    self.over(i, j, k).wait_send()
                if i < NZ - 1:
                    t = order(z, i)

                    @pl.when(t > z)
                    def _():
                        self.up(t, i, k).wait_send()

                    @pl.when(t < z)
                    def _():
                        self.down(t, i, k).wait_send()


def scatter_kernel(chunks, dp, kind, span, p_ref, *refs):
    job = None
    ns = 14
    if kind is None:
        o_ref, *scratch = refs
    else:
        src, o_ref, out, *scratch = refs
        job = side_job(kind, dp, span, src, out, scratch[ns:])
    s = Scatter(p_ref, o_ref, chunks, scratch[:ns])
    enter(s.me, s.z, s.core, s.side, 1 if job is None else dp)
    s.start()
    if job is not None:
        job.start()
    s.run()
    s.finish()
    if job is not None:
        job.finish()


VMEM = pl.BlockSpec(memory_space=pltpu.VMEM)


def scatter16(p, cid, chunks=2, out_dtype=jnp.float32, dp=1, kind=None, span=None, side=None):
    _, rows, width = p.shape
    extra = kind is not None
    out = pl.pallas_call(
        functools.partial(scatter_kernel, chunks, dp, kind, span),
        out_shape=(jax.ShapeDtypeStruct((rows, width), out_dtype),)
        + ((kind.out_shape(dp, span[1], side),) if extra else ()),
        in_specs=[ANY] * (2 if extra else 1),
        out_specs=(VMEM,) + ((ANY,) if extra else ()),
        scratch_shapes=Scatter.scratch(rows, width, chunks, p.dtype) + (kind.scratch(dp) if extra else []),
        compiler_params=pltpu.CompilerParams(
            collective_id=cid, has_side_effects=True, vmem_limit_bytes=60 * 1024 * 1024),
        cost_estimate=COST,
        name="scatter16",
    )(*((p, side) if extra else (p,)))
    return out if extra else out[0]


def return_kernel(dp, chunks, p_ref, parts_ref, rows_ref, o_ref, parts_in, rows_in, parts_far, rows_far, *scratch):
    ns = 14
    s = Scatter(p_ref, o_ref, chunks, scratch[:ns])
    ps, pr, os_, or_, pl_sem, ol_sem, ys, yr = scratch[ns:]
    me = s.me
    plane = lax.axis_index("dp")
    enter_all(me, plane, dp)

    def part(r):
        e = (me + r) % NE
        return pltpu.make_async_remote_copy(
            src_ref=parts_ref.at[:, e], dst_ref=parts_in.at[:, me],
            send_sem=ps.at[r], recv_sem=pr.at[r],
            device_id={"expert": e}, device_id_type=MESH)

    def part_in(r):
        h = (me - r + NE) % NE
        return pltpu.make_async_remote_copy(
            src_ref=parts_in.at[:, h], dst_ref=parts_in.at[:, h],
            send_sem=ps.at[r], recv_sem=pr.at[r],
            device_id={"expert": h}, device_id_type=MESH)

    def part_kept():
        return pltpu.make_async_copy(parts_ref.at[:, me], parts_in.at[:, me], pl_sem)

    def row(j):
        b = dp * me + j
        return pltpu.make_async_remote_copy(
            src_ref=rows_ref.at[j], dst_ref=rows_in.at[b // NE],
            send_sem=os_.at[j], recv_sem=or_.at[b // NE],
            device_id={"expert": b % NE}, device_id_type=MESH)

    def row_kept(j):
        b = dp * me + j
        return pltpu.make_async_copy(rows_ref.at[j], rows_in.at[b // NE], ol_sem.at[j])

    def row_in(d):
        return pltpu.make_async_remote_copy(
            src_ref=rows_in.at[d], dst_ref=rows_in.at[d], send_sem=os_.at[d], recv_sem=or_.at[d],
            device_id={"expert": s.core}, device_id_type=MESH)

    def lift(i, r):
        to = (plane + r) % dp
        src, dst = ((parts_in.at[to], parts_far.at[r - 1]), (rows_in.at[to], rows_far.at[r - 1]))[i]
        return pltpu.make_async_remote_copy(
            src_ref=src, dst_ref=dst, send_sem=ys.at[i, r], recv_sem=yr.at[i, r],
            device_id={"dp": to}, device_id_type=MESH)

    s.start()
    for r in range(1, NE):
        part(r).start()
    part_kept().start()
    for j in range(dp):
        @pl.when((dp * me + j) % NE != me)
        def _():
            row(j).start()

        @pl.when((dp * me + j) % NE == me)
        def _():
            row_kept(j).start()
    s.first(0)
    s.first(1)
    s.second(0)
    for r in range(1, NE):
        part_in(r).wait_recv()
    part_kept().wait()
    for j in range(dp):
        @pl.when((dp * me + j) % NE == me)
        def _():
            row_kept(j).wait()
    for d in range(dp):
        @pl.when((NE * d + me) // dp != me)
        def _():
            row_in(d).wait_recv()
    for i in range(2):
        for r in range(1, dp):
            lift(i, r).start()
    s.first(2)
    s.second(1)
    s.first(3)
    s.second(2)
    s.second(3)
    for i in range(2):
        for r in range(1, dp):
            lift(i, r).wait_recv()
            lift(i, r).wait_send()
    for r in range(1, NE):
        part(r).wait_send()
    for j in range(dp):
        @pl.when((dp * me + j) % NE != me)
        def _():
            row(j).wait_send()
    s.finish()


def returning(dp, p, parts, rows, cid, chunks=2):
    dma = pltpu.SemaphoreType.DMA
    _, n, width = p.shape
    shape = jax.ShapeDtypeStruct
    out, parts_in, rows_in, parts_far, rows_far = pl.pallas_call(
        functools.partial(return_kernel, dp, chunks),
        out_shape=(
            shape((n, width), jnp.float32), shape(parts.shape, parts.dtype), shape(rows.shape, rows.dtype),
            shape((dp - 1,) + parts.shape[1:], parts.dtype), shape((dp - 1,) + rows.shape[1:], rows.dtype)),
        in_specs=[ANY] * 3,
        out_specs=[VMEM] + [ANY] * 4,
        scratch_shapes=Scatter.scratch(n, width, chunks, p.dtype) + [
            dma((NE,)), dma((NE,)), dma((dp,)), dma((dp,)), dma, dma((dp,)), dma((2, dp)), dma((2, dp))],
        compiler_params=pltpu.CompilerParams(
            collective_id=cid, has_side_effects=True, vmem_limit_bytes=60 * 1024 * 1024),
        cost_estimate=COST,
        name="returning",
    )(p, parts, rows)
    plane = lax.axis_index("dp")

    def total(near, far):
        own = lax.dynamic_index_in_dim(near, plane, 0, False).astype(jnp.float32)
        return own + jnp.sum(far.astype(jnp.float32), axis=0)

    return out, total(parts_in, parts_far), total(rows_in, rows_far)


def closing_kernel(dp, chunks, p_ref, o_ref, far_ref, *scratch):
    ns = 14
    s = Scatter(p_ref, o_ref, chunks, scratch[:ns])
    ys, yr = scratch[ns:]
    plane = lax.axis_index("dp")
    rows = o_ref.shape[0] // dp
    enter(s.me, s.z, s.core, s.side, dp)

    def lift(r):
        to = (plane + r) % dp
        return pltpu.make_async_remote_copy(
            src_ref=o_ref.at[pl.ds(pl.multiple_of(to * rows, 16), rows)], dst_ref=far_ref.at[r - 1],
            send_sem=ys.at[r], recv_sem=yr.at[r],
            device_id={"dp": to}, device_id_type=MESH)

    s.start()
    s.run()
    for r in range(1, dp):
        lift(r).start()
    s.finish()
    for r in range(1, dp):
        lift(r).wait_recv()
        lift(r).wait_send()


def closing(dp, p, cid):
    dma = pltpu.SemaphoreType.DMA
    _, n, width = p.shape
    shape = jax.ShapeDtypeStruct
    near, far = pl.pallas_call(
        functools.partial(closing_kernel, dp, 1),
        out_shape=(shape((n, width), p.dtype), shape((dp - 1, n // dp, width), p.dtype)),
        in_specs=[ANY],
        out_specs=[VMEM, VMEM],
        scratch_shapes=Scatter.scratch(n, width, 1, p.dtype) + [dma((dp,)), dma((dp,))],
        compiler_params=pltpu.CompilerParams(
            collective_id=cid, has_side_effects=True, vmem_limit_bytes=32 * 1024 * 1024),
        cost_estimate=COST,
        name="closing",
    )(p)
    own = lax.dynamic_slice_in_dim(near, lax.axis_index("dp") * (n // dp), n // dp).astype(jnp.float32)
    return own + jnp.sum(far.astype(jnp.float32), axis=0)
BF = jnp.bfloat16
F32 = jnp.float32


def mm(a, b):
    return jnp.dot(a, b, preferred_element_type=F32)


def mm_t(a, b):
    return lax.dot_general(a, b, (((1,), (1,)), ((), ())), preferred_element_type=F32)


def silu_pair(gate_in):
    sigmoid = 1.0 / (1.0 + jnp.exp(-gate_in))
    return (gate_in * sigmoid, sigmoid * (1.0 + gate_in * (1.0 - sigmoid)))


TILE = 256
WIDE = 512
SHARE = 176


def down_copies(a_ref, b_ref, out, sem):
    dp, a, _ = a_ref.shape
    rows = a + b_ref.shape[1]
    copies = []
    for d in range(dp):
        copies.append(pltpu.make_async_copy(a_ref.at[d], out.at[pl.ds(d * rows, a)], sem.at[2 * d]))
        copies.append(pltpu.make_async_copy(b_ref.at[d], out.at[pl.ds(d * rows + a, rows - a)], sem.at[2 * d + 1]))
    return copies


def one_hots(slot_row, slot_col, groups, slots):
    to_slot, to_token = [], []
    for g in range(groups):
        row = slot_row[:, g * 256:(g + 1) * 256]
        col = slot_col[g * 256:(g + 1) * 256, :]
        to_slot.append((lax.broadcasted_iota(jnp.int32, (slots, 256), 0) == row).astype(BF))
        to_token.append((lax.broadcasted_iota(jnp.int32, (256, slots), 1) == col).astype(BF))
    return to_slot, to_token


def lanes(j):
    return pl.ds(pl.multiple_of(j * WIDE, WIDE), WIDE)


def over_columns(total, body):
    def step(j, _):
        body(pl.multiple_of(j * WIDE, WIDE), WIDE)
        return 0

    lax.fori_loop(0, total // WIDE, step, 0)
    if total % WIDE:
        body(total // WIDE * WIDE, total % WIDE)


def forward_kernel(chunks, pick_ref, mix_ref, routes_ref, slot_row, slot_col, valid_ref, wg_ref, wu_ref, fan_ref, sd_ref,
                   wda_ref, wdb_ref, dy_ref,
                   out_ref, rows_ref, hid_ref, act_ref, slo_ref, eo_ref, sh_ref, sact_ref, sslo_ref, gate_ref,
                   dy_all, wd_ref, wd_sem, *sems):
    step = pl.program_id(0)
    tokens, width = mix_ref.shape
    groups, slots = tokens // 256, 128
    ff = hid_ref.shape[1]
    g = Gather(dy_ref, dy_all, chunks, sems)

    @pl.when(step == 0)
    def _():
        enter(g.me, g.z, g.core, g.side)
        g.start()
        for copy in down_copies(wda_ref, wdb_ref, wd_ref, wd_sem):
            copy.start()

    mix = mix_ref[...]
    fanned = mm_t(mix, fan_ref[:TILE, :])
    s_up = mm_t(mix, fan_ref[TILE:, :])
    s_act, s_slope = silu_pair(fanned)
    s_hidden = (s_act * s_up).astype(BF)
    sh_ref[...] = s_hidden
    sact_ref[...] = s_act.astype(BF)
    sslo_ref[...] = (s_up * s_slope).astype(BF)
    logits = fanned[:, SHARE:SHARE + 16]
    lane16 = lax.broadcasted_iota(jnp.int32, (tokens, 16), 1)
    mask = lane16 < 0
    for k in range(routes_ref.shape[1]):
        mask = mask | (lane16 == routes_ref[:, k:k + 1])
    held = jnp.where(mask, logits, -1e30)
    raised = jnp.where(mask, jnp.exp(held - jnp.max(held, axis=1, keepdims=True)), 0.0)
    soft = raised / jnp.sum(raised, axis=1, keepdims=True)
    gate = jnp.sum(soft * pick_ref[:, :16], axis=1, keepdims=True) * valid_ref[...]
    gate_ref[...] = gate
    to_slot, to_token = one_hots(slot_row, slot_col, groups, slots)

    def dispatch(j, _):
        for n in range(groups):
            rows_ref[n * slots:(n + 1) * slots, lanes(j)] = mm(
                to_slot[n], mix_ref[n * 256:(n + 1) * 256, lanes(j)]).astype(BF)
        return 0

    lax.fori_loop(0, width // WIDE, dispatch, 0)

    def fan_in(start, size):
        cols = pl.ds(start, size)
        gate_in = mm(rows_ref[...], wg_ref[:, cols])
        up_in = mm(rows_ref[...], wu_ref[:, cols])
        act, slope = silu_pair(gate_in)
        hid_ref[:, cols] = (act * up_in).astype(BF)
        act_ref[:, cols] = act.astype(BF)
        slo_ref[:, cols] = (up_in * slope).astype(BF)

    over_columns(ff, fan_in)

    @pl.when(step == 0)
    def _():
        for copy in down_copies(wda_ref, wdb_ref, wd_ref, wd_sem):
            copy.wait()


    def fan_out(j, _):
        eo = mm(hid_ref[...], wd_ref[:, lanes(j)]).astype(BF)
        eo_ref[:, lanes(j)] = eo
        shared = mm(s_hidden, sd_ref[:, lanes(j)])
        picked = jnp.concatenate(
            [mm(to_token[n], eo[n * slots:(n + 1) * slots]) for n in range(groups)], axis=0)
        out_ref[:, lanes(j)] = (shared + gate * picked).astype(BF)
        return 0

    lax.fori_loop(0, width // WIDE, fan_out, 0)
    steps = pl.num_programs(0)
    for r in range(1, NZ + 1):
        @pl.when(step == r - 1)
        def _():
            g.round(r)

    @pl.when(step == steps - 1)
    def _():
        g.finish()


def backward_kernel(chunks, pick_ref, dy_ref, slot_row, slot_col, wg_ref, wu_ref, fan_ref, sd_ref, wda_ref, wdb_ref,
                    act_ref, slo_ref, eo_ref, sact_ref, sslo_ref, gate_ref, part_ref,
                    dh_ref, deo_ref, dg_ref, du_ref, ds_ref, sum_ref, wd_ref, wd_sem, *scratch):
    step = pl.program_id(0)
    tokens, width = dy_ref.shape
    groups, slots = tokens // 256, 128
    ff = dg_ref.shape[1]
    sc = Scatter(part_ref, sum_ref, chunks, scratch)

    @pl.when(step == 0)
    def _():
        enter(sc.me, sc.z, sc.core, sc.side)
        for copy in down_copies(wda_ref, wdb_ref, wd_ref, wd_sem):
            copy.start()
        sc.start()

    d_sh = mm_t(dy_ref[...], sd_ref[...])
    ds_ref[:, :TILE] = (d_sh * sslo_ref[...].astype(F32)).astype(BF)
    ds_ref[:, TILE:] = (d_sh * sact_ref[...].astype(F32)).astype(BF)
    to_slot, to_token = one_hots(slot_row, slot_col, groups, slots)
    gate = gate_ref[...]

    def dispatch(j, total):
        dy = dy_ref[:, lanes(j)].astype(F32)
        gated = (gate * dy).astype(BF)
        for n in range(groups):
            deo_ref[n * slots:(n + 1) * slots, lanes(j)] = mm(to_slot[n], gated[n * 256:(n + 1) * 256]).astype(BF)
        picked = jnp.concatenate(
            [mm(to_token[n], eo_ref[n * slots:(n + 1) * slots, lanes(j)]) for n in range(groups)], axis=0)
        return total + jnp.sum(dy * picked, axis=1, keepdims=True)

    d_gates = lax.fori_loop(0, width // WIDE, dispatch, jnp.zeros((tokens, 1), F32))

    @pl.when(step == 0)
    def _():
        sc.first(0)
        sc.first(1)
        for copy in down_copies(wda_ref, wdb_ref, wd_ref, wd_sem):
            copy.wait()

    def back_out(start, size):
        cols = pl.ds(start, size)
        d_eh = mm_t(deo_ref[...], wd_ref[cols, :])
        dg_ref[:, cols] = (d_eh * slo_ref[:, cols].astype(F32)).astype(BF)
        du_ref[:, cols] = (d_eh * act_ref[:, cols].astype(F32)).astype(BF)

    over_columns(ff, back_out)

    @pl.when(step == 0)
    def _():
        sc.first(2)
        sc.first(3)

    d_s = ds_ref[...]

    def back_in(j, _):
        d_rows = (mm_t(dg_ref[...], wg_ref[lanes(j), :]) + mm_t(du_ref[...], wu_ref[lanes(j), :])).astype(BF)
        shared = mm(d_s, fan_ref[:, lanes(j)])
        taken = jnp.concatenate(
            [mm(to_token[n], d_rows[n * slots:(n + 1) * slots]) for n in range(groups)], axis=0)
        dh_ref[:, lanes(j)] = (shared + taken).astype(BF)
        return 0

    lax.fori_loop(0, width // WIDE, back_in, 0)
    high = d_gates.astype(BF).astype(F32)
    dh_ref[:, width:] = (high * pick_ref[:, :128] + (d_gates - high) * pick_ref[:, 128:]).astype(BF)

    outer = (sc.z == 0) | (sc.z == NZ - 1)
    for i in range(NZ - 1):
        @pl.when((step == i) & outer)
        def _():
            sc.second(i)

        @pl.when((step == min(i + 1, 2)) & jnp.logical_not(outer))
        def _():
            sc.second(i)

    @pl.when(step == 3)
    def _():
        sc.second(3)
        sc.finish()


def whole(v):
    return pl.BlockSpec(v.shape, lambda i: (0, 0), pipeline_mode=pl.Buffered(buffer_count=1))


def tiles(rows, w):
    return pl.BlockSpec((rows, w), lambda i: (i, 0))


def mixture_forward(pick, mix, routes, slot, valid, wg, wu, wda, wdb, fan, sd, dy, cid, chunks=2):
    total, width = mix.shape
    step, half = total // 4, total // 8
    ff = wg.shape[1]
    shape = jax.ShapeDtypeStruct
    rows = total // 2
    return pl.pallas_call(
        functools.partial(forward_kernel, chunks),
        grid=(4,),
        out_shape=(
            shape((total, width), BF), shape((rows, width), BF), shape((rows, ff), BF), shape((rows, ff), BF),
            shape((rows, ff), BF), shape((rows, width), BF), shape((total, TILE), BF), shape((total, TILE), BF),
            shape((total, TILE), BF), shape((total, 1), F32), shape((NE,) + dy.shape, BF)),
        in_specs=[whole(pick), tiles(step, width), tiles(step, routes.shape[1]), pl.BlockSpec((1, step), lambda i: (0, i)),
                  tiles(step, 1), tiles(step, 1), whole(wg), whole(wu), whole(fan), whole(sd), ANY, ANY, ANY],
        out_specs=[tiles(step, width), tiles(half, width), tiles(half, ff), tiles(half, ff), tiles(half, ff),
                   tiles(half, width), tiles(step, TILE), tiles(step, TILE), tiles(step, TILE), tiles(step, 1), ANY],
        scratch_shapes=[pltpu.VMEM((ff, width), BF), pltpu.SemaphoreType.DMA((2 * wda.shape[0],))]
        + Gather.scratch(chunks),
        compiler_params=pltpu.CompilerParams(
            collective_id=cid, has_side_effects=True, vmem_limit_bytes=60 * 1024 * 1024),
        cost_estimate=COST,
        name="mixture_forward",
    )(pick, mix, routes, slot[None, :], slot[:, None], valid, wg, wu, fan, sd, wda, wdb, dy)


def mixture_backward(pick, dy, slot, wg, wu, wda, wdb, fan, sd, act, slo, eo, sact, sslo, gate, part, cid, chunks=2):
    total, width = dy.shape
    step, half = total // 4, total // 8
    ff = wg.shape[1]
    shape = jax.ShapeDtypeStruct
    rows = total // 2
    _, own, _ = part.shape
    return pl.pallas_call(
        functools.partial(backward_kernel, chunks),
        grid=(4,),
        out_shape=(
            shape((total, width + 128), BF), shape((rows, width), BF), shape((rows, ff), BF), shape((rows, ff), BF),
            shape((total, 2 * TILE), BF), shape((own, width), F32)),
        in_specs=[whole(pick), tiles(step, width), pl.BlockSpec((1, step), lambda i: (0, i)), tiles(step, 1),
                  whole(wg), whole(wu), whole(fan), whole(sd), ANY, ANY,
                  tiles(half, ff), tiles(half, ff), tiles(half, width), tiles(step, TILE), tiles(step, TILE),
                  tiles(step, 1), ANY],
        out_specs=[tiles(step, width + 128), tiles(half, width), tiles(half, ff), tiles(half, ff),
                   tiles(step, 2 * TILE), pl.BlockSpec((own, width), lambda i: (0, 0))],
        scratch_shapes=[pltpu.VMEM((ff, width), BF), pltpu.SemaphoreType.DMA((2 * wda.shape[0],))]
        + Scatter.scratch(own, width, chunks, BF),
        compiler_params=pltpu.CompilerParams(
            collective_id=cid, has_side_effects=True, vmem_limit_bytes=60 * 1024 * 1024),
        cost_estimate=COST,
        name="mixture_backward",
    )(pick, dy, slot[None, :], slot[:, None], wg, wu, fan, sd, wda, wdb, act, slo, eo, sact, sslo, gate, part)


def mm_lead(a, b):
    return lax.dot_general(a, b, (((0,), (0,)), ((), ())), preferred_element_type=F32)


def turn(v, cosine, sine):
    half = v.shape[1] // 2
    a, b = v[:, :half], v[:, half:]
    return jnp.concatenate([a * cosine - b * sine, b * cosine + a * sine], axis=1)


def project_kernel(x_ref, gain_ref, lgain_ref, wq_ref, wl_ref, we_ref, cos_ref, sin_ref,
                   h_ref, q_ref, k_ref, v_ref, lat_ref):
    blocks = x_ref.shape[0]
    batches, rows, _ = q_ref.shape
    here = rows // blocks
    x = x_ref[...].reshape(blocks * batches * here, x_ref.shape[2]).astype(F32)
    h = x * lax.rsqrt(jnp.mean(x * x, axis=1, keepdims=True) + 1e-6) * gain_ref[...]
    h = h.astype(BF)
    h_ref[...] = h
    raw = mm(h, wq_ref[...])
    raw_lat = mm(h, wl_ref[...])
    cosine, sine = cos_ref[...], sin_ref[...]
    zeros = jnp.zeros((raw.shape[0], 64), BF)
    q = jnp.concatenate([raw[:, :128].astype(BF), turn(raw[:, 128:192], cosine, sine).astype(BF), zeros], axis=1)
    k_rope = turn(raw_lat[:, 512:576], cosine, sine).astype(BF)
    lat = raw_lat[:, :512]
    lat = (lat * lax.rsqrt(jnp.mean(lat * lat, axis=1, keepdims=True) + 1e-6) * lgain_ref[...]).astype(BF)
    expanded = mm(lat, we_ref[...]).astype(BF)
    k = jnp.concatenate([expanded[:, :128], k_rope, zeros], axis=1)
    for e in range(blocks):
        for m in range(batches):
            src = slice((e * batches + m) * here, (e * batches + m + 1) * here)
            dst = slice(e * here, (e + 1) * here)
            q_ref[m, dst] = q[src]
            k_ref[m, dst] = k[src]
            v_ref[m, dst] = expanded[src, 128:]
            lat_ref[m, dst] = lat[src]


def project(x_all, gain, lgain, wq, wl, we, cosine, sine, batches):
    groups, rows, width = x_all.shape
    here = rows // batches
    per = 4
    seq = groups * here
    shape = jax.ShapeDtypeStruct

    def whole(v):
        return pl.BlockSpec(v.shape, lambda i: (0, 0))

    def by_seq(w):
        return pl.BlockSpec((batches, per * here, w), lambda i: (0, i, 0))

    table = pl.BlockSpec((per * rows, 32), lambda i: (i, 0))
    return pl.pallas_call(
        project_kernel,
        grid=(groups // per,),
        out_shape=(shape((groups * rows, width), BF), shape((batches, seq, 256), BF), shape((batches, seq, 256), BF),
                   shape((batches, seq, 128), BF), shape((batches, seq, 512), BF)),
        in_specs=[pl.BlockSpec((per, rows, width), lambda i: (i, 0, 0)), whole(gain), whole(lgain), whole(wq), whole(wl), whole(we),
                  table, table],
        out_specs=[pl.BlockSpec((per * rows, width), lambda i: (i, 0)), by_seq(256), by_seq(256), by_seq(128), by_seq(512)],
        compiler_params=pltpu.CompilerParams(vmem_limit_bytes=48 * 1024 * 1024),
        cost_estimate=pl.CostEstimate(flops=7_000_000_000, bytes_accessed=20_000_000, transcendentals=0),
        name="project",
    )(x_all, gain, lgain, wq, wl, we, cosine, sine)


ROWS = 256
SCALE = 192.0 ** -0.5


def held_scores(q, k, first, length):
    s = mm_t(q, k) * SCALE
    t = lax.broadcasted_iota(jnp.int32, s.shape, 0) + first
    u = lax.broadcasted_iota(jnp.int32, s.shape, 1)
    return jnp.where((u <= t) & (u < length), s, -1e30)


def attend_kernel(len_ref, q_ref, k_ref, v_ref, wo_ref, part_ref, att_ref, lse_ref):
    length = len_ref[pl.program_id(0)]
    seq = q_ref.shape[1]
    groups, _, here, width = part_ref.shape
    for i in range(seq // ROWS):
        tile = slice(i * ROWS, (i + 1) * ROWS)
        ext = (i + 1) * ROWS
        s = held_scores(q_ref[0, tile], k_ref[0, :ext], i * ROWS, length)
        peak = jnp.max(s, axis=1, keepdims=True)
        raised = jnp.exp(s - peak)
        total = jnp.sum(raised, axis=1, keepdims=True)
        lse_ref[0, tile] = peak + jnp.log(total)
        p = (raised / total).astype(BF)
        att = mm(p, v_ref[0, :ext]).astype(BF)
        per = ROWS // here
        att_ref[i * per:(i + 1) * per, 0] = att.reshape(per, here, att.shape[1])
        for j in range(width // 512):
            cols = slice(j * 512, (j + 1) * 512)
            part_ref[i * per:(i + 1) * per, 0, :, cols] = mm(att, wo_ref[:, cols]).astype(BF).reshape(per, here, 512)


def attend(lengths, q, k, v, wo, groups):
    batches, seq, _ = q.shape
    here = seq // groups
    width = wo.shape[1]
    shape = jax.ShapeDtypeStruct

    def by_seq(w):
        return pl.BlockSpec((1, seq, w), lambda m: (m, 0, 0))

    def by_dev(w):
        return pl.BlockSpec((groups, 1, here, w), lambda m: (0, m, 0, 0))

    return pl.pallas_call(
        attend_kernel,
        grid=(batches,),
        out_shape=(shape((groups, batches, here, width), BF), shape((groups, batches, here, 128), BF),
                   shape((batches, seq, 1), F32)),
        in_specs=[pl.BlockSpec(memory_space=pltpu.SMEM), by_seq(256), by_seq(256), by_seq(128),
                  pl.BlockSpec(wo.shape, lambda m: (0, 0))],
        out_specs=[by_dev(width), by_dev(128), by_seq(1)],
        compiler_params=pltpu.CompilerParams(vmem_limit_bytes=48 * 1024 * 1024),
        cost_estimate=pl.CostEstimate(flops=4_000_000_000, bytes_accessed=15_000_000, transcendentals=2_000_000),
        name="attend",
    )(lengths, q, k, v, wo)


def attend_back_kernel(len_ref, dout_ref, q_ref, k_ref, v_ref, lat_ref, att_ref, lse_ref, wo_ref, wq_ref, we_ref,
                       cos_ref, sin_ref, part_ref, dq_ref, gwo_ref, gwe_ref, dk, dv, datt):
    m = pl.program_id(0)
    length = len_ref[m]
    seq = q_ref.shape[1]
    groups, _, here, width = dout_ref.shape
    per = ROWS // here

    @pl.when(m == 0)
    def _():
        gwo_ref[...] = jnp.zeros_like(gwo_ref)
        gwe_ref[...] = jnp.zeros_like(gwe_ref)

    for j in range(4):
        blocks = slice(j * groups // 4, (j + 1) * groups // 4)
        dout = dout_ref[blocks].reshape(seq // 4, width)
        rows = slice(j * seq // 4, (j + 1) * seq // 4)
        datt[rows] = mm_t(dout, wo_ref[...]).astype(BF)
        gwo_ref[...] += mm_lead(att_ref[blocks].reshape(seq // 4, 128), dout)
    dk[...] = jnp.zeros_like(dk)
    dv[...] = jnp.zeros_like(dv)
    for i in range(seq // ROWS):
        tile = slice(i * ROWS, (i + 1) * ROWS)
        ext = (i + 1) * ROWS
        q = q_ref[0, tile]
        p = jnp.exp(held_scores(q, k_ref[0, :ext], i * ROWS, length) - lse_ref[0, tile])
        da = datt[tile]
        dp = mm_t(da, v_ref[0, :ext])
        inner = jnp.sum(dp * p, axis=1, keepdims=True)
        ds = (p * (dp - inner)).astype(BF)
        dq = mm(ds, k_ref[0, :ext]) * SCALE
        dk[:ext] += mm_lead(ds, q)
        dv[:ext] += mm_lead(p.astype(BF), da)
        rope = turn(dq[:, 128:192], cos_ref[tile], -sin_ref[tile])
        dq = jnp.concatenate([dq[:, :128].astype(BF), rope.astype(BF), jnp.zeros((ROWS, 64), BF)], axis=1)
        dq_ref[i * per:(i + 1) * per, 0] = dq.reshape(per, here, 256)
        for j in range(width // 512):
            cols = slice(j * 512, (j + 1) * 512)
            part_ref[i * per:(i + 1) * per, 0, :, cols] = mm_t(dq, wq_ref[cols]).astype(BF).reshape(per, here, 512)
    for i in range(seq // ROWS):
        tile = slice(i * ROWS, (i + 1) * ROWS)
        d_k = dk[tile] * SCALE
        d_exp = jnp.concatenate([d_k[:, :128].astype(BF), dv[tile].astype(BF)], axis=1)
        gwe_ref[...] += mm_lead(lat_ref[0, tile], d_exp)
        d_lat = mm_t(d_exp, we_ref[...]).astype(BF)
        tail = jnp.concatenate([d_lat, d_k[:, 128:].astype(BF)], axis=1)
        pad = part_ref.shape[3] - width - tail.shape[1]
        if pad > 0:
            tail = jnp.concatenate([tail, jnp.zeros((ROWS, pad), BF)], axis=1)
        part_ref[i * per:(i + 1) * per, 0, :, width:] = tail[:, :part_ref.shape[3] - width].reshape(per, here, -1)


def attend_back(lengths, dout, q, k, v, lat, att, lse, wo, wq, we, cosine, sine, tail):
    groups, batches, here, width = dout.shape
    seq = groups * here
    shape = jax.ShapeDtypeStruct

    def by_seq(w):
        return pl.BlockSpec((1, seq, w), lambda m: (m, 0, 0))

    def by_dev(w):
        return pl.BlockSpec((groups, 1, here, w), lambda m: (0, m, 0, 0))

    def whole(v):
        return pl.BlockSpec(v.shape, lambda m: (0, 0))

    return pl.pallas_call(
        attend_back_kernel,
        grid=(batches,),
        out_shape=(shape((groups, batches, here, width + tail), BF), shape((groups, batches, here, 256), BF),
                   shape(wo.shape, F32), shape(we.shape, F32)),
        in_specs=[pl.BlockSpec(memory_space=pltpu.SMEM), by_dev(width), by_seq(256), by_seq(256), by_seq(128),
                  by_seq(512), by_dev(128), by_seq(1), whole(wo), whole(wq), whole(we), whole(cosine), whole(sine)],
        out_specs=[by_dev(width + tail), by_dev(256), whole(wo), whole(we)],
        scratch_shapes=[pltpu.VMEM((seq, 256), F32), pltpu.VMEM((seq, 128), F32), pltpu.VMEM((seq, 128), BF)],
        compiler_params=pltpu.CompilerParams(vmem_limit_bytes=56 * 1024 * 1024),
        cost_estimate=pl.CostEstimate(flops=14_000_000_000, bytes_accessed=25_000_000, transcendentals=2_000_000),
        name="attend_back",
    )(lengths, dout, q, k, v, lat, att, lse, wo, wq, we, cosine, sine)


H = 16
QK_NOPE = 128
ROPE = 64
V_DIM = 128
KV_RANK = 512
GROUPS = 16
EPSILON = 1e-06
ROTARY_BASE = 10000.0


def product(left_side, right_side):
    return jnp.dot(left_side, right_side, preferred_element_type=F32)


def product_lead(left_side, right_side):
    return lax.dot_general(
        left_side, right_side, (((0,), (0,)), ((), ())), preferred_element_type=F32
    )


def product_trail(left_side, right_side):
    return lax.dot_general(
        left_side, right_side, (((1,), (1,)), ((), ())), preferred_element_type=F32
    )


def rotary_tables(count):
    frequency = ROTARY_BASE ** (-np.arange(ROPE // 2, dtype=np.float32) * np.float32(2.0) / np.float32(ROPE))
    angles = np.arange(count, dtype=np.float32)[:, None] * frequency.astype(np.float32)[None, :]
    return np.cos(angles).astype(np.float32), np.sin(angles).astype(np.float32)


def rotate(values, cosine, sine_table):
    first_half, second_half = jnp.split(values, 2, axis=-1)
    return jnp.concatenate(
        [
            first_half * cosine - second_half * sine_table,
            second_half * cosine + first_half * sine_table,
        ],
        axis=-1,
    )


def norm_forward(values, gains):
    factor = lax.rsqrt(jnp.mean(values * values, axis=-1, keepdims=True) + EPSILON)
    normed = values * factor
    return (normed * gains, normed, factor)


def norm_backward(gradient, normed, factor, gains):
    gain_grad = jnp.sum(gradient * normed, axis=0)
    scaled = gradient * gains
    return (
        factor * (scaled - normed * jnp.mean(scaled * normed, axis=-1, keepdims=True)),
        gain_grad,
    )


def selected_experts(routes):
    chosen = routes[:, :, None] == jnp.arange(GROUPS, dtype=routes.dtype)
    return jnp.any(chosen, axis=1)


def masked_softmax(logits, mask):
    held = jnp.where(mask, logits, -1e30)
    peak = jnp.max(held, axis=-1, keepdims=True)
    raised = jnp.where(mask, jnp.exp(held - peak), 0.0)
    return raised / jnp.sum(raised, axis=-1, keepdims=True)


def per_device(
    layer_input,
    out_cotangent,
    lengths,
    routes,
    attn_gain,
    query_weight,
    latent_weight,
    latent_gain,
    expand_weight,
    output_weight,
    mixer_gain,
    router_weight,
    gate_weight,
    up_weight,
    down_weight,
    shared_gate,
    shared_up,
    shared_down,
):
    dp = lax.axis_size("dp")
    me = lax.axis_index("expert")
    plane = lax.axis_index("dp")
    batches, _, here, width = layer_input.shape
    own = batches * here
    total = own * GROUPS
    seq_total = here * GROUPS
    rows_w = query_weight.shape[0]
    rows_l = expand_weight.shape[0]

    x_own = layer_input.reshape(own, width)
    routes_own = routes.reshape(own, -1)
    choices = routes_own.shape[1]
    route_columns = routes_own.astype(BF).reshape(rows_w, -1)
    small_width = -(-(595 + route_columns.shape[1]) // 128) * 128
    latent_column = jnp.zeros((rows_w,), BF).at[:rows_l].set(latent_gain)
    small = jnp.concatenate(
        [
            latent_weight,
            router_weight,
            attn_gain[:, None],
            mixer_gain[:, None],
            latent_column[:, None],
            route_columns,
            jnp.zeros((rows_w, small_width - 595 - route_columns.shape[1]), BF),
        ],
        axis=1,
    )
    query_parts = query_weight.reshape(rows_w, H, QK_NOPE + ROPE).transpose(1, 0, 2)
    expand_parts = expand_weight.reshape(rows_l, H, QK_NOPE + V_DIM).transpose(1, 0, 2)
    parts = jnp.concatenate([query_parts, expand_parts.reshape(H, rows_w, ROPE)], axis=2)
    x_all, small, parts_head, output_head = opening(dp, x_own, small, parts, output_weight, 1)
    x_all = x_all.reshape(total, width)
    routes_all = lax.dynamic_index_in_dim(small, plane, 0, False)[..., 595 : 595 + route_columns.shape[1]]
    routes_all = routes_all.reshape(total, choices).astype(jnp.int32)
    small = small.reshape(width, small_width)
    parts_head = parts_head.reshape(width, TILE)
    latent_full = small[:, :576]
    router_full = small[:, 576:592]
    gain_attn = small[:, 592].astype(F32)
    gain_mixer = small[:, 593].astype(F32)
    gain_latent = small[:, 594].reshape(dp * GROUPS, rows_w)[:, :rows_l].reshape(-1).astype(F32)
    expand_head = parts_head[:, QK_NOPE + ROPE :].reshape(KV_RANK, QK_NOPE + V_DIM)
    output_head = output_head.reshape(V_DIM, width)

    ff = gate_weight.shape[2]
    share_own = jnp.concatenate([shared_gate.T, shared_up.T, shared_down], axis=0)
    share_width = shared_down.shape[0]
    gate_full = lax.all_gather(gate_weight[0], "dp", axis=0, tiled=True)
    up_full = lax.all_gather(up_weight[0], "dp", axis=0, tiled=True)
    share_full = lax.all_gather(share_own, "dp", axis=0)
    share_full = share_full.transpose(1, 0, 2).reshape(3 * share_width, width)

    seq_lengths = lengths.reshape(batches)
    own_positions = me * here + jnp.arange(here, dtype=jnp.int32)
    valid_own = (own_positions[None, :] < seq_lengths[:, None]).reshape(own).astype(F32)
    all_positions = jnp.arange(seq_total, dtype=jnp.int32).reshape(GROUPS, 1, here)
    valid_all = jnp.broadcast_to(
        all_positions < seq_lengths[None, :, None], (GROUPS, batches, here)
    ).reshape(total)
    cosine, sine_table = rotary_tables(seq_total)
    cosine_own = lax.dynamic_slice_in_dim(jnp.asarray(cosine), me * here, here)
    sine_own = lax.dynamic_slice_in_dim(jnp.asarray(sine_table), me * here, here)

    grad_own = out_cotangent.reshape(own, width) * valid_own[:, None].astype(BF)
    taken = jnp.any(routes_all == me, axis=1) & valid_all
    places = jnp.cumsum(taken.reshape(-1, here).astype(jnp.int32), axis=1) - 1
    places = places + 32 * (jnp.arange(places.shape[0], dtype=jnp.int32) % 4)[:, None]
    slot = jnp.where(taken, places.reshape(total), -1)

    def by_token(table):
        return jnp.asarray(np.broadcast_to(
            table.reshape(GROUPS, 1, here, -1), (GROUPS, batches, here, table.shape[1])).reshape(total, -1))

    hidden_all, query, key, values, latent = project(
        x_all.reshape(GROUPS, own, width), gain_attn[None], gain_latent[None], parts_head, small, expand_head,
        by_token(cosine), by_token(sine_table), batches)
    attn_part, attended, log_total = attend(seq_lengths, query, key, values, output_head, GROUPS)
    attn_part = attn_part.reshape(GROUPS, own, width)
    down_own = down_weight[0]
    cut = down_own.shape[0] // 32 * 16
    spans = ((0, cut), (cut, down_own.shape[0] - cut))
    attn_out, down_a = scatter16(attn_part, 2, dp=dp, kind=Spread, span=spans[0], side=down_own)

    x_wide = x_own.astype(F32)
    middle = x_wide + attn_out
    normed_mix, unit_mix, factor_mix = norm_forward(middle, gain_mixer)
    hidden_mix = normed_mix.astype(BF)
    mix_all, down_b = gather16(hidden_mix, 3, dp=dp, kind=Spread, span=spans[1], side=down_own)
    mix_all = mix_all.reshape(total, width)

    pad = TILE - share_width
    fan_share = jnp.concatenate(
        [share_full[:share_width], router_full.T, jnp.zeros((pad - GROUPS, width), BF),
         share_full[share_width : 2 * share_width], jnp.zeros((pad, width), BF)], axis=0)
    down_share = jnp.concatenate([share_full[2 * share_width :], jnp.zeros((pad, width), BF)], axis=0)
    lane = jnp.arange(128)[None, :]
    pick = jnp.concatenate([lane == me, lane == me + GROUPS], axis=1).astype(F32)
    out_part, rows, hidden, act, slope, result, share_hidden, share_act, share_slope, gates, grad_all = mixture_forward(
        pick, mix_all, routes_all, slot, valid_all.astype(F32)[:, None],
        gate_full, up_full, down_a, down_b, fan_share, down_share, grad_own, 4)
    grad_all = grad_all.reshape(total, width)
    mix_part, grad_result, grad_gate_in, grad_up_in, grad_share_in, mixed = mixture_backward(
        pick, grad_all, slot, gate_full, up_full, down_a, down_b, fan_share, down_share, act, slope, result,
        share_act, share_slope, gates, out_part.reshape(GROUPS, own, width), 8)
    grad_down = product_lead(hidden, grad_result).astype(BF)
    grad_gate = product_lead(rows, grad_gate_in).astype(BF)
    grad_up = product_lead(rows, grad_up_in).astype(BF)
    grad_share_fan = product_lead(grad_share_in, mix_all).astype(BF)
    grad_share_down = product_lead(share_hidden, grad_all).astype(BF)
    mix_part, grad_down, grad_gate, grad_up = lax.optimization_barrier((mix_part, grad_down, grad_gate, grad_up))
    grad_down = grad_down.reshape(dp, ff // dp, width)
    mix_sum, far_a = scatter16(
        mix_part.reshape(GROUPS, own, width + 128), 5, dp=dp, kind=Swap, span=spans[0], side=grad_down)
    layer_output = valid_own[:, None] * (middle + mixed)

    out_gate = lax.psum_scatter(grad_gate, "dp", scatter_dimension=0, tiled=True)
    out_up = lax.psum_scatter(grad_up, "dp", scatter_dimension=0, tiled=True)
    grad_share = jnp.concatenate(
        [grad_share_fan[:share_width], grad_share_fan[TILE : TILE + share_width], grad_share_down[:share_width]],
        axis=0)
    grad_share = grad_share.reshape(3 * share_width, dp, width // dp).swapaxes(0, 1)
    out_share = lax.psum_scatter(grad_share, "dp", scatter_dimension=0, tiled=False).astype(F32)

    mask_own = selected_experts(routes_own)
    soft_own = masked_softmax(product(hidden_mix, router_full), mask_own)
    grad_masked = (mix_sum[:, width : width + GROUPS] + mix_sum[:, width + GROUPS : width + 2 * GROUPS])
    grad_masked = grad_masked * valid_own[:, None]
    grad_logits = soft_own * (grad_masked - jnp.sum(grad_masked * soft_own, axis=1, keepdims=True))
    grad_logits = grad_logits.astype(BF)
    grad_mix = mix_sum[:, :width] + product_trail(grad_logits, router_full)
    grad_middle_norm, grad_gain_mixer = norm_backward(grad_mix, unit_mix, factor_mix, gain_mixer)
    grad_middle = grad_own.astype(F32) + grad_middle_norm

    grad_attn_all, far_b = gather16(
        grad_middle.astype(BF), 6, dp=dp, kind=Swap, span=spans[1], side=grad_down)
    grad_attn_all = grad_attn_all.reshape(GROUPS, batches, here, width)
    out_down = lax.dynamic_index_in_dim(grad_down, plane, 0, False).astype(F32)
    out_down = out_down + jnp.sum(jnp.concatenate([far_a, far_b], axis=1).astype(F32), axis=0)
    back_part, grad_query, grad_output, grad_expand = attend_back(
        seq_lengths, grad_attn_all, query, key, values, latent, attended, log_total, output_head, parts_head,
        expand_head, jnp.asarray(cosine), jnp.asarray(sine_table), 640)
    grad_query_w = product_lead(hidden_all, grad_query.reshape(total, TILE)).astype(BF)
    parts_grad = jnp.concatenate(
        [grad_query_w[:, : QK_NOPE + ROPE], grad_expand.astype(BF).reshape(width, ROPE)], axis=1)
    back_sum, out_parts, out_output = returning(
        dp, back_part.reshape(GROUPS, own, back_part.shape[3]),
        parts_grad.reshape(dp, GROUPS, rows_w, TILE), grad_output.astype(BF).reshape(dp, rows_w, width), 7)
    out_query = out_parts[..., : QK_NOPE + ROPE].transpose(1, 0, 2).reshape(rows_w, -1)
    out_expand = out_parts[..., QK_NOPE + ROPE :].reshape(H, rows_l, QK_NOPE + V_DIM)
    out_expand = out_expand.transpose(1, 0, 2).reshape(rows_l, -1)

    x_normed, unit_attn, factor_attn = norm_forward(x_wide, gain_attn)
    hidden_own = x_normed.astype(BF)
    latent_own = product(hidden_own, latent_full)
    _, unit_latent, factor_latent = norm_forward(latent_own[:, :KV_RANK], gain_latent)
    grad_latent_in, grad_gain_latent = norm_backward(
        back_sum[:, width : width + KV_RANK], unit_latent, factor_latent, gain_latent
    )
    grad_rope = back_sum[:, width + KV_RANK : width + KV_RANK + ROPE].reshape(batches, here, ROPE)
    grad_rope = rotate(grad_rope, cosine_own, -sine_own).reshape(own, ROPE)
    grad_latent_raw = jnp.concatenate([grad_latent_in, grad_rope], axis=1).astype(BF)
    grad_hidden_attn = back_sum[:, :width] + product_trail(grad_latent_raw, latent_full)
    grad_input_norm, grad_gain_attn = norm_backward(grad_hidden_attn, unit_attn, factor_attn, gain_attn)
    grad_input = grad_middle + grad_input_norm

    latent_rows = grad_gain_latent.reshape(dp * GROUPS, rows_l)
    latent_rows = jnp.pad(latent_rows, ((0, 0), (0, rows_w - rows_l))).reshape(width, 1)
    tokens_side = jnp.concatenate([hidden_own, hidden_mix], axis=0)
    grads_side = jnp.concatenate(
        [jnp.pad(grad_latent_raw, ((0, 0), (0, 64))), jnp.pad(grad_logits, ((0, 0), (576, 640 - 592)))], axis=0)
    lane = jnp.arange(640)[None, :]
    small_grad = product_lead(tokens_side, grads_side)
    small_grad = small_grad + jnp.where(lane == 592, grad_gain_attn[:, None], 0.0)
    small_grad = small_grad + jnp.where(lane == 593, grad_gain_mixer[:, None], 0.0)
    small_grad = (small_grad + jnp.where(lane == 594, latent_rows, 0.0)).astype(BF)
    small_grad = small_grad.reshape(dp, GROUPS, rows_w, 640).swapaxes(0, 1).reshape(GROUPS, dp * rows_w, 640)
    small_sum = closing(dp, small_grad, 9)

    def as_input(v):
        return v.reshape(batches, 1, here, width)

    return (
        as_input(layer_output),
        as_input(grad_input),
        small_sum[:, 592],
        out_query,
        small_sum[:, :576],
        small_sum[:rows_l, 594],
        out_expand,
        out_output,
        small_sum[:, 593],
        small_sum[:, 576:592],
        out_gate.astype(F32)[None],
        out_up.astype(F32)[None],
        out_down[None],
        out_share[:share_width].T,
        out_share[share_width : 2 * share_width].T,
        out_share[2 * share_width :],
    )


def solution(mesh):
    split = P(("dp", "expert"), None)
    line = P(("dp", "expert"))
    tokens = P(None, "dp", "expert", None)
    expert = P("expert", "dp", None)
    return jax.shard_map(
        per_device,
        mesh=mesh,
        in_specs=(
            tokens, tokens, P(None, "dp"), tokens, line, split, split, line, split, split, line, split,
            expert, expert, expert, P("dp", "expert"), P("dp", "expert"), P("expert", "dp"),
        ),
        out_specs=(
            tokens, tokens, line, split, split, line, split, split, line, split,
            expert, expert, expert, P("dp", "expert"), P("dp", "expert"), P("expert", "dp"),
        ),
        check_vma=False,
    )
```

```python
import functools
import jax
import jax.numpy as jnp
import numpy as np
from jax import lax
from jax.experimental import pallas as pl
from jax.experimental.pallas import tpu as pltpu
from jax.sharding import PartitionSpec as P

MESH = pl.DeviceIdType.MESH
NZ = 4
NE = 16


def place():
    me = lax.axis_index("expert")
    z = me // 4
    x = (me // 2) % 2
    c = me % 2
    return me, z, x, c, me + 1 - 2 * c, me + 2 - 4 * x


def enter(me, z, core, side, dp=1):
    barrier = pltpu.get_barrier_semaphore()
    plane = lax.axis_index("dp")
    for r in range(1, dp):
        pl.semaphore_signal(barrier, inc=1, device_id={"dp": (plane + r) % dp}, device_id_type=MESH)
    for other in (core, side):
        pl.semaphore_signal(barrier, inc=1, device_id={"expert": other}, device_id_type=MESH)

    @pl.when(z < NZ - 1)
    def _():
        pl.semaphore_signal(barrier, inc=1, device_id={"expert": me + 4}, device_id_type=MESH)

    @pl.when(z > 0)
    def _():
        pl.semaphore_signal(barrier, inc=1, device_id={"expert": me - 4}, device_id_type=MESH)

    pl.semaphore_wait(barrier, dp + 1 + (z < NZ - 1).astype(jnp.int32) + (z > 0).astype(jnp.int32))


class Spread:
    def __init__(self, dp, src, out, sems):
        self.dp, self.src, self.out = dp, src, out
        self.own, self.send, self.recv = sems
        self.plane = lax.axis_index("dp")

    @staticmethod
    def scratch(dp):
        dma = pltpu.SemaphoreType.DMA
        return [dma, dma((dp,)), dma((dp,))]

    def out_shape(dp, rows, v):
        return jax.ShapeDtypeStruct((dp, rows, v.shape[1]), v.dtype)

    def copy(self, r):
        return pltpu.make_async_remote_copy(
            src_ref=self.src, dst_ref=self.out.at[self.plane], send_sem=self.send.at[r], recv_sem=self.recv.at[r],
            device_id={"dp": (self.plane + r) % self.dp}, device_id_type=MESH)

    def arrival(self, r):
        p = (self.plane - r + self.dp) % self.dp
        return pltpu.make_async_remote_copy(
            src_ref=self.src, dst_ref=self.out.at[p], send_sem=self.send.at[r], recv_sem=self.recv.at[r],
            device_id={"dp": p}, device_id_type=MESH)

    def start(self):
        for r in range(1, self.dp):
            self.copy(r).start()
        self.kept = pltpu.make_async_copy(self.src, self.out.at[self.plane], self.own)
        self.kept.start()

    def finish(self):
        self.kept.wait()
        for r in range(1, self.dp):
            self.arrival(r).wait_recv()
            self.copy(r).wait_send()


class Swap:
    def __init__(self, dp, src, out, sems):
        self.dp, self.src, self.out = dp, src, out
        self.send, self.recv = sems
        self.plane = lax.axis_index("dp")

    @staticmethod
    def scratch(dp):
        dma = pltpu.SemaphoreType.DMA
        return [dma((dp,)), dma((dp,))]

    def out_shape(dp, rows, v):
        return jax.ShapeDtypeStruct((dp - 1, rows, v.shape[2]), v.dtype)

    def copy(self, r):
        to = (self.plane + r) % self.dp
        return pltpu.make_async_remote_copy(
            src_ref=self.src.at[to], dst_ref=self.out.at[r - 1], send_sem=self.send.at[r], recv_sem=self.recv.at[r],
            device_id={"dp": to}, device_id_type=MESH)

    def start(self):
        for r in range(1, self.dp):
            self.copy(r).start()

    def finish(self):
        for r in range(1, self.dp):
            self.copy(r).wait_recv()
            self.copy(r).wait_send()


def side_job(kind, dp, span, src, out, sems):
    first, rows = span
    part = pl.ds(first, rows)
    return kind(dp, src.at[part] if kind is Spread else src.at[:, part], out, sems)


def enter_all(me, plane, dp):
    barrier = pltpu.get_barrier_semaphore()
    for r in range(1, NE):
        pl.semaphore_signal(
            barrier, inc=1, device_id={"expert": (me + r) % NE}, device_id_type=MESH)
    for r in range(1, dp):
        pl.semaphore_signal(
            barrier, inc=1, device_id={"dp": (plane + r) % dp}, device_id_type=MESH)
    pl.semaphore_wait(barrier, NE - 1 + dp - 1)


class Gather:
    def __init__(self, src, out, chunks, sems, view=lambda ref, b: ref.at[b]):
        self.src, self.out, self.chunks, self.view = src, out, chunks, view
        self.rows = src.shape[0] // chunks
        self.own_sem, self.us, self.ur, self.ds, self.dr, self.xs, self.xr, self.cs, self.cr = sems
        self.me, self.z, self.x, self.c, self.core, self.side = place()

    @staticmethod
    def scratch(chunks):
        dma = pltpu.SemaphoreType.DMA
        return [dma] + [dma((4, chunks))] * 4 + [dma((7, chunks))] * 2 + [dma((14, chunks))] * 2

    def copy(self, block, k, src, send, recv, to):
        src_ref = self.src if src is None else self.view(self.out, src)
        dst_ref = self.view(self.out, block)
        if self.chunks > 1:
            part = pl.ds(k * self.rows, self.rows)
            src_ref, dst_ref = src_ref.at[part], dst_ref.at[part]
        return pltpu.make_async_remote_copy(
            src_ref=src_ref,
            dst_ref=dst_ref,
            send_sem=send, recv_sem=recv,
            device_id={"expert": to}, device_id_type=MESH,
        )

    def up(self, k, s, src=None):
        return self.copy(self.me - 4 * s, k, src, self.us.at[s, k], self.ur.at[s, k], self.me + 4)

    def down(self, k, s, src=None):
        return self.copy(self.me + 4 * s, k, src, self.ds.at[s, k], self.dr.at[s, k], self.me - 4)

    def across(self, k, slot, block, src=None):
        return self.copy(block, k, src, self.xs.at[slot, k], self.xr.at[slot, k], self.side)

    def over(self, k, slot, block, src=None):
        return self.copy(block, k, src, self.cs.at[slot, k], self.cr.at[slot, k], self.core)

    def up_in(self, k, s):
        b = self.me - 4 * s
        return self.copy(b, k, b, self.us.at[s - 1, k], self.ur.at[s - 1, k], self.side)

    def dn_in(self, k, s):
        b = self.me + 4 * s
        return self.copy(b, k, b, self.ds.at[s - 1, k], self.dr.at[s - 1, k], self.side)

    def shift(self, base, slot):
        return base - 4 * slot if slot <= 3 else base + 4 * (slot - 3)

    def core_block(self, slot):
        if slot < 7:
            return self.shift(self.core, slot)
        return self.shift(self.core + 2 - 4 * self.x, slot - 7)

    def has(self, slot):
        slot = slot % 7
        if slot == 0:
            return self.z >= 0
        return self.z >= slot if slot <= 3 else self.z + (slot - 3) <= NZ - 1

    def start(self):
        z, me = self.z, self.me
        self.own = pltpu.make_async_copy(self.src, self.view(self.out, me), self.own_sem)
        self.own.start()
        for k in range(self.chunks):
            self.across(k, 0, me).start()

            @pl.when(z < NZ - 1)
            def _():
                self.up(k, 0).start()

            @pl.when(z > 0)
            def _():
                self.down(k, 0).start()

            self.over(k, 0, me).start()

    def line(self, k, s):
        z, me = self.z, self.me

        @pl.when(z >= s)
        def _():
            b = me - 4 * s
            self.up_in(k, s).wait_recv()
            self.across(k, s, b, b).start()

            @pl.when(z < NZ - 1)
            def _():
                self.up(k, s, b).start()

            self.over(k, s, b, b).start()

        @pl.when(z + s <= NZ - 1)
        def _():
            b = me + 4 * s
            self.dn_in(k, s).wait_recv()
            self.across(k, 3 + s, b, b).start()

            @pl.when(z > 0)
            def _():
                self.down(k, s, b).start()

            self.over(k, 3 + s, b, b).start()

    def from_side(self, k, slot):
        @pl.when(self.has(slot))
        def _():
            b = self.shift(self.side, slot)
            self.across(k, slot, b, b).wait_recv()
            self.over(k, 7 + slot, b, b).start()

    def round(self, s):
        if s < NZ:
            for k in range(self.chunks):
                self.line(k, s)
        for k in range(self.chunks):
            for slot in ((0,) if s == 1 else (s - 1, s + 2)):
                self.from_side(k, slot)

    def finish(self):
        z = self.z
        self.own.wait()
        for k in range(self.chunks):
            for slot in range(14):
                @pl.when(self.has(slot))
                def _():
                    b = self.core_block(slot)
                    self.over(k, slot, b, b).wait_recv()
                    self.over(k, slot, b, b).wait_send()
            for slot in range(7):
                @pl.when(self.has(slot))
                def _():
                    self.across(k, slot, self.me).wait_send()
            for s in range(NZ - 1):
                @pl.when((z >= s) & (z < NZ - 1))
                def _():
                    self.up(k, s).wait_send()

                @pl.when((z + s <= NZ - 1) & (z > 0))
                def _():
                    self.down(k, s).wait_send()


def gather_kernel(chunks, dp, kind, span, x_ref, *refs):
    job = None
    ng = 9
    if kind is None:
        o_ref, *sems = refs
    else:
        src, o_ref, out, *sems = refs
        job = side_job(kind, dp, span, src, out, sems[ng:])
    g = Gather(x_ref, o_ref, chunks, sems[:ng])
    enter(g.me, g.z, g.core, g.side, 1 if job is None else dp)
    g.start()
    if job is not None:
        job.start()
    for s in range(1, NZ + 1):
        g.round(s)
    g.finish()
    if job is not None:
        job.finish()


COST = pl.CostEstimate(flops=0, bytes_accessed=4_000_000, transcendentals=0)
ANY = pl.BlockSpec(memory_space=pl.ANY)


def gather16(v, cid, chunks=4, dp=1, kind=None, span=None, side=None):
    rows, width = v.shape
    extra = kind is not None
    out = pl.pallas_call(
        functools.partial(gather_kernel, chunks, dp, kind, span),
        out_shape=(jax.ShapeDtypeStruct((NE, rows, width), v.dtype),)
        + ((kind.out_shape(dp, span[1], side),) if extra else ()),
        in_specs=[ANY] * (2 if extra else 1),
        out_specs=(ANY,) * (2 if extra else 1),
        scratch_shapes=Gather.scratch(chunks) + (kind.scratch(dp) if extra else []),
        compiler_params=pltpu.CompilerParams(collective_id=cid, has_side_effects=True),
        cost_estimate=COST,
        name="gather16",
    )(*((v, side) if extra else (v,)))
    return out if extra else out[0]


def opening_kernel(dp, chunks, x_ref, small_ref, parts_ref, out_ref,
                   x_all, small_all, parts_head, out_head, small_dp, parts_dp, out_dp, *sems):
    ng = 9
    gx = Gather(x_ref, x_all, chunks, sems[:ng])
    gs = Gather(small_dp, small_all, 1, sems[ng:2 * ng], lambda ref, b: ref.at[:, b])
    loc, ys, yr, ps, pr, os_, or_, pl_sem, ol_sem = sems[2 * ng:]
    me = gx.me
    plane = lax.axis_index("dp")
    enter_all(me, plane, dp)
    pairs = ((small_ref, small_dp.at[plane]), (parts_ref, parts_dp.at[plane]),
             (out_ref, out_dp.at[plane]))

    def lift(i, r):
        src, dst = pairs[i]
        return pltpu.make_async_remote_copy(
            src_ref=src, dst_ref=dst, send_sem=ys.at[i, r], recv_sem=yr.at[i, r],
            device_id={"dp": (plane + r) % dp}, device_id_type=MESH)

    def landed(i, r):
        p = (plane - r + dp) % dp
        dst = (small_dp.at[p], parts_dp.at[p], out_dp.at[p])[i]
        return pltpu.make_async_remote_copy(
            src_ref=dst, dst_ref=dst, send_sem=ys.at[i, r], recv_sem=yr.at[i, r],
            device_id={"dp": p}, device_id_type=MESH)

    def kept(i):
        src, dst = pairs[i]
        return pltpu.make_async_copy(src, dst, loc.at[i])

    for i in range(3):
        for r in range(1, dp):
            lift(i, r).start()
        kept(i).start()
    gx.start()
    gx.round(1)

    kept(0).wait()
    for r in range(1, dp):
        landed(0, r).wait_recv()
    gs.start()

    def part(r):
        h = (me + r) % NE
        return pltpu.make_async_remote_copy(
            src_ref=parts_dp.at[:, h], dst_ref=parts_head.at[:, me],
            send_sem=ps.at[r], recv_sem=pr.at[r],
            device_id={"expert": h}, device_id_type=MESH)

    def part_in(r):
        e = (me - r + NE) % NE
        return pltpu.make_async_remote_copy(
            src_ref=parts_head.at[:, e], dst_ref=parts_head.at[:, e],
            send_sem=ps.at[r], recv_sem=pr.at[r],
            device_id={"expert": e}, device_id_type=MESH)

    def part_kept():
        return pltpu.make_async_copy(parts_dp.at[:, me], parts_head.at[:, me], pl_sem)

    kept(1).wait()
    for r in range(1, dp):
        landed(1, r).wait_recv()
    for r in range(1, NE):
        part(r).start()
    part_kept().start()
    gx.round(2)

    def row(d):
        b = NE * d + me
        return pltpu.make_async_remote_copy(
            src_ref=out_dp.at[d], dst_ref=out_head.at[b % dp],
            send_sem=os_.at[d], recv_sem=or_.at[b % dp],
            device_id={"expert": b // dp}, device_id_type=MESH)

    def row_kept(d):
        b = NE * d + me
        return pltpu.make_async_copy(out_dp.at[d], out_head.at[b % dp], ol_sem.at[d])

    kept(2).wait()
    for r in range(1, dp):
        landed(2, r).wait_recv()
    for d in range(dp):
        home = (NE * d + me) // dp

        @pl.when(home != me)
        def _():
            row(d).start()

        @pl.when(home == me)
        def _():
            row_kept(d).start()

    gs.round(1)
    gx.round(3)
    gs.round(2)
    gx.round(4)
    gs.round(3)
    gs.round(4)

    def row_in(j):
        return pltpu.make_async_remote_copy(
            src_ref=out_head.at[j], dst_ref=out_head.at[j], send_sem=os_.at[j], recv_sem=or_.at[j],
            device_id={"expert": gx.core}, device_id_type=MESH)

    for r in range(1, NE):
        part_in(r).wait_recv()
        part(r).wait_send()
    part_kept().wait()
    for j in range(dp):
        @pl.when((dp * me + j) % NE != me)
        def _():
            row_in(j).wait_recv()
    for d in range(dp):
        home = (NE * d + me) // dp

        @pl.when(home != me)
        def _():
            row(d).wait_send()

        @pl.when(home == me)
        def _():
            row_kept(d).wait()
    for i in range(3):
        for r in range(1, dp):
            lift(i, r).wait_send()
    gx.finish()
    gs.finish()


def opening(dp, x, small, parts, out, cid, chunks=4):
    dma = pltpu.SemaphoreType.DMA
    rows, ws = small.shape
    bf = x.dtype
    wo = out.shape[1]
    shape = jax.ShapeDtypeStruct
    res = pl.pallas_call(
        functools.partial(opening_kernel, dp, chunks),
        out_shape=(
            shape((NE,) + x.shape, bf), shape((dp, NE, rows, ws), bf), shape((dp, NE) + parts.shape[1:], bf),
            shape((dp, rows, wo), bf),
            shape((dp, rows, ws), bf), shape((dp,) + parts.shape, bf), shape((dp, rows, wo), bf),
        ),
        in_specs=[ANY] * 4,
        out_specs=[ANY] * 7,
        scratch_shapes=Gather.scratch(chunks) + Gather.scratch(1) + [
            dma((3,)), dma((3, dp)), dma((3, dp)), dma((NE,)), dma((NE,)), dma((dp,)), dma((dp,)), dma, dma((dp,))],
        compiler_params=pltpu.CompilerParams(collective_id=cid, has_side_effects=True),
        cost_estimate=COST,
        name="opening",
    )(x, small, parts, out)
    return res[:4]


def order(z, i):
    a, b = (3, 2, 1, 0)[i], (3, 2, 0, 1)[i]
    return jnp.where(z == 0, a, jnp.where(z == 1, b, jnp.where(z == 2, 3 - b, 3 - a)))


class Scatter:
    def __init__(self, p_ref, o_ref, chunks, scratch):
        self.p, self.o, self.chunks = p_ref, o_ref, chunks
        (self.cbuf, self.own, self.xbuf, self.ubuf, self.dbuf, self.ld, self.cs, self.cr, self.xs, self.xr,
         self.us, self.ur, self.ds, self.dr) = scratch
        self.rows = o_ref.shape[0] // chunks
        self.me, self.z, self.x, self.c, self.core, self.side = place()

    @staticmethod
    def scratch(rows, width, chunks, bf):
        dma = pltpu.SemaphoreType.DMA
        return [pltpu.VMEM((n, rows, width), bf) for n in (8, 8, 4, 4, 4)] + [
            dma((8,)), dma((8, chunks)), dma((8, chunks))] + [dma((4, chunks))] * 6

    def rng(self, k):
        return pl.ds(k * self.rows, self.rows)

    def column(self, i, j):
        return 4 * order(self.z, i) + 2 * jnp.where(j == 0, 1 - self.x, self.x)

    def remote(self, src, dst, send, recv, to):
        return pltpu.make_async_remote_copy(
            src_ref=src, dst_ref=dst, send_sem=send, recv_sem=recv,
            device_id={"expert": to}, device_id_type=MESH)

    def over(self, i, j, k):
        n = 2 * i + j
        return self.remote(
            self.p.at[self.column(i, j) + 1 - self.c, self.rng(k)], self.cbuf.at[n, self.rng(k)],
            self.cs.at[n, k], self.cr.at[n, k], self.core)

    def load(self, i, j):
        n = 2 * i + j
        return pltpu.make_async_copy(self.p.at[self.column(i, j) + self.c], self.own.at[n], self.ld.at[n])

    def across(self, i, k):
        return self.remote(self.own.at[2 * i, self.rng(k)], self.xbuf.at[i, self.rng(k)],
                           self.xs.at[i, k], self.xr.at[i, k], self.side)

    def up(self, t, i, k):
        return self.remote(self.own.at[2 * i + 1, self.rng(k)], self.ubuf.at[t, self.rng(k)],
                           self.us.at[t, k], self.ur.at[t, k], self.me + 4)

    def down(self, t, i, k):
        return self.remote(self.own.at[2 * i + 1, self.rng(k)], self.dbuf.at[t, self.rng(k)],
                           self.ds.at[t, k], self.dr.at[t, k], self.me - 4)

    def start(self):
        for i in range(NZ):
            for j in range(2):
                self.load(i, j).start()
                for k in range(self.chunks):
                    self.over(i, j, k).start()

    def first(self, i):
        f32 = jnp.float32
        self.load(i, 0).wait()
        for k in range(self.chunks):
            self.over(i, 0, k).wait_recv()
            s = self.rng(k)
            self.own[2 * i, s] = (
                self.own[2 * i, s].astype(f32) + self.cbuf[2 * i, s].astype(f32)).astype(self.own.dtype)
            self.across(i, k).start()

    def second(self, i):
        f32 = jnp.float32
        z, own, o = self.z, self.own, self.o
        t = order(z, i)
        self.load(i, 1).wait()
        for k in range(self.chunks):
            s = self.rng(k)
            self.over(i, 1, k).wait_recv()
            self.across(i, k).wait_recv()

            def base():
                return (own[2 * i + 1, s].astype(f32) + self.cbuf[2 * i + 1, s].astype(f32)
                        + self.xbuf[i, s].astype(f32))

            if i < NZ - 1:
                @pl.when(t > z)
                def _():
                    @pl.when(z > 0)
                    def _():
                        self.up(t, i, k).wait_recv()
                        own[2 * i + 1, s] = (base() + self.ubuf[t, s].astype(f32)).astype(own.dtype)

                    @pl.when(z == 0)
                    def _():
                        own[2 * i + 1, s] = base().astype(own.dtype)

                    self.up(t, i, k).start()

                @pl.when(t < z)
                def _():
                    @pl.when(z < NZ - 1)
                    def _():
                        self.down(t, i, k).wait_recv()
                        own[2 * i + 1, s] = (base() + self.dbuf[t, s].astype(f32)).astype(own.dtype)

                    @pl.when(z == NZ - 1)
                    def _():
                        own[2 * i + 1, s] = base().astype(own.dtype)

                    self.down(t, i, k).start()
            else:
                @pl.when(z > 0)
                def _():
                    self.up(t, i, k).wait_recv()

                @pl.when(z < NZ - 1)
                def _():
                    self.down(t, i, k).wait_recv()

                @pl.when((z > 0) & (z < NZ - 1))
                def _():
                    o[s] = (base() + self.ubuf[t, s].astype(f32) + self.dbuf[t, s].astype(f32)).astype(o.dtype)

                @pl.when(z == 0)
                def _():
                    o[s] = (base() + self.dbuf[t, s].astype(f32)).astype(o.dtype)

                @pl.when(z == NZ - 1)
                def _():
                    o[s] = (base() + self.ubuf[t, s].astype(f32)).astype(o.dtype)

    def run(self):
        self.first(0)
        for i in range(NZ):
            if i + 1 < NZ:
                self.first(i + 1)
            self.second(i)

    def finish(self):
        z = self.z
        for k in range(self.chunks):
            for i in range(NZ):
                self.across(i, k).wait_send()
                for j in range(2):
                    self.over(i, j, k).wait_send()
                if i < NZ - 1:
                    t = order(z, i)

                    @pl.when(t > z)
                    def _():
                        self.up(t, i, k).wait_send()

                    @pl.when(t < z)
                    def _():
                        self.down(t, i, k).wait_send()


def scatter_kernel(chunks, dp, kind, span, p_ref, *refs):
    job = None
    ns = 14
    if kind is None:
        o_ref, *scratch = refs
    else:
        src, o_ref, out, *scratch = refs
        job = side_job(kind, dp, span, src, out, scratch[ns:])
    s = Scatter(p_ref, o_ref, chunks, scratch[:ns])
    enter(s.me, s.z, s.core, s.side, 1 if job is None else dp)
    s.start()
    if job is not None:
        job.start()
    s.run()
    s.finish()
    if job is not None:
        job.finish()


VMEM = pl.BlockSpec(memory_space=pltpu.VMEM)


def scatter16(p, cid, chunks=2, out_dtype=jnp.float32, dp=1, kind=None, span=None, side=None):
    _, rows, width = p.shape
    extra = kind is not None
    out = pl.pallas_call(
        functools.partial(scatter_kernel, chunks, dp, kind, span),
        out_shape=(jax.ShapeDtypeStruct((rows, width), out_dtype),)
        + ((kind.out_shape(dp, span[1], side),) if extra else ()),
        in_specs=[ANY] * (2 if extra else 1),
        out_specs=(VMEM,) + ((ANY,) if extra else ()),
        scratch_shapes=Scatter.scratch(rows, width, chunks, p.dtype) + (kind.scratch(dp) if extra else []),
        compiler_params=pltpu.CompilerParams(
            collective_id=cid, has_side_effects=True, vmem_limit_bytes=60 * 1024 * 1024),
        cost_estimate=COST,
        name="scatter16",
    )(*((p, side) if extra else (p,)))
    return out if extra else out[0]


def return_kernel(dp, chunks, p_ref, parts_ref, rows_ref, o_ref, parts_in, rows_in, parts_far, rows_far, *scratch):
    ns = 14
    s = Scatter(p_ref, o_ref, chunks, scratch[:ns])
    ps, pr, os_, or_, pl_sem, ol_sem, ys, yr = scratch[ns:]
    me = s.me
    plane = lax.axis_index("dp")
    enter_all(me, plane, dp)

    def part(r):
        e = (me + r) % NE
        return pltpu.make_async_remote_copy(
            src_ref=parts_ref.at[:, e], dst_ref=parts_in.at[:, me],
            send_sem=ps.at[r], recv_sem=pr.at[r],
            device_id={"expert": e}, device_id_type=MESH)

    def part_in(r):
        h = (me - r + NE) % NE
        return pltpu.make_async_remote_copy(
            src_ref=parts_in.at[:, h], dst_ref=parts_in.at[:, h],
            send_sem=ps.at[r], recv_sem=pr.at[r],
            device_id={"expert": h}, device_id_type=MESH)

    def part_kept():
        return pltpu.make_async_copy(parts_ref.at[:, me], parts_in.at[:, me], pl_sem)

    def row(j):
        b = dp * me + j
        return pltpu.make_async_remote_copy(
            src_ref=rows_ref.at[j], dst_ref=rows_in.at[b // NE],
            send_sem=os_.at[j], recv_sem=or_.at[b // NE],
            device_id={"expert": b % NE}, device_id_type=MESH)

    def row_kept(j):
        b = dp * me + j
        return pltpu.make_async_copy(rows_ref.at[j], rows_in.at[b // NE], ol_sem.at[j])

    def row_in(d):
        return pltpu.make_async_remote_copy(
            src_ref=rows_in.at[d], dst_ref=rows_in.at[d], send_sem=os_.at[d], recv_sem=or_.at[d],
            device_id={"expert": s.core}, device_id_type=MESH)

    def lift(i, r):
        to = (plane + r) % dp
        src, dst = ((parts_in.at[to], parts_far.at[r - 1]), (rows_in.at[to], rows_far.at[r - 1]))[i]
        return pltpu.make_async_remote_copy(
            src_ref=src, dst_ref=dst, send_sem=ys.at[i, r], recv_sem=yr.at[i, r],
            device_id={"dp": to}, device_id_type=MESH)

    s.start()
    for r in range(1, NE):
        part(r).start()
    part_kept().start()
    for j in range(dp):
        @pl.when((dp * me + j) % NE != me)
        def _():
            row(j).start()

        @pl.when((dp * me + j) % NE == me)
        def _():
            row_kept(j).start()
    s.first(0)
    s.first(1)
    s.second(0)
    for r in range(1, NE):
        part_in(r).wait_recv()
    part_kept().wait()
    for j in range(dp):
        @pl.when((dp * me + j) % NE == me)
        def _():
            row_kept(j).wait()
    for d in range(dp):
        @pl.when((NE * d + me) // dp != me)
        def _():
            row_in(d).wait_recv()
    for i in range(2):
        for r in range(1, dp):
            lift(i, r).start()
    s.first(2)
    s.second(1)
    s.first(3)
    s.second(2)
    s.second(3)
    for i in range(2):
        for r in range(1, dp):
            lift(i, r).wait_recv()
            lift(i, r).wait_send()
    for r in range(1, NE):
        part(r).wait_send()
    for j in range(dp):
        @pl.when((dp * me + j) % NE != me)
        def _():
            row(j).wait_send()
    s.finish()


def returning(dp, p, parts, rows, cid, chunks=2):
    dma = pltpu.SemaphoreType.DMA
    _, n, width = p.shape
    shape = jax.ShapeDtypeStruct
    out, parts_in, rows_in, parts_far, rows_far = pl.pallas_call(
        functools.partial(return_kernel, dp, chunks),
        out_shape=(
            shape((n, width), jnp.float32), shape(parts.shape, parts.dtype), shape(rows.shape, rows.dtype),
            shape((dp - 1,) + parts.shape[1:], parts.dtype), shape((dp - 1,) + rows.shape[1:], rows.dtype)),
        in_specs=[ANY] * 3,
        out_specs=[VMEM] + [ANY] * 4,
        scratch_shapes=Scatter.scratch(n, width, chunks, p.dtype) + [
            dma((NE,)), dma((NE,)), dma((dp,)), dma((dp,)), dma, dma((dp,)), dma((2, dp)), dma((2, dp))],
        compiler_params=pltpu.CompilerParams(
            collective_id=cid, has_side_effects=True, vmem_limit_bytes=60 * 1024 * 1024),
        cost_estimate=COST,
        name="returning",
    )(p, parts, rows)
    plane = lax.axis_index("dp")

    def total(near, far):
        own = lax.dynamic_index_in_dim(near, plane, 0, False).astype(jnp.float32)
        return own + jnp.sum(far.astype(jnp.float32), axis=0)

    return out, total(parts_in, parts_far), total(rows_in, rows_far)


def closing_kernel(dp, chunks, p_ref, o_ref, far_ref, *scratch):
    ns = 14
    s = Scatter(p_ref, o_ref, chunks, scratch[:ns])
    ys, yr = scratch[ns:]
    plane = lax.axis_index("dp")
    rows = o_ref.shape[0] // dp
    enter(s.me, s.z, s.core, s.side, dp)

    def lift(r):
        to = (plane + r) % dp
        return pltpu.make_async_remote_copy(
            src_ref=o_ref.at[pl.ds(pl.multiple_of(to * rows, 16), rows)], dst_ref=far_ref.at[r - 1],
            send_sem=ys.at[r], recv_sem=yr.at[r],
            device_id={"dp": to}, device_id_type=MESH)

    s.start()
    s.run()
    for r in range(1, dp):
        lift(r).start()
    s.finish()
    for r in range(1, dp):
        lift(r).wait_recv()
        lift(r).wait_send()


def closing(dp, p, cid):
    dma = pltpu.SemaphoreType.DMA
    _, n, width = p.shape
    shape = jax.ShapeDtypeStruct
    near, far = pl.pallas_call(
        functools.partial(closing_kernel, dp, 1),
        out_shape=(shape((n, width), p.dtype), shape((dp - 1, n // dp, width), p.dtype)),
        in_specs=[ANY],
        out_specs=[VMEM, VMEM],
        scratch_shapes=Scatter.scratch(n, width, 1, p.dtype) + [dma((dp,)), dma((dp,))],
        compiler_params=pltpu.CompilerParams(
            collective_id=cid, has_side_effects=True, vmem_limit_bytes=32 * 1024 * 1024),
        cost_estimate=COST,
        name="closing",
    )(p)
    own = lax.dynamic_slice_in_dim(near, lax.axis_index("dp") * (n // dp), n // dp).astype(jnp.float32)
    return own + jnp.sum(far.astype(jnp.float32), axis=0)
BF = jnp.bfloat16
F32 = jnp.float32


def mm(a, b):
    return jnp.dot(a, b, preferred_element_type=F32)


def mm_t(a, b):
    return lax.dot_general(a, b, (((1,), (1,)), ((), ())), preferred_element_type=F32)


def silu_pair(gate_in):
    sigmoid = 1.0 / (1.0 + jnp.exp(-gate_in))
    return (gate_in * sigmoid, sigmoid * (1.0 + gate_in * (1.0 - sigmoid)))


TILE = 256
WIDE = 512
SHARE = 176


def down_copies(a_ref, b_ref, out, sem, which):
    dp, a, _ = a_ref.shape
    rows = a + b_ref.shape[1]
    if which == 0:
        return [pltpu.make_async_copy(a_ref.at[d], out.at[pl.ds(d * rows, a)], sem.at[d]) for d in range(dp)]
    return [pltpu.make_async_copy(b_ref.at[d], out.at[pl.ds(d * rows + a, rows - a)], sem.at[dp + d])
            for d in range(dp)]


def share_copies(share_ref, fan, down, sem):
    dp, rows, w = share_ref.shape
    n = rows // 3
    copies = []
    for d in range(dp):
        cols = pl.ds(d * w, w)
        for i, (dst, first) in enumerate(((fan, 0), (fan, TILE), (down, 0))):
            copies.append(pltpu.make_async_copy(
                share_ref.at[d, pl.ds(i * n, n)], dst.at[pl.ds(first, n), cols], sem.at[3 * d + i]))
    return copies


def share_blank(fan, down):
    pad = jnp.zeros((TILE - SHARE, fan.shape[1]), BF)
    fan[SHARE:TILE] = pad
    fan[TILE + SHARE:] = pad
    down[SHARE:] = pad


def mine_of(routes_ref, pick_ref):
    tokens = routes_ref.shape[0]
    lane16 = lax.broadcasted_iota(jnp.int32, (tokens, 16), 1)
    mask = lane16 < 0
    for k in range(routes_ref.shape[1]):
        mask = mask | (lane16 == routes_ref[:, k:k + 1])
    mine = jnp.sum(jnp.where(mask, pick_ref[:, :16], 0.0), axis=1, keepdims=True)
    return mask, mine


def valid_of(len_ref, first_device, tokens, batches, here):
    n = lax.broadcasted_iota(jnp.int32, (tokens, 1), 0)
    device = n // (batches * here)
    batch = (n // here) % batches
    position = (first_device + device) * here + n % here
    length = jnp.zeros((tokens, 1), jnp.int32)
    for b in range(batches):
        length = jnp.where(batch == b, len_ref[b], length)
    return (position < length).astype(F32)


def one_hots(taken, groups, slots, here):
    r = lax.broadcasted_iota(jnp.int32, (256, 256), 0)
    c = lax.broadcasted_iota(jnp.int32, (256, 256), 1)
    same = r // here == c // here
    before = (same & (c < r)).astype(BF)
    after = (same & (r < c)).astype(BF)
    base_c = (lax.broadcasted_iota(jnp.int32, (256, slots), 0) // here * 32).astype(F32)
    base_r = (lax.broadcasted_iota(jnp.int32, (slots, 256), 1) // here * 32).astype(F32)
    lane = lax.broadcasted_iota(jnp.int32, (256, slots), 1).astype(F32)
    row = lax.broadcasted_iota(jnp.int32, (slots, 256), 0).astype(F32)
    ones = jnp.ones((256, slots), BF)
    to_slot, to_token = [], []
    for g in range(groups):
        t = jnp.broadcast_to(taken[g * 256:(g + 1) * 256], (256, slots))
        low = t.astype(BF)
        place_c = mm(before, low) + base_c
        place_r = mm_lead(low, after) + base_r
        taken_r = mm_lead(low, (r == c).astype(BF))
        to_token.append(jnp.where((place_c == lane) & (t > 0.5), 1.0, 0.0).astype(BF))
        to_slot.append(jnp.where((place_r == row) & (taken_r > 0.5), 1.0, 0.0).astype(BF))
    return to_slot, to_token


def mm_lead(a, b):
    return lax.dot_general(a, b, (((0,), (0,)), ((), ())), preferred_element_type=F32)


def lanes(j):
    return pl.ds(pl.multiple_of(j * WIDE, WIDE), WIDE)


def over_columns(total, body):
    def step(j, _):
        body(pl.multiple_of(j * WIDE, WIDE), WIDE)
        return 0

    lax.fori_loop(0, total // WIDE, step, 0)
    if total % WIDE:
        body(total // WIDE * WIDE, total % WIDE)


def forward_kernel(chunks, dp, span, batches, here, len_ref, pick_ref, mix_ref, routes_ref, wg_ref, wu_ref, router_ref,
                   share_ref, wda_ref, down_ref, dy_ref,
                   out_ref, rows_ref, hid_ref, act_ref, slo_ref, eo_ref, sh_ref, sact_ref, sslo_ref, gate_ref,
                   dy_all, wdb_ref,
                   wd_ref, fan_ref, sd_ref, hid_buf, sh_buf, gate_buf, taken_buf, wd_sem, sh_sem, *sems):
    step = pl.program_id(0)
    tokens, width = mix_ref.shape
    groups, slots = tokens // 256, 128
    half = groups * slots
    ff = hid_ref.shape[1]
    phase = pl.num_programs(0) // 2
    g = Gather(dy_ref, dy_all, chunks, sems[:9])
    job = side_job(Spread, dp, span, down_ref, wdb_ref, sems[9:])

    @pl.when(step == 0)
    def _():
        enter(g.me, g.z, g.core, g.side, dp)
        g.start()
        job.start()
        for copy in down_copies(wda_ref, wdb_ref, wd_ref, wd_sem, 0) + share_copies(share_ref, fan_ref, sd_ref, sh_sem):
            copy.start()
        share_blank(fan_ref, sd_ref)
        fan_ref[SHARE:SHARE + 16] = router_ref[...]
        for copy in share_copies(share_ref, fan_ref, sd_ref, sh_sem):
            copy.wait()

    @pl.when(step < phase)
    def _():
        mix = mix_ref[...]
        fanned = mm_t(mix, fan_ref[:TILE, :])
        s_up = mm_t(mix, fan_ref[TILE:, :])
        s_act, s_slope = silu_pair(fanned)
        s_hidden = (s_act * s_up).astype(BF)
        at = pl.ds(pl.multiple_of(step * tokens, tokens), tokens)
        sh_ref[...] = s_hidden
        sh_buf[at] = s_hidden
        sact_ref[...] = s_act.astype(BF)
        sslo_ref[...] = (s_up * s_slope).astype(BF)
        logits = fanned[:, SHARE:SHARE + 16]
        mask, mine = mine_of(routes_ref, pick_ref)
        taken = mine * valid_of(len_ref, step * (tokens // (batches * here)), tokens, batches, here)
        held = jnp.where(mask, logits, -1e30)
        raised = jnp.where(mask, jnp.exp(held - jnp.max(held, axis=1, keepdims=True)), 0.0)
        soft = raised / jnp.sum(raised, axis=1, keepdims=True)
        gate = jnp.sum(soft * pick_ref[:, :16], axis=1, keepdims=True) * taken
        gate_ref[...] = jnp.concatenate([gate, taken], axis=1)
        gate_buf[at] = gate
        taken_buf[at] = taken
        to_slot, _ = one_hots(taken, groups, slots, here)

        def dispatch(j, _):
            for n in range(groups):
                rows_ref[n * slots:(n + 1) * slots, lanes(j)] = mm(
                    to_slot[n], mix_ref[n * 256:(n + 1) * 256, lanes(j)]).astype(BF)
            return 0

        lax.fori_loop(0, width // WIDE, dispatch, 0)
        rows_at = pl.ds(pl.multiple_of(step * half, half), half)

        def fan_in(start, size):
            cols = pl.ds(start, size)
            gate_in = mm(rows_ref[...], wg_ref[:, cols])
            up_in = mm(rows_ref[...], wu_ref[:, cols])
            act, slope = silu_pair(gate_in)
            hidden = (act * up_in).astype(BF)
            hid_ref[:, cols] = hidden
            hid_buf[rows_at, cols] = hidden
            act_ref[:, cols] = act.astype(BF)
            slo_ref[:, cols] = (up_in * slope).astype(BF)

        over_columns(ff, fan_in)

    @pl.when(step == phase)
    def _():
        job.finish()
        for copy in down_copies(wda_ref, wdb_ref, wd_ref, wd_sem, 1):
            copy.start()
        for which in range(2):
            for copy in down_copies(wda_ref, wdb_ref, wd_ref, wd_sem, which):
                copy.wait()

    @pl.when(step >= phase)
    def _():
        tile = step - phase
        at = pl.ds(pl.multiple_of(tile * tokens, tokens), tokens)
        rows_at = pl.ds(pl.multiple_of(tile * half, half), half)
        gate = gate_buf[at]
        s_hidden = sh_buf[at]
        _, to_token = one_hots(taken_buf[at], groups, slots, here)

        def fan_out(j, _):
            eo = mm(hid_buf[rows_at], wd_ref[:, lanes(j)]).astype(BF)
            eo_ref[:, lanes(j)] = eo
            shared = mm(s_hidden, sd_ref[:, lanes(j)])
            picked = jnp.concatenate(
                [mm(to_token[n], eo[n * slots:(n + 1) * slots]) for n in range(groups)], axis=0)
            out_ref[:, lanes(j)] = (shared + gate * picked).astype(BF)
            return 0

        lax.fori_loop(0, width // WIDE, fan_out, 0)

    for r, s in ((1, 1), (2, 3), (3, 5), (4, 7)):
        @pl.when(step == s)
        def _():
            g.round(r)

    @pl.when(step == 2 * phase - 1)
    def _():
        g.finish()


def backward_kernel(here, pick_ref, dy_ref, mix_ref, sh_ref, wg_ref, wu_ref, share_ref, wda_ref, wdb_ref,
                    act_ref, slo_ref, eo_ref, sact_ref, sslo_ref, gate_ref,
                    dh_ref, deo_ref, dg_ref, du_ref, gshare_ref,
                    wd_ref, fan_ref, sd_ref, gfan, gsd, wd_sem, sh_sem):
    step = pl.program_id(0)
    tokens, width = dy_ref.shape
    groups, slots = tokens // 256, 128
    ff = dg_ref.shape[1]

    @pl.when(step == 0)
    def _():
        copies = share_copies(share_ref, fan_ref, sd_ref, sh_sem)
        for which in range(2):
            copies += down_copies(wda_ref, wdb_ref, wd_ref, wd_sem, which)
        for copy in copies:
            copy.start()
        share_blank(fan_ref, sd_ref)
        gfan[...] = jnp.zeros_like(gfan)
        gsd[...] = jnp.zeros_like(gsd)
        for copy in copies:
            copy.wait()

    d_sh = mm_t(dy_ref[...], sd_ref[...])
    d_s = jnp.concatenate([(d_sh * sslo_ref[...].astype(F32)).astype(BF),
                           (d_sh * sact_ref[...].astype(F32)).astype(BF)], axis=1)
    gate, taken = gate_ref[:, :1], gate_ref[:, 1:]
    to_slot, to_token = one_hots(taken, groups, slots, here)

    def dispatch(j, total):
        low = dy_ref[:, lanes(j)]
        dy = low.astype(F32)
        gated = (gate * dy).astype(BF)
        for n in range(groups):
            deo_ref[n * slots:(n + 1) * slots, lanes(j)] = mm(to_slot[n], gated[n * 256:(n + 1) * 256]).astype(BF)
        picked = jnp.concatenate(
            [mm(to_token[n], eo_ref[n * slots:(n + 1) * slots, lanes(j)]) for n in range(groups)], axis=0)
        gfan[:, lanes(j)] += mm_lead(d_s, mix_ref[:, lanes(j)])
        gsd[:, lanes(j)] += mm_lead(sh_ref[...], low)
        return total + jnp.sum(dy * picked, axis=1, keepdims=True)

    d_gates = lax.fori_loop(0, width // WIDE, dispatch, jnp.zeros((tokens, 1), F32))

    def back_out(start, size):
        cols = pl.ds(start, size)
        d_eh = mm_t(deo_ref[...], wd_ref[cols, :])
        dg_ref[:, cols] = (d_eh * slo_ref[:, cols].astype(F32)).astype(BF)
        du_ref[:, cols] = (d_eh * act_ref[:, cols].astype(F32)).astype(BF)

    over_columns(ff, back_out)

    def back_in(j, _):
        d_rows = (mm_t(dg_ref[...], wg_ref[lanes(j), :]) + mm_t(du_ref[...], wu_ref[lanes(j), :])).astype(BF)
        shared = mm(d_s, fan_ref[:, lanes(j)])
        taken_rows = jnp.concatenate(
            [mm(to_token[n], d_rows[n * slots:(n + 1) * slots]) for n in range(groups)], axis=0)
        dh_ref[:, lanes(j)] = (shared + taken_rows).astype(BF)
        return 0

    lax.fori_loop(0, width // WIDE, back_in, 0)
    high = d_gates.astype(BF).astype(F32)
    dh_ref[:, width:] = (high * pick_ref[:, :128] + (d_gates - high) * pick_ref[:, 128:]).astype(BF)

    @pl.when(step == pl.num_programs(0) - 1)
    def _():
        dp, rows, w = share_ref.shape
        n = rows // 3
        for d in range(dp):
            cols = slice(d * w, (d + 1) * w)
            gshare_ref[d, :n] = gfan[:n, cols].astype(BF)
            gshare_ref[d, n:2 * n] = gfan[TILE:TILE + n, cols].astype(BF)
            gshare_ref[d, 2 * n:] = gsd[:n, cols].astype(BF)


def whole(v):
    zeros = (0,) * v.ndim
    return pl.BlockSpec(v.shape, lambda i: zeros, pipeline_mode=pl.Buffered(buffer_count=1))


def tiles(rows, w):
    return pl.BlockSpec((rows, w), lambda i: (i, 0))


SMEM = pl.BlockSpec(memory_space=pltpu.SMEM)


def mixture_forward(dp, batches, here, lengths, pick, mix, routes, wg, wu, router, share, wda, span, down, dy, cid,
                    chunks=2):
    total, width = mix.shape
    step, half = total // 4, total // 8
    ff = wg.shape[1]
    shape = jax.ShapeDtypeStruct
    rows = total // 2
    dma = pltpu.SemaphoreType.DMA

    def early(n, w):
        return pl.BlockSpec((n, w), lambda i: (jnp.minimum(i, 3), 0))

    def late(n, w):
        return pl.BlockSpec((n, w), lambda i: (jnp.maximum(i - 4, 0), 0))

    return pl.pallas_call(
        functools.partial(forward_kernel, chunks, dp, span, batches, here),
        grid=(8,),
        out_shape=(
            shape((total, width), BF), shape((rows, width), BF), shape((rows, ff), BF), shape((rows, ff), BF),
            shape((rows, ff), BF), shape((rows, width), BF), shape((total, TILE), BF), shape((total, TILE), BF),
            shape((total, TILE), BF), shape((total, 2), F32), shape((NE,) + dy.shape, BF),
            shape((dp, span[1], width), BF)),
        in_specs=[SMEM, whole(pick), early(step, width), early(step, routes.shape[1]), whole(wg), whole(wu),
                  whole(router), ANY, ANY, ANY, ANY],
        out_specs=[late(step, width), early(half, width), early(half, ff), early(half, ff), early(half, ff),
                   late(half, width), early(step, TILE), early(step, TILE), early(step, TILE), early(step, 2), ANY, ANY],
        scratch_shapes=[
            pltpu.VMEM((ff, width), BF), pltpu.VMEM((2 * TILE, width), BF), pltpu.VMEM((TILE, width), BF),
            pltpu.VMEM((rows, ff), BF), pltpu.VMEM((total, TILE), BF), pltpu.VMEM((total, 1), F32),
            pltpu.VMEM((total, 1), F32), dma((2 * dp,)), dma((3 * dp,))] + Gather.scratch(chunks) + Spread.scratch(dp),
        compiler_params=pltpu.CompilerParams(
            collective_id=cid, has_side_effects=True, vmem_limit_bytes=60 * 1024 * 1024),
        cost_estimate=COST,
        name="mixture_forward",
    )(lengths, pick, mix, routes, wg, wu, router, share, wda, down, dy)


def mixture_backward(here, pick, dy, mix, sh, wg, wu, share, wda, wdb, act, slo, eo, sact, sslo, gate):
    total, width = dy.shape
    step, half = total // 4, total // 8
    ff = wg.shape[1]
    shape = jax.ShapeDtypeStruct
    rows = total // 2
    dp = wda.shape[0]
    dma = pltpu.SemaphoreType.DMA
    return pl.pallas_call(
        functools.partial(backward_kernel, here),
        grid=(4,),
        out_shape=(
            shape((total, width + 128), BF), shape((rows, width), BF), shape((rows, ff), BF), shape((rows, ff), BF),
            shape(share.shape, BF)),
        in_specs=[whole(pick), tiles(step, width), tiles(step, width), tiles(step, TILE), whole(wg), whole(wu),
                  ANY, ANY, ANY,
                  tiles(half, ff), tiles(half, ff), tiles(half, width), tiles(step, TILE), tiles(step, TILE),
                  tiles(step, 2)],
        out_specs=[tiles(step, width + 128), tiles(half, width), tiles(half, ff), tiles(half, ff),
                   pl.BlockSpec(share.shape, lambda i: (0, 0, 0))],
        scratch_shapes=[
            pltpu.VMEM((ff, width), BF), pltpu.VMEM((2 * TILE, width), BF), pltpu.VMEM((TILE, width), BF),
            pltpu.VMEM((2 * TILE, width), F32), pltpu.VMEM((TILE, width), F32), dma((2 * dp,)), dma((3 * dp,))],
        compiler_params=pltpu.CompilerParams(vmem_limit_bytes=60 * 1024 * 1024),
        cost_estimate=COST,
        name="mixture_backward",
    )(pick, dy, mix, sh, wg, wu, share, wda, wdb, act, slo, eo, sact, sslo, gate)


def turn(v, cosine, sine):
    half = v.shape[1] // 2
    a, b = v[:, :half], v[:, half:]
    return jnp.concatenate([a * cosine - b * sine, b * cosine + a * sine], axis=1)


def project_kernel(x_ref, gain_ref, lgain_ref, wq_ref, wl_ref, we_ref, cos_ref, sin_ref,
                   h_ref, q_ref, k_ref, v_ref, lat_ref):
    blocks = x_ref.shape[0]
    batches, rows, _ = q_ref.shape
    here = rows // blocks
    x = x_ref[...].reshape(blocks * batches * here, x_ref.shape[2]).astype(F32)
    h = x * lax.rsqrt(jnp.mean(x * x, axis=1, keepdims=True) + 1e-6) * gain_ref[...]
    h = h.astype(BF)
    h_ref[...] = h
    raw = mm(h, wq_ref[...])
    raw_lat = mm(h, wl_ref[...])
    cosine, sine = cos_ref[...], sin_ref[...]
    zeros = jnp.zeros((raw.shape[0], 64), BF)
    q = jnp.concatenate([raw[:, :128].astype(BF), turn(raw[:, 128:192], cosine, sine).astype(BF), zeros], axis=1)
    k_rope = turn(raw_lat[:, 512:576], cosine, sine).astype(BF)
    lat = raw_lat[:, :512]
    lat = (lat * lax.rsqrt(jnp.mean(lat * lat, axis=1, keepdims=True) + 1e-6) * lgain_ref[...]).astype(BF)
    expanded = mm(lat, we_ref[...]).astype(BF)
    k = jnp.concatenate([expanded[:, :128], k_rope, zeros], axis=1)
    for e in range(blocks):
        for m in range(batches):
            src = slice((e * batches + m) * here, (e * batches + m + 1) * here)
            dst = slice(e * here, (e + 1) * here)
            q_ref[m, dst] = q[src]
            k_ref[m, dst] = k[src]
            v_ref[m, dst] = expanded[src, 128:]
            lat_ref[m, dst] = lat[src]


def project(x_all, gain, lgain, wq, wl, we, cosine, sine, batches):
    groups, rows, width = x_all.shape
    here = rows // batches
    per = 4
    seq = groups * here
    shape = jax.ShapeDtypeStruct

    def whole(v):
        return pl.BlockSpec(v.shape, lambda i: (0, 0))

    def by_seq(w):
        return pl.BlockSpec((batches, per * here, w), lambda i: (0, i, 0))

    table = pl.BlockSpec((per * rows, 32), lambda i: (i, 0))
    return pl.pallas_call(
        project_kernel,
        grid=(groups // per,),
        out_shape=(shape((groups * rows, width), BF), shape((batches, seq, 256), BF), shape((batches, seq, 256), BF),
                   shape((batches, seq, 128), BF), shape((batches, seq, 512), BF)),
        in_specs=[pl.BlockSpec((per, rows, width), lambda i: (i, 0, 0)), whole(gain), whole(lgain), whole(wq), whole(wl), whole(we),
                  table, table],
        out_specs=[pl.BlockSpec((per * rows, width), lambda i: (i, 0)), by_seq(256), by_seq(256), by_seq(128), by_seq(512)],
        compiler_params=pltpu.CompilerParams(vmem_limit_bytes=48 * 1024 * 1024),
        cost_estimate=pl.CostEstimate(flops=7_000_000_000, bytes_accessed=20_000_000, transcendentals=0),
        name="project",
    )(x_all, gain, lgain, wq, wl, we, cosine, sine)


ROWS = 256
SCALE = 192.0 ** -0.5


def held_scores(q, k, first, length):
    s = mm_t(q, k) * SCALE
    t = lax.broadcasted_iota(jnp.int32, s.shape, 0) + first
    u = lax.broadcasted_iota(jnp.int32, s.shape, 1)
    return jnp.where((u <= t) & (u < length), s, -1e30)


def attend_kernel(len_ref, q_ref, k_ref, v_ref, wo_ref, part_ref, att_ref, lse_ref):
    length = len_ref[pl.program_id(0)]
    seq = q_ref.shape[1]
    groups, _, here, width = part_ref.shape
    for i in range(seq // ROWS):
        tile = slice(i * ROWS, (i + 1) * ROWS)
        ext = (i + 1) * ROWS
        s = held_scores(q_ref[0, tile], k_ref[0, :ext], i * ROWS, length)
        peak = jnp.max(s, axis=1, keepdims=True)
        raised = jnp.exp(s - peak)
        total = jnp.sum(raised, axis=1, keepdims=True)
        lse_ref[0, tile] = peak + jnp.log(total)
        p = (raised / total).astype(BF)
        att = mm(p, v_ref[0, :ext]).astype(BF)
        per = ROWS // here
        att_ref[i * per:(i + 1) * per, 0] = att.reshape(per, here, att.shape[1])
        for j in range(width // 512):
            cols = slice(j * 512, (j + 1) * 512)
            part_ref[i * per:(i + 1) * per, 0, :, cols] = mm(att, wo_ref[:, cols]).astype(BF).reshape(per, here, 512)


def attend(lengths, q, k, v, wo, groups):
    batches, seq, _ = q.shape
    here = seq // groups
    width = wo.shape[1]
    shape = jax.ShapeDtypeStruct

    def by_seq(w):
        return pl.BlockSpec((1, seq, w), lambda m: (m, 0, 0))

    def by_dev(w):
        return pl.BlockSpec((groups, 1, here, w), lambda m: (0, m, 0, 0))

    return pl.pallas_call(
        attend_kernel,
        grid=(batches,),
        out_shape=(shape((groups, batches, here, width), BF), shape((groups, batches, here, 128), BF),
                   shape((batches, seq, 1), F32)),
        in_specs=[pl.BlockSpec(memory_space=pltpu.SMEM), by_seq(256), by_seq(256), by_seq(128),
                  pl.BlockSpec(wo.shape, lambda m: (0, 0))],
        out_specs=[by_dev(width), by_dev(128), by_seq(1)],
        compiler_params=pltpu.CompilerParams(vmem_limit_bytes=48 * 1024 * 1024),
        cost_estimate=pl.CostEstimate(flops=4_000_000_000, bytes_accessed=15_000_000, transcendentals=2_000_000),
        name="attend",
    )(lengths, q, k, v, wo)


def attend_back_kernel(len_ref, dout_ref, q_ref, k_ref, v_ref, lat_ref, att_ref, lse_ref, wo_ref, wq_ref, we_ref,
                       cos_ref, sin_ref, part_ref, dq_ref, gwo_ref, gwe_ref, dk, dv, datt):
    m = pl.program_id(0)
    length = len_ref[m]
    seq = q_ref.shape[1]
    groups, _, here, width = dout_ref.shape
    per = ROWS // here

    @pl.when(m == 0)
    def _():
        gwo_ref[...] = jnp.zeros_like(gwo_ref)
        gwe_ref[...] = jnp.zeros_like(gwe_ref)

    for j in range(4):
        blocks = slice(j * groups // 4, (j + 1) * groups // 4)
        dout = dout_ref[blocks].reshape(seq // 4, width)
        rows = slice(j * seq // 4, (j + 1) * seq // 4)
        datt[rows] = mm_t(dout, wo_ref[...]).astype(BF)
        gwo_ref[...] += mm_lead(att_ref[blocks].reshape(seq // 4, 128), dout)
    dk[...] = jnp.zeros_like(dk)
    dv[...] = jnp.zeros_like(dv)
    for i in range(seq // ROWS):
        tile = slice(i * ROWS, (i + 1) * ROWS)
        ext = (i + 1) * ROWS
        q = q_ref[0, tile]
        p = jnp.exp(held_scores(q, k_ref[0, :ext], i * ROWS, length) - lse_ref[0, tile])
        da = datt[tile]
        dp = mm_t(da, v_ref[0, :ext])
        inner = jnp.sum(dp * p, axis=1, keepdims=True)
        ds = (p * (dp - inner)).astype(BF)
        dq = mm(ds, k_ref[0, :ext]) * SCALE
        dk[:ext] += mm_lead(ds, q)
        dv[:ext] += mm_lead(p.astype(BF), da)
        rope = turn(dq[:, 128:192], cos_ref[tile], -sin_ref[tile])
        dq = jnp.concatenate([dq[:, :128].astype(BF), rope.astype(BF), jnp.zeros((ROWS, 64), BF)], axis=1)
        dq_ref[i * per:(i + 1) * per, 0] = dq.reshape(per, here, 256)
        for j in range(width // 512):
            cols = slice(j * 512, (j + 1) * 512)
            part_ref[i * per:(i + 1) * per, 0, :, cols] = mm_t(dq, wq_ref[cols]).astype(BF).reshape(per, here, 512)
    for i in range(seq // ROWS):
        tile = slice(i * ROWS, (i + 1) * ROWS)
        d_k = dk[tile] * SCALE
        d_exp = jnp.concatenate([d_k[:, :128].astype(BF), dv[tile].astype(BF)], axis=1)
        gwe_ref[...] += mm_lead(lat_ref[0, tile], d_exp)
        d_lat = mm_t(d_exp, we_ref[...]).astype(BF)
        tail = jnp.concatenate([d_lat, d_k[:, 128:].astype(BF)], axis=1)
        pad = part_ref.shape[3] - width - tail.shape[1]
        if pad > 0:
            tail = jnp.concatenate([tail, jnp.zeros((ROWS, pad), BF)], axis=1)
        part_ref[i * per:(i + 1) * per, 0, :, width:] = tail[:, :part_ref.shape[3] - width].reshape(per, here, -1)


def attend_back(lengths, dout, q, k, v, lat, att, lse, wo, wq, we, cosine, sine, tail):
    groups, batches, here, width = dout.shape
    seq = groups * here
    shape = jax.ShapeDtypeStruct

    def by_seq(w):
        return pl.BlockSpec((1, seq, w), lambda m: (m, 0, 0))

    def by_dev(w):
        return pl.BlockSpec((groups, 1, here, w), lambda m: (0, m, 0, 0))

    def whole(v):
        return pl.BlockSpec(v.shape, lambda m: (0, 0))

    return pl.pallas_call(
        attend_back_kernel,
        grid=(batches,),
        out_shape=(shape((groups, batches, here, width + tail), BF), shape((groups, batches, here, 256), BF),
                   shape(wo.shape, F32), shape(we.shape, F32)),
        in_specs=[pl.BlockSpec(memory_space=pltpu.SMEM), by_dev(width), by_seq(256), by_seq(256), by_seq(128),
                  by_seq(512), by_dev(128), by_seq(1), whole(wo), whole(wq), whole(we), whole(cosine), whole(sine)],
        out_specs=[by_dev(width + tail), by_dev(256), whole(wo), whole(we)],
        scratch_shapes=[pltpu.VMEM((seq, 256), F32), pltpu.VMEM((seq, 128), F32), pltpu.VMEM((seq, 128), BF)],
        compiler_params=pltpu.CompilerParams(vmem_limit_bytes=56 * 1024 * 1024),
        cost_estimate=pl.CostEstimate(flops=14_000_000_000, bytes_accessed=25_000_000, transcendentals=2_000_000),
        name="attend_back",
    )(lengths, dout, q, k, v, lat, att, lse, wo, wq, we, cosine, sine)


H = 16
QK_NOPE = 128
ROPE = 64
V_DIM = 128
KV_RANK = 512
GROUPS = 16
EPSILON = 1e-06
ROTARY_BASE = 10000.0


def product(left_side, right_side):
    return jnp.dot(left_side, right_side, preferred_element_type=F32)


def product_lead(left_side, right_side):
    return lax.dot_general(
        left_side, right_side, (((0,), (0,)), ((), ())), preferred_element_type=F32
    )


def product_trail(left_side, right_side):
    return lax.dot_general(
        left_side, right_side, (((1,), (1,)), ((), ())), preferred_element_type=F32
    )


def rotary_tables(count):
    frequency = ROTARY_BASE ** (-np.arange(ROPE // 2, dtype=np.float32) * np.float32(2.0) / np.float32(ROPE))
    angles = np.arange(count, dtype=np.float32)[:, None] * frequency.astype(np.float32)[None, :]
    return np.cos(angles).astype(np.float32), np.sin(angles).astype(np.float32)


def rotate(values, cosine, sine_table):
    first_half, second_half = jnp.split(values, 2, axis=-1)
    return jnp.concatenate(
        [
            first_half * cosine - second_half * sine_table,
            second_half * cosine + first_half * sine_table,
        ],
        axis=-1,
    )


def norm_forward(values, gains):
    factor = lax.rsqrt(jnp.mean(values * values, axis=-1, keepdims=True) + EPSILON)
    normed = values * factor
    return (normed * gains, normed, factor)


def norm_backward(gradient, normed, factor, gains):
    gain_grad = jnp.sum(gradient * normed, axis=0)
    scaled = gradient * gains
    return (
        factor * (scaled - normed * jnp.mean(scaled * normed, axis=-1, keepdims=True)),
        gain_grad,
    )


def selected_experts(routes):
    chosen = routes[:, :, None] == jnp.arange(GROUPS, dtype=routes.dtype)
    return jnp.any(chosen, axis=1)


def masked_softmax(logits, mask):
    held = jnp.where(mask, logits, -1e30)
    peak = jnp.max(held, axis=-1, keepdims=True)
    raised = jnp.where(mask, jnp.exp(held - peak), 0.0)
    return raised / jnp.sum(raised, axis=-1, keepdims=True)


def per_device(
    layer_input,
    out_cotangent,
    lengths,
    routes,
    attn_gain,
    query_weight,
    latent_weight,
    latent_gain,
    expand_weight,
    output_weight,
    mixer_gain,
    router_weight,
    gate_weight,
    up_weight,
    down_weight,
    shared_gate,
    shared_up,
    shared_down,
):
    dp = lax.axis_size("dp")
    me = lax.axis_index("expert")
    plane = lax.axis_index("dp")
    batches, _, here, width = layer_input.shape
    own = batches * here
    total = own * GROUPS
    seq_total = here * GROUPS
    rows_w = query_weight.shape[0]
    rows_l = expand_weight.shape[0]

    x_own = layer_input.reshape(own, width)
    routes_own = routes.reshape(own, -1)
    choices = routes_own.shape[1]
    route_columns = routes_own.astype(BF).reshape(rows_w, -1)
    small_width = -(-(595 + route_columns.shape[1]) // 128) * 128
    latent_column = jnp.zeros((rows_w,), BF).at[:rows_l].set(latent_gain)
    small = jnp.concatenate(
        [
            latent_weight,
            router_weight,
            attn_gain[:, None],
            mixer_gain[:, None],
            latent_column[:, None],
            route_columns,
            jnp.zeros((rows_w, small_width - 595 - route_columns.shape[1]), BF),
        ],
        axis=1,
    )
    query_parts = query_weight.reshape(rows_w, H, QK_NOPE + ROPE).transpose(1, 0, 2)
    expand_parts = expand_weight.reshape(rows_l, H, QK_NOPE + V_DIM).transpose(1, 0, 2)
    parts = jnp.concatenate([query_parts, expand_parts.reshape(H, rows_w, ROPE)], axis=2)
    x_all, small, parts_head, output_head = opening(dp, x_own, small, parts, output_weight, 1)
    x_all = x_all.reshape(total, width)
    routes_all = lax.dynamic_index_in_dim(small, plane, 0, False)[..., 595 : 595 + route_columns.shape[1]]
    routes_all = routes_all.reshape(total, choices).astype(jnp.int32)
    small = small.reshape(width, small_width)
    parts_head = parts_head.reshape(width, TILE)
    latent_full = small[:, :576]
    router_full = small[:, 576:592]
    gain_attn = small[:, 592].astype(F32)
    gain_mixer = small[:, 593].astype(F32)
    gain_latent = small[:, 594].reshape(dp * GROUPS, rows_w)[:, :rows_l].reshape(-1).astype(F32)
    expand_head = parts_head[:, QK_NOPE + ROPE :].reshape(KV_RANK, QK_NOPE + V_DIM)
    output_head = output_head.reshape(V_DIM, width)

    ff = gate_weight.shape[2]
    share_own = jnp.concatenate([shared_gate.T, shared_up.T, shared_down], axis=0)
    share_width = shared_down.shape[0]
    gate_full = lax.all_gather(gate_weight[0], "dp", axis=0, tiled=True)
    up_full = lax.all_gather(up_weight[0], "dp", axis=0, tiled=True)
    share_full = lax.all_gather(share_own, "dp", axis=0)
    seq_lengths = lengths.reshape(batches)
    own_positions = me * here + jnp.arange(here, dtype=jnp.int32)
    valid_own = (own_positions[None, :] < seq_lengths[:, None]).reshape(own).astype(F32)
    cosine, sine_table = rotary_tables(seq_total)
    cosine_own = lax.dynamic_slice_in_dim(jnp.asarray(cosine), me * here, here)
    sine_own = lax.dynamic_slice_in_dim(jnp.asarray(sine_table), me * here, here)

    grad_own = out_cotangent.reshape(own, width) * valid_own[:, None].astype(BF)

    def by_token(table):
        return jnp.asarray(np.broadcast_to(
            table.reshape(GROUPS, 1, here, -1), (GROUPS, batches, here, table.shape[1])).reshape(total, -1))

    hidden_all, query, key, values, latent = project(
        x_all.reshape(GROUPS, own, width), gain_attn[None], gain_latent[None], parts_head, small, expand_head,
        by_token(cosine), by_token(sine_table), batches)
    attn_part, attended, log_total = attend(seq_lengths, query, key, values, output_head, GROUPS)
    attn_part = attn_part.reshape(GROUPS, own, width)
    down_own = down_weight[0]
    cut = down_own.shape[0] * 3 // 80 * 16
    spans = ((0, cut), (cut, down_own.shape[0] - cut))
    attn_out = scatter16(attn_part, 2)

    x_wide = x_own.astype(F32)
    middle = x_wide + attn_out
    normed_mix, unit_mix, factor_mix = norm_forward(middle, gain_mixer)
    hidden_mix = normed_mix.astype(BF)
    mix_all, down_a = gather16(hidden_mix, 3, dp=dp, kind=Spread, span=spans[0], side=down_own)
    mix_all = mix_all.reshape(total, width)

    lane = jnp.arange(128)[None, :]
    pick = jnp.concatenate([lane == me, lane == me + GROUPS], axis=1).astype(F32)
    (out_part, rows, hidden, act, slope, result, share_hidden, share_act, share_slope, gates, grad_all,
     down_b) = mixture_forward(
        dp, batches, here, seq_lengths, pick, mix_all, routes_all, gate_full, up_full, router_full.T, share_full,
        down_a, spans[1], down_own, grad_own, 4)
    grad_all = grad_all.reshape(total, width)
    mixed = lax.psum_scatter(out_part, "expert", scatter_dimension=0, tiled=True).astype(F32)
    mix_part, grad_result, grad_gate_in, grad_up_in, grad_share = mixture_backward(
        here, pick, grad_all, mix_all, share_hidden, gate_full, up_full, share_full, down_a, down_b, act, slope, result,
        share_act, share_slope, gates)
    grad_down = product_lead(hidden, grad_result).astype(BF)
    grad_gate = product_lead(rows, grad_gate_in).astype(BF)
    grad_up = product_lead(rows, grad_up_in).astype(BF)
    mix_part, grad_down, grad_gate, grad_up = lax.optimization_barrier((mix_part, grad_down, grad_gate, grad_up))
    mix_sum = scatter16(mix_part.reshape(GROUPS, own, width + 128), 5)
    layer_output = valid_own[:, None] * (middle + mixed)

    out_down = lax.psum_scatter(grad_down, "dp", scatter_dimension=0, tiled=True)
    out_gate = lax.psum_scatter(grad_gate, "dp", scatter_dimension=0, tiled=True)
    out_up = lax.psum_scatter(grad_up, "dp", scatter_dimension=0, tiled=True)
    out_share = lax.psum_scatter(grad_share, "dp", scatter_dimension=0, tiled=False).astype(F32)

    mask_own = selected_experts(routes_own)
    soft_own = masked_softmax(product(hidden_mix, router_full), mask_own)
    grad_masked = (mix_sum[:, width : width + GROUPS] + mix_sum[:, width + GROUPS : width + 2 * GROUPS])
    grad_masked = grad_masked * valid_own[:, None]
    grad_logits = soft_own * (grad_masked - jnp.sum(grad_masked * soft_own, axis=1, keepdims=True))
    grad_logits = grad_logits.astype(BF)
    grad_mix = mix_sum[:, :width] + product_trail(grad_logits, router_full)
    grad_middle_norm, grad_gain_mixer = norm_backward(grad_mix, unit_mix, factor_mix, gain_mixer)
    grad_middle = grad_own.astype(F32) + grad_middle_norm

    grad_attn_all = gather16(grad_middle.astype(BF), 6).reshape(GROUPS, batches, here, width)
    back_part, grad_query, grad_output, grad_expand = attend_back(
        seq_lengths, grad_attn_all, query, key, values, latent, attended, log_total, output_head, parts_head,
        expand_head, jnp.asarray(cosine), jnp.asarray(sine_table), 640)
    grad_query_w = product_lead(hidden_all, grad_query.reshape(total, TILE)).astype(BF)
    parts_grad = jnp.concatenate(
        [grad_query_w[:, : QK_NOPE + ROPE], grad_expand.astype(BF).reshape(width, ROPE)], axis=1)
    back_sum, out_parts, out_output = returning(
        dp, back_part.reshape(GROUPS, own, back_part.shape[3]),
        parts_grad.reshape(dp, GROUPS, rows_w, TILE), grad_output.astype(BF).reshape(dp, rows_w, width), 7)
    out_query = out_parts[..., : QK_NOPE + ROPE].transpose(1, 0, 2).reshape(rows_w, -1)
    out_expand = out_parts[..., QK_NOPE + ROPE :].reshape(H, rows_l, QK_NOPE + V_DIM)
    out_expand = out_expand.transpose(1, 0, 2).reshape(rows_l, -1)

    x_normed, unit_attn, factor_attn = norm_forward(x_wide, gain_attn)
    hidden_own = x_normed.astype(BF)
    latent_own = product(hidden_own, latent_full)
    _, unit_latent, factor_latent = norm_forward(latent_own[:, :KV_RANK], gain_latent)
    grad_latent_in, grad_gain_latent = norm_backward(
        back_sum[:, width : width + KV_RANK], unit_latent, factor_latent, gain_latent
    )
    grad_rope = back_sum[:, width + KV_RANK : width + KV_RANK + ROPE].reshape(batches, here, ROPE)
    grad_rope = rotate(grad_rope, cosine_own, -sine_own).reshape(own, ROPE)
    grad_latent_raw = jnp.concatenate([grad_latent_in, grad_rope], axis=1).astype(BF)
    grad_hidden_attn = back_sum[:, :width] + product_trail(grad_latent_raw, latent_full)
    grad_input_norm, grad_gain_attn = norm_backward(grad_hidden_attn, unit_attn, factor_attn, gain_attn)
    grad_input = grad_middle + grad_input_norm

    latent_rows = grad_gain_latent.reshape(dp * GROUPS, rows_l)
    latent_rows = jnp.pad(latent_rows, ((0, 0), (0, rows_w - rows_l))).reshape(width, 1)
    tokens_side = jnp.concatenate([hidden_own, hidden_mix], axis=0)
    grads_side = jnp.concatenate(
        [jnp.pad(grad_latent_raw, ((0, 0), (0, 64))), jnp.pad(grad_logits, ((0, 0), (576, 640 - 592)))], axis=0)
    lane = jnp.arange(640)[None, :]
    small_grad = product_lead(tokens_side, grads_side)
    small_grad = small_grad + jnp.where(lane == 592, grad_gain_attn[:, None], 0.0)
    small_grad = small_grad + jnp.where(lane == 593, grad_gain_mixer[:, None], 0.0)
    small_grad = (small_grad + jnp.where(lane == 594, latent_rows, 0.0)).astype(BF)
    small_grad = small_grad.reshape(dp, GROUPS, rows_w, 640).swapaxes(0, 1).reshape(GROUPS, dp * rows_w, 640)
    small_sum = closing(dp, small_grad, 9)

    def as_input(v):
        return v.reshape(batches, 1, here, width)

    return (
        as_input(layer_output),
        as_input(grad_input),
        small_sum[:, 592],
        out_query,
        small_sum[:, :576],
        small_sum[:rows_l, 594],
        out_expand,
        out_output,
        small_sum[:, 593],
        small_sum[:, 576:592],
        out_gate.astype(F32)[None],
        out_up.astype(F32)[None],
        out_down.astype(F32)[None],
        out_share[:share_width].T,
        out_share[share_width : 2 * share_width].T,
        out_share[2 * share_width :],
    )


def solution(mesh):
    split = P(("dp", "expert"), None)
    line = P(("dp", "expert"))
    tokens = P(None, "dp", "expert", None)
    expert = P("expert", "dp", None)
    return jax.shard_map(
        per_device,
        mesh=mesh,
        in_specs=(
            tokens, tokens, P(None, "dp"), tokens, line, split, split, line, split, split, line, split,
            expert, expert, expert, P("dp", "expert"), P("dp", "expert"), P("expert", "dp"),
        ),
        out_specs=(
            tokens, tokens, line, split, split, line, split, split, line, split,
            expert, expert, expert, P("dp", "expert"), P("dp", "expert"), P("expert", "dp"),
        ),
        check_vma=False,
    )
```

```python
import functools
import jax
import jax.numpy as jnp
import numpy as np
from jax import lax
from jax.experimental import pallas as pl
from jax.experimental.pallas import tpu as pltpu
from jax.sharding import PartitionSpec as P

MESH = pl.DeviceIdType.MESH
NZ = 4
NE = 16


def place():
    me = lax.axis_index("expert")
    z = me // 4
    x = (me // 2) % 2
    c = me % 2
    return me, z, x, c, me + 1 - 2 * c, me + 2 - 4 * x


def enter(me, z, core, side, dp=1):
    barrier = pltpu.get_barrier_semaphore()
    plane = lax.axis_index("dp")
    for r in range(1, dp):
        pl.semaphore_signal(barrier, inc=1, device_id={"dp": (plane + r) % dp}, device_id_type=MESH)
    for other in (core, side):
        pl.semaphore_signal(barrier, inc=1, device_id={"expert": other}, device_id_type=MESH)

    @pl.when(z < NZ - 1)
    def _():
        pl.semaphore_signal(barrier, inc=1, device_id={"expert": me + 4}, device_id_type=MESH)

    @pl.when(z > 0)
    def _():
        pl.semaphore_signal(barrier, inc=1, device_id={"expert": me - 4}, device_id_type=MESH)

    pl.semaphore_wait(barrier, dp + 1 + (z < NZ - 1).astype(jnp.int32) + (z > 0).astype(jnp.int32))


class Spread:
    def __init__(self, dp, src, out, sems):
        self.dp, self.src, self.out = dp, src, out
        self.own, self.send, self.recv = sems
        self.plane = lax.axis_index("dp")

    @staticmethod
    def scratch(dp):
        dma = pltpu.SemaphoreType.DMA
        return [dma, dma((dp,)), dma((dp,))]

    def copy(self, r):
        return pltpu.make_async_remote_copy(
            src_ref=self.src, dst_ref=self.out.at[self.plane], send_sem=self.send.at[r], recv_sem=self.recv.at[r],
            device_id={"dp": (self.plane + r) % self.dp}, device_id_type=MESH)

    def arrival(self, r):
        p = (self.plane - r + self.dp) % self.dp
        return pltpu.make_async_remote_copy(
            src_ref=self.src, dst_ref=self.out.at[p], send_sem=self.send.at[r], recv_sem=self.recv.at[r],
            device_id={"dp": p}, device_id_type=MESH)

    def start(self):
        for r in range(1, self.dp):
            self.copy(r).start()
        self.kept = pltpu.make_async_copy(self.src, self.out.at[self.plane], self.own)
        self.kept.start()

    def finish(self):
        self.kept.wait()
        for r in range(1, self.dp):
            self.arrival(r).wait_recv()
            self.copy(r).wait_send()


def side_job(dp, span, src, out, sems):
    return Spread(dp, src.at[pl.ds(span[0], span[1])], out, sems)


def enter_all(me, plane, dp):
    barrier = pltpu.get_barrier_semaphore()
    for r in range(1, NE):
        pl.semaphore_signal(
            barrier, inc=1, device_id={"expert": (me + r) % NE}, device_id_type=MESH)
    for r in range(1, dp):
        pl.semaphore_signal(
            barrier, inc=1, device_id={"dp": (plane + r) % dp}, device_id_type=MESH)
    pl.semaphore_wait(barrier, NE - 1 + dp - 1)


class Gather:
    def __init__(self, src, out, chunks, sems, view=lambda ref, b: ref.at[b]):
        self.src, self.out, self.chunks, self.view = src, out, chunks, view
        self.rows = src.shape[0] // chunks
        (self.own_sem, self.us, self.ur, self.ds, self.dr, self.bus, self.bur, self.bds, self.bdr,
         self.xs, self.xr, self.cs, self.cr) = sems
        self.me, self.z, self.x, self.c, self.core, self.side = place()

    COUNT = 13

    @staticmethod
    def scratch(chunks):
        dma = pltpu.SemaphoreType.DMA
        return [dma] + [dma((4, chunks))] * 8 + [dma((7, chunks))] * 2 + [dma((14, chunks))] * 2

    def alt(self, k):
        return k >= (self.chunks + 1) // 2

    def order(self):
        return range(self.chunks - 1, -1, -1)

    def copy(self, block, k, src, send, recv, to):
        src_ref = self.src if src is None else self.view(self.out, src)
        dst_ref = self.view(self.out, block)
        if self.chunks > 1:
            part = pl.ds(k * self.rows, self.rows)
            src_ref, dst_ref = src_ref.at[part], dst_ref.at[part]
        return pltpu.make_async_remote_copy(
            src_ref=src_ref,
            dst_ref=dst_ref,
            send_sem=send, recv_sem=recv,
            device_id={"expert": to}, device_id_type=MESH,
        )

    def up(self, k, s, src=None):
        return self.copy(self.me - 4 * s, k, src, self.us.at[s, k], self.ur.at[s, k], self.me + 4)

    def down(self, k, s, src=None):
        return self.copy(self.me + 4 * s, k, src, self.ds.at[s, k], self.dr.at[s, k], self.me - 4)

    def up_b(self, k, s):
        b = self.side - 4 * s
        return self.copy(b, k, b, self.bus.at[s, k], self.bur.at[s, k], self.me + 4)

    def down_b(self, k, s):
        b = self.side + 4 * s
        return self.copy(b, k, b, self.bds.at[s, k], self.bdr.at[s, k], self.me - 4)

    def across(self, k, slot, block, src=None):
        return self.copy(block, k, src, self.xs.at[slot, k], self.xr.at[slot, k], self.side)

    def over(self, k, slot, block, src=None):
        return self.copy(block, k, src, self.cs.at[slot, k], self.cr.at[slot, k], self.core)

    def arrived(self, b, k, sems, s):
        return self.copy(b, k, b, sems[0].at[s - 1, k], sems[1].at[s - 1, k], self.side)

    def shift(self, base, slot):
        return base - 4 * slot if slot <= 3 else base + 4 * (slot - 3)

    def core_block(self, slot):
        if slot < 7:
            return self.shift(self.core, slot)
        return self.shift(self.core + 2 - 4 * self.x, slot - 7)

    def has(self, slot):
        slot = slot % 7
        if slot == 0:
            return self.z >= 0
        return self.z >= slot if slot <= 3 else self.z + (slot - 3) <= NZ - 1

    def crosses(self, k, slot):
        if slot == 0 or not self.alt(k):
            return self.has(slot)
        return self.z > slot if slot <= 3 else self.z + (slot - 3) < NZ - 1

    def start(self):
        z, me = self.z, self.me
        self.own = pltpu.make_async_copy(self.src, self.view(self.out, me), self.own_sem)
        self.own.start()
        for k in self.order():
            self.across(k, 0, me).start()

            @pl.when(z < NZ - 1)
            def _():
                self.up(k, 0).start()

            @pl.when(z > 0)
            def _():
                self.down(k, 0).start()

            self.over(k, 0, me).start()

    def line(self, k, s):
        z, me = self.z, self.me

        @pl.when(z >= s)
        def _():
            b = me - 4 * s
            self.arrived(b, k, (self.us, self.ur), s).wait_recv()

            @pl.when(self.crosses(k, s))
            def _():
                self.across(k, s, b, b).start()

            @pl.when(z < NZ - 1)
            def _():
                self.up(k, s, b).start()

            self.over(k, s, b, b).start()

        @pl.when(z + s <= NZ - 1)
        def _():
            b = me + 4 * s
            self.arrived(b, k, (self.ds, self.dr), s).wait_recv()

            @pl.when(self.crosses(k, 3 + s))
            def _():
                self.across(k, 3 + s, b, b).start()

            @pl.when(z > 0)
            def _():
                self.down(k, s, b).start()

            self.over(k, 3 + s, b, b).start()

    def line_b(self, k, s):
        z = self.z

        @pl.when(z == s)
        def _():
            b = self.side - 4 * s
            self.arrived(b, k, (self.bus, self.bur), s).wait_recv()

            @pl.when(z < NZ - 1)
            def _():
                self.up_b(k, s).start()

            self.over(k, 7 + s, b, b).start()

        @pl.when(z + s == NZ - 1)
        def _():
            b = self.side + 4 * s
            self.arrived(b, k, (self.bds, self.bdr), s).wait_recv()

            @pl.when(z > 0)
            def _():
                self.down_b(k, s).start()

            self.over(k, 10 + s, b, b).start()

    def from_side(self, k, slot):
        @pl.when(self.crosses(k, slot))
        def _():
            b = self.shift(self.side, slot)
            self.across(k, slot, b, b).wait_recv()
            if slot == 0 and self.alt(k):
                @pl.when(self.z == 0)
                def _():
                    self.up_b(k, 0).start()

                @pl.when(self.z == NZ - 1)
                def _():
                    self.down_b(k, 0).start()

            self.over(k, 7 + slot, b, b).start()

    def round(self, s):
        if s < NZ:
            for k in self.order():
                self.line(k, s)
        for k in self.order():
            for slot in ((0,) if s == 1 else (s - 1, s + 2)):
                self.from_side(k, slot)
        if s > 1:
            for k in self.order():
                if self.alt(k):
                    self.line_b(k, s - 1)

    def finish(self):
        z = self.z
        self.own.wait()
        for k in self.order():
            for slot in range(14):
                @pl.when(self.has(slot))
                def _():
                    b = self.core_block(slot)
                    self.over(k, slot, b, b).wait_recv()
                    self.over(k, slot, b, b).wait_send()
            for slot in range(7):
                @pl.when(self.crosses(k, slot))
                def _():
                    self.across(k, slot, self.me).wait_send()
            for s in range(NZ - 1):
                @pl.when((z >= s) & (z < NZ - 1))
                def _():
                    self.up(k, s).wait_send()

                @pl.when((z + s <= NZ - 1) & (z > 0))
                def _():
                    self.down(k, s).wait_send()

                if self.alt(k):
                    @pl.when(z == s)
                    def _():
                        self.up_b(k, s).wait_send()

                    @pl.when(z + s == NZ - 1)
                    def _():
                        self.down_b(k, s).wait_send()


def gather_kernel(chunks, dp, span, x_ref, *refs):
    job = None
    ng = Gather.COUNT
    if span is None:
        o_ref, *sems = refs
    else:
        src, o_ref, out, *sems = refs
        job = side_job(dp, span, src, out, sems[ng:])
    g = Gather(x_ref, o_ref, chunks, sems[:ng])
    enter(g.me, g.z, g.core, g.side, 1 if job is None else dp)
    g.start()
    if job is not None:
        job.start()
    for s in range(1, NZ + 1):
        g.round(s)
    g.finish()
    if job is not None:
        job.finish()


COST = pl.CostEstimate(flops=0, bytes_accessed=4_000_000, transcendentals=0)
ANY = pl.BlockSpec(memory_space=pl.ANY)


def gather16(v, cid, chunks=2, dp=1, span=None, side=None):
    rows, width = v.shape
    extra = span is not None
    out = pl.pallas_call(
        functools.partial(gather_kernel, chunks, dp, span),
        out_shape=(jax.ShapeDtypeStruct((NE, rows, width), v.dtype),)
        + ((jax.ShapeDtypeStruct((dp, span[1], side.shape[1]), side.dtype),) if extra else ()),
        in_specs=[ANY] * (2 if extra else 1),
        out_specs=(ANY,) * (2 if extra else 1),
        scratch_shapes=Gather.scratch(chunks) + (Spread.scratch(dp) if extra else []),
        compiler_params=pltpu.CompilerParams(collective_id=cid, has_side_effects=True),
        cost_estimate=COST,
        name="gather16",
    )(*((v, side) if extra else (v,)))
    return out if extra else out[0]


def opening_kernel(dp, chunks, x_ref, small_ref, parts_ref, out_ref,
                   x_all, small_all, parts_head, out_head, small_dp, parts_dp, out_dp, *sems):
    ng = Gather.COUNT
    gx = Gather(x_ref, x_all, chunks, sems[:ng])
    gs = Gather(small_dp, small_all, 1, sems[ng:2 * ng], lambda ref, b: ref.at[:, b])
    loc, ys, yr, ps, pr, os_, or_, pl_sem, ol_sem = sems[2 * ng:]
    me = gx.me
    plane = lax.axis_index("dp")
    enter_all(me, plane, dp)
    pairs = ((small_ref, small_dp.at[plane]), (parts_ref, parts_dp.at[plane]),
             (out_ref, out_dp.at[plane]))

    def lift(i, r):
        src, dst = pairs[i]
        return pltpu.make_async_remote_copy(
            src_ref=src, dst_ref=dst, send_sem=ys.at[i, r], recv_sem=yr.at[i, r],
            device_id={"dp": (plane + r) % dp}, device_id_type=MESH)

    def landed(i, r):
        p = (plane - r + dp) % dp
        dst = (small_dp.at[p], parts_dp.at[p], out_dp.at[p])[i]
        return pltpu.make_async_remote_copy(
            src_ref=dst, dst_ref=dst, send_sem=ys.at[i, r], recv_sem=yr.at[i, r],
            device_id={"dp": p}, device_id_type=MESH)

    def kept(i):
        src, dst = pairs[i]
        return pltpu.make_async_copy(src, dst, loc.at[i])

    for i in range(3):
        for r in range(1, dp):
            lift(i, r).start()
        kept(i).start()
    gx.start()
    gx.round(1)

    kept(0).wait()
    for r in range(1, dp):
        landed(0, r).wait_recv()
    gs.start()

    def part(r):
        h = (me + r) % NE
        return pltpu.make_async_remote_copy(
            src_ref=parts_dp.at[:, h], dst_ref=parts_head.at[:, me],
            send_sem=ps.at[r], recv_sem=pr.at[r],
            device_id={"expert": h}, device_id_type=MESH)

    def part_in(r):
        e = (me - r + NE) % NE
        return pltpu.make_async_remote_copy(
            src_ref=parts_head.at[:, e], dst_ref=parts_head.at[:, e],
            send_sem=ps.at[r], recv_sem=pr.at[r],
            device_id={"expert": e}, device_id_type=MESH)

    def part_kept():
        return pltpu.make_async_copy(parts_dp.at[:, me], parts_head.at[:, me], pl_sem)

    kept(1).wait()
    for r in range(1, dp):
        landed(1, r).wait_recv()
    for r in range(1, NE):
        part(r).start()
    part_kept().start()
    gx.round(2)

    def row(d):
        b = NE * d + me
        return pltpu.make_async_remote_copy(
            src_ref=out_dp.at[d], dst_ref=out_head.at[b % dp],
            send_sem=os_.at[d], recv_sem=or_.at[b % dp],
            device_id={"expert": b // dp}, device_id_type=MESH)

    def row_kept(d):
        b = NE * d + me
        return pltpu.make_async_copy(out_dp.at[d], out_head.at[b % dp], ol_sem.at[d])

    kept(2).wait()
    for r in range(1, dp):
        landed(2, r).wait_recv()
    for d in range(dp):
        home = (NE * d + me) // dp

        @pl.when(home != me)
        def _():
            row(d).start()

        @pl.when(home == me)
        def _():
            row_kept(d).start()

    gs.round(1)
    gx.round(3)
    gs.round(2)
    gx.round(4)
    gs.round(3)
    gs.round(4)

    def row_in(j):
        return pltpu.make_async_remote_copy(
            src_ref=out_head.at[j], dst_ref=out_head.at[j], send_sem=os_.at[j], recv_sem=or_.at[j],
            device_id={"expert": gx.core}, device_id_type=MESH)

    for r in range(1, NE):
        part_in(r).wait_recv()
        part(r).wait_send()
    part_kept().wait()
    for j in range(dp):
        @pl.when((dp * me + j) % NE != me)
        def _():
            row_in(j).wait_recv()
    for d in range(dp):
        home = (NE * d + me) // dp

        @pl.when(home != me)
        def _():
            row(d).wait_send()

        @pl.when(home == me)
        def _():
            row_kept(d).wait()
    for i in range(3):
        for r in range(1, dp):
            lift(i, r).wait_send()
    gx.finish()
    gs.finish()


def opening(dp, x, small, parts, out, cid, chunks=2):
    dma = pltpu.SemaphoreType.DMA
    rows, ws = small.shape
    bf = x.dtype
    wo = out.shape[1]
    shape = jax.ShapeDtypeStruct
    res = pl.pallas_call(
        functools.partial(opening_kernel, dp, chunks),
        out_shape=(
            shape((NE,) + x.shape, bf), shape((dp, NE, rows, ws), bf), shape((dp, NE) + parts.shape[1:], bf),
            shape((dp, rows, wo), bf),
            shape((dp, rows, ws), bf), shape((dp,) + parts.shape, bf), shape((dp, rows, wo), bf),
        ),
        in_specs=[ANY] * 4,
        out_specs=[ANY] * 7,
        scratch_shapes=Gather.scratch(chunks) + Gather.scratch(1) + [
            dma((3,)), dma((3, dp)), dma((3, dp)), dma((NE,)), dma((NE,)), dma((dp,)), dma((dp,)), dma, dma((dp,))],
        compiler_params=pltpu.CompilerParams(collective_id=cid, has_side_effects=True),
        cost_estimate=COST,
        name="opening",
    )(x, small, parts, out)
    return res[:4]


def order(z, i):
    a, b = (3, 2, 1, 0)[i], (3, 2, 0, 1)[i]
    return jnp.where(z == 0, a, jnp.where(z == 1, b, jnp.where(z == 2, 3 - b, 3 - a)))


class Scatter:
    COUNT = 14

    def __init__(self, p_ref, o_ref, chunks, scratch):
        self.p, self.o, self.chunks = p_ref, o_ref, chunks
        (self.cbuf, self.own, self.xbuf, self.ubuf, self.dbuf, self.ld, self.cs, self.cr, self.xs, self.xr,
         self.us, self.ur, self.ds, self.dr) = scratch
        self.rows = o_ref.shape[0] // chunks
        self.me, self.z, self.x, self.c, self.core, self.side = place()

    @staticmethod
    def scratch(rows, width, chunks, bf):
        dma = pltpu.SemaphoreType.DMA
        return [pltpu.VMEM((n, rows, width), bf) for n in (8, 8, 4, 4, 4)] + [
            dma((8,)), dma((8, chunks)), dma((8, chunks))] + [dma((4, chunks))] * 6

    def rng(self, k):
        return pl.ds(k * self.rows, self.rows)

    def column(self, i, j):
        return 4 * order(self.z, i) + 2 * jnp.where(j == 0, 1 - self.x, self.x)

    def remote(self, src, dst, send, recv, to):
        return pltpu.make_async_remote_copy(
            src_ref=src, dst_ref=dst, send_sem=send, recv_sem=recv,
            device_id={"expert": to}, device_id_type=MESH)

    def over(self, i, j, k):
        n = 2 * i + j
        return self.remote(
            self.p.at[self.column(i, j) + 1 - self.c, self.rng(k)], self.cbuf.at[n, self.rng(k)],
            self.cs.at[n, k], self.cr.at[n, k], self.core)

    def load(self, i, j):
        n = 2 * i + j
        return pltpu.make_async_copy(self.p.at[self.column(i, j) + self.c], self.own.at[n], self.ld.at[n])

    def across(self, i, k):
        return self.remote(self.own.at[2 * i, self.rng(k)], self.xbuf.at[i, self.rng(k)],
                           self.xs.at[i, k], self.xr.at[i, k], self.side)

    def up(self, t, i, k):
        return self.remote(self.own.at[2 * i + 1, self.rng(k)], self.ubuf.at[t, self.rng(k)],
                           self.us.at[t, k], self.ur.at[t, k], self.me + 4)

    def down(self, t, i, k):
        return self.remote(self.own.at[2 * i + 1, self.rng(k)], self.dbuf.at[t, self.rng(k)],
                           self.ds.at[t, k], self.dr.at[t, k], self.me - 4)

    def start(self):
        for i in range(NZ):
            for j in range(2):
                self.load(i, j).start()
                for k in range(self.chunks):
                    self.over(i, j, k).start()

    def first(self, i):
        f32 = jnp.float32
        self.load(i, 0).wait()
        for k in range(self.chunks):
            self.over(i, 0, k).wait_recv()
            s = self.rng(k)
            self.own[2 * i, s] = (
                self.own[2 * i, s].astype(f32) + self.cbuf[2 * i, s].astype(f32)).astype(self.own.dtype)
            self.across(i, k).start()

    def second(self, i):
        f32 = jnp.float32
        z, own, o = self.z, self.own, self.o
        t = order(z, i)
        self.load(i, 1).wait()
        for k in range(self.chunks):
            s = self.rng(k)
            self.over(i, 1, k).wait_recv()
            self.across(i, k).wait_recv()

            def base():
                return (own[2 * i + 1, s].astype(f32) + self.cbuf[2 * i + 1, s].astype(f32)
                        + self.xbuf[i, s].astype(f32))

            if i < NZ - 1:
                @pl.when(t > z)
                def _():
                    @pl.when(z > 0)
                    def _():
                        self.up(t, i, k).wait_recv()
                        own[2 * i + 1, s] = (base() + self.ubuf[t, s].astype(f32)).astype(own.dtype)

                    @pl.when(z == 0)
                    def _():
                        own[2 * i + 1, s] = base().astype(own.dtype)

                    self.up(t, i, k).start()

                @pl.when(t < z)
                def _():
                    @pl.when(z < NZ - 1)
                    def _():
                        self.down(t, i, k).wait_recv()
                        own[2 * i + 1, s] = (base() + self.dbuf[t, s].astype(f32)).astype(own.dtype)

                    @pl.when(z == NZ - 1)
                    def _():
                        own[2 * i + 1, s] = base().astype(own.dtype)

                    self.down(t, i, k).start()
            else:
                @pl.when(z > 0)
                def _():
                    self.up(t, i, k).wait_recv()

                @pl.when(z < NZ - 1)
                def _():
                    self.down(t, i, k).wait_recv()

                @pl.when((z > 0) & (z < NZ - 1))
                def _():
                    o[s] = (base() + self.ubuf[t, s].astype(f32) + self.dbuf[t, s].astype(f32)).astype(o.dtype)

                @pl.when(z == 0)
                def _():
                    o[s] = (base() + self.dbuf[t, s].astype(f32)).astype(o.dtype)

                @pl.when(z == NZ - 1)
                def _():
                    o[s] = (base() + self.ubuf[t, s].astype(f32)).astype(o.dtype)

    def run(self, between=lambda: None):
        self.first(0)
        for i in range(NZ):
            if i + 1 < NZ:
                self.first(i + 1)
            between()
            self.second(i)
            between()

    def finish(self):
        z = self.z
        for k in range(self.chunks):
            for i in range(NZ):
                self.across(i, k).wait_send()
                for j in range(2):
                    self.over(i, j, k).wait_send()
                if i < NZ - 1:
                    t = order(z, i)

                    @pl.when(t > z)
                    def _():
                        self.up(t, i, k).wait_send()

                    @pl.when(t < z)
                    def _():
                        self.down(t, i, k).wait_send()


def scatter_kernel(chunks, p_ref, o_ref, *scratch):
    s = Scatter(p_ref, o_ref, chunks, scratch)
    enter(s.me, s.z, s.core, s.side)
    s.start()
    s.run()
    s.finish()


VMEM = pl.BlockSpec(memory_space=pltpu.VMEM)


def scatter16(p, cid, chunks=2):
    _, rows, width = p.shape
    return pl.pallas_call(
        functools.partial(scatter_kernel, chunks),
        out_shape=jax.ShapeDtypeStruct((rows, width), jnp.float32),
        in_specs=[ANY],
        out_specs=VMEM,
        scratch_shapes=Scatter.scratch(rows, width, chunks, p.dtype),
        compiler_params=pltpu.CompilerParams(
            collective_id=cid, has_side_effects=True, vmem_limit_bytes=60 * 1024 * 1024),
        cost_estimate=COST,
        name="scatter16",
    )(p)


def return_kernel(dp, chunks, p_ref, parts_ref, rows_ref, o_ref, parts_in, rows_in, parts_far, rows_far, *scratch):
    ns = Scatter.COUNT
    s = Scatter(p_ref, o_ref, chunks, scratch[:ns])
    ps, pr, os_, or_, pl_sem, ol_sem, ys, yr = scratch[ns:]
    me = s.me
    plane = lax.axis_index("dp")
    enter_all(me, plane, dp)

    def part(r):
        e = (me + r) % NE
        return pltpu.make_async_remote_copy(
            src_ref=parts_ref.at[:, e], dst_ref=parts_in.at[:, me],
            send_sem=ps.at[r], recv_sem=pr.at[r],
            device_id={"expert": e}, device_id_type=MESH)

    def part_in(r):
        h = (me - r + NE) % NE
        return pltpu.make_async_remote_copy(
            src_ref=parts_in.at[:, h], dst_ref=parts_in.at[:, h],
            send_sem=ps.at[r], recv_sem=pr.at[r],
            device_id={"expert": h}, device_id_type=MESH)

    def part_kept():
        return pltpu.make_async_copy(parts_ref.at[:, me], parts_in.at[:, me], pl_sem)

    def row(j):
        b = dp * me + j
        return pltpu.make_async_remote_copy(
            src_ref=rows_ref.at[j], dst_ref=rows_in.at[b // NE],
            send_sem=os_.at[j], recv_sem=or_.at[b // NE],
            device_id={"expert": b % NE}, device_id_type=MESH)

    def row_kept(j):
        b = dp * me + j
        return pltpu.make_async_copy(rows_ref.at[j], rows_in.at[b // NE], ol_sem.at[j])

    def row_in(d):
        return pltpu.make_async_remote_copy(
            src_ref=rows_in.at[d], dst_ref=rows_in.at[d], send_sem=os_.at[d], recv_sem=or_.at[d],
            device_id={"expert": s.core}, device_id_type=MESH)

    def lift(i, r):
        to = (plane + r) % dp
        src, dst = ((parts_in.at[to], parts_far.at[r - 1]), (rows_in.at[to], rows_far.at[r - 1]))[i]
        return pltpu.make_async_remote_copy(
            src_ref=src, dst_ref=dst, send_sem=ys.at[i, r], recv_sem=yr.at[i, r],
            device_id={"dp": to}, device_id_type=MESH)

    s.start()
    for r in range(1, NE):
        part(r).start()
    part_kept().start()
    for j in range(dp):
        @pl.when((dp * me + j) % NE != me)
        def _():
            row(j).start()

        @pl.when((dp * me + j) % NE == me)
        def _():
            row_kept(j).start()
    s.first(0)
    s.first(1)
    s.second(0)
    for r in range(1, NE):
        part_in(r).wait_recv()
    part_kept().wait()
    for j in range(dp):
        @pl.when((dp * me + j) % NE == me)
        def _():
            row_kept(j).wait()
    for d in range(dp):
        @pl.when((NE * d + me) // dp != me)
        def _():
            row_in(d).wait_recv()
    for i in range(2):
        for r in range(1, dp):
            lift(i, r).start()
    s.first(2)
    s.second(1)
    s.first(3)
    s.second(2)
    s.second(3)
    for i in range(2):
        for r in range(1, dp):
            lift(i, r).wait_recv()
            lift(i, r).wait_send()
    for r in range(1, NE):
        part(r).wait_send()
    for j in range(dp):
        @pl.when((dp * me + j) % NE != me)
        def _():
            row(j).wait_send()
    s.finish()


def returning(dp, p, parts, rows, cid, chunks=2):
    dma = pltpu.SemaphoreType.DMA
    _, n, width = p.shape
    shape = jax.ShapeDtypeStruct
    out, parts_in, rows_in, parts_far, rows_far = pl.pallas_call(
        functools.partial(return_kernel, dp, chunks),
        out_shape=(
            shape((n, width), jnp.float32), shape(parts.shape, parts.dtype), shape(rows.shape, rows.dtype),
            shape((dp - 1,) + parts.shape[1:], parts.dtype), shape((dp - 1,) + rows.shape[1:], rows.dtype)),
        in_specs=[ANY] * 3,
        out_specs=[VMEM] + [ANY] * 4,
        scratch_shapes=Scatter.scratch(n, width, chunks, p.dtype) + [
            dma((NE,)), dma((NE,)), dma((dp,)), dma((dp,)), dma, dma((dp,)), dma((2, dp)), dma((2, dp))],
        compiler_params=pltpu.CompilerParams(
            collective_id=cid, has_side_effects=True, vmem_limit_bytes=60 * 1024 * 1024),
        cost_estimate=COST,
        name="returning",
    )(p, parts, rows)
    plane = lax.axis_index("dp")

    def total(near, far):
        own = lax.dynamic_index_in_dim(near, plane, 0, False).astype(jnp.float32)
        return own + jnp.sum(far.astype(jnp.float32), axis=0)

    return out, total(parts_in, parts_far), total(rows_in, rows_far)


def closing_kernel(dp, chunks, p_ref, o_ref, far_ref, *scratch):
    ns = Scatter.COUNT
    s = Scatter(p_ref, o_ref, chunks, scratch[:ns])
    ys, yr = scratch[ns:]
    plane = lax.axis_index("dp")
    rows = o_ref.shape[0] // dp
    enter(s.me, s.z, s.core, s.side, dp)

    def lift(r):
        to = (plane + r) % dp
        return pltpu.make_async_remote_copy(
            src_ref=o_ref.at[pl.ds(pl.multiple_of(to * rows, 16), rows)], dst_ref=far_ref.at[r - 1],
            send_sem=ys.at[r], recv_sem=yr.at[r],
            device_id={"dp": to}, device_id_type=MESH)

    s.start()
    s.run()
    for r in range(1, dp):
        lift(r).start()
    s.finish()
    for r in range(1, dp):
        lift(r).wait_recv()
        lift(r).wait_send()


def closing(dp, p, cid):
    dma = pltpu.SemaphoreType.DMA
    _, n, width = p.shape
    shape = jax.ShapeDtypeStruct
    near, far = pl.pallas_call(
        functools.partial(closing_kernel, dp, 1),
        out_shape=(shape((n, width), p.dtype), shape((dp - 1, n // dp, width), p.dtype)),
        in_specs=[ANY],
        out_specs=[VMEM, VMEM],
        scratch_shapes=Scatter.scratch(n, width, 1, p.dtype) + [dma((dp,)), dma((dp,))],
        compiler_params=pltpu.CompilerParams(
            collective_id=cid, has_side_effects=True, vmem_limit_bytes=32 * 1024 * 1024),
        cost_estimate=COST,
        name="closing",
    )(p)
    own = lax.dynamic_slice_in_dim(near, lax.axis_index("dp") * (n // dp), n // dp).astype(jnp.float32)
    return own + jnp.sum(far.astype(jnp.float32), axis=0)
BF = jnp.bfloat16
F32 = jnp.float32


def mm(a, b):
    return jnp.dot(a, b, preferred_element_type=F32)


def mm_t(a, b):
    return lax.dot_general(a, b, (((1,), (1,)), ((), ())), preferred_element_type=F32)


def silu_pair(gate_in):
    sigmoid = 1.0 / (1.0 + jnp.exp(-gate_in))
    return (gate_in * sigmoid, sigmoid * (1.0 + gate_in * (1.0 - sigmoid)))


TILE = 256
WIDE = 512
SHARE = 176


def down_copies(a_ref, b_ref, out, sem, which):
    dp, a, _ = a_ref.shape
    rows = a + b_ref.shape[1]
    if which == 0:
        return [pltpu.make_async_copy(a_ref.at[d], out.at[pl.ds(d * rows, a)], sem.at[d]) for d in range(dp)]
    return [pltpu.make_async_copy(b_ref.at[d], out.at[pl.ds(d * rows + a, rows - a)], sem.at[dp + d])
            for d in range(dp)]


def share_copies(share_ref, fan, down, sem):
    dp, rows, w = share_ref.shape
    n = rows // 3
    copies = []
    for d in range(dp):
        cols = pl.ds(d * w, w)
        for i, (dst, first) in enumerate(((fan, 0), (fan, TILE), (down, 0))):
            copies.append(pltpu.make_async_copy(
                share_ref.at[d, pl.ds(i * n, n)], dst.at[pl.ds(first, n), cols], sem.at[3 * d + i]))
    return copies


def share_blank(fan, down):
    pad = jnp.zeros((TILE - SHARE, fan.shape[1]), BF)
    fan[SHARE:TILE] = pad
    fan[TILE + SHARE:] = pad
    down[SHARE:] = pad


def mine_of(routes_ref, pick_ref):
    tokens = routes_ref.shape[0]
    lane16 = lax.broadcasted_iota(jnp.int32, (tokens, 16), 1)
    mask = lane16 < 0
    for k in range(routes_ref.shape[1]):
        mask = mask | (lane16 == routes_ref[:, k:k + 1])
    mine = jnp.sum(jnp.where(mask, pick_ref[:, :16], 0.0), axis=1, keepdims=True)
    return mask, mine


def valid_of(len_ref, first_device, tokens, batches, here):
    n = lax.broadcasted_iota(jnp.int32, (tokens, 1), 0)
    device = n // (batches * here)
    batch = (n // here) % batches
    position = (first_device + device) * here + n % here
    length = jnp.zeros((tokens, 1), jnp.int32)
    for b in range(batches):
        length = jnp.where(batch == b, len_ref[b], length)
    return (position < length).astype(F32)


def one_hots(taken, groups, slots, here):
    r = lax.broadcasted_iota(jnp.int32, (256, 256), 0)
    c = lax.broadcasted_iota(jnp.int32, (256, 256), 1)
    same = r // here == c // here
    before = (same & (c < r)).astype(BF)
    after = (same & (r < c)).astype(BF)
    base_c = (lax.broadcasted_iota(jnp.int32, (256, slots), 0) // here * 32).astype(F32)
    base_r = (lax.broadcasted_iota(jnp.int32, (slots, 256), 1) // here * 32).astype(F32)
    lane = lax.broadcasted_iota(jnp.int32, (256, slots), 1).astype(F32)
    row = lax.broadcasted_iota(jnp.int32, (slots, 256), 0).astype(F32)
    ones = jnp.ones((256, slots), BF)
    to_slot, to_token = [], []
    for g in range(groups):
        t = jnp.broadcast_to(taken[g * 256:(g + 1) * 256], (256, slots))
        low = t.astype(BF)
        place_c = mm(before, low) + base_c
        place_r = mm_lead(low, after) + base_r
        taken_r = mm_lead(low, (r == c).astype(BF))
        to_token.append(jnp.where((place_c == lane) & (t > 0.5), 1.0, 0.0).astype(BF))
        to_slot.append(jnp.where((place_r == row) & (taken_r > 0.5), 1.0, 0.0).astype(BF))
    return to_slot, to_token


def mm_lead(a, b):
    return lax.dot_general(a, b, (((0,), (0,)), ((), ())), preferred_element_type=F32)


def lanes(j):
    return pl.ds(pl.multiple_of(j * WIDE, WIDE), WIDE)


def over_columns(total, body):
    def step(j, _):
        body(pl.multiple_of(j * WIDE, WIDE), WIDE)
        return 0

    lax.fori_loop(0, total // WIDE, step, 0)
    if total % WIDE:
        body(total // WIDE * WIDE, total % WIDE)


def forward_kernel(chunks, dp, span, batches, here, len_ref, pick_ref, mix_ref, routes_ref, wg_ref, wu_ref, router_ref,
                   share_ref, wda_ref, down_ref, dy_ref,
                   out_ref, rows_ref, hid_ref, act_ref, slo_ref, eo_ref, sh_ref, sact_ref, sslo_ref, gate_ref,
                   dy_all, wdb_ref,
                   wd_ref, fan_ref, sd_ref, hid_buf, sh_buf, gate_buf, taken_buf, wd_sem, sh_sem, *sems):
    step = pl.program_id(0)
    tokens, width = mix_ref.shape
    groups, slots = tokens // 256, 128
    half = groups * slots
    ff = hid_ref.shape[1]
    phase = pl.num_programs(0) // 2
    g = Gather(dy_ref, dy_all, chunks, sems[:Gather.COUNT])
    job = side_job(dp, span, down_ref, wdb_ref, sems[Gather.COUNT:])

    @pl.when(step == 0)
    def _():
        enter(g.me, g.z, g.core, g.side, dp)
        g.start()
        job.start()
        for copy in down_copies(wda_ref, wdb_ref, wd_ref, wd_sem, 0) + share_copies(share_ref, fan_ref, sd_ref, sh_sem):
            copy.start()
        share_blank(fan_ref, sd_ref)
        fan_ref[SHARE:SHARE + 16] = router_ref[...]
        for copy in share_copies(share_ref, fan_ref, sd_ref, sh_sem):
            copy.wait()

    @pl.when(step < phase)
    def _():
        mix = mix_ref[...]
        fanned = mm_t(mix, fan_ref[:TILE, :])
        s_up = mm_t(mix, fan_ref[TILE:, :])
        s_act, s_slope = silu_pair(fanned)
        s_hidden = (s_act * s_up).astype(BF)
        at = pl.ds(pl.multiple_of(step * tokens, tokens), tokens)
        sh_ref[...] = s_hidden
        sh_buf[at] = s_hidden
        sact_ref[...] = s_act.astype(BF)
        sslo_ref[...] = (s_up * s_slope).astype(BF)
        logits = fanned[:, SHARE:SHARE + 16]
        mask, mine = mine_of(routes_ref, pick_ref)
        taken = mine * valid_of(len_ref, step * (tokens // (batches * here)), tokens, batches, here)
        held = jnp.where(mask, logits, -1e30)
        raised = jnp.where(mask, jnp.exp(held - jnp.max(held, axis=1, keepdims=True)), 0.0)
        soft = raised / jnp.sum(raised, axis=1, keepdims=True)
        gate = jnp.sum(soft * pick_ref[:, :16], axis=1, keepdims=True) * taken
        gate_ref[...] = jnp.concatenate([gate, taken], axis=1)
        gate_buf[at] = gate
        taken_buf[at] = taken
        to_slot, _ = one_hots(taken, groups, slots, here)

        def dispatch(j, _):
            for n in range(groups):
                rows_ref[n * slots:(n + 1) * slots, lanes(j)] = mm(
                    to_slot[n], mix_ref[n * 256:(n + 1) * 256, lanes(j)]).astype(BF)
            return 0

        lax.fori_loop(0, width // WIDE, dispatch, 0)
        rows_at = pl.ds(pl.multiple_of(step * half, half), half)

        def fan_in(start, size):
            cols = pl.ds(start, size)
            gate_in = mm(rows_ref[...], wg_ref[:, cols])
            up_in = mm(rows_ref[...], wu_ref[:, cols])
            act, slope = silu_pair(gate_in)
            hidden = (act * up_in).astype(BF)
            hid_ref[:, cols] = hidden
            hid_buf[rows_at, cols] = hidden
            act_ref[:, cols] = act.astype(BF)
            slo_ref[:, cols] = (up_in * slope).astype(BF)

        over_columns(ff, fan_in)

    @pl.when(step == phase)
    def _():
        job.finish()
        for copy in down_copies(wda_ref, wdb_ref, wd_ref, wd_sem, 1):
            copy.start()
        for which in range(2):
            for copy in down_copies(wda_ref, wdb_ref, wd_ref, wd_sem, which):
                copy.wait()

    @pl.when(step >= phase)
    def _():
        tile = step - phase
        at = pl.ds(pl.multiple_of(tile * tokens, tokens), tokens)
        rows_at = pl.ds(pl.multiple_of(tile * half, half), half)
        gate = gate_buf[at]
        s_hidden = sh_buf[at]
        _, to_token = one_hots(taken_buf[at], groups, slots, here)

        def fan_out(j, _):
            eo = mm(hid_buf[rows_at], wd_ref[:, lanes(j)]).astype(BF)
            eo_ref[:, lanes(j)] = eo
            shared = mm(s_hidden, sd_ref[:, lanes(j)])
            picked = jnp.concatenate(
                [mm(to_token[n], eo[n * slots:(n + 1) * slots]) for n in range(groups)], axis=0)
            out_ref[:, lanes(j)] = (shared + gate * picked).astype(BF)
            return 0

        lax.fori_loop(0, width // WIDE, fan_out, 0)

    for r, s in ((1, 1), (2, 3), (3, 5), (4, 7)):
        @pl.when(step == s)
        def _():
            g.round(r)

    @pl.when(step == 2 * phase - 1)
    def _():
        g.finish()


def backward_kernel(here, chunks, pick_ref, dy_ref, wg_ref, wu_ref, share_ref, wda_ref, wdb_ref,
                    act_ref, slo_ref, eo_ref, sact_ref, sslo_ref, gate_ref, part_ref,
                    dh_ref, deo_ref, dg_ref, du_ref, ds_ref, sum_ref,
                    wd_ref, fan_ref, sd_ref, wd_sem, sh_sem, *scratch):
    step = pl.program_id(0)
    tokens, width = dy_ref.shape
    groups, slots = tokens // 256, 128
    ff = dg_ref.shape[1]
    sc = Scatter(part_ref, sum_ref, chunks, scratch)

    @pl.when(step == 0)
    def _():
        enter(sc.me, sc.z, sc.core, sc.side)
        copies = share_copies(share_ref, fan_ref, sd_ref, sh_sem)
        for which in range(2):
            copies += down_copies(wda_ref, wdb_ref, wd_ref, wd_sem, which)
        for copy in copies:
            copy.start()
        sc.start()
        share_blank(fan_ref, sd_ref)
        for copy in copies:
            copy.wait()

    d_sh = mm_t(dy_ref[...], sd_ref[...])
    d_s = jnp.concatenate([(d_sh * sslo_ref[...].astype(F32)).astype(BF),
                           (d_sh * sact_ref[...].astype(F32)).astype(BF)], axis=1)
    ds_ref[...] = d_s
    gate, taken = gate_ref[:, :1], gate_ref[:, 1:]
    to_slot, to_token = one_hots(taken, groups, slots, here)

    @pl.when(step == 0)
    def _():
        sc.first(0)
        sc.first(1)

    def dispatch(j, total):
        dy = dy_ref[:, lanes(j)].astype(F32)
        gated = (gate * dy).astype(BF)
        for n in range(groups):
            deo_ref[n * slots:(n + 1) * slots, lanes(j)] = mm(to_slot[n], gated[n * 256:(n + 1) * 256]).astype(BF)
        picked = jnp.concatenate(
            [mm(to_token[n], eo_ref[n * slots:(n + 1) * slots, lanes(j)]) for n in range(groups)], axis=0)
        return total + jnp.sum(dy * picked, axis=1, keepdims=True)

    d_gates = lax.fori_loop(0, width // WIDE, dispatch, jnp.zeros((tokens, 1), F32))

    def back_out(start, size):
        cols = pl.ds(start, size)
        d_eh = mm_t(deo_ref[...], wd_ref[cols, :])
        dg_ref[:, cols] = (d_eh * slo_ref[:, cols].astype(F32)).astype(BF)
        du_ref[:, cols] = (d_eh * act_ref[:, cols].astype(F32)).astype(BF)

    over_columns(ff, back_out)

    @pl.when(step == 0)
    def _():
        sc.first(2)
        sc.first(3)

    def back_in(j, _):
        d_rows = (mm_t(dg_ref[...], wg_ref[lanes(j), :]) + mm_t(du_ref[...], wu_ref[lanes(j), :])).astype(BF)
        shared = mm(d_s, fan_ref[:, lanes(j)])
        taken_rows = jnp.concatenate(
            [mm(to_token[n], d_rows[n * slots:(n + 1) * slots]) for n in range(groups)], axis=0)
        dh_ref[:, lanes(j)] = (shared + taken_rows).astype(BF)
        return 0

    lax.fori_loop(0, width // WIDE, back_in, 0)
    high = d_gates.astype(BF).astype(F32)
    dh_ref[:, width:] = (high * pick_ref[:, :128] + (d_gates - high) * pick_ref[:, 128:]).astype(BF)

    outer = (sc.z == 0) | (sc.z == NZ - 1)
    for i in range(NZ - 1):
        @pl.when((step == i) & outer)
        def _():
            sc.second(i)

        @pl.when((step == min(i + 1, 2)) & jnp.logical_not(outer))
        def _():
            sc.second(i)

    @pl.when(step == NZ - 1)
    def _():
        sc.second(NZ - 1)
        sc.finish()


def whole(v):
    zeros = (0,) * v.ndim
    return pl.BlockSpec(v.shape, lambda i: zeros, pipeline_mode=pl.Buffered(buffer_count=1))


def tiles(rows, w):
    return pl.BlockSpec((rows, w), lambda i: (i, 0))


SMEM = pl.BlockSpec(memory_space=pltpu.SMEM)


def mixture_forward(dp, batches, here, lengths, pick, mix, routes, wg, wu, router, share, wda, span, down, dy, cid,
                    chunks=2):
    total, width = mix.shape
    step, half = total // 4, total // 8
    ff = wg.shape[1]
    shape = jax.ShapeDtypeStruct
    rows = total // 2
    dma = pltpu.SemaphoreType.DMA

    def early(n, w):
        return pl.BlockSpec((n, w), lambda i: (jnp.minimum(i, 3), 0))

    def late(n, w):
        return pl.BlockSpec((n, w), lambda i: (jnp.maximum(i - 4, 0), 0))

    return pl.pallas_call(
        functools.partial(forward_kernel, chunks, dp, span, batches, here),
        grid=(8,),
        out_shape=(
            shape((total, width), BF), shape((rows, width), BF), shape((rows, ff), BF), shape((rows, ff), BF),
            shape((rows, ff), BF), shape((rows, width), BF), shape((total, TILE), BF), shape((total, TILE), BF),
            shape((total, TILE), BF), shape((total, 2), F32), shape((NE,) + dy.shape, BF),
            shape((dp, span[1], width), BF)),
        in_specs=[SMEM, whole(pick), early(step, width), early(step, routes.shape[1]), whole(wg), whole(wu),
                  whole(router), ANY, ANY, ANY, ANY],
        out_specs=[late(step, width), early(half, width), early(half, ff), early(half, ff), early(half, ff),
                   late(half, width), early(step, TILE), early(step, TILE), early(step, TILE), early(step, 2), ANY, ANY],
        scratch_shapes=[
            pltpu.VMEM((ff, width), BF), pltpu.VMEM((2 * TILE, width), BF), pltpu.VMEM((TILE, width), BF),
            pltpu.VMEM((rows, ff), BF), pltpu.VMEM((total, TILE), BF), pltpu.VMEM((total, 1), F32),
            pltpu.VMEM((total, 1), F32), dma((2 * dp,)), dma((3 * dp,))] + Gather.scratch(chunks) + Spread.scratch(dp),
        compiler_params=pltpu.CompilerParams(
            collective_id=cid, has_side_effects=True, vmem_limit_bytes=60 * 1024 * 1024),
        cost_estimate=COST,
        name="mixture_forward",
    )(lengths, pick, mix, routes, wg, wu, router, share, wda, down, dy)


def mixture_backward(here, pick, dy, wg, wu, share, wda, wdb, act, slo, eo, sact, sslo, gate, part, cid, chunks=2):
    total, width = dy.shape
    step, half = total // NZ, total // NZ // 2
    ff = wg.shape[1]
    shape = jax.ShapeDtypeStruct
    rows = total // 2
    dp = wda.shape[0]
    _, own, _ = part.shape
    dma = pltpu.SemaphoreType.DMA
    return pl.pallas_call(
        functools.partial(backward_kernel, here, chunks),
        grid=(NZ,),
        out_shape=(
            shape((total, width + 128), BF), shape((rows, width), BF), shape((rows, ff), BF), shape((rows, ff), BF),
            shape((total, 2 * TILE), BF), shape((own, width), F32)),
        in_specs=[whole(pick), tiles(step, width), whole(wg), whole(wu), ANY, ANY, ANY,
                  tiles(half, ff), tiles(half, ff), tiles(half, width), tiles(step, TILE), tiles(step, TILE),
                  tiles(step, 2), ANY],
        out_specs=[tiles(step, width + 128), tiles(half, width), tiles(half, ff), tiles(half, ff),
                   tiles(step, 2 * TILE), pl.BlockSpec((own, width), lambda i: (0, 0))],
        scratch_shapes=[
            pltpu.VMEM((ff, width), BF), pltpu.VMEM((2 * TILE, width), BF), pltpu.VMEM((TILE, width), BF),
            dma((2 * dp,)), dma((3 * dp,))] + Scatter.scratch(own, width, chunks, BF),
        compiler_params=pltpu.CompilerParams(
            collective_id=cid, has_side_effects=True, vmem_limit_bytes=62 * 1024 * 1024),
        cost_estimate=COST,
        name="mixture_backward",
    )(pick, dy, wg, wu, share, wda, wdb, act, slo, eo, sact, sslo, gate, part)


class ShareWork:
    ROWS = 256

    def __init__(self, ds_ref, sh_ref, mix_ref, dy_ref, out_ref, scratch):
        self.sources = (ds_ref, sh_ref, mix_ref, dy_ref)
        self.out = out_ref
        *self.buffers, self.gfan, self.gsd, self.sem = scratch
        self.steps = mix_ref.shape[0] // self.ROWS
        self.done = 0

    @staticmethod
    def scratch(width):
        r = ShareWork.ROWS
        return [pltpu.VMEM((2, r, w), BF) for w in (2 * TILE, TILE, width, width)] + [
            pltpu.VMEM((2 * TILE, width), F32), pltpu.VMEM((TILE, width), F32), pltpu.SemaphoreType.DMA((2, 4))]

    COUNT = 7

    def copies(self, n):
        return [pltpu.make_async_copy(src.at[pl.ds(n * self.ROWS, self.ROWS)], buf.at[n % 2], self.sem.at[n % 2, i])
                for i, (src, buf) in enumerate(zip(self.sources, self.buffers))]

    def start(self):
        for copy in self.copies(0):
            copy.start()
        self.gfan[...] = jnp.zeros_like(self.gfan)
        self.gsd[...] = jnp.zeros_like(self.gsd)

    def step(self):
        n = self.done
        if n == self.steps:
            return
        self.done += 1
        for copy in self.copies(n):
            copy.wait()
        if n + 1 < self.steps:
            for copy in self.copies(n + 1):
                copy.start()
        ds, sh, mix, dy = self.buffers

        def columns(j, _):
            self.gfan[:, lanes(j)] += mm_lead(ds[n % 2], mix[n % 2, :, lanes(j)])
            self.gsd[:, lanes(j)] += mm_lead(sh[n % 2], dy[n % 2, :, lanes(j)])
            return 0

        lax.fori_loop(0, mix.shape[2] // WIDE, columns, 0)

    def finish(self):
        while self.done < self.steps:
            self.step()
        dp, rows, w = self.out.shape
        n = rows // 3
        for d in range(dp):
            cols = slice(d * w, (d + 1) * w)
            self.out[d, :n] = self.gfan[:n, cols].astype(BF)
            self.out[d, n:2 * n] = self.gfan[TILE:TILE + n, cols].astype(BF)
            self.out[d, 2 * n:] = self.gsd[:n, cols].astype(BF)


def scatter_share_kernel(chunks, p_ref, ds_ref, sh_ref, mix_ref, dy_ref, o_ref, g_ref, *scratch):
    s = Scatter(p_ref, o_ref, chunks, scratch[:Scatter.COUNT])
    work = ShareWork(ds_ref, sh_ref, mix_ref, dy_ref, g_ref, scratch[Scatter.COUNT:])
    enter(s.me, s.z, s.core, s.side)
    s.start()
    work.start()
    s.run(work.step)
    work.finish()
    s.finish()


def scatter_share(p, ds, sh, mix, dy, share_shape, cid, chunks=2):
    _, rows, width = p.shape
    return pl.pallas_call(
        functools.partial(scatter_share_kernel, chunks),
        out_shape=(jax.ShapeDtypeStruct((rows, width), F32), jax.ShapeDtypeStruct(share_shape, BF)),
        in_specs=[ANY] * 5,
        out_specs=(VMEM, VMEM),
        scratch_shapes=Scatter.scratch(rows, width, chunks, p.dtype) + ShareWork.scratch(mix.shape[1]),
        compiler_params=pltpu.CompilerParams(
            collective_id=cid, has_side_effects=True, vmem_limit_bytes=60 * 1024 * 1024),
        cost_estimate=COST,
        name="scatter_share",
    )(p, ds, sh, mix, dy)


def turn(v, cosine, sine):
    half = v.shape[1] // 2
    a, b = v[:, :half], v[:, half:]
    return jnp.concatenate([a * cosine - b * sine, b * cosine + a * sine], axis=1)


def project_kernel(x_ref, gain_ref, lgain_ref, wq_ref, wl_ref, we_ref, cos_ref, sin_ref,
                   h_ref, q_ref, k_ref, v_ref, lat_ref):
    blocks = x_ref.shape[0]
    batches, rows, _ = q_ref.shape
    here = rows // blocks
    x = x_ref[...].reshape(blocks * batches * here, x_ref.shape[2]).astype(F32)
    h = x * lax.rsqrt(jnp.mean(x * x, axis=1, keepdims=True) + 1e-6) * gain_ref[...]
    h = h.astype(BF)
    h_ref[...] = h
    raw = mm(h, wq_ref[...])
    raw_lat = mm(h, wl_ref[...])
    cosine, sine = cos_ref[...], sin_ref[...]
    zeros = jnp.zeros((raw.shape[0], 64), BF)
    q = jnp.concatenate([raw[:, :128].astype(BF), turn(raw[:, 128:192], cosine, sine).astype(BF), zeros], axis=1)
    k_rope = turn(raw_lat[:, 512:576], cosine, sine).astype(BF)
    lat = raw_lat[:, :512]
    lat = (lat * lax.rsqrt(jnp.mean(lat * lat, axis=1, keepdims=True) + 1e-6) * lgain_ref[...]).astype(BF)
    expanded = mm(lat, we_ref[...]).astype(BF)
    k = jnp.concatenate([expanded[:, :128], k_rope, zeros], axis=1)
    for e in range(blocks):
        for m in range(batches):
            src = slice((e * batches + m) * here, (e * batches + m + 1) * here)
            dst = slice(e * here, (e + 1) * here)
            q_ref[m, dst] = q[src]
            k_ref[m, dst] = k[src]
            v_ref[m, dst] = expanded[src, 128:]
            lat_ref[m, dst] = lat[src]


def project(x_all, gain, lgain, wq, wl, we, cosine, sine, batches):
    groups, rows, width = x_all.shape
    here = rows // batches
    per = 4
    seq = groups * here
    shape = jax.ShapeDtypeStruct

    def whole(v):
        return pl.BlockSpec(v.shape, lambda i: (0, 0))

    def by_seq(w):
        return pl.BlockSpec((batches, per * here, w), lambda i: (0, i, 0))

    table = pl.BlockSpec((per * rows, 32), lambda i: (i, 0))
    return pl.pallas_call(
        project_kernel,
        grid=(groups // per,),
        out_shape=(shape((groups * rows, width), BF), shape((batches, seq, 256), BF), shape((batches, seq, 256), BF),
                   shape((batches, seq, 128), BF), shape((batches, seq, 512), BF)),
        in_specs=[pl.BlockSpec((per, rows, width), lambda i: (i, 0, 0)), whole(gain), whole(lgain), whole(wq), whole(wl), whole(we),
                  table, table],
        out_specs=[pl.BlockSpec((per * rows, width), lambda i: (i, 0)), by_seq(256), by_seq(256), by_seq(128), by_seq(512)],
        compiler_params=pltpu.CompilerParams(vmem_limit_bytes=48 * 1024 * 1024),
        cost_estimate=pl.CostEstimate(flops=7_000_000_000, bytes_accessed=20_000_000, transcendentals=0),
        name="project",
    )(x_all, gain, lgain, wq, wl, we, cosine, sine)


ROWS = 256
SCALE = 192.0 ** -0.5


def held_scores(q, k, first, length):
    s = mm_t(q, k) * SCALE
    t = lax.broadcasted_iota(jnp.int32, s.shape, 0) + first
    u = lax.broadcasted_iota(jnp.int32, s.shape, 1)
    return jnp.where((u <= t) & (u < length), s, -1e30)


def attend_kernel(len_ref, q_ref, k_ref, v_ref, wo_ref, part_ref, att_ref, lse_ref):
    length = len_ref[pl.program_id(0)]
    seq = q_ref.shape[1]
    groups, _, here, width = part_ref.shape
    for i in range(seq // ROWS):
        tile = slice(i * ROWS, (i + 1) * ROWS)
        ext = (i + 1) * ROWS
        s = held_scores(q_ref[0, tile], k_ref[0, :ext], i * ROWS, length)
        peak = jnp.max(s, axis=1, keepdims=True)
        raised = jnp.exp(s - peak)
        total = jnp.sum(raised, axis=1, keepdims=True)
        lse_ref[0, tile] = peak + jnp.log(total)
        p = (raised / total).astype(BF)
        att = mm(p, v_ref[0, :ext]).astype(BF)
        per = ROWS // here
        att_ref[i * per:(i + 1) * per, 0] = att.reshape(per, here, att.shape[1])
        for j in range(width // 512):
            cols = slice(j * 512, (j + 1) * 512)
            part_ref[i * per:(i + 1) * per, 0, :, cols] = mm(att, wo_ref[:, cols]).astype(BF).reshape(per, here, 512)


def attend(lengths, q, k, v, wo, groups):
    batches, seq, _ = q.shape
    here = seq // groups
    width = wo.shape[1]
    shape = jax.ShapeDtypeStruct

    def by_seq(w):
        return pl.BlockSpec((1, seq, w), lambda m: (m, 0, 0))

    def by_dev(w):
        return pl.BlockSpec((groups, 1, here, w), lambda m: (0, m, 0, 0))

    return pl.pallas_call(
        attend_kernel,
        grid=(batches,),
        out_shape=(shape((groups, batches, here, width), BF), shape((groups, batches, here, 128), BF),
                   shape((batches, seq, 1), F32)),
        in_specs=[pl.BlockSpec(memory_space=pltpu.SMEM), by_seq(256), by_seq(256), by_seq(128),
                  pl.BlockSpec(wo.shape, lambda m: (0, 0))],
        out_specs=[by_dev(width), by_dev(128), by_seq(1)],
        compiler_params=pltpu.CompilerParams(vmem_limit_bytes=48 * 1024 * 1024),
        cost_estimate=pl.CostEstimate(flops=4_000_000_000, bytes_accessed=15_000_000, transcendentals=2_000_000),
        name="attend",
    )(lengths, q, k, v, wo)


def attend_back_kernel(len_ref, dout_ref, q_ref, k_ref, v_ref, lat_ref, att_ref, lse_ref, wo_ref, wq_ref, we_ref,
                       cos_ref, sin_ref, part_ref, dq_ref, gwo_ref, gwe_ref, dk, dv, datt):
    m = pl.program_id(0)
    length = len_ref[m]
    seq = q_ref.shape[1]
    groups, _, here, width = dout_ref.shape
    per = ROWS // here

    @pl.when(m == 0)
    def _():
        gwo_ref[...] = jnp.zeros_like(gwo_ref)
        gwe_ref[...] = jnp.zeros_like(gwe_ref)

    for j in range(4):
        blocks = slice(j * groups // 4, (j + 1) * groups // 4)
        dout = dout_ref[blocks].reshape(seq // 4, width)
        rows = slice(j * seq // 4, (j + 1) * seq // 4)
        datt[rows] = mm_t(dout, wo_ref[...]).astype(BF)
        gwo_ref[...] += mm_lead(att_ref[blocks].reshape(seq // 4, 128), dout)
    dk[...] = jnp.zeros_like(dk)
    dv[...] = jnp.zeros_like(dv)
    for i in range(seq // ROWS):
        tile = slice(i * ROWS, (i + 1) * ROWS)
        ext = (i + 1) * ROWS
        q = q_ref[0, tile]
        p = jnp.exp(held_scores(q, k_ref[0, :ext], i * ROWS, length) - lse_ref[0, tile])
        da = datt[tile]
        dp = mm_t(da, v_ref[0, :ext])
        inner = jnp.sum(dp * p, axis=1, keepdims=True)
        ds = (p * (dp - inner)).astype(BF)
        dq = mm(ds, k_ref[0, :ext]) * SCALE
        dk[:ext] += mm_lead(ds, q)
        dv[:ext] += mm_lead(p.astype(BF), da)
        rope = turn(dq[:, 128:192], cos_ref[tile], -sin_ref[tile])
        dq = jnp.concatenate([dq[:, :128].astype(BF), rope.astype(BF), jnp.zeros((ROWS, 64), BF)], axis=1)
        dq_ref[i * per:(i + 1) * per, 0] = dq.reshape(per, here, 256)
        for j in range(width // 512):
            cols = slice(j * 512, (j + 1) * 512)
            part_ref[i * per:(i + 1) * per, 0, :, cols] = mm_t(dq, wq_ref[cols]).astype(BF).reshape(per, here, 512)
    for i in range(seq // ROWS):
        tile = slice(i * ROWS, (i + 1) * ROWS)
        d_k = dk[tile] * SCALE
        d_exp = jnp.concatenate([d_k[:, :128].astype(BF), dv[tile].astype(BF)], axis=1)
        gwe_ref[...] += mm_lead(lat_ref[0, tile], d_exp)
        d_lat = mm_t(d_exp, we_ref[...]).astype(BF)
        tail = jnp.concatenate([d_lat, d_k[:, 128:].astype(BF)], axis=1)
        pad = part_ref.shape[3] - width - tail.shape[1]
        if pad > 0:
            tail = jnp.concatenate([tail, jnp.zeros((ROWS, pad), BF)], axis=1)
        part_ref[i * per:(i + 1) * per, 0, :, width:] = tail[:, :part_ref.shape[3] - width].reshape(per, here, -1)


def attend_back(lengths, dout, q, k, v, lat, att, lse, wo, wq, we, cosine, sine, tail):
    groups, batches, here, width = dout.shape
    seq = groups * here
    shape = jax.ShapeDtypeStruct

    def by_seq(w):
        return pl.BlockSpec((1, seq, w), lambda m: (m, 0, 0))

    def by_dev(w):
        return pl.BlockSpec((groups, 1, here, w), lambda m: (0, m, 0, 0))

    def whole(v):
        return pl.BlockSpec(v.shape, lambda m: (0, 0))

    return pl.pallas_call(
        attend_back_kernel,
        grid=(batches,),
        out_shape=(shape((groups, batches, here, width + tail), BF), shape((groups, batches, here, 256), BF),
                   shape(wo.shape, F32), shape(we.shape, F32)),
        in_specs=[pl.BlockSpec(memory_space=pltpu.SMEM), by_dev(width), by_seq(256), by_seq(256), by_seq(128),
                  by_seq(512), by_dev(128), by_seq(1), whole(wo), whole(wq), whole(we), whole(cosine), whole(sine)],
        out_specs=[by_dev(width + tail), by_dev(256), whole(wo), whole(we)],
        scratch_shapes=[pltpu.VMEM((seq, 256), F32), pltpu.VMEM((seq, 128), F32), pltpu.VMEM((seq, 128), BF)],
        compiler_params=pltpu.CompilerParams(vmem_limit_bytes=56 * 1024 * 1024),
        cost_estimate=pl.CostEstimate(flops=14_000_000_000, bytes_accessed=25_000_000, transcendentals=2_000_000),
        name="attend_back",
    )(lengths, dout, q, k, v, lat, att, lse, wo, wq, we, cosine, sine)


H = 16
QK_NOPE = 128
ROPE = 64
V_DIM = 128
KV_RANK = 512
GROUPS = 16
EPSILON = 1e-06
ROTARY_BASE = 10000.0


def product(left_side, right_side):
    return jnp.dot(left_side, right_side, preferred_element_type=F32)


def product_lead(left_side, right_side):
    return lax.dot_general(
        left_side, right_side, (((0,), (0,)), ((), ())), preferred_element_type=F32
    )


def product_trail(left_side, right_side):
    return lax.dot_general(
        left_side, right_side, (((1,), (1,)), ((), ())), preferred_element_type=F32
    )


def rotary_tables(count):
    frequency = ROTARY_BASE ** (-np.arange(ROPE // 2, dtype=np.float32) * np.float32(2.0) / np.float32(ROPE))
    angles = np.arange(count, dtype=np.float32)[:, None] * frequency.astype(np.float32)[None, :]
    return np.cos(angles).astype(np.float32), np.sin(angles).astype(np.float32)


def rotate(values, cosine, sine_table):
    first_half, second_half = jnp.split(values, 2, axis=-1)
    return jnp.concatenate(
        [
            first_half * cosine - second_half * sine_table,
            second_half * cosine + first_half * sine_table,
        ],
        axis=-1,
    )


def norm_forward(values, gains):
    factor = lax.rsqrt(jnp.mean(values * values, axis=-1, keepdims=True) + EPSILON)
    normed = values * factor
    return (normed * gains, normed, factor)


def norm_backward(gradient, normed, factor, gains):
    gain_grad = jnp.sum(gradient * normed, axis=0)
    scaled = gradient * gains
    return (
        factor * (scaled - normed * jnp.mean(scaled * normed, axis=-1, keepdims=True)),
        gain_grad,
    )


def selected_experts(routes):
    chosen = routes[:, :, None] == jnp.arange(GROUPS, dtype=routes.dtype)
    return jnp.any(chosen, axis=1)


def masked_softmax(logits, mask):
    held = jnp.where(mask, logits, -1e30)
    peak = jnp.max(held, axis=-1, keepdims=True)
    raised = jnp.where(mask, jnp.exp(held - peak), 0.0)
    return raised / jnp.sum(raised, axis=-1, keepdims=True)


def per_device(
    layer_input,
    out_cotangent,
    lengths,
    routes,
    attn_gain,
    query_weight,
    latent_weight,
    latent_gain,
    expand_weight,
    output_weight,
    mixer_gain,
    router_weight,
    gate_weight,
    up_weight,
    down_weight,
    shared_gate,
    shared_up,
    shared_down,
):
    dp = lax.axis_size("dp")
    me = lax.axis_index("expert")
    plane = lax.axis_index("dp")
    batches, _, here, width = layer_input.shape
    own = batches * here
    total = own * GROUPS
    seq_total = here * GROUPS
    rows_w = query_weight.shape[0]
    rows_l = expand_weight.shape[0]

    x_own = layer_input.reshape(own, width)
    routes_own = routes.reshape(own, -1)
    choices = routes_own.shape[1]
    route_columns = routes_own.astype(BF).reshape(rows_w, -1)
    small_width = -(-(595 + route_columns.shape[1]) // 128) * 128
    latent_column = jnp.zeros((rows_w,), BF).at[:rows_l].set(latent_gain)
    small = jnp.concatenate(
        [
            latent_weight,
            router_weight,
            attn_gain[:, None],
            mixer_gain[:, None],
            latent_column[:, None],
            route_columns,
            jnp.zeros((rows_w, small_width - 595 - route_columns.shape[1]), BF),
        ],
        axis=1,
    )
    query_parts = query_weight.reshape(rows_w, H, QK_NOPE + ROPE).transpose(1, 0, 2)
    expand_parts = expand_weight.reshape(rows_l, H, QK_NOPE + V_DIM).transpose(1, 0, 2)
    parts = jnp.concatenate([query_parts, expand_parts.reshape(H, rows_w, ROPE)], axis=2)
    x_all, small, parts_head, output_head = opening(dp, x_own, small, parts, output_weight, 1)
    x_all = x_all.reshape(total, width)
    routes_all = lax.dynamic_index_in_dim(small, plane, 0, False)[..., 595 : 595 + route_columns.shape[1]]
    routes_all = routes_all.reshape(total, choices).astype(jnp.int32)
    small = small.reshape(width, small_width)
    parts_head = parts_head.reshape(width, TILE)
    latent_full = small[:, :576]
    router_full = small[:, 576:592]
    gain_attn = small[:, 592].astype(F32)
    gain_mixer = small[:, 593].astype(F32)
    gain_latent = small[:, 594].reshape(dp * GROUPS, rows_w)[:, :rows_l].reshape(-1).astype(F32)
    expand_head = parts_head[:, QK_NOPE + ROPE :].reshape(KV_RANK, QK_NOPE + V_DIM)
    output_head = output_head.reshape(V_DIM, width)

    ff = gate_weight.shape[2]
    share_own = jnp.concatenate([shared_gate.T, shared_up.T, shared_down], axis=0)
    share_width = shared_down.shape[0]
    gate_full = lax.all_gather(gate_weight[0], "dp", axis=0, tiled=True)
    up_full = lax.all_gather(up_weight[0], "dp", axis=0, tiled=True)
    share_full = lax.all_gather(share_own, "dp", axis=0)
    seq_lengths = lengths.reshape(batches)
    own_positions = me * here + jnp.arange(here, dtype=jnp.int32)
    valid_own = (own_positions[None, :] < seq_lengths[:, None]).reshape(own).astype(F32)
    cosine, sine_table = rotary_tables(seq_total)
    cosine_own = lax.dynamic_slice_in_dim(jnp.asarray(cosine), me * here, here)
    sine_own = lax.dynamic_slice_in_dim(jnp.asarray(sine_table), me * here, here)

    grad_own = out_cotangent.reshape(own, width) * valid_own[:, None].astype(BF)

    def by_token(table):
        return jnp.asarray(np.broadcast_to(
            table.reshape(GROUPS, 1, here, -1), (GROUPS, batches, here, table.shape[1])).reshape(total, -1))

    hidden_all, query, key, values, latent = project(
        x_all.reshape(GROUPS, own, width), gain_attn[None], gain_latent[None], parts_head, small, expand_head,
        by_token(cosine), by_token(sine_table), batches)
    attn_part, attended, log_total = attend(seq_lengths, query, key, values, output_head, GROUPS)
    attn_part = attn_part.reshape(GROUPS, own, width)
    down_own = down_weight[0]
    cut = down_own.shape[0] * 9 // 320 * 16
    spans = ((0, cut), (cut, down_own.shape[0] - cut))
    attn_out = scatter16(attn_part, 2)

    x_wide = x_own.astype(F32)
    middle = x_wide + attn_out
    normed_mix, unit_mix, factor_mix = norm_forward(middle, gain_mixer)
    hidden_mix = normed_mix.astype(BF)
    mix_all, down_a = gather16(hidden_mix, 3, dp=dp, span=spans[0], side=down_own)
    mix_all = mix_all.reshape(total, width)

    lane = jnp.arange(128)[None, :]
    pick = jnp.concatenate([lane == me, lane == me + GROUPS], axis=1).astype(F32)
    (out_part, rows, hidden, act, slope, result, share_hidden, share_act, share_slope, gates, grad_all,
     down_b) = mixture_forward(
        dp, batches, here, seq_lengths, pick, mix_all, routes_all, gate_full, up_full, router_full.T, share_full,
        down_a, spans[1], down_own, grad_own, 4)
    grad_all = grad_all.reshape(total, width)
    mix_part, grad_result, grad_gate_in, grad_up_in, grad_share_in, mixed = mixture_backward(
        here, pick, grad_all, gate_full, up_full, share_full, down_a, down_b, act, slope, result,
        share_act, share_slope, gates, out_part.reshape(GROUPS, own, width), 8)
    grad_down = product_lead(hidden, grad_result).astype(BF)
    grad_gate = product_lead(rows, grad_gate_in).astype(BF)
    grad_up = product_lead(rows, grad_up_in).astype(BF)
    mix_part, grad_down, grad_gate, grad_up = lax.optimization_barrier((mix_part, grad_down, grad_gate, grad_up))
    mix_sum, grad_share = scatter_share(
        mix_part.reshape(GROUPS, own, width + 128), grad_share_in, share_hidden, mix_all, grad_all, share_full.shape, 5)
    layer_output = valid_own[:, None] * (middle + mixed)

    out_down = lax.psum_scatter(grad_down, "dp", scatter_dimension=0, tiled=True)
    out_gate = lax.psum_scatter(grad_gate, "dp", scatter_dimension=0, tiled=True)
    out_up = lax.psum_scatter(grad_up, "dp", scatter_dimension=0, tiled=True)
    out_share = lax.psum_scatter(grad_share, "dp", scatter_dimension=0, tiled=False).astype(F32)

    mask_own = selected_experts(routes_own)
    soft_own = masked_softmax(product(hidden_mix, router_full), mask_own)
    grad_masked = (mix_sum[:, width : width + GROUPS] + mix_sum[:, width + GROUPS : width + 2 * GROUPS])
    grad_masked = grad_masked * valid_own[:, None]
    grad_logits = soft_own * (grad_masked - jnp.sum(grad_masked * soft_own, axis=1, keepdims=True))
    grad_logits = grad_logits.astype(BF)
    grad_mix = mix_sum[:, :width] + product_trail(grad_logits, router_full)
    grad_middle_norm, grad_gain_mixer = norm_backward(grad_mix, unit_mix, factor_mix, gain_mixer)
    grad_middle = grad_own.astype(F32) + grad_middle_norm

    grad_attn_all = gather16(grad_middle.astype(BF), 6).reshape(GROUPS, batches, here, width)
    back_part, grad_query, grad_output, grad_expand = attend_back(
        seq_lengths, grad_attn_all, query, key, values, latent, attended, log_total, output_head, parts_head,
        expand_head, jnp.asarray(cosine), jnp.asarray(sine_table), 640)
    grad_query_w = product_lead(hidden_all, grad_query.reshape(total, TILE)).astype(BF)
    parts_grad = jnp.concatenate(
        [grad_query_w[:, : QK_NOPE + ROPE], grad_expand.astype(BF).reshape(width, ROPE)], axis=1)
    back_sum, out_parts, out_output = returning(
        dp, back_part.reshape(GROUPS, own, back_part.shape[3]),
        parts_grad.reshape(dp, GROUPS, rows_w, TILE), grad_output.astype(BF).reshape(dp, rows_w, width), 7)
    out_query = out_parts[..., : QK_NOPE + ROPE].transpose(1, 0, 2).reshape(rows_w, -1)
    out_expand = out_parts[..., QK_NOPE + ROPE :].reshape(H, rows_l, QK_NOPE + V_DIM)
    out_expand = out_expand.transpose(1, 0, 2).reshape(rows_l, -1)

    x_normed, unit_attn, factor_attn = norm_forward(x_wide, gain_attn)
    hidden_own = x_normed.astype(BF)
    latent_own = product(hidden_own, latent_full)
    _, unit_latent, factor_latent = norm_forward(latent_own[:, :KV_RANK], gain_latent)
    grad_latent_in, grad_gain_latent = norm_backward(
        back_sum[:, width : width + KV_RANK], unit_latent, factor_latent, gain_latent
    )
    grad_rope = back_sum[:, width + KV_RANK : width + KV_RANK + ROPE].reshape(batches, here, ROPE)
    grad_rope = rotate(grad_rope, cosine_own, -sine_own).reshape(own, ROPE)
    grad_latent_raw = jnp.concatenate([grad_latent_in, grad_rope], axis=1).astype(BF)
    grad_hidden_attn = back_sum[:, :width] + product_trail(grad_latent_raw, latent_full)
    grad_input_norm, grad_gain_attn = norm_backward(grad_hidden_attn, unit_attn, factor_attn, gain_attn)
    grad_input = grad_middle + grad_input_norm

    latent_rows = grad_gain_latent.reshape(dp * GROUPS, rows_l)
    latent_rows = jnp.pad(latent_rows, ((0, 0), (0, rows_w - rows_l))).reshape(width, 1)
    tokens_side = jnp.concatenate([hidden_own, hidden_mix], axis=0)
    grads_side = jnp.concatenate(
        [jnp.pad(grad_latent_raw, ((0, 0), (0, 64))), jnp.pad(grad_logits, ((0, 0), (576, 640 - 592)))], axis=0)
    lane = jnp.arange(640)[None, :]
    small_grad = product_lead(tokens_side, grads_side)
    small_grad = small_grad + jnp.where(lane == 592, grad_gain_attn[:, None], 0.0)
    small_grad = small_grad + jnp.where(lane == 593, grad_gain_mixer[:, None], 0.0)
    small_grad = (small_grad + jnp.where(lane == 594, latent_rows, 0.0)).astype(BF)
    small_grad = small_grad.reshape(dp, GROUPS, rows_w, 640).swapaxes(0, 1).reshape(GROUPS, dp * rows_w, 640)
    small_sum = closing(dp, small_grad, 9)

    def as_input(v):
        return v.reshape(batches, 1, here, width)

    return (
        as_input(layer_output),
        as_input(grad_input),
        small_sum[:, 592],
        out_query,
        small_sum[:, :576],
        small_sum[:rows_l, 594],
        out_expand,
        out_output,
        small_sum[:, 593],
        small_sum[:, 576:592],
        out_gate.astype(F32)[None],
        out_up.astype(F32)[None],
        out_down.astype(F32)[None],
        out_share[:share_width].T,
        out_share[share_width : 2 * share_width].T,
        out_share[2 * share_width :],
    )


def solution(mesh):
    split = P(("dp", "expert"), None)
    line = P(("dp", "expert"))
    tokens = P(None, "dp", "expert", None)
    expert = P("expert", "dp", None)
    return jax.shard_map(
        per_device,
        mesh=mesh,
        in_specs=(
            tokens, tokens, P(None, "dp"), tokens, line, split, split, line, split, split, line, split,
            expert, expert, expert, P("dp", "expert"), P("dp", "expert"), P("expert", "dp"),
        ),
        out_specs=(
            tokens, tokens, line, split, split, line, split, split, line, split,
            expert, expert, expert, P("dp", "expert"), P("dp", "expert"), P("expert", "dp"),
        ),
        check_vma=False,
    )
```

```python
import functools
import jax
import jax.numpy as jnp
import numpy as np
from jax import lax
from jax.experimental import pallas as pl
from jax.experimental.pallas import tpu as pltpu
from jax.sharding import PartitionSpec as P

MESH = pl.DeviceIdType.MESH
NZ = 4
NE = 16


def place():
    me = lax.axis_index("expert")
    z = me // 4
    x = (me // 2) % 2
    c = me % 2
    return me, z, x, c, me + 1 - 2 * c, me + 2 - 4 * x


def enter(me, z, core, side, dp=1):
    barrier = pltpu.get_barrier_semaphore()
    plane = lax.axis_index("dp")
    for r in range(1, dp):
        pl.semaphore_signal(barrier, inc=1, device_id={"dp": (plane + r) % dp}, device_id_type=MESH)
    for other in (core, side):
        pl.semaphore_signal(barrier, inc=1, device_id={"expert": other}, device_id_type=MESH)

    @pl.when(z < NZ - 1)
    def _():
        pl.semaphore_signal(barrier, inc=1, device_id={"expert": me + 4}, device_id_type=MESH)

    @pl.when(z > 0)
    def _():
        pl.semaphore_signal(barrier, inc=1, device_id={"expert": me - 4}, device_id_type=MESH)

    pl.semaphore_wait(barrier, dp + 1 + (z < NZ - 1).astype(jnp.int32) + (z > 0).astype(jnp.int32))


class Spread:
    def __init__(self, dp, src, out, sems):
        self.dp, self.src, self.out = dp, src, out
        self.own, self.send, self.recv = sems
        self.plane = lax.axis_index("dp")

    @staticmethod
    def scratch(dp):
        dma = pltpu.SemaphoreType.DMA
        return [dma, dma((dp,)), dma((dp,))]

    def copy(self, r):
        return pltpu.make_async_remote_copy(
            src_ref=self.src, dst_ref=self.out.at[self.plane], send_sem=self.send.at[r], recv_sem=self.recv.at[r],
            device_id={"dp": (self.plane + r) % self.dp}, device_id_type=MESH)

    def arrival(self, r):
        p = (self.plane - r + self.dp) % self.dp
        return pltpu.make_async_remote_copy(
            src_ref=self.src, dst_ref=self.out.at[p], send_sem=self.send.at[r], recv_sem=self.recv.at[r],
            device_id={"dp": p}, device_id_type=MESH)

    def start(self):
        for r in range(1, self.dp):
            self.copy(r).start()
        self.kept = pltpu.make_async_copy(self.src, self.out.at[self.plane], self.own)
        self.kept.start()

    def finish(self):
        self.kept.wait()
        for r in range(1, self.dp):
            self.arrival(r).wait_recv()
            self.copy(r).wait_send()


def side_job(dp, span, src, out, sems):
    return Spread(dp, src.at[pl.ds(span[0], span[1])], out, sems)


def enter_all(me, plane, dp):
    barrier = pltpu.get_barrier_semaphore()
    for r in range(1, NE):
        pl.semaphore_signal(
            barrier, inc=1, device_id={"expert": (me + r) % NE}, device_id_type=MESH)
    for r in range(1, dp):
        pl.semaphore_signal(
            barrier, inc=1, device_id={"dp": (plane + r) % dp}, device_id_type=MESH)
    pl.semaphore_wait(barrier, NE - 1 + dp - 1)


class Gather:
    def __init__(self, src, out, chunks, sems, view=lambda ref, b: ref.at[b]):
        self.src, self.out, self.chunks, self.view = src, out, chunks, view
        self.rows = src.shape[0] // chunks
        (self.own_sem, self.us, self.ur, self.ds, self.dr, self.bus, self.bur, self.bds, self.bdr,
         self.xs, self.xr, self.cs, self.cr) = sems
        self.me, self.z, self.x, self.c, self.core, self.side = place()

    COUNT = 13

    @staticmethod
    def scratch(chunks):
        dma = pltpu.SemaphoreType.DMA
        return [dma] + [dma((4, chunks))] * 8 + [dma((7, chunks))] * 2 + [dma((14, chunks))] * 2

    def alt(self, k):
        return k >= (self.chunks + 1) // 2

    def order(self):
        return range(self.chunks - 1, -1, -1)

    def copy(self, block, k, src, send, recv, to):
        src_ref = self.src if src is None else self.view(self.out, src)
        dst_ref = self.view(self.out, block)
        if self.chunks > 1:
            part = pl.ds(k * self.rows, self.rows)
            src_ref, dst_ref = src_ref.at[part], dst_ref.at[part]
        return pltpu.make_async_remote_copy(
            src_ref=src_ref,
            dst_ref=dst_ref,
            send_sem=send, recv_sem=recv,
            device_id={"expert": to}, device_id_type=MESH,
        )

    def up(self, k, s, src=None):
        return self.copy(self.me - 4 * s, k, src, self.us.at[s, k], self.ur.at[s, k], self.me + 4)

    def down(self, k, s, src=None):
        return self.copy(self.me + 4 * s, k, src, self.ds.at[s, k], self.dr.at[s, k], self.me - 4)

    def up_b(self, k, s):
        b = self.side - 4 * s
        return self.copy(b, k, b, self.bus.at[s, k], self.bur.at[s, k], self.me + 4)

    def down_b(self, k, s):
        b = self.side + 4 * s
        return self.copy(b, k, b, self.bds.at[s, k], self.bdr.at[s, k], self.me - 4)

    def across(self, k, slot, block, src=None):
        return self.copy(block, k, src, self.xs.at[slot, k], self.xr.at[slot, k], self.side)

    def over(self, k, slot, block, src=None):
        return self.copy(block, k, src, self.cs.at[slot, k], self.cr.at[slot, k], self.core)

    def arrived(self, b, k, sems, s):
        return self.copy(b, k, b, sems[0].at[s - 1, k], sems[1].at[s - 1, k], self.side)

    def shift(self, base, slot):
        return base - 4 * slot if slot <= 3 else base + 4 * (slot - 3)

    def core_block(self, slot):
        if slot < 7:
            return self.shift(self.core, slot)
        return self.shift(self.core + 2 - 4 * self.x, slot - 7)

    def has(self, slot):
        slot = slot % 7
        if slot == 0:
            return self.z >= 0
        return self.z >= slot if slot <= 3 else self.z + (slot - 3) <= NZ - 1

    def crosses(self, k, slot):
        if slot == 0 or not self.alt(k):
            return self.has(slot)
        return self.z > slot if slot <= 3 else self.z + (slot - 3) < NZ - 1

    def start(self):
        z, me = self.z, self.me
        self.own = pltpu.make_async_copy(self.src, self.view(self.out, me), self.own_sem)
        self.own.start()
        for k in self.order():
            self.across(k, 0, me).start()

            @pl.when(z < NZ - 1)
            def _():
                self.up(k, 0).start()

            @pl.when(z > 0)
            def _():
                self.down(k, 0).start()

            self.over(k, 0, me).start()

    def line(self, k, s):
        z, me = self.z, self.me

        @pl.when(z >= s)
        def _():
            b = me - 4 * s
            self.arrived(b, k, (self.us, self.ur), s).wait_recv()

            @pl.when(self.crosses(k, s))
            def _():
                self.across(k, s, b, b).start()

            @pl.when(z < NZ - 1)
            def _():
                self.up(k, s, b).start()

            self.over(k, s, b, b).start()

        @pl.when(z + s <= NZ - 1)
        def _():
            b = me + 4 * s
            self.arrived(b, k, (self.ds, self.dr), s).wait_recv()

            @pl.when(self.crosses(k, 3 + s))
            def _():
                self.across(k, 3 + s, b, b).start()

            @pl.when(z > 0)
            def _():
                self.down(k, s, b).start()

            self.over(k, 3 + s, b, b).start()

    def line_b(self, k, s):
        z = self.z

        @pl.when(z == s)
        def _():
            b = self.side - 4 * s
            self.arrived(b, k, (self.bus, self.bur), s).wait_recv()

            @pl.when(z < NZ - 1)
            def _():
                self.up_b(k, s).start()

            self.over(k, 7 + s, b, b).start()

        @pl.when(z + s == NZ - 1)
        def _():
            b = self.side + 4 * s
            self.arrived(b, k, (self.bds, self.bdr), s).wait_recv()

            @pl.when(z > 0)
            def _():
                self.down_b(k, s).start()

            self.over(k, 10 + s, b, b).start()

    def from_side(self, k, slot):
        @pl.when(self.crosses(k, slot))
        def _():
            b = self.shift(self.side, slot)
            self.across(k, slot, b, b).wait_recv()
            if slot == 0 and self.alt(k):
                @pl.when(self.z == 0)
                def _():
                    self.up_b(k, 0).start()

                @pl.when(self.z == NZ - 1)
                def _():
                    self.down_b(k, 0).start()

            self.over(k, 7 + slot, b, b).start()

    def round(self, s):
        if s < NZ:
            for k in self.order():
                self.line(k, s)
        for k in self.order():
            for slot in ((0,) if s == 1 else (s - 1, s + 2)):
                self.from_side(k, slot)
        if s > 1:
            for k in self.order():
                if self.alt(k):
                    self.line_b(k, s - 1)

    def finish(self):
        z = self.z
        self.own.wait()
        for k in self.order():
            for slot in range(14):
                @pl.when(self.has(slot))
                def _():
                    b = self.core_block(slot)
                    self.over(k, slot, b, b).wait_recv()
                    self.over(k, slot, b, b).wait_send()
            for slot in range(7):
                @pl.when(self.crosses(k, slot))
                def _():
                    self.across(k, slot, self.me).wait_send()
            for s in range(NZ - 1):
                @pl.when((z >= s) & (z < NZ - 1))
                def _():
                    self.up(k, s).wait_send()

                @pl.when((z + s <= NZ - 1) & (z > 0))
                def _():
                    self.down(k, s).wait_send()

                if self.alt(k):
                    @pl.when(z == s)
                    def _():
                        self.up_b(k, s).wait_send()

                    @pl.when(z + s == NZ - 1)
                    def _():
                        self.down_b(k, s).wait_send()


def gather_kernel(chunks, dp, span, x_ref, *refs):
    job = None
    ng = Gather.COUNT
    if span is None:
        o_ref, *sems = refs
    else:
        src, o_ref, out, *sems = refs
        job = side_job(dp, span, src, out, sems[ng:])
    g = Gather(x_ref, o_ref, chunks, sems[:ng])
    enter(g.me, g.z, g.core, g.side, 1 if job is None else dp)
    g.start()
    if job is not None:
        job.start()
    for s in range(1, NZ + 1):
        g.round(s)
    g.finish()
    if job is not None:
        job.finish()


COST = pl.CostEstimate(flops=0, bytes_accessed=4_000_000, transcendentals=0)
ANY = pl.BlockSpec(memory_space=pl.ANY)


def gather16(v, cid, chunks=2, dp=1, span=None, side=None):
    rows, width = v.shape
    extra = span is not None
    out = pl.pallas_call(
        functools.partial(gather_kernel, chunks, dp, span),
        out_shape=(jax.ShapeDtypeStruct((NE, rows, width), v.dtype),)
        + ((jax.ShapeDtypeStruct((dp, span[1], side.shape[1]), side.dtype),) if extra else ()),
        in_specs=[ANY] * (2 if extra else 1),
        out_specs=(ANY,) * (2 if extra else 1),
        scratch_shapes=Gather.scratch(chunks) + (Spread.scratch(dp) if extra else []),
        compiler_params=pltpu.CompilerParams(collective_id=cid, has_side_effects=True),
        cost_estimate=COST,
        name="gather16",
    )(*((v, side) if extra else (v,)))
    return out if extra else out[0]


def opening_kernel(dp, chunks, x_ref, small_ref, parts_ref, out_ref,
                   x_all, small_all, parts_head, out_head, small_dp, parts_dp, out_dp, *sems):
    ng = Gather.COUNT
    gx = Gather(x_ref, x_all, chunks, sems[:ng])
    gs = Gather(small_dp, small_all, 1, sems[ng:2 * ng], lambda ref, b: ref.at[:, b])
    loc, ys, yr, ps, pr, os_, or_, pl_sem, ol_sem = sems[2 * ng:]
    me = gx.me
    plane = lax.axis_index("dp")
    enter_all(me, plane, dp)
    pairs = ((small_ref, small_dp.at[plane]), (parts_ref, parts_dp.at[plane]),
             (out_ref, out_dp.at[plane]))

    def lift(i, r):
        src, dst = pairs[i]
        return pltpu.make_async_remote_copy(
            src_ref=src, dst_ref=dst, send_sem=ys.at[i, r], recv_sem=yr.at[i, r],
            device_id={"dp": (plane + r) % dp}, device_id_type=MESH)

    def landed(i, r):
        p = (plane - r + dp) % dp
        dst = (small_dp.at[p], parts_dp.at[p], out_dp.at[p])[i]
        return pltpu.make_async_remote_copy(
            src_ref=dst, dst_ref=dst, send_sem=ys.at[i, r], recv_sem=yr.at[i, r],
            device_id={"dp": p}, device_id_type=MESH)

    def kept(i):
        src, dst = pairs[i]
        return pltpu.make_async_copy(src, dst, loc.at[i])

    for i in range(3):
        for r in range(1, dp):
            lift(i, r).start()
        kept(i).start()
    gx.start()
    gx.round(1)

    kept(0).wait()
    for r in range(1, dp):
        landed(0, r).wait_recv()
    gs.start()

    def part(r):
        h = (me + r) % NE
        return pltpu.make_async_remote_copy(
            src_ref=parts_dp.at[:, h], dst_ref=parts_head.at[:, me],
            send_sem=ps.at[r], recv_sem=pr.at[r],
            device_id={"expert": h}, device_id_type=MESH)

    def part_in(r):
        e = (me - r + NE) % NE
        return pltpu.make_async_remote_copy(
            src_ref=parts_head.at[:, e], dst_ref=parts_head.at[:, e],
            send_sem=ps.at[r], recv_sem=pr.at[r],
            device_id={"expert": e}, device_id_type=MESH)

    def part_kept():
        return pltpu.make_async_copy(parts_dp.at[:, me], parts_head.at[:, me], pl_sem)

    kept(1).wait()
    for r in range(1, dp):
        landed(1, r).wait_recv()
    for r in range(1, NE):
        part(r).start()
    part_kept().start()
    gx.round(2)

    def row(d):
        b = NE * d + me
        return pltpu.make_async_remote_copy(
            src_ref=out_dp.at[d], dst_ref=out_head.at[b % dp],
            send_sem=os_.at[d], recv_sem=or_.at[b % dp],
            device_id={"expert": b // dp}, device_id_type=MESH)

    def row_kept(d):
        b = NE * d + me
        return pltpu.make_async_copy(out_dp.at[d], out_head.at[b % dp], ol_sem.at[d])

    kept(2).wait()
    for r in range(1, dp):
        landed(2, r).wait_recv()
    for d in range(dp):
        home = (NE * d + me) // dp

        @pl.when(home != me)
        def _():
            row(d).start()

        @pl.when(home == me)
        def _():
            row_kept(d).start()

    gs.round(1)
    gx.round(3)
    gs.round(2)
    gx.round(4)
    gs.round(3)
    gs.round(4)

    def row_in(j):
        return pltpu.make_async_remote_copy(
            src_ref=out_head.at[j], dst_ref=out_head.at[j], send_sem=os_.at[j], recv_sem=or_.at[j],
            device_id={"expert": gx.core}, device_id_type=MESH)

    for r in range(1, NE):
        part_in(r).wait_recv()
        part(r).wait_send()
    part_kept().wait()
    for j in range(dp):
        @pl.when((dp * me + j) % NE != me)
        def _():
            row_in(j).wait_recv()
    for d in range(dp):
        home = (NE * d + me) // dp

        @pl.when(home != me)
        def _():
            row(d).wait_send()

        @pl.when(home == me)
        def _():
            row_kept(d).wait()
    for i in range(3):
        for r in range(1, dp):
            lift(i, r).wait_send()
    gx.finish()
    gs.finish()


def opening(dp, x, small, parts, out, cid, chunks=2):
    dma = pltpu.SemaphoreType.DMA
    rows, ws = small.shape
    bf = x.dtype
    wo = out.shape[1]
    shape = jax.ShapeDtypeStruct
    res = pl.pallas_call(
        functools.partial(opening_kernel, dp, chunks),
        out_shape=(
            shape((NE,) + x.shape, bf), shape((dp, NE, rows, ws), bf), shape((dp, NE) + parts.shape[1:], bf),
            shape((dp, rows, wo), bf),
            shape((dp, rows, ws), bf), shape((dp,) + parts.shape, bf), shape((dp, rows, wo), bf),
        ),
        in_specs=[ANY] * 4,
        out_specs=[ANY] * 7,
        scratch_shapes=Gather.scratch(chunks) + Gather.scratch(1) + [
            dma((3,)), dma((3, dp)), dma((3, dp)), dma((NE,)), dma((NE,)), dma((dp,)), dma((dp,)), dma, dma((dp,))],
        compiler_params=pltpu.CompilerParams(collective_id=cid, has_side_effects=True),
        cost_estimate=COST,
        name="opening",
    )(x, small, parts, out)
    return res[:4]


def order(z, i):
    a, b = (3, 2, 1, 0)[i], (3, 2, 0, 1)[i]
    return jnp.where(z == 0, a, jnp.where(z == 1, b, jnp.where(z == 2, 3 - b, 3 - a)))


class Scatter:
    COUNT = 14

    def __init__(self, p_ref, o_ref, chunks, scratch):
        self.p, self.o, self.chunks = p_ref, o_ref, chunks
        (self.cbuf, self.own, self.xbuf, self.ubuf, self.dbuf, self.ld, self.cs, self.cr, self.xs, self.xr,
         self.us, self.ur, self.ds, self.dr) = scratch
        self.rows = o_ref.shape[0] // chunks
        self.me, self.z, self.x, self.c, self.core, self.side = place()

    @staticmethod
    def scratch(rows, width, chunks, bf):
        dma = pltpu.SemaphoreType.DMA
        return [pltpu.VMEM((n, rows, width), bf) for n in (8, 8, 4, 4, 4)] + [
            dma((8,)), dma((8, chunks)), dma((8, chunks))] + [dma((4, chunks))] * 6

    def rng(self, k):
        return pl.ds(k * self.rows, self.rows)

    def column(self, i, j):
        return 4 * order(self.z, i) + 2 * jnp.where(j == 0, 1 - self.x, self.x)

    def remote(self, src, dst, send, recv, to):
        return pltpu.make_async_remote_copy(
            src_ref=src, dst_ref=dst, send_sem=send, recv_sem=recv,
            device_id={"expert": to}, device_id_type=MESH)

    def over(self, i, j, k):
        n = 2 * i + j
        return self.remote(
            self.p.at[self.column(i, j) + 1 - self.c, self.rng(k)], self.cbuf.at[n, self.rng(k)],
            self.cs.at[n, k], self.cr.at[n, k], self.core)

    def load(self, i, j):
        n = 2 * i + j
        return pltpu.make_async_copy(self.p.at[self.column(i, j) + self.c], self.own.at[n], self.ld.at[n])

    def across(self, i, k):
        return self.remote(self.own.at[2 * i, self.rng(k)], self.xbuf.at[i, self.rng(k)],
                           self.xs.at[i, k], self.xr.at[i, k], self.side)

    def up(self, t, i, k):
        return self.remote(self.own.at[2 * i + 1, self.rng(k)], self.ubuf.at[t, self.rng(k)],
                           self.us.at[t, k], self.ur.at[t, k], self.me + 4)

    def down(self, t, i, k):
        return self.remote(self.own.at[2 * i + 1, self.rng(k)], self.dbuf.at[t, self.rng(k)],
                           self.ds.at[t, k], self.dr.at[t, k], self.me - 4)

    def start(self):
        for i in range(NZ):
            for j in range(2):
                self.load(i, j).start()
                for k in range(self.chunks):
                    self.over(i, j, k).start()

    def first(self, i):
        f32 = jnp.float32
        self.load(i, 0).wait()
        for k in range(self.chunks):
            self.over(i, 0, k).wait_recv()
            s = self.rng(k)
            self.own[2 * i, s] = (
                self.own[2 * i, s].astype(f32) + self.cbuf[2 * i, s].astype(f32)).astype(self.own.dtype)
            self.across(i, k).start()

    def second(self, i):
        f32 = jnp.float32
        z, own, o = self.z, self.own, self.o
        t = order(z, i)
        self.load(i, 1).wait()
        for k in range(self.chunks):
            s = self.rng(k)
            self.over(i, 1, k).wait_recv()
            self.across(i, k).wait_recv()

            def base():
                return (own[2 * i + 1, s].astype(f32) + self.cbuf[2 * i + 1, s].astype(f32)
                        + self.xbuf[i, s].astype(f32))

            if i < NZ - 1:
                @pl.when(t > z)
                def _():
                    @pl.when(z > 0)
                    def _():
                        self.up(t, i, k).wait_recv()
                        own[2 * i + 1, s] = (base() + self.ubuf[t, s].astype(f32)).astype(own.dtype)

                    @pl.when(z == 0)
                    def _():
                        own[2 * i + 1, s] = base().astype(own.dtype)

                    self.up(t, i, k).start()

                @pl.when(t < z)
                def _():
                    @pl.when(z < NZ - 1)
                    def _():
                        self.down(t, i, k).wait_recv()
                        own[2 * i + 1, s] = (base() + self.dbuf[t, s].astype(f32)).astype(own.dtype)

                    @pl.when(z == NZ - 1)
                    def _():
                        own[2 * i + 1, s] = base().astype(own.dtype)

                    self.down(t, i, k).start()
            else:
                @pl.when(z > 0)
                def _():
                    self.up(t, i, k).wait_recv()

                @pl.when(z < NZ - 1)
                def _():
                    self.down(t, i, k).wait_recv()

                @pl.when((z > 0) & (z < NZ - 1))
                def _():
                    o[s] = (base() + self.ubuf[t, s].astype(f32) + self.dbuf[t, s].astype(f32)).astype(o.dtype)

                @pl.when(z == 0)
                def _():
                    o[s] = (base() + self.dbuf[t, s].astype(f32)).astype(o.dtype)

                @pl.when(z == NZ - 1)
                def _():
                    o[s] = (base() + self.ubuf[t, s].astype(f32)).astype(o.dtype)

    def run(self, between=lambda: None):
        self.first(0)
        for i in range(NZ):
            if i + 1 < NZ:
                self.first(i + 1)
            between()
            self.second(i)
            between()

    def finish(self):
        z = self.z
        for k in range(self.chunks):
            for i in range(NZ):
                self.across(i, k).wait_send()
                for j in range(2):
                    self.over(i, j, k).wait_send()
                if i < NZ - 1:
                    t = order(z, i)

                    @pl.when(t > z)
                    def _():
                        self.up(t, i, k).wait_send()

                    @pl.when(t < z)
                    def _():
                        self.down(t, i, k).wait_send()


def scatter_kernel(chunks, dp, span, p_ref, *refs):
    job = None
    ns = Scatter.COUNT
    if span is None:
        o_ref, *scratch = refs
    else:
        src, o_ref, out, *scratch = refs
        job = side_job(dp, span, src, out, scratch[ns:])
    s = Scatter(p_ref, o_ref, chunks, scratch[:ns])
    enter(s.me, s.z, s.core, s.side, 1 if job is None else dp)
    s.start()
    if job is not None:
        job.start()
    s.run()
    s.finish()
    if job is not None:
        job.finish()


VMEM = pl.BlockSpec(memory_space=pltpu.VMEM)


def scatter16(p, cid, chunks=2, dp=1, span=None, side=None):
    _, rows, width = p.shape
    extra = span is not None
    out = pl.pallas_call(
        functools.partial(scatter_kernel, chunks, dp, span),
        out_shape=(jax.ShapeDtypeStruct((rows, width), jnp.float32),)
        + ((jax.ShapeDtypeStruct((dp, span[1], side.shape[1]), side.dtype),) if extra else ()),
        in_specs=[ANY] * (2 if extra else 1),
        out_specs=(VMEM,) + ((ANY,) if extra else ()),
        scratch_shapes=Scatter.scratch(rows, width, chunks, p.dtype) + (Spread.scratch(dp) if extra else []),
        compiler_params=pltpu.CompilerParams(
            collective_id=cid, has_side_effects=True, vmem_limit_bytes=60 * 1024 * 1024),
        cost_estimate=COST,
        name="scatter16",
    )(*((p, side) if extra else (p,)))
    return out if extra else out[0]


def return_kernel(dp, chunks, p_ref, parts_ref, rows_ref, o_ref, parts_in, rows_in, parts_far, rows_far, *scratch):
    ns = Scatter.COUNT
    s = Scatter(p_ref, o_ref, chunks, scratch[:ns])
    ps, pr, os_, or_, pl_sem, ol_sem, ys, yr = scratch[ns:]
    me = s.me
    plane = lax.axis_index("dp")
    enter_all(me, plane, dp)

    def part(r):
        e = (me + r) % NE
        return pltpu.make_async_remote_copy(
            src_ref=parts_ref.at[:, e], dst_ref=parts_in.at[:, me],
            send_sem=ps.at[r], recv_sem=pr.at[r],
            device_id={"expert": e}, device_id_type=MESH)

    def part_in(r):
        h = (me - r + NE) % NE
        return pltpu.make_async_remote_copy(
            src_ref=parts_in.at[:, h], dst_ref=parts_in.at[:, h],
            send_sem=ps.at[r], recv_sem=pr.at[r],
            device_id={"expert": h}, device_id_type=MESH)

    def part_kept():
        return pltpu.make_async_copy(parts_ref.at[:, me], parts_in.at[:, me], pl_sem)

    def row(j):
        b = dp * me + j
        return pltpu.make_async_remote_copy(
            src_ref=rows_ref.at[j], dst_ref=rows_in.at[b // NE],
            send_sem=os_.at[j], recv_sem=or_.at[b // NE],
            device_id={"expert": b % NE}, device_id_type=MESH)

    def row_kept(j):
        b = dp * me + j
        return pltpu.make_async_copy(rows_ref.at[j], rows_in.at[b // NE], ol_sem.at[j])

    def row_in(d):
        return pltpu.make_async_remote_copy(
            src_ref=rows_in.at[d], dst_ref=rows_in.at[d], send_sem=os_.at[d], recv_sem=or_.at[d],
            device_id={"expert": s.core}, device_id_type=MESH)

    def lift(i, r):
        to = (plane + r) % dp
        src, dst = ((parts_in.at[to], parts_far.at[r - 1]), (rows_in.at[to], rows_far.at[r - 1]))[i]
        return pltpu.make_async_remote_copy(
            src_ref=src, dst_ref=dst, send_sem=ys.at[i, r], recv_sem=yr.at[i, r],
            device_id={"dp": to}, device_id_type=MESH)

    s.start()
    for r in range(1, NE):
        part(r).start()
    part_kept().start()
    for j in range(dp):
        @pl.when((dp * me + j) % NE != me)
        def _():
            row(j).start()

        @pl.when((dp * me + j) % NE == me)
        def _():
            row_kept(j).start()
    s.first(0)
    s.first(1)
    s.second(0)
    for r in range(1, NE):
        part_in(r).wait_recv()
    part_kept().wait()
    for j in range(dp):
        @pl.when((dp * me + j) % NE == me)
        def _():
            row_kept(j).wait()
    for d in range(dp):
        @pl.when((NE * d + me) // dp != me)
        def _():
            row_in(d).wait_recv()
    for i in range(2):
        for r in range(1, dp):
            lift(i, r).start()
    s.first(2)
    s.second(1)
    s.first(3)
    s.second(2)
    s.second(3)
    for i in range(2):
        for r in range(1, dp):
            lift(i, r).wait_recv()
            lift(i, r).wait_send()
    for r in range(1, NE):
        part(r).wait_send()
    for j in range(dp):
        @pl.when((dp * me + j) % NE != me)
        def _():
            row(j).wait_send()
    s.finish()


def returning(dp, p, parts, rows, cid, chunks=2):
    dma = pltpu.SemaphoreType.DMA
    _, n, width = p.shape
    shape = jax.ShapeDtypeStruct
    out, parts_in, rows_in, parts_far, rows_far = pl.pallas_call(
        functools.partial(return_kernel, dp, chunks),
        out_shape=(
            shape((n, width), jnp.float32), shape(parts.shape, parts.dtype), shape(rows.shape, rows.dtype),
            shape((dp - 1,) + parts.shape[1:], parts.dtype), shape((dp - 1,) + rows.shape[1:], rows.dtype)),
        in_specs=[ANY] * 3,
        out_specs=[VMEM] + [ANY] * 4,
        scratch_shapes=Scatter.scratch(n, width, chunks, p.dtype) + [
            dma((NE,)), dma((NE,)), dma((dp,)), dma((dp,)), dma, dma((dp,)), dma((2, dp)), dma((2, dp))],
        compiler_params=pltpu.CompilerParams(
            collective_id=cid, has_side_effects=True, vmem_limit_bytes=60 * 1024 * 1024),
        cost_estimate=COST,
        name="returning",
    )(p, parts, rows)
    plane = lax.axis_index("dp")

    def total(near, far):
        own = lax.dynamic_index_in_dim(near, plane, 0, False).astype(jnp.float32)
        return own + jnp.sum(far.astype(jnp.float32), axis=0)

    return out, total(parts_in, parts_far), total(rows_in, rows_far)


def closing_kernel(dp, chunks, p_ref, o_ref, far_ref, *scratch):
    ns = Scatter.COUNT
    s = Scatter(p_ref, o_ref, chunks, scratch[:ns])
    ys, yr = scratch[ns:]
    plane = lax.axis_index("dp")
    rows = o_ref.shape[0] // dp
    enter(s.me, s.z, s.core, s.side, dp)

    def lift(r):
        to = (plane + r) % dp
        return pltpu.make_async_remote_copy(
            src_ref=o_ref.at[pl.ds(pl.multiple_of(to * rows, 16), rows)], dst_ref=far_ref.at[r - 1],
            send_sem=ys.at[r], recv_sem=yr.at[r],
            device_id={"dp": to}, device_id_type=MESH)

    s.start()
    s.run()
    for r in range(1, dp):
        lift(r).start()
    s.finish()
    for r in range(1, dp):
        lift(r).wait_recv()
        lift(r).wait_send()


def closing(dp, p, cid):
    dma = pltpu.SemaphoreType.DMA
    _, n, width = p.shape
    shape = jax.ShapeDtypeStruct
    near, far = pl.pallas_call(
        functools.partial(closing_kernel, dp, 1),
        out_shape=(shape((n, width), p.dtype), shape((dp - 1, n // dp, width), p.dtype)),
        in_specs=[ANY],
        out_specs=[VMEM, VMEM],
        scratch_shapes=Scatter.scratch(n, width, 1, p.dtype) + [dma((dp,)), dma((dp,))],
        compiler_params=pltpu.CompilerParams(
            collective_id=cid, has_side_effects=True, vmem_limit_bytes=32 * 1024 * 1024),
        cost_estimate=COST,
        name="closing",
    )(p)
    own = lax.dynamic_slice_in_dim(near, lax.axis_index("dp") * (n // dp), n // dp).astype(jnp.float32)
    return own + jnp.sum(far.astype(jnp.float32), axis=0)
BF = jnp.bfloat16
F32 = jnp.float32


def mm(a, b):
    return jnp.dot(a, b, preferred_element_type=F32)


def mm_t(a, b):
    return lax.dot_general(a, b, (((1,), (1,)), ((), ())), preferred_element_type=F32)


def silu_pair(gate_in):
    sigmoid = 1.0 / (1.0 + jnp.exp(-gate_in))
    return (gate_in * sigmoid, sigmoid * (1.0 + gate_in * (1.0 - sigmoid)))


TILE = 256
WIDE = 512
SHARE = 176


def down_copies(parts, out, sem, which):
    dp = parts[0].shape[0]
    sizes = [part.shape[1] for part in parts]
    rows, first = sum(sizes), sum(sizes[:which])
    return [
        pltpu.make_async_copy(
            parts[which].at[d], out.at[pl.ds(d * rows + first, sizes[which])], sem.at[len(parts) * d + which])
        for d in range(dp)
    ]


def share_copies(share_ref, fan, down, sem):
    dp, rows, w = share_ref.shape
    n = rows // 3
    copies = []
    for d in range(dp):
        cols = pl.ds(d * w, w)
        for i, (dst, first) in enumerate(((fan, 0), (fan, TILE), (down, 0))):
            copies.append(pltpu.make_async_copy(
                share_ref.at[d, pl.ds(i * n, n)], dst.at[pl.ds(first, n), cols], sem.at[3 * d + i]))
    return copies


def share_blank(fan, down):
    pad = jnp.zeros((TILE - SHARE, fan.shape[1]), BF)
    fan[SHARE:TILE] = pad
    fan[TILE + SHARE:] = pad
    down[SHARE:] = pad


def mine_of(routes_ref, pick_ref):
    tokens = routes_ref.shape[0]
    lane16 = lax.broadcasted_iota(jnp.int32, (tokens, 16), 1)
    mask = lane16 < 0
    for k in range(routes_ref.shape[1]):
        mask = mask | (lane16 == routes_ref[:, k:k + 1])
    mine = jnp.sum(jnp.where(mask, pick_ref[:, :16], 0.0), axis=1, keepdims=True)
    return mask, mine


def valid_of(len_ref, first_device, tokens, batches, here):
    n = lax.broadcasted_iota(jnp.int32, (tokens, 1), 0)
    device = n // (batches * here)
    batch = (n // here) % batches
    position = (first_device + device) * here + n % here
    length = jnp.zeros((tokens, 1), jnp.int32)
    for b in range(batches):
        length = jnp.where(batch == b, len_ref[b], length)
    return (position < length).astype(F32)


def one_hots(taken, groups, slots, here):
    r = lax.broadcasted_iota(jnp.int32, (256, 256), 0)
    c = lax.broadcasted_iota(jnp.int32, (256, 256), 1)
    same = r // here == c // here
    before = (same & (c < r)).astype(BF)
    after = (same & (r < c)).astype(BF)
    base_c = (lax.broadcasted_iota(jnp.int32, (256, slots), 0) // here * 32).astype(F32)
    base_r = (lax.broadcasted_iota(jnp.int32, (slots, 256), 1) // here * 32).astype(F32)
    lane = lax.broadcasted_iota(jnp.int32, (256, slots), 1).astype(F32)
    row = lax.broadcasted_iota(jnp.int32, (slots, 256), 0).astype(F32)
    ones = jnp.ones((256, slots), BF)
    to_slot, to_token = [], []
    for g in range(groups):
        t = jnp.broadcast_to(taken[g * 256:(g + 1) * 256], (256, slots))
        low = t.astype(BF)
        place_c = mm(before, low) + base_c
        place_r = mm_lead(low, after) + base_r
        taken_r = mm_lead(low, (r == c).astype(BF))
        to_token.append(jnp.where((place_c == lane) & (t > 0.5), 1.0, 0.0).astype(BF))
        to_slot.append(jnp.where((place_r == row) & (taken_r > 0.5), 1.0, 0.0).astype(BF))
    return to_slot, to_token


def mm_lead(a, b):
    return lax.dot_general(a, b, (((0,), (0,)), ((), ())), preferred_element_type=F32)


def lanes(j):
    return pl.ds(pl.multiple_of(j * WIDE, WIDE), WIDE)


def over_columns(total, body):
    def step(j, _):
        body(pl.multiple_of(j * WIDE, WIDE), WIDE)
        return 0

    lax.fori_loop(0, total // WIDE, step, 0)
    if total % WIDE:
        body(total // WIDE * WIDE, total % WIDE)


def forward_kernel(chunks, dp, span, batches, here, len_ref, pick_ref, mix_ref, routes_ref, wg_ref, wu_ref, router_ref,
                   share_ref, wda_ref, wdb_ref, down_ref, dy_ref,
                   out_ref, rows_ref, hid_ref, act_ref, slo_ref, eo_ref, sh_ref, sact_ref, sslo_ref, gate_ref,
                   dy_all, wdc_ref,
                   wd_ref, fan_ref, sd_ref, hid_buf, sh_buf, gate_buf, taken_buf, wd_sem, sh_sem, *sems):
    step = pl.program_id(0)
    tokens, width = mix_ref.shape
    groups, slots = tokens // 256, 128
    half = groups * slots
    ff = hid_ref.shape[1]
    phase = pl.num_programs(0) // 2
    g = Gather(dy_ref, dy_all, chunks, sems[:Gather.COUNT])
    job = side_job(dp, span, down_ref, wdc_ref, sems[Gather.COUNT:])
    parts = (wda_ref, wdb_ref, wdc_ref)

    @pl.when(step == 0)
    def _():
        enter(g.me, g.z, g.core, g.side, dp)
        g.start()
        job.start()
        copies = share_copies(share_ref, fan_ref, sd_ref, sh_sem)
        for copy in copies + down_copies(parts, wd_ref, wd_sem, 0) + down_copies(parts, wd_ref, wd_sem, 1):
            copy.start()
        share_blank(fan_ref, sd_ref)
        fan_ref[SHARE:SHARE + 16] = router_ref[...]
        for copy in copies:
            copy.wait()

    @pl.when(step < phase)
    def _():
        mix = mix_ref[...]
        fanned = mm_t(mix, fan_ref[:TILE, :])
        s_up = mm_t(mix, fan_ref[TILE:, :])
        s_act, s_slope = silu_pair(fanned)
        s_hidden = (s_act * s_up).astype(BF)
        at = pl.ds(pl.multiple_of(step * tokens, tokens), tokens)
        sh_ref[...] = s_hidden
        sh_buf[at] = s_hidden
        sact_ref[...] = s_act.astype(BF)
        sslo_ref[...] = (s_up * s_slope).astype(BF)
        logits = fanned[:, SHARE:SHARE + 16]
        mask, mine = mine_of(routes_ref, pick_ref)
        taken = mine * valid_of(len_ref, step * (tokens // (batches * here)), tokens, batches, here)
        held = jnp.where(mask, logits, -1e30)
        raised = jnp.where(mask, jnp.exp(held - jnp.max(held, axis=1, keepdims=True)), 0.0)
        soft = raised / jnp.sum(raised, axis=1, keepdims=True)
        gate = jnp.sum(soft * pick_ref[:, :16], axis=1, keepdims=True) * taken
        gate_ref[...] = jnp.concatenate([gate, taken], axis=1)
        gate_buf[at] = gate
        taken_buf[at] = taken
        to_slot, _ = one_hots(taken, groups, slots, here)

        def dispatch(j, _):
            for n in range(groups):
                rows_ref[n * slots:(n + 1) * slots, lanes(j)] = mm(
                    to_slot[n], mix_ref[n * 256:(n + 1) * 256, lanes(j)]).astype(BF)
            return 0

        lax.fori_loop(0, width // WIDE, dispatch, 0)
        rows_at = pl.ds(pl.multiple_of(step * half, half), half)

        def fan_in(start, size):
            cols = pl.ds(start, size)
            gate_in = mm(rows_ref[...], wg_ref[:, cols])
            up_in = mm(rows_ref[...], wu_ref[:, cols])
            act, slope = silu_pair(gate_in)
            hidden = (act * up_in).astype(BF)
            hid_ref[:, cols] = hidden
            hid_buf[rows_at, cols] = hidden
            act_ref[:, cols] = act.astype(BF)
            slo_ref[:, cols] = (up_in * slope).astype(BF)

        over_columns(ff, fan_in)

    @pl.when(step == phase)
    def _():
        job.finish()
        for copy in down_copies(parts, wd_ref, wd_sem, 2):
            copy.start()
        for which in range(3):
            for copy in down_copies(parts, wd_ref, wd_sem, which):
                copy.wait()

    @pl.when(step >= phase)
    def _():
        tile = step - phase
        at = pl.ds(pl.multiple_of(tile * tokens, tokens), tokens)
        rows_at = pl.ds(pl.multiple_of(tile * half, half), half)
        gate = gate_buf[at]
        s_hidden = sh_buf[at]
        _, to_token = one_hots(taken_buf[at], groups, slots, here)

        def fan_out(j, _):
            eo = mm(hid_buf[rows_at], wd_ref[:, lanes(j)]).astype(BF)
            eo_ref[:, lanes(j)] = eo
            shared = mm(s_hidden, sd_ref[:, lanes(j)])
            picked = jnp.concatenate(
                [mm(to_token[n], eo[n * slots:(n + 1) * slots]) for n in range(groups)], axis=0)
            out_ref[:, lanes(j)] = (shared + gate * picked).astype(BF)
            return 0

        lax.fori_loop(0, width // WIDE, fan_out, 0)

    for r, s in ((1, 1), (2, 2), (3, 4), (4, 6)):
        @pl.when(step == s)
        def _():
            g.round(r)

    @pl.when(step == 2 * phase - 1)
    def _():
        g.finish()


def backward_kernel(here, chunks, pick_ref, dy_ref, wg_ref, wu_ref, share_ref, wda_ref, wdb_ref, wdc_ref,
                    act_ref, slo_ref, eo_ref, sact_ref, sslo_ref, gate_ref, part_ref,
                    dh_ref, deo_ref, dg_ref, du_ref, ds_ref, sum_ref,
                    wd_ref, fan_ref, sd_ref, wd_sem, sh_sem, *scratch):
    step = pl.program_id(0)
    tokens, width = dy_ref.shape
    groups, slots = tokens // 256, 128
    ff = dg_ref.shape[1]
    sc = Scatter(part_ref, sum_ref, chunks, scratch)

    @pl.when(step == 0)
    def _():
        enter(sc.me, sc.z, sc.core, sc.side)
        copies = share_copies(share_ref, fan_ref, sd_ref, sh_sem)
        for which in range(3):
            copies += down_copies((wda_ref, wdb_ref, wdc_ref), wd_ref, wd_sem, which)
        for copy in copies:
            copy.start()
        sc.start()
        share_blank(fan_ref, sd_ref)
        for copy in copies:
            copy.wait()

    d_sh = mm_t(dy_ref[...], sd_ref[...])
    d_s = jnp.concatenate([(d_sh * sslo_ref[...].astype(F32)).astype(BF),
                           (d_sh * sact_ref[...].astype(F32)).astype(BF)], axis=1)
    ds_ref[...] = d_s
    gate, taken = gate_ref[:, :1], gate_ref[:, 1:]
    to_slot, to_token = one_hots(taken, groups, slots, here)

    @pl.when(step == 0)
    def _():
        sc.first(0)
        sc.first(1)

    def dispatch(j, total):
        dy = dy_ref[:, lanes(j)].astype(F32)
        gated = (gate * dy).astype(BF)
        for n in range(groups):
            deo_ref[n * slots:(n + 1) * slots, lanes(j)] = mm(to_slot[n], gated[n * 256:(n + 1) * 256]).astype(BF)
        picked = jnp.concatenate(
            [mm(to_token[n], eo_ref[n * slots:(n + 1) * slots, lanes(j)]) for n in range(groups)], axis=0)
        return total + jnp.sum(dy * picked, axis=1, keepdims=True)

    d_gates = lax.fori_loop(0, width // WIDE, dispatch, jnp.zeros((tokens, 1), F32))

    def back_out(start, size):
        cols = pl.ds(start, size)
        d_eh = mm_t(deo_ref[...], wd_ref[cols, :])
        dg_ref[:, cols] = (d_eh * slo_ref[:, cols].astype(F32)).astype(BF)
        du_ref[:, cols] = (d_eh * act_ref[:, cols].astype(F32)).astype(BF)

    over_columns(ff, back_out)

    @pl.when(step == 0)
    def _():
        sc.first(2)
        sc.first(3)

    def back_in(j, _):
        d_rows = (mm_t(dg_ref[...], wg_ref[lanes(j), :]) + mm_t(du_ref[...], wu_ref[lanes(j), :])).astype(BF)
        shared = mm(d_s, fan_ref[:, lanes(j)])
        taken_rows = jnp.concatenate(
            [mm(to_token[n], d_rows[n * slots:(n + 1) * slots]) for n in range(groups)], axis=0)
        dh_ref[:, lanes(j)] = (shared + taken_rows).astype(BF)
        return 0

    lax.fori_loop(0, width // WIDE, back_in, 0)
    high = d_gates.astype(BF).astype(F32)
    dh_ref[:, width:] = (high * pick_ref[:, :128] + (d_gates - high) * pick_ref[:, 128:]).astype(BF)

    outer = (sc.z == 0) | (sc.z == NZ - 1)
    for i in range(NZ - 1):
        @pl.when((step == i) & outer)
        def _():
            sc.second(i)

        @pl.when((step == min(i + 1, 2)) & jnp.logical_not(outer))
        def _():
            sc.second(i)

    @pl.when(step == NZ - 1)
    def _():
        sc.second(NZ - 1)
        sc.finish()


def whole(v):
    zeros = (0,) * v.ndim
    return pl.BlockSpec(v.shape, lambda i: zeros, pipeline_mode=pl.Buffered(buffer_count=1))


def tiles(rows, w):
    return pl.BlockSpec((rows, w), lambda i: (i, 0))


SMEM = pl.BlockSpec(memory_space=pltpu.SMEM)


def mixture_forward(dp, batches, here, lengths, pick, mix, routes, wg, wu, router, share, wda, wdb, span, down, dy, cid,
                    chunks=2):
    total, width = mix.shape
    step, half = total // 4, total // 8
    ff = wg.shape[1]
    shape = jax.ShapeDtypeStruct
    rows = total // 2
    dma = pltpu.SemaphoreType.DMA

    def early(n, w):
        return pl.BlockSpec((n, w), lambda i: (jnp.minimum(i, 3), 0))

    def late(n, w):
        return pl.BlockSpec((n, w), lambda i: (jnp.maximum(i - 4, 0), 0))

    return pl.pallas_call(
        functools.partial(forward_kernel, chunks, dp, span, batches, here),
        grid=(8,),
        out_shape=(
            shape((total, width), BF), shape((rows, width), BF), shape((rows, ff), BF), shape((rows, ff), BF),
            shape((rows, ff), BF), shape((rows, width), BF), shape((total, TILE), BF), shape((total, TILE), BF),
            shape((total, TILE), BF), shape((total, 2), F32), shape((NE,) + dy.shape, BF),
            shape((dp, span[1], width), BF)),
        in_specs=[SMEM, whole(pick), early(step, width), early(step, routes.shape[1]), whole(wg), whole(wu),
                  whole(router), ANY, ANY, ANY, ANY, ANY],
        out_specs=[late(step, width), early(half, width), early(half, ff), early(half, ff), early(half, ff),
                   late(half, width), early(step, TILE), early(step, TILE), early(step, TILE), early(step, 2), ANY, ANY],
        scratch_shapes=[
            pltpu.VMEM((ff, width), BF), pltpu.VMEM((2 * TILE, width), BF), pltpu.VMEM((TILE, width), BF),
            pltpu.VMEM((rows, ff), BF), pltpu.VMEM((total, TILE), BF), pltpu.VMEM((total, 1), F32),
            pltpu.VMEM((total, 1), F32), dma((3 * dp,)), dma((3 * dp,))] + Gather.scratch(chunks) + Spread.scratch(dp),
        compiler_params=pltpu.CompilerParams(
            collective_id=cid, has_side_effects=True, vmem_limit_bytes=60 * 1024 * 1024),
        cost_estimate=COST,
        name="mixture_forward",
    )(lengths, pick, mix, routes, wg, wu, router, share, wda, wdb, down, dy)


def mixture_backward(here, pick, dy, wg, wu, share, wda, wdb, wdc, act, slo, eo, sact, sslo, gate, part, cid, chunks=2):
    total, width = dy.shape
    step, half = total // NZ, total // NZ // 2
    ff = wg.shape[1]
    shape = jax.ShapeDtypeStruct
    rows = total // 2
    dp = wda.shape[0]
    _, own, _ = part.shape
    dma = pltpu.SemaphoreType.DMA
    return pl.pallas_call(
        functools.partial(backward_kernel, here, chunks),
        grid=(NZ,),
        out_shape=(
            shape((total, width + 128), BF), shape((rows, width), BF), shape((rows, ff), BF), shape((rows, ff), BF),
            shape((total, 2 * TILE), BF), shape((own, width), F32)),
        in_specs=[whole(pick), tiles(step, width), whole(wg), whole(wu), ANY, ANY, ANY, ANY,
                  tiles(half, ff), tiles(half, ff), tiles(half, width), tiles(step, TILE), tiles(step, TILE),
                  tiles(step, 2), ANY],
        out_specs=[tiles(step, width + 128), tiles(half, width), tiles(half, ff), tiles(half, ff),
                   tiles(step, 2 * TILE), pl.BlockSpec((own, width), lambda i: (0, 0))],
        scratch_shapes=[
            pltpu.VMEM((ff, width), BF), pltpu.VMEM((2 * TILE, width), BF), pltpu.VMEM((TILE, width), BF),
            dma((3 * dp,)), dma((3 * dp,))] + Scatter.scratch(own, width, chunks, BF),
        compiler_params=pltpu.CompilerParams(
            collective_id=cid, has_side_effects=True, vmem_limit_bytes=62 * 1024 * 1024),
        cost_estimate=COST,
        name="mixture_backward",
    )(pick, dy, wg, wu, share, wda, wdb, wdc, act, slo, eo, sact, sslo, gate, part)


class ShareWork:
    ROWS = 256

    def __init__(self, ds_ref, sh_ref, mix_ref, dy_ref, out_ref, scratch):
        self.sources = (ds_ref, sh_ref, mix_ref, dy_ref)
        self.out = out_ref
        *self.buffers, self.gfan, self.gsd, self.sem = scratch
        self.steps = mix_ref.shape[0] // self.ROWS
        self.done = 0

    @staticmethod
    def scratch(width):
        r = ShareWork.ROWS
        return [pltpu.VMEM((2, r, w), BF) for w in (2 * TILE, TILE, width, width)] + [
            pltpu.VMEM((2 * TILE, width), F32), pltpu.VMEM((TILE, width), F32), pltpu.SemaphoreType.DMA((2, 4))]

    COUNT = 7

    def copies(self, n):
        return [pltpu.make_async_copy(src.at[pl.ds(n * self.ROWS, self.ROWS)], buf.at[n % 2], self.sem.at[n % 2, i])
                for i, (src, buf) in enumerate(zip(self.sources, self.buffers))]

    def start(self):
        for copy in self.copies(0):
            copy.start()
        self.gfan[...] = jnp.zeros_like(self.gfan)
        self.gsd[...] = jnp.zeros_like(self.gsd)

    def step(self):
        n = self.done
        if n == self.steps:
            return
        self.done += 1
        for copy in self.copies(n):
            copy.wait()
        if n + 1 < self.steps:
            for copy in self.copies(n + 1):
                copy.start()
        ds, sh, mix, dy = self.buffers

        def columns(j, _):
            self.gfan[:, lanes(j)] += mm_lead(ds[n % 2], mix[n % 2, :, lanes(j)])
            self.gsd[:, lanes(j)] += mm_lead(sh[n % 2], dy[n % 2, :, lanes(j)])
            return 0

        lax.fori_loop(0, mix.shape[2] // WIDE, columns, 0)

    def finish(self):
        while self.done < self.steps:
            self.step()
        dp, rows, w = self.out.shape
        n = rows // 3
        for d in range(dp):
            cols = slice(d * w, (d + 1) * w)
            self.out[d, :n] = self.gfan[:n, cols].astype(BF)
            self.out[d, n:2 * n] = self.gfan[TILE:TILE + n, cols].astype(BF)
            self.out[d, 2 * n:] = self.gsd[:n, cols].astype(BF)


def scatter_share_kernel(chunks, p_ref, ds_ref, sh_ref, mix_ref, dy_ref, o_ref, g_ref, *scratch):
    s = Scatter(p_ref, o_ref, chunks, scratch[:Scatter.COUNT])
    work = ShareWork(ds_ref, sh_ref, mix_ref, dy_ref, g_ref, scratch[Scatter.COUNT:])
    enter(s.me, s.z, s.core, s.side)
    s.start()
    work.start()
    s.run(work.step)
    work.finish()
    s.finish()


def scatter_share(p, ds, sh, mix, dy, share_shape, cid, chunks=2):
    _, rows, width = p.shape
    return pl.pallas_call(
        functools.partial(scatter_share_kernel, chunks),
        out_shape=(jax.ShapeDtypeStruct((rows, width), F32), jax.ShapeDtypeStruct(share_shape, BF)),
        in_specs=[ANY] * 5,
        out_specs=(VMEM, VMEM),
        scratch_shapes=Scatter.scratch(rows, width, chunks, p.dtype) + ShareWork.scratch(mix.shape[1]),
        compiler_params=pltpu.CompilerParams(
            collective_id=cid, has_side_effects=True, vmem_limit_bytes=60 * 1024 * 1024),
        cost_estimate=COST,
        name="scatter_share",
    )(p, ds, sh, mix, dy)


def turn(v, cosine, sine):
    half = v.shape[1] // 2
    a, b = v[:, :half], v[:, half:]
    return jnp.concatenate([a * cosine - b * sine, b * cosine + a * sine], axis=1)


def project_kernel(x_ref, gain_ref, lgain_ref, wq_ref, wl_ref, we_ref, cos_ref, sin_ref,
                   h_ref, q_ref, k_ref, v_ref, lat_ref):
    blocks = x_ref.shape[0]
    batches, rows, _ = q_ref.shape
    here = rows // blocks
    x = x_ref[...].reshape(blocks * batches * here, x_ref.shape[2]).astype(F32)
    h = x * lax.rsqrt(jnp.mean(x * x, axis=1, keepdims=True) + 1e-6) * gain_ref[...]
    h = h.astype(BF)
    h_ref[...] = h
    raw = mm(h, wq_ref[...])
    raw_lat = mm(h, wl_ref[...])
    cosine, sine = cos_ref[...], sin_ref[...]
    zeros = jnp.zeros((raw.shape[0], 64), BF)
    q = jnp.concatenate([raw[:, :128].astype(BF), turn(raw[:, 128:192], cosine, sine).astype(BF), zeros], axis=1)
    k_rope = turn(raw_lat[:, 512:576], cosine, sine).astype(BF)
    lat = raw_lat[:, :512]
    lat = (lat * lax.rsqrt(jnp.mean(lat * lat, axis=1, keepdims=True) + 1e-6) * lgain_ref[...]).astype(BF)
    expanded = mm(lat, we_ref[...]).astype(BF)
    k = jnp.concatenate([expanded[:, :128], k_rope, zeros], axis=1)
    for e in range(blocks):
        for m in range(batches):
            src = slice((e * batches + m) * here, (e * batches + m + 1) * here)
            dst = slice(e * here, (e + 1) * here)
            q_ref[m, dst] = q[src]
            k_ref[m, dst] = k[src]
            v_ref[m, dst] = expanded[src, 128:]
            lat_ref[m, dst] = lat[src]


def project(x_all, gain, lgain, wq, wl, we, cosine, sine, batches):
    groups, rows, width = x_all.shape
    here = rows // batches
    per = 4
    seq = groups * here
    shape = jax.ShapeDtypeStruct

    def whole(v):
        return pl.BlockSpec(v.shape, lambda i: (0, 0))

    def by_seq(w):
        return pl.BlockSpec((batches, per * here, w), lambda i: (0, i, 0))

    table = pl.BlockSpec((per * rows, 32), lambda i: (i, 0))
    return pl.pallas_call(
        project_kernel,
        grid=(groups // per,),
        out_shape=(shape((groups * rows, width), BF), shape((batches, seq, 256), BF), shape((batches, seq, 256), BF),
                   shape((batches, seq, 128), BF), shape((batches, seq, 512), BF)),
        in_specs=[pl.BlockSpec((per, rows, width), lambda i: (i, 0, 0)), whole(gain), whole(lgain), whole(wq), whole(wl), whole(we),
                  table, table],
        out_specs=[pl.BlockSpec((per * rows, width), lambda i: (i, 0)), by_seq(256), by_seq(256), by_seq(128), by_seq(512)],
        compiler_params=pltpu.CompilerParams(vmem_limit_bytes=48 * 1024 * 1024),
        cost_estimate=pl.CostEstimate(flops=7_000_000_000, bytes_accessed=20_000_000, transcendentals=0),
        name="project",
    )(x_all, gain, lgain, wq, wl, we, cosine, sine)


ROWS = 256
SCALE = 192.0 ** -0.5


def held_scores(q, k, first, length):
    s = mm_t(q, k) * SCALE
    t = lax.broadcasted_iota(jnp.int32, s.shape, 0) + first
    u = lax.broadcasted_iota(jnp.int32, s.shape, 1)
    return jnp.where((u <= t) & (u < length), s, -1e30)


def attend_kernel(len_ref, q_ref, k_ref, v_ref, wo_ref, part_ref, att_ref, lse_ref):
    length = len_ref[pl.program_id(0)]
    seq = q_ref.shape[1]
    groups, _, here, width = part_ref.shape
    for i in range(seq // ROWS):
        tile = slice(i * ROWS, (i + 1) * ROWS)
        ext = (i + 1) * ROWS
        s = held_scores(q_ref[0, tile], k_ref[0, :ext], i * ROWS, length)
        peak = jnp.max(s, axis=1, keepdims=True)
        raised = jnp.exp(s - peak)
        total = jnp.sum(raised, axis=1, keepdims=True)
        lse_ref[0, tile] = peak + jnp.log(total)
        p = (raised / total).astype(BF)
        att = mm(p, v_ref[0, :ext]).astype(BF)
        per = ROWS // here
        att_ref[i * per:(i + 1) * per, 0] = att.reshape(per, here, att.shape[1])
        for j in range(width // 512):
            cols = slice(j * 512, (j + 1) * 512)
            part_ref[i * per:(i + 1) * per, 0, :, cols] = mm(att, wo_ref[:, cols]).astype(BF).reshape(per, here, 512)


def attend(lengths, q, k, v, wo, groups):
    batches, seq, _ = q.shape
    here = seq // groups
    width = wo.shape[1]
    shape = jax.ShapeDtypeStruct

    def by_seq(w):
        return pl.BlockSpec((1, seq, w), lambda m: (m, 0, 0))

    def by_dev(w):
        return pl.BlockSpec((groups, 1, here, w), lambda m: (0, m, 0, 0))

    return pl.pallas_call(
        attend_kernel,
        grid=(batches,),
        out_shape=(shape((groups, batches, here, width), BF), shape((groups, batches, here, 128), BF),
                   shape((batches, seq, 1), F32)),
        in_specs=[pl.BlockSpec(memory_space=pltpu.SMEM), by_seq(256), by_seq(256), by_seq(128),
                  pl.BlockSpec(wo.shape, lambda m: (0, 0))],
        out_specs=[by_dev(width), by_dev(128), by_seq(1)],
        compiler_params=pltpu.CompilerParams(vmem_limit_bytes=48 * 1024 * 1024),
        cost_estimate=pl.CostEstimate(flops=4_000_000_000, bytes_accessed=15_000_000, transcendentals=2_000_000),
        name="attend",
    )(lengths, q, k, v, wo)


def attend_back_kernel(len_ref, dout_ref, q_ref, k_ref, v_ref, lat_ref, att_ref, lse_ref, wo_ref, wq_ref, we_ref,
                       cos_ref, sin_ref, part_ref, dq_ref, gwo_ref, gwe_ref, dk, dv, datt):
    m = pl.program_id(0)
    length = len_ref[m]
    seq = q_ref.shape[1]
    groups, _, here, width = dout_ref.shape
    per = ROWS // here

    @pl.when(m == 0)
    def _():
        gwo_ref[...] = jnp.zeros_like(gwo_ref)
        gwe_ref[...] = jnp.zeros_like(gwe_ref)

    for j in range(4):
        blocks = slice(j * groups // 4, (j + 1) * groups // 4)
        dout = dout_ref[blocks].reshape(seq // 4, width)
        rows = slice(j * seq // 4, (j + 1) * seq // 4)
        datt[rows] = mm_t(dout, wo_ref[...]).astype(BF)
        gwo_ref[...] += mm_lead(att_ref[blocks].reshape(seq // 4, 128), dout)
    dk[...] = jnp.zeros_like(dk)
    dv[...] = jnp.zeros_like(dv)
    for i in range(seq // ROWS):
        tile = slice(i * ROWS, (i + 1) * ROWS)
        ext = (i + 1) * ROWS
        q = q_ref[0, tile]
        p = jnp.exp(held_scores(q, k_ref[0, :ext], i * ROWS, length) - lse_ref[0, tile])
        da = datt[tile]
        dp = mm_t(da, v_ref[0, :ext])
        inner = jnp.sum(dp * p, axis=1, keepdims=True)
        ds = (p * (dp - inner)).astype(BF)
        dq = mm(ds, k_ref[0, :ext]) * SCALE
        dk[:ext] += mm_lead(ds, q)
        dv[:ext] += mm_lead(p.astype(BF), da)
        rope = turn(dq[:, 128:192], cos_ref[tile], -sin_ref[tile])
        dq = jnp.concatenate([dq[:, :128].astype(BF), rope.astype(BF), jnp.zeros((ROWS, 64), BF)], axis=1)
        dq_ref[i * per:(i + 1) * per, 0] = dq.reshape(per, here, 256)
        for j in range(width // 512):
            cols = slice(j * 512, (j + 1) * 512)
            part_ref[i * per:(i + 1) * per, 0, :, cols] = mm_t(dq, wq_ref[cols]).astype(BF).reshape(per, here, 512)
    for i in range(seq // ROWS):
        tile = slice(i * ROWS, (i + 1) * ROWS)
        d_k = dk[tile] * SCALE
        d_exp = jnp.concatenate([d_k[:, :128].astype(BF), dv[tile].astype(BF)], axis=1)
        gwe_ref[...] += mm_lead(lat_ref[0, tile], d_exp)
        d_lat = mm_t(d_exp, we_ref[...]).astype(BF)
        tail = jnp.concatenate([d_lat, d_k[:, 128:].astype(BF)], axis=1)
        pad = part_ref.shape[3] - width - tail.shape[1]
        if pad > 0:
            tail = jnp.concatenate([tail, jnp.zeros((ROWS, pad), BF)], axis=1)
        part_ref[i * per:(i + 1) * per, 0, :, width:] = tail[:, :part_ref.shape[3] - width].reshape(per, here, -1)


def attend_back(lengths, dout, q, k, v, lat, att, lse, wo, wq, we, cosine, sine, tail):
    groups, batches, here, width = dout.shape
    seq = groups * here
    shape = jax.ShapeDtypeStruct

    def by_seq(w):
        return pl.BlockSpec((1, seq, w), lambda m: (m, 0, 0))

    def by_dev(w):
        return pl.BlockSpec((groups, 1, here, w), lambda m: (0, m, 0, 0))

    def whole(v):
        return pl.BlockSpec(v.shape, lambda m: (0, 0))

    return pl.pallas_call(
        attend_back_kernel,
        grid=(batches,),
        out_shape=(shape((groups, batches, here, width + tail), BF), shape((groups, batches, here, 256), BF),
                   shape(wo.shape, F32), shape(we.shape, F32)),
        in_specs=[pl.BlockSpec(memory_space=pltpu.SMEM), by_dev(width), by_seq(256), by_seq(256), by_seq(128),
                  by_seq(512), by_dev(128), by_seq(1), whole(wo), whole(wq), whole(we), whole(cosine), whole(sine)],
        out_specs=[by_dev(width + tail), by_dev(256), whole(wo), whole(we)],
        scratch_shapes=[pltpu.VMEM((seq, 256), F32), pltpu.VMEM((seq, 128), F32), pltpu.VMEM((seq, 128), BF)],
        compiler_params=pltpu.CompilerParams(vmem_limit_bytes=56 * 1024 * 1024),
        cost_estimate=pl.CostEstimate(flops=14_000_000_000, bytes_accessed=25_000_000, transcendentals=2_000_000),
        name="attend_back",
    )(lengths, dout, q, k, v, lat, att, lse, wo, wq, we, cosine, sine)


H = 16
QK_NOPE = 128
ROPE = 64
V_DIM = 128
KV_RANK = 512
GROUPS = 16
EPSILON = 1e-06
ROTARY_BASE = 10000.0


def product(left_side, right_side):
    return jnp.dot(left_side, right_side, preferred_element_type=F32)


def product_lead(left_side, right_side):
    return lax.dot_general(
        left_side, right_side, (((0,), (0,)), ((), ())), preferred_element_type=F32
    )


def product_trail(left_side, right_side):
    return lax.dot_general(
        left_side, right_side, (((1,), (1,)), ((), ())), preferred_element_type=F32
    )


def rotary_tables(count):
    frequency = ROTARY_BASE ** (-np.arange(ROPE // 2, dtype=np.float32) * np.float32(2.0) / np.float32(ROPE))
    angles = np.arange(count, dtype=np.float32)[:, None] * frequency.astype(np.float32)[None, :]
    return np.cos(angles).astype(np.float32), np.sin(angles).astype(np.float32)


def rotate(values, cosine, sine_table):
    first_half, second_half = jnp.split(values, 2, axis=-1)
    return jnp.concatenate(
        [
            first_half * cosine - second_half * sine_table,
            second_half * cosine + first_half * sine_table,
        ],
        axis=-1,
    )


def norm_forward(values, gains):
    factor = lax.rsqrt(jnp.mean(values * values, axis=-1, keepdims=True) + EPSILON)
    normed = values * factor
    return (normed * gains, normed, factor)


def norm_backward(gradient, normed, factor, gains):
    gain_grad = jnp.sum(gradient * normed, axis=0)
    scaled = gradient * gains
    return (
        factor * (scaled - normed * jnp.mean(scaled * normed, axis=-1, keepdims=True)),
        gain_grad,
    )


def selected_experts(routes):
    chosen = routes[:, :, None] == jnp.arange(GROUPS, dtype=routes.dtype)
    return jnp.any(chosen, axis=1)


def masked_softmax(logits, mask):
    held = jnp.where(mask, logits, -1e30)
    peak = jnp.max(held, axis=-1, keepdims=True)
    raised = jnp.where(mask, jnp.exp(held - peak), 0.0)
    return raised / jnp.sum(raised, axis=-1, keepdims=True)


def per_device(
    layer_input,
    out_cotangent,
    lengths,
    routes,
    attn_gain,
    query_weight,
    latent_weight,
    latent_gain,
    expand_weight,
    output_weight,
    mixer_gain,
    router_weight,
    gate_weight,
    up_weight,
    down_weight,
    shared_gate,
    shared_up,
    shared_down,
):
    dp = lax.axis_size("dp")
    me = lax.axis_index("expert")
    plane = lax.axis_index("dp")
    batches, _, here, width = layer_input.shape
    own = batches * here
    total = own * GROUPS
    seq_total = here * GROUPS
    rows_w = query_weight.shape[0]
    rows_l = expand_weight.shape[0]

    x_own = layer_input.reshape(own, width)
    routes_own = routes.reshape(own, -1)
    choices = routes_own.shape[1]
    route_columns = routes_own.astype(BF).reshape(rows_w, -1)
    small_width = -(-(595 + route_columns.shape[1]) // 128) * 128
    latent_column = jnp.zeros((rows_w,), BF).at[:rows_l].set(latent_gain)
    small = jnp.concatenate(
        [
            latent_weight,
            router_weight,
            attn_gain[:, None],
            mixer_gain[:, None],
            latent_column[:, None],
            route_columns,
            jnp.zeros((rows_w, small_width - 595 - route_columns.shape[1]), BF),
        ],
        axis=1,
    )
    query_parts = query_weight.reshape(rows_w, H, QK_NOPE + ROPE).transpose(1, 0, 2)
    expand_parts = expand_weight.reshape(rows_l, H, QK_NOPE + V_DIM).transpose(1, 0, 2)
    parts = jnp.concatenate([query_parts, expand_parts.reshape(H, rows_w, ROPE)], axis=2)
    x_all, small, parts_head, output_head = opening(dp, x_own, small, parts, output_weight, 1)
    x_all = x_all.reshape(total, width)
    routes_all = lax.dynamic_index_in_dim(small, plane, 0, False)[..., 595 : 595 + route_columns.shape[1]]
    routes_all = routes_all.reshape(total, choices).astype(jnp.int32)
    small = small.reshape(width, small_width)
    parts_head = parts_head.reshape(width, TILE)
    latent_full = small[:, :576]
    router_full = small[:, 576:592]
    gain_attn = small[:, 592].astype(F32)
    gain_mixer = small[:, 593].astype(F32)
    gain_latent = small[:, 594].reshape(dp * GROUPS, rows_w)[:, :rows_l].reshape(-1).astype(F32)
    expand_head = parts_head[:, QK_NOPE + ROPE :].reshape(KV_RANK, QK_NOPE + V_DIM)
    output_head = output_head.reshape(V_DIM, width)

    ff = gate_weight.shape[2]
    share_own = jnp.concatenate([shared_gate.T, shared_up.T, shared_down], axis=0)
    share_width = shared_down.shape[0]
    gate_full = lax.all_gather(gate_weight[0], "dp", axis=0, tiled=True)
    up_full = lax.all_gather(up_weight[0], "dp", axis=0, tiled=True)
    share_full = lax.all_gather(share_own, "dp", axis=0)
    seq_lengths = lengths.reshape(batches)
    own_positions = me * here + jnp.arange(here, dtype=jnp.int32)
    valid_own = (own_positions[None, :] < seq_lengths[:, None]).reshape(own).astype(F32)
    cosine, sine_table = rotary_tables(seq_total)
    cosine_own = lax.dynamic_slice_in_dim(jnp.asarray(cosine), me * here, here)
    sine_own = lax.dynamic_slice_in_dim(jnp.asarray(sine_table), me * here, here)

    grad_own = out_cotangent.reshape(own, width) * valid_own[:, None].astype(BF)

    def by_token(table):
        return jnp.asarray(np.broadcast_to(
            table.reshape(GROUPS, 1, here, -1), (GROUPS, batches, here, table.shape[1])).reshape(total, -1))

    hidden_all, query, key, values, latent = project(
        x_all.reshape(GROUPS, own, width), gain_attn[None], gain_latent[None], parts_head, small, expand_head,
        by_token(cosine), by_token(sine_table), batches)
    attn_part, attended, log_total = attend(seq_lengths, query, key, values, output_head, GROUPS)
    attn_part = attn_part.reshape(GROUPS, own, width)
    down_own = down_weight[0]
    cut = down_own.shape[0] * 3 // 160 * 16
    cuts = (0, cut, 2 * cut + cut // 48 * 16, down_own.shape[0])
    spans = [(first, last - first) for first, last in zip(cuts, cuts[1:])]
    attn_out, down_a = scatter16(attn_part, 2, dp=dp, span=spans[0], side=down_own)

    x_wide = x_own.astype(F32)
    middle = x_wide + attn_out
    normed_mix, unit_mix, factor_mix = norm_forward(middle, gain_mixer)
    hidden_mix = normed_mix.astype(BF)
    mix_all, down_b = gather16(hidden_mix, 3, dp=dp, span=spans[1], side=down_own)
    mix_all = mix_all.reshape(total, width)

    lane = jnp.arange(128)[None, :]
    pick = jnp.concatenate([lane == me, lane == me + GROUPS], axis=1).astype(F32)
    (out_part, rows, hidden, act, slope, result, share_hidden, share_act, share_slope, gates, grad_all,
     down_c) = mixture_forward(
        dp, batches, here, seq_lengths, pick, mix_all, routes_all, gate_full, up_full, router_full.T, share_full,
        down_a, down_b, spans[2], down_own, grad_own, 4)
    grad_all = grad_all.reshape(total, width)
    mix_part, grad_result, grad_gate_in, grad_up_in, grad_share_in, mixed = mixture_backward(
        here, pick, grad_all, gate_full, up_full, share_full, down_a, down_b, down_c, act, slope, result,
        share_act, share_slope, gates, out_part.reshape(GROUPS, own, width), 8)
    grad_down = product_lead(hidden, grad_result).astype(BF)
    grad_gate = product_lead(rows, grad_gate_in).astype(BF)
    grad_up = product_lead(rows, grad_up_in).astype(BF)
    mix_part, _, _, _ = lax.optimization_barrier((mix_part, grad_down, grad_gate, grad_up))
    mix_sum, grad_share = scatter_share(
        mix_part.reshape(GROUPS, own, width + 128), grad_share_in, share_hidden, mix_all, grad_all, share_full.shape, 5)
    layer_output = valid_own[:, None] * (middle + mixed)

    out_down = lax.psum_scatter(grad_down, "dp", scatter_dimension=0, tiled=True)
    out_gate = lax.psum_scatter(grad_gate, "dp", scatter_dimension=0, tiled=True)
    out_up = lax.psum_scatter(grad_up, "dp", scatter_dimension=0, tiled=True)
    grad_share, out_down, out_gate, out_up = lax.optimization_barrier((grad_share, out_down, out_gate, out_up))
    out_share = lax.psum_scatter(grad_share, "dp", scatter_dimension=0, tiled=False).astype(F32)

    mask_own = selected_experts(routes_own)
    soft_own = masked_softmax(product(hidden_mix, router_full), mask_own)
    grad_masked = (mix_sum[:, width : width + GROUPS] + mix_sum[:, width + GROUPS : width + 2 * GROUPS])
    grad_masked = grad_masked * valid_own[:, None]
    grad_logits = soft_own * (grad_masked - jnp.sum(grad_masked * soft_own, axis=1, keepdims=True))
    grad_logits = grad_logits.astype(BF)
    grad_mix = mix_sum[:, :width] + product_trail(grad_logits, router_full)
    grad_middle_norm, grad_gain_mixer = norm_backward(grad_mix, unit_mix, factor_mix, gain_mixer)
    grad_middle = grad_own.astype(F32) + grad_middle_norm

    grad_attn_all = gather16(grad_middle.astype(BF), 6).reshape(GROUPS, batches, here, width)
    back_part, grad_query, grad_output, grad_expand = attend_back(
        seq_lengths, grad_attn_all, query, key, values, latent, attended, log_total, output_head, parts_head,
        expand_head, jnp.asarray(cosine), jnp.asarray(sine_table), 640)
    grad_query_w = product_lead(hidden_all, grad_query.reshape(total, TILE)).astype(BF)
    parts_grad = jnp.concatenate(
        [grad_query_w[:, : QK_NOPE + ROPE], grad_expand.astype(BF).reshape(width, ROPE)], axis=1)
    back_sum, out_parts, out_output = returning(
        dp, back_part.reshape(GROUPS, own, back_part.shape[3]),
        parts_grad.reshape(dp, GROUPS, rows_w, TILE), grad_output.astype(BF).reshape(dp, rows_w, width), 7)
    out_query = out_parts[..., : QK_NOPE + ROPE].transpose(1, 0, 2).reshape(rows_w, -1)
    out_expand = out_parts[..., QK_NOPE + ROPE :].reshape(H, rows_l, QK_NOPE + V_DIM)
    out_expand = out_expand.transpose(1, 0, 2).reshape(rows_l, -1)

    x_normed, unit_attn, factor_attn = norm_forward(x_wide, gain_attn)
    hidden_own = x_normed.astype(BF)
    latent_own = product(hidden_own, latent_full)
    _, unit_latent, factor_latent = norm_forward(latent_own[:, :KV_RANK], gain_latent)
    grad_latent_in, grad_gain_latent = norm_backward(
        back_sum[:, width : width + KV_RANK], unit_latent, factor_latent, gain_latent
    )
    grad_rope = back_sum[:, width + KV_RANK : width + KV_RANK + ROPE].reshape(batches, here, ROPE)
    grad_rope = rotate(grad_rope, cosine_own, -sine_own).reshape(own, ROPE)
    grad_latent_raw = jnp.concatenate([grad_latent_in, grad_rope], axis=1).astype(BF)
    grad_hidden_attn = back_sum[:, :width] + product_trail(grad_latent_raw, latent_full)
    grad_input_norm, grad_gain_attn = norm_backward(grad_hidden_attn, unit_attn, factor_attn, gain_attn)
    grad_input = grad_middle + grad_input_norm

    latent_rows = grad_gain_latent.reshape(dp * GROUPS, rows_l)
    latent_rows = jnp.pad(latent_rows, ((0, 0), (0, rows_w - rows_l))).reshape(width, 1)
    tokens_side = jnp.concatenate([hidden_own, hidden_mix], axis=0)
    grads_side = jnp.concatenate(
        [jnp.pad(grad_latent_raw, ((0, 0), (0, 64))), jnp.pad(grad_logits, ((0, 0), (576, 640 - 592)))], axis=0)
    lane = jnp.arange(640)[None, :]
    small_grad = product_lead(tokens_side, grads_side)
    small_grad = small_grad + jnp.where(lane == 592, grad_gain_attn[:, None], 0.0)
    small_grad = small_grad + jnp.where(lane == 593, grad_gain_mixer[:, None], 0.0)
    small_grad = (small_grad + jnp.where(lane == 594, latent_rows, 0.0)).astype(BF)
    small_grad = small_grad.reshape(dp, GROUPS, rows_w, 640).swapaxes(0, 1).reshape(GROUPS, dp * rows_w, 640)
    small_sum = closing(dp, small_grad, 9)

    def as_input(v):
        return v.reshape(batches, 1, here, width)

    return (
        as_input(layer_output),
        as_input(grad_input),
        small_sum[:, 592],
        out_query,
        small_sum[:, :576],
        small_sum[:rows_l, 594],
        out_expand,
        out_output,
        small_sum[:, 593],
        small_sum[:, 576:592],
        out_gate.astype(F32)[None],
        out_up.astype(F32)[None],
        out_down.astype(F32)[None],
        out_share[:share_width].T,
        out_share[share_width : 2 * share_width].T,
        out_share[2 * share_width :],
    )


def solution(mesh):
    split = P(("dp", "expert"), None)
    line = P(("dp", "expert"))
    tokens = P(None, "dp", "expert", None)
    expert = P("expert", "dp", None)
    return jax.shard_map(
        per_device,
        mesh=mesh,
        in_specs=(
            tokens, tokens, P(None, "dp"), tokens, line, split, split, line, split, split, line, split,
            expert, expert, expert, P("dp", "expert"), P("dp", "expert"), P("expert", "dp"),
        ),
        out_specs=(
            tokens, tokens, line, split, split, line, split, split, line, split,
            expert, expert, expert, P("dp", "expert"), P("dp", "expert"), P("expert", "dp"),
        ),
        check_vma=False,
    )
```

```python
import functools
import jax
import jax.numpy as jnp
import numpy as np
from jax import lax
from jax.experimental import pallas as pl
from jax.experimental.pallas import tpu as pltpu
from jax.sharding import PartitionSpec as P

MESH = pl.DeviceIdType.MESH
NZ = 4
NE = 16


def place():
    me = lax.axis_index("expert")
    z = me // 4
    x = (me // 2) % 2
    c = me % 2
    return me, z, x, c, me + 1 - 2 * c, me + 2 - 4 * x


def enter(me, z, core, side, dp=1):
    barrier = pltpu.get_barrier_semaphore()
    plane = lax.axis_index("dp")
    for r in range(1, dp):
        pl.semaphore_signal(barrier, inc=1, device_id={"dp": (plane + r) % dp}, device_id_type=MESH)
    for other in (core, side):
        pl.semaphore_signal(barrier, inc=1, device_id={"expert": other}, device_id_type=MESH)

    @pl.when(z < NZ - 1)
    def _():
        pl.semaphore_signal(barrier, inc=1, device_id={"expert": me + 4}, device_id_type=MESH)

    @pl.when(z > 0)
    def _():
        pl.semaphore_signal(barrier, inc=1, device_id={"expert": me - 4}, device_id_type=MESH)

    pl.semaphore_wait(barrier, dp + 1 + (z < NZ - 1).astype(jnp.int32) + (z > 0).astype(jnp.int32))


class Spread:
    def __init__(self, dp, src, out, sems):
        self.dp, self.src, self.out = dp, src, out
        self.own, self.send, self.recv = sems
        self.plane = lax.axis_index("dp")

    @staticmethod
    def scratch(dp):
        dma = pltpu.SemaphoreType.DMA
        return [dma, dma((dp,)), dma((dp,))]

    def copy(self, r):
        return pltpu.make_async_remote_copy(
            src_ref=self.src, dst_ref=self.out.at[self.plane], send_sem=self.send.at[r], recv_sem=self.recv.at[r],
            device_id={"dp": (self.plane + r) % self.dp}, device_id_type=MESH)

    def arrival(self, r):
        p = (self.plane - r + self.dp) % self.dp
        return pltpu.make_async_remote_copy(
            src_ref=self.src, dst_ref=self.out.at[p], send_sem=self.send.at[r], recv_sem=self.recv.at[r],
            device_id={"dp": p}, device_id_type=MESH)

    def start(self):
        for r in range(1, self.dp):
            self.copy(r).start()
        self.kept = pltpu.make_async_copy(self.src, self.out.at[self.plane], self.own)
        self.kept.start()

    def finish(self):
        self.kept.wait()
        for r in range(1, self.dp):
            self.arrival(r).wait_recv()
            self.copy(r).wait_send()


class Swap:
    def __init__(self, dp, src, out, sems):
        self.dp, self.src, self.out = dp, src, out
        self.send, self.recv = sems
        self.plane = lax.axis_index("dp")

    @staticmethod
    def scratch(dp):
        dma = pltpu.SemaphoreType.DMA
        return [dma((dp,)), dma((dp,))]

    def copy(self, r):
        to = (self.plane + r) % self.dp
        return pltpu.make_async_remote_copy(
            src_ref=self.src.at[to], dst_ref=self.out.at[r - 1], send_sem=self.send.at[r], recv_sem=self.recv.at[r],
            device_id={"dp": to}, device_id_type=MESH)

    def start(self):
        for r in range(1, self.dp):
            self.copy(r).start()

    def finish(self):
        for r in range(1, self.dp):
            self.copy(r).wait_recv()
            self.copy(r).wait_send()


def side_job(dp, span, src, out, sems):
    if span is None:
        return Swap(dp, src, out, sems)
    return Spread(dp, src.at[pl.ds(span[0], span[1])], out, sems)


def side_shape(dp, span, side):
    if span is None:
        return jax.ShapeDtypeStruct((dp - 1,) + side.shape[1:], side.dtype)
    return jax.ShapeDtypeStruct((dp, span[1], side.shape[1]), side.dtype)


def side_scratch(dp, span):
    return (Swap if span is None else Spread).scratch(dp)


def enter_all(me, plane, dp):
    barrier = pltpu.get_barrier_semaphore()
    for r in range(1, NE):
        pl.semaphore_signal(
            barrier, inc=1, device_id={"expert": (me + r) % NE}, device_id_type=MESH)
    for r in range(1, dp):
        pl.semaphore_signal(
            barrier, inc=1, device_id={"dp": (plane + r) % dp}, device_id_type=MESH)
    pl.semaphore_wait(barrier, NE - 1 + dp - 1)


class Gather:
    def __init__(self, src, out, chunks, sems, view=lambda ref, b: ref.at[b]):
        self.src, self.out, self.chunks, self.view = src, out, chunks, view
        self.rows = src.shape[0] // chunks
        (self.own_sem, self.us, self.ur, self.ds, self.dr, self.bus, self.bur, self.bds, self.bdr,
         self.xs, self.xr, self.cs, self.cr) = sems
        self.me, self.z, self.x, self.c, self.core, self.side = place()

    COUNT = 13

    @staticmethod
    def scratch(chunks):
        dma = pltpu.SemaphoreType.DMA
        return [dma] + [dma((4, chunks))] * 8 + [dma((7, chunks))] * 2 + [dma((14, chunks))] * 2

    def alt(self, k):
        return k >= (self.chunks + 1) // 2

    def order(self):
        return range(self.chunks - 1, -1, -1)

    def copy(self, block, k, src, send, recv, to):
        src_ref = self.src if src is None else self.view(self.out, src)
        dst_ref = self.view(self.out, block)
        if self.chunks > 1:
            part = pl.ds(k * self.rows, self.rows)
            src_ref, dst_ref = src_ref.at[part], dst_ref.at[part]
        return pltpu.make_async_remote_copy(
            src_ref=src_ref,
            dst_ref=dst_ref,
            send_sem=send, recv_sem=recv,
            device_id={"expert": to}, device_id_type=MESH,
        )

    def up(self, k, s, src=None):
        return self.copy(self.me - 4 * s, k, src, self.us.at[s, k], self.ur.at[s, k], self.me + 4)

    def down(self, k, s, src=None):
        return self.copy(self.me + 4 * s, k, src, self.ds.at[s, k], self.dr.at[s, k], self.me - 4)

    def up_b(self, k, s):
        b = self.side - 4 * s
        return self.copy(b, k, b, self.bus.at[s, k], self.bur.at[s, k], self.me + 4)

    def down_b(self, k, s):
        b = self.side + 4 * s
        return self.copy(b, k, b, self.bds.at[s, k], self.bdr.at[s, k], self.me - 4)

    def across(self, k, slot, block, src=None):
        return self.copy(block, k, src, self.xs.at[slot, k], self.xr.at[slot, k], self.side)

    def over(self, k, slot, block, src=None):
        return self.copy(block, k, src, self.cs.at[slot, k], self.cr.at[slot, k], self.core)

    def arrived(self, b, k, sems, s):
        return self.copy(b, k, b, sems[0].at[s - 1, k], sems[1].at[s - 1, k], self.side)

    def shift(self, base, slot):
        return base - 4 * slot if slot <= 3 else base + 4 * (slot - 3)

    def core_block(self, slot):
        if slot < 7:
            return self.shift(self.core, slot)
        return self.shift(self.core + 2 - 4 * self.x, slot - 7)

    def has(self, slot):
        slot = slot % 7
        if slot == 0:
            return self.z >= 0
        return self.z >= slot if slot <= 3 else self.z + (slot - 3) <= NZ - 1

    def crosses(self, k, slot):
        if slot == 0 or not self.alt(k):
            return self.has(slot)
        return self.z > slot if slot <= 3 else self.z + (slot - 3) < NZ - 1

    def start(self):
        z, me = self.z, self.me
        self.own = pltpu.make_async_copy(self.src, self.view(self.out, me), self.own_sem)
        self.own.start()
        for k in self.order():
            self.across(k, 0, me).start()

            @pl.when(z < NZ - 1)
            def _():
                self.up(k, 0).start()

            @pl.when(z > 0)
            def _():
                self.down(k, 0).start()

            self.over(k, 0, me).start()

    def line(self, k, s):
        z, me = self.z, self.me

        @pl.when(z >= s)
        def _():
            b = me - 4 * s
            self.arrived(b, k, (self.us, self.ur), s).wait_recv()

            @pl.when(self.crosses(k, s))
            def _():
                self.across(k, s, b, b).start()

            @pl.when(z < NZ - 1)
            def _():
                self.up(k, s, b).start()

            self.over(k, s, b, b).start()

        @pl.when(z + s <= NZ - 1)
        def _():
            b = me + 4 * s
            self.arrived(b, k, (self.ds, self.dr), s).wait_recv()

            @pl.when(self.crosses(k, 3 + s))
            def _():
                self.across(k, 3 + s, b, b).start()

            @pl.when(z > 0)
            def _():
                self.down(k, s, b).start()

            self.over(k, 3 + s, b, b).start()

    def line_b(self, k, s):
        z = self.z

        @pl.when(z == s)
        def _():
            b = self.side - 4 * s
            self.arrived(b, k, (self.bus, self.bur), s).wait_recv()

            @pl.when(z < NZ - 1)
            def _():
                self.up_b(k, s).start()

            self.over(k, 7 + s, b, b).start()

        @pl.when(z + s == NZ - 1)
        def _():
            b = self.side + 4 * s
            self.arrived(b, k, (self.bds, self.bdr), s).wait_recv()

            @pl.when(z > 0)
            def _():
                self.down_b(k, s).start()

            self.over(k, 10 + s, b, b).start()

    def from_side(self, k, slot):
        @pl.when(self.crosses(k, slot))
        def _():
            b = self.shift(self.side, slot)
            self.across(k, slot, b, b).wait_recv()
            if slot == 0 and self.alt(k):
                @pl.when(self.z == 0)
                def _():
                    self.up_b(k, 0).start()

                @pl.when(self.z == NZ - 1)
                def _():
                    self.down_b(k, 0).start()

            self.over(k, 7 + slot, b, b).start()

    def round(self, s):
        if s < NZ:
            for k in self.order():
                self.line(k, s)
        for k in self.order():
            for slot in ((0,) if s == 1 else (s - 1, s + 2)):
                self.from_side(k, slot)
        if s > 1:
            for k in self.order():
                if self.alt(k):
                    self.line_b(k, s - 1)

    def finish(self):
        z = self.z
        self.own.wait()
        for k in self.order():
            for slot in range(14):
                @pl.when(self.has(slot))
                def _():
                    b = self.core_block(slot)
                    self.over(k, slot, b, b).wait_recv()
                    self.over(k, slot, b, b).wait_send()
            for slot in range(7):
                @pl.when(self.crosses(k, slot))
                def _():
                    self.across(k, slot, self.me).wait_send()
            for s in range(NZ - 1):
                @pl.when((z >= s) & (z < NZ - 1))
                def _():
                    self.up(k, s).wait_send()

                @pl.when((z + s <= NZ - 1) & (z > 0))
                def _():
                    self.down(k, s).wait_send()

                if self.alt(k):
                    @pl.when(z == s)
                    def _():
                        self.up_b(k, s).wait_send()

                    @pl.when(z + s == NZ - 1)
                    def _():
                        self.down_b(k, s).wait_send()


def gather_kernel(chunks, dp, span, extra, x_ref, *refs):
    job = None
    ng = Gather.COUNT
    if not extra:
        o_ref, *sems = refs
    else:
        src, o_ref, out, *sems = refs
        job = side_job(dp, span, src, out, sems[ng:])
    g = Gather(x_ref, o_ref, chunks, sems[:ng])
    enter(g.me, g.z, g.core, g.side, 1 if job is None else dp)
    g.start()
    if job is not None:
        job.start()
    for s in range(1, NZ + 1):
        g.round(s)
    g.finish()
    if job is not None:
        job.finish()


COST = pl.CostEstimate(flops=0, bytes_accessed=4_000_000, transcendentals=0)
ANY = pl.BlockSpec(memory_space=pl.ANY)


def gather16(v, cid, chunks=2, dp=1, span=None, side=None):
    rows, width = v.shape
    extra = side is not None
    out = pl.pallas_call(
        functools.partial(gather_kernel, chunks, dp, span, extra),
        out_shape=(jax.ShapeDtypeStruct((NE, rows, width), v.dtype),)
        + ((side_shape(dp, span, side),) if extra else ()),
        in_specs=[ANY] * (2 if extra else 1),
        out_specs=(ANY,) * (2 if extra else 1),
        scratch_shapes=Gather.scratch(chunks) + (side_scratch(dp, span) if extra else []),
        compiler_params=pltpu.CompilerParams(collective_id=cid, has_side_effects=True),
        cost_estimate=COST,
        name="gather16",
    )(*((v, side) if extra else (v,)))
    return out if extra else out[0]


def opening_kernel(dp, chunks, x_ref, small_ref, parts_ref, out_ref,
                   x_all, small_all, parts_head, out_head, small_dp, parts_dp, out_dp, *sems):
    ng = Gather.COUNT
    gx = Gather(x_ref, x_all, chunks, sems[:ng])
    gs = Gather(small_dp, small_all, 1, sems[ng:2 * ng], lambda ref, b: ref.at[:, b])
    loc, ys, yr, ps, pr, os_, or_, pl_sem, ol_sem = sems[2 * ng:]
    me = gx.me
    plane = lax.axis_index("dp")
    enter_all(me, plane, dp)
    pairs = ((small_ref, small_dp.at[plane]), (parts_ref, parts_dp.at[plane]),
             (out_ref, out_dp.at[plane]))

    def lift(i, r):
        src, dst = pairs[i]
        return pltpu.make_async_remote_copy(
            src_ref=src, dst_ref=dst, send_sem=ys.at[i, r], recv_sem=yr.at[i, r],
            device_id={"dp": (plane + r) % dp}, device_id_type=MESH)

    def landed(i, r):
        p = (plane - r + dp) % dp
        dst = (small_dp.at[p], parts_dp.at[p], out_dp.at[p])[i]
        return pltpu.make_async_remote_copy(
            src_ref=dst, dst_ref=dst, send_sem=ys.at[i, r], recv_sem=yr.at[i, r],
            device_id={"dp": p}, device_id_type=MESH)

    def kept(i):
        src, dst = pairs[i]
        return pltpu.make_async_copy(src, dst, loc.at[i])

    for i in range(3):
        for r in range(1, dp):
            lift(i, r).start()
        kept(i).start()
    gx.start()
    gx.round(1)

    kept(0).wait()
    for r in range(1, dp):
        landed(0, r).wait_recv()
    gs.start()

    def part(r):
        h = (me + r) % NE
        return pltpu.make_async_remote_copy(
            src_ref=parts_dp.at[:, h], dst_ref=parts_head.at[:, me],
            send_sem=ps.at[r], recv_sem=pr.at[r],
            device_id={"expert": h}, device_id_type=MESH)

    def part_in(r):
        e = (me - r + NE) % NE
        return pltpu.make_async_remote_copy(
            src_ref=parts_head.at[:, e], dst_ref=parts_head.at[:, e],
            send_sem=ps.at[r], recv_sem=pr.at[r],
            device_id={"expert": e}, device_id_type=MESH)

    def part_kept():
        return pltpu.make_async_copy(parts_dp.at[:, me], parts_head.at[:, me], pl_sem)

    kept(1).wait()
    for r in range(1, dp):
        landed(1, r).wait_recv()
    for r in range(1, NE):
        part(r).start()
    part_kept().start()
    gx.round(2)

    def row(d):
        b = NE * d + me
        return pltpu.make_async_remote_copy(
            src_ref=out_dp.at[d], dst_ref=out_head.at[b % dp],
            send_sem=os_.at[d], recv_sem=or_.at[b % dp],
            device_id={"expert": b // dp}, device_id_type=MESH)

    def row_kept(d):
        b = NE * d + me
        return pltpu.make_async_copy(out_dp.at[d], out_head.at[b % dp], ol_sem.at[d])

    kept(2).wait()
    for r in range(1, dp):
        landed(2, r).wait_recv()
    for d in range(dp):
        home = (NE * d + me) // dp

        @pl.when(home != me)
        def _():
            row(d).start()

        @pl.when(home == me)
        def _():
            row_kept(d).start()

    gs.round(1)
    gx.round(3)
    gs.round(2)
    gx.round(4)
    gs.round(3)
    gs.round(4)

    def row_in(j):
        return pltpu.make_async_remote_copy(
            src_ref=out_head.at[j], dst_ref=out_head.at[j], send_sem=os_.at[j], recv_sem=or_.at[j],
            device_id={"expert": gx.core}, device_id_type=MESH)

    for r in range(1, NE):
        part_in(r).wait_recv()
        part(r).wait_send()
    part_kept().wait()
    for j in range(dp):
        @pl.when((dp * me + j) % NE != me)
        def _():
            row_in(j).wait_recv()
    for d in range(dp):
        home = (NE * d + me) // dp

        @pl.when(home != me)
        def _():
            row(d).wait_send()

        @pl.when(home == me)
        def _():
            row_kept(d).wait()
    for i in range(3):
        for r in range(1, dp):
            lift(i, r).wait_send()
    gx.finish()
    gs.finish()


def opening(dp, x, small, parts, out, cid, chunks=2):
    dma = pltpu.SemaphoreType.DMA
    rows, ws = small.shape
    bf = x.dtype
    wo = out.shape[1]
    shape = jax.ShapeDtypeStruct
    res = pl.pallas_call(
        functools.partial(opening_kernel, dp, chunks),
        out_shape=(
            shape((NE,) + x.shape, bf), shape((dp, NE, rows, ws), bf), shape((dp, NE) + parts.shape[1:], bf),
            shape((dp, rows, wo), bf),
            shape((dp, rows, ws), bf), shape((dp,) + parts.shape, bf), shape((dp, rows, wo), bf),
        ),
        in_specs=[ANY] * 4,
        out_specs=[ANY] * 7,
        scratch_shapes=Gather.scratch(chunks) + Gather.scratch(1) + [
            dma((3,)), dma((3, dp)), dma((3, dp)), dma((NE,)), dma((NE,)), dma((dp,)), dma((dp,)), dma, dma((dp,))],
        compiler_params=pltpu.CompilerParams(collective_id=cid, has_side_effects=True),
        cost_estimate=COST,
        name="opening",
    )(x, small, parts, out)
    return res[:4]


def order(z, i):
    a, b = (3, 2, 1, 0)[i], (3, 2, 0, 1)[i]
    return jnp.where(z == 0, a, jnp.where(z == 1, b, jnp.where(z == 2, 3 - b, 3 - a)))


class Scatter:
    COUNT = 14

    def __init__(self, p_ref, o_ref, chunks, scratch):
        self.p, self.o, self.chunks = p_ref, o_ref, chunks
        (self.cbuf, self.own, self.xbuf, self.ubuf, self.dbuf, self.ld, self.cs, self.cr, self.xs, self.xr,
         self.us, self.ur, self.ds, self.dr) = scratch
        self.rows = o_ref.shape[0] // chunks
        self.me, self.z, self.x, self.c, self.core, self.side = place()

    @staticmethod
    def scratch(rows, width, chunks, bf):
        dma = pltpu.SemaphoreType.DMA
        return [pltpu.VMEM((n, rows, width), bf) for n in (8, 8, 4, 4, 4)] + [
            dma((8,)), dma((8, chunks)), dma((8, chunks))] + [dma((4, chunks))] * 6

    def rng(self, k):
        return pl.ds(k * self.rows, self.rows)

    def column(self, i, j):
        return 4 * order(self.z, i) + 2 * jnp.where(j == 0, 1 - self.x, self.x)

    def remote(self, src, dst, send, recv, to):
        return pltpu.make_async_remote_copy(
            src_ref=src, dst_ref=dst, send_sem=send, recv_sem=recv,
            device_id={"expert": to}, device_id_type=MESH)

    def over(self, i, j, k):
        n = 2 * i + j
        return self.remote(
            self.p.at[self.column(i, j) + 1 - self.c, self.rng(k)], self.cbuf.at[n, self.rng(k)],
            self.cs.at[n, k], self.cr.at[n, k], self.core)

    def load(self, i, j):
        n = 2 * i + j
        return pltpu.make_async_copy(self.p.at[self.column(i, j) + self.c], self.own.at[n], self.ld.at[n])

    def across(self, i, k):
        return self.remote(self.own.at[2 * i, self.rng(k)], self.xbuf.at[i, self.rng(k)],
                           self.xs.at[i, k], self.xr.at[i, k], self.side)

    def up(self, t, i, k):
        return self.remote(self.own.at[2 * i + 1, self.rng(k)], self.ubuf.at[t, self.rng(k)],
                           self.us.at[t, k], self.ur.at[t, k], self.me + 4)

    def down(self, t, i, k):
        return self.remote(self.own.at[2 * i + 1, self.rng(k)], self.dbuf.at[t, self.rng(k)],
                           self.ds.at[t, k], self.dr.at[t, k], self.me - 4)

    def start(self):
        for i in range(NZ):
            for j in range(2):
                self.load(i, j).start()
                for k in range(self.chunks):
                    self.over(i, j, k).start()

    def first(self, i):
        f32 = jnp.float32
        self.load(i, 0).wait()
        for k in range(self.chunks):
            self.over(i, 0, k).wait_recv()
            s = self.rng(k)
            self.own[2 * i, s] = (
                self.own[2 * i, s].astype(f32) + self.cbuf[2 * i, s].astype(f32)).astype(self.own.dtype)
            self.across(i, k).start()

    def second(self, i):
        f32 = jnp.float32
        z, own, o = self.z, self.own, self.o
        t = order(z, i)
        self.load(i, 1).wait()
        for k in range(self.chunks):
            s = self.rng(k)
            self.over(i, 1, k).wait_recv()
            self.across(i, k).wait_recv()

            def base():
                return (own[2 * i + 1, s].astype(f32) + self.cbuf[2 * i + 1, s].astype(f32)
                        + self.xbuf[i, s].astype(f32))

            if i < NZ - 1:
                @pl.when(t > z)
                def _():
                    @pl.when(z > 0)
                    def _():
                        self.up(t, i, k).wait_recv()
                        own[2 * i + 1, s] = (base() + self.ubuf[t, s].astype(f32)).astype(own.dtype)

                    @pl.when(z == 0)
                    def _():
                        own[2 * i + 1, s] = base().astype(own.dtype)

                    self.up(t, i, k).start()

                @pl.when(t < z)
                def _():
                    @pl.when(z < NZ - 1)
                    def _():
                        self.down(t, i, k).wait_recv()
                        own[2 * i + 1, s] = (base() + self.dbuf[t, s].astype(f32)).astype(own.dtype)

                    @pl.when(z == NZ - 1)
                    def _():
                        own[2 * i + 1, s] = base().astype(own.dtype)

                    self.down(t, i, k).start()
            else:
                @pl.when(z > 0)
                def _():
                    self.up(t, i, k).wait_recv()

                @pl.when(z < NZ - 1)
                def _():
                    self.down(t, i, k).wait_recv()

                @pl.when((z > 0) & (z < NZ - 1))
                def _():
                    o[s] = (base() + self.ubuf[t, s].astype(f32) + self.dbuf[t, s].astype(f32)).astype(o.dtype)

                @pl.when(z == 0)
                def _():
                    o[s] = (base() + self.dbuf[t, s].astype(f32)).astype(o.dtype)

                @pl.when(z == NZ - 1)
                def _():
                    o[s] = (base() + self.ubuf[t, s].astype(f32)).astype(o.dtype)

    def run(self, between=lambda: None):
        self.first(0)
        for i in range(NZ):
            if i + 1 < NZ:
                self.first(i + 1)
            between()
            self.second(i)
            between()

    def finish(self):
        z = self.z
        for k in range(self.chunks):
            for i in range(NZ):
                self.across(i, k).wait_send()
                for j in range(2):
                    self.over(i, j, k).wait_send()
                if i < NZ - 1:
                    t = order(z, i)

                    @pl.when(t > z)
                    def _():
                        self.up(t, i, k).wait_send()

                    @pl.when(t < z)
                    def _():
                        self.down(t, i, k).wait_send()


def scatter_kernel(chunks, dp, span, extra, p_ref, *refs):
    job = None
    ns = Scatter.COUNT
    if not extra:
        o_ref, *scratch = refs
    else:
        src, o_ref, out, *scratch = refs
        job = side_job(dp, span, src, out, scratch[ns:])
    s = Scatter(p_ref, o_ref, chunks, scratch[:ns])
    enter(s.me, s.z, s.core, s.side, 1 if job is None else dp)
    s.start()
    if job is not None:
        job.start()
    s.run()
    s.finish()
    if job is not None:
        job.finish()


VMEM = pl.BlockSpec(memory_space=pltpu.VMEM)


def scatter16(p, cid, chunks=2, dp=1, span=None, side=None):
    _, rows, width = p.shape
    extra = side is not None
    out = pl.pallas_call(
        functools.partial(scatter_kernel, chunks, dp, span, extra),
        out_shape=(jax.ShapeDtypeStruct((rows, width), jnp.float32),)
        + ((side_shape(dp, span, side),) if extra else ()),
        in_specs=[ANY] * (2 if extra else 1),
        out_specs=(VMEM,) + ((ANY,) if extra else ()),
        scratch_shapes=Scatter.scratch(rows, width, chunks, p.dtype) + (side_scratch(dp, span) if extra else []),
        compiler_params=pltpu.CompilerParams(
            collective_id=cid, has_side_effects=True, vmem_limit_bytes=60 * 1024 * 1024),
        cost_estimate=COST,
        name="scatter16",
    )(*((p, side) if extra else (p,)))
    return out if extra else out[0]


def return_kernel(dp, chunks, p_ref, parts_ref, rows_ref, o_ref, parts_far, rows_far, *scratch):
    ns = Scatter.COUNT
    s = Scatter(p_ref, o_ref, chunks, scratch[:ns])
    swap = Swap(dp, parts_ref, parts_far, scratch[ns:ns + 2])
    rs, rr = scratch[ns + 2:]
    plane = lax.axis_index("dp")
    keeper = s.me * dp // NE
    enter(s.me, s.z, s.core, s.side, dp)

    def row(r):
        return pltpu.make_async_remote_copy(
            src_ref=rows_ref, dst_ref=rows_far.at[r - 1], send_sem=rs.at[r], recv_sem=rr.at[r],
            device_id={"dp": (plane + r) % dp}, device_id_type=MESH)

    s.start()
    swap.start()
    for r in range(1, dp):
        @pl.when((plane + r) % dp == keeper)
        def _():
            row(r).start()
    s.run()
    s.finish()
    swap.finish()
    for r in range(1, dp):
        @pl.when((plane + r) % dp == keeper)
        def _():
            row(r).wait_send()

        @pl.when(plane == keeper)
        def _():
            row(r).wait_recv()


def returning(dp, p, parts, rows, cid, chunks=2):
    dma = pltpu.SemaphoreType.DMA
    _, n, width = p.shape
    shape = jax.ShapeDtypeStruct
    return pl.pallas_call(
        functools.partial(return_kernel, dp, chunks),
        out_shape=(
            shape((n, width), jnp.float32), shape((dp - 1,) + parts.shape[1:], parts.dtype),
            shape((dp - 1,) + rows.shape, rows.dtype)),
        in_specs=[ANY] * 3,
        out_specs=[VMEM, ANY, ANY],
        scratch_shapes=Scatter.scratch(n, width, chunks, p.dtype) + [dma((dp,))] * 4,
        compiler_params=pltpu.CompilerParams(
            collective_id=cid, has_side_effects=True, vmem_limit_bytes=60 * 1024 * 1024),
        cost_estimate=COST,
        name="returning",
    )(p, parts, rows)


def closing_kernel(dp, p_ref, parts_ref, rows_ref, o_ref, far_ref, query_ref, expand_ref, output_ref,
                   parts_in, row_in, *scratch):
    ns = Scatter.COUNT
    s = Scatter(p_ref, o_ref, 1, scratch[:ns])
    ys, yr, ps, pr, kept_sem, rs, rr = scratch[ns:]
    me = s.me
    plane = lax.axis_index("dp")
    rows = o_ref.shape[0] // dp
    enter_all(me, plane, dp)

    def lift(r):
        to = (plane + r) % dp
        return pltpu.make_async_remote_copy(
            src_ref=o_ref.at[pl.ds(pl.multiple_of(to * rows, 16), rows)], dst_ref=far_ref.at[r - 1],
            send_sem=ys.at[r], recv_sem=yr.at[r],
            device_id={"dp": to}, device_id_type=MESH)

    def part(r):
        e = (me + r) % NE
        return pltpu.make_async_remote_copy(
            src_ref=parts_ref.at[e], dst_ref=parts_in.at[me], send_sem=ps.at[r], recv_sem=pr.at[r],
            device_id={"expert": e}, device_id_type=MESH)

    def part_in(r):
        h = (me - r + NE) % NE
        return pltpu.make_async_remote_copy(
            src_ref=parts_in.at[h], dst_ref=parts_in.at[h], send_sem=ps.at[r], recv_sem=pr.at[r],
            device_id={"expert": h}, device_id_type=MESH)

    def part_kept():
        return pltpu.make_async_copy(parts_ref.at[me], parts_in.at[me], kept_sem.at[0])

    keeper = plane == me * dp // NE
    source = (NE * plane + me) // dp

    def row(j):
        return pltpu.make_async_remote_copy(
            src_ref=rows_ref.at[j], dst_ref=row_in, send_sem=rs.at[j], recv_sem=rr,
            device_id={"expert": (dp * me + j) % NE}, device_id_type=MESH)

    def row_kept(j):
        return pltpu.make_async_copy(rows_ref.at[j], row_in, kept_sem.at[1])

    s.start()
    for r in range(1, NE):
        part(r).start()
    part_kept().start()
    for j in range(dp):
        home = (dp * me + j) % NE

        @pl.when(keeper & (home != me))
        def _():
            row(j).start()

        @pl.when(keeper & (home == me))
        def _():
            row_kept(j).start()
    s.run()
    for r in range(1, dp):
        lift(r).start()
    for r in range(1, NE):
        part_in(r).wait_recv()
    part_kept().wait()
    rows_l = expand_ref.shape[0]
    f32 = jnp.float32
    for h in range(0, NE, 2):
        pair = [parts_in[h + i].astype(f32) for i in range(2)]
        query_ref[:, h * 192:(h + 2) * 192] = jnp.concatenate([v[:, :192] for v in pair], axis=1)
        for i, v in enumerate(pair):
            expand_ref[:, (h + i) * 256:(h + i + 1) * 256] = jnp.concatenate(
                [v[c * rows_l:(c + 1) * rows_l, 192:] for c in range(4)], axis=1)

    @pl.when(source != me)
    def _():
        row(0).wait_recv()

    for j in range(dp):
        home = (dp * me + j) % NE

        @pl.when(keeper & (home != me))
        def _():
            row(j).wait_send()

        @pl.when(keeper & (home == me))
        def _():
            row_kept(j).wait()
    output_ref[...] = row_in[...].astype(f32)
    for r in range(1, NE):
        part(r).wait_send()
    s.finish()
    for r in range(1, dp):
        lift(r).wait_recv()
        lift(r).wait_send()


def closing(dp, p, parts, rows, rows_l, cid):
    dma = pltpu.SemaphoreType.DMA
    _, n, width = p.shape
    shape = jax.ShapeDtypeStruct
    rows_w = parts.shape[1]
    near, far, query, expand, output = pl.pallas_call(
        functools.partial(closing_kernel, dp),
        out_shape=(
            shape((n, width), p.dtype), shape((dp - 1, n // dp, width), p.dtype),
            shape((rows_w, NE * 192), jnp.float32), shape((rows_l, NE * 256), jnp.float32),
            shape(rows.shape[1:], jnp.float32)),
        in_specs=[ANY] * 3,
        out_specs=[VMEM] * 5,
        scratch_shapes=[pltpu.VMEM(parts.shape, parts.dtype), pltpu.VMEM(rows.shape[1:], rows.dtype)]
        + Scatter.scratch(n, width, 1, p.dtype)
        + [dma((dp,)), dma((dp,)), dma((NE,)), dma((NE,)), dma((2,)), dma((dp,)), dma],
        compiler_params=pltpu.CompilerParams(
            collective_id=cid, has_side_effects=True, vmem_limit_bytes=60 * 1024 * 1024),
        cost_estimate=COST,
        name="closing",
    )(p, parts, rows)
    own = lax.dynamic_slice_in_dim(near, lax.axis_index("dp") * (n // dp), n // dp).astype(jnp.float32)
    return own + jnp.sum(far.astype(jnp.float32), axis=0), query, expand, output
BF = jnp.bfloat16
F32 = jnp.float32


def mm(a, b):
    return jnp.dot(a, b, preferred_element_type=F32)


def mm_t(a, b):
    return lax.dot_general(a, b, (((1,), (1,)), ((), ())), preferred_element_type=F32)


def silu_pair(gate_in):
    sigmoid = 1.0 / (1.0 + jnp.exp(-gate_in))
    return (gate_in * sigmoid, sigmoid * (1.0 + gate_in * (1.0 - sigmoid)))


TILE = 256
WIDE = 512
SHARE = 176


def down_copies(parts, out, sem, which):
    dp = parts[0].shape[0]
    sizes = [part.shape[1] for part in parts]
    rows, first = sum(sizes), sum(sizes[:which])
    return [
        pltpu.make_async_copy(
            parts[which].at[d], out.at[pl.ds(d * rows + first, sizes[which])], sem.at[len(parts) * d + which])
        for d in range(dp)
    ]


def share_copies(share_ref, fan, down, sem):
    dp, rows, w = share_ref.shape
    n = rows // 3
    copies = []
    for d in range(dp):
        cols = pl.ds(d * w, w)
        for i, (dst, first) in enumerate(((fan, 0), (fan, TILE), (down, 0))):
            copies.append(pltpu.make_async_copy(
                share_ref.at[d, pl.ds(i * n, n)], dst.at[pl.ds(first, n), cols], sem.at[3 * d + i]))
    return copies


def share_blank(fan, down):
    pad = jnp.zeros((TILE - SHARE, fan.shape[1]), BF)
    fan[SHARE:TILE] = pad
    fan[TILE + SHARE:] = pad
    down[SHARE:] = pad


def mine_of(routes_ref, pick_ref):
    tokens = routes_ref.shape[0]
    lane16 = lax.broadcasted_iota(jnp.int32, (tokens, 16), 1)
    mask = lane16 < 0
    for k in range(routes_ref.shape[1]):
        mask = mask | (lane16 == routes_ref[:, k:k + 1])
    mine = jnp.sum(jnp.where(mask, pick_ref[:, :16], 0.0), axis=1, keepdims=True)
    return mask, mine


def valid_of(len_ref, first_device, tokens, batches, here):
    n = lax.broadcasted_iota(jnp.int32, (tokens, 1), 0)
    device = n // (batches * here)
    batch = (n // here) % batches
    position = (first_device + device) * here + n % here
    length = jnp.zeros((tokens, 1), jnp.int32)
    for b in range(batches):
        length = jnp.where(batch == b, len_ref[b], length)
    return (position < length).astype(F32)


def one_hots(taken, groups, slots, here):
    r = lax.broadcasted_iota(jnp.int32, (256, 256), 0)
    c = lax.broadcasted_iota(jnp.int32, (256, 256), 1)
    same = r // here == c // here
    before = (same & (c < r)).astype(BF)
    after = (same & (r < c)).astype(BF)
    base_c = (lax.broadcasted_iota(jnp.int32, (256, slots), 0) // here * 32).astype(F32)
    base_r = (lax.broadcasted_iota(jnp.int32, (slots, 256), 1) // here * 32).astype(F32)
    lane = lax.broadcasted_iota(jnp.int32, (256, slots), 1).astype(F32)
    row = lax.broadcasted_iota(jnp.int32, (slots, 256), 0).astype(F32)
    ones = jnp.ones((256, slots), BF)
    to_slot, to_token = [], []
    for g in range(groups):
        t = jnp.broadcast_to(taken[g * 256:(g + 1) * 256], (256, slots))
        low = t.astype(BF)
        place_c = mm(before, low) + base_c
        place_r = mm_lead(low, after) + base_r
        taken_r = mm_lead(low, (r == c).astype(BF))
        to_token.append(jnp.where((place_c == lane) & (t > 0.5), 1.0, 0.0).astype(BF))
        to_slot.append(jnp.where((place_r == row) & (taken_r > 0.5), 1.0, 0.0).astype(BF))
    return to_slot, to_token


def mm_lead(a, b):
    return lax.dot_general(a, b, (((0,), (0,)), ((), ())), preferred_element_type=F32)


def lanes(j):
    return pl.ds(pl.multiple_of(j * WIDE, WIDE), WIDE)


def over_columns(total, body):
    def step(j, _):
        body(pl.multiple_of(j * WIDE, WIDE), WIDE)
        return 0

    lax.fori_loop(0, total // WIDE, step, 0)
    if total % WIDE:
        body(total // WIDE * WIDE, total % WIDE)


def forward_kernel(chunks, dp, span, batches, here, len_ref, pick_ref, mix_ref, routes_ref, wg_ref, wu_ref, router_ref,
                   share_ref, wda_ref, wdb_ref, down_ref, dy_ref,
                   out_ref, rows_ref, hid_ref, act_ref, slo_ref, eo_ref, sh_ref, sact_ref, sslo_ref, gate_ref,
                   dy_all, wdc_ref,
                   wd_ref, fan_ref, sd_ref, hid_buf, sh_buf, gate_buf, taken_buf, wd_sem, sh_sem, *sems):
    step = pl.program_id(0)
    tokens, width = mix_ref.shape
    groups, slots = tokens // 256, 128
    half = groups * slots
    ff = hid_ref.shape[1]
    phase = pl.num_programs(0) // 2
    g = Gather(dy_ref, dy_all, chunks, sems[:Gather.COUNT])
    job = side_job(dp, span, down_ref, wdc_ref, sems[Gather.COUNT:])
    parts = (wda_ref, wdb_ref, wdc_ref)

    @pl.when(step == 0)
    def _():
        enter(g.me, g.z, g.core, g.side, dp)
        g.start()
        job.start()
        copies = share_copies(share_ref, fan_ref, sd_ref, sh_sem)
        for copy in copies + down_copies(parts, wd_ref, wd_sem, 0) + down_copies(parts, wd_ref, wd_sem, 1):
            copy.start()
        share_blank(fan_ref, sd_ref)
        fan_ref[SHARE:SHARE + 16] = router_ref[...]
        for copy in copies:
            copy.wait()

    @pl.when(step < phase)
    def _():
        mix = mix_ref[...]
        fanned = mm_t(mix, fan_ref[:TILE, :])
        s_up = mm_t(mix, fan_ref[TILE:, :])
        s_act, s_slope = silu_pair(fanned)
        s_hidden = (s_act * s_up).astype(BF)
        at = pl.ds(pl.multiple_of(step * tokens, tokens), tokens)
        sh_ref[...] = s_hidden
        sh_buf[at] = s_hidden
        sact_ref[...] = s_act.astype(BF)
        sslo_ref[...] = (s_up * s_slope).astype(BF)
        logits = fanned[:, SHARE:SHARE + 16]
        mask, mine = mine_of(routes_ref, pick_ref)
        taken = mine * valid_of(len_ref, step * (tokens // (batches * here)), tokens, batches, here)
        held = jnp.where(mask, logits, -1e30)
        raised = jnp.where(mask, jnp.exp(held - jnp.max(held, axis=1, keepdims=True)), 0.0)
        soft = raised / jnp.sum(raised, axis=1, keepdims=True)
        gate = jnp.sum(soft * pick_ref[:, :16], axis=1, keepdims=True) * taken
        gate_ref[...] = jnp.concatenate([gate, taken], axis=1)
        gate_buf[at] = gate
        taken_buf[at] = taken
        to_slot, _ = one_hots(taken, groups, slots, here)

        def dispatch(j, _):
            for n in range(groups):
                rows_ref[n * slots:(n + 1) * slots, lanes(j)] = mm(
                    to_slot[n], mix_ref[n * 256:(n + 1) * 256, lanes(j)]).astype(BF)
            return 0

        lax.fori_loop(0, width // WIDE, dispatch, 0)
        rows_at = pl.ds(pl.multiple_of(step * half, half), half)

        def fan_in(start, size):
            cols = pl.ds(start, size)
            gate_in = mm(rows_ref[...], wg_ref[:, cols])
            up_in = mm(rows_ref[...], wu_ref[:, cols])
            act, slope = silu_pair(gate_in)
            hidden = (act * up_in).astype(BF)
            hid_ref[:, cols] = hidden
            hid_buf[rows_at, cols] = hidden
            act_ref[:, cols] = act.astype(BF)
            slo_ref[:, cols] = (up_in * slope).astype(BF)

        over_columns(ff, fan_in)

    @pl.when(step == phase)
    def _():
        job.finish()
        for copy in down_copies(parts, wd_ref, wd_sem, 2):
            copy.start()
        for which in range(3):
            for copy in down_copies(parts, wd_ref, wd_sem, which):
                copy.wait()

    @pl.when(step >= phase)
    def _():
        tile = step - phase
        at = pl.ds(pl.multiple_of(tile * tokens, tokens), tokens)
        rows_at = pl.ds(pl.multiple_of(tile * half, half), half)
        gate = gate_buf[at]
        s_hidden = sh_buf[at]
        _, to_token = one_hots(taken_buf[at], groups, slots, here)

        def fan_out(j, _):
            eo = mm(hid_buf[rows_at], wd_ref[:, lanes(j)]).astype(BF)
            eo_ref[:, lanes(j)] = eo
            shared = mm(s_hidden, sd_ref[:, lanes(j)])
            picked = jnp.concatenate(
                [mm(to_token[n], eo[n * slots:(n + 1) * slots]) for n in range(groups)], axis=0)
            out_ref[:, lanes(j)] = (shared + gate * picked).astype(BF)
            return 0

        lax.fori_loop(0, width // WIDE, fan_out, 0)

    for r, s in ((1, 1), (2, 2), (3, 4), (4, 6)):
        @pl.when(step == s)
        def _():
            g.round(r)

    @pl.when(step == 2 * phase - 1)
    def _():
        g.finish()


def backward_kernel(here, chunks, pick_ref, dy_ref, wg_ref, wu_ref, share_ref, wda_ref, wdb_ref, wdc_ref,
                    act_ref, slo_ref, eo_ref, sact_ref, sslo_ref, gate_ref, part_ref,
                    dh_ref, deo_ref, dg_ref, du_ref, ds_ref, sum_ref,
                    wd_ref, fan_ref, sd_ref, wd_sem, sh_sem, *scratch):
    step = pl.program_id(0)
    tokens, width = dy_ref.shape
    groups, slots = tokens // 256, 128
    ff = dg_ref.shape[1]
    sc = Scatter(part_ref, sum_ref, chunks, scratch)

    @pl.when(step == 0)
    def _():
        enter(sc.me, sc.z, sc.core, sc.side)
        copies = share_copies(share_ref, fan_ref, sd_ref, sh_sem)
        for which in range(3):
            copies += down_copies((wda_ref, wdb_ref, wdc_ref), wd_ref, wd_sem, which)
        for copy in copies:
            copy.start()
        sc.start()
        share_blank(fan_ref, sd_ref)
        for copy in copies:
            copy.wait()

    d_sh = mm_t(dy_ref[...], sd_ref[...])
    d_s = jnp.concatenate([(d_sh * sslo_ref[...].astype(F32)).astype(BF),
                           (d_sh * sact_ref[...].astype(F32)).astype(BF)], axis=1)
    ds_ref[...] = d_s
    gate, taken = gate_ref[:, :1], gate_ref[:, 1:]
    to_slot, to_token = one_hots(taken, groups, slots, here)

    @pl.when(step == 0)
    def _():
        sc.first(0)
        sc.first(1)

    def dispatch(j, total):
        dy = dy_ref[:, lanes(j)].astype(F32)
        gated = (gate * dy).astype(BF)
        for n in range(groups):
            deo_ref[n * slots:(n + 1) * slots, lanes(j)] = mm(to_slot[n], gated[n * 256:(n + 1) * 256]).astype(BF)
        picked = jnp.concatenate(
            [mm(to_token[n], eo_ref[n * slots:(n + 1) * slots, lanes(j)]) for n in range(groups)], axis=0)
        return total + jnp.sum(dy * picked, axis=1, keepdims=True)

    d_gates = lax.fori_loop(0, width // WIDE, dispatch, jnp.zeros((tokens, 1), F32))

    def back_out(start, size):
        cols = pl.ds(start, size)
        d_eh = mm_t(deo_ref[...], wd_ref[cols, :])
        dg_ref[:, cols] = (d_eh * slo_ref[:, cols].astype(F32)).astype(BF)
        du_ref[:, cols] = (d_eh * act_ref[:, cols].astype(F32)).astype(BF)

    over_columns(ff, back_out)

    @pl.when(step == 0)
    def _():
        sc.first(2)
        sc.first(3)

    def back_in(j, _):
        d_rows = (mm_t(dg_ref[...], wg_ref[lanes(j), :]) + mm_t(du_ref[...], wu_ref[lanes(j), :])).astype(BF)
        shared = mm(d_s, fan_ref[:, lanes(j)])
        taken_rows = jnp.concatenate(
            [mm(to_token[n], d_rows[n * slots:(n + 1) * slots]) for n in range(groups)], axis=0)
        dh_ref[:, lanes(j)] = (shared + taken_rows).astype(BF)
        return 0

    lax.fori_loop(0, width // WIDE, back_in, 0)
    high = d_gates.astype(BF).astype(F32)
    dh_ref[:, width:] = (high * pick_ref[:, :128] + (d_gates - high) * pick_ref[:, 128:]).astype(BF)

    outer = (sc.z == 0) | (sc.z == NZ - 1)
    for i in range(NZ - 1):
        @pl.when((step == i) & outer)
        def _():
            sc.second(i)

        @pl.when((step == min(i + 1, 2)) & jnp.logical_not(outer))
        def _():
            sc.second(i)

    @pl.when(step == NZ - 1)
    def _():
        sc.second(NZ - 1)
        sc.finish()


def whole(v):
    zeros = (0,) * v.ndim
    return pl.BlockSpec(v.shape, lambda i: zeros, pipeline_mode=pl.Buffered(buffer_count=1))


def tiles(rows, w):
    return pl.BlockSpec((rows, w), lambda i: (i, 0))


SMEM = pl.BlockSpec(memory_space=pltpu.SMEM)


def mixture_forward(dp, batches, here, lengths, pick, mix, routes, wg, wu, router, share, wda, wdb, span, down, dy, cid,
                    chunks=2):
    total, width = mix.shape
    step, half = total // 4, total // 8
    ff = wg.shape[1]
    shape = jax.ShapeDtypeStruct
    rows = total // 2
    dma = pltpu.SemaphoreType.DMA

    def early(n, w):
        return pl.BlockSpec((n, w), lambda i: (jnp.minimum(i, 3), 0))

    def late(n, w):
        return pl.BlockSpec((n, w), lambda i: (jnp.maximum(i - 4, 0), 0))

    return pl.pallas_call(
        functools.partial(forward_kernel, chunks, dp, span, batches, here),
        grid=(8,),
        out_shape=(
            shape((total, width), BF), shape((rows, width), BF), shape((rows, ff), BF), shape((rows, ff), BF),
            shape((rows, ff), BF), shape((rows, width), BF), shape((total, TILE), BF), shape((total, TILE), BF),
            shape((total, TILE), BF), shape((total, 2), F32), shape((NE,) + dy.shape, BF),
            shape((dp, span[1], width), BF)),
        in_specs=[SMEM, whole(pick), early(step, width), early(step, routes.shape[1]), whole(wg), whole(wu),
                  whole(router), ANY, ANY, ANY, ANY, ANY],
        out_specs=[late(step, width), early(half, width), early(half, ff), early(half, ff), early(half, ff),
                   late(half, width), early(step, TILE), early(step, TILE), early(step, TILE), early(step, 2), ANY, ANY],
        scratch_shapes=[
            pltpu.VMEM((ff, width), BF), pltpu.VMEM((2 * TILE, width), BF), pltpu.VMEM((TILE, width), BF),
            pltpu.VMEM((rows, ff), BF), pltpu.VMEM((total, TILE), BF), pltpu.VMEM((total, 1), F32),
            pltpu.VMEM((total, 1), F32), dma((3 * dp,)), dma((3 * dp,))] + Gather.scratch(chunks) + Spread.scratch(dp),
        compiler_params=pltpu.CompilerParams(
            collective_id=cid, has_side_effects=True, vmem_limit_bytes=60 * 1024 * 1024),
        cost_estimate=COST,
        name="mixture_forward",
    )(lengths, pick, mix, routes, wg, wu, router, share, wda, wdb, down, dy)


def mixture_backward(here, pick, dy, wg, wu, share, wda, wdb, wdc, act, slo, eo, sact, sslo, gate, part, cid, chunks=2):
    total, width = dy.shape
    step, half = total // NZ, total // NZ // 2
    ff = wg.shape[1]
    shape = jax.ShapeDtypeStruct
    rows = total // 2
    dp = wda.shape[0]
    _, own, _ = part.shape
    dma = pltpu.SemaphoreType.DMA
    return pl.pallas_call(
        functools.partial(backward_kernel, here, chunks),
        grid=(NZ,),
        out_shape=(
            shape((total, width + 128), BF), shape((rows, width), BF), shape((rows, ff), BF), shape((rows, ff), BF),
            shape((total, 2 * TILE), BF), shape((own, width), F32)),
        in_specs=[whole(pick), tiles(step, width), whole(wg), whole(wu), ANY, ANY, ANY, ANY,
                  tiles(half, ff), tiles(half, ff), tiles(half, width), tiles(step, TILE), tiles(step, TILE),
                  tiles(step, 2), ANY],
        out_specs=[tiles(step, width + 128), tiles(half, width), tiles(half, ff), tiles(half, ff),
                   tiles(step, 2 * TILE), pl.BlockSpec((own, width), lambda i: (0, 0))],
        scratch_shapes=[
            pltpu.VMEM((ff, width), BF), pltpu.VMEM((2 * TILE, width), BF), pltpu.VMEM((TILE, width), BF),
            dma((3 * dp,)), dma((3 * dp,))] + Scatter.scratch(own, width, chunks, BF),
        compiler_params=pltpu.CompilerParams(
            collective_id=cid, has_side_effects=True, vmem_limit_bytes=62 * 1024 * 1024),
        cost_estimate=COST,
        name="mixture_backward",
    )(pick, dy, wg, wu, share, wda, wdb, wdc, act, slo, eo, sact, sslo, gate, part)


class ShareWork:
    ROWS = 256

    def __init__(self, ds_ref, sh_ref, mix_ref, dy_ref, out_ref, scratch):
        self.sources = (ds_ref, sh_ref, mix_ref, dy_ref)
        self.out = out_ref
        *self.buffers, self.gfan, self.gsd, self.sem = scratch
        self.steps = mix_ref.shape[0] // self.ROWS
        self.done = 0

    @staticmethod
    def scratch(width):
        r = ShareWork.ROWS
        return [pltpu.VMEM((2, r, w), BF) for w in (2 * TILE, TILE, width, width)] + [
            pltpu.VMEM((2 * TILE, width), F32), pltpu.VMEM((TILE, width), F32), pltpu.SemaphoreType.DMA((2, 4))]

    COUNT = 7

    def copies(self, n):
        return [pltpu.make_async_copy(src.at[pl.ds(n * self.ROWS, self.ROWS)], buf.at[n % 2], self.sem.at[n % 2, i])
                for i, (src, buf) in enumerate(zip(self.sources, self.buffers))]

    def start(self):
        for copy in self.copies(0):
            copy.start()
        self.gfan[...] = jnp.zeros_like(self.gfan)
        self.gsd[...] = jnp.zeros_like(self.gsd)

    def step(self):
        n = self.done
        if n == self.steps:
            return
        self.done += 1
        for copy in self.copies(n):
            copy.wait()
        if n + 1 < self.steps:
            for copy in self.copies(n + 1):
                copy.start()
        ds, sh, mix, dy = self.buffers

        def columns(j, _):
            self.gfan[:, lanes(j)] += mm_lead(ds[n % 2], mix[n % 2, :, lanes(j)])
            self.gsd[:, lanes(j)] += mm_lead(sh[n % 2], dy[n % 2, :, lanes(j)])
            return 0

        lax.fori_loop(0, mix.shape[2] // WIDE, columns, 0)

    def finish(self):
        while self.done < self.steps:
            self.step()
        dp, rows, w = self.out.shape
        n = rows // 3
        for d in range(dp):
            cols = slice(d * w, (d + 1) * w)
            self.out[d, :n] = self.gfan[:n, cols].astype(BF)
            self.out[d, n:2 * n] = self.gfan[TILE:TILE + n, cols].astype(BF)
            self.out[d, 2 * n:] = self.gsd[:n, cols].astype(BF)


def scatter_share_kernel(chunks, p_ref, ds_ref, sh_ref, mix_ref, dy_ref, o_ref, g_ref, *scratch):
    s = Scatter(p_ref, o_ref, chunks, scratch[:Scatter.COUNT])
    work = ShareWork(ds_ref, sh_ref, mix_ref, dy_ref, g_ref, scratch[Scatter.COUNT:])
    enter(s.me, s.z, s.core, s.side)
    s.start()
    work.start()
    s.run(work.step)
    work.finish()
    s.finish()


def scatter_share(p, ds, sh, mix, dy, share_shape, cid, chunks=2):
    _, rows, width = p.shape
    return pl.pallas_call(
        functools.partial(scatter_share_kernel, chunks),
        out_shape=(jax.ShapeDtypeStruct((rows, width), F32), jax.ShapeDtypeStruct(share_shape, BF)),
        in_specs=[ANY] * 5,
        out_specs=(VMEM, VMEM),
        scratch_shapes=Scatter.scratch(rows, width, chunks, p.dtype) + ShareWork.scratch(mix.shape[1]),
        compiler_params=pltpu.CompilerParams(
            collective_id=cid, has_side_effects=True, vmem_limit_bytes=60 * 1024 * 1024),
        cost_estimate=COST,
        name="scatter_share",
    )(p, ds, sh, mix, dy)


def turn(v, cosine, sine):
    half = v.shape[1] // 2
    a, b = v[:, :half], v[:, half:]
    return jnp.concatenate([a * cosine - b * sine, b * cosine + a * sine], axis=1)


def project_kernel(x_ref, gain_ref, lgain_ref, wq_ref, wl_ref, we_ref, cos_ref, sin_ref,
                   h_ref, q_ref, k_ref, v_ref, lat_ref):
    blocks = x_ref.shape[0]
    batches, rows, _ = q_ref.shape
    here = rows // blocks
    x = x_ref[...].reshape(blocks * batches * here, x_ref.shape[2]).astype(F32)
    h = x * lax.rsqrt(jnp.mean(x * x, axis=1, keepdims=True) + 1e-6) * gain_ref[...]
    h = h.astype(BF)
    h_ref[...] = h
    raw = mm(h, wq_ref[...])
    raw_lat = mm(h, wl_ref[...])
    cosine, sine = cos_ref[...], sin_ref[...]
    zeros = jnp.zeros((raw.shape[0], 64), BF)
    q = jnp.concatenate([raw[:, :128].astype(BF), turn(raw[:, 128:192], cosine, sine).astype(BF), zeros], axis=1)
    k_rope = turn(raw_lat[:, 512:576], cosine, sine).astype(BF)
    lat = raw_lat[:, :512]
    lat = (lat * lax.rsqrt(jnp.mean(lat * lat, axis=1, keepdims=True) + 1e-6) * lgain_ref[...]).astype(BF)
    expanded = mm(lat, we_ref[...]).astype(BF)
    k = jnp.concatenate([expanded[:, :128], k_rope, zeros], axis=1)
    for e in range(blocks):
        for m in range(batches):
            src = slice((e * batches + m) * here, (e * batches + m + 1) * here)
            dst = slice(e * here, (e + 1) * here)
            q_ref[m, dst] = q[src]
            k_ref[m, dst] = k[src]
            v_ref[m, dst] = expanded[src, 128:]
            lat_ref[m, dst] = lat[src]


def project(x_all, gain, lgain, wq, wl, we, cosine, sine, batches):
    groups, rows, width = x_all.shape
    here = rows // batches
    per = 4
    seq = groups * here
    shape = jax.ShapeDtypeStruct

    def whole(v):
        return pl.BlockSpec(v.shape, lambda i: (0, 0))

    def by_seq(w):
        return pl.BlockSpec((batches, per * here, w), lambda i: (0, i, 0))

    table = pl.BlockSpec((per * rows, 32), lambda i: (i, 0))
    return pl.pallas_call(
        project_kernel,
        grid=(groups // per,),
        out_shape=(shape((groups * rows, width), BF), shape((batches, seq, 256), BF), shape((batches, seq, 256), BF),
                   shape((batches, seq, 128), BF), shape((batches, seq, 512), BF)),
        in_specs=[pl.BlockSpec((per, rows, width), lambda i: (i, 0, 0)), whole(gain), whole(lgain), whole(wq), whole(wl), whole(we),
                  table, table],
        out_specs=[pl.BlockSpec((per * rows, width), lambda i: (i, 0)), by_seq(256), by_seq(256), by_seq(128), by_seq(512)],
        compiler_params=pltpu.CompilerParams(vmem_limit_bytes=48 * 1024 * 1024),
        cost_estimate=pl.CostEstimate(flops=7_000_000_000, bytes_accessed=20_000_000, transcendentals=0),
        name="project",
    )(x_all, gain, lgain, wq, wl, we, cosine, sine)


ROWS = 256
SCALE = 192.0 ** -0.5


def held_scores(q, k, first, length):
    s = mm_t(q, k) * SCALE
    t = lax.broadcasted_iota(jnp.int32, s.shape, 0) + first
    u = lax.broadcasted_iota(jnp.int32, s.shape, 1)
    return jnp.where((u <= t) & (u < length), s, -1e30)


def attend_kernel(len_ref, q_ref, k_ref, v_ref, wo_ref, part_ref, att_ref, lse_ref):
    length = len_ref[pl.program_id(0)]
    seq = q_ref.shape[1]
    groups, _, here, width = part_ref.shape
    for i in range(seq // ROWS):
        tile = slice(i * ROWS, (i + 1) * ROWS)
        ext = (i + 1) * ROWS
        s = held_scores(q_ref[0, tile], k_ref[0, :ext], i * ROWS, length)
        peak = jnp.max(s, axis=1, keepdims=True)
        raised = jnp.exp(s - peak)
        total = jnp.sum(raised, axis=1, keepdims=True)
        lse_ref[0, tile] = peak + jnp.log(total)
        p = (raised / total).astype(BF)
        att = mm(p, v_ref[0, :ext]).astype(BF)
        per = ROWS // here
        att_ref[i * per:(i + 1) * per, 0] = att.reshape(per, here, att.shape[1])
        for j in range(width // 512):
            cols = slice(j * 512, (j + 1) * 512)
            part_ref[i * per:(i + 1) * per, 0, :, cols] = mm(att, wo_ref[:, cols]).astype(BF).reshape(per, here, 512)


def attend(lengths, q, k, v, wo, groups):
    batches, seq, _ = q.shape
    here = seq // groups
    width = wo.shape[1]
    shape = jax.ShapeDtypeStruct

    def by_seq(w):
        return pl.BlockSpec((1, seq, w), lambda m: (m, 0, 0))

    def by_dev(w):
        return pl.BlockSpec((groups, 1, here, w), lambda m: (0, m, 0, 0))

    return pl.pallas_call(
        attend_kernel,
        grid=(batches,),
        out_shape=(shape((groups, batches, here, width), BF), shape((groups, batches, here, 128), BF),
                   shape((batches, seq, 1), F32)),
        in_specs=[pl.BlockSpec(memory_space=pltpu.SMEM), by_seq(256), by_seq(256), by_seq(128),
                  pl.BlockSpec(wo.shape, lambda m: (0, 0))],
        out_specs=[by_dev(width), by_dev(128), by_seq(1)],
        compiler_params=pltpu.CompilerParams(vmem_limit_bytes=48 * 1024 * 1024),
        cost_estimate=pl.CostEstimate(flops=4_000_000_000, bytes_accessed=15_000_000, transcendentals=2_000_000),
        name="attend",
    )(lengths, q, k, v, wo)


def attend_back_kernel(len_ref, dout_ref, h_ref, q_ref, k_ref, v_ref, lat_ref, att_ref, lse_ref, wo_ref, wq_ref, we_ref,
                       cos_ref, sin_ref, part_ref, gwq_ref, gwo_out, gwe_out, dk, dv, datt, gwq, gwo_ref, gwe_ref):
    m = pl.program_id(0)
    length = len_ref[m]
    seq = q_ref.shape[1]
    groups, _, here, width = dout_ref.shape
    per = ROWS // here

    @pl.when(m == 0)
    def _():
        gwo_ref[...] = jnp.zeros_like(gwo_ref)
        gwe_ref[...] = jnp.zeros_like(gwe_ref)
        gwq[...] = jnp.zeros_like(gwq)

    for j in range(4):
        blocks = slice(j * groups // 4, (j + 1) * groups // 4)
        dout = dout_ref[blocks].reshape(seq // 4, width)
        rows = slice(j * seq // 4, (j + 1) * seq // 4)
        datt[rows] = mm_t(dout, wo_ref[...]).astype(BF)
        gwo_ref[...] += mm_lead(att_ref[blocks].reshape(seq // 4, 128), dout)
    dk[...] = jnp.zeros_like(dk)
    dv[...] = jnp.zeros_like(dv)
    for i in range(seq // ROWS):
        tile = slice(i * ROWS, (i + 1) * ROWS)
        ext = (i + 1) * ROWS
        q = q_ref[0, tile]
        p = jnp.exp(held_scores(q, k_ref[0, :ext], i * ROWS, length) - lse_ref[0, tile])
        da = datt[tile]
        dp = mm_t(da, v_ref[0, :ext])
        inner = jnp.sum(dp * p, axis=1, keepdims=True)
        ds = (p * (dp - inner)).astype(BF)
        dq = mm(ds, k_ref[0, :ext]) * SCALE
        dk[:ext] += mm_lead(ds, q)
        dv[:ext] += mm_lead(p.astype(BF), da)
        rope = turn(dq[:, 128:192], cos_ref[tile], -sin_ref[tile])
        dq = jnp.concatenate([dq[:, :128].astype(BF), rope.astype(BF), jnp.zeros((ROWS, 64), BF)], axis=1)
        hidden = h_ref[i * per:(i + 1) * per, 0].reshape(ROWS, width)
        for j in range(width // 512):
            cols = slice(j * 512, (j + 1) * 512)
            gwq[:, cols] += mm_lead(dq, hidden[:, cols])
        for j in range(width // 512):
            cols = slice(j * 512, (j + 1) * 512)
            part_ref[i * per:(i + 1) * per, 0, :, cols] = mm_t(dq, wq_ref[cols]).astype(BF).reshape(per, here, 512)
    for i in range(seq // ROWS):
        tile = slice(i * ROWS, (i + 1) * ROWS)
        d_k = dk[tile] * SCALE
        d_exp = jnp.concatenate([d_k[:, :128].astype(BF), dv[tile].astype(BF)], axis=1)
        gwe_ref[...] += mm_lead(lat_ref[0, tile], d_exp)
        d_lat = mm_t(d_exp, we_ref[...]).astype(BF)
        tail = jnp.concatenate([d_lat, d_k[:, 128:].astype(BF)], axis=1)
        pad = part_ref.shape[3] - width - tail.shape[1]
        if pad > 0:
            tail = jnp.concatenate([tail, jnp.zeros((ROWS, pad), BF)], axis=1)
        part_ref[i * per:(i + 1) * per, 0, :, width:] = tail[:, :part_ref.shape[3] - width].reshape(per, here, -1)

    @pl.when(m == pl.num_programs(0) - 1)
    def _():
        for j in range(width // 256):
            cols = slice(j * 256, (j + 1) * 256)
            gwq_ref[cols] = gwq[:, cols].T.astype(BF)
        gwo_out[...] = gwo_ref[...].astype(BF)
        gwe_out[...] = gwe_ref[...].astype(BF)


def attend_back(lengths, dout, h, q, k, v, lat, att, lse, wo, wq, we, cosine, sine, tail):
    groups, batches, here, width = dout.shape
    seq = groups * here
    shape = jax.ShapeDtypeStruct

    def by_seq(w):
        return pl.BlockSpec((1, seq, w), lambda m: (m, 0, 0))

    def by_dev(w):
        return pl.BlockSpec((groups, 1, here, w), lambda m: (0, m, 0, 0))

    def whole(v):
        return pl.BlockSpec(v.shape, lambda m: (0, 0))

    return pl.pallas_call(
        attend_back_kernel,
        grid=(batches,),
        out_shape=(shape((groups, batches, here, width + tail), BF), shape(wq.shape, BF),
                   shape(wo.shape, BF), shape(we.shape, BF)),
        in_specs=[pl.BlockSpec(memory_space=pltpu.SMEM), by_dev(width), by_dev(width), by_seq(256), by_seq(256), by_seq(128),
                  by_seq(512), by_dev(128), by_seq(1), whole(wo), whole(wq), whole(we), whole(cosine), whole(sine)],
        out_specs=[by_dev(width + tail), whole(wq), whole(wo), whole(we)],
        scratch_shapes=[pltpu.VMEM((seq, 256), F32), pltpu.VMEM((seq, 128), F32), pltpu.VMEM((seq, 128), BF),
                        pltpu.VMEM((256, width), F32), pltpu.VMEM(wo.shape, F32), pltpu.VMEM(we.shape, F32)],
        compiler_params=pltpu.CompilerParams(vmem_limit_bytes=56 * 1024 * 1024),
        cost_estimate=pl.CostEstimate(flops=14_000_000_000, bytes_accessed=25_000_000, transcendentals=2_000_000),
        name="attend_back",
    )(lengths, dout, h, q, k, v, lat, att, lse, wo, wq, we, cosine, sine)


H = 16
QK_NOPE = 128
ROPE = 64
V_DIM = 128
KV_RANK = 512
GROUPS = 16
EPSILON = 1e-06
ROTARY_BASE = 10000.0


def product(left_side, right_side):
    return jnp.dot(left_side, right_side, preferred_element_type=F32)


def product_lead(left_side, right_side):
    return lax.dot_general(
        left_side, right_side, (((0,), (0,)), ((), ())), preferred_element_type=F32
    )


def product_trail(left_side, right_side):
    return lax.dot_general(
        left_side, right_side, (((1,), (1,)), ((), ())), preferred_element_type=F32
    )


def rotary_tables(count):
    frequency = ROTARY_BASE ** (-np.arange(ROPE // 2, dtype=np.float32) * np.float32(2.0) / np.float32(ROPE))
    angles = np.arange(count, dtype=np.float32)[:, None] * frequency.astype(np.float32)[None, :]
    return np.cos(angles).astype(np.float32), np.sin(angles).astype(np.float32)


def rotate(values, cosine, sine_table):
    first_half, second_half = jnp.split(values, 2, axis=-1)
    return jnp.concatenate(
        [
            first_half * cosine - second_half * sine_table,
            second_half * cosine + first_half * sine_table,
        ],
        axis=-1,
    )


def norm_forward(values, gains):
    factor = lax.rsqrt(jnp.mean(values * values, axis=-1, keepdims=True) + EPSILON)
    normed = values * factor
    return (normed * gains, normed, factor)


def norm_backward(gradient, normed, factor, gains):
    gain_grad = jnp.sum(gradient * normed, axis=0)
    scaled = gradient * gains
    return (
        factor * (scaled - normed * jnp.mean(scaled * normed, axis=-1, keepdims=True)),
        gain_grad,
    )


def selected_experts(routes):
    chosen = routes[:, :, None] == jnp.arange(GROUPS, dtype=routes.dtype)
    return jnp.any(chosen, axis=1)


def masked_softmax(logits, mask):
    held = jnp.where(mask, logits, -1e30)
    peak = jnp.max(held, axis=-1, keepdims=True)
    raised = jnp.where(mask, jnp.exp(held - peak), 0.0)
    return raised / jnp.sum(raised, axis=-1, keepdims=True)


def per_device(
    layer_input,
    out_cotangent,
    lengths,
    routes,
    attn_gain,
    query_weight,
    latent_weight,
    latent_gain,
    expand_weight,
    output_weight,
    mixer_gain,
    router_weight,
    gate_weight,
    up_weight,
    down_weight,
    shared_gate,
    shared_up,
    shared_down,
):
    dp = lax.axis_size("dp")
    me = lax.axis_index("expert")
    plane = lax.axis_index("dp")
    batches, _, here, width = layer_input.shape
    own = batches * here
    total = own * GROUPS
    seq_total = here * GROUPS
    rows_w = query_weight.shape[0]
    rows_l = expand_weight.shape[0]

    x_own = layer_input.reshape(own, width)
    routes_own = routes.reshape(own, -1)
    choices = routes_own.shape[1]
    route_columns = routes_own.astype(BF).reshape(rows_w, -1)
    small_width = -(-(595 + route_columns.shape[1]) // 128) * 128
    latent_column = jnp.zeros((rows_w,), BF).at[:rows_l].set(latent_gain)
    small = jnp.concatenate(
        [
            latent_weight,
            router_weight,
            attn_gain[:, None],
            mixer_gain[:, None],
            latent_column[:, None],
            route_columns,
            jnp.zeros((rows_w, small_width - 595 - route_columns.shape[1]), BF),
        ],
        axis=1,
    )
    query_parts = query_weight.reshape(rows_w, H, QK_NOPE + ROPE).transpose(1, 0, 2)
    expand_parts = expand_weight.reshape(rows_l, H, QK_NOPE + V_DIM).transpose(1, 0, 2)
    expand_parts = expand_parts.reshape(H, rows_l, 4, ROPE).swapaxes(1, 2).reshape(H, rows_w, ROPE)
    parts = jnp.concatenate([query_parts, expand_parts], axis=2)
    x_all, small, parts_head, output_head = opening(dp, x_own, small, parts, output_weight, 1)
    x_all = x_all.reshape(total, width)
    routes_all = lax.dynamic_index_in_dim(small, plane, 0, False)[..., 595 : 595 + route_columns.shape[1]]
    routes_all = routes_all.reshape(total, choices).astype(jnp.int32)
    small = small.reshape(width, small_width)
    parts_head = parts_head.reshape(width, TILE)
    latent_full = small[:, :576]
    router_full = small[:, 576:592]
    gain_attn = small[:, 592].astype(F32)
    gain_mixer = small[:, 593].astype(F32)
    gain_latent = small[:, 594].reshape(dp * GROUPS, rows_w)[:, :rows_l].reshape(-1).astype(F32)
    expand_head = parts_head[:, QK_NOPE + ROPE :].reshape(dp * GROUPS, 4, rows_l, ROPE)
    expand_head = expand_head.swapaxes(1, 2).reshape(KV_RANK, QK_NOPE + V_DIM)
    output_head = output_head.reshape(V_DIM, width)

    ff = gate_weight.shape[2]
    share_own = jnp.concatenate([shared_gate.T, shared_up.T, shared_down], axis=0)
    share_width = shared_down.shape[0]
    gate_full = lax.all_gather(gate_weight[0], "dp", axis=0, tiled=True)
    up_full = lax.all_gather(up_weight[0], "dp", axis=0, tiled=True)
    share_full = lax.all_gather(share_own, "dp", axis=0)
    seq_lengths = lengths.reshape(batches)
    own_positions = me * here + jnp.arange(here, dtype=jnp.int32)
    valid_own = (own_positions[None, :] < seq_lengths[:, None]).reshape(own).astype(F32)
    cosine, sine_table = rotary_tables(seq_total)
    cosine_own = lax.dynamic_slice_in_dim(jnp.asarray(cosine), me * here, here)
    sine_own = lax.dynamic_slice_in_dim(jnp.asarray(sine_table), me * here, here)

    grad_own = out_cotangent.reshape(own, width) * valid_own[:, None].astype(BF)

    def by_token(table):
        return jnp.asarray(np.broadcast_to(
            table.reshape(GROUPS, 1, here, -1), (GROUPS, batches, here, table.shape[1])).reshape(total, -1))

    hidden_all, query, key, values, latent = project(
        x_all.reshape(GROUPS, own, width), gain_attn[None], gain_latent[None], parts_head, small, expand_head,
        by_token(cosine), by_token(sine_table), batches)
    attn_part, attended, log_total = attend(seq_lengths, query, key, values, output_head, GROUPS)
    attn_part = attn_part.reshape(GROUPS, own, width)
    down_own = down_weight[0]
    cut = down_own.shape[0] * 3 // 160 * 16
    cuts = (0, cut, 2 * cut + cut // 48 * 16, down_own.shape[0])
    spans = [(first, last - first) for first, last in zip(cuts, cuts[1:])]
    attn_out, down_a = scatter16(attn_part, 2, dp=dp, span=spans[0], side=down_own)

    x_wide = x_own.astype(F32)
    middle = x_wide + attn_out
    normed_mix, unit_mix, factor_mix = norm_forward(middle, gain_mixer)
    hidden_mix = normed_mix.astype(BF)
    mix_all, down_b = gather16(hidden_mix, 3, dp=dp, span=spans[1], side=down_own)
    mix_all = mix_all.reshape(total, width)

    lane = jnp.arange(128)[None, :]
    pick = jnp.concatenate([lane == me, lane == me + GROUPS], axis=1).astype(F32)
    (out_part, rows, hidden, act, slope, result, share_hidden, share_act, share_slope, gates, grad_all,
     down_c) = mixture_forward(
        dp, batches, here, seq_lengths, pick, mix_all, routes_all, gate_full, up_full, router_full.T, share_full,
        down_a, down_b, spans[2], down_own, grad_own, 4)
    grad_all = grad_all.reshape(total, width)
    mix_part, grad_result, grad_gate_in, grad_up_in, grad_share_in, mixed = mixture_backward(
        here, pick, grad_all, gate_full, up_full, share_full, down_a, down_b, down_c, act, slope, result,
        share_act, share_slope, gates, out_part.reshape(GROUPS, own, width), 8)
    grad_down = product_lead(hidden, grad_result).astype(BF)
    grad_gate = product_lead(rows, grad_gate_in).astype(BF)
    grad_up = product_lead(rows, grad_up_in).astype(BF)
    mix_part, _, _, _ = lax.optimization_barrier((mix_part, grad_down, grad_gate, grad_up))
    mix_sum, grad_share = scatter_share(
        mix_part.reshape(GROUPS, own, width + 128), grad_share_in, share_hidden, mix_all, grad_all, share_full.shape, 5)
    layer_output = valid_own[:, None] * (middle + mixed)

    out_down = lax.psum_scatter(grad_down, "dp", scatter_dimension=0, tiled=True)
    out_gate = lax.psum_scatter(grad_gate, "dp", scatter_dimension=0, tiled=True)
    out_up = lax.psum_scatter(grad_up, "dp", scatter_dimension=0, tiled=True)

    mask_own = selected_experts(routes_own)
    soft_own = masked_softmax(product(hidden_mix, router_full), mask_own)
    grad_masked = (mix_sum[:, width : width + GROUPS] + mix_sum[:, width + GROUPS : width + 2 * GROUPS])
    grad_masked = grad_masked * valid_own[:, None]
    grad_logits = soft_own * (grad_masked - jnp.sum(grad_masked * soft_own, axis=1, keepdims=True))
    grad_logits = grad_logits.astype(BF)
    grad_mix = mix_sum[:, :width] + product_trail(grad_logits, router_full)
    grad_middle_norm, grad_gain_mixer = norm_backward(grad_mix, unit_mix, factor_mix, gain_mixer)
    grad_middle = grad_own.astype(F32) + grad_middle_norm

    grad_attn_all, share_far = gather16(grad_middle.astype(BF), 6, dp=dp, side=grad_share)
    grad_attn_all = grad_attn_all.reshape(GROUPS, batches, here, width)
    out_share = lax.dynamic_index_in_dim(grad_share, plane, 0, False).astype(F32)
    out_share = out_share + jnp.sum(share_far.astype(F32), axis=0)
    back_part, grad_query_w, grad_output, grad_expand = attend_back(
        seq_lengths, grad_attn_all, hidden_all.reshape(GROUPS, batches, here, width), query, key, values, latent,
        attended, log_total, output_head, parts_head, expand_head, jnp.asarray(cosine), jnp.asarray(sine_table), 640)
    grad_expand = grad_expand.reshape(dp * GROUPS, rows_l, 4, ROPE).swapaxes(1, 2).reshape(width, ROPE)
    parts_grad = grad_query_w + jnp.pad(grad_expand, ((0, 0), (QK_NOPE + ROPE, 0)))
    parts_grad = parts_grad.reshape(dp, GROUPS, rows_w, TILE)
    rows_grad = grad_output.reshape(dp, rows_w, width)
    back_sum, parts_far, rows_far = returning(
        dp, back_part.reshape(GROUPS, own, back_part.shape[3]), parts_grad, rows_grad, 7)
    parts_sum = lax.dynamic_index_in_dim(parts_grad, plane, 0, False).astype(F32)
    parts_sum = (parts_sum + jnp.sum(parts_far.astype(F32), axis=0)).astype(BF)
    rows_sum = (rows_grad.astype(F32) + jnp.sum(rows_far.astype(F32), axis=0)).astype(BF)

    x_normed, unit_attn, factor_attn = norm_forward(x_wide, gain_attn)
    hidden_own = x_normed.astype(BF)
    latent_own = product(hidden_own, latent_full)
    _, unit_latent, factor_latent = norm_forward(latent_own[:, :KV_RANK], gain_latent)
    grad_latent_in, grad_gain_latent = norm_backward(
        back_sum[:, width : width + KV_RANK], unit_latent, factor_latent, gain_latent
    )
    grad_rope = back_sum[:, width + KV_RANK : width + KV_RANK + ROPE].reshape(batches, here, ROPE)
    grad_rope = rotate(grad_rope, cosine_own, -sine_own).reshape(own, ROPE)
    grad_latent_raw = jnp.concatenate([grad_latent_in, grad_rope], axis=1).astype(BF)
    grad_hidden_attn = back_sum[:, :width] + product_trail(grad_latent_raw, latent_full)
    grad_input_norm, grad_gain_attn = norm_backward(grad_hidden_attn, unit_attn, factor_attn, gain_attn)
    grad_input = grad_middle + grad_input_norm

    latent_rows = grad_gain_latent.reshape(dp * GROUPS, rows_l)
    latent_rows = jnp.pad(latent_rows, ((0, 0), (0, rows_w - rows_l))).reshape(width, 1)
    tokens_side = jnp.concatenate([hidden_own, hidden_mix], axis=0)
    grads_side = jnp.concatenate(
        [jnp.pad(grad_latent_raw, ((0, 0), (0, 64))), jnp.pad(grad_logits, ((0, 0), (576, 640 - 592)))], axis=0)
    lane = jnp.arange(640)[None, :]
    small_grad = product_lead(tokens_side, grads_side)
    small_grad = small_grad + jnp.where(lane == 592, grad_gain_attn[:, None], 0.0)
    small_grad = small_grad + jnp.where(lane == 593, grad_gain_mixer[:, None], 0.0)
    small_grad = (small_grad + jnp.where(lane == 594, latent_rows, 0.0)).astype(BF)
    small_grad = small_grad.reshape(dp, GROUPS, rows_w, 640).swapaxes(0, 1).reshape(GROUPS, dp * rows_w, 640)
    small_sum, out_query, out_expand, out_output = closing(dp, small_grad, parts_sum, rows_sum, rows_l, 9)

    def as_input(v):
        return v.reshape(batches, 1, here, width)

    return (
        as_input(layer_output),
        as_input(grad_input),
        small_sum[:, 592],
        out_query,
        small_sum[:, :576],
        small_sum[:rows_l, 594],
        out_expand,
        out_output,
        small_sum[:, 593],
        small_sum[:, 576:592],
        out_gate.astype(F32)[None],
        out_up.astype(F32)[None],
        out_down.astype(F32)[None],
        out_share[:share_width].T,
        out_share[share_width : 2 * share_width].T,
        out_share[2 * share_width :],
    )


def solution(mesh):
    split = P(("dp", "expert"), None)
    line = P(("dp", "expert"))
    tokens = P(None, "dp", "expert", None)
    expert = P("expert", "dp", None)
    return jax.shard_map(
        per_device,
        mesh=mesh,
        in_specs=(
            tokens, tokens, P(None, "dp"), tokens, line, split, split, line, split, split, line, split,
            expert, expert, expert, P("dp", "expert"), P("dp", "expert"), P("expert", "dp"),
        ),
        out_specs=(
            tokens, tokens, line, split, split, line, split, split, line, split,
            expert, expert, expert, P("dp", "expert"), P("dp", "expert"), P("expert", "dp"),
        ),
        check_vma=False,
    )
```

```python
import functools
import jax
import jax.numpy as jnp
import numpy as np
from jax import lax
from jax.experimental import pallas as pl
from jax.experimental.pallas import tpu as pltpu
from jax.sharding import PartitionSpec as P

MESH = pl.DeviceIdType.MESH
NZ = 4
NE = 16


def place():
    me = lax.axis_index("expert")
    z = me // 4
    x = (me // 2) % 2
    c = me % 2
    return me, z, x, c, me + 1 - 2 * c, me + 2 - 4 * x


def enter(me, z, core, side, dp=1):
    barrier = pltpu.get_barrier_semaphore()
    plane = lax.axis_index("dp")
    for r in range(1, dp):
        pl.semaphore_signal(barrier, inc=1, device_id={"dp": (plane + r) % dp}, device_id_type=MESH)
    for other in (core, side):
        pl.semaphore_signal(barrier, inc=1, device_id={"expert": other}, device_id_type=MESH)

    @pl.when(z < NZ - 1)
    def _():
        pl.semaphore_signal(barrier, inc=1, device_id={"expert": me + 4}, device_id_type=MESH)

    @pl.when(z > 0)
    def _():
        pl.semaphore_signal(barrier, inc=1, device_id={"expert": me - 4}, device_id_type=MESH)

    pl.semaphore_wait(barrier, dp + 1 + (z < NZ - 1).astype(jnp.int32) + (z > 0).astype(jnp.int32))


class Spread:
    def __init__(self, dp, src, out, sems):
        self.dp, self.src, self.out = dp, src, out
        self.own, self.send, self.recv = sems
        self.plane = lax.axis_index("dp")

    @staticmethod
    def scratch(dp):
        dma = pltpu.SemaphoreType.DMA
        return [dma, dma((dp,)), dma((dp,))]

    def copy(self, r):
        return pltpu.make_async_remote_copy(
            src_ref=self.src, dst_ref=self.out.at[self.plane], send_sem=self.send.at[r], recv_sem=self.recv.at[r],
            device_id={"dp": (self.plane + r) % self.dp}, device_id_type=MESH)

    def arrival(self, r):
        p = (self.plane - r + self.dp) % self.dp
        return pltpu.make_async_remote_copy(
            src_ref=self.src, dst_ref=self.out.at[p], send_sem=self.send.at[r], recv_sem=self.recv.at[r],
            device_id={"dp": p}, device_id_type=MESH)

    def start(self):
        for r in range(1, self.dp):
            self.copy(r).start()
        self.kept = pltpu.make_async_copy(self.src, self.out.at[self.plane], self.own)
        self.kept.start()

    def finish(self):
        self.kept.wait()
        for r in range(1, self.dp):
            self.arrival(r).wait_recv()
            self.copy(r).wait_send()


class Swap:
    def __init__(self, dp, src, out, sems):
        self.dp, self.src, self.out = dp, src, out
        self.send, self.recv = sems
        self.plane = lax.axis_index("dp")

    @staticmethod
    def scratch(dp):
        dma = pltpu.SemaphoreType.DMA
        return [dma((dp,)), dma((dp,))]

    def copy(self, r):
        to = (self.plane + r) % self.dp
        return pltpu.make_async_remote_copy(
            src_ref=self.src.at[to], dst_ref=self.out.at[r - 1], send_sem=self.send.at[r], recv_sem=self.recv.at[r],
            device_id={"dp": to}, device_id_type=MESH)

    def start(self):
        for r in range(1, self.dp):
            self.copy(r).start()

    def finish(self):
        for r in range(1, self.dp):
            self.copy(r).wait_recv()
            self.copy(r).wait_send()


def side_job(dp, span, src, out, sems):
    if span is None:
        return Swap(dp, src, out, sems)
    return Spread(dp, src.at[pl.ds(span[0], span[1])], out, sems)


def side_shape(dp, span, side):
    if span is None:
        return jax.ShapeDtypeStruct((dp - 1,) + side.shape[1:], side.dtype)
    return jax.ShapeDtypeStruct((dp, span[1], side.shape[1]), side.dtype)


def side_scratch(dp, span):
    return (Swap if span is None else Spread).scratch(dp)


def enter_all(me, plane, dp):
    barrier = pltpu.get_barrier_semaphore()
    for r in range(1, NE):
        pl.semaphore_signal(
            barrier, inc=1, device_id={"expert": (me + r) % NE}, device_id_type=MESH)
    for r in range(1, dp):
        pl.semaphore_signal(
            barrier, inc=1, device_id={"dp": (plane + r) % dp}, device_id_type=MESH)
    pl.semaphore_wait(barrier, NE - 1 + dp - 1)


class Gather:
    def __init__(self, src, out, chunks, sems, view=lambda ref, b: ref.at[b]):
        self.src, self.out, self.chunks, self.view = src, out, chunks, view
        self.rows = src.shape[0] // chunks
        (self.own_sem, self.us, self.ur, self.ds, self.dr, self.bus, self.bur, self.bds, self.bdr,
         self.xs, self.xr, self.cs, self.cr) = sems
        self.me, self.z, self.x, self.c, self.core, self.side = place()

    COUNT = 13

    @staticmethod
    def scratch(chunks):
        dma = pltpu.SemaphoreType.DMA
        return [dma] + [dma((4, chunks))] * 8 + [dma((7, chunks))] * 2 + [dma((14, chunks))] * 2

    def alt(self, k):
        return k >= (self.chunks + 1) // 2

    def order(self):
        return range(self.chunks - 1, -1, -1)

    def copy(self, block, k, src, send, recv, to):
        src_ref = self.src if src is None else self.view(self.out, src)
        dst_ref = self.view(self.out, block)
        if self.chunks > 1:
            part = pl.ds(k * self.rows, self.rows)
            src_ref, dst_ref = src_ref.at[part], dst_ref.at[part]
        return pltpu.make_async_remote_copy(
            src_ref=src_ref,
            dst_ref=dst_ref,
            send_sem=send, recv_sem=recv,
            device_id={"expert": to}, device_id_type=MESH,
        )

    def up(self, k, s, src=None):
        return self.copy(self.me - 4 * s, k, src, self.us.at[s, k], self.ur.at[s, k], self.me + 4)

    def down(self, k, s, src=None):
        return self.copy(self.me + 4 * s, k, src, self.ds.at[s, k], self.dr.at[s, k], self.me - 4)

    def up_b(self, k, s):
        b = self.side - 4 * s
        return self.copy(b, k, b, self.bus.at[s, k], self.bur.at[s, k], self.me + 4)

    def down_b(self, k, s):
        b = self.side + 4 * s
        return self.copy(b, k, b, self.bds.at[s, k], self.bdr.at[s, k], self.me - 4)

    def across(self, k, slot, block, src=None):
        return self.copy(block, k, src, self.xs.at[slot, k], self.xr.at[slot, k], self.side)

    def over(self, k, slot, block, src=None):
        return self.copy(block, k, src, self.cs.at[slot, k], self.cr.at[slot, k], self.core)

    def arrived(self, b, k, sems, s):
        return self.copy(b, k, b, sems[0].at[s - 1, k], sems[1].at[s - 1, k], self.side)

    def shift(self, base, slot):
        return base - 4 * slot if slot <= 3 else base + 4 * (slot - 3)

    def core_block(self, slot):
        if slot < 7:
            return self.shift(self.core, slot)
        return self.shift(self.core + 2 - 4 * self.x, slot - 7)

    def has(self, slot):
        slot = slot % 7
        if slot == 0:
            return self.z >= 0
        return self.z >= slot if slot <= 3 else self.z + (slot - 3) <= NZ - 1

    def crosses(self, k, slot):
        if slot == 0 or not self.alt(k):
            return self.has(slot)
        return self.z > slot if slot <= 3 else self.z + (slot - 3) < NZ - 1

    def start(self):
        z, me = self.z, self.me
        self.own = pltpu.make_async_copy(self.src, self.view(self.out, me), self.own_sem)
        self.own.start()
        for k in self.order():
            self.across(k, 0, me).start()

            @pl.when(z < NZ - 1)
            def _():
                self.up(k, 0).start()

            @pl.when(z > 0)
            def _():
                self.down(k, 0).start()

            self.over(k, 0, me).start()

    def line(self, k, s):
        z, me = self.z, self.me

        @pl.when(z >= s)
        def _():
            b = me - 4 * s
            self.arrived(b, k, (self.us, self.ur), s).wait_recv()

            @pl.when(self.crosses(k, s))
            def _():
                self.across(k, s, b, b).start()

            @pl.when(z < NZ - 1)
            def _():
                self.up(k, s, b).start()

            self.over(k, s, b, b).start()

        @pl.when(z + s <= NZ - 1)
        def _():
            b = me + 4 * s
            self.arrived(b, k, (self.ds, self.dr), s).wait_recv()

            @pl.when(self.crosses(k, 3 + s))
            def _():
                self.across(k, 3 + s, b, b).start()

            @pl.when(z > 0)
            def _():
                self.down(k, s, b).start()

            self.over(k, 3 + s, b, b).start()

    def line_b(self, k, s):
        z = self.z

        @pl.when(z == s)
        def _():
            b = self.side - 4 * s
            self.arrived(b, k, (self.bus, self.bur), s).wait_recv()

            @pl.when(z < NZ - 1)
            def _():
                self.up_b(k, s).start()

            self.over(k, 7 + s, b, b).start()

        @pl.when(z + s == NZ - 1)
        def _():
            b = self.side + 4 * s
            self.arrived(b, k, (self.bds, self.bdr), s).wait_recv()

            @pl.when(z > 0)
            def _():
                self.down_b(k, s).start()

            self.over(k, 10 + s, b, b).start()

    def from_side(self, k, slot):
        @pl.when(self.crosses(k, slot))
        def _():
            b = self.shift(self.side, slot)
            self.across(k, slot, b, b).wait_recv()
            if slot == 0 and self.alt(k):
                @pl.when(self.z == 0)
                def _():
                    self.up_b(k, 0).start()

                @pl.when(self.z == NZ - 1)
                def _():
                    self.down_b(k, 0).start()

            self.over(k, 7 + slot, b, b).start()

    def round(self, s):
        if s < NZ:
            for k in self.order():
                self.line(k, s)
        for k in self.order():
            for slot in ((0,) if s == 1 else (s - 1, s + 2)):
                self.from_side(k, slot)
        if s > 1:
            for k in self.order():
                if self.alt(k):
                    self.line_b(k, s - 1)

    def finish(self):
        z = self.z
        self.own.wait()
        for k in self.order():
            for slot in range(14):
                @pl.when(self.has(slot))
                def _():
                    b = self.core_block(slot)
                    self.over(k, slot, b, b).wait_recv()
                    self.over(k, slot, b, b).wait_send()
            for slot in range(7):
                @pl.when(self.crosses(k, slot))
                def _():
                    self.across(k, slot, self.me).wait_send()
            for s in range(NZ - 1):
                @pl.when((z >= s) & (z < NZ - 1))
                def _():
                    self.up(k, s).wait_send()

                @pl.when((z + s <= NZ - 1) & (z > 0))
                def _():
                    self.down(k, s).wait_send()

                if self.alt(k):
                    @pl.when(z == s)
                    def _():
                        self.up_b(k, s).wait_send()

                    @pl.when(z + s == NZ - 1)
                    def _():
                        self.down_b(k, s).wait_send()


def gather_kernel(chunks, dp, span, extra, x_ref, *refs):
    job = None
    ng = Gather.COUNT
    if not extra:
        o_ref, *sems = refs
    else:
        src, o_ref, out, *sems = refs
        job = side_job(dp, span, src, out, sems[ng:])
    g = Gather(x_ref, o_ref, chunks, sems[:ng])
    enter(g.me, g.z, g.core, g.side, 1 if job is None else dp)
    if job is not None:
        job.start()
    g.start()
    for s in range(1, NZ + 1):
        g.round(s)
    g.finish()
    if job is not None:
        job.finish()


COST = pl.CostEstimate(flops=0, bytes_accessed=4_000_000, transcendentals=0)
ANY = pl.BlockSpec(memory_space=pl.ANY)


def gather16(v, cid, chunks=2, dp=1, span=None, side=None):
    rows, width = v.shape
    extra = side is not None
    out = pl.pallas_call(
        functools.partial(gather_kernel, chunks, dp, span, extra),
        out_shape=(jax.ShapeDtypeStruct((NE, rows, width), v.dtype),)
        + ((side_shape(dp, span, side),) if extra else ()),
        in_specs=[ANY] * (2 if extra else 1),
        out_specs=(ANY,) * (2 if extra else 1),
        scratch_shapes=Gather.scratch(chunks) + (side_scratch(dp, span) if extra else []),
        compiler_params=pltpu.CompilerParams(collective_id=cid, has_side_effects=True),
        cost_estimate=COST,
        name="gather16",
    )(*((v, side) if extra else (v,)))
    return out if extra else out[0]


def opening_kernel(dp, chunks, x_ref, small_ref, parts_ref, out_ref,
                   x_all, small_all, parts_head, out_head, small_dp, out_dp, *sems):
    ng = Gather.COUNT
    gx = Gather(x_ref, x_all, chunks, sems[:ng])
    gs = Gather(small_dp, small_all, 1, sems[ng:2 * ng], lambda ref, b: ref.at[:, b])
    loc, ys, yr, ps, pr, os_, or_, pl_sem, ol_sem = sems[2 * ng:]
    me = gx.me
    plane = lax.axis_index("dp")
    enter_all(me, plane, dp)
    pairs = ((small_ref, small_dp), (out_ref, out_dp), (parts_head.at[plane], parts_head))

    def lift(i, r):
        src, dst = pairs[i]
        return pltpu.make_async_remote_copy(
            src_ref=src, dst_ref=dst.at[plane], send_sem=ys.at[i, r], recv_sem=yr.at[i, r],
            device_id={"dp": (plane + r) % dp}, device_id_type=MESH)

    def landed(i, r):
        p = (plane - r + dp) % dp
        dst = pairs[i][1].at[p]
        return pltpu.make_async_remote_copy(
            src_ref=dst, dst_ref=dst, send_sem=ys.at[i, r], recv_sem=yr.at[i, r],
            device_id={"dp": p}, device_id_type=MESH)

    def kept(i):
        src, dst = pairs[i]
        return pltpu.make_async_copy(src, dst.at[plane], loc.at[i])

    def part(r):
        h = (me + r) % NE
        return pltpu.make_async_remote_copy(
            src_ref=parts_ref.at[h], dst_ref=parts_head.at[plane, me],
            send_sem=ps.at[r], recv_sem=pr.at[r],
            device_id={"expert": h}, device_id_type=MESH)

    def part_in(r):
        e = (me - r + NE) % NE
        return pltpu.make_async_remote_copy(
            src_ref=parts_head.at[plane, e], dst_ref=parts_head.at[plane, e],
            send_sem=ps.at[r], recv_sem=pr.at[r],
            device_id={"expert": e}, device_id_type=MESH)

    def part_kept():
        return pltpu.make_async_copy(parts_ref.at[me], parts_head.at[plane, me], pl_sem)

    for i in range(2):
        for r in range(1, dp):
            lift(i, r).start()
        kept(i).start()
    for r in range(1, NE):
        part(r).start()
    part_kept().start()
    gx.start()
    gx.round(1)

    kept(0).wait()
    for r in range(1, dp):
        landed(0, r).wait_recv()
    gs.start()

    for r in range(1, NE):
        part_in(r).wait_recv()
    part_kept().wait()
    for r in range(1, dp):
        lift(2, r).start()
    gx.round(2)

    def row(d):
        b = NE * d + me
        return pltpu.make_async_remote_copy(
            src_ref=out_dp.at[d], dst_ref=out_head.at[b % dp],
            send_sem=os_.at[d], recv_sem=or_.at[b % dp],
            device_id={"expert": b // dp}, device_id_type=MESH)

    def row_kept(d):
        b = NE * d + me
        return pltpu.make_async_copy(out_dp.at[d], out_head.at[b % dp], ol_sem.at[d])

    kept(1).wait()
    for r in range(1, dp):
        landed(1, r).wait_recv()
    for d in range(dp):
        home = (NE * d + me) // dp

        @pl.when(home != me)
        def _():
            row(d).start()

        @pl.when(home == me)
        def _():
            row_kept(d).start()

    gs.round(1)
    gx.round(3)
    gs.round(2)
    gx.round(4)
    gs.round(3)
    gs.round(4)

    def row_in(j):
        return pltpu.make_async_remote_copy(
            src_ref=out_head.at[j], dst_ref=out_head.at[j], send_sem=os_.at[j], recv_sem=or_.at[j],
            device_id={"expert": gx.core}, device_id_type=MESH)

    for r in range(1, NE):
        part(r).wait_send()
    for j in range(dp):
        @pl.when((dp * me + j) % NE != me)
        def _():
            row_in(j).wait_recv()
    for d in range(dp):
        home = (NE * d + me) // dp

        @pl.when(home != me)
        def _():
            row(d).wait_send()

        @pl.when(home == me)
        def _():
            row_kept(d).wait()
    for r in range(1, dp):
        landed(2, r).wait_recv()
    for i in range(3):
        for r in range(1, dp):
            lift(i, r).wait_send()
    gx.finish()
    gs.finish()


def opening(dp, x, small, parts, out, cid, chunks=2):
    dma = pltpu.SemaphoreType.DMA
    rows, ws = small.shape
    bf = x.dtype
    wo = out.shape[1]
    shape = jax.ShapeDtypeStruct
    res = pl.pallas_call(
        functools.partial(opening_kernel, dp, chunks),
        out_shape=(
            shape((NE,) + x.shape, bf), shape((dp, NE, rows, ws), bf), shape((dp, NE) + parts.shape[1:], bf),
            shape((dp, rows, wo), bf),
            shape((dp, rows, ws), bf), shape((dp, rows, wo), bf),
        ),
        in_specs=[ANY] * 4,
        out_specs=[ANY] * 6,
        scratch_shapes=Gather.scratch(chunks) + Gather.scratch(1) + [
            dma((2,)), dma((3, dp)), dma((3, dp)), dma((NE,)), dma((NE,)), dma((dp,)), dma((dp,)), dma, dma((dp,))],
        compiler_params=pltpu.CompilerParams(collective_id=cid, has_side_effects=True),
        cost_estimate=COST,
        name="opening",
    )(x, small, parts, out)
    return res[:4]


def order(z, i):
    a, b = (3, 2, 1, 0)[i], (3, 2, 0, 1)[i]
    return jnp.where(z == 0, a, jnp.where(z == 1, b, jnp.where(z == 2, 3 - b, 3 - a)))


class Scatter:
    COUNT = 14

    def __init__(self, p_ref, o_ref, chunks, scratch):
        self.p, self.o, self.chunks = p_ref, o_ref, chunks
        (self.cbuf, self.own, self.xbuf, self.ubuf, self.dbuf, self.ld, self.cs, self.cr, self.xs, self.xr,
         self.us, self.ur, self.ds, self.dr) = scratch
        self.rows = o_ref.shape[0] // chunks
        self.me, self.z, self.x, self.c, self.core, self.side = place()

    @staticmethod
    def scratch(rows, width, chunks, bf):
        dma = pltpu.SemaphoreType.DMA
        return [pltpu.VMEM((n, rows, width), bf) for n in (8, 8, 4, 4, 4)] + [
            dma((8,)), dma((8, chunks)), dma((8, chunks))] + [dma((4, chunks))] * 6

    def rng(self, k):
        return pl.ds(k * self.rows, self.rows)

    def column(self, i, j):
        return 4 * order(self.z, i) + 2 * jnp.where(j == 0, 1 - self.x, self.x)

    def remote(self, src, dst, send, recv, to):
        return pltpu.make_async_remote_copy(
            src_ref=src, dst_ref=dst, send_sem=send, recv_sem=recv,
            device_id={"expert": to}, device_id_type=MESH)

    def over(self, i, j, k):
        n = 2 * i + j
        return self.remote(
            self.p.at[self.column(i, j) + 1 - self.c, self.rng(k)], self.cbuf.at[n, self.rng(k)],
            self.cs.at[n, k], self.cr.at[n, k], self.core)

    def load(self, i, j):
        n = 2 * i + j
        return pltpu.make_async_copy(self.p.at[self.column(i, j) + self.c], self.own.at[n], self.ld.at[n])

    def across(self, i, k):
        return self.remote(self.own.at[2 * i, self.rng(k)], self.xbuf.at[i, self.rng(k)],
                           self.xs.at[i, k], self.xr.at[i, k], self.side)

    def up(self, t, i, k):
        return self.remote(self.own.at[2 * i + 1, self.rng(k)], self.ubuf.at[t, self.rng(k)],
                           self.us.at[t, k], self.ur.at[t, k], self.me + 4)

    def down(self, t, i, k):
        return self.remote(self.own.at[2 * i + 1, self.rng(k)], self.dbuf.at[t, self.rng(k)],
                           self.ds.at[t, k], self.dr.at[t, k], self.me - 4)

    def start(self):
        for i in range(NZ):
            for j in range(2):
                self.load(i, j).start()
                for k in range(self.chunks):
                    self.over(i, j, k).start()

    def first(self, i):
        f32 = jnp.float32
        self.load(i, 0).wait()
        for k in range(self.chunks):
            self.over(i, 0, k).wait_recv()
            s = self.rng(k)
            self.own[2 * i, s] = (
                self.own[2 * i, s].astype(f32) + self.cbuf[2 * i, s].astype(f32)).astype(self.own.dtype)
            self.across(i, k).start()

    def second(self, i):
        f32 = jnp.float32
        z, own, o = self.z, self.own, self.o
        t = order(z, i)
        self.load(i, 1).wait()
        for k in range(self.chunks):
            s = self.rng(k)
            self.over(i, 1, k).wait_recv()
            self.across(i, k).wait_recv()

            def base():
                return (own[2 * i + 1, s].astype(f32) + self.cbuf[2 * i + 1, s].astype(f32)
                        + self.xbuf[i, s].astype(f32))

            if i < NZ - 1:
                @pl.when(t > z)
                def _():
                    @pl.when(z > 0)
                    def _():
                        self.up(t, i, k).wait_recv()
                        own[2 * i + 1, s] = (base() + self.ubuf[t, s].astype(f32)).astype(own.dtype)

                    @pl.when(z == 0)
                    def _():
                        own[2 * i + 1, s] = base().astype(own.dtype)

                    self.up(t, i, k).start()

                @pl.when(t < z)
                def _():
                    @pl.when(z < NZ - 1)
                    def _():
                        self.down(t, i, k).wait_recv()
                        own[2 * i + 1, s] = (base() + self.dbuf[t, s].astype(f32)).astype(own.dtype)

                    @pl.when(z == NZ - 1)
                    def _():
                        own[2 * i + 1, s] = base().astype(own.dtype)

                    self.down(t, i, k).start()
            else:
                @pl.when(z > 0)
                def _():
                    self.up(t, i, k).wait_recv()

                @pl.when(z < NZ - 1)
                def _():
                    self.down(t, i, k).wait_recv()

                @pl.when((z > 0) & (z < NZ - 1))
                def _():
                    o[s] = (base() + self.ubuf[t, s].astype(f32) + self.dbuf[t, s].astype(f32)).astype(o.dtype)

                @pl.when(z == 0)
                def _():
                    o[s] = (base() + self.dbuf[t, s].astype(f32)).astype(o.dtype)

                @pl.when(z == NZ - 1)
                def _():
                    o[s] = (base() + self.ubuf[t, s].astype(f32)).astype(o.dtype)

    def run(self, between=lambda: None):
        self.first(0)
        for i in range(NZ):
            if i + 1 < NZ:
                self.first(i + 1)
            between()
            self.second(i)
            between()

    def finish(self):
        z = self.z
        for k in range(self.chunks):
            for i in range(NZ):
                self.across(i, k).wait_send()
                for j in range(2):
                    self.over(i, j, k).wait_send()
                if i < NZ - 1:
                    t = order(z, i)

                    @pl.when(t > z)
                    def _():
                        self.up(t, i, k).wait_send()

                    @pl.when(t < z)
                    def _():
                        self.down(t, i, k).wait_send()


def scatter_kernel(chunks, dp, span, extra, p_ref, *refs):
    job = None
    ns = Scatter.COUNT
    if not extra:
        o_ref, *scratch = refs
    else:
        src, o_ref, out, *scratch = refs
        job = side_job(dp, span, src, out, scratch[ns:])
    s = Scatter(p_ref, o_ref, chunks, scratch[:ns])
    enter(s.me, s.z, s.core, s.side, 1 if job is None else dp)
    if job is not None:
        job.start()
    s.start()
    s.run()
    s.finish()
    if job is not None:
        job.finish()


VMEM = pl.BlockSpec(memory_space=pltpu.VMEM)


def scatter16(p, cid, chunks=2, dp=1, span=None, side=None):
    _, rows, width = p.shape
    extra = side is not None
    out = pl.pallas_call(
        functools.partial(scatter_kernel, chunks, dp, span, extra),
        out_shape=(jax.ShapeDtypeStruct((rows, width), jnp.float32),)
        + ((side_shape(dp, span, side),) if extra else ()),
        in_specs=[ANY] * (2 if extra else 1),
        out_specs=(VMEM,) + ((ANY,) if extra else ()),
        scratch_shapes=Scatter.scratch(rows, width, chunks, p.dtype) + (side_scratch(dp, span) if extra else []),
        compiler_params=pltpu.CompilerParams(
            collective_id=cid, has_side_effects=True, vmem_limit_bytes=60 * 1024 * 1024),
        cost_estimate=COST,
        name="scatter16",
    )(*((p, side) if extra else (p,)))
    return out if extra else out[0]


def return_kernel(dp, chunks, p_ref, parts_ref, rows_ref, o_ref, parts_far, rows_far, *scratch):
    ns = Scatter.COUNT
    s = Scatter(p_ref, o_ref, chunks, scratch[:ns])
    swap = Swap(dp, parts_ref, parts_far, scratch[ns:ns + 2])
    rs, rr = scratch[ns + 2:]
    plane = lax.axis_index("dp")
    keeper = s.me * dp // NE
    enter(s.me, s.z, s.core, s.side, dp)

    def row(r):
        return pltpu.make_async_remote_copy(
            src_ref=rows_ref, dst_ref=rows_far.at[r - 1], send_sem=rs.at[r], recv_sem=rr.at[r],
            device_id={"dp": (plane + r) % dp}, device_id_type=MESH)

    swap.start()
    for r in range(1, dp):
        @pl.when((plane + r) % dp == keeper)
        def _():
            row(r).start()
    s.start()
    s.run()
    s.finish()
    swap.finish()
    for r in range(1, dp):
        @pl.when((plane + r) % dp == keeper)
        def _():
            row(r).wait_send()

        @pl.when(plane == keeper)
        def _():
            row(r).wait_recv()


def returning(dp, p, parts, rows, cid, chunks=2):
    dma = pltpu.SemaphoreType.DMA
    _, n, width = p.shape
    shape = jax.ShapeDtypeStruct
    return pl.pallas_call(
        functools.partial(return_kernel, dp, chunks),
        out_shape=(
            shape((n, width), jnp.float32), shape((dp - 1,) + parts.shape[1:], parts.dtype),
            shape((dp - 1,) + rows.shape, rows.dtype)),
        in_specs=[ANY] * 3,
        out_specs=[VMEM, ANY, ANY],
        scratch_shapes=Scatter.scratch(n, width, chunks, p.dtype) + [dma((dp,))] * 4,
        compiler_params=pltpu.CompilerParams(
            collective_id=cid, has_side_effects=True, vmem_limit_bytes=60 * 1024 * 1024),
        cost_estimate=COST,
        name="returning",
    )(p, parts, rows)


def closing_kernel(dp, p_ref, parts_ref, rows_ref, o_ref, far_ref, query_ref, expand_ref, output_ref,
                   parts_in, row_in, *scratch):
    ns = Scatter.COUNT
    s = Scatter(p_ref, o_ref, 1, scratch[:ns])
    ys, yr, ps, pr, kept_sem, rs, rr = scratch[ns:]
    me = s.me
    plane = lax.axis_index("dp")
    rows = o_ref.shape[0] // dp
    enter_all(me, plane, dp)

    def lift(r):
        to = (plane + r) % dp
        return pltpu.make_async_remote_copy(
            src_ref=o_ref.at[pl.ds(pl.multiple_of(to * rows, 16), rows)], dst_ref=far_ref.at[r - 1],
            send_sem=ys.at[r], recv_sem=yr.at[r],
            device_id={"dp": to}, device_id_type=MESH)

    def part(r):
        e = (me + r) % NE
        return pltpu.make_async_remote_copy(
            src_ref=parts_ref.at[e], dst_ref=parts_in.at[me], send_sem=ps.at[r], recv_sem=pr.at[r],
            device_id={"expert": e}, device_id_type=MESH)

    def part_in(r):
        h = (me - r + NE) % NE
        return pltpu.make_async_remote_copy(
            src_ref=parts_in.at[h], dst_ref=parts_in.at[h], send_sem=ps.at[r], recv_sem=pr.at[r],
            device_id={"expert": h}, device_id_type=MESH)

    def part_kept():
        return pltpu.make_async_copy(parts_ref.at[me], parts_in.at[me], kept_sem.at[0])

    keeper = plane == me * dp // NE
    source = (NE * plane + me) // dp

    def row(j):
        return pltpu.make_async_remote_copy(
            src_ref=rows_ref.at[j], dst_ref=row_in, send_sem=rs.at[j], recv_sem=rr,
            device_id={"expert": (dp * me + j) % NE}, device_id_type=MESH)

    def row_kept(j):
        return pltpu.make_async_copy(rows_ref.at[j], row_in, kept_sem.at[1])

    s.start()
    for r in range(1, NE):
        part(r).start()
    part_kept().start()
    for j in range(dp):
        home = (dp * me + j) % NE

        @pl.when(keeper & (home != me))
        def _():
            row(j).start()

        @pl.when(keeper & (home == me))
        def _():
            row_kept(j).start()
    s.run()
    for r in range(1, dp):
        lift(r).start()
    for r in range(1, NE):
        part_in(r).wait_recv()
    part_kept().wait()
    rows_l = expand_ref.shape[0]
    f32 = jnp.float32
    for h in range(0, NE, 2):
        pair = [parts_in[h + i].astype(f32) for i in range(2)]
        query_ref[:, h * 192:(h + 2) * 192] = jnp.concatenate([v[:, :192] for v in pair], axis=1)
        for i, v in enumerate(pair):
            expand_ref[:, (h + i) * 256:(h + i + 1) * 256] = jnp.concatenate(
                [v[c * rows_l:(c + 1) * rows_l, 192:] for c in range(4)], axis=1)

    @pl.when(source != me)
    def _():
        row(0).wait_recv()

    for j in range(dp):
        home = (dp * me + j) % NE

        @pl.when(keeper & (home != me))
        def _():
            row(j).wait_send()

        @pl.when(keeper & (home == me))
        def _():
            row_kept(j).wait()
    output_ref[...] = row_in[...].astype(f32)
    for r in range(1, NE):
        part(r).wait_send()
    s.finish()
    for r in range(1, dp):
        lift(r).wait_recv()
        lift(r).wait_send()


def closing(dp, p, parts, rows, rows_l, cid):
    dma = pltpu.SemaphoreType.DMA
    _, n, width = p.shape
    shape = jax.ShapeDtypeStruct
    rows_w = parts.shape[1]
    near, far, query, expand, output = pl.pallas_call(
        functools.partial(closing_kernel, dp),
        out_shape=(
            shape((n, width), p.dtype), shape((dp - 1, n // dp, width), p.dtype),
            shape((rows_w, NE * 192), jnp.float32), shape((rows_l, NE * 256), jnp.float32),
            shape(rows.shape[1:], jnp.float32)),
        in_specs=[ANY] * 3,
        out_specs=[VMEM] * 5,
        scratch_shapes=[pltpu.VMEM(parts.shape, parts.dtype), pltpu.VMEM(rows.shape[1:], rows.dtype)]
        + Scatter.scratch(n, width, 1, p.dtype)
        + [dma((dp,)), dma((dp,)), dma((NE,)), dma((NE,)), dma((2,)), dma((dp,)), dma],
        compiler_params=pltpu.CompilerParams(
            collective_id=cid, has_side_effects=True, vmem_limit_bytes=60 * 1024 * 1024),
        cost_estimate=COST,
        name="closing",
    )(p, parts, rows)
    own = lax.dynamic_slice_in_dim(near, lax.axis_index("dp") * (n // dp), n // dp).astype(jnp.float32)
    return own + jnp.sum(far.astype(jnp.float32), axis=0), query, expand, output
BF = jnp.bfloat16
F32 = jnp.float32


def mm(a, b):
    return jnp.dot(a, b, preferred_element_type=F32)


def mm_t(a, b):
    return lax.dot_general(a, b, (((1,), (1,)), ((), ())), preferred_element_type=F32)


def silu_pair(gate_in):
    sigmoid = 1.0 / (1.0 + jnp.exp(-gate_in))
    return (gate_in * sigmoid, sigmoid * (1.0 + gate_in * (1.0 - sigmoid)))


TILE = 256
WIDE = 512
SHARE = 176


def down_copies(parts, out, sem, which):
    dp = parts[0].shape[0]
    sizes = [part.shape[1] for part in parts]
    rows, first = sum(sizes), sum(sizes[:which])
    return [
        pltpu.make_async_copy(
            parts[which].at[d], out.at[pl.ds(d * rows + first, sizes[which])], sem.at[len(parts) * d + which])
        for d in range(dp)
    ]


def share_copies(share_ref, fan, down, sem):
    dp, rows, w = share_ref.shape
    n = rows // 3
    copies = []
    for d in range(dp):
        cols = pl.ds(d * w, w)
        for i, (dst, first) in enumerate(((fan, 0), (fan, TILE), (down, 0))):
            copies.append(pltpu.make_async_copy(
                share_ref.at[d, pl.ds(i * n, n)], dst.at[pl.ds(first, n), cols], sem.at[3 * d + i]))
    return copies


def share_blank(fan, down):
    pad = jnp.zeros((TILE - SHARE, fan.shape[1]), BF)
    fan[SHARE:TILE] = pad
    fan[TILE + SHARE:] = pad
    down[SHARE:] = pad


def valid_of(len_ref, first_device, tokens, batches, here):
    n = lax.broadcasted_iota(jnp.int32, (tokens, 1), 0)
    if here & (here - 1) or batches & (batches - 1):
        device, batch, place_in = n // (batches * here), (n // here) % batches, n % here
    else:
        bits, more = here.bit_length() - 1, (batches * here).bit_length() - 1
        device, batch, place_in = n >> more, (n >> bits) & (batches - 1), n & (here - 1)
    position = (first_device + device) * here + place_in
    length = jnp.zeros((tokens, 1), jnp.int32)
    for b in range(batches):
        length = jnp.where(batch == b, len_ref[b], length)
    return (position < length).astype(F32)


def slot_tables(here, slots=128):
    n = np.arange(256)
    same = n[:, None] // here == n[None, :] // here
    before = same & (n[None, :] < n[:, None])
    tables = np.stack([before, before.T, np.eye(256, dtype=bool)]).astype(np.float32)
    base = np.broadcast_to((n // here * 32)[:, None], (256, slots)).astype(np.float32)
    return jnp.asarray(tables, BF), jnp.asarray(base), jnp.asarray(base.T)


def one_hots(taken, tables, base_c, base_r, groups, slots):
    lane = lax.broadcasted_iota(jnp.int32, (256, slots), 1).astype(F32)
    row = lax.broadcasted_iota(jnp.int32, (slots, 256), 0).astype(F32)
    to_slot, to_token = [], []
    for g in range(groups):
        t = jnp.broadcast_to(taken[g * 256:(g + 1) * 256], (256, slots))
        low = t.astype(BF)
        place_c = mm(tables[0], low) + base_c[...]
        place_r = mm_lead(low, tables[1]) + base_r[...]
        taken_r = mm_lead(low, tables[2])
        to_token.append(jnp.where((place_c == lane) & (t > 0.5), 1.0, 0.0).astype(BF))
        to_slot.append(jnp.where((place_r == row) & (taken_r > 0.5), 1.0, 0.0).astype(BF))
    return to_slot, to_token


def mm_lead(a, b):
    return lax.dot_general(a, b, (((0,), (0,)), ((), ())), preferred_element_type=F32)


def lanes(j):
    return pl.ds(pl.multiple_of(j * WIDE, WIDE), WIDE)


def over_columns(total, body):
    def step(j, _):
        body(pl.multiple_of(j * WIDE, WIDE), WIDE)
        return 0

    lax.fori_loop(0, total // WIDE, step, 0)
    if total % WIDE:
        body(total // WIDE * WIDE, total % WIDE)


def forward_kernel(chunks, dp, span, batches, here, len_ref, pick_ref, mix_ref, mask_ref, tab_ref, basec_ref, baser_ref, wg_ref, wu_ref, router_ref,
                   share_ref, wda_ref, wdb_ref, down_ref, dy_ref,
                   out_ref, rows_ref, hid_ref, act_ref, slo_ref, eo_ref, sh_ref, sact_ref, sslo_ref, gate_ref,
                   slot_ref, token_ref, dy_all, wdc_ref,
                   wd_ref, fan_ref, sd_ref, hid_buf, sh_buf, gate_buf, token_buf, wd_sem, sh_sem, *sems):
    step = pl.program_id(0)
    tokens, width = mix_ref.shape
    groups, slots = tokens // 256, 128
    half = groups * slots
    ff = hid_ref.shape[1]
    phase = pl.num_programs(0) // 2
    g = Gather(dy_ref, dy_all, chunks, sems[:Gather.COUNT])
    job = side_job(dp, span, down_ref, wdc_ref, sems[Gather.COUNT:])
    parts = (wda_ref, wdb_ref, wdc_ref)

    @pl.when(step == 0)
    def _():
        enter(g.me, g.z, g.core, g.side, dp)
        job.start()
        g.start()
        copies = share_copies(share_ref, fan_ref, sd_ref, sh_sem)
        for copy in copies + down_copies(parts, wd_ref, wd_sem, 0) + down_copies(parts, wd_ref, wd_sem, 1):
            copy.start()
        share_blank(fan_ref, sd_ref)
        fan_ref[SHARE:SHARE + 16] = router_ref[...]
        for copy in copies:
            copy.wait()

    @pl.when(step < phase)
    def _():
        mix = mix_ref[...]
        fanned = mm_t(mix, fan_ref[:TILE, :])
        s_up = mm_t(mix, fan_ref[TILE:, :])
        s_act, s_slope = silu_pair(fanned)
        s_hidden = (s_act * s_up).astype(BF)
        at = pl.ds(pl.multiple_of(step * tokens, tokens), tokens)
        sh_ref[...] = s_hidden
        sh_buf[at] = s_hidden
        sact_ref[...] = s_act.astype(BF)
        sslo_ref[...] = (s_up * s_slope).astype(BF)
        logits = fanned[:, SHARE:SHARE + 16]
        mask = mask_ref[...].astype(F32)
        taken = jnp.sum(mask * pick_ref[:, :16], axis=1, keepdims=True) * valid_of(len_ref, step * (tokens // (batches * here)), tokens, batches, here)
        held = jnp.where(mask > 0.5, logits, -1e30)
        raised = jnp.exp(held - jnp.max(held, axis=1, keepdims=True)) * mask
        gate = jnp.sum(raised * pick_ref[:, :16], axis=1, keepdims=True) / jnp.sum(raised, axis=1, keepdims=True) * taken
        gate_ref[...] = gate
        gate_buf[at] = gate
        to_slot, to_token = one_hots(taken, tab_ref, basec_ref, baser_ref, groups, slots)
        for n in range(groups):
            slot_ref[n * slots:(n + 1) * slots] = to_slot[n]
            token_ref[n * 256:(n + 1) * 256] = to_token[n]
            token_buf[pl.ds(pl.multiple_of(step * tokens + n * 256, 256), 256)] = to_token[n]

        def dispatch(j, _):
            for n in range(groups):
                rows_ref[n * slots:(n + 1) * slots, lanes(j)] = mm(
                    to_slot[n], mix_ref[n * 256:(n + 1) * 256, lanes(j)]).astype(BF)
            return 0

        lax.fori_loop(0, width // WIDE, dispatch, 0)
        rows_at = pl.ds(pl.multiple_of(step * half, half), half)

        def fan_in(start, size):
            cols = pl.ds(start, size)
            gate_in = mm(rows_ref[...], wg_ref[:, cols])
            up_in = mm(rows_ref[...], wu_ref[:, cols])
            act, slope = silu_pair(gate_in)
            hidden = (act * up_in).astype(BF)
            hid_ref[:, cols] = hidden
            hid_buf[rows_at, cols] = hidden
            act_ref[:, cols] = act.astype(BF)
            slo_ref[:, cols] = (up_in * slope).astype(BF)

        over_columns(ff, fan_in)

    @pl.when(step == phase)
    def _():
        job.finish()
        for copy in down_copies(parts, wd_ref, wd_sem, 2):
            copy.start()
        for which in range(3):
            for copy in down_copies(parts, wd_ref, wd_sem, which):
                copy.wait()

    @pl.when(step >= phase)
    def _():
        tile = step - phase
        at = pl.ds(pl.multiple_of(tile * tokens, tokens), tokens)
        rows_at = pl.ds(pl.multiple_of(tile * half, half), half)
        gate = gate_buf[at]
        s_hidden = sh_buf[at]
        to_token = [token_buf[pl.ds(pl.multiple_of(tile * tokens + n * 256, 256), 256)] for n in range(groups)]

        def fan_out(j, _):
            eo = mm(hid_buf[rows_at], wd_ref[:, lanes(j)]).astype(BF)
            eo_ref[:, lanes(j)] = eo
            shared = mm(s_hidden, sd_ref[:, lanes(j)])
            picked = jnp.concatenate(
                [mm(to_token[n], eo[n * slots:(n + 1) * slots]) for n in range(groups)], axis=0)
            out_ref[:, lanes(j)] = (shared + gate * picked).astype(BF)
            return 0

        lax.fori_loop(0, width // WIDE, fan_out, 0)

    for r, s in ((1, 1), (2, 2), (3, 3), (4, 5)):
        @pl.when(step == s)
        def _():
            g.round(r)

    @pl.when(step == 2 * phase - 1)
    def _():
        g.finish()


def backward_kernel(chunks, pick_ref, dy_ref, wg_ref, wu_ref, share_ref, wda_ref, wdb_ref, wdc_ref,
                    act_ref, slo_ref, eo_ref, sact_ref, sslo_ref, gate_ref, slot_ref, token_ref, part_ref,
                    dh_ref, deo_ref, dg_ref, du_ref, ds_ref, sum_ref,
                    wd_ref, fan_ref, sd_ref, wd_sem, sh_sem, *scratch):
    step = pl.program_id(0)
    tokens, width = dy_ref.shape
    groups, slots = tokens // 256, 128
    ff = dg_ref.shape[1]
    sc = Scatter(part_ref, sum_ref, chunks, scratch)

    @pl.when(step == 0)
    def _():
        enter(sc.me, sc.z, sc.core, sc.side)
        copies = share_copies(share_ref, fan_ref, sd_ref, sh_sem)
        for which in range(3):
            copies += down_copies((wda_ref, wdb_ref, wdc_ref), wd_ref, wd_sem, which)
        for copy in copies:
            copy.start()
        sc.start()
        share_blank(fan_ref, sd_ref)
        for copy in copies:
            copy.wait()

    d_sh = mm_t(dy_ref[...], sd_ref[...])
    d_s = jnp.concatenate([(d_sh * sslo_ref[...].astype(F32)).astype(BF),
                           (d_sh * sact_ref[...].astype(F32)).astype(BF)], axis=1)
    ds_ref[...] = d_s
    gate = gate_ref[...]
    to_slot = [slot_ref[n * slots:(n + 1) * slots] for n in range(groups)]
    to_token = [token_ref[n * 256:(n + 1) * 256] for n in range(groups)]

    @pl.when(step == 0)
    def _():
        sc.first(0)
        sc.first(1)

    def dispatch(j, total):
        dy = dy_ref[:, lanes(j)].astype(F32)
        gated = (gate * dy).astype(BF)
        for n in range(groups):
            deo_ref[n * slots:(n + 1) * slots, lanes(j)] = mm(to_slot[n], gated[n * 256:(n + 1) * 256]).astype(BF)
        picked = jnp.concatenate(
            [mm(to_token[n], eo_ref[n * slots:(n + 1) * slots, lanes(j)]) for n in range(groups)], axis=0)
        return total + jnp.sum(dy * picked, axis=1, keepdims=True)

    d_gates = lax.fori_loop(0, width // WIDE, dispatch, jnp.zeros((tokens, 1), F32))

    def back_out(start, size):
        cols = pl.ds(start, size)
        d_eh = mm_t(deo_ref[...], wd_ref[cols, :])
        dg_ref[:, cols] = (d_eh * slo_ref[:, cols].astype(F32)).astype(BF)
        du_ref[:, cols] = (d_eh * act_ref[:, cols].astype(F32)).astype(BF)

    over_columns(ff, back_out)

    @pl.when(step == 0)
    def _():
        sc.first(2)
        sc.first(3)

    def back_in(j, _):
        d_rows = (mm_t(dg_ref[...], wg_ref[lanes(j), :]) + mm_t(du_ref[...], wu_ref[lanes(j), :])).astype(BF)
        shared = mm(d_s, fan_ref[:, lanes(j)])
        taken_rows = jnp.concatenate(
            [mm(to_token[n], d_rows[n * slots:(n + 1) * slots]) for n in range(groups)], axis=0)
        dh_ref[:, lanes(j)] = (shared + taken_rows).astype(BF)
        return 0

    lax.fori_loop(0, width // WIDE, back_in, 0)
    high = d_gates.astype(BF).astype(F32)
    dh_ref[:, width:] = (high * pick_ref[:, :128] + (d_gates - high) * pick_ref[:, 128:]).astype(BF)

    outer = (sc.z == 0) | (sc.z == NZ - 1)
    for i in range(NZ - 1):
        @pl.when((step == i) & outer)
        def _():
            sc.second(i)

        @pl.when((step == min(i + 1, 2)) & jnp.logical_not(outer))
        def _():
            sc.second(i)

    @pl.when(step == NZ - 1)
    def _():
        sc.second(NZ - 1)
        sc.finish()


def whole(v):
    zeros = (0,) * v.ndim
    return pl.BlockSpec(v.shape, lambda i: zeros, pipeline_mode=pl.Buffered(buffer_count=1))


def tiles(rows, w):
    return pl.BlockSpec((rows, w), lambda i: (i, 0))


SMEM = pl.BlockSpec(memory_space=pltpu.SMEM)


def mixture_forward(dp, batches, here, lengths, pick, mix, mask, wg, wu, router, share, wda, wdb, span, down, dy, cid,
                    chunks=2):
    total, width = mix.shape
    step, half = total // 4, total // 8
    ff = wg.shape[1]
    tables = slot_tables(here)
    shape = jax.ShapeDtypeStruct
    rows = total // 2
    dma = pltpu.SemaphoreType.DMA

    def early(n, w):
        return pl.BlockSpec((n, w), lambda i: (jnp.minimum(i, 3), 0))

    def late(n, w):
        return pl.BlockSpec((n, w), lambda i: (jnp.maximum(i - 4, 0), 0))

    return pl.pallas_call(
        functools.partial(forward_kernel, chunks, dp, span, batches, here),
        grid=(8,),
        out_shape=(
            shape((total, width), BF), shape((rows, width), BF), shape((rows, ff), BF), shape((rows, ff), BF),
            shape((rows, ff), BF), shape((rows, width), BF), shape((total, TILE), BF), shape((total, TILE), BF),
            shape((total, TILE), BF), shape((total, 1), F32), shape((rows, 256), BF), shape((total, 128), BF),
            shape((NE,) + dy.shape, BF),
            shape((dp, span[1], width), BF)),
        in_specs=[SMEM, whole(pick), early(step, width), early(step, mask.shape[1])] + [whole(v) for v in tables] + [whole(wg), whole(wu),
                  whole(router), ANY, ANY, ANY, ANY, ANY],
        out_specs=[late(step, width), early(half, width), early(half, ff), early(half, ff), early(half, ff),
                   late(half, width), early(step, TILE), early(step, TILE), early(step, TILE), early(step, 1),
                   early(half, 256), early(step, 128), ANY, ANY],
        scratch_shapes=[
            pltpu.VMEM((ff, width), BF), pltpu.VMEM((2 * TILE, width), BF), pltpu.VMEM((TILE, width), BF),
            pltpu.VMEM((rows, ff), BF), pltpu.VMEM((total, TILE), BF), pltpu.VMEM((total, 1), F32),
            pltpu.VMEM((total, 128), BF), dma((3 * dp,)), dma((3 * dp,))] + Gather.scratch(chunks) + Spread.scratch(dp),
        compiler_params=pltpu.CompilerParams(
            collective_id=cid, has_side_effects=True, vmem_limit_bytes=60 * 1024 * 1024),
        cost_estimate=COST,
        name="mixture_forward",
    )(lengths, pick, mix, mask, *tables, wg, wu, router, share, wda, wdb, down, dy)


def mixture_backward(pick, dy, wg, wu, share, wda, wdb, wdc, act, slo, eo, sact, sslo, gate, slot, token, part, cid, chunks=2):
    total, width = dy.shape
    step, half = total // NZ, total // NZ // 2
    ff = wg.shape[1]
    shape = jax.ShapeDtypeStruct
    rows = total // 2
    dp = wda.shape[0]
    _, own, _ = part.shape
    dma = pltpu.SemaphoreType.DMA
    return pl.pallas_call(
        functools.partial(backward_kernel, chunks),
        grid=(NZ,),
        out_shape=(
            shape((total, width + 128), BF), shape((rows, width), BF), shape((rows, ff), BF), shape((rows, ff), BF),
            shape((total, 2 * TILE), BF), shape((own, width), F32)),
        in_specs=[whole(pick), tiles(step, width), whole(wg), whole(wu), ANY, ANY, ANY, ANY,
                  tiles(half, ff), tiles(half, ff), tiles(half, width), tiles(step, TILE), tiles(step, TILE),
                  tiles(step, 1), tiles(half, 256), tiles(step, 128), ANY],
        out_specs=[tiles(step, width + 128), tiles(half, width), tiles(half, ff), tiles(half, ff),
                   tiles(step, 2 * TILE), pl.BlockSpec((own, width), lambda i: (0, 0))],
        scratch_shapes=[
            pltpu.VMEM((ff, width), BF), pltpu.VMEM((2 * TILE, width), BF), pltpu.VMEM((TILE, width), BF),
            dma((3 * dp,)), dma((3 * dp,))] + Scatter.scratch(own, width, chunks, BF),
        compiler_params=pltpu.CompilerParams(
            collective_id=cid, has_side_effects=True, vmem_limit_bytes=62 * 1024 * 1024),
        cost_estimate=COST,
        name="mixture_backward",
    )(pick, dy, wg, wu, share, wda, wdb, wdc, act, slo, eo, sact, sslo, gate, slot, token, part)


class ShareWork:
    ROWS = 256

    def __init__(self, ds_ref, sh_ref, mix_ref, dy_ref, out_ref, scratch):
        self.sources = (ds_ref, sh_ref, mix_ref, dy_ref)
        self.out = out_ref
        *self.buffers, self.gfan, self.gsd, self.sem = scratch
        self.steps = mix_ref.shape[0] // self.ROWS
        self.done = 0

    @staticmethod
    def scratch(width):
        r = ShareWork.ROWS
        return [pltpu.VMEM((2, r, w), BF) for w in (2 * TILE, TILE, width, width)] + [
            pltpu.VMEM((2 * TILE, width), F32), pltpu.VMEM((TILE, width), F32), pltpu.SemaphoreType.DMA((2, 4))]

    COUNT = 7

    def copies(self, n):
        return [pltpu.make_async_copy(src.at[pl.ds(n * self.ROWS, self.ROWS)], buf.at[n % 2], self.sem.at[n % 2, i])
                for i, (src, buf) in enumerate(zip(self.sources, self.buffers))]

    def start(self):
        for copy in self.copies(0):
            copy.start()
        self.gfan[...] = jnp.zeros_like(self.gfan)
        self.gsd[...] = jnp.zeros_like(self.gsd)

    def step(self):
        n = self.done
        if n == self.steps:
            return
        self.done += 1
        for copy in self.copies(n):
            copy.wait()
        if n + 1 < self.steps:
            for copy in self.copies(n + 1):
                copy.start()
        ds, sh, mix, dy = self.buffers

        def columns(j, _):
            self.gfan[:, lanes(j)] += mm_lead(ds[n % 2], mix[n % 2, :, lanes(j)])
            self.gsd[:, lanes(j)] += mm_lead(sh[n % 2], dy[n % 2, :, lanes(j)])
            return 0

        lax.fori_loop(0, mix.shape[2] // WIDE, columns, 0)

    def finish(self):
        while self.done < self.steps:
            self.step()
        dp, rows, w = self.out.shape
        n = rows // 3
        for d in range(dp):
            cols = slice(d * w, (d + 1) * w)
            self.out[d, :n] = self.gfan[:n, cols].astype(BF)
            self.out[d, n:2 * n] = self.gfan[TILE:TILE + n, cols].astype(BF)
            self.out[d, 2 * n:] = self.gsd[:n, cols].astype(BF)


class WeightWork:
    COUNT = 6
    ROWS = 256

    def __init__(self, lhs, rhs, outs, scratch):
        self.sources, self.outs = (lhs,) + tuple(rhs), outs
        *self.held, self.buf, self.in_sem, self.out_sem = scratch
        self.steps = lhs.shape[1] // self.ROWS

    @staticmethod
    def scratch(lhs, rhs):
        dma = pltpu.SemaphoreType.DMA
        return [pltpu.VMEM(v.shape, BF) for v in (lhs,) + tuple(rhs)] + [
            pltpu.VMEM((2, WeightWork.ROWS, rhs[0].shape[1]), BF), dma((3,)), dma((2,))]

    def loads(self):
        return [pltpu.make_async_copy(v, held, self.in_sem.at[i])
                for i, (v, held) in enumerate(zip(self.sources, self.held))]

    def start(self):
        for copy in self.loads():
            copy.start()

    def ready(self):
        for copy in self.loads():
            copy.wait()

    def store(self, p, n):
        at = pl.ds(pl.multiple_of(n * self.ROWS, self.ROWS), self.ROWS)
        return pltpu.make_async_copy(self.buf.at[p], self.outs[p].at[at], self.out_sem.at[p])

    def step(self, begin, end):
        def body(n, _):
            left = self.held[0][:, pl.ds(pl.multiple_of(n * self.ROWS, self.ROWS), self.ROWS)]
            for p in range(2):
                @pl.when(n > 0)
                def _():
                    self.store(p, n - 1).wait()

                rhs = self.held[1 + p]
                width = rhs.shape[1]
                for at in range(0, width, WIDE):
                    size = min(WIDE, width - at)
                    self.buf[p, :, at:at + size] = mm_lead(left, rhs[:, at:at + size]).astype(BF)
                self.store(p, n).start()
            return 0

        lax.fori_loop(begin, end, body, 0)

    def finish(self):
        for p in range(2):
            self.store(p, self.steps - 1).wait()


def scatter_share_kernel(chunks, dp, p_ref, ds_ref, sh_ref, mix_ref, dy_ref, rows_ref, dg_ref, du_ref, down_ref,
                         o_ref, g_ref, ggate_ref, gup_ref, far_ref, *scratch):
    ns, nw = Scatter.COUNT, ShareWork.COUNT
    s = Scatter(p_ref, o_ref, chunks, scratch[:ns])
    share = ShareWork(ds_ref, sh_ref, mix_ref, dy_ref, g_ref, scratch[ns:ns + nw])
    work = WeightWork(rows_ref, (dg_ref, du_ref), (ggate_ref, gup_ref), scratch[ns + nw:-2])
    swap = Swap(dp, down_ref, far_ref, scratch[-2:])
    enter(s.me, s.z, s.core, s.side, dp)
    swap.start()
    s.start()
    work.start()
    share.start()
    s.first(0)
    s.first(1)
    work.ready()
    third = work.steps // 3
    work.step(0, third)
    s.second(0)
    s.first(2)
    s.first(3)
    work.step(third, 2 * third)
    s.second(1)
    work.step(2 * third, work.steps)
    s.second(2)
    work.finish()
    while share.done < share.steps:
        share.step()
    s.second(3)
    share.finish()
    s.finish()
    swap.finish()


def scatter_share(p, ds, sh, mix, dy, rows, dg, du, down, share_shape, cid, chunks=2):
    _, n, width = p.shape
    shape = jax.ShapeDtypeStruct
    grad = shape((rows.shape[1], dg.shape[1]), BF)
    return pl.pallas_call(
        functools.partial(scatter_share_kernel, chunks, down.shape[0]),
        out_shape=(shape((n, width), F32), shape(share_shape, BF), grad, grad,
                   shape((down.shape[0] - 1,) + down.shape[1:], BF)),
        in_specs=[ANY] * 9,
        out_specs=(VMEM, VMEM, ANY, ANY, ANY),
        scratch_shapes=Scatter.scratch(n, width, chunks, p.dtype) + ShareWork.scratch(mix.shape[1])
        + WeightWork.scratch(rows, (dg, du)) + Swap.scratch(down.shape[0]),
        compiler_params=pltpu.CompilerParams(
            collective_id=cid, has_side_effects=True, vmem_limit_bytes=60 * 1024 * 1024),
        cost_estimate=COST,
        name="scatter_share",
    )(p, ds, sh, mix, dy, rows, dg, du, down)


def turn(v, cosine, sine):
    half = v.shape[1] // 2
    a, b = v[:, :half], v[:, half:]
    return jnp.concatenate([a * cosine - b * sine, b * cosine + a * sine], axis=1)


def project_kernel(x_ref, gain_ref, lgain_ref, wq_ref, wl_ref, we_ref, cos_ref, sin_ref,
                   h_ref, q_ref, k_ref, v_ref, lat_ref):
    blocks = x_ref.shape[0]
    batches, rows, _ = q_ref.shape
    here = rows // blocks
    x = x_ref[...].reshape(blocks * batches * here, x_ref.shape[2]).astype(F32)
    h = x * lax.rsqrt(jnp.mean(x * x, axis=1, keepdims=True) + 1e-6) * gain_ref[...]
    h = h.astype(BF)
    h_ref[...] = h
    raw = mm(h, wq_ref[...])
    raw_lat = mm(h, wl_ref[...])
    cosine, sine = cos_ref[...], sin_ref[...]
    zeros = jnp.zeros((raw.shape[0], 64), BF)
    q = jnp.concatenate([raw[:, :128].astype(BF), turn(raw[:, 128:192], cosine, sine).astype(BF), zeros], axis=1)
    k_rope = turn(raw_lat[:, 512:576], cosine, sine).astype(BF)
    lat = raw_lat[:, :512]
    lat = (lat * lax.rsqrt(jnp.mean(lat * lat, axis=1, keepdims=True) + 1e-6) * lgain_ref[...]).astype(BF)
    expanded = mm(lat, we_ref[...]).astype(BF)
    k = jnp.concatenate([expanded[:, :128], k_rope, zeros], axis=1)
    for e in range(blocks):
        for m in range(batches):
            src = slice((e * batches + m) * here, (e * batches + m + 1) * here)
            dst = slice(e * here, (e + 1) * here)
            q_ref[m, dst] = q[src]
            k_ref[m, dst] = k[src]
            v_ref[m, dst] = expanded[src, 128:]
            lat_ref[m, dst] = lat[src]


def project(x_all, gain, lgain, wq, wl, we, cosine, sine, batches):
    groups, rows, width = x_all.shape
    here = rows // batches
    per = 4
    seq = groups * here
    shape = jax.ShapeDtypeStruct

    def whole(v):
        return pl.BlockSpec(v.shape, lambda i: (0, 0))

    def by_seq(w):
        return pl.BlockSpec((batches, per * here, w), lambda i: (0, i, 0))

    table = pl.BlockSpec((per * rows, 32), lambda i: (i, 0))
    return pl.pallas_call(
        project_kernel,
        grid=(groups // per,),
        out_shape=(shape((groups * rows, width), BF), shape((batches, seq, 256), BF), shape((batches, seq, 256), BF),
                   shape((batches, seq, 128), BF), shape((batches, seq, 512), BF)),
        in_specs=[pl.BlockSpec((per, rows, width), lambda i: (i, 0, 0)), whole(gain), whole(lgain), whole(wq), whole(wl), whole(we),
                  table, table],
        out_specs=[pl.BlockSpec((per * rows, width), lambda i: (i, 0)), by_seq(256), by_seq(256), by_seq(128), by_seq(512)],
        compiler_params=pltpu.CompilerParams(vmem_limit_bytes=48 * 1024 * 1024),
        cost_estimate=pl.CostEstimate(flops=7_000_000_000, bytes_accessed=20_000_000, transcendentals=0),
        name="project",
    )(x_all, gain, lgain, wq, wl, we, cosine, sine)


ROWS = 256
SCALE = 192.0 ** -0.5


def held_scores(q, k, first, length):
    s = mm_t(q, k) * SCALE
    t = lax.broadcasted_iota(jnp.int32, s.shape, 0) + first
    u = lax.broadcasted_iota(jnp.int32, s.shape, 1)
    return jnp.where((u <= t) & (u < length), s, -1e30)


def attend_kernel(len_ref, q_ref, k_ref, v_ref, wo_ref, part_ref, att_ref, lse_ref):
    length = len_ref[pl.program_id(0)]
    seq = q_ref.shape[1]
    groups, _, here, width = part_ref.shape
    for i in range(seq // ROWS):
        tile = slice(i * ROWS, (i + 1) * ROWS)
        ext = (i + 1) * ROWS
        s = held_scores(q_ref[0, tile], k_ref[0, :ext], i * ROWS, length)
        peak = jnp.max(s, axis=1, keepdims=True)
        raised = jnp.exp(s - peak)
        total = jnp.sum(raised, axis=1, keepdims=True)
        lse_ref[0, tile] = peak + jnp.log(total)
        p = (raised / total).astype(BF)
        att = mm(p, v_ref[0, :ext]).astype(BF)
        per = ROWS // here
        att_ref[i * per:(i + 1) * per, 0] = att.reshape(per, here, att.shape[1])
        for j in range(width // 512):
            cols = slice(j * 512, (j + 1) * 512)
            part_ref[i * per:(i + 1) * per, 0, :, cols] = mm(att, wo_ref[:, cols]).astype(BF).reshape(per, here, 512)


def attend(lengths, q, k, v, wo, groups):
    batches, seq, _ = q.shape
    here = seq // groups
    width = wo.shape[1]
    shape = jax.ShapeDtypeStruct

    def by_seq(w):
        return pl.BlockSpec((1, seq, w), lambda m: (m, 0, 0))

    def by_dev(w):
        return pl.BlockSpec((groups, 1, here, w), lambda m: (0, m, 0, 0))

    return pl.pallas_call(
        attend_kernel,
        grid=(batches,),
        out_shape=(shape((groups, batches, here, width), BF), shape((groups, batches, here, 128), BF),
                   shape((batches, seq, 1), F32)),
        in_specs=[pl.BlockSpec(memory_space=pltpu.SMEM), by_seq(256), by_seq(256), by_seq(128),
                  pl.BlockSpec(wo.shape, lambda m: (0, 0))],
        out_specs=[by_dev(width), by_dev(128), by_seq(1)],
        compiler_params=pltpu.CompilerParams(vmem_limit_bytes=48 * 1024 * 1024),
        cost_estimate=pl.CostEstimate(flops=4_000_000_000, bytes_accessed=15_000_000, transcendentals=2_000_000),
        name="attend",
    )(lengths, q, k, v, wo)


def attend_back_kernel(len_ref, dout_ref, h_ref, q_ref, k_ref, v_ref, lat_ref, att_ref, lse_ref, wo_ref, wq_ref, we_ref,
                       cos_ref, sin_ref, part_ref, gwq_ref, gwo_out, gwe_out, dk, dv, datt, gwq, gwo_ref, gwe_ref):
    m = pl.program_id(0)
    length = len_ref[m]
    seq = q_ref.shape[1]
    groups, _, here, width = dout_ref.shape
    per = ROWS // here

    @pl.when(m == 0)
    def _():
        gwo_ref[...] = jnp.zeros_like(gwo_ref)
        gwe_ref[...] = jnp.zeros_like(gwe_ref)
        gwq[...] = jnp.zeros_like(gwq)

    for j in range(4):
        blocks = slice(j * groups // 4, (j + 1) * groups // 4)
        dout = dout_ref[blocks].reshape(seq // 4, width)
        rows = slice(j * seq // 4, (j + 1) * seq // 4)
        datt[rows] = mm_t(dout, wo_ref[...]).astype(BF)
        gwo_ref[...] += mm_lead(att_ref[blocks].reshape(seq // 4, 128), dout)
    dk[...] = jnp.zeros_like(dk)
    dv[...] = jnp.zeros_like(dv)
    for i in range(seq // ROWS):
        tile = slice(i * ROWS, (i + 1) * ROWS)
        ext = (i + 1) * ROWS
        q = q_ref[0, tile]
        p = jnp.exp(held_scores(q, k_ref[0, :ext], i * ROWS, length) - lse_ref[0, tile])
        da = datt[tile]
        dp = mm_t(da, v_ref[0, :ext])
        inner = jnp.sum(dp * p, axis=1, keepdims=True)
        ds = (p * (dp - inner)).astype(BF)
        dq = mm(ds, k_ref[0, :ext]) * SCALE
        dk[:ext] += mm_lead(ds, q)
        dv[:ext] += mm_lead(p.astype(BF), da)
        rope = turn(dq[:, 128:192], cos_ref[tile], -sin_ref[tile])
        dq = jnp.concatenate([dq[:, :128].astype(BF), rope.astype(BF), jnp.zeros((ROWS, 64), BF)], axis=1)
        hidden = h_ref[i * per:(i + 1) * per, 0].reshape(ROWS, width)
        for j in range(width // 512):
            cols = slice(j * 512, (j + 1) * 512)
            gwq[:, cols] += mm_lead(dq, hidden[:, cols])
        for j in range(width // 512):
            cols = slice(j * 512, (j + 1) * 512)
            part_ref[i * per:(i + 1) * per, 0, :, cols] = mm_t(dq, wq_ref[cols]).astype(BF).reshape(per, here, 512)
    for i in range(seq // ROWS):
        tile = slice(i * ROWS, (i + 1) * ROWS)
        d_k = dk[tile] * SCALE
        d_exp = jnp.concatenate([d_k[:, :128].astype(BF), dv[tile].astype(BF)], axis=1)
        gwe_ref[...] += mm_lead(lat_ref[0, tile], d_exp)
        d_lat = mm_t(d_exp, we_ref[...]).astype(BF)
        tail = jnp.concatenate([d_lat, d_k[:, 128:].astype(BF)], axis=1)
        pad = part_ref.shape[3] - width - tail.shape[1]
        if pad > 0:
            tail = jnp.concatenate([tail, jnp.zeros((ROWS, pad), BF)], axis=1)
        part_ref[i * per:(i + 1) * per, 0, :, width:] = tail[:, :part_ref.shape[3] - width].reshape(per, here, -1)

    @pl.when(m == pl.num_programs(0) - 1)
    def _():
        for j in range(width // 256):
            cols = slice(j * 256, (j + 1) * 256)
            gwq_ref[cols] = gwq[:, cols].T.astype(BF)
        gwo_out[...] = gwo_ref[...].astype(BF)
        gwe_out[...] = gwe_ref[...].astype(BF)


def attend_back(lengths, dout, h, q, k, v, lat, att, lse, wo, wq, we, cosine, sine, tail):
    groups, batches, here, width = dout.shape
    seq = groups * here
    shape = jax.ShapeDtypeStruct

    def by_seq(w):
        return pl.BlockSpec((1, seq, w), lambda m: (m, 0, 0))

    def by_dev(w):
        return pl.BlockSpec((groups, 1, here, w), lambda m: (0, m, 0, 0))

    def whole(v):
        return pl.BlockSpec(v.shape, lambda m: (0, 0))

    return pl.pallas_call(
        attend_back_kernel,
        grid=(batches,),
        out_shape=(shape((groups, batches, here, width + tail), BF), shape(wq.shape, BF),
                   shape(wo.shape, BF), shape(we.shape, BF)),
        in_specs=[pl.BlockSpec(memory_space=pltpu.SMEM), by_dev(width), by_dev(width), by_seq(256), by_seq(256), by_seq(128),
                  by_seq(512), by_dev(128), by_seq(1), whole(wo), whole(wq), whole(we), whole(cosine), whole(sine)],
        out_specs=[by_dev(width + tail), whole(wq), whole(wo), whole(we)],
        scratch_shapes=[pltpu.VMEM((seq, 256), F32), pltpu.VMEM((seq, 128), F32), pltpu.VMEM((seq, 128), BF),
                        pltpu.VMEM((256, width), F32), pltpu.VMEM(wo.shape, F32), pltpu.VMEM(we.shape, F32)],
        compiler_params=pltpu.CompilerParams(vmem_limit_bytes=56 * 1024 * 1024),
        cost_estimate=pl.CostEstimate(flops=14_000_000_000, bytes_accessed=25_000_000, transcendentals=2_000_000),
        name="attend_back",
    )(lengths, dout, h, q, k, v, lat, att, lse, wo, wq, we, cosine, sine)


H = 16
QK_NOPE = 128
ROPE = 64
V_DIM = 128
KV_RANK = 512
GROUPS = 16
EPSILON = 1e-06
ROTARY_BASE = 10000.0


def product(left_side, right_side):
    return jnp.dot(left_side, right_side, preferred_element_type=F32)


def product_lead(left_side, right_side):
    return lax.dot_general(
        left_side, right_side, (((0,), (0,)), ((), ())), preferred_element_type=F32
    )


def product_trail(left_side, right_side):
    return lax.dot_general(
        left_side, right_side, (((1,), (1,)), ((), ())), preferred_element_type=F32
    )


def rotary_tables(count):
    frequency = ROTARY_BASE ** (-np.arange(ROPE // 2, dtype=np.float32) * np.float32(2.0) / np.float32(ROPE))
    angles = np.arange(count, dtype=np.float32)[:, None] * frequency.astype(np.float32)[None, :]
    return np.cos(angles).astype(np.float32), np.sin(angles).astype(np.float32)


def rotate(values, cosine, sine_table):
    first_half, second_half = jnp.split(values, 2, axis=-1)
    return jnp.concatenate(
        [
            first_half * cosine - second_half * sine_table,
            second_half * cosine + first_half * sine_table,
        ],
        axis=-1,
    )


def norm_forward(values, gains):
    factor = lax.rsqrt(jnp.mean(values * values, axis=-1, keepdims=True) + EPSILON)
    normed = values * factor
    return (normed * gains, normed, factor)


def norm_backward(gradient, normed, factor, gains):
    gain_grad = jnp.sum(gradient * normed, axis=0)
    scaled = gradient * gains
    return (
        factor * (scaled - normed * jnp.mean(scaled * normed, axis=-1, keepdims=True)),
        gain_grad,
    )


def selected_experts(routes):
    chosen = routes[:, :, None] == jnp.arange(GROUPS, dtype=routes.dtype)
    return jnp.any(chosen, axis=1)


def masked_softmax(logits, mask):
    held = jnp.where(mask, logits, -1e30)
    peak = jnp.max(held, axis=-1, keepdims=True)
    raised = jnp.where(mask, jnp.exp(held - peak), 0.0)
    return raised / jnp.sum(raised, axis=-1, keepdims=True)


def per_device(
    layer_input,
    out_cotangent,
    lengths,
    routes,
    attn_gain,
    query_weight,
    latent_weight,
    latent_gain,
    expand_weight,
    output_weight,
    mixer_gain,
    router_weight,
    gate_weight,
    up_weight,
    down_weight,
    shared_gate,
    shared_up,
    shared_down,
):
    dp = lax.axis_size("dp")
    me = lax.axis_index("expert")
    plane = lax.axis_index("dp")
    batches, _, here, width = layer_input.shape
    own = batches * here
    total = own * GROUPS
    seq_total = here * GROUPS
    rows_w = query_weight.shape[0]
    rows_l = expand_weight.shape[0]

    x_own = layer_input.reshape(own, width)
    mask_own = selected_experts(routes.reshape(own, -1))
    mask_columns = mask_own.astype(BF).reshape(rows_w, -1)
    small_width = -(-(595 + mask_columns.shape[1]) // 128) * 128
    latent_column = jnp.zeros((rows_w,), BF).at[:rows_l].set(latent_gain)
    small = jnp.concatenate(
        [
            latent_weight,
            router_weight,
            attn_gain[:, None],
            mixer_gain[:, None],
            latent_column[:, None],
            mask_columns,
            jnp.zeros((rows_w, small_width - 595 - mask_columns.shape[1]), BF),
        ],
        axis=1,
    )
    query_parts = query_weight.reshape(rows_w, H, QK_NOPE + ROPE).transpose(1, 0, 2)
    expand_parts = expand_weight.reshape(rows_l, H, QK_NOPE + V_DIM).transpose(1, 0, 2)
    expand_parts = expand_parts.reshape(H, rows_l, 4, ROPE).swapaxes(1, 2).reshape(H, rows_w, ROPE)
    parts = jnp.concatenate([query_parts, expand_parts], axis=2)
    x_all, small, parts_head, output_head = opening(dp, x_own, small, parts, output_weight, 1)
    x_all = x_all.reshape(total, width)
    mask_all = lax.dynamic_index_in_dim(small, plane, 0, False)[..., 595 : 595 + mask_columns.shape[1]]
    mask_all = mask_all.reshape(total, GROUPS)
    small = small.reshape(width, small_width)
    parts_head = parts_head.reshape(width, TILE)
    latent_full = small[:, :576]
    router_full = small[:, 576:592]
    gain_attn = small[:, 592].astype(F32)
    gain_mixer = small[:, 593].astype(F32)
    gain_latent = small[:, 594].reshape(dp * GROUPS, rows_w)[:, :rows_l].reshape(-1).astype(F32)
    expand_head = parts_head[:, QK_NOPE + ROPE :].reshape(dp * GROUPS, 4, rows_l, ROPE)
    expand_head = expand_head.swapaxes(1, 2).reshape(KV_RANK, QK_NOPE + V_DIM)
    output_head = output_head.reshape(V_DIM, width)

    ff = gate_weight.shape[2]
    share_own = jnp.concatenate([shared_gate.T, shared_up.T, shared_down], axis=0)
    share_width = shared_down.shape[0]
    gate_full = lax.all_gather(gate_weight[0], "dp", axis=0, tiled=True)
    up_full = lax.all_gather(up_weight[0], "dp", axis=0, tiled=True)
    share_full = lax.all_gather(share_own, "dp", axis=0)
    seq_lengths = lengths.reshape(batches)
    own_positions = me * here + jnp.arange(here, dtype=jnp.int32)
    valid_own = (own_positions[None, :] < seq_lengths[:, None]).reshape(own).astype(F32)
    cosine, sine_table = rotary_tables(seq_total)
    cosine_own = lax.dynamic_slice_in_dim(jnp.asarray(cosine), me * here, here)
    sine_own = lax.dynamic_slice_in_dim(jnp.asarray(sine_table), me * here, here)

    grad_own = out_cotangent.reshape(own, width) * valid_own[:, None].astype(BF)

    def by_token(table):
        return jnp.asarray(np.broadcast_to(
            table.reshape(GROUPS, 1, here, -1), (GROUPS, batches, here, table.shape[1])).reshape(total, -1))

    hidden_all, query, key, values, latent = project(
        x_all.reshape(GROUPS, own, width), gain_attn[None], gain_latent[None], parts_head, small, expand_head,
        by_token(cosine), by_token(sine_table), batches)
    attn_part, attended, log_total = attend(seq_lengths, query, key, values, output_head, GROUPS)
    attn_part = attn_part.reshape(GROUPS, own, width)
    down_own = down_weight[0]
    cut = down_own.shape[0] * 3 // 160 * 16
    cuts = (0, cut, 2 * cut + cut // 48 * 16, down_own.shape[0])
    spans = [(first, last - first) for first, last in zip(cuts, cuts[1:])]
    attn_out, down_a = scatter16(attn_part, 2, dp=dp, span=spans[0], side=down_own)

    x_wide = x_own.astype(F32)
    middle = x_wide + attn_out
    normed_mix, unit_mix, factor_mix = norm_forward(middle, gain_mixer)
    hidden_mix = normed_mix.astype(BF)
    mix_all, down_b = gather16(hidden_mix, 3, dp=dp, span=spans[1], side=down_own)
    mix_all = mix_all.reshape(total, width)

    lane = jnp.arange(128)[None, :]
    pick = jnp.concatenate([lane == me, lane == me + GROUPS], axis=1).astype(F32)
    (out_part, rows, hidden, act, slope, result, share_hidden, share_act, share_slope, gates, to_slot, to_token,
     grad_all, down_c) = mixture_forward(
        dp, batches, here, seq_lengths, pick, mix_all, mask_all, gate_full, up_full, router_full.T, share_full,
        down_a, down_b, spans[2], down_own, grad_own, 4)
    grad_all = grad_all.reshape(total, width)
    mix_part, grad_result, grad_gate_in, grad_up_in, grad_share_in, mixed = mixture_backward(
        pick, grad_all, gate_full, up_full, share_full, down_a, down_b, down_c, act, slope, result,
        share_act, share_slope, gates, to_slot, to_token, out_part.reshape(GROUPS, own, width), 8)
    grad_down = product_lead(hidden, grad_result).astype(BF)
    grad_down = grad_down.reshape(dp, ff // dp, width)
    mix_sum, grad_share, grad_gate, grad_up, far_down = scatter_share(
        mix_part.reshape(GROUPS, own, width + 128), grad_share_in, share_hidden, mix_all, grad_all,
        rows, grad_gate_in, grad_up_in, grad_down, share_full.shape, 5)
    out_down = lax.dynamic_index_in_dim(grad_down, plane, 0, False).astype(F32)
    out_down = out_down + jnp.sum(far_down.astype(F32), axis=0)
    layer_output = valid_own[:, None] * (middle + mixed)

    out_gate = lax.psum_scatter(grad_gate, "dp", scatter_dimension=0, tiled=True)
    out_up = lax.psum_scatter(grad_up, "dp", scatter_dimension=0, tiled=True)

    soft_own = masked_softmax(product(hidden_mix, router_full), mask_own)
    grad_masked = (mix_sum[:, width : width + GROUPS] + mix_sum[:, width + GROUPS : width + 2 * GROUPS])
    grad_masked = grad_masked * valid_own[:, None]
    grad_logits = soft_own * (grad_masked - jnp.sum(grad_masked * soft_own, axis=1, keepdims=True))
    grad_logits = grad_logits.astype(BF)
    grad_mix = mix_sum[:, :width] + product_trail(grad_logits, router_full)
    grad_middle_norm, grad_gain_mixer = norm_backward(grad_mix, unit_mix, factor_mix, gain_mixer)
    grad_middle = grad_own.astype(F32) + grad_middle_norm

    grad_attn_all, share_far = gather16(grad_middle.astype(BF), 6, dp=dp, side=grad_share)
    grad_attn_all = grad_attn_all.reshape(GROUPS, batches, here, width)
    out_share = lax.dynamic_index_in_dim(grad_share, plane, 0, False).astype(F32)
    out_share = out_share + jnp.sum(share_far.astype(F32), axis=0)
    back_part, grad_query_w, grad_output, grad_expand = attend_back(
        seq_lengths, grad_attn_all, hidden_all.reshape(GROUPS, batches, here, width), query, key, values, latent,
        attended, log_total, output_head, parts_head, expand_head, jnp.asarray(cosine), jnp.asarray(sine_table), 640)
    grad_expand = grad_expand.reshape(dp * GROUPS, rows_l, 4, ROPE).swapaxes(1, 2).reshape(width, ROPE)
    parts_grad = grad_query_w + jnp.pad(grad_expand, ((0, 0), (QK_NOPE + ROPE, 0)))
    parts_grad = parts_grad.reshape(dp, GROUPS, rows_w, TILE)
    rows_grad = grad_output.reshape(dp, rows_w, width)
    back_sum, parts_far, rows_far = returning(
        dp, back_part.reshape(GROUPS, own, back_part.shape[3]), parts_grad, rows_grad, 7)
    parts_sum = lax.dynamic_index_in_dim(parts_grad, plane, 0, False).astype(F32)
    parts_sum = (parts_sum + jnp.sum(parts_far.astype(F32), axis=0)).astype(BF)
    rows_sum = (rows_grad.astype(F32) + jnp.sum(rows_far.astype(F32), axis=0)).astype(BF)

    x_normed, unit_attn, factor_attn = norm_forward(x_wide, gain_attn)
    hidden_own = x_normed.astype(BF)
    latent_own = product(hidden_own, latent_full)
    _, unit_latent, factor_latent = norm_forward(latent_own[:, :KV_RANK], gain_latent)
    grad_latent_in, grad_gain_latent = norm_backward(
        back_sum[:, width : width + KV_RANK], unit_latent, factor_latent, gain_latent
    )
    grad_rope = back_sum[:, width + KV_RANK : width + KV_RANK + ROPE].reshape(batches, here, ROPE)
    grad_rope = rotate(grad_rope, cosine_own, -sine_own).reshape(own, ROPE)
    grad_latent_raw = jnp.concatenate([grad_latent_in, grad_rope], axis=1).astype(BF)
    grad_hidden_attn = back_sum[:, :width] + product_trail(grad_latent_raw, latent_full)
    grad_input_norm, grad_gain_attn = norm_backward(grad_hidden_attn, unit_attn, factor_attn, gain_attn)
    grad_input = grad_middle + grad_input_norm

    latent_rows = grad_gain_latent.reshape(dp * GROUPS, rows_l)
    latent_rows = jnp.pad(latent_rows, ((0, 0), (0, rows_w - rows_l))).reshape(width, 1)
    tokens_side = jnp.concatenate([hidden_own, hidden_mix], axis=0)
    grads_side = jnp.concatenate(
        [jnp.pad(grad_latent_raw, ((0, 0), (0, 64))), jnp.pad(grad_logits, ((0, 0), (576, 640 - 592)))], axis=0)
    lane = jnp.arange(640)[None, :]
    small_grad = product_lead(tokens_side, grads_side)
    small_grad = small_grad + jnp.where(lane == 592, grad_gain_attn[:, None], 0.0)
    small_grad = small_grad + jnp.where(lane == 593, grad_gain_mixer[:, None], 0.0)
    small_grad = (small_grad + jnp.where(lane == 594, latent_rows, 0.0)).astype(BF)
    small_grad = small_grad.reshape(dp, GROUPS, rows_w, 640).swapaxes(0, 1).reshape(GROUPS, dp * rows_w, 640)
    small_sum, out_query, out_expand, out_output = closing(dp, small_grad, parts_sum, rows_sum, rows_l, 9)

    def as_input(v):
        return v.reshape(batches, 1, here, width)

    return (
        as_input(layer_output),
        as_input(grad_input),
        small_sum[:, 592],
        out_query,
        small_sum[:, :576],
        small_sum[:rows_l, 594],
        out_expand,
        out_output,
        small_sum[:, 593],
        small_sum[:, 576:592],
        out_gate.astype(F32)[None],
        out_up.astype(F32)[None],
        out_down[None],
        out_share[:share_width].T,
        out_share[share_width : 2 * share_width].T,
        out_share[2 * share_width :],
    )


def solution(mesh):
    split = P(("dp", "expert"), None)
    line = P(("dp", "expert"))
    tokens = P(None, "dp", "expert", None)
    expert = P("expert", "dp", None)
    return jax.shard_map(
        per_device,
        mesh=mesh,
        in_specs=(
            tokens, tokens, P(None, "dp"), tokens, line, split, split, line, split, split, line, split,
            expert, expert, expert, P("dp", "expert"), P("dp", "expert"), P("expert", "dp"),
        ),
        out_specs=(
            tokens, tokens, line, split, split, line, split, split, line, split,
            expert, expert, expert, P("dp", "expert"), P("dp", "expert"), P("expert", "dp"),
        ),
        check_vma=False,
    )
```

```python
import functools
import jax
import jax.numpy as jnp
import numpy as np
from jax import lax
from jax.experimental import pallas as pl
from jax.experimental.pallas import tpu as pltpu
from jax.sharding import PartitionSpec as P

MESH = pl.DeviceIdType.MESH
NZ = 4
NE = 16


def place():
    me = lax.axis_index("expert")
    z = me // 4
    x = (me // 2) % 2
    c = me % 2
    return me, z, x, c, me + 1 - 2 * c, me + 2 - 4 * x


def enter(me, z, core, side, dp=1):
    barrier = pltpu.get_barrier_semaphore()
    plane = lax.axis_index("dp")
    for r in range(1, dp):
        pl.semaphore_signal(barrier, inc=1, device_id={"dp": (plane + r) % dp}, device_id_type=MESH)
    for other in (core, side):
        pl.semaphore_signal(barrier, inc=1, device_id={"expert": other}, device_id_type=MESH)

    @pl.when(z < NZ - 1)
    def _():
        pl.semaphore_signal(barrier, inc=1, device_id={"expert": me + 4}, device_id_type=MESH)

    @pl.when(z > 0)
    def _():
        pl.semaphore_signal(barrier, inc=1, device_id={"expert": me - 4}, device_id_type=MESH)

    pl.semaphore_wait(barrier, dp + 1 + (z < NZ - 1).astype(jnp.int32) + (z > 0).astype(jnp.int32))


class Spread:
    def __init__(self, dp, src, out, sems):
        self.dp, self.src, self.out = dp, src, out
        self.own, self.send, self.recv = sems
        self.plane = lax.axis_index("dp")

    @staticmethod
    def scratch(dp):
        dma = pltpu.SemaphoreType.DMA
        return [dma, dma((dp,)), dma((dp,))]

    def copy(self, r):
        return pltpu.make_async_remote_copy(
            src_ref=self.src, dst_ref=self.out.at[self.plane], send_sem=self.send.at[r], recv_sem=self.recv.at[r],
            device_id={"dp": (self.plane + r) % self.dp}, device_id_type=MESH)

    def arrival(self, r):
        p = (self.plane - r + self.dp) % self.dp
        return pltpu.make_async_remote_copy(
            src_ref=self.src, dst_ref=self.out.at[p], send_sem=self.send.at[r], recv_sem=self.recv.at[r],
            device_id={"dp": p}, device_id_type=MESH)

    def start(self):
        for r in range(1, self.dp):
            self.copy(r).start()
        self.kept = pltpu.make_async_copy(self.src, self.out.at[self.plane], self.own)
        self.kept.start()

    def finish(self):
        self.kept.wait()
        for r in range(1, self.dp):
            self.arrival(r).wait_recv()
            self.copy(r).wait_send()


class Swap:
    def __init__(self, dp, src, out, sems):
        self.dp, self.src, self.out = dp, src, out
        self.send, self.recv = sems
        self.plane = lax.axis_index("dp")

    @staticmethod
    def scratch(dp):
        dma = pltpu.SemaphoreType.DMA
        return [dma((dp,)), dma((dp,))]

    def copy(self, r):
        to = (self.plane + r) % self.dp
        return pltpu.make_async_remote_copy(
            src_ref=self.src.at[to], dst_ref=self.out.at[r - 1], send_sem=self.send.at[r], recv_sem=self.recv.at[r],
            device_id={"dp": to}, device_id_type=MESH)

    def start(self):
        for r in range(1, self.dp):
            self.copy(r).start()

    def finish(self):
        for r in range(1, self.dp):
            self.copy(r).wait_recv()
            self.copy(r).wait_send()


def side_job(dp, span, src, out, sems):
    if span is None:
        return Swap(dp, src, out, sems)
    return Spread(dp, src.at[pl.ds(span[0], span[1])], out, sems)


def side_shape(dp, span, side):
    if span is None:
        return jax.ShapeDtypeStruct((dp - 1,) + side.shape[1:], side.dtype)
    return jax.ShapeDtypeStruct((dp, span[1], side.shape[1]), side.dtype)


def side_scratch(dp, span):
    return (Swap if span is None else Spread).scratch(dp)


def enter_all(me, plane, dp):
    barrier = pltpu.get_barrier_semaphore()
    for r in range(1, NE):
        pl.semaphore_signal(
            barrier, inc=1, device_id={"expert": (me + r) % NE}, device_id_type=MESH)
    for r in range(1, dp):
        pl.semaphore_signal(
            barrier, inc=1, device_id={"dp": (plane + r) % dp}, device_id_type=MESH)
    pl.semaphore_wait(barrier, NE - 1 + dp - 1)


class Gather:
    def __init__(self, src, out, chunks, sems, view=lambda ref, b: ref.at[b]):
        self.src, self.out, self.chunks, self.view = src, out, chunks, view
        self.rows = src.shape[0] // chunks
        (self.own_sem, self.us, self.ur, self.ds, self.dr, self.bus, self.bur, self.bds, self.bdr,
         self.xs, self.xr, self.cs, self.cr) = sems
        self.me, self.z, self.x, self.c, self.core, self.side = place()

    COUNT = 13

    @staticmethod
    def scratch(chunks):
        dma = pltpu.SemaphoreType.DMA
        return [dma] + [dma((4, chunks))] * 8 + [dma((7, chunks))] * 2 + [dma((14, chunks))] * 2

    def alt(self, k):
        return k >= (self.chunks + 1) // 2

    def order(self, ks=None):
        return range(self.chunks - 1, -1, -1) if ks is None else ks

    def copy(self, block, k, src, send, recv, to):
        src_ref = self.src if src is None else self.view(self.out, src)
        dst_ref = self.view(self.out, block)
        if self.chunks > 1:
            part = pl.ds(k * self.rows, self.rows)
            src_ref, dst_ref = src_ref.at[part], dst_ref.at[part]
        return pltpu.make_async_remote_copy(
            src_ref=src_ref,
            dst_ref=dst_ref,
            send_sem=send, recv_sem=recv,
            device_id={"expert": to}, device_id_type=MESH,
        )

    def up(self, k, s, src=None):
        return self.copy(self.me - 4 * s, k, src, self.us.at[s, k], self.ur.at[s, k], self.me + 4)

    def down(self, k, s, src=None):
        return self.copy(self.me + 4 * s, k, src, self.ds.at[s, k], self.dr.at[s, k], self.me - 4)

    def up_b(self, k, s):
        b = self.side - 4 * s
        return self.copy(b, k, b, self.bus.at[s, k], self.bur.at[s, k], self.me + 4)

    def down_b(self, k, s):
        b = self.side + 4 * s
        return self.copy(b, k, b, self.bds.at[s, k], self.bdr.at[s, k], self.me - 4)

    def across(self, k, slot, block, src=None):
        return self.copy(block, k, src, self.xs.at[slot, k], self.xr.at[slot, k], self.side)

    def over(self, k, slot, block, src=None):
        return self.copy(block, k, src, self.cs.at[slot, k], self.cr.at[slot, k], self.core)

    def arrived(self, b, k, sems, s):
        return self.copy(b, k, b, sems[0].at[s - 1, k], sems[1].at[s - 1, k], self.side)

    def shift(self, base, slot):
        return base - 4 * slot if slot <= 3 else base + 4 * (slot - 3)

    def core_block(self, slot):
        if slot < 7:
            return self.shift(self.core, slot)
        return self.shift(self.core + 2 - 4 * self.x, slot - 7)

    def has(self, slot):
        slot = slot % 7
        if slot == 0:
            return self.z >= 0
        return self.z >= slot if slot <= 3 else self.z + (slot - 3) <= NZ - 1

    def crosses(self, k, slot):
        if slot == 0 or not self.alt(k):
            return self.has(slot)
        return self.z > slot if slot <= 3 else self.z + (slot - 3) < NZ - 1

    def kept(self):
        return pltpu.make_async_copy(self.src, self.view(self.out, self.me), self.own_sem)

    def start(self, ks=None):
        z, me = self.z, self.me
        if ks is None or 0 in ks:
            self.kept().start()
        for k in self.order(ks):
            self.across(k, 0, me).start()

            @pl.when(z < NZ - 1)
            def _():
                self.up(k, 0).start()

            @pl.when(z > 0)
            def _():
                self.down(k, 0).start()

            self.over(k, 0, me).start()

    def line(self, k, s):
        z, me = self.z, self.me

        @pl.when(z >= s)
        def _():
            b = me - 4 * s
            self.arrived(b, k, (self.us, self.ur), s).wait_recv()

            @pl.when(self.crosses(k, s))
            def _():
                self.across(k, s, b, b).start()

            @pl.when(z < NZ - 1)
            def _():
                self.up(k, s, b).start()

            self.over(k, s, b, b).start()

        @pl.when(z + s <= NZ - 1)
        def _():
            b = me + 4 * s
            self.arrived(b, k, (self.ds, self.dr), s).wait_recv()

            @pl.when(self.crosses(k, 3 + s))
            def _():
                self.across(k, 3 + s, b, b).start()

            @pl.when(z > 0)
            def _():
                self.down(k, s, b).start()

            self.over(k, 3 + s, b, b).start()

    def line_b(self, k, s):
        z = self.z

        @pl.when(z == s)
        def _():
            b = self.side - 4 * s
            self.arrived(b, k, (self.bus, self.bur), s).wait_recv()

            @pl.when(z < NZ - 1)
            def _():
                self.up_b(k, s).start()

            self.over(k, 7 + s, b, b).start()

        @pl.when(z + s == NZ - 1)
        def _():
            b = self.side + 4 * s
            self.arrived(b, k, (self.bds, self.bdr), s).wait_recv()

            @pl.when(z > 0)
            def _():
                self.down_b(k, s).start()

            self.over(k, 10 + s, b, b).start()

    def from_side(self, k, slot):
        @pl.when(self.crosses(k, slot))
        def _():
            b = self.shift(self.side, slot)
            self.across(k, slot, b, b).wait_recv()
            if slot == 0 and self.alt(k):
                @pl.when(self.z == 0)
                def _():
                    self.up_b(k, 0).start()

                @pl.when(self.z == NZ - 1)
                def _():
                    self.down_b(k, 0).start()

            self.over(k, 7 + slot, b, b).start()

    def round(self, s, ks=None):
        if s < NZ:
            for k in self.order(ks):
                self.line(k, s)
        for k in self.order(ks):
            for slot in ((0,) if s == 1 else (s - 1, s + 2)):
                self.from_side(k, slot)
        if s > 1:
            for k in self.order(ks):
                if self.alt(k):
                    self.line_b(k, s - 1)

    def landed(self, ks=None):
        for k in self.order(ks):
            for slot in range(14):
                @pl.when(self.has(slot))
                def _():
                    b = self.core_block(slot)
                    self.over(k, slot, b, b).wait_recv()

    def finish(self, landed=True):
        z = self.z
        if landed:
            self.kept().wait()
            self.landed()
        for k in self.order():
            for slot in range(14):
                @pl.when(self.has(slot))
                def _():
                    b = self.core_block(slot)
                    self.over(k, slot, b, b).wait_send()
            for slot in range(7):
                @pl.when(self.crosses(k, slot))
                def _():
                    self.across(k, slot, self.me).wait_send()
            for s in range(NZ - 1):
                @pl.when((z >= s) & (z < NZ - 1))
                def _():
                    self.up(k, s).wait_send()

                @pl.when((z + s <= NZ - 1) & (z > 0))
                def _():
                    self.down(k, s).wait_send()

                if self.alt(k):
                    @pl.when(z == s)
                    def _():
                        self.up_b(k, s).wait_send()

                    @pl.when(z + s == NZ - 1)
                    def _():
                        self.down_b(k, s).wait_send()


def gather_kernel(chunks, dp, span, extra, x_ref, *refs):
    job = None
    ng = Gather.COUNT
    if not extra:
        o_ref, *sems = refs
    else:
        src, o_ref, out, *sems = refs
        job = side_job(dp, span, src, out, sems[ng:])
    g = Gather(x_ref, o_ref, chunks, sems[:ng])
    enter(g.me, g.z, g.core, g.side, 1 if job is None else dp)
    if job is not None:
        job.start()
    g.start()
    for s in range(1, NZ + 1):
        g.round(s)
    g.finish()
    if job is not None:
        job.finish()


COST = pl.CostEstimate(flops=0, bytes_accessed=4_000_000, transcendentals=0)
ANY = pl.BlockSpec(memory_space=pl.ANY)


def gather16(v, cid, chunks=2, dp=1, span=None, side=None):
    rows, width = v.shape
    extra = side is not None
    out = pl.pallas_call(
        functools.partial(gather_kernel, chunks, dp, span, extra),
        out_shape=(jax.ShapeDtypeStruct((NE, rows, width), v.dtype),)
        + ((side_shape(dp, span, side),) if extra else ()),
        in_specs=[ANY] * (2 if extra else 1),
        out_specs=(ANY,) * (2 if extra else 1),
        scratch_shapes=Gather.scratch(chunks) + (side_scratch(dp, span) if extra else []),
        compiler_params=pltpu.CompilerParams(collective_id=cid, has_side_effects=True),
        cost_estimate=COST,
        name="gather16",
    )(*((v, side) if extra else (v,)))
    return out if extra else out[0]


def opening_kernel(dp, chunks, x_ref, small_ref, parts_ref, out_ref,
                   x_all, small_all, parts_head, out_head, small_dp, out_dp, *sems):
    ng = Gather.COUNT
    gx = Gather(x_ref, x_all, chunks, sems[:ng])
    gs = Gather(small_dp, small_all, 1, sems[ng:2 * ng], lambda ref, b: ref.at[:, b])
    loc, ys, yr, ps, pr, os_, or_, pl_sem, ol_sem = sems[2 * ng:]
    me = gx.me
    plane = lax.axis_index("dp")
    enter_all(me, plane, dp)
    pairs = ((small_ref, small_dp), (out_ref, out_dp), (parts_head.at[plane], parts_head))

    def lift(i, r):
        src, dst = pairs[i]
        return pltpu.make_async_remote_copy(
            src_ref=src, dst_ref=dst.at[plane], send_sem=ys.at[i, r], recv_sem=yr.at[i, r],
            device_id={"dp": (plane + r) % dp}, device_id_type=MESH)

    def landed(i, r):
        p = (plane - r + dp) % dp
        dst = pairs[i][1].at[p]
        return pltpu.make_async_remote_copy(
            src_ref=dst, dst_ref=dst, send_sem=ys.at[i, r], recv_sem=yr.at[i, r],
            device_id={"dp": p}, device_id_type=MESH)

    def kept(i):
        src, dst = pairs[i]
        return pltpu.make_async_copy(src, dst.at[plane], loc.at[i])

    def part(r):
        h = (me + r) % NE
        return pltpu.make_async_remote_copy(
            src_ref=parts_ref.at[h], dst_ref=parts_head.at[plane, me],
            send_sem=ps.at[r], recv_sem=pr.at[r],
            device_id={"expert": h}, device_id_type=MESH)

    def part_in(r):
        e = (me - r + NE) % NE
        return pltpu.make_async_remote_copy(
            src_ref=parts_head.at[plane, e], dst_ref=parts_head.at[plane, e],
            send_sem=ps.at[r], recv_sem=pr.at[r],
            device_id={"expert": e}, device_id_type=MESH)

    def part_kept():
        return pltpu.make_async_copy(parts_ref.at[me], parts_head.at[plane, me], pl_sem)

    for i in range(2):
        for r in range(1, dp):
            lift(i, r).start()
        kept(i).start()
    for r in range(1, NE):
        part(r).start()
    part_kept().start()
    gx.start()
    gx.round(1)

    kept(0).wait()
    for r in range(1, dp):
        landed(0, r).wait_recv()
    gs.start()

    for r in range(1, NE):
        part_in(r).wait_recv()
    part_kept().wait()
    for r in range(1, dp):
        lift(2, r).start()
    gx.round(2)

    def row(d):
        b = NE * d + me
        return pltpu.make_async_remote_copy(
            src_ref=out_dp.at[d], dst_ref=out_head.at[b % dp],
            send_sem=os_.at[d], recv_sem=or_.at[b % dp],
            device_id={"expert": b // dp}, device_id_type=MESH)

    def row_kept(d):
        b = NE * d + me
        return pltpu.make_async_copy(out_dp.at[d], out_head.at[b % dp], ol_sem.at[d])

    kept(1).wait()
    for r in range(1, dp):
        landed(1, r).wait_recv()
    for d in range(dp):
        home = (NE * d + me) // dp

        @pl.when(home != me)
        def _():
            row(d).start()

        @pl.when(home == me)
        def _():
            row_kept(d).start()

    gs.round(1)
    gx.round(3)
    gs.round(2)
    gx.round(4)
    gs.round(3)
    gs.round(4)

    def row_in(j):
        return pltpu.make_async_remote_copy(
            src_ref=out_head.at[j], dst_ref=out_head.at[j], send_sem=os_.at[j], recv_sem=or_.at[j],
            device_id={"expert": gx.core}, device_id_type=MESH)

    for r in range(1, NE):
        part(r).wait_send()
    for j in range(dp):
        @pl.when((dp * me + j) % NE != me)
        def _():
            row_in(j).wait_recv()
    for d in range(dp):
        home = (NE * d + me) // dp

        @pl.when(home != me)
        def _():
            row(d).wait_send()

        @pl.when(home == me)
        def _():
            row_kept(d).wait()
    for r in range(1, dp):
        landed(2, r).wait_recv()
    for i in range(3):
        for r in range(1, dp):
            lift(i, r).wait_send()
    gx.finish()
    gs.finish()


def opening(dp, x, small, parts, out, cid, chunks=2):
    dma = pltpu.SemaphoreType.DMA
    rows, ws = small.shape
    bf = x.dtype
    wo = out.shape[1]
    shape = jax.ShapeDtypeStruct
    res = pl.pallas_call(
        functools.partial(opening_kernel, dp, chunks),
        out_shape=(
            shape((NE,) + x.shape, bf), shape((dp, NE, rows, ws), bf), shape((dp, NE) + parts.shape[1:], bf),
            shape((dp, rows, wo), bf),
            shape((dp, rows, ws), bf), shape((dp, rows, wo), bf),
        ),
        in_specs=[ANY] * 4,
        out_specs=[ANY] * 6,
        scratch_shapes=Gather.scratch(chunks) + Gather.scratch(1) + [
            dma((2,)), dma((3, dp)), dma((3, dp)), dma((NE,)), dma((NE,)), dma((dp,)), dma((dp,)), dma, dma((dp,))],
        compiler_params=pltpu.CompilerParams(collective_id=cid, has_side_effects=True),
        cost_estimate=COST,
        name="opening",
    )(x, small, parts, out)
    return res[:4]


def order(z, i):
    a, b = (3, 2, 1, 0)[i], (3, 2, 0, 1)[i]
    return jnp.where(z == 0, a, jnp.where(z == 1, b, jnp.where(z == 2, 3 - b, 3 - a)))


class Scatter:
    COUNT = 14

    def __init__(self, p_ref, o_ref, chunks, scratch):
        self.p, self.o, self.chunks = p_ref, o_ref, chunks
        (self.cbuf, self.own, self.xbuf, self.ubuf, self.dbuf, self.ld, self.cs, self.cr, self.xs, self.xr,
         self.us, self.ur, self.ds, self.dr) = scratch
        self.rows = o_ref.shape[0] // chunks
        self.me, self.z, self.x, self.c, self.core, self.side = place()

    @staticmethod
    def scratch(rows, width, chunks, bf):
        dma = pltpu.SemaphoreType.DMA
        return [pltpu.VMEM((n, rows, width), bf) for n in (8, 8, 4, 4, 4)] + [
            dma((8, chunks)), dma((8, chunks)), dma((8, chunks))] + [dma((4, chunks))] * 6

    def rng(self, k):
        return pl.ds(k * self.rows, self.rows)

    def column(self, i, j):
        return 4 * order(self.z, i) + 2 * jnp.where(j == 0, 1 - self.x, self.x)

    def remote(self, src, dst, send, recv, to):
        return pltpu.make_async_remote_copy(
            src_ref=src, dst_ref=dst, send_sem=send, recv_sem=recv,
            device_id={"expert": to}, device_id_type=MESH)

    def over(self, i, j, k):
        n = 2 * i + j
        return self.remote(
            self.p.at[self.column(i, j) + 1 - self.c, self.rng(k)], self.cbuf.at[n, self.rng(k)],
            self.cs.at[n, k], self.cr.at[n, k], self.core)

    def load(self, i, j, k):
        n = 2 * i + j
        return pltpu.make_async_copy(
            self.p.at[self.column(i, j) + self.c, self.rng(k)], self.own.at[n, self.rng(k)], self.ld.at[n, k])

    def which(self, ks):
        return range(self.chunks) if ks is None else ks

    def across(self, i, k):
        return self.remote(self.own.at[2 * i, self.rng(k)], self.xbuf.at[i, self.rng(k)],
                           self.xs.at[i, k], self.xr.at[i, k], self.side)

    def up(self, t, i, k):
        return self.remote(self.own.at[2 * i + 1, self.rng(k)], self.ubuf.at[t, self.rng(k)],
                           self.us.at[t, k], self.ur.at[t, k], self.me + 4)

    def down(self, t, i, k):
        return self.remote(self.own.at[2 * i + 1, self.rng(k)], self.dbuf.at[t, self.rng(k)],
                           self.ds.at[t, k], self.dr.at[t, k], self.me - 4)

    def start(self, ks=None):
        for i in range(NZ):
            for j in range(2):
                for k in self.which(ks):
                    self.load(i, j, k).start()
                    self.over(i, j, k).start()

    def first(self, i, ks=None):
        f32 = jnp.float32
        for k in self.which(ks):
            self.load(i, 0, k).wait()
            self.over(i, 0, k).wait_recv()
            s = self.rng(k)
            self.own[2 * i, s] = (
                self.own[2 * i, s].astype(f32) + self.cbuf[2 * i, s].astype(f32)).astype(self.own.dtype)
            self.across(i, k).start()

    def second(self, i, ks=None):
        f32 = jnp.float32
        z, own, o = self.z, self.own, self.o
        t = order(z, i)
        for k in self.which(ks):
            self.load(i, 1, k).wait()
            s = self.rng(k)
            self.over(i, 1, k).wait_recv()
            self.across(i, k).wait_recv()

            def base():
                return (own[2 * i + 1, s].astype(f32) + self.cbuf[2 * i + 1, s].astype(f32)
                        + self.xbuf[i, s].astype(f32))

            if i < NZ - 1:
                @pl.when(t > z)
                def _():
                    @pl.when(z > 0)
                    def _():
                        self.up(t, i, k).wait_recv()
                        own[2 * i + 1, s] = (base() + self.ubuf[t, s].astype(f32)).astype(own.dtype)

                    @pl.when(z == 0)
                    def _():
                        own[2 * i + 1, s] = base().astype(own.dtype)

                    self.up(t, i, k).start()

                @pl.when(t < z)
                def _():
                    @pl.when(z < NZ - 1)
                    def _():
                        self.down(t, i, k).wait_recv()
                        own[2 * i + 1, s] = (base() + self.dbuf[t, s].astype(f32)).astype(own.dtype)

                    @pl.when(z == NZ - 1)
                    def _():
                        own[2 * i + 1, s] = base().astype(own.dtype)

                    self.down(t, i, k).start()
            else:
                @pl.when(z > 0)
                def _():
                    self.up(t, i, k).wait_recv()

                @pl.when(z < NZ - 1)
                def _():
                    self.down(t, i, k).wait_recv()

                @pl.when((z > 0) & (z < NZ - 1))
                def _():
                    o[s] = (base() + self.ubuf[t, s].astype(f32) + self.dbuf[t, s].astype(f32)).astype(o.dtype)

                @pl.when(z == 0)
                def _():
                    o[s] = (base() + self.dbuf[t, s].astype(f32)).astype(o.dtype)

                @pl.when(z == NZ - 1)
                def _():
                    o[s] = (base() + self.ubuf[t, s].astype(f32)).astype(o.dtype)

    def run(self, between=lambda: None):
        self.first(0)
        for i in range(NZ):
            if i + 1 < NZ:
                self.first(i + 1)
            between()
            self.second(i)
            between()

    def finish(self):
        z = self.z
        for k in range(self.chunks):
            for i in range(NZ):
                self.across(i, k).wait_send()
                for j in range(2):
                    self.over(i, j, k).wait_send()
                if i < NZ - 1:
                    t = order(z, i)

                    @pl.when(t > z)
                    def _():
                        self.up(t, i, k).wait_send()

                    @pl.when(t < z)
                    def _():
                        self.down(t, i, k).wait_send()


def scatter_kernel(chunks, dp, span, extra, p_ref, *refs):
    job = None
    ns = Scatter.COUNT
    if not extra:
        o_ref, *scratch = refs
    else:
        src, o_ref, out, *scratch = refs
        job = side_job(dp, span, src, out, scratch[ns:])
    s = Scatter(p_ref, o_ref, chunks, scratch[:ns])
    enter(s.me, s.z, s.core, s.side, 1 if job is None else dp)
    if job is not None:
        job.start()
    s.start()
    s.run()
    s.finish()
    if job is not None:
        job.finish()


VMEM = pl.BlockSpec(memory_space=pltpu.VMEM)


def scatter16(p, cid, chunks=2, dp=1, span=None, side=None):
    _, rows, width = p.shape
    extra = side is not None
    out = pl.pallas_call(
        functools.partial(scatter_kernel, chunks, dp, span, extra),
        out_shape=(jax.ShapeDtypeStruct((rows, width), jnp.float32),)
        + ((side_shape(dp, span, side),) if extra else ()),
        in_specs=[ANY] * (2 if extra else 1),
        out_specs=(VMEM,) + ((ANY,) if extra else ()),
        scratch_shapes=Scatter.scratch(rows, width, chunks, p.dtype) + (side_scratch(dp, span) if extra else []),
        compiler_params=pltpu.CompilerParams(
            collective_id=cid, has_side_effects=True, vmem_limit_bytes=60 * 1024 * 1024),
        cost_estimate=COST,
        name="scatter16",
    )(*((p, side) if extra else (p,)))
    return out if extra else out[0]


def return_kernel(dp, chunks, p_ref, parts_ref, rows_ref, o_ref, parts_far, rows_far, *scratch):
    ns = Scatter.COUNT
    s = Scatter(p_ref, o_ref, chunks, scratch[:ns])
    swap = Swap(dp, parts_ref, parts_far, scratch[ns:ns + 2])
    rs, rr = scratch[ns + 2:]
    plane = lax.axis_index("dp")
    keeper = s.me * dp // NE
    enter(s.me, s.z, s.core, s.side, dp)

    def row(r):
        return pltpu.make_async_remote_copy(
            src_ref=rows_ref, dst_ref=rows_far.at[r - 1], send_sem=rs.at[r], recv_sem=rr.at[r],
            device_id={"dp": (plane + r) % dp}, device_id_type=MESH)

    swap.start()
    for r in range(1, dp):
        @pl.when((plane + r) % dp == keeper)
        def _():
            row(r).start()
    s.start()
    s.run()
    s.finish()
    swap.finish()
    for r in range(1, dp):
        @pl.when((plane + r) % dp == keeper)
        def _():
            row(r).wait_send()

        @pl.when(plane == keeper)
        def _():
            row(r).wait_recv()


def returning(dp, p, parts, rows, cid, chunks=2):
    dma = pltpu.SemaphoreType.DMA
    _, n, width = p.shape
    shape = jax.ShapeDtypeStruct
    return pl.pallas_call(
        functools.partial(return_kernel, dp, chunks),
        out_shape=(
            shape((n, width), jnp.float32), shape((dp - 1,) + parts.shape[1:], parts.dtype),
            shape((dp - 1,) + rows.shape, rows.dtype)),
        in_specs=[ANY] * 3,
        out_specs=[VMEM, ANY, ANY],
        scratch_shapes=Scatter.scratch(n, width, chunks, p.dtype) + [dma((dp,))] * 4,
        compiler_params=pltpu.CompilerParams(
            collective_id=cid, has_side_effects=True, vmem_limit_bytes=60 * 1024 * 1024),
        cost_estimate=COST,
        name="returning",
    )(p, parts, rows)


def closing_kernel(dp, p_ref, parts_ref, rows_ref, o_ref, far_ref, query_ref, expand_ref, output_ref,
                   parts_in, row_in, *scratch):
    ns = Scatter.COUNT
    s = Scatter(p_ref, o_ref, 1, scratch[:ns])
    ys, yr, ps, pr, kept_sem, rs, rr = scratch[ns:]
    me = s.me
    plane = lax.axis_index("dp")
    rows = o_ref.shape[0] // dp
    enter_all(me, plane, dp)

    def lift(r):
        to = (plane + r) % dp
        return pltpu.make_async_remote_copy(
            src_ref=o_ref.at[pl.ds(pl.multiple_of(to * rows, 16), rows)], dst_ref=far_ref.at[r - 1],
            send_sem=ys.at[r], recv_sem=yr.at[r],
            device_id={"dp": to}, device_id_type=MESH)

    def part(r):
        e = (me + r) % NE
        return pltpu.make_async_remote_copy(
            src_ref=parts_ref.at[e], dst_ref=parts_in.at[me], send_sem=ps.at[r], recv_sem=pr.at[r],
            device_id={"expert": e}, device_id_type=MESH)

    def part_in(r):
        h = (me - r + NE) % NE
        return pltpu.make_async_remote_copy(
            src_ref=parts_in.at[h], dst_ref=parts_in.at[h], send_sem=ps.at[r], recv_sem=pr.at[r],
            device_id={"expert": h}, device_id_type=MESH)

    def part_kept():
        return pltpu.make_async_copy(parts_ref.at[me], parts_in.at[me], kept_sem.at[0])

    keeper = plane == me * dp // NE
    source = (NE * plane + me) // dp

    def row(j):
        return pltpu.make_async_remote_copy(
            src_ref=rows_ref.at[j], dst_ref=row_in, send_sem=rs.at[j], recv_sem=rr,
            device_id={"expert": (dp * me + j) % NE}, device_id_type=MESH)

    def row_kept(j):
        return pltpu.make_async_copy(rows_ref.at[j], row_in, kept_sem.at[1])

    s.start()
    for r in range(1, NE):
        part(r).start()
    part_kept().start()
    for j in range(dp):
        home = (dp * me + j) % NE

        @pl.when(keeper & (home != me))
        def _():
            row(j).start()

        @pl.when(keeper & (home == me))
        def _():
            row_kept(j).start()
    s.run()
    for r in range(1, dp):
        lift(r).start()
    for r in range(1, NE):
        part_in(r).wait_recv()
    part_kept().wait()
    rows_l = expand_ref.shape[0]
    f32 = jnp.float32
    for h in range(0, NE, 2):
        pair = [parts_in[h + i].astype(f32) for i in range(2)]
        query_ref[:, h * 192:(h + 2) * 192] = jnp.concatenate([v[:, :192] for v in pair], axis=1)
        for i, v in enumerate(pair):
            expand_ref[:, (h + i) * 256:(h + i + 1) * 256] = jnp.concatenate(
                [v[c * rows_l:(c + 1) * rows_l, 192:] for c in range(4)], axis=1)

    @pl.when(source != me)
    def _():
        row(0).wait_recv()

    for j in range(dp):
        home = (dp * me + j) % NE

        @pl.when(keeper & (home != me))
        def _():
            row(j).wait_send()

        @pl.when(keeper & (home == me))
        def _():
            row_kept(j).wait()
    output_ref[...] = row_in[...].astype(f32)
    for r in range(1, NE):
        part(r).wait_send()
    s.finish()
    for r in range(1, dp):
        lift(r).wait_recv()
        lift(r).wait_send()


def closing(dp, p, parts, rows, rows_l, cid):
    dma = pltpu.SemaphoreType.DMA
    _, n, width = p.shape
    shape = jax.ShapeDtypeStruct
    rows_w = parts.shape[1]
    near, far, query, expand, output = pl.pallas_call(
        functools.partial(closing_kernel, dp),
        out_shape=(
            shape((n, width), p.dtype), shape((dp - 1, n // dp, width), p.dtype),
            shape((rows_w, NE * 192), jnp.float32), shape((rows_l, NE * 256), jnp.float32),
            shape(rows.shape[1:], jnp.float32)),
        in_specs=[ANY] * 3,
        out_specs=[VMEM] * 5,
        scratch_shapes=[pltpu.VMEM(parts.shape, parts.dtype), pltpu.VMEM(rows.shape[1:], rows.dtype)]
        + Scatter.scratch(n, width, 1, p.dtype)
        + [dma((dp,)), dma((dp,)), dma((NE,)), dma((NE,)), dma((2,)), dma((dp,)), dma],
        compiler_params=pltpu.CompilerParams(
            collective_id=cid, has_side_effects=True, vmem_limit_bytes=60 * 1024 * 1024),
        cost_estimate=COST,
        name="closing",
    )(p, parts, rows)
    own = lax.dynamic_slice_in_dim(near, lax.axis_index("dp") * (n // dp), n // dp).astype(jnp.float32)
    return own + jnp.sum(far.astype(jnp.float32), axis=0), query, expand, output
BF = jnp.bfloat16
F32 = jnp.float32


def mm(a, b):
    return jnp.dot(a, b, preferred_element_type=F32)


def mm_t(a, b):
    return lax.dot_general(a, b, (((1,), (1,)), ((), ())), preferred_element_type=F32)


def silu_pair(gate_in):
    sigmoid = 1.0 / (1.0 + jnp.exp(-gate_in))
    return (gate_in * sigmoid, sigmoid * (1.0 + gate_in * (1.0 - sigmoid)))


TILE = 256
WIDE = 512
SHARE = 176


def down_copies(parts, out, sem, which):
    dp = parts[0].shape[0]
    sizes = [part.shape[1] for part in parts]
    rows, first = sum(sizes), sum(sizes[:which])
    return [
        pltpu.make_async_copy(
            parts[which].at[d], out.at[pl.ds(d * rows + first, sizes[which])], sem.at[len(parts) * d + which])
        for d in range(dp)
    ]


def share_copies(share_ref, fan, down, sem):
    dp, rows, w = share_ref.shape
    n = rows // 3
    copies = []
    for d in range(dp):
        cols = pl.ds(d * w, w)
        for i, (dst, first) in enumerate(((fan, 0), (fan, TILE), (down, 0))):
            copies.append(pltpu.make_async_copy(
                share_ref.at[d, pl.ds(i * n, n)], dst.at[pl.ds(first, n), cols], sem.at[3 * d + i]))
    return copies


def share_blank(fan, down):
    pad = jnp.zeros((TILE - SHARE, fan.shape[1]), BF)
    fan[SHARE:TILE] = pad
    fan[TILE + SHARE:] = pad
    down[SHARE:] = pad


def valid_of(len_ref, first_device, tokens, batches, here):
    n = lax.broadcasted_iota(jnp.int32, (tokens, 1), 0)
    if here & (here - 1) or batches & (batches - 1):
        device, batch, place_in = n // (batches * here), (n // here) % batches, n % here
    else:
        bits, more = here.bit_length() - 1, (batches * here).bit_length() - 1
        device, batch, place_in = n >> more, (n >> bits) & (batches - 1), n & (here - 1)
    position = (first_device + device) * here + place_in
    length = jnp.zeros((tokens, 1), jnp.int32)
    for b in range(batches):
        length = jnp.where(batch == b, len_ref[b], length)
    return (position < length).astype(F32)


def slot_tables(here, slots=128):
    n = np.arange(256)
    same = n[:, None] // here == n[None, :] // here
    before = same & (n[None, :] < n[:, None])
    tables = np.stack([before, before.T, np.eye(256, dtype=bool)]).astype(np.float32)
    base = np.broadcast_to((n // here * 32)[:, None], (256, slots)).astype(np.float32)
    return jnp.asarray(tables, BF), jnp.asarray(base), jnp.asarray(base.T)


def one_hots(taken, tables, base_c, base_r, groups, slots):
    lane = lax.broadcasted_iota(jnp.int32, (256, slots), 1).astype(F32)
    row = lax.broadcasted_iota(jnp.int32, (slots, 256), 0).astype(F32)
    to_slot, to_token = [], []
    for g in range(groups):
        t = jnp.broadcast_to(taken[g * 256:(g + 1) * 256], (256, slots))
        low = t.astype(BF)
        place_c = mm(tables[0], low) + base_c[...]
        place_r = mm_lead(low, tables[1]) + base_r[...]
        taken_r = mm_lead(low, tables[2])
        to_token.append(jnp.where((place_c == lane) & (t > 0.5), 1.0, 0.0).astype(BF))
        to_slot.append(jnp.where((place_r == row) & (taken_r > 0.5), 1.0, 0.0).astype(BF))
    return to_slot, to_token


def mm_lead(a, b):
    return lax.dot_general(a, b, (((0,), (0,)), ((), ())), preferred_element_type=F32)


def lanes(j):
    return pl.ds(pl.multiple_of(j * WIDE, WIDE), WIDE)


def over_columns(total, body):
    def step(j, _):
        body(pl.multiple_of(j * WIDE, WIDE), WIDE)
        return 0

    lax.fori_loop(0, total // WIDE, step, 0)
    if total % WIDE:
        body(total // WIDE * WIDE, total % WIDE)


def forward_kernel(chunks, dp, span, batches, here, len_ref, pick_ref, mix_ref, mask_ref, tab_ref, basec_ref, baser_ref, wg_ref, wu_ref, router_ref,
                   share_ref, wda_ref, wdb_ref, down_ref, dy_ref,
                   out_ref, rows_ref, hid_ref, act_ref, slo_ref, eo_ref, sh_ref, sact_ref, sslo_ref, gate_ref,
                   slot_ref, token_ref, dy_all, wdc_ref,
                   wd_ref, fan_ref, sd_ref, hid_buf, sh_buf, gate_buf, token_buf, wd_sem, sh_sem, *sems):
    step = pl.program_id(0)
    tokens, width = mix_ref.shape
    groups, slots = tokens // 256, 128
    half = groups * slots
    ff = hid_ref.shape[1]
    phase = pl.num_programs(0) // 2
    g = Gather(dy_ref, dy_all, chunks, sems[:Gather.COUNT])
    job = side_job(dp, span, down_ref, wdc_ref, sems[Gather.COUNT:])
    parts = (wda_ref, wdb_ref, wdc_ref)

    @pl.when(step == 0)
    def _():
        enter(g.me, g.z, g.core, g.side, dp)
        job.start()
        g.start()
        copies = share_copies(share_ref, fan_ref, sd_ref, sh_sem)
        for copy in copies + down_copies(parts, wd_ref, wd_sem, 0) + down_copies(parts, wd_ref, wd_sem, 1):
            copy.start()
        share_blank(fan_ref, sd_ref)
        fan_ref[SHARE:SHARE + 16] = router_ref[...]
        for copy in copies:
            copy.wait()

    @pl.when(step < phase)
    def _():
        mix = mix_ref[...]
        fanned = mm_t(mix, fan_ref[:TILE, :])
        s_up = mm_t(mix, fan_ref[TILE:, :])
        s_act, s_slope = silu_pair(fanned)
        s_hidden = (s_act * s_up).astype(BF)
        at = pl.ds(pl.multiple_of(step * tokens, tokens), tokens)
        sh_ref[...] = s_hidden
        sh_buf[at] = s_hidden
        sact_ref[...] = s_act.astype(BF)
        sslo_ref[...] = (s_up * s_slope).astype(BF)
        logits = fanned[:, SHARE:SHARE + 16]
        mask = mask_ref[...].astype(F32)
        taken = jnp.sum(mask * pick_ref[:, :16], axis=1, keepdims=True) * valid_of(len_ref, step * (tokens // (batches * here)), tokens, batches, here)
        held = jnp.where(mask > 0.5, logits, -1e30)
        raised = jnp.exp(held - jnp.max(held, axis=1, keepdims=True)) * mask
        gate = jnp.sum(raised * pick_ref[:, :16], axis=1, keepdims=True) / jnp.sum(raised, axis=1, keepdims=True) * taken
        gate_ref[...] = gate
        gate_buf[at] = gate
        to_slot, to_token = one_hots(taken, tab_ref, basec_ref, baser_ref, groups, slots)
        for n in range(groups):
            slot_ref[n * slots:(n + 1) * slots] = to_slot[n]
            token_ref[n * 256:(n + 1) * 256] = to_token[n]
            token_buf[pl.ds(pl.multiple_of(step * tokens + n * 256, 256), 256)] = to_token[n]

        def dispatch(j, _):
            for n in range(groups):
                rows_ref[n * slots:(n + 1) * slots, lanes(j)] = mm(
                    to_slot[n], mix_ref[n * 256:(n + 1) * 256, lanes(j)]).astype(BF)
            return 0

        lax.fori_loop(0, width // WIDE, dispatch, 0)
        rows_at = pl.ds(pl.multiple_of(step * half, half), half)

        def fan_in(start, size):
            cols = pl.ds(start, size)
            gate_in = mm(rows_ref[...], wg_ref[:, cols])
            up_in = mm(rows_ref[...], wu_ref[:, cols])
            act, slope = silu_pair(gate_in)
            hidden = (act * up_in).astype(BF)
            hid_ref[:, cols] = hidden
            hid_buf[rows_at, cols] = hidden
            act_ref[:, cols] = act.astype(BF)
            slo_ref[:, cols] = (up_in * slope).astype(BF)

        over_columns(ff, fan_in)

    @pl.when(step == phase)
    def _():
        job.finish()
        for copy in down_copies(parts, wd_ref, wd_sem, 2):
            copy.start()
        for which in range(3):
            for copy in down_copies(parts, wd_ref, wd_sem, which):
                copy.wait()

    @pl.when(step >= phase)
    def _():
        tile = step - phase
        at = pl.ds(pl.multiple_of(tile * tokens, tokens), tokens)
        rows_at = pl.ds(pl.multiple_of(tile * half, half), half)
        gate = gate_buf[at]
        s_hidden = sh_buf[at]
        to_token = [token_buf[pl.ds(pl.multiple_of(tile * tokens + n * 256, 256), 256)] for n in range(groups)]

        def fan_out(j, _):
            eo = mm(hid_buf[rows_at], wd_ref[:, lanes(j)]).astype(BF)
            eo_ref[:, lanes(j)] = eo
            shared = mm(s_hidden, sd_ref[:, lanes(j)])
            picked = jnp.concatenate(
                [mm(to_token[n], eo[n * slots:(n + 1) * slots]) for n in range(groups)], axis=0)
            out_ref[:, lanes(j)] = (shared + gate * picked).astype(BF)
            return 0

        lax.fori_loop(0, width // WIDE, fan_out, 0)

    for r, s in ((1, 1), (2, 2), (3, 3), (4, 5)):
        @pl.when(step == s)
        def _():
            g.round(r)

    @pl.when(step == 2 * phase - 1)
    def _():
        g.finish()


def backward_kernel(chunks, pick_ref, dy_ref, wg_ref, wu_ref, share_ref, wda_ref, wdb_ref, wdc_ref,
                    act_ref, slo_ref, eo_ref, sact_ref, sslo_ref, gate_ref, slot_ref, token_ref, part_ref,
                    dh_ref, deo_ref, dg_ref, du_ref, ds_ref, sum_ref,
                    wd_ref, fan_ref, sd_ref, wd_sem, sh_sem, *scratch):
    step = pl.program_id(0)
    tokens, width = dy_ref.shape
    groups, slots = tokens // 256, 128
    ff = dg_ref.shape[1]
    sc = Scatter(part_ref, sum_ref, chunks, scratch)

    @pl.when(step == 0)
    def _():
        enter(sc.me, sc.z, sc.core, sc.side)
        copies = share_copies(share_ref, fan_ref, sd_ref, sh_sem)
        for which in range(3):
            copies += down_copies((wda_ref, wdb_ref, wdc_ref), wd_ref, wd_sem, which)
        for copy in copies:
            copy.start()
        sc.start()
        share_blank(fan_ref, sd_ref)
        for copy in copies:
            copy.wait()

    d_sh = mm_t(dy_ref[...], sd_ref[...])
    d_s = jnp.concatenate([(d_sh * sslo_ref[...].astype(F32)).astype(BF),
                           (d_sh * sact_ref[...].astype(F32)).astype(BF)], axis=1)
    ds_ref[...] = d_s
    gate = gate_ref[...]
    to_slot = [slot_ref[n * slots:(n + 1) * slots] for n in range(groups)]
    to_token = [token_ref[n * 256:(n + 1) * 256] for n in range(groups)]

    @pl.when(step == 0)
    def _():
        sc.first(0)
        sc.first(1)

    def dispatch(j, total):
        dy = dy_ref[:, lanes(j)].astype(F32)
        gated = (gate * dy).astype(BF)
        for n in range(groups):
            deo_ref[n * slots:(n + 1) * slots, lanes(j)] = mm(to_slot[n], gated[n * 256:(n + 1) * 256]).astype(BF)
        picked = jnp.concatenate(
            [mm(to_token[n], eo_ref[n * slots:(n + 1) * slots, lanes(j)]) for n in range(groups)], axis=0)
        return total + jnp.sum(dy * picked, axis=1, keepdims=True)

    d_gates = lax.fori_loop(0, width // WIDE, dispatch, jnp.zeros((tokens, 1), F32))

    def back_out(start, size):
        cols = pl.ds(start, size)
        d_eh = mm_t(deo_ref[...], wd_ref[cols, :])
        dg_ref[:, cols] = (d_eh * slo_ref[:, cols].astype(F32)).astype(BF)
        du_ref[:, cols] = (d_eh * act_ref[:, cols].astype(F32)).astype(BF)

    over_columns(ff, back_out)

    @pl.when(step == 0)
    def _():
        sc.first(2)
        sc.first(3)

    def back_in(j, _):
        d_rows = (mm_t(dg_ref[...], wg_ref[lanes(j), :]) + mm_t(du_ref[...], wu_ref[lanes(j), :])).astype(BF)
        shared = mm(d_s, fan_ref[:, lanes(j)])
        taken_rows = jnp.concatenate(
            [mm(to_token[n], d_rows[n * slots:(n + 1) * slots]) for n in range(groups)], axis=0)
        dh_ref[:, lanes(j)] = (shared + taken_rows).astype(BF)
        return 0

    lax.fori_loop(0, width // WIDE, back_in, 0)
    high = d_gates.astype(BF).astype(F32)
    dh_ref[:, width:] = (high * pick_ref[:, :128] + (d_gates - high) * pick_ref[:, 128:]).astype(BF)

    outer = (sc.z == 0) | (sc.z == NZ - 1)
    for i in range(NZ - 1):
        @pl.when((step == i) & outer)
        def _():
            sc.second(i)

        @pl.when((step == min(i + 1, 2)) & jnp.logical_not(outer))
        def _():
            sc.second(i)

    @pl.when(step == NZ - 1)
    def _():
        sc.second(NZ - 1)
        sc.finish()


def whole(v):
    zeros = (0,) * v.ndim
    return pl.BlockSpec(v.shape, lambda i: zeros, pipeline_mode=pl.Buffered(buffer_count=1))


def tiles(rows, w):
    return pl.BlockSpec((rows, w), lambda i: (i, 0))


SMEM = pl.BlockSpec(memory_space=pltpu.SMEM)


def mixture_forward(dp, batches, here, lengths, pick, mix, mask, wg, wu, router, share, wda, wdb, span, down, dy, cid,
                    chunks=2):
    total, width = mix.shape
    step, half = total // 4, total // 8
    ff = wg.shape[1]
    tables = slot_tables(here)
    shape = jax.ShapeDtypeStruct
    rows = total // 2
    dma = pltpu.SemaphoreType.DMA

    def early(n, w):
        return pl.BlockSpec((n, w), lambda i: (jnp.minimum(i, 3), 0))

    def late(n, w):
        return pl.BlockSpec((n, w), lambda i: (jnp.maximum(i - 4, 0), 0))

    return pl.pallas_call(
        functools.partial(forward_kernel, chunks, dp, span, batches, here),
        grid=(8,),
        out_shape=(
            shape((total, width), BF), shape((rows, width), BF), shape((rows, ff), BF), shape((rows, ff), BF),
            shape((rows, ff), BF), shape((rows, width), BF), shape((total, TILE), BF), shape((total, TILE), BF),
            shape((total, TILE), BF), shape((total, 1), F32), shape((rows, 256), BF), shape((total, 128), BF),
            shape((NE,) + dy.shape, BF),
            shape((dp, span[1], width), BF)),
        in_specs=[SMEM, whole(pick), early(step, width), early(step, mask.shape[1])] + [whole(v) for v in tables] + [whole(wg), whole(wu),
                  whole(router), ANY, ANY, ANY, ANY, ANY],
        out_specs=[late(step, width), early(half, width), early(half, ff), early(half, ff), early(half, ff),
                   late(half, width), early(step, TILE), early(step, TILE), early(step, TILE), early(step, 1),
                   early(half, 256), early(step, 128), ANY, ANY],
        scratch_shapes=[
            pltpu.VMEM((ff, width), BF), pltpu.VMEM((2 * TILE, width), BF), pltpu.VMEM((TILE, width), BF),
            pltpu.VMEM((rows, ff), BF), pltpu.VMEM((total, TILE), BF), pltpu.VMEM((total, 1), F32),
            pltpu.VMEM((total, 128), BF), dma((3 * dp,)), dma((3 * dp,))] + Gather.scratch(chunks) + Spread.scratch(dp),
        compiler_params=pltpu.CompilerParams(
            collective_id=cid, has_side_effects=True, vmem_limit_bytes=60 * 1024 * 1024),
        cost_estimate=COST,
        name="mixture_forward",
    )(lengths, pick, mix, mask, *tables, wg, wu, router, share, wda, wdb, down, dy)


def mixture_backward(pick, dy, wg, wu, share, wda, wdb, wdc, act, slo, eo, sact, sslo, gate, slot, token, part, cid, chunks=2):
    total, width = dy.shape
    step, half = total // NZ, total // NZ // 2
    ff = wg.shape[1]
    shape = jax.ShapeDtypeStruct
    rows = total // 2
    dp = wda.shape[0]
    _, own, _ = part.shape
    dma = pltpu.SemaphoreType.DMA
    return pl.pallas_call(
        functools.partial(backward_kernel, chunks),
        grid=(NZ,),
        out_shape=(
            shape((total, width + 128), BF), shape((rows, width), BF), shape((rows, ff), BF), shape((rows, ff), BF),
            shape((total, 2 * TILE), BF), shape((own, width), F32)),
        in_specs=[whole(pick), tiles(step, width), whole(wg), whole(wu), ANY, ANY, ANY, ANY,
                  tiles(half, ff), tiles(half, ff), tiles(half, width), tiles(step, TILE), tiles(step, TILE),
                  tiles(step, 1), tiles(half, 256), tiles(step, 128), ANY],
        out_specs=[tiles(step, width + 128), tiles(half, width), tiles(half, ff), tiles(half, ff),
                   tiles(step, 2 * TILE), pl.BlockSpec((own, width), lambda i: (0, 0))],
        scratch_shapes=[
            pltpu.VMEM((ff, width), BF), pltpu.VMEM((2 * TILE, width), BF), pltpu.VMEM((TILE, width), BF),
            dma((3 * dp,)), dma((3 * dp,))] + Scatter.scratch(own, width, chunks, BF),
        compiler_params=pltpu.CompilerParams(
            collective_id=cid, has_side_effects=True, vmem_limit_bytes=62 * 1024 * 1024),
        cost_estimate=COST,
        name="mixture_backward",
    )(pick, dy, wg, wu, share, wda, wdb, wdc, act, slo, eo, sact, sslo, gate, slot, token, part)


class ShareWork:
    ROWS = 256

    def __init__(self, ds_ref, sh_ref, mix_ref, dy_ref, out_ref, scratch):
        self.sources = (ds_ref, sh_ref, mix_ref, dy_ref)
        self.out = out_ref
        *self.buffers, self.gfan, self.gsd, self.sem = scratch
        self.steps = mix_ref.shape[0] // self.ROWS
        self.done = 0

    @staticmethod
    def scratch(width):
        r = ShareWork.ROWS
        return [pltpu.VMEM((2, r, w), BF) for w in (2 * TILE, TILE, width, width)] + [
            pltpu.VMEM((2 * TILE, width), F32), pltpu.VMEM((TILE, width), F32), pltpu.SemaphoreType.DMA((2, 4))]

    COUNT = 7

    def copies(self, n):
        return [pltpu.make_async_copy(src.at[pl.ds(n * self.ROWS, self.ROWS)], buf.at[n % 2], self.sem.at[n % 2, i])
                for i, (src, buf) in enumerate(zip(self.sources, self.buffers))]

    def start(self):
        for copy in self.copies(0):
            copy.start()
        self.gfan[...] = jnp.zeros_like(self.gfan)
        self.gsd[...] = jnp.zeros_like(self.gsd)

    def step(self):
        n = self.done
        if n == self.steps:
            return
        self.done += 1
        for copy in self.copies(n):
            copy.wait()
        if n + 1 < self.steps:
            for copy in self.copies(n + 1):
                copy.start()
        ds, sh, mix, dy = self.buffers

        def columns(j, _):
            self.gfan[:, lanes(j)] += mm_lead(ds[n % 2], mix[n % 2, :, lanes(j)])
            self.gsd[:, lanes(j)] += mm_lead(sh[n % 2], dy[n % 2, :, lanes(j)])
            return 0

        lax.fori_loop(0, mix.shape[2] // WIDE, columns, 0)

    def finish(self):
        while self.done < self.steps:
            self.step()
        dp, rows, w = self.out.shape
        n = rows // 3
        for d in range(dp):
            cols = slice(d * w, (d + 1) * w)
            self.out[d, :n] = self.gfan[:n, cols].astype(BF)
            self.out[d, n:2 * n] = self.gfan[TILE:TILE + n, cols].astype(BF)
            self.out[d, 2 * n:] = self.gsd[:n, cols].astype(BF)


class WeightWork:
    COUNT = 6
    ROWS = 256

    def __init__(self, lhs, rhs, outs, scratch):
        self.sources, self.outs = (lhs,) + tuple(rhs), outs
        *self.held, self.buf, self.in_sem, self.out_sem = scratch
        self.steps = lhs.shape[1] // self.ROWS

    @staticmethod
    def scratch(lhs, rhs):
        dma = pltpu.SemaphoreType.DMA
        return [pltpu.VMEM(v.shape, BF) for v in (lhs,) + tuple(rhs)] + [
            pltpu.VMEM((2, WeightWork.ROWS, rhs[0].shape[1]), BF), dma((3,)), dma((2,))]

    def loads(self):
        return [pltpu.make_async_copy(v, held, self.in_sem.at[i])
                for i, (v, held) in enumerate(zip(self.sources, self.held))]

    def start(self):
        for copy in self.loads():
            copy.start()

    def ready(self):
        for copy in self.loads():
            copy.wait()

    def store(self, p, n):
        at = pl.ds(pl.multiple_of(n * self.ROWS, self.ROWS), self.ROWS)
        return pltpu.make_async_copy(self.buf.at[p], self.outs[p].at[at], self.out_sem.at[p])

    def step(self, begin, end):
        def body(n, _):
            left = self.held[0][:, pl.ds(pl.multiple_of(n * self.ROWS, self.ROWS), self.ROWS)]
            for p in range(2):
                @pl.when(n > 0)
                def _():
                    self.store(p, n - 1).wait()

                rhs = self.held[1 + p]
                width = rhs.shape[1]
                for at in range(0, width, WIDE):
                    size = min(WIDE, width - at)
                    self.buf[p, :, at:at + size] = mm_lead(left, rhs[:, at:at + size]).astype(BF)
                self.store(p, n).start()
            return 0

        lax.fori_loop(begin, end, body, 0)

    def finish(self):
        for p in range(2):
            self.store(p, self.steps - 1).wait()


def scatter_share_kernel(chunks, dp, p_ref, ds_ref, sh_ref, mix_ref, dy_ref, rows_ref, dg_ref, du_ref, down_ref,
                         o_ref, g_ref, ggate_ref, gup_ref, far_ref, *scratch):
    ns, nw = Scatter.COUNT, ShareWork.COUNT
    s = Scatter(p_ref, o_ref, chunks, scratch[:ns])
    share = ShareWork(ds_ref, sh_ref, mix_ref, dy_ref, g_ref, scratch[ns:ns + nw])
    work = WeightWork(rows_ref, (dg_ref, du_ref), (ggate_ref, gup_ref), scratch[ns + nw:-2])
    swap = Swap(dp, down_ref, far_ref, scratch[-2:])
    enter(s.me, s.z, s.core, s.side, dp)
    swap.start()
    s.start()
    work.start()
    share.start()
    s.first(0)
    s.first(1)
    work.ready()
    third = work.steps // 3
    work.step(0, third)
    s.second(0)
    s.first(2)
    s.first(3)
    work.step(third, 2 * third)
    s.second(1)
    work.step(2 * third, work.steps)
    s.second(2)
    work.finish()
    while share.done < share.steps:
        share.step()
    s.second(3)
    share.finish()
    s.finish()
    swap.finish()


def scatter_share(p, ds, sh, mix, dy, rows, dg, du, down, share_shape, cid, chunks=2):
    _, n, width = p.shape
    shape = jax.ShapeDtypeStruct
    grad = shape((rows.shape[1], dg.shape[1]), BF)
    return pl.pallas_call(
        functools.partial(scatter_share_kernel, chunks, down.shape[0]),
        out_shape=(shape((n, width), F32), shape(share_shape, BF), grad, grad,
                   shape((down.shape[0] - 1,) + down.shape[1:], BF)),
        in_specs=[ANY] * 9,
        out_specs=(VMEM, VMEM, ANY, ANY, ANY),
        scratch_shapes=Scatter.scratch(n, width, chunks, p.dtype) + ShareWork.scratch(mix.shape[1])
        + WeightWork.scratch(rows, (dg, du)) + Swap.scratch(down.shape[0]),
        compiler_params=pltpu.CompilerParams(
            collective_id=cid, has_side_effects=True, vmem_limit_bytes=60 * 1024 * 1024),
        cost_estimate=COST,
        name="scatter_share",
    )(p, ds, sh, mix, dy, rows, dg, du, down)


def turn(v, cosine, sine):
    half = v.shape[1] // 2
    a, b = v[:, :half], v[:, half:]
    return jnp.concatenate([a * cosine - b * sine, b * cosine + a * sine], axis=1)


def project_kernel(x_ref, gain_ref, lgain_ref, wq_ref, wl_ref, we_ref, cos_ref, sin_ref,
                   h_ref, q_ref, k_ref, v_ref, lat_ref):
    blocks = x_ref.shape[0]
    batches, rows, _ = q_ref.shape
    here = rows // blocks
    x = x_ref[...].reshape(blocks * batches * here, x_ref.shape[2]).astype(F32)
    h = x * lax.rsqrt(jnp.mean(x * x, axis=1, keepdims=True) + 1e-6) * gain_ref[...]
    h = h.astype(BF)
    h_ref[...] = h
    raw = mm(h, wq_ref[...])
    raw_lat = mm(h, wl_ref[...])
    cosine, sine = cos_ref[...], sin_ref[...]
    zeros = jnp.zeros((raw.shape[0], 64), BF)
    q = jnp.concatenate([raw[:, :128].astype(BF), turn(raw[:, 128:192], cosine, sine).astype(BF), zeros], axis=1)
    k_rope = turn(raw_lat[:, 512:576], cosine, sine).astype(BF)
    lat = raw_lat[:, :512]
    lat = (lat * lax.rsqrt(jnp.mean(lat * lat, axis=1, keepdims=True) + 1e-6) * lgain_ref[...]).astype(BF)
    expanded = mm(lat, we_ref[...]).astype(BF)
    k = jnp.concatenate([expanded[:, :128], k_rope, zeros], axis=1)
    for e in range(blocks):
        for m in range(batches):
            src = slice((e * batches + m) * here, (e * batches + m + 1) * here)
            dst = slice(e * here, (e + 1) * here)
            q_ref[m, dst] = q[src]
            k_ref[m, dst] = k[src]
            v_ref[m, dst] = expanded[src, 128:]
            lat_ref[m, dst] = lat[src]


def project(x_all, gain, lgain, wq, wl, we, cosine, sine, batches):
    groups, rows, width = x_all.shape
    here = rows // batches
    per = 4
    seq = groups * here
    shape = jax.ShapeDtypeStruct

    def whole(v):
        return pl.BlockSpec(v.shape, lambda i: (0, 0))

    def by_seq(w):
        return pl.BlockSpec((batches, per * here, w), lambda i: (0, i, 0))

    table = pl.BlockSpec((per * rows, 32), lambda i: (i, 0))
    return pl.pallas_call(
        project_kernel,
        grid=(groups // per,),
        out_shape=(shape((groups * rows, width), BF), shape((batches, seq, 256), BF), shape((batches, seq, 256), BF),
                   shape((batches, seq, 128), BF), shape((batches, seq, 512), BF)),
        in_specs=[pl.BlockSpec((per, rows, width), lambda i: (i, 0, 0)), whole(gain), whole(lgain), whole(wq), whole(wl), whole(we),
                  table, table],
        out_specs=[pl.BlockSpec((per * rows, width), lambda i: (i, 0)), by_seq(256), by_seq(256), by_seq(128), by_seq(512)],
        compiler_params=pltpu.CompilerParams(vmem_limit_bytes=48 * 1024 * 1024),
        cost_estimate=pl.CostEstimate(flops=7_000_000_000, bytes_accessed=20_000_000, transcendentals=0),
        name="project",
    )(x_all, gain, lgain, wq, wl, we, cosine, sine)


ROWS = 256
SCALE = 192.0 ** -0.5


def held_scores(q, k, first, length):
    s = mm_t(q, k) * SCALE
    t = lax.broadcasted_iota(jnp.int32, s.shape, 0) + first
    u = lax.broadcasted_iota(jnp.int32, s.shape, 1)
    return jnp.where((u <= t) & (u < length), s, -1e30)


def attend_kernel(dp, span, len_ref, q_ref, k_ref, v_ref, wo_ref, side_ref, sum_ref, att_ref, lse_ref, side_out,
                  part, *scratch):
    m = pl.program_id(0)
    length = len_ref[m]
    seq = q_ref.shape[1]
    groups, rows, width = part.shape
    here = rows // 2
    per = ROWS // here
    sc = Scatter(part, sum_ref, 2, scratch[:Scatter.COUNT])
    job = side_job(dp, span, side_ref, side_out, scratch[Scatter.COUNT:])

    @pl.when(m == 0)
    def _():
        enter(sc.me, sc.z, sc.core, sc.side, dp)
        job.start()

    mine = pl.ds(pl.multiple_of(m * here, here), here)
    for i in range(seq // ROWS):
        tile = slice(i * ROWS, (i + 1) * ROWS)
        ext = (i + 1) * ROWS
        s = held_scores(q_ref[0, tile], k_ref[0, :ext], i * ROWS, length)
        peak = jnp.max(s, axis=1, keepdims=True)
        raised = jnp.exp(s - peak)
        total = jnp.sum(raised, axis=1, keepdims=True)
        lse_ref[0, tile] = peak + jnp.log(total)
        p = (raised / total).astype(BF)
        att = mm(p, v_ref[0, :ext]).astype(BF)
        att_ref[i * per:(i + 1) * per, 0] = att.reshape(per, here, att.shape[1])
        for j in range(width // 512):
            cols = slice(j * 512, (j + 1) * 512)
            part[i * per:(i + 1) * per, mine, cols] = mm(att, wo_ref[:, cols]).astype(BF).reshape(per, here, 512)

        @pl.when(m == 1)
        def _():
            sc.first(i, [0])

    @pl.when(m == 0)
    def _():
        sc.start([0])

    @pl.when(m == 1)
    def _():
        sc.start([1])
        sc.first(0, [1])
        sc.first(1, [1])
        sc.second(0, [0])
        sc.first(2, [1])
        sc.first(3, [1])
        sc.second(1, [0])
        sc.second(2, [0])
        sc.second(0, [1])
        sc.second(3, [0])
        sc.second(1, [1])
        sc.second(2, [1])
        sc.second(3, [1])
        sc.finish()
        job.finish()


def attend(lengths, q, k, v, wo, groups, dp, span, side, cid):
    batches, seq, _ = q.shape
    here = seq // groups
    width = wo.shape[1]
    shape = jax.ShapeDtypeStruct

    def by_seq(w):
        return pl.BlockSpec((1, seq, w), lambda m: (m, 0, 0))

    return pl.pallas_call(
        functools.partial(attend_kernel, dp, span),
        grid=(batches,),
        out_shape=(shape((batches * here, width), F32), shape((groups, batches, here, 128), BF),
                   shape((batches, seq, 1), F32), side_shape(dp, span, side)),
        in_specs=[pl.BlockSpec(memory_space=pltpu.SMEM), by_seq(256), by_seq(256), by_seq(128),
                  pl.BlockSpec(wo.shape, lambda m: (0, 0)), ANY],
        out_specs=[pl.BlockSpec((batches * here, width), lambda m: (0, 0)),
                   pl.BlockSpec((groups, 1, here, 128), lambda m: (0, m, 0, 0)), by_seq(1), ANY],
        scratch_shapes=[pltpu.VMEM((groups, batches * here, width), BF)]
        + Scatter.scratch(batches * here, width, 2, BF) + side_scratch(dp, span),
        compiler_params=pltpu.CompilerParams(
            collective_id=cid, has_side_effects=True, vmem_limit_bytes=60 * 1024 * 1024),
        cost_estimate=COST,
        name="attend",
    )(lengths, q, k, v, wo, side)


def attend_back_kernel(dp, len_ref, own_ref, side_ref, h_ref, q_ref, k_ref, v_ref, lat_ref, att_ref, lse_ref, wo_ref, wq_ref, we_ref,
                       cos_ref, sin_ref, part_ref, gwq_ref, gwo_out, gwe_out, side_out,
                       dout_ref, dk, dv, datt, gwq, gwo_ref, gwe_ref, *scratch):
    m = pl.program_id(0)
    length = len_ref[m]
    seq = q_ref.shape[1]
    groups, _, width = dout_ref.shape
    here = h_ref.shape[2]
    per = ROWS // here
    g = Gather(own_ref, dout_ref, 2, scratch[:Gather.COUNT])
    job = side_job(dp, None, side_ref, side_out, scratch[Gather.COUNT:])

    @pl.when(m == 0)
    def _():
        enter(g.me, g.z, g.core, g.side, dp)
        job.start()
        g.start([0])
        g.start([1])
        g.round(1, [0])
        g.round(2, [0])
        g.round(1, [1])
        g.round(3, [0])
        g.round(2, [1])
        g.round(4, [0])
        g.kept().wait()
        g.landed([0])
        gwo_ref[...] = jnp.zeros_like(gwo_ref)
        gwe_ref[...] = jnp.zeros_like(gwe_ref)
        gwq[...] = jnp.zeros_like(gwq)

    @pl.when(m == 1)
    def _():
        g.round(4, [1])
        g.landed([1])

    mine = pl.ds(pl.multiple_of(m * here, here), here)
    for j in range(4):
        blocks = slice(j * groups // 4, (j + 1) * groups // 4)
        dout = dout_ref[blocks, mine].reshape(seq // 4, width)
        rows = slice(j * seq // 4, (j + 1) * seq // 4)
        datt[rows] = mm_t(dout, wo_ref[...]).astype(BF)
        gwo_ref[...] += mm_lead(att_ref[blocks].reshape(seq // 4, 128), dout)
    @pl.when(m == 0)
    def _():
        g.round(3, [1])

    dk[...] = jnp.zeros_like(dk)
    dv[...] = jnp.zeros_like(dv)
    for i in range(seq // ROWS):
        tile = slice(i * ROWS, (i + 1) * ROWS)
        ext = (i + 1) * ROWS
        q = q_ref[0, tile]
        p = jnp.exp(held_scores(q, k_ref[0, :ext], i * ROWS, length) - lse_ref[0, tile])
        da = datt[tile]
        dp = mm_t(da, v_ref[0, :ext])
        inner = jnp.sum(dp * p, axis=1, keepdims=True)
        ds = (p * (dp - inner)).astype(BF)
        dq = mm(ds, k_ref[0, :ext]) * SCALE
        dk[:ext] += mm_lead(ds, q)
        dv[:ext] += mm_lead(p.astype(BF), da)
        rope = turn(dq[:, 128:192], cos_ref[tile], -sin_ref[tile])
        dq = jnp.concatenate([dq[:, :128].astype(BF), rope.astype(BF), jnp.zeros((ROWS, 64), BF)], axis=1)
        hidden = h_ref[i * per:(i + 1) * per, 0].reshape(ROWS, width)
        for j in range(width // 512):
            cols = slice(j * 512, (j + 1) * 512)
            gwq[:, cols] += mm_lead(dq, hidden[:, cols])
        for j in range(width // 512):
            cols = slice(j * 512, (j + 1) * 512)
            part_ref[i * per:(i + 1) * per, 0, :, cols] = mm_t(dq, wq_ref[cols]).astype(BF).reshape(per, here, 512)
    for i in range(seq // ROWS):
        tile = slice(i * ROWS, (i + 1) * ROWS)
        d_k = dk[tile] * SCALE
        d_exp = jnp.concatenate([d_k[:, :128].astype(BF), dv[tile].astype(BF)], axis=1)
        gwe_ref[...] += mm_lead(lat_ref[0, tile], d_exp)
        d_lat = mm_t(d_exp, we_ref[...]).astype(BF)
        tail = jnp.concatenate([d_lat, d_k[:, 128:].astype(BF)], axis=1)
        pad = part_ref.shape[3] - width - tail.shape[1]
        if pad > 0:
            tail = jnp.concatenate([tail, jnp.zeros((ROWS, pad), BF)], axis=1)
        part_ref[i * per:(i + 1) * per, 0, :, width:] = tail[:, :part_ref.shape[3] - width].reshape(per, here, -1)

    @pl.when(m == pl.num_programs(0) - 1)
    def _():
        for j in range(width // 256):
            cols = slice(j * 256, (j + 1) * 256)
            gwq_ref[cols] = gwq[:, cols].T.astype(BF)
        gwo_out[...] = gwo_ref[...].astype(BF)
        gwe_out[...] = gwe_ref[...].astype(BF)
        g.finish(False)
        job.finish()


def attend_back(dp, lengths, dout, side, h, q, k, v, lat, att, lse, wo, wq, we, cosine, sine, tail, cid):
    groups, batches, here, width = h.shape
    seq = groups * here
    shape = jax.ShapeDtypeStruct

    def by_seq(w):
        return pl.BlockSpec((1, seq, w), lambda m: (m, 0, 0))

    def by_dev(w):
        return pl.BlockSpec((groups, 1, here, w), lambda m: (0, m, 0, 0))

    def whole(v):
        return pl.BlockSpec(v.shape, lambda m: (0, 0))

    return pl.pallas_call(
        functools.partial(attend_back_kernel, dp),
        grid=(batches,),
        out_shape=(shape((groups, batches, here, width + tail), BF), shape(wq.shape, BF),
                   shape(wo.shape, BF), shape(we.shape, BF), side_shape(dp, None, side)),
        in_specs=[pl.BlockSpec(memory_space=pltpu.SMEM), ANY, ANY, by_dev(width), by_seq(256), by_seq(256), by_seq(128),
                  by_seq(512), by_dev(128), by_seq(1), whole(wo), whole(wq), whole(we), whole(cosine), whole(sine)],
        out_specs=[by_dev(width + tail), whole(wq), whole(wo), whole(we), ANY],
        scratch_shapes=[pltpu.VMEM((groups, batches * here, width), BF), pltpu.VMEM((seq, 256), F32), pltpu.VMEM((seq, 128), F32), pltpu.VMEM((seq, 128), BF),
                        pltpu.VMEM((256, width), F32), pltpu.VMEM(wo.shape, F32), pltpu.VMEM(we.shape, F32)]
        + Gather.scratch(2) + side_scratch(dp, None),
        compiler_params=pltpu.CompilerParams(
            collective_id=cid, has_side_effects=True, vmem_limit_bytes=60 * 1024 * 1024),
        cost_estimate=COST,
        name="attend_back",
    )(lengths, dout, side, h, q, k, v, lat, att, lse, wo, wq, we, cosine, sine)


def turn_kernel(v_ref, o_ref):
    for i in range(v_ref.shape[0] // 128):
        rows = slice(i * 128, (i + 1) * 128)
        o_ref[:, rows] = v_ref[rows].astype(F32).T.astype(o_ref.dtype)


def turned(v, block):
    return pl.pallas_call(
        turn_kernel,
        grid=(1,),
        out_shape=jax.ShapeDtypeStruct((128, v.shape[0]), v.dtype),
        in_specs=[pl.BlockSpec((v.shape[0], 128), lambda i: (0, block))],
        out_specs=pl.BlockSpec((128, v.shape[0]), lambda i: (0, 0)),
        compiler_params=pltpu.CompilerParams(vmem_limit_bytes=16 * 1024 * 1024),
        cost_estimate=COST,
        name="turned",
    )(v)


def split_rows(v):
    high = v.astype(BF)
    return [high, (v - high.astype(F32)).astype(BF)]


def own_back_kernel(dp, back_ref, x_ref, mix_ref, logit_ref, gmix_ref, gain_ref, lgain_ref, small_ref, cos_ref, sin_ref,
                    mid_ref, place_ref, grad_ref, out_ref):
    width = x_ref.shape[1]
    rows_w = out_ref.shape[1] // dp
    lanes_w = out_ref.shape[2]
    x = x_ref[...].astype(F32)
    factor = lax.rsqrt(jnp.mean(x * x, axis=1, keepdims=True) + 1e-6)
    unit = x * factor
    hidden = (unit * gain_ref[...]).astype(BF)
    lat = mm(hidden, small_ref[:, :512])
    factor_l = lax.rsqrt(jnp.mean(lat * lat, axis=1, keepdims=True) + 1e-6)
    unit_l = lat * factor_l
    d_lat = back_ref[:, width:width + 512]
    scaled = d_lat * lgain_ref[...]
    d_in = factor_l * (scaled - unit_l * jnp.mean(scaled * unit_l, axis=1, keepdims=True))
    g_lat = jnp.sum(d_lat * unit_l, axis=0, keepdims=True)
    d_rope = turn(back_ref[:, width + 512:width + 576], cos_ref[...], -sin_ref[...])
    tokens = x.shape[0]
    d_raw = jnp.concatenate(
        [d_in.astype(BF), d_rope.astype(BF), jnp.zeros((tokens, lanes_w - 576), BF)], axis=1)
    d_hidden = back_ref[:, :width] + mm_t(d_raw, small_ref[...])
    scaled = d_hidden * gain_ref[...]
    grad_ref[...] = mid_ref[...] + factor * (scaled - unit * jnp.mean(scaled * unit, axis=1, keepdims=True))
    g_gain = jnp.sum(d_hidden * unit, axis=0, keepdims=True)
    spread = [mm(v, place_ref[...]).astype(BF) for v in split_rows(g_lat)]
    extra = split_rows(g_gain) + split_rows(gmix_ref[...]) + spread + [jnp.zeros((10, width), BF)]
    left = jnp.concatenate([hidden, mix_ref[...]] + extra, axis=0)
    logit = jnp.concatenate(
        [jnp.zeros((tokens, 576), BF), logit_ref[...], jnp.zeros((tokens, lanes_w - 592), BF)], axis=1)
    n = lax.broadcasted_iota(jnp.int32, (16, lanes_w), 0)
    at = 592 + (n >> 1)
    hot = jnp.where((lax.broadcasted_iota(jnp.int32, (16, lanes_w), 1) == at) & (n < 6), 1.0, 0.0).astype(BF)
    right = jnp.concatenate([d_raw, logit, hot], axis=0)
    for j in range(width // 256):
        part = mm_lead(left[:, j * 256:(j + 1) * 256], right).astype(BF)
        for i in range(256 // rows_w):
            owner = j * (256 // rows_w) + i
            d, e = owner // NE, owner % NE
            out_ref[e, d * rows_w:(d + 1) * rows_w] = part[i * rows_w:(i + 1) * rows_w]


def own_back(dp, back, x, mix, logit, gmix, gain, lgain, small, cosine, sine, mid, rows_l):
    tokens, width = x.shape
    rows_w = width // (dp * NE)
    count = np.arange(width)
    place = (count // rows_w * rows_l + count % rows_w)[None, :] == np.arange(512)[:, None]
    place = place & (count % rows_w < rows_l)[None, :]
    shape = jax.ShapeDtypeStruct
    return pl.pallas_call(
        functools.partial(own_back_kernel, dp),
        out_shape=(shape((tokens, width), F32), shape((NE, dp * rows_w, small.shape[1]), BF)),
        in_specs=[VMEM] * 12,
        out_specs=(VMEM, VMEM),
        compiler_params=pltpu.CompilerParams(vmem_limit_bytes=40 * 1024 * 1024),
        cost_estimate=COST,
        name="own_back",
    )(back, x, mix, logit, gmix, gain, lgain, small, cosine, sine, mid, jnp.asarray(place.astype(np.float32), BF))


def widen_kernel(gate_ref, up_ref, down_ref, down_far, share_ref, share_far, gate_out, up_out, down_out, sg_out, su_out,
                 sd_out):
    gate_out[...] = gate_ref[...].astype(F32)
    up_out[...] = up_ref[...].astype(F32)
    down = down_ref[...].astype(F32)
    for r in range(down_far.shape[0]):
        down = down + down_far[r].astype(F32)
    down_out[...] = down

    @pl.when(pl.program_id(0) == 0)
    def _():
        n = sg_out.shape[0]
        for i, out in enumerate((sg_out, su_out, sd_out)):
            rows = slice(i * n, (i + 1) * n)
            v = share_ref[rows].astype(F32)
            for r in range(share_far.shape[0]):
                v = v + share_far[r, rows].astype(F32)
            out[...] = v


def widen(gate, up, down, down_far, share, share_far):
    steps = 2 if down.shape[0] % 32 == 0 else 1
    shape = jax.ShapeDtypeStruct

    def cut(v):
        return pl.BlockSpec((v.shape[0] // steps, v.shape[1]), lambda i: (i, 0))

    def cut_far(v):
        return pl.BlockSpec((v.shape[0], v.shape[1] // steps, v.shape[2]), lambda i: (0, i, 0))

    def full(shape_):
        zeros = (0,) * len(shape_)
        return pl.BlockSpec(shape_, lambda i: zeros)

    third = (share.shape[0] // 3, share.shape[1])
    return pl.pallas_call(
        widen_kernel,
        grid=(steps,),
        out_shape=tuple(shape(v.shape, F32) for v in (gate, up, down)) + (shape(third, F32),) * 3,
        in_specs=[cut(gate), cut(up), cut(down), cut_far(down_far), full(share.shape), full(share_far.shape)],
        out_specs=[cut(gate), cut(up), cut(down)] + [full(third)] * 3,
        compiler_params=pltpu.CompilerParams(vmem_limit_bytes=56 * 1024 * 1024),
        cost_estimate=COST,
        name="widen",
    )(gate, up, down, down_far, share, share_far)


H = 16
QK_NOPE = 128
ROPE = 64
V_DIM = 128
KV_RANK = 512
GROUPS = 16
EPSILON = 1e-06
ROTARY_BASE = 10000.0


def product(left_side, right_side):
    return jnp.dot(left_side, right_side, preferred_element_type=F32)


def product_lead(left_side, right_side):
    return lax.dot_general(
        left_side, right_side, (((0,), (0,)), ((), ())), preferred_element_type=F32
    )


def product_trail(left_side, right_side):
    return lax.dot_general(
        left_side, right_side, (((1,), (1,)), ((), ())), preferred_element_type=F32
    )


def rotary_tables(count):
    frequency = ROTARY_BASE ** (-np.arange(ROPE // 2, dtype=np.float32) * np.float32(2.0) / np.float32(ROPE))
    angles = np.arange(count, dtype=np.float32)[:, None] * frequency.astype(np.float32)[None, :]
    return np.cos(angles).astype(np.float32), np.sin(angles).astype(np.float32)


def rotate(values, cosine, sine_table):
    first_half, second_half = jnp.split(values, 2, axis=-1)
    return jnp.concatenate(
        [
            first_half * cosine - second_half * sine_table,
            second_half * cosine + first_half * sine_table,
        ],
        axis=-1,
    )


def norm_forward(values, gains):
    factor = lax.rsqrt(jnp.mean(values * values, axis=-1, keepdims=True) + EPSILON)
    normed = values * factor
    return (normed * gains, normed, factor)


def norm_backward(gradient, normed, factor, gains):
    gain_grad = jnp.sum(gradient * normed, axis=0)
    scaled = gradient * gains
    return (
        factor * (scaled - normed * jnp.mean(scaled * normed, axis=-1, keepdims=True)),
        gain_grad,
    )


def selected_experts(routes):
    chosen = routes[:, :, None] == jnp.arange(GROUPS, dtype=routes.dtype)
    return jnp.any(chosen, axis=1)


def masked_softmax(logits, mask):
    held = jnp.where(mask, logits, -1e30)
    peak = jnp.max(held, axis=-1, keepdims=True)
    raised = jnp.where(mask, jnp.exp(held - peak), 0.0)
    return raised / jnp.sum(raised, axis=-1, keepdims=True)


def per_device(
    layer_input,
    out_cotangent,
    lengths,
    routes,
    attn_gain,
    query_weight,
    latent_weight,
    latent_gain,
    expand_weight,
    output_weight,
    mixer_gain,
    router_weight,
    gate_weight,
    up_weight,
    down_weight,
    shared_gate,
    shared_up,
    shared_down,
):
    dp = lax.axis_size("dp")
    me = lax.axis_index("expert")
    plane = lax.axis_index("dp")
    batches, _, here, width = layer_input.shape
    own = batches * here
    total = own * GROUPS
    seq_total = here * GROUPS
    rows_w = query_weight.shape[0]
    rows_l = expand_weight.shape[0]

    x_own = layer_input.reshape(own, width)
    mask_own = selected_experts(routes.reshape(own, -1))
    mask_columns = mask_own.astype(BF).reshape(rows_w, -1)
    small_width = -(-(595 + mask_columns.shape[1]) // 128) * 128
    latent_column = jnp.zeros((rows_w,), BF).at[:rows_l].set(latent_gain)
    small = jnp.concatenate(
        [
            latent_weight,
            router_weight,
            attn_gain[:, None],
            mixer_gain[:, None],
            latent_column[:, None],
            mask_columns,
            jnp.zeros((rows_w, small_width - 595 - mask_columns.shape[1]), BF),
        ],
        axis=1,
    )
    query_parts = query_weight.reshape(rows_w, H, QK_NOPE + ROPE).transpose(1, 0, 2)
    expand_parts = expand_weight.reshape(rows_l, H, QK_NOPE + V_DIM).transpose(1, 0, 2)
    expand_parts = expand_parts.reshape(H, rows_l, 4, ROPE).swapaxes(1, 2).reshape(H, rows_w, ROPE)
    parts = jnp.concatenate([query_parts, expand_parts], axis=2)
    x_all, small, parts_head, output_head = opening(dp, x_own, small, parts, output_weight, 1)
    x_all = x_all.reshape(total, width)
    mask_all = lax.dynamic_index_in_dim(small, plane, 0, False)[..., 595 : 595 + mask_columns.shape[1]]
    mask_all = mask_all.reshape(total, GROUPS)
    small = small.reshape(width, small_width)
    parts_head = parts_head.reshape(width, TILE)
    latent_full = small[:, :576]
    lines = turned(small, 4)
    router_lines = lines[64:80]
    gain_attn = lines[80].astype(F32)
    gain_mixer = lines[81].astype(F32)
    gain_latent = lines[82].reshape(dp * GROUPS, rows_w)[:, :rows_l].reshape(-1).astype(F32)
    expand_head = parts_head[:, QK_NOPE + ROPE :].reshape(dp * GROUPS, 4, rows_l, ROPE)
    expand_head = expand_head.swapaxes(1, 2).reshape(KV_RANK, QK_NOPE + V_DIM)
    output_head = output_head.reshape(V_DIM, width)

    ff = gate_weight.shape[2]
    share_own = jnp.concatenate([shared_gate.T, shared_up.T, shared_down], axis=0)
    share_width = shared_down.shape[0]
    gate_full = lax.all_gather(gate_weight[0], "dp", axis=0, tiled=True)
    up_full = lax.all_gather(up_weight[0], "dp", axis=0, tiled=True)
    share_full = lax.all_gather(share_own, "dp", axis=0)
    seq_lengths = lengths.reshape(batches)
    own_positions = me * here + jnp.arange(here, dtype=jnp.int32)
    valid_own = (own_positions[None, :] < seq_lengths[:, None]).reshape(own).astype(F32)
    cosine, sine_table = rotary_tables(seq_total)

    grad_own = out_cotangent.reshape(own, width) * valid_own[:, None].astype(BF)

    def by_token(table):
        return jnp.asarray(np.broadcast_to(
            table.reshape(GROUPS, 1, here, -1), (GROUPS, batches, here, table.shape[1])).reshape(total, -1))

    hidden_all, query, key, values, latent = project(
        x_all.reshape(GROUPS, own, width), gain_attn[None], gain_latent[None], parts_head, small, expand_head,
        by_token(cosine), by_token(sine_table), batches)
    down_own = down_weight[0]
    cut = down_own.shape[0] * 3 // 160 * 16
    cuts = (0, cut, 2 * cut + cut // 48 * 16, down_own.shape[0])
    spans = [(first, last - first) for first, last in zip(cuts, cuts[1:])]
    attn_out, attended, log_total, down_a = attend(
        seq_lengths, query, key, values, output_head, GROUPS, dp, spans[0], down_own, 2)

    x_wide = x_own.astype(F32)
    middle = x_wide + attn_out
    normed_mix, unit_mix, factor_mix = norm_forward(middle, gain_mixer)
    hidden_mix = normed_mix.astype(BF)
    mix_all, down_b = gather16(hidden_mix, 3, dp=dp, span=spans[1], side=down_own)
    mix_all = mix_all.reshape(total, width)

    lane = jnp.arange(128)[None, :]
    pick = jnp.concatenate([lane == me, lane == me + GROUPS], axis=1).astype(F32)
    (out_part, rows, hidden, act, slope, result, share_hidden, share_act, share_slope, gates, to_slot, to_token,
     grad_all, down_c) = mixture_forward(
        dp, batches, here, seq_lengths, pick, mix_all, mask_all, gate_full, up_full, router_lines, share_full,
        down_a, down_b, spans[2], down_own, grad_own, 4)
    grad_all = grad_all.reshape(total, width)
    mix_part, grad_result, grad_gate_in, grad_up_in, grad_share_in, mixed = mixture_backward(
        pick, grad_all, gate_full, up_full, share_full, down_a, down_b, down_c, act, slope, result,
        share_act, share_slope, gates, to_slot, to_token, out_part.reshape(GROUPS, own, width), 8)
    grad_down = product_lead(hidden, grad_result).astype(BF)
    grad_down = grad_down.reshape(dp, ff // dp, width)
    mix_sum, grad_share, grad_gate, grad_up, far_down = scatter_share(
        mix_part.reshape(GROUPS, own, width + 128), grad_share_in, share_hidden, mix_all, grad_all,
        rows, grad_gate_in, grad_up_in, grad_down, share_full.shape, 5)
    down_own_grad = lax.dynamic_index_in_dim(grad_down, plane, 0, False)
    layer_output = valid_own[:, None] * (middle + mixed)

    out_gate = lax.psum_scatter(grad_gate, "dp", scatter_dimension=0, tiled=True)
    out_up = lax.psum_scatter(grad_up, "dp", scatter_dimension=0, tiled=True)

    soft_own = masked_softmax(product_trail(hidden_mix, router_lines), mask_own)
    grad_masked = (mix_sum[:, width : width + GROUPS] + mix_sum[:, width + GROUPS : width + 2 * GROUPS])
    grad_masked = grad_masked * valid_own[:, None]
    grad_logits = soft_own * (grad_masked - jnp.sum(grad_masked * soft_own, axis=1, keepdims=True))
    grad_logits = grad_logits.astype(BF)
    grad_mix = mix_sum[:, :width] + product(grad_logits, router_lines)
    grad_middle_norm, grad_gain_mixer = norm_backward(grad_mix, unit_mix, factor_mix, gain_mixer)
    grad_middle = grad_own.astype(F32) + grad_middle_norm

    back_part, grad_query_w, grad_output, grad_expand, share_far = attend_back(
        dp, seq_lengths, grad_middle.astype(BF), grad_share, hidden_all.reshape(GROUPS, batches, here, width), query, key,
        values, latent, attended, log_total, output_head, parts_head, expand_head, jnp.asarray(cosine),
        jnp.asarray(sine_table), 640, 6)
    share_own_grad = lax.dynamic_index_in_dim(grad_share, plane, 0, False)
    grad_expand = grad_expand.reshape(dp * GROUPS, rows_l, 4, ROPE).swapaxes(1, 2).reshape(width, ROPE)
    parts_grad = grad_query_w + jnp.pad(grad_expand, ((0, 0), (QK_NOPE + ROPE, 0)))
    parts_grad = parts_grad.reshape(dp, GROUPS, rows_w, TILE)
    rows_grad = grad_output.reshape(dp, rows_w, width)
    back_sum, parts_far, rows_far = returning(
        dp, back_part.reshape(GROUPS, own, back_part.shape[3]), parts_grad, rows_grad, 7)
    parts_sum = lax.dynamic_index_in_dim(parts_grad, plane, 0, False).astype(F32)
    parts_sum = (parts_sum + jnp.sum(parts_far.astype(F32), axis=0)).astype(BF)
    rows_sum = (rows_grad.astype(F32) + jnp.sum(rows_far.astype(F32), axis=0)).astype(BF)

    def own_table(table):
        own_rows = lax.dynamic_slice_in_dim(jnp.asarray(table), me * here, here)
        return jnp.broadcast_to(own_rows[None], (batches, here, ROPE // 2)).reshape(own, ROPE // 2)

    grad_input, small_grad = own_back(
        dp, back_sum, x_own, hidden_mix, grad_logits, grad_gain_mixer[None], gain_attn[None], gain_latent[None], small,
        own_table(cosine), own_table(sine_table), grad_middle, rows_l)
    small_sum, out_query, out_expand, out_output = closing(dp, small_grad, parts_sum, rows_sum, rows_l, 9)

    out_gate, out_up, out_down, out_sgate, out_sup, out_sdown = widen(
        out_gate, out_up, down_own_grad, far_down, share_own_grad, share_far)

    def as_input(v):
        return v.reshape(batches, 1, here, width)

    return (
        as_input(layer_output),
        as_input(grad_input),
        small_sum[:, 592],
        out_query,
        small_sum[:, :576],
        small_sum[:rows_l, 594],
        out_expand,
        out_output,
        small_sum[:, 593],
        small_sum[:, 576:592],
        out_gate[None],
        out_up[None],
        out_down[None],
        out_sgate.T,
        out_sup.T,
        out_sdown,
    )


def solution(mesh):
    split = P(("dp", "expert"), None)
    line = P(("dp", "expert"))
    tokens = P(None, "dp", "expert", None)
    expert = P("expert", "dp", None)
    return jax.shard_map(
        per_device,
        mesh=mesh,
        in_specs=(
            tokens, tokens, P(None, "dp"), tokens, line, split, split, line, split, split, line, split,
            expert, expert, expert, P("dp", "expert"), P("dp", "expert"), P("expert", "dp"),
        ),
        out_specs=(
            tokens, tokens, line, split, split, line, split, split, line, split,
            expert, expert, expert, P("dp", "expert"), P("dp", "expert"), P("expert", "dp"),
        ),
        check_vma=False,
    )
```

```python
import functools
import jax
import jax.numpy as jnp
import numpy as np
from jax import lax
from jax.experimental import pallas as pl
from jax.experimental.pallas import tpu as pltpu
from jax.sharding import PartitionSpec as P

MESH = pl.DeviceIdType.MESH
NZ = 4
NE = 16


def place():
    me = lax.axis_index("expert")
    z = me // 4
    x = (me // 2) % 2
    c = me % 2
    return me, z, x, c, me + 1 - 2 * c, me + 2 - 4 * x


def enter(me, z, core, side, dp=1):
    barrier = pltpu.get_barrier_semaphore()
    plane = lax.axis_index("dp")
    for r in range(1, dp):
        pl.semaphore_signal(barrier, inc=1, device_id={"dp": (plane + r) % dp}, device_id_type=MESH)
    for other in (core, side):
        pl.semaphore_signal(barrier, inc=1, device_id={"expert": other}, device_id_type=MESH)

    @pl.when(z < NZ - 1)
    def _():
        pl.semaphore_signal(barrier, inc=1, device_id={"expert": me + 4}, device_id_type=MESH)

    @pl.when(z > 0)
    def _():
        pl.semaphore_signal(barrier, inc=1, device_id={"expert": me - 4}, device_id_type=MESH)

    pl.semaphore_wait(barrier, dp + 1 + (z < NZ - 1).astype(jnp.int32) + (z > 0).astype(jnp.int32))


class Spread:
    def __init__(self, dp, src, out, sems):
        self.dp, self.src, self.out = dp, src, out
        self.own, self.send, self.recv = sems
        self.plane = lax.axis_index("dp")

    @staticmethod
    def scratch(dp):
        dma = pltpu.SemaphoreType.DMA
        return [dma, dma((dp,)), dma((dp,))]

    def copy(self, r):
        return pltpu.make_async_remote_copy(
            src_ref=self.src, dst_ref=self.out.at[self.plane], send_sem=self.send.at[r], recv_sem=self.recv.at[r],
            device_id={"dp": (self.plane + r) % self.dp}, device_id_type=MESH)

    def arrival(self, r):
        p = (self.plane - r + self.dp) % self.dp
        return pltpu.make_async_remote_copy(
            src_ref=self.src, dst_ref=self.out.at[p], send_sem=self.send.at[r], recv_sem=self.recv.at[r],
            device_id={"dp": p}, device_id_type=MESH)

    def start(self):
        for r in range(1, self.dp):
            self.copy(r).start()
        self.kept = pltpu.make_async_copy(self.src, self.out.at[self.plane], self.own)
        self.kept.start()

    def finish(self):
        self.kept.wait()
        for r in range(1, self.dp):
            self.arrival(r).wait_recv()
            self.copy(r).wait_send()


class Swap:
    def __init__(self, dp, src, out, sems):
        self.dp, self.src, self.out = dp, src, out
        self.send, self.recv = sems
        self.plane = lax.axis_index("dp")

    @staticmethod
    def scratch(dp):
        dma = pltpu.SemaphoreType.DMA
        return [dma((dp,)), dma((dp,))]

    def copy(self, r):
        to = (self.plane + r) % self.dp
        return pltpu.make_async_remote_copy(
            src_ref=self.src.at[to], dst_ref=self.out.at[r - 1], send_sem=self.send.at[r], recv_sem=self.recv.at[r],
            device_id={"dp": to}, device_id_type=MESH)

    def start(self):
        for r in range(1, self.dp):
            self.copy(r).start()

    def finish(self):
        for r in range(1, self.dp):
            self.copy(r).wait_recv()
            self.copy(r).wait_send()


def side_job(dp, span, src, out, sems):
    if span is None:
        return Swap(dp, src, out, sems)
    return Spread(dp, src.at[pl.ds(span[0], span[1])], out, sems)


def side_shape(dp, span, side):
    if span is None:
        return jax.ShapeDtypeStruct((dp - 1,) + side.shape[1:], side.dtype)
    return jax.ShapeDtypeStruct((dp, span[1], side.shape[1]), side.dtype)


def side_scratch(dp, span):
    return (Swap if span is None else Spread).scratch(dp)


def enter_all(me, plane, dp):
    barrier = pltpu.get_barrier_semaphore()
    for r in range(1, NE):
        pl.semaphore_signal(
            barrier, inc=1, device_id={"expert": (me + r) % NE}, device_id_type=MESH)
    for r in range(1, dp):
        pl.semaphore_signal(
            barrier, inc=1, device_id={"dp": (plane + r) % dp}, device_id_type=MESH)
    pl.semaphore_wait(barrier, NE - 1 + dp - 1)


class Gather:
    def __init__(self, src, out, chunks, sems, view=lambda ref, b: ref.at[b]):
        self.src, self.out, self.chunks, self.view = src, out, chunks, view
        self.rows = src.shape[0] // chunks
        (self.own_sem, self.us, self.ur, self.ds, self.dr, self.bus, self.bur, self.bds, self.bdr,
         self.xs, self.xr, self.cs, self.cr) = sems
        self.me, self.z, self.x, self.c, self.core, self.side = place()

    COUNT = 13

    @staticmethod
    def scratch(chunks):
        dma = pltpu.SemaphoreType.DMA
        return [dma] + [dma((4, chunks))] * 8 + [dma((7, chunks))] * 2 + [dma((14, chunks))] * 2

    def alt(self, k):
        return k >= (self.chunks + 1) // 2

    def order(self, ks=None):
        return range(self.chunks - 1, -1, -1) if ks is None else ks

    def copy(self, block, k, src, send, recv, to):
        src_ref = self.src if src is None else self.view(self.out, src)
        dst_ref = self.view(self.out, block)
        if self.chunks > 1:
            part = pl.ds(k * self.rows, self.rows)
            src_ref, dst_ref = src_ref.at[part], dst_ref.at[part]
        return pltpu.make_async_remote_copy(
            src_ref=src_ref,
            dst_ref=dst_ref,
            send_sem=send, recv_sem=recv,
            device_id={"expert": to}, device_id_type=MESH,
        )

    def up(self, k, s, src=None):
        return self.copy(self.me - 4 * s, k, src, self.us.at[s, k], self.ur.at[s, k], self.me + 4)

    def down(self, k, s, src=None):
        return self.copy(self.me + 4 * s, k, src, self.ds.at[s, k], self.dr.at[s, k], self.me - 4)

    def up_b(self, k, s):
        b = self.side - 4 * s
        return self.copy(b, k, b, self.bus.at[s, k], self.bur.at[s, k], self.me + 4)

    def down_b(self, k, s):
        b = self.side + 4 * s
        return self.copy(b, k, b, self.bds.at[s, k], self.bdr.at[s, k], self.me - 4)

    def across(self, k, slot, block, src=None):
        return self.copy(block, k, src, self.xs.at[slot, k], self.xr.at[slot, k], self.side)

    def over(self, k, slot, block, src=None):
        return self.copy(block, k, src, self.cs.at[slot, k], self.cr.at[slot, k], self.core)

    def arrived(self, b, k, sems, s):
        return self.copy(b, k, b, sems[0].at[s - 1, k], sems[1].at[s - 1, k], self.side)

    def shift(self, base, slot):
        return base - 4 * slot if slot <= 3 else base + 4 * (slot - 3)

    def core_block(self, slot):
        if slot < 7:
            return self.shift(self.core, slot)
        return self.shift(self.core + 2 - 4 * self.x, slot - 7)

    def has(self, slot):
        slot = slot % 7
        if slot == 0:
            return self.z >= 0
        return self.z >= slot if slot <= 3 else self.z + (slot - 3) <= NZ - 1

    def crosses(self, k, slot):
        if slot == 0 or not self.alt(k):
            return self.has(slot)
        return self.z > slot if slot <= 3 else self.z + (slot - 3) < NZ - 1

    def kept(self):
        return pltpu.make_async_copy(self.src, self.view(self.out, self.me), self.own_sem)

    def start(self, ks=None):
        z, me = self.z, self.me
        if ks is None or 0 in ks:
            self.kept().start()
        for k in self.order(ks):
            self.across(k, 0, me).start()

            @pl.when(z < NZ - 1)
            def _():
                self.up(k, 0).start()

            @pl.when(z > 0)
            def _():
                self.down(k, 0).start()

            self.over(k, 0, me).start()

    def line(self, k, s):
        z, me = self.z, self.me

        @pl.when(z >= s)
        def _():
            b = me - 4 * s
            self.arrived(b, k, (self.us, self.ur), s).wait_recv()

            @pl.when(self.crosses(k, s))
            def _():
                self.across(k, s, b, b).start()

            @pl.when(z < NZ - 1)
            def _():
                self.up(k, s, b).start()

            self.over(k, s, b, b).start()

        @pl.when(z + s <= NZ - 1)
        def _():
            b = me + 4 * s
            self.arrived(b, k, (self.ds, self.dr), s).wait_recv()

            @pl.when(self.crosses(k, 3 + s))
            def _():
                self.across(k, 3 + s, b, b).start()

            @pl.when(z > 0)
            def _():
                self.down(k, s, b).start()

            self.over(k, 3 + s, b, b).start()

    def line_b(self, k, s):
        z = self.z

        @pl.when(z == s)
        def _():
            b = self.side - 4 * s
            self.arrived(b, k, (self.bus, self.bur), s).wait_recv()

            @pl.when(z < NZ - 1)
            def _():
                self.up_b(k, s).start()

            self.over(k, 7 + s, b, b).start()

        @pl.when(z + s == NZ - 1)
        def _():
            b = self.side + 4 * s
            self.arrived(b, k, (self.bds, self.bdr), s).wait_recv()

            @pl.when(z > 0)
            def _():
                self.down_b(k, s).start()

            self.over(k, 10 + s, b, b).start()

    def from_side(self, k, slot):
        @pl.when(self.crosses(k, slot))
        def _():
            b = self.shift(self.side, slot)
            self.across(k, slot, b, b).wait_recv()
            if slot == 0 and self.alt(k):
                @pl.when(self.z == 0)
                def _():
                    self.up_b(k, 0).start()

                @pl.when(self.z == NZ - 1)
                def _():
                    self.down_b(k, 0).start()

            self.over(k, 7 + slot, b, b).start()

    def round(self, s, ks=None):
        if s < NZ:
            for k in self.order(ks):
                self.line(k, s)
        for k in self.order(ks):
            for slot in ((0,) if s == 1 else (s - 1, s + 2)):
                self.from_side(k, slot)
        if s > 1:
            for k in self.order(ks):
                if self.alt(k):
                    self.line_b(k, s - 1)

    def landed(self, ks=None):
        for k in self.order(ks):
            for slot in range(14):
                @pl.when(self.has(slot))
                def _():
                    b = self.core_block(slot)
                    self.over(k, slot, b, b).wait_recv()

    def finish(self, landed=True):
        z = self.z
        if landed:
            self.kept().wait()
            self.landed()
        for k in self.order():
            for slot in range(14):
                @pl.when(self.has(slot))
                def _():
                    b = self.core_block(slot)
                    self.over(k, slot, b, b).wait_send()
            for slot in range(7):
                @pl.when(self.crosses(k, slot))
                def _():
                    self.across(k, slot, self.me).wait_send()
            for s in range(NZ - 1):
                @pl.when((z >= s) & (z < NZ - 1))
                def _():
                    self.up(k, s).wait_send()

                @pl.when((z + s <= NZ - 1) & (z > 0))
                def _():
                    self.down(k, s).wait_send()

                if self.alt(k):
                    @pl.when(z == s)
                    def _():
                        self.up_b(k, s).wait_send()

                    @pl.when(z + s == NZ - 1)
                    def _():
                        self.down_b(k, s).wait_send()


def gather_kernel(chunks, dp, span, extra, x_ref, *refs):
    job = None
    ng = Gather.COUNT
    if not extra:
        o_ref, *sems = refs
    else:
        src, o_ref, out, *sems = refs
        job = side_job(dp, span, src, out, sems[ng:])
    g = Gather(x_ref, o_ref, chunks, sems[:ng])
    enter(g.me, g.z, g.core, g.side, 1 if job is None else dp)
    if job is not None:
        job.start()
    g.start()
    for s in range(1, NZ + 1):
        g.round(s)
    g.finish()
    if job is not None:
        job.finish()


COST = pl.CostEstimate(flops=0, bytes_accessed=4_000_000, transcendentals=0)
ANY = pl.BlockSpec(memory_space=pl.ANY)


def gather16(v, cid, chunks=2, dp=1, span=None, side=None):
    rows, width = v.shape
    extra = side is not None
    out = pl.pallas_call(
        functools.partial(gather_kernel, chunks, dp, span, extra),
        out_shape=(jax.ShapeDtypeStruct((NE, rows, width), v.dtype),)
        + ((side_shape(dp, span, side),) if extra else ()),
        in_specs=[ANY] * (2 if extra else 1),
        out_specs=(ANY,) * (2 if extra else 1),
        scratch_shapes=Gather.scratch(chunks) + (side_scratch(dp, span) if extra else []),
        compiler_params=pltpu.CompilerParams(collective_id=cid, has_side_effects=True),
        cost_estimate=COST,
        name="gather16",
    )(*((v, side) if extra else (v,)))
    return out if extra else out[0]


def opening_kernel(dp, chunks, x_ref, small_ref, parts_ref, out_ref,
                   x_all, small_all, parts_head, out_head, small_dp, out_dp, *sems):
    ng = Gather.COUNT
    gx = Gather(x_ref, x_all, chunks, sems[:ng])
    gs = Gather(small_dp, small_all, 1, sems[ng:2 * ng], lambda ref, b: ref.at[:, b])
    loc, ys, yr, ps, pr, os_, or_, pl_sem, ol_sem = sems[2 * ng:]
    me = gx.me
    plane = lax.axis_index("dp")
    enter_all(me, plane, dp)
    pairs = ((small_ref, small_dp), (out_ref, out_dp), (parts_head.at[plane], parts_head))

    def lift(i, r):
        src, dst = pairs[i]
        return pltpu.make_async_remote_copy(
            src_ref=src, dst_ref=dst.at[plane], send_sem=ys.at[i, r], recv_sem=yr.at[i, r],
            device_id={"dp": (plane + r) % dp}, device_id_type=MESH)

    def landed(i, r):
        p = (plane - r + dp) % dp
        dst = pairs[i][1].at[p]
        return pltpu.make_async_remote_copy(
            src_ref=dst, dst_ref=dst, send_sem=ys.at[i, r], recv_sem=yr.at[i, r],
            device_id={"dp": p}, device_id_type=MESH)

    def kept(i):
        src, dst = pairs[i]
        return pltpu.make_async_copy(src, dst.at[plane], loc.at[i])

    def part(r):
        h = (me + r) % NE
        return pltpu.make_async_remote_copy(
            src_ref=parts_ref.at[h], dst_ref=parts_head.at[plane, me],
            send_sem=ps.at[r], recv_sem=pr.at[r],
            device_id={"expert": h}, device_id_type=MESH)

    def part_in(r):
        e = (me - r + NE) % NE
        return pltpu.make_async_remote_copy(
            src_ref=parts_head.at[plane, e], dst_ref=parts_head.at[plane, e],
            send_sem=ps.at[r], recv_sem=pr.at[r],
            device_id={"expert": e}, device_id_type=MESH)

    def part_kept():
        return pltpu.make_async_copy(parts_ref.at[me], parts_head.at[plane, me], pl_sem)

    for i in range(2):
        for r in range(1, dp):
            lift(i, r).start()
        kept(i).start()
    for r in range(1, NE):
        part(r).start()
    part_kept().start()
    gx.start()
    gx.round(1)

    kept(0).wait()
    for r in range(1, dp):
        landed(0, r).wait_recv()
    gs.start()

    for r in range(1, NE):
        part_in(r).wait_recv()
    part_kept().wait()
    for r in range(1, dp):
        lift(2, r).start()
    gx.round(2)

    def row(d):
        b = NE * d + me
        return pltpu.make_async_remote_copy(
            src_ref=out_dp.at[d], dst_ref=out_head.at[b % dp],
            send_sem=os_.at[d], recv_sem=or_.at[b % dp],
            device_id={"expert": b // dp}, device_id_type=MESH)

    def row_kept(d):
        b = NE * d + me
        return pltpu.make_async_copy(out_dp.at[d], out_head.at[b % dp], ol_sem.at[d])

    kept(1).wait()
    for r in range(1, dp):
        landed(1, r).wait_recv()
    for d in range(dp):
        home = (NE * d + me) // dp

        @pl.when(home != me)
        def _():
            row(d).start()

        @pl.when(home == me)
        def _():
            row_kept(d).start()

    gs.round(1)
    gx.round(3)
    gs.round(2)
    gx.round(4)
    gs.round(3)
    gs.round(4)

    def row_in(j):
        return pltpu.make_async_remote_copy(
            src_ref=out_head.at[j], dst_ref=out_head.at[j], send_sem=os_.at[j], recv_sem=or_.at[j],
            device_id={"expert": gx.core}, device_id_type=MESH)

    for r in range(1, NE):
        part(r).wait_send()
    for j in range(dp):
        @pl.when((dp * me + j) % NE != me)
        def _():
            row_in(j).wait_recv()
    for d in range(dp):
        home = (NE * d + me) // dp

        @pl.when(home != me)
        def _():
            row(d).wait_send()

        @pl.when(home == me)
        def _():
            row_kept(d).wait()
    for r in range(1, dp):
        landed(2, r).wait_recv()
    for i in range(3):
        for r in range(1, dp):
            lift(i, r).wait_send()
    gx.finish()
    gs.finish()


def opening(dp, x, small, parts, out, cid, chunks=2):
    dma = pltpu.SemaphoreType.DMA
    rows, ws = small.shape
    bf = x.dtype
    wo = out.shape[1]
    shape = jax.ShapeDtypeStruct
    res = pl.pallas_call(
        functools.partial(opening_kernel, dp, chunks),
        out_shape=(
            shape((NE,) + x.shape, bf), shape((dp, NE, rows, ws), bf), shape((dp, NE) + parts.shape[1:], bf),
            shape((dp, rows, wo), bf),
            shape((dp, rows, ws), bf), shape((dp, rows, wo), bf),
        ),
        in_specs=[ANY] * 4,
        out_specs=[ANY] * 6,
        scratch_shapes=Gather.scratch(chunks) + Gather.scratch(1) + [
            dma((2,)), dma((3, dp)), dma((3, dp)), dma((NE,)), dma((NE,)), dma((dp,)), dma((dp,)), dma, dma((dp,))],
        compiler_params=pltpu.CompilerParams(collective_id=cid, has_side_effects=True),
        cost_estimate=COST,
        name="opening",
    )(x, small, parts, out)
    return res[:4]


def order(z, i):
    a, b = (3, 2, 1, 0)[i], (3, 2, 0, 1)[i]
    return jnp.where(z == 0, a, jnp.where(z == 1, b, jnp.where(z == 2, 3 - b, 3 - a)))


class Scatter:
    COUNT = 14

    def __init__(self, p_ref, o_ref, chunks, scratch):
        self.p, self.o, self.chunks = p_ref, o_ref, chunks
        (self.cbuf, self.own, self.xbuf, self.ubuf, self.dbuf, self.ld, self.cs, self.cr, self.xs, self.xr,
         self.us, self.ur, self.ds, self.dr) = scratch
        self.rows = o_ref.shape[0] // chunks
        self.me, self.z, self.x, self.c, self.core, self.side = place()

    @staticmethod
    def scratch(rows, width, chunks, bf):
        dma = pltpu.SemaphoreType.DMA
        return [pltpu.VMEM((n, rows, width), bf) for n in (8, 8, 4, 4, 4)] + [
            dma((8, chunks)), dma((8, chunks)), dma((8, chunks))] + [dma((4, chunks))] * 6

    def rng(self, k):
        return pl.ds(k * self.rows, self.rows)

    def column(self, i, j):
        return 4 * order(self.z, i) + 2 * jnp.where(j == 0, 1 - self.x, self.x)

    def remote(self, src, dst, send, recv, to):
        return pltpu.make_async_remote_copy(
            src_ref=src, dst_ref=dst, send_sem=send, recv_sem=recv,
            device_id={"expert": to}, device_id_type=MESH)

    def over(self, i, j, k):
        n = 2 * i + j
        return self.remote(
            self.p.at[self.column(i, j) + 1 - self.c, self.rng(k)], self.cbuf.at[n, self.rng(k)],
            self.cs.at[n, k], self.cr.at[n, k], self.core)

    def load(self, i, j, k):
        n = 2 * i + j
        return pltpu.make_async_copy(
            self.p.at[self.column(i, j) + self.c, self.rng(k)], self.own.at[n, self.rng(k)], self.ld.at[n, k])

    def which(self, ks):
        return range(self.chunks) if ks is None else ks

    def across(self, i, k):
        return self.remote(self.own.at[2 * i, self.rng(k)], self.xbuf.at[i, self.rng(k)],
                           self.xs.at[i, k], self.xr.at[i, k], self.side)

    def up(self, t, i, k):
        return self.remote(self.own.at[2 * i + 1, self.rng(k)], self.ubuf.at[t, self.rng(k)],
                           self.us.at[t, k], self.ur.at[t, k], self.me + 4)

    def down(self, t, i, k):
        return self.remote(self.own.at[2 * i + 1, self.rng(k)], self.dbuf.at[t, self.rng(k)],
                           self.ds.at[t, k], self.dr.at[t, k], self.me - 4)

    def start(self, ks=None):
        for i in range(NZ):
            for j in range(2):
                for k in self.which(ks):
                    self.load(i, j, k).start()
                    self.over(i, j, k).start()

    def first(self, i, ks=None):
        f32 = jnp.float32
        for k in self.which(ks):
            self.load(i, 0, k).wait()
            self.over(i, 0, k).wait_recv()
            s = self.rng(k)
            self.own[2 * i, s] = (
                self.own[2 * i, s].astype(f32) + self.cbuf[2 * i, s].astype(f32)).astype(self.own.dtype)
            self.across(i, k).start()

    def second(self, i, ks=None):
        f32 = jnp.float32
        z, own, o = self.z, self.own, self.o
        t = order(z, i)
        for k in self.which(ks):
            self.load(i, 1, k).wait()
            s = self.rng(k)
            self.over(i, 1, k).wait_recv()
            self.across(i, k).wait_recv()

            def base():
                return (own[2 * i + 1, s].astype(f32) + self.cbuf[2 * i + 1, s].astype(f32)
                        + self.xbuf[i, s].astype(f32))

            if i < NZ - 1:
                @pl.when(t > z)
                def _():
                    @pl.when(z > 0)
                    def _():
                        self.up(t, i, k).wait_recv()
                        own[2 * i + 1, s] = (base() + self.ubuf[t, s].astype(f32)).astype(own.dtype)

                    @pl.when(z == 0)
                    def _():
                        own[2 * i + 1, s] = base().astype(own.dtype)

                    self.up(t, i, k).start()

                @pl.when(t < z)
                def _():
                    @pl.when(z < NZ - 1)
                    def _():
                        self.down(t, i, k).wait_recv()
                        own[2 * i + 1, s] = (base() + self.dbuf[t, s].astype(f32)).astype(own.dtype)

                    @pl.when(z == NZ - 1)
                    def _():
                        own[2 * i + 1, s] = base().astype(own.dtype)

                    self.down(t, i, k).start()
            else:
                @pl.when(z > 0)
                def _():
                    self.up(t, i, k).wait_recv()

                @pl.when(z < NZ - 1)
                def _():
                    self.down(t, i, k).wait_recv()

                @pl.when((z > 0) & (z < NZ - 1))
                def _():
                    o[s] = (base() + self.ubuf[t, s].astype(f32) + self.dbuf[t, s].astype(f32)).astype(o.dtype)

                @pl.when(z == 0)
                def _():
                    o[s] = (base() + self.dbuf[t, s].astype(f32)).astype(o.dtype)

                @pl.when(z == NZ - 1)
                def _():
                    o[s] = (base() + self.ubuf[t, s].astype(f32)).astype(o.dtype)

    def run(self, between=lambda: None):
        self.first(0)
        for i in range(NZ):
            if i + 1 < NZ:
                self.first(i + 1)
            between()
            self.second(i)
            between()

    def finish(self):
        z = self.z
        for k in range(self.chunks):
            for i in range(NZ):
                self.across(i, k).wait_send()
                for j in range(2):
                    self.over(i, j, k).wait_send()
                if i < NZ - 1:
                    t = order(z, i)

                    @pl.when(t > z)
                    def _():
                        self.up(t, i, k).wait_send()

                    @pl.when(t < z)
                    def _():
                        self.down(t, i, k).wait_send()


def scatter_kernel(chunks, dp, span, extra, p_ref, *refs):
    job = None
    ns = Scatter.COUNT
    if not extra:
        o_ref, *scratch = refs
    else:
        src, o_ref, out, *scratch = refs
        job = side_job(dp, span, src, out, scratch[ns:])
    s = Scatter(p_ref, o_ref, chunks, scratch[:ns])
    enter(s.me, s.z, s.core, s.side, 1 if job is None else dp)
    if job is not None:
        job.start()
    s.start()
    s.run()
    s.finish()
    if job is not None:
        job.finish()


VMEM = pl.BlockSpec(memory_space=pltpu.VMEM)


def scatter16(p, cid, chunks=2, dp=1, span=None, side=None):
    _, rows, width = p.shape
    extra = side is not None
    out = pl.pallas_call(
        functools.partial(scatter_kernel, chunks, dp, span, extra),
        out_shape=(jax.ShapeDtypeStruct((rows, width), jnp.float32),)
        + ((side_shape(dp, span, side),) if extra else ()),
        in_specs=[ANY] * (2 if extra else 1),
        out_specs=(VMEM,) + ((ANY,) if extra else ()),
        scratch_shapes=Scatter.scratch(rows, width, chunks, p.dtype) + (side_scratch(dp, span) if extra else []),
        compiler_params=pltpu.CompilerParams(
            collective_id=cid, has_side_effects=True, vmem_limit_bytes=60 * 1024 * 1024),
        cost_estimate=COST,
        name="scatter16",
    )(*((p, side) if extra else (p,)))
    return out if extra else out[0]


def return_kernel(dp, chunks, p_ref, parts_ref, rows_ref, o_ref, parts_far, rows_far, *scratch):
    ns = Scatter.COUNT
    s = Scatter(p_ref, o_ref, chunks, scratch[:ns])
    swap = Swap(dp, parts_ref, parts_far, scratch[ns:ns + 2])
    rs, rr = scratch[ns + 2:]
    plane = lax.axis_index("dp")
    keeper = s.me * dp // NE
    enter(s.me, s.z, s.core, s.side, dp)

    def row(r):
        return pltpu.make_async_remote_copy(
            src_ref=rows_ref, dst_ref=rows_far.at[r - 1], send_sem=rs.at[r], recv_sem=rr.at[r],
            device_id={"dp": (plane + r) % dp}, device_id_type=MESH)

    swap.start()
    for r in range(1, dp):
        @pl.when((plane + r) % dp == keeper)
        def _():
            row(r).start()
    s.start()
    s.run()
    s.finish()
    swap.finish()
    for r in range(1, dp):
        @pl.when((plane + r) % dp == keeper)
        def _():
            row(r).wait_send()

        @pl.when(plane == keeper)
        def _():
            row(r).wait_recv()


def returning(dp, p, parts, rows, cid, chunks=2):
    dma = pltpu.SemaphoreType.DMA
    _, n, width = p.shape
    shape = jax.ShapeDtypeStruct
    return pl.pallas_call(
        functools.partial(return_kernel, dp, chunks),
        out_shape=(
            shape((n, width), jnp.float32), shape((dp - 1,) + parts.shape[1:], parts.dtype),
            shape((dp - 1,) + rows.shape, rows.dtype)),
        in_specs=[ANY] * 3,
        out_specs=[VMEM, ANY, ANY],
        scratch_shapes=Scatter.scratch(n, width, chunks, p.dtype) + [dma((dp,))] * 4,
        compiler_params=pltpu.CompilerParams(
            collective_id=cid, has_side_effects=True, vmem_limit_bytes=60 * 1024 * 1024),
        cost_estimate=COST,
        name="returning",
    )(p, parts, rows)


def closing_kernel(dp, p_ref, parts_ref, rows_ref, o_ref, far_ref, query_ref, expand_ref, output_ref,
                   parts_in, row_in, *scratch):
    ns = Scatter.COUNT
    s = Scatter(p_ref, o_ref, 1, scratch[:ns])
    ys, yr, ps, pr, kept_sem, rs, rr = scratch[ns:]
    me = s.me
    plane = lax.axis_index("dp")
    rows = o_ref.shape[0] // dp
    enter_all(me, plane, dp)

    def lift(r):
        to = (plane + r) % dp
        return pltpu.make_async_remote_copy(
            src_ref=o_ref.at[pl.ds(pl.multiple_of(to * rows, 16), rows)], dst_ref=far_ref.at[r - 1],
            send_sem=ys.at[r], recv_sem=yr.at[r],
            device_id={"dp": to}, device_id_type=MESH)

    def part(r):
        e = (me + r) % NE
        return pltpu.make_async_remote_copy(
            src_ref=parts_ref.at[e], dst_ref=parts_in.at[me], send_sem=ps.at[r], recv_sem=pr.at[r],
            device_id={"expert": e}, device_id_type=MESH)

    def part_in(r):
        h = (me - r + NE) % NE
        return pltpu.make_async_remote_copy(
            src_ref=parts_in.at[h], dst_ref=parts_in.at[h], send_sem=ps.at[r], recv_sem=pr.at[r],
            device_id={"expert": h}, device_id_type=MESH)

    def part_kept():
        return pltpu.make_async_copy(parts_ref.at[me], parts_in.at[me], kept_sem.at[0])

    keeper = plane == me * dp // NE
    source = (NE * plane + me) // dp

    def row(j):
        return pltpu.make_async_remote_copy(
            src_ref=rows_ref.at[j], dst_ref=row_in, send_sem=rs.at[j], recv_sem=rr,
            device_id={"expert": (dp * me + j) % NE}, device_id_type=MESH)

    def row_kept(j):
        return pltpu.make_async_copy(rows_ref.at[j], row_in, kept_sem.at[1])

    s.start()
    for i in range(NZ):
        s.first(i)
    for r in range(1, NE):
        part(r).start()
    part_kept().start()
    for j in range(dp):
        home = (dp * me + j) % NE

        @pl.when(keeper & (home != me))
        def _():
            row(j).start()

        @pl.when(keeper & (home == me))
        def _():
            row_kept(j).start()
    for i in range(NZ):
        s.second(i)
    for r in range(1, dp):
        lift(r).start()
    for r in range(1, NE):
        part_in(r).wait_recv()
    part_kept().wait()
    rows_l = expand_ref.shape[0]
    f32 = jnp.float32
    for h in range(0, NE, 2):
        pair = [parts_in[h + i].astype(f32) for i in range(2)]
        query_ref[:, h * 192:(h + 2) * 192] = jnp.concatenate([v[:, :192] for v in pair], axis=1)
        for i, v in enumerate(pair):
            expand_ref[:, (h + i) * 256:(h + i + 1) * 256] = jnp.concatenate(
                [v[c * rows_l:(c + 1) * rows_l, 192:] for c in range(4)], axis=1)

    @pl.when(source != me)
    def _():
        row(0).wait_recv()

    for j in range(dp):
        home = (dp * me + j) % NE

        @pl.when(keeper & (home != me))
        def _():
            row(j).wait_send()

        @pl.when(keeper & (home == me))
        def _():
            row_kept(j).wait()
    output_ref[...] = row_in[...].astype(f32)
    for r in range(1, NE):
        part(r).wait_send()
    s.finish()
    for r in range(1, dp):
        lift(r).wait_recv()
        lift(r).wait_send()


def closing(dp, p, parts, rows, rows_l, cid):
    dma = pltpu.SemaphoreType.DMA
    _, n, width = p.shape
    shape = jax.ShapeDtypeStruct
    rows_w = parts.shape[1]
    near, far, query, expand, output = pl.pallas_call(
        functools.partial(closing_kernel, dp),
        out_shape=(
            shape((n, width), p.dtype), shape((dp - 1, n // dp, width), p.dtype),
            shape((rows_w, NE * 192), jnp.float32), shape((rows_l, NE * 256), jnp.float32),
            shape(rows.shape[1:], jnp.float32)),
        in_specs=[ANY] * 3,
        out_specs=[VMEM] * 5,
        scratch_shapes=[pltpu.VMEM(parts.shape, parts.dtype), pltpu.VMEM(rows.shape[1:], rows.dtype)]
        + Scatter.scratch(n, width, 1, p.dtype)
        + [dma((dp,)), dma((dp,)), dma((NE,)), dma((NE,)), dma((2,)), dma((dp,)), dma],
        compiler_params=pltpu.CompilerParams(
            collective_id=cid, has_side_effects=True, vmem_limit_bytes=60 * 1024 * 1024),
        cost_estimate=COST,
        name="closing",
    )(p, parts, rows)
    own = lax.dynamic_slice_in_dim(near, lax.axis_index("dp") * (n // dp), n // dp).astype(jnp.float32)
    return own + jnp.sum(far.astype(jnp.float32), axis=0), query, expand, output
BF = jnp.bfloat16
F32 = jnp.float32


def mm(a, b):
    return jnp.dot(a, b, preferred_element_type=F32)


def mm_t(a, b):
    return lax.dot_general(a, b, (((1,), (1,)), ((), ())), preferred_element_type=F32)


def silu_pair(gate_in):
    sigmoid = 1.0 / (1.0 + jnp.exp(-gate_in))
    return (gate_in * sigmoid, sigmoid * (1.0 + gate_in * (1.0 - sigmoid)))


TILE = 256
WIDE = 512
SHARE = 176


def down_copies(parts, out, sem, which):
    dp = parts[0].shape[0]
    sizes = [part.shape[1] for part in parts]
    rows, first = sum(sizes), sum(sizes[:which])
    return [
        pltpu.make_async_copy(
            parts[which].at[d], out.at[pl.ds(d * rows + first, sizes[which])], sem.at[len(parts) * d + which])
        for d in range(dp)
    ]


def share_copies(share_ref, fan, down, sem):
    dp, rows, w = share_ref.shape
    n = rows // 3
    copies = []
    for d in range(dp):
        cols = pl.ds(d * w, w)
        for i, (dst, first) in enumerate(((fan, 0), (fan, TILE), (down, 0))):
            copies.append(pltpu.make_async_copy(
                share_ref.at[d, pl.ds(i * n, n)], dst.at[pl.ds(first, n), cols], sem.at[3 * d + i]))
    return copies


def share_blank(fan, down):
    pad = jnp.zeros((TILE - SHARE, fan.shape[1]), BF)
    fan[SHARE:TILE] = pad
    fan[TILE + SHARE:] = pad
    down[SHARE:] = pad


def valid_of(len_ref, first_device, tokens, batches, here):
    n = lax.broadcasted_iota(jnp.int32, (tokens, 1), 0)
    if here & (here - 1) or batches & (batches - 1):
        device, batch, place_in = n // (batches * here), (n // here) % batches, n % here
    else:
        bits, more = here.bit_length() - 1, (batches * here).bit_length() - 1
        device, batch, place_in = n >> more, (n >> bits) & (batches - 1), n & (here - 1)
    position = (first_device + device) * here + place_in
    length = jnp.zeros((tokens, 1), jnp.int32)
    for b in range(batches):
        length = jnp.where(batch == b, len_ref[b], length)
    return (position < length).astype(F32)


def slot_tables(here, slots=128):
    n = np.arange(256)
    same = n[:, None] // here == n[None, :] // here
    before = same & (n[None, :] < n[:, None])
    tables = np.stack([before, before.T, np.eye(256, dtype=bool)]).astype(np.float32)
    base = np.broadcast_to((n // here * 32)[:, None], (256, slots)).astype(np.float32)
    return jnp.asarray(tables, BF), jnp.asarray(base), jnp.asarray(base.T)


def one_hots(taken, tables, base_c, base_r, groups, slots):
    lane = lax.broadcasted_iota(jnp.int32, (256, slots), 1).astype(F32)
    row = lax.broadcasted_iota(jnp.int32, (slots, 256), 0).astype(F32)
    to_slot, to_token = [], []
    for g in range(groups):
        t = jnp.broadcast_to(taken[g * 256:(g + 1) * 256], (256, slots))
        low = t.astype(BF)
        place_c = mm(tables[0], low) + base_c[...]
        place_r = mm_lead(low, tables[1]) + base_r[...]
        taken_r = mm_lead(low, tables[2])
        to_token.append(jnp.where((place_c == lane) & (t > 0.5), 1.0, 0.0).astype(BF))
        to_slot.append(jnp.where((place_r == row) & (taken_r > 0.5), 1.0, 0.0).astype(BF))
    return to_slot, to_token


def mm_lead(a, b):
    return lax.dot_general(a, b, (((0,), (0,)), ((), ())), preferred_element_type=F32)


def lanes(j):
    return pl.ds(pl.multiple_of(j * WIDE, WIDE), WIDE)


def over_columns(total, body):
    def step(j, _):
        body(pl.multiple_of(j * WIDE, WIDE), WIDE)
        return 0

    lax.fori_loop(0, total // WIDE, step, 0)
    if total % WIDE:
        body(total // WIDE * WIDE, total % WIDE)


def forward_kernel(chunks, dp, span, batches, here, len_ref, pick_ref, mix_ref, mask_ref, tab_ref, basec_ref, baser_ref, wg_ref, wu_ref, router_ref,
                   share_ref, wda_ref, wdb_ref, down_ref, dy_ref,
                   out_ref, rows_ref, hid_ref, act_ref, slo_ref, eo_ref, sh_ref, sact_ref, sslo_ref, gate_ref,
                   slot_ref, token_ref, dy_all, wdc_ref,
                   wd_ref, fan_ref, sd_ref, hid_buf, sh_buf, gate_buf, token_buf, wd_sem, sh_sem, *sems):
    step = pl.program_id(0)
    tokens, width = mix_ref.shape
    groups, slots = tokens // 256, 128
    half = groups * slots
    ff = hid_ref.shape[1]
    phase = pl.num_programs(0) // 2
    g = Gather(dy_ref, dy_all, chunks, sems[:Gather.COUNT])
    job = side_job(dp, span, down_ref, wdc_ref, sems[Gather.COUNT:])
    parts = (wda_ref, wdb_ref, wdc_ref)

    @pl.when(step == 0)
    def _():
        enter(g.me, g.z, g.core, g.side, dp)
        job.start()
        g.start()
        copies = share_copies(share_ref, fan_ref, sd_ref, sh_sem)
        for copy in copies + down_copies(parts, wd_ref, wd_sem, 0) + down_copies(parts, wd_ref, wd_sem, 1):
            copy.start()
        share_blank(fan_ref, sd_ref)
        fan_ref[SHARE:SHARE + 16] = router_ref[...]
        for copy in copies:
            copy.wait()

    @pl.when(step < phase)
    def _():
        mix = mix_ref[...]
        fanned = mm_t(mix, fan_ref[:TILE, :])
        s_up = mm_t(mix, fan_ref[TILE:, :])
        s_act, s_slope = silu_pair(fanned)
        s_hidden = (s_act * s_up).astype(BF)
        at = pl.ds(pl.multiple_of(step * tokens, tokens), tokens)
        sh_ref[...] = s_hidden
        sh_buf[at] = s_hidden
        sact_ref[...] = s_act.astype(BF)
        sslo_ref[...] = (s_up * s_slope).astype(BF)
        logits = fanned[:, SHARE:SHARE + 16]
        mask = mask_ref[...].astype(F32)
        taken = jnp.sum(mask * pick_ref[:, :16], axis=1, keepdims=True) * valid_of(len_ref, step * (tokens // (batches * here)), tokens, batches, here)
        held = jnp.where(mask > 0.5, logits, -1e30)
        raised = jnp.exp(held - jnp.max(held, axis=1, keepdims=True)) * mask
        gate = jnp.sum(raised * pick_ref[:, :16], axis=1, keepdims=True) / jnp.sum(raised, axis=1, keepdims=True) * taken
        gate_ref[...] = gate
        gate_buf[at] = gate
        to_slot, to_token = one_hots(taken, tab_ref, basec_ref, baser_ref, groups, slots)
        for n in range(groups):
            slot_ref[n * slots:(n + 1) * slots] = to_slot[n]
            token_ref[n * 256:(n + 1) * 256] = to_token[n]
            token_buf[pl.ds(pl.multiple_of(step * tokens + n * 256, 256), 256)] = to_token[n]

        def dispatch(j, _):
            for n in range(groups):
                rows_ref[n * slots:(n + 1) * slots, lanes(j)] = mm(
                    to_slot[n], mix_ref[n * 256:(n + 1) * 256, lanes(j)]).astype(BF)
            return 0

        lax.fori_loop(0, width // WIDE, dispatch, 0)
        rows_at = pl.ds(pl.multiple_of(step * half, half), half)

        def fan_in(start, size):
            cols = pl.ds(start, size)
            gate_in = mm(rows_ref[...], wg_ref[:, cols])
            up_in = mm(rows_ref[...], wu_ref[:, cols])
            act, slope = silu_pair(gate_in)
            hidden = (act * up_in).astype(BF)
            hid_ref[:, cols] = hidden
            hid_buf[rows_at, cols] = hidden
            act_ref[:, cols] = act.astype(BF)
            slo_ref[:, cols] = (up_in * slope).astype(BF)

        over_columns(ff, fan_in)

    @pl.when(step == phase)
    def _():
        job.finish()
        for copy in down_copies(parts, wd_ref, wd_sem, 2):
            copy.start()
        for which in range(3):
            for copy in down_copies(parts, wd_ref, wd_sem, which):
                copy.wait()

    @pl.when(step >= phase)
    def _():
        tile = step - phase
        at = pl.ds(pl.multiple_of(tile * tokens, tokens), tokens)
        rows_at = pl.ds(pl.multiple_of(tile * half, half), half)
        gate = gate_buf[at]
        s_hidden = sh_buf[at]
        to_token = [token_buf[pl.ds(pl.multiple_of(tile * tokens + n * 256, 256), 256)] for n in range(groups)]

        def fan_out(j, _):
            eo = mm(hid_buf[rows_at], wd_ref[:, lanes(j)]).astype(BF)
            eo_ref[:, lanes(j)] = eo
            shared = mm(s_hidden, sd_ref[:, lanes(j)])
            picked = jnp.concatenate(
                [mm(to_token[n], eo[n * slots:(n + 1) * slots]) for n in range(groups)], axis=0)
            out_ref[:, lanes(j)] = (shared + gate * picked).astype(BF)
            return 0

        lax.fori_loop(0, width // WIDE, fan_out, 0)

    for r, s in ((1, 1), (2, 3), (3, 5), (4, 7)):
        @pl.when(step == s)
        def _():
            g.round(r)

    @pl.when(step == 2 * phase - 1)
    def _():
        g.finish()


def backward_kernel(chunks, pick_ref, dy_ref, wg_ref, wu_ref, share_ref, wda_ref, wdb_ref, wdc_ref,
                    act_ref, slo_ref, eo_ref, sact_ref, sslo_ref, gate_ref, slot_ref, token_ref, part_ref,
                    dh_ref, deo_ref, dg_ref, du_ref, ds_ref, sum_ref,
                    wd_ref, fan_ref, sd_ref, wd_sem, sh_sem, *scratch):
    step = pl.program_id(0)
    tokens, width = dy_ref.shape
    groups, slots = tokens // 256, 128
    ff = dg_ref.shape[1]
    sc = Scatter(part_ref, sum_ref, chunks, scratch)

    @pl.when(step == 0)
    def _():
        enter(sc.me, sc.z, sc.core, sc.side)
        copies = share_copies(share_ref, fan_ref, sd_ref, sh_sem)
        for which in range(3):
            copies += down_copies((wda_ref, wdb_ref, wdc_ref), wd_ref, wd_sem, which)
        for copy in copies:
            copy.start()
        sc.start()
        share_blank(fan_ref, sd_ref)
        for copy in copies:
            copy.wait()

    d_sh = mm_t(dy_ref[...], sd_ref[...])
    d_s = jnp.concatenate([(d_sh * sslo_ref[...].astype(F32)).astype(BF),
                           (d_sh * sact_ref[...].astype(F32)).astype(BF)], axis=1)
    ds_ref[...] = d_s
    gate = gate_ref[...]
    to_slot = [slot_ref[n * slots:(n + 1) * slots] for n in range(groups)]
    to_token = [token_ref[n * 256:(n + 1) * 256] for n in range(groups)]

    @pl.when(step == 0)
    def _():
        sc.first(0)
        sc.first(1)

    def dispatch(j, total):
        dy = dy_ref[:, lanes(j)].astype(F32)
        gated = (gate * dy).astype(BF)
        for n in range(groups):
            deo_ref[n * slots:(n + 1) * slots, lanes(j)] = mm(to_slot[n], gated[n * 256:(n + 1) * 256]).astype(BF)
        picked = jnp.concatenate(
            [mm(to_token[n], eo_ref[n * slots:(n + 1) * slots, lanes(j)]) for n in range(groups)], axis=0)
        return total + jnp.sum(dy * picked, axis=1, keepdims=True)

    d_gates = lax.fori_loop(0, width // WIDE, dispatch, jnp.zeros((tokens, 1), F32))

    def back_out(start, size):
        cols = pl.ds(start, size)
        d_eh = mm_t(deo_ref[...], wd_ref[cols, :])
        dg_ref[:, cols] = (d_eh * slo_ref[:, cols].astype(F32)).astype(BF)
        du_ref[:, cols] = (d_eh * act_ref[:, cols].astype(F32)).astype(BF)

    over_columns(ff, back_out)

    @pl.when(step == 0)
    def _():
        sc.first(2)
        sc.first(3)

    def back_in(j, _):
        d_rows = (mm_t(dg_ref[...], wg_ref[lanes(j), :]) + mm_t(du_ref[...], wu_ref[lanes(j), :])).astype(BF)
        shared = mm(d_s, fan_ref[:, lanes(j)])
        taken_rows = jnp.concatenate(
            [mm(to_token[n], d_rows[n * slots:(n + 1) * slots]) for n in range(groups)], axis=0)
        dh_ref[:, lanes(j)] = (shared + taken_rows).astype(BF)
        return 0

    lax.fori_loop(0, width // WIDE, back_in, 0)
    high = d_gates.astype(BF).astype(F32)
    dh_ref[:, width:] = (high * pick_ref[:, :128] + (d_gates - high) * pick_ref[:, 128:]).astype(BF)

    outer = (sc.z == 0) | (sc.z == NZ - 1)
    for i in range(NZ - 1):
        @pl.when((step == i) & outer)
        def _():
            sc.second(i)

        @pl.when((step == min(i + 1, 2)) & jnp.logical_not(outer))
        def _():
            sc.second(i)

    @pl.when(step == NZ - 1)
    def _():
        sc.second(NZ - 1)
        sc.finish()


def whole(v):
    zeros = (0,) * v.ndim
    return pl.BlockSpec(v.shape, lambda i: zeros, pipeline_mode=pl.Buffered(buffer_count=1))


def tiles(rows, w):
    return pl.BlockSpec((rows, w), lambda i: (i, 0))


SMEM = pl.BlockSpec(memory_space=pltpu.SMEM)


def mixture_forward(dp, batches, here, lengths, pick, mix, mask, wg, wu, router, share, wda, wdb, span, down, dy, cid,
                    chunks=2):
    total, width = mix.shape
    step, half = total // 4, total // 8
    ff = wg.shape[1]
    tables = slot_tables(here)
    shape = jax.ShapeDtypeStruct
    rows = total // 2
    dma = pltpu.SemaphoreType.DMA

    def early(n, w):
        return pl.BlockSpec((n, w), lambda i: (jnp.minimum(i, 3), 0))

    def late(n, w):
        return pl.BlockSpec((n, w), lambda i: (jnp.maximum(i - 4, 0), 0))

    return pl.pallas_call(
        functools.partial(forward_kernel, chunks, dp, span, batches, here),
        grid=(8,),
        out_shape=(
            shape((total, width), BF), shape((rows, width), BF), shape((rows, ff), BF), shape((rows, ff), BF),
            shape((rows, ff), BF), shape((rows, width), BF), shape((total, TILE), BF), shape((total, TILE), BF),
            shape((total, TILE), BF), shape((total, 1), F32), shape((rows, 256), BF), shape((total, 128), BF),
            shape((NE,) + dy.shape, BF),
            shape((dp, span[1], width), BF)),
        in_specs=[SMEM, whole(pick), early(step, width), early(step, mask.shape[1])] + [whole(v) for v in tables] + [whole(wg), whole(wu),
                  whole(router), ANY, ANY, ANY, ANY, ANY],
        out_specs=[late(step, width), early(half, width), early(half, ff), early(half, ff), early(half, ff),
                   late(half, width), early(step, TILE), early(step, TILE), early(step, TILE), early(step, 1),
                   early(half, 256), early(step, 128), ANY, ANY],
        scratch_shapes=[
            pltpu.VMEM((ff, width), BF), pltpu.VMEM((2 * TILE, width), BF), pltpu.VMEM((TILE, width), BF),
            pltpu.VMEM((rows, ff), BF), pltpu.VMEM((total, TILE), BF), pltpu.VMEM((total, 1), F32),
            pltpu.VMEM((total, 128), BF), dma((3 * dp,)), dma((3 * dp,))] + Gather.scratch(chunks) + Spread.scratch(dp),
        compiler_params=pltpu.CompilerParams(
            collective_id=cid, has_side_effects=True, vmem_limit_bytes=60 * 1024 * 1024),
        cost_estimate=COST,
        name="mixture_forward",
    )(lengths, pick, mix, mask, *tables, wg, wu, router, share, wda, wdb, down, dy)


def mixture_backward(pick, dy, wg, wu, share, wda, wdb, wdc, act, slo, eo, sact, sslo, gate, slot, token, part, cid, chunks=2):
    total, width = dy.shape
    step, half = total // NZ, total // NZ // 2
    ff = wg.shape[1]
    shape = jax.ShapeDtypeStruct
    rows = total // 2
    dp = wda.shape[0]
    _, own, _ = part.shape
    dma = pltpu.SemaphoreType.DMA
    return pl.pallas_call(
        functools.partial(backward_kernel, chunks),
        grid=(NZ,),
        out_shape=(
            shape((total, width + 128), BF), shape((rows, width), BF), shape((rows, ff), BF), shape((rows, ff), BF),
            shape((total, 2 * TILE), BF), shape((own, width), F32)),
        in_specs=[whole(pick), tiles(step, width), whole(wg), whole(wu), ANY, ANY, ANY, ANY,
                  tiles(half, ff), tiles(half, ff), tiles(half, width), tiles(step, TILE), tiles(step, TILE),
                  tiles(step, 1), tiles(half, 256), tiles(step, 128), ANY],
        out_specs=[tiles(step, width + 128), tiles(half, width), tiles(half, ff), tiles(half, ff),
                   tiles(step, 2 * TILE), pl.BlockSpec((own, width), lambda i: (0, 0))],
        scratch_shapes=[
            pltpu.VMEM((ff, width), BF), pltpu.VMEM((2 * TILE, width), BF), pltpu.VMEM((TILE, width), BF),
            dma((3 * dp,)), dma((3 * dp,))] + Scatter.scratch(own, width, chunks, BF),
        compiler_params=pltpu.CompilerParams(
            collective_id=cid, has_side_effects=True, vmem_limit_bytes=62 * 1024 * 1024),
        cost_estimate=COST,
        name="mixture_backward",
    )(pick, dy, wg, wu, share, wda, wdb, wdc, act, slo, eo, sact, sslo, gate, slot, token, part)


class ShareWork:
    ROWS = 256

    def __init__(self, ds_ref, sh_ref, mix_ref, dy_ref, out_ref, scratch):
        self.sources = (ds_ref, sh_ref, mix_ref, dy_ref)
        self.out = out_ref
        *self.buffers, self.gfan, self.gsd, self.sem = scratch
        self.steps = mix_ref.shape[0] // self.ROWS
        self.done = 0

    @staticmethod
    def scratch(width):
        r = ShareWork.ROWS
        return [pltpu.VMEM((2, r, w), BF) for w in (2 * TILE, TILE, width, width)] + [
            pltpu.VMEM((2 * TILE, width), F32), pltpu.VMEM((TILE, width), F32), pltpu.SemaphoreType.DMA((2, 4))]

    COUNT = 7

    def copies(self, n):
        return [pltpu.make_async_copy(src.at[pl.ds(n * self.ROWS, self.ROWS)], buf.at[n % 2], self.sem.at[n % 2, i])
                for i, (src, buf) in enumerate(zip(self.sources, self.buffers))]

    def start(self):
        for copy in self.copies(0):
            copy.start()
        self.gfan[...] = jnp.zeros_like(self.gfan)
        self.gsd[...] = jnp.zeros_like(self.gsd)

    def step(self):
        n = self.done
        if n == self.steps:
            return
        self.done += 1
        for copy in self.copies(n):
            copy.wait()
        if n + 1 < self.steps:
            for copy in self.copies(n + 1):
                copy.start()
        ds, sh, mix, dy = self.buffers

        def columns(j, _):
            self.gfan[:, lanes(j)] += mm_lead(ds[n % 2], mix[n % 2, :, lanes(j)])
            self.gsd[:, lanes(j)] += mm_lead(sh[n % 2], dy[n % 2, :, lanes(j)])
            return 0

        lax.fori_loop(0, mix.shape[2] // WIDE, columns, 0)

    def finish(self):
        while self.done < self.steps:
            self.step()
        dp, rows, w = self.out.shape
        n = rows // 3
        for d in range(dp):
            cols = slice(d * w, (d + 1) * w)
            self.out[d, :n] = self.gfan[:n, cols].astype(BF)
            self.out[d, n:2 * n] = self.gfan[TILE:TILE + n, cols].astype(BF)
            self.out[d, 2 * n:] = self.gsd[:n, cols].astype(BF)


class WeightWork:
    COUNT = 6
    ROWS = 256

    def __init__(self, lhs, rhs, outs, scratch):
        self.sources, self.outs = (lhs,) + tuple(rhs), outs
        *self.held, self.buf, self.in_sem, self.out_sem = scratch
        self.steps = lhs.shape[1] // self.ROWS

    @staticmethod
    def scratch(lhs, rhs):
        dma = pltpu.SemaphoreType.DMA
        return [pltpu.VMEM(v.shape, BF) for v in (lhs,) + tuple(rhs)] + [
            pltpu.VMEM((2, WeightWork.ROWS, rhs[0].shape[1]), BF), dma((3,)), dma((2,))]

    def loads(self):
        return [pltpu.make_async_copy(v, held, self.in_sem.at[i])
                for i, (v, held) in enumerate(zip(self.sources, self.held))]

    def start(self):
        for copy in self.loads():
            copy.start()

    def ready(self):
        for copy in self.loads():
            copy.wait()

    def store(self, p, n):
        at = pl.ds(pl.multiple_of(n * self.ROWS, self.ROWS), self.ROWS)
        return pltpu.make_async_copy(self.buf.at[p], self.outs[p].at[at], self.out_sem.at[p])

    def step(self, begin, end):
        def body(n, _):
            left = self.held[0][:, pl.ds(pl.multiple_of(n * self.ROWS, self.ROWS), self.ROWS)]
            for p in range(2):
                @pl.when(n > 0)
                def _():
                    self.store(p, n - 1).wait()

                rhs = self.held[1 + p]
                width = rhs.shape[1]
                for at in range(0, width, WIDE):
                    size = min(WIDE, width - at)
                    self.buf[p, :, at:at + size] = mm_lead(left, rhs[:, at:at + size]).astype(BF)
                self.store(p, n).start()
            return 0

        lax.fori_loop(begin, end, body, 0)

    def finish(self):
        for p in range(2):
            self.store(p, self.steps - 1).wait()


def scatter_share_kernel(chunks, dp, p_ref, ds_ref, sh_ref, mix_ref, dy_ref, rows_ref, dg_ref, du_ref, down_ref,
                         o_ref, g_ref, ggate_ref, gup_ref, far_ref, *scratch):
    ns, nw = Scatter.COUNT, ShareWork.COUNT
    s = Scatter(p_ref, o_ref, chunks, scratch[:ns])
    share = ShareWork(ds_ref, sh_ref, mix_ref, dy_ref, g_ref, scratch[ns:ns + nw])
    work = WeightWork(rows_ref, (dg_ref, du_ref), (ggate_ref, gup_ref), scratch[ns + nw:-2])
    swap = Swap(dp, down_ref, far_ref, scratch[-2:])
    enter(s.me, s.z, s.core, s.side, dp)
    swap.start()
    s.start()
    work.start()
    share.start()
    s.first(0)
    s.first(1)
    work.ready()
    third = work.steps // 3
    work.step(0, third)
    s.second(0)
    s.first(2)
    s.first(3)
    work.step(third, 2 * third)
    s.second(1)
    work.step(2 * third, work.steps)
    s.second(2)
    work.finish()
    while share.done < share.steps:
        share.step()
    s.second(3)
    share.finish()
    s.finish()
    swap.finish()


def scatter_share(p, ds, sh, mix, dy, rows, dg, du, down, share_shape, cid, chunks=2):
    _, n, width = p.shape
    shape = jax.ShapeDtypeStruct
    grad = shape((rows.shape[1], dg.shape[1]), BF)
    return pl.pallas_call(
        functools.partial(scatter_share_kernel, chunks, down.shape[0]),
        out_shape=(shape((n, width), F32), shape(share_shape, BF), grad, grad,
                   shape((down.shape[0] - 1,) + down.shape[1:], BF)),
        in_specs=[ANY] * 9,
        out_specs=(VMEM, VMEM, ANY, ANY, ANY),
        scratch_shapes=Scatter.scratch(n, width, chunks, p.dtype) + ShareWork.scratch(mix.shape[1])
        + WeightWork.scratch(rows, (dg, du)) + Swap.scratch(down.shape[0]),
        compiler_params=pltpu.CompilerParams(
            collective_id=cid, has_side_effects=True, vmem_limit_bytes=60 * 1024 * 1024),
        cost_estimate=COST,
        name="scatter_share",
    )(p, ds, sh, mix, dy, rows, dg, du, down)


def turn(v, cosine, sine):
    half = v.shape[1] // 2
    a, b = v[:, :half], v[:, half:]
    return jnp.concatenate([a * cosine - b * sine, b * cosine + a * sine], axis=1)


def project_kernel(x_ref, gain_ref, lgain_ref, wq_ref, wl_ref, we_ref, cos_ref, sin_ref,
                   h_ref, q_ref, k_ref, v_ref, lat_ref):
    blocks = x_ref.shape[0]
    batches, rows, _ = q_ref.shape
    here = rows // blocks
    x = x_ref[...].reshape(blocks * batches * here, x_ref.shape[2]).astype(F32)
    h = x * lax.rsqrt(jnp.mean(x * x, axis=1, keepdims=True) + 1e-6) * gain_ref[...]
    h = h.astype(BF)
    h_ref[...] = h
    raw = mm(h, wq_ref[...])
    raw_lat = mm(h, wl_ref[...])
    cosine, sine = cos_ref[...], sin_ref[...]
    zeros = jnp.zeros((raw.shape[0], 64), BF)
    q = jnp.concatenate([raw[:, :128].astype(BF), turn(raw[:, 128:192], cosine, sine).astype(BF), zeros], axis=1)
    k_rope = turn(raw_lat[:, 512:576], cosine, sine).astype(BF)
    lat = raw_lat[:, :512]
    lat = (lat * lax.rsqrt(jnp.mean(lat * lat, axis=1, keepdims=True) + 1e-6) * lgain_ref[...]).astype(BF)
    expanded = mm(lat, we_ref[...]).astype(BF)
    k = jnp.concatenate([expanded[:, :128], k_rope, zeros], axis=1)
    for e in range(blocks):
        for m in range(batches):
            src = slice((e * batches + m) * here, (e * batches + m + 1) * here)
            dst = slice(e * here, (e + 1) * here)
            q_ref[m, dst] = q[src]
            k_ref[m, dst] = k[src]
            v_ref[m, dst] = expanded[src, 128:]
            lat_ref[m, dst] = lat[src]


def project(x_all, gain, lgain, wq, wl, we, cosine, sine, batches):
    groups, rows, width = x_all.shape
    here = rows // batches
    per = 4
    seq = groups * here
    shape = jax.ShapeDtypeStruct

    def whole(v):
        return pl.BlockSpec(v.shape, lambda i: (0, 0))

    def by_seq(w):
        return pl.BlockSpec((batches, per * here, w), lambda i: (0, i, 0))

    table = pl.BlockSpec((per * rows, 32), lambda i: (i, 0))
    return pl.pallas_call(
        project_kernel,
        grid=(groups // per,),
        out_shape=(shape((groups * rows, width), BF), shape((batches, seq, 256), BF), shape((batches, seq, 256), BF),
                   shape((batches, seq, 128), BF), shape((batches, seq, 512), BF)),
        in_specs=[pl.BlockSpec((per, rows, width), lambda i: (i, 0, 0)), whole(gain), whole(lgain), whole(wq), whole(wl), whole(we),
                  table, table],
        out_specs=[pl.BlockSpec((per * rows, width), lambda i: (i, 0)), by_seq(256), by_seq(256), by_seq(128), by_seq(512)],
        compiler_params=pltpu.CompilerParams(vmem_limit_bytes=48 * 1024 * 1024),
        cost_estimate=pl.CostEstimate(flops=7_000_000_000, bytes_accessed=20_000_000, transcendentals=0),
        name="project",
    )(x_all, gain, lgain, wq, wl, we, cosine, sine)


ROWS = 256
SCALE = 192.0 ** -0.5


def held_scores(q, k, first, length):
    s = mm_t(q, k) * SCALE
    t = lax.broadcasted_iota(jnp.int32, s.shape, 0) + first
    u = lax.broadcasted_iota(jnp.int32, s.shape, 1)
    return jnp.where((u <= t) & (u < length), s, -1e30)


def attend_kernel(dp, span, len_ref, q_ref, k_ref, v_ref, wo_ref, side_ref, sum_ref, att_ref, lse_ref, side_out,
                  part, *scratch):
    m = pl.program_id(0)
    length = len_ref[m]
    seq = q_ref.shape[1]
    groups, rows, width = part.shape
    here = rows // 2
    per = ROWS // here
    sc = Scatter(part, sum_ref, 2, scratch[:Scatter.COUNT])
    job = side_job(dp, span, side_ref, side_out, scratch[Scatter.COUNT:])

    @pl.when(m == 0)
    def _():
        enter(sc.me, sc.z, sc.core, sc.side, dp)
        job.start()

    mine = pl.ds(pl.multiple_of(m * here, here), here)
    for i in range(seq // ROWS):
        tile = slice(i * ROWS, (i + 1) * ROWS)
        ext = (i + 1) * ROWS
        s = held_scores(q_ref[0, tile], k_ref[0, :ext], i * ROWS, length)
        peak = jnp.max(s, axis=1, keepdims=True)
        raised = jnp.exp(s - peak)
        total = jnp.sum(raised, axis=1, keepdims=True)
        lse_ref[0, tile] = peak + jnp.log(total)
        p = (raised / total).astype(BF)
        att = mm(p, v_ref[0, :ext]).astype(BF)
        att_ref[i * per:(i + 1) * per, 0] = att.reshape(per, here, att.shape[1])
        for j in range(width // 512):
            cols = slice(j * 512, (j + 1) * 512)
            part[i * per:(i + 1) * per, mine, cols] = mm(att, wo_ref[:, cols]).astype(BF).reshape(per, here, 512)

        @pl.when(m == 1)
        def _():
            sc.first(i, [0])

    @pl.when(m == 0)
    def _():
        sc.start([0])

    @pl.when(m == 1)
    def _():
        sc.start([1])
        sc.first(0, [1])
        sc.first(1, [1])
        sc.second(0, [0])
        sc.first(2, [1])
        sc.first(3, [1])
        sc.second(1, [0])
        sc.second(2, [0])
        sc.second(0, [1])
        sc.second(3, [0])
        sc.second(1, [1])
        sc.second(2, [1])
        sc.second(3, [1])
        sc.finish()
        job.finish()


def attend(lengths, q, k, v, wo, groups, dp, span, side, cid):
    batches, seq, _ = q.shape
    here = seq // groups
    width = wo.shape[1]
    shape = jax.ShapeDtypeStruct

    def by_seq(w):
        return pl.BlockSpec((1, seq, w), lambda m: (m, 0, 0))

    return pl.pallas_call(
        functools.partial(attend_kernel, dp, span),
        grid=(batches,),
        out_shape=(shape((batches * here, width), F32), shape((groups, batches, here, 128), BF),
                   shape((batches, seq, 1), F32), side_shape(dp, span, side)),
        in_specs=[pl.BlockSpec(memory_space=pltpu.SMEM), by_seq(256), by_seq(256), by_seq(128),
                  pl.BlockSpec(wo.shape, lambda m: (0, 0)), ANY],
        out_specs=[pl.BlockSpec((batches * here, width), lambda m: (0, 0)),
                   pl.BlockSpec((groups, 1, here, 128), lambda m: (0, m, 0, 0)), by_seq(1), ANY],
        scratch_shapes=[pltpu.VMEM((groups, batches * here, width), BF)]
        + Scatter.scratch(batches * here, width, 2, BF) + side_scratch(dp, span),
        compiler_params=pltpu.CompilerParams(
            collective_id=cid, has_side_effects=True, vmem_limit_bytes=60 * 1024 * 1024),
        cost_estimate=COST,
        name="attend",
    )(lengths, q, k, v, wo, side)


def attend_back_kernel(dp, len_ref, own_ref, side_ref, h_ref, q_ref, k_ref, v_ref, lat_ref, att_ref, lse_ref, wo_ref, wq_ref, we_ref,
                       cos_ref, sin_ref, part_ref, gwq_ref, gwo_out, gwe_out, side_out,
                       dout_ref, dk, dv, datt, gwq, gwo_ref, gwe_ref, *scratch):
    m = pl.program_id(0)
    length = len_ref[m]
    seq = q_ref.shape[1]
    groups, _, width = dout_ref.shape
    here = h_ref.shape[2]
    per = ROWS // here
    g = Gather(own_ref, dout_ref, 2, scratch[:Gather.COUNT])
    job = side_job(dp, None, side_ref, side_out, scratch[Gather.COUNT:])

    @pl.when(m == 0)
    def _():
        enter(g.me, g.z, g.core, g.side, dp)
        job.start()
        g.start([0])
        g.start([1])
        g.round(1, [0])
        g.round(2, [0])
        g.round(1, [1])
        g.round(3, [0])
        g.round(2, [1])
        g.round(4, [0])
        g.kept().wait()
        g.landed([0])
        gwo_ref[...] = jnp.zeros_like(gwo_ref)
        gwe_ref[...] = jnp.zeros_like(gwe_ref)
        gwq[...] = jnp.zeros_like(gwq)

    @pl.when(m == 1)
    def _():
        g.round(4, [1])
        g.landed([1])

    mine = pl.ds(pl.multiple_of(m * here, here), here)
    for j in range(4):
        blocks = slice(j * groups // 4, (j + 1) * groups // 4)
        dout = dout_ref[blocks, mine].reshape(seq // 4, width)
        rows = slice(j * seq // 4, (j + 1) * seq // 4)
        datt[rows] = mm_t(dout, wo_ref[...]).astype(BF)
        gwo_ref[...] += mm_lead(att_ref[blocks].reshape(seq // 4, 128), dout)
    @pl.when(m == 0)
    def _():
        g.round(3, [1])

    dk[...] = jnp.zeros_like(dk)
    dv[...] = jnp.zeros_like(dv)
    for i in range(seq // ROWS):
        tile = slice(i * ROWS, (i + 1) * ROWS)
        ext = (i + 1) * ROWS
        q = q_ref[0, tile]
        p = jnp.exp(held_scores(q, k_ref[0, :ext], i * ROWS, length) - lse_ref[0, tile])
        da = datt[tile]
        dp = mm_t(da, v_ref[0, :ext])
        inner = jnp.sum(dp * p, axis=1, keepdims=True)
        ds = (p * (dp - inner)).astype(BF)
        dq = mm(ds, k_ref[0, :ext]) * SCALE
        dk[:ext] += mm_lead(ds, q)
        dv[:ext] += mm_lead(p.astype(BF), da)
        rope = turn(dq[:, 128:192], cos_ref[tile], -sin_ref[tile])
        dq = jnp.concatenate([dq[:, :128].astype(BF), rope.astype(BF), jnp.zeros((ROWS, 64), BF)], axis=1)
        hidden = h_ref[i * per:(i + 1) * per, 0].reshape(ROWS, width)
        for j in range(width // 512):
            cols = slice(j * 512, (j + 1) * 512)
            gwq[:, cols] += mm_lead(dq, hidden[:, cols])
        for j in range(width // 512):
            cols = slice(j * 512, (j + 1) * 512)
            part_ref[i * per:(i + 1) * per, 0, :, cols] = mm_t(dq, wq_ref[cols]).astype(BF).reshape(per, here, 512)
    for i in range(seq // ROWS):
        tile = slice(i * ROWS, (i + 1) * ROWS)
        d_k = dk[tile] * SCALE
        d_exp = jnp.concatenate([d_k[:, :128].astype(BF), dv[tile].astype(BF)], axis=1)
        gwe_ref[...] += mm_lead(lat_ref[0, tile], d_exp)
        d_lat = mm_t(d_exp, we_ref[...]).astype(BF)
        tail = jnp.concatenate([d_lat, d_k[:, 128:].astype(BF)], axis=1)
        pad = part_ref.shape[3] - width - tail.shape[1]
        if pad > 0:
            tail = jnp.concatenate([tail, jnp.zeros((ROWS, pad), BF)], axis=1)
        part_ref[i * per:(i + 1) * per, 0, :, width:] = tail[:, :part_ref.shape[3] - width].reshape(per, here, -1)

    @pl.when(m == pl.num_programs(0) - 1)
    def _():
        for j in range(width // 256):
            cols = slice(j * 256, (j + 1) * 256)
            gwq_ref[cols] = gwq[:, cols].T.astype(BF)
        gwo_out[...] = gwo_ref[...].astype(BF)
        gwe_out[...] = gwe_ref[...].astype(BF)
        g.finish(False)
        job.finish()


def attend_back(dp, lengths, dout, side, h, q, k, v, lat, att, lse, wo, wq, we, cosine, sine, tail, cid):
    groups, batches, here, width = h.shape
    seq = groups * here
    shape = jax.ShapeDtypeStruct

    def by_seq(w):
        return pl.BlockSpec((1, seq, w), lambda m: (m, 0, 0))

    def by_dev(w):
        return pl.BlockSpec((groups, 1, here, w), lambda m: (0, m, 0, 0))

    def whole(v):
        return pl.BlockSpec(v.shape, lambda m: (0, 0))

    return pl.pallas_call(
        functools.partial(attend_back_kernel, dp),
        grid=(batches,),
        out_shape=(shape((groups, batches, here, width + tail), BF), shape(wq.shape, BF),
                   shape(wo.shape, BF), shape(we.shape, BF), side_shape(dp, None, side)),
        in_specs=[pl.BlockSpec(memory_space=pltpu.SMEM), ANY, ANY, by_dev(width), by_seq(256), by_seq(256), by_seq(128),
                  by_seq(512), by_dev(128), by_seq(1), whole(wo), whole(wq), whole(we), whole(cosine), whole(sine)],
        out_specs=[by_dev(width + tail), whole(wq), whole(wo), whole(we), ANY],
        scratch_shapes=[pltpu.VMEM((groups, batches * here, width), BF), pltpu.VMEM((seq, 256), F32), pltpu.VMEM((seq, 128), F32), pltpu.VMEM((seq, 128), BF),
                        pltpu.VMEM((256, width), F32), pltpu.VMEM(wo.shape, F32), pltpu.VMEM(we.shape, F32)]
        + Gather.scratch(2) + side_scratch(dp, None),
        compiler_params=pltpu.CompilerParams(
            collective_id=cid, has_side_effects=True, vmem_limit_bytes=60 * 1024 * 1024),
        cost_estimate=COST,
        name="attend_back",
    )(lengths, dout, side, h, q, k, v, lat, att, lse, wo, wq, we, cosine, sine)


def turn_kernel(v_ref, o_ref):
    for i in range(v_ref.shape[0] // 128):
        rows = slice(i * 128, (i + 1) * 128)
        o_ref[:, rows] = v_ref[rows].astype(F32).T.astype(o_ref.dtype)


def turned(v, block):
    return pl.pallas_call(
        turn_kernel,
        grid=(1,),
        out_shape=jax.ShapeDtypeStruct((128, v.shape[0]), v.dtype),
        in_specs=[pl.BlockSpec((v.shape[0], 128), lambda i: (0, block))],
        out_specs=pl.BlockSpec((128, v.shape[0]), lambda i: (0, 0)),
        compiler_params=pltpu.CompilerParams(vmem_limit_bytes=16 * 1024 * 1024),
        cost_estimate=COST,
        name="turned",
    )(v)


def split_rows(v):
    high = v.astype(BF)
    return [high, (v - high.astype(F32)).astype(BF)]


def own_back_kernel(dp, back_ref, x_ref, mix_ref, logit_ref, gmix_ref, gain_ref, lgain_ref, small_ref, cos_ref, sin_ref,
                    mid_ref, place_ref, grad_ref, out_ref):
    width = x_ref.shape[1]
    rows_w = out_ref.shape[1] // dp
    lanes_w = out_ref.shape[2]
    x = x_ref[...].astype(F32)
    factor = lax.rsqrt(jnp.mean(x * x, axis=1, keepdims=True) + 1e-6)
    unit = x * factor
    hidden = (unit * gain_ref[...]).astype(BF)
    lat = mm(hidden, small_ref[:, :512])
    factor_l = lax.rsqrt(jnp.mean(lat * lat, axis=1, keepdims=True) + 1e-6)
    unit_l = lat * factor_l
    d_lat = back_ref[:, width:width + 512]
    scaled = d_lat * lgain_ref[...]
    d_in = factor_l * (scaled - unit_l * jnp.mean(scaled * unit_l, axis=1, keepdims=True))
    g_lat = jnp.sum(d_lat * unit_l, axis=0, keepdims=True)
    d_rope = turn(back_ref[:, width + 512:width + 576], cos_ref[...], -sin_ref[...])
    tokens = x.shape[0]
    d_raw = jnp.concatenate(
        [d_in.astype(BF), d_rope.astype(BF), jnp.zeros((tokens, lanes_w - 576), BF)], axis=1)
    d_hidden = back_ref[:, :width] + mm_t(d_raw, small_ref[...])
    scaled = d_hidden * gain_ref[...]
    grad_ref[...] = mid_ref[...] + factor * (scaled - unit * jnp.mean(scaled * unit, axis=1, keepdims=True))
    g_gain = jnp.sum(d_hidden * unit, axis=0, keepdims=True)
    spread = [mm(v, place_ref[...]).astype(BF) for v in split_rows(g_lat)]
    extra = split_rows(g_gain) + split_rows(gmix_ref[...]) + spread + [jnp.zeros((10, width), BF)]
    left = jnp.concatenate([hidden, mix_ref[...]] + extra, axis=0)
    logit = jnp.concatenate(
        [jnp.zeros((tokens, 576), BF), logit_ref[...], jnp.zeros((tokens, lanes_w - 592), BF)], axis=1)
    n = lax.broadcasted_iota(jnp.int32, (16, lanes_w), 0)
    at = 592 + (n >> 1)
    hot = jnp.where((lax.broadcasted_iota(jnp.int32, (16, lanes_w), 1) == at) & (n < 6), 1.0, 0.0).astype(BF)
    right = jnp.concatenate([d_raw, logit, hot], axis=0)
    for j in range(width // 256):
        part = mm_lead(left[:, j * 256:(j + 1) * 256], right).astype(BF)
        for i in range(256 // rows_w):
            owner = j * (256 // rows_w) + i
            d, e = owner // NE, owner % NE
            out_ref[e, d * rows_w:(d + 1) * rows_w] = part[i * rows_w:(i + 1) * rows_w]


def one_step(*arrays):
    return [pl.BlockSpec(v.shape, lambda i, n=v.ndim if hasattr(v, "ndim") else len(v.shape): (0,) * n) for v in arrays]


def own_back(dp, back, x, mix, logit, gmix, gain, lgain, small, cosine, sine, mid, rows_l):
    tokens, width = x.shape
    rows_w = width // (dp * NE)
    count = np.arange(width)
    place = (count // rows_w * rows_l + count % rows_w)[None, :] == np.arange(512)[:, None]
    place = place & (count % rows_w < rows_l)[None, :]
    shape = jax.ShapeDtypeStruct
    args = (back, x, mix, logit, gmix, gain, lgain, small, cosine, sine, mid, jnp.asarray(place.astype(np.float32), BF))
    outs = (shape((tokens, width), F32), shape((NE, dp * rows_w, small.shape[1]), BF))
    return pl.pallas_call(
        functools.partial(own_back_kernel, dp),
        grid=(1,),
        out_shape=outs,
        in_specs=one_step(*args),
        out_specs=tuple(one_step(*outs)),
        compiler_params=pltpu.CompilerParams(vmem_limit_bytes=60 * 1024 * 1024),
        cost_estimate=COST,
        name="own_back",
    )(*args)


def own_middle_kernel(sum_ref, mix_ref, mask_ref, router_ref, middle_ref, gain_ref, dy_ref, valid_ref,
                      grad_ref, low_ref, logit_ref, gmix_ref):
    width = mix_ref.shape[1]
    middle = middle_ref[...]
    factor = lax.rsqrt(jnp.mean(middle * middle, axis=1, keepdims=True) + 1e-6)
    unit = middle * factor
    mask = mask_ref[...].astype(F32)
    held = jnp.where(mask > 0.5, mm_t(mix_ref[...], router_ref[...]), -1e30)
    raised = jnp.exp(held - jnp.max(held, axis=1, keepdims=True)) * mask
    soft = raised / jnp.sum(raised, axis=1, keepdims=True)
    d_gates = (sum_ref[:, width:width + 16] + sum_ref[:, width + 16:width + 32]) * valid_ref[...]
    d_logits = (soft * (d_gates - jnp.sum(d_gates * soft, axis=1, keepdims=True))).astype(BF)
    logit_ref[...] = d_logits
    d_mix = sum_ref[:, :width] + mm(d_logits, router_ref[...])
    gmix_ref[...] = jnp.sum(d_mix * unit, axis=0, keepdims=True)
    scaled = d_mix * gain_ref[...]
    grad = dy_ref[...].astype(F32) + factor * (scaled - unit * jnp.mean(scaled * unit, axis=1, keepdims=True))
    grad_ref[...] = grad
    low_ref[...] = grad.astype(BF)


def own_middle(total, mix, mask, router, middle, gain, dy, valid):
    shape = jax.ShapeDtypeStruct
    args = (total, mix, mask, router, middle, gain, dy, valid)
    outs = (shape(middle.shape, F32), shape(middle.shape, BF), shape(mask.shape, BF), shape(gain.shape, F32))
    return pl.pallas_call(
        own_middle_kernel,
        grid=(1,),
        out_shape=outs,
        in_specs=one_step(*args),
        out_specs=tuple(one_step(*outs)),
        compiler_params=pltpu.CompilerParams(vmem_limit_bytes=60 * 1024 * 1024),
        cost_estimate=COST,
        name="own_middle",
    )(*args)


def widen_kernel(plane_ref, gate_ref, up_ref, down_ref, down_far, share_ref, share_far, gate_out, up_out, down_out, sg_out,
                 su_out, sd_out):
    gate_out[...] = gate_ref[...].astype(F32)
    up_out[...] = up_ref[...].astype(F32)
    down = down_ref[0].astype(F32)
    for r in range(down_far.shape[0]):
        down = down + down_far[r].astype(F32)
    down_out[...] = down

    @pl.when(pl.program_id(0) == 0)
    def _():
        n = sg_out.shape[0]
        for i, out in enumerate((sg_out, su_out, sd_out)):
            rows = slice(i * n, (i + 1) * n)
            v = share_ref[0, rows].astype(F32)
            for r in range(share_far.shape[0]):
                v = v + share_far[r, rows].astype(F32)
            out[...] = v


def widen(plane, gate, up, down, down_far, share, share_far):
    steps = 2 if down.shape[1] % 32 == 0 else 1
    shape = jax.ShapeDtypeStruct

    def cut(rows, w):
        return pl.BlockSpec((rows // steps, w), lambda i, p: (i, 0))

    def full(shape_):
        zeros = (0,) * len(shape_)
        return pl.BlockSpec(shape_, lambda i, p: zeros)

    _, rows, w = down.shape
    third = (share.shape[1] // 3, share.shape[2])
    return pl.pallas_call(
        widen_kernel,
        grid_spec=pltpu.PrefetchScalarGridSpec(
            num_scalar_prefetch=1,
            grid=(steps,),
            in_specs=[cut(*gate.shape), cut(*up.shape),
                      pl.BlockSpec((1, rows // steps, w), lambda i, p: (p[0], i, 0)),
                      pl.BlockSpec((down_far.shape[0], rows // steps, w), lambda i, p: (0, i, 0)),
                      pl.BlockSpec((1,) + share.shape[1:], lambda i, p: (p[0], 0, 0)), full(share_far.shape)],
            out_specs=[cut(*gate.shape), cut(*up.shape), cut(rows, w)] + [full(third)] * 3,
        ),
        out_shape=tuple(shape(v, F32) for v in (gate.shape, up.shape, (rows, w))) + (shape(third, F32),) * 3,
        compiler_params=pltpu.CompilerParams(vmem_limit_bytes=56 * 1024 * 1024),
        cost_estimate=COST,
        name="widen",
    )(plane, gate, up, down, down_far, share, share_far)


H = 16
QK_NOPE = 128
ROPE = 64
V_DIM = 128
KV_RANK = 512
GROUPS = 16
EPSILON = 1e-06
ROTARY_BASE = 10000.0


def product(left_side, right_side):
    return jnp.dot(left_side, right_side, preferred_element_type=F32)


def product_lead(left_side, right_side):
    return lax.dot_general(
        left_side, right_side, (((0,), (0,)), ((), ())), preferred_element_type=F32
    )


def product_trail(left_side, right_side):
    return lax.dot_general(
        left_side, right_side, (((1,), (1,)), ((), ())), preferred_element_type=F32
    )


def rotary_tables(count):
    frequency = ROTARY_BASE ** (-np.arange(ROPE // 2, dtype=np.float32) * np.float32(2.0) / np.float32(ROPE))
    angles = np.arange(count, dtype=np.float32)[:, None] * frequency.astype(np.float32)[None, :]
    return np.cos(angles).astype(np.float32), np.sin(angles).astype(np.float32)


def rotate(values, cosine, sine_table):
    first_half, second_half = jnp.split(values, 2, axis=-1)
    return jnp.concatenate(
        [
            first_half * cosine - second_half * sine_table,
            second_half * cosine + first_half * sine_table,
        ],
        axis=-1,
    )


def norm_forward(values, gains):
    factor = lax.rsqrt(jnp.mean(values * values, axis=-1, keepdims=True) + EPSILON)
    normed = values * factor
    return (normed * gains, normed, factor)


def norm_backward(gradient, normed, factor, gains):
    gain_grad = jnp.sum(gradient * normed, axis=0)
    scaled = gradient * gains
    return (
        factor * (scaled - normed * jnp.mean(scaled * normed, axis=-1, keepdims=True)),
        gain_grad,
    )


def selected_experts(routes):
    chosen = routes[:, :, None] == jnp.arange(GROUPS, dtype=routes.dtype)
    return jnp.any(chosen, axis=1)


def masked_softmax(logits, mask):
    held = jnp.where(mask, logits, -1e30)
    peak = jnp.max(held, axis=-1, keepdims=True)
    raised = jnp.where(mask, jnp.exp(held - peak), 0.0)
    return raised / jnp.sum(raised, axis=-1, keepdims=True)


def per_device(
    layer_input,
    out_cotangent,
    lengths,
    routes,
    attn_gain,
    query_weight,
    latent_weight,
    latent_gain,
    expand_weight,
    output_weight,
    mixer_gain,
    router_weight,
    gate_weight,
    up_weight,
    down_weight,
    shared_gate,
    shared_up,
    shared_down,
):
    dp = lax.axis_size("dp")
    me = lax.axis_index("expert")
    plane = lax.axis_index("dp")
    batches, _, here, width = layer_input.shape
    own = batches * here
    total = own * GROUPS
    seq_total = here * GROUPS
    rows_w = query_weight.shape[0]
    rows_l = expand_weight.shape[0]

    x_own = layer_input.reshape(own, width)
    mask_own = selected_experts(routes.reshape(own, -1))
    mask_columns = mask_own.astype(BF).reshape(rows_w, -1)
    small_width = -(-(595 + mask_columns.shape[1]) // 128) * 128
    latent_column = jnp.zeros((rows_w,), BF).at[:rows_l].set(latent_gain)
    small = jnp.concatenate(
        [
            latent_weight,
            router_weight,
            attn_gain[:, None],
            mixer_gain[:, None],
            latent_column[:, None],
            mask_columns,
            jnp.zeros((rows_w, small_width - 595 - mask_columns.shape[1]), BF),
        ],
        axis=1,
    )
    query_parts = query_weight.reshape(rows_w, H, QK_NOPE + ROPE).transpose(1, 0, 2)
    expand_parts = expand_weight.reshape(rows_l, H, QK_NOPE + V_DIM).transpose(1, 0, 2)
    expand_parts = expand_parts.reshape(H, rows_l, 4, ROPE).swapaxes(1, 2).reshape(H, rows_w, ROPE)
    parts = jnp.concatenate([query_parts, expand_parts], axis=2)
    x_all, small, parts_head, output_head = opening(dp, x_own, small, parts, output_weight, 1)
    x_all = x_all.reshape(total, width)
    mask_all = lax.dynamic_index_in_dim(small, plane, 0, False)[..., 595 : 595 + mask_columns.shape[1]]
    mask_all = mask_all.reshape(total, GROUPS)
    small = small.reshape(width, small_width)
    parts_head = parts_head.reshape(width, TILE)
    latent_full = small[:, :576]
    lines = turned(small, 4)
    router_lines = lines[64:80]
    gain_attn = lines[80].astype(F32)
    gain_mixer = lines[81].astype(F32)
    gain_latent = lines[82].reshape(dp * GROUPS, rows_w)[:, :rows_l].reshape(-1).astype(F32)
    expand_head = parts_head[:, QK_NOPE + ROPE :].reshape(dp * GROUPS, 4, rows_l, ROPE)
    expand_head = expand_head.swapaxes(1, 2).reshape(KV_RANK, QK_NOPE + V_DIM)
    output_head = output_head.reshape(V_DIM, width)

    ff = gate_weight.shape[2]
    share_own = jnp.concatenate([shared_gate.T, shared_up.T, shared_down], axis=0)
    share_width = shared_down.shape[0]
    gate_full = lax.all_gather(gate_weight[0], "dp", axis=0, tiled=True)
    up_full = lax.all_gather(up_weight[0], "dp", axis=0, tiled=True)
    share_full = lax.all_gather(share_own, "dp", axis=0)
    seq_lengths = lengths.reshape(batches)
    own_positions = me * here + jnp.arange(here, dtype=jnp.int32)
    valid_own = (own_positions[None, :] < seq_lengths[:, None]).reshape(own).astype(F32)
    cosine, sine_table = rotary_tables(seq_total)

    grad_own = out_cotangent.reshape(own, width) * valid_own[:, None].astype(BF)

    def by_token(table):
        return jnp.asarray(np.broadcast_to(
            table.reshape(GROUPS, 1, here, -1), (GROUPS, batches, here, table.shape[1])).reshape(total, -1))

    hidden_all, query, key, values, latent = project(
        x_all.reshape(GROUPS, own, width), gain_attn[None], gain_latent[None], parts_head, small, expand_head,
        by_token(cosine), by_token(sine_table), batches)
    down_own = down_weight[0]
    cut = down_own.shape[0] * 3 // 160 * 16
    cuts = (0, cut, 2 * cut + cut // 48 * 16, down_own.shape[0])
    spans = [(first, last - first) for first, last in zip(cuts, cuts[1:])]
    attn_out, attended, log_total, down_a = attend(
        seq_lengths, query, key, values, output_head, GROUPS, dp, spans[0], down_own, 2)

    x_wide = x_own.astype(F32)
    middle = x_wide + attn_out
    normed_mix, unit_mix, factor_mix = norm_forward(middle, gain_mixer)
    hidden_mix = normed_mix.astype(BF)
    mix_all, down_b = gather16(hidden_mix, 3, dp=dp, span=spans[1], side=down_own)
    mix_all = mix_all.reshape(total, width)

    lane = jnp.arange(128)[None, :]
    pick = jnp.concatenate([lane == me, lane == me + GROUPS], axis=1).astype(F32)
    (out_part, rows, hidden, act, slope, result, share_hidden, share_act, share_slope, gates, to_slot, to_token,
     grad_all, down_c) = mixture_forward(
        dp, batches, here, seq_lengths, pick, mix_all, mask_all, gate_full, up_full, router_lines, share_full,
        down_a, down_b, spans[2], down_own, grad_own, 4)
    grad_all = grad_all.reshape(total, width)
    mix_part, grad_result, grad_gate_in, grad_up_in, grad_share_in, mixed = mixture_backward(
        pick, grad_all, gate_full, up_full, share_full, down_a, down_b, down_c, act, slope, result,
        share_act, share_slope, gates, to_slot, to_token, out_part.reshape(GROUPS, own, width), 8)
    grad_down = product_lead(hidden, grad_result).astype(BF)
    grad_down = grad_down.reshape(dp, ff // dp, width)
    mix_sum, grad_share, grad_gate, grad_up, far_down = scatter_share(
        mix_part.reshape(GROUPS, own, width + 128), grad_share_in, share_hidden, mix_all, grad_all,
        rows, grad_gate_in, grad_up_in, grad_down, share_full.shape, 5)
    layer_output = valid_own[:, None] * (middle + mixed)

    out_gate = lax.psum_scatter(grad_gate, "dp", scatter_dimension=0, tiled=True)
    out_up = lax.psum_scatter(grad_up, "dp", scatter_dimension=0, tiled=True)

    grad_middle, grad_middle_low, grad_logits, grad_gain_mixer = own_middle(
        mix_sum, hidden_mix, mask_own.astype(BF), router_lines, middle, gain_mixer[None], grad_own, valid_own[:, None])

    back_part, grad_query_w, grad_output, grad_expand, share_far = attend_back(
        dp, seq_lengths, grad_middle_low, grad_share, hidden_all.reshape(GROUPS, batches, here, width), query, key,
        values, latent, attended, log_total, output_head, parts_head, expand_head, jnp.asarray(cosine),
        jnp.asarray(sine_table), 640, 6)
    grad_expand = grad_expand.reshape(dp * GROUPS, rows_l, 4, ROPE).swapaxes(1, 2).reshape(width, ROPE)
    parts_grad = grad_query_w + jnp.pad(grad_expand, ((0, 0), (QK_NOPE + ROPE, 0)))
    parts_grad = parts_grad.reshape(dp, GROUPS, rows_w, TILE)
    rows_grad = grad_output.reshape(dp, rows_w, width)
    back_sum, parts_far, rows_far = returning(
        dp, back_part.reshape(GROUPS, own, back_part.shape[3]), parts_grad, rows_grad, 7)
    parts_sum = lax.dynamic_index_in_dim(parts_grad, plane, 0, False).astype(F32)
    parts_sum = (parts_sum + jnp.sum(parts_far.astype(F32), axis=0)).astype(BF)
    rows_sum = (rows_grad.astype(F32) + jnp.sum(rows_far.astype(F32), axis=0)).astype(BF)

    def own_table(table):
        own_rows = lax.dynamic_slice_in_dim(jnp.asarray(table), me * here, here)
        return jnp.broadcast_to(own_rows[None], (batches, here, ROPE // 2)).reshape(own, ROPE // 2)

    grad_input, small_grad = own_back(
        dp, back_sum, x_own, hidden_mix, grad_logits, grad_gain_mixer, gain_attn[None], gain_latent[None], small,
        own_table(cosine), own_table(sine_table), grad_middle, rows_l)
    small_sum, out_query, out_expand, out_output = closing(dp, small_grad, parts_sum, rows_sum, rows_l, 9)

    out_gate, out_up, out_down, out_sgate, out_sup, out_sdown = widen(
        plane.reshape(1).astype(jnp.int32), out_gate, out_up, grad_down, far_down, grad_share, share_far)

    def as_input(v):
        return v.reshape(batches, 1, here, width)

    return (
        as_input(layer_output),
        as_input(grad_input),
        small_sum[:, 592],
        out_query,
        small_sum[:, :576],
        small_sum[:rows_l, 594],
        out_expand,
        out_output,
        small_sum[:, 593],
        small_sum[:, 576:592],
        out_gate[None],
        out_up[None],
        out_down[None],
        out_sgate.T,
        out_sup.T,
        out_sdown,
    )


def solution(mesh):
    split = P(("dp", "expert"), None)
    line = P(("dp", "expert"))
    tokens = P(None, "dp", "expert", None)
    expert = P("expert", "dp", None)
    return jax.shard_map(
        per_device,
        mesh=mesh,
        in_specs=(
            tokens, tokens, P(None, "dp"), tokens, line, split, split, line, split, split, line, split,
            expert, expert, expert, P("dp", "expert"), P("dp", "expert"), P("expert", "dp"),
        ),
        out_specs=(
            tokens, tokens, line, split, split, line, split, split, line, split,
            expert, expert, expert, P("dp", "expert"), P("dp", "expert"), P("expert", "dp"),
        ),
        check_vma=False,
    )
```

```python
import functools
import jax
import jax.numpy as jnp
import numpy as np
from jax import lax
from jax.experimental import pallas as pl
from jax.experimental.pallas import tpu as pltpu
from jax.sharding import PartitionSpec as P

MESH = pl.DeviceIdType.MESH
NZ = 4
NE = 16


def place():
    me = lax.axis_index("expert")
    z = me // 4
    x = (me // 2) % 2
    c = me % 2
    return me, z, x, c, me + 1 - 2 * c, me + 2 - 4 * x


def enter(me, z, core, side, dp=1):
    barrier = pltpu.get_barrier_semaphore()
    plane = lax.axis_index("dp")
    for r in range(1, dp):
        pl.semaphore_signal(barrier, inc=1, device_id={"dp": (plane + r) % dp}, device_id_type=MESH)
    for other in (core, side):
        pl.semaphore_signal(barrier, inc=1, device_id={"expert": other}, device_id_type=MESH)

    @pl.when(z < NZ - 1)
    def _():
        pl.semaphore_signal(barrier, inc=1, device_id={"expert": me + 4}, device_id_type=MESH)

    @pl.when(z > 0)
    def _():
        pl.semaphore_signal(barrier, inc=1, device_id={"expert": me - 4}, device_id_type=MESH)

    pl.semaphore_wait(barrier, dp + 1 + (z < NZ - 1).astype(jnp.int32) + (z > 0).astype(jnp.int32))


class Spread:
    def __init__(self, dp, src, out, sems):
        self.dp, self.src, self.out = dp, src, out
        self.own, self.send, self.recv = sems
        self.plane = lax.axis_index("dp")

    @staticmethod
    def scratch(dp):
        dma = pltpu.SemaphoreType.DMA
        return [dma, dma((dp,)), dma((dp,))]

    def copy(self, r):
        return pltpu.make_async_remote_copy(
            src_ref=self.src, dst_ref=self.out.at[self.plane], send_sem=self.send.at[r], recv_sem=self.recv.at[r],
            device_id={"dp": (self.plane + r) % self.dp}, device_id_type=MESH)

    def arrival(self, r):
        p = (self.plane - r + self.dp) % self.dp
        return pltpu.make_async_remote_copy(
            src_ref=self.src, dst_ref=self.out.at[p], send_sem=self.send.at[r], recv_sem=self.recv.at[r],
            device_id={"dp": p}, device_id_type=MESH)

    def start(self):
        for r in range(1, self.dp):
            self.copy(r).start()
        self.kept = pltpu.make_async_copy(self.src, self.out.at[self.plane], self.own)
        self.kept.start()

    def finish(self):
        self.kept.wait()
        for r in range(1, self.dp):
            self.arrival(r).wait_recv()
            self.copy(r).wait_send()


class Swap:
    def __init__(self, dp, src, out, sems):
        self.dp, self.src, self.out = dp, src, out
        self.send, self.recv = sems
        self.plane = lax.axis_index("dp")

    @staticmethod
    def scratch(dp):
        dma = pltpu.SemaphoreType.DMA
        return [dma((dp,)), dma((dp,))]

    def copy(self, r):
        to = (self.plane + r) % self.dp
        return pltpu.make_async_remote_copy(
            src_ref=self.src.at[to], dst_ref=self.out.at[r - 1], send_sem=self.send.at[r], recv_sem=self.recv.at[r],
            device_id={"dp": to}, device_id_type=MESH)

    def start(self):
        for r in range(1, self.dp):
            self.copy(r).start()

    def finish(self):
        for r in range(1, self.dp):
            self.copy(r).wait_recv()
            self.copy(r).wait_send()


def side_job(dp, span, src, out, sems):
    if span is None:
        return Swap(dp, src, out, sems)
    return Spread(dp, src.at[pl.ds(span[0], span[1])], out, sems)


def side_shape(dp, span, side):
    if span is None:
        return jax.ShapeDtypeStruct((dp - 1,) + side.shape[1:], side.dtype)
    return jax.ShapeDtypeStruct((dp, span[1], side.shape[1]), side.dtype)


def side_scratch(dp, span):
    return (Swap if span is None else Spread).scratch(dp)


def enter_all(me, plane, dp):
    barrier = pltpu.get_barrier_semaphore()
    for r in range(1, NE):
        pl.semaphore_signal(
            barrier, inc=1, device_id={"expert": (me + r) % NE}, device_id_type=MESH)
    for r in range(1, dp):
        pl.semaphore_signal(
            barrier, inc=1, device_id={"dp": (plane + r) % dp}, device_id_type=MESH)
    pl.semaphore_wait(barrier, NE - 1 + dp - 1)


class Gather:
    def __init__(self, src, out, chunks, sems, view=lambda ref, b: ref.at[b]):
        self.src, self.out, self.chunks, self.view = src, out, chunks, view
        self.rows = src.shape[0] // chunks
        (self.own_sem, self.us, self.ur, self.ds, self.dr, self.bus, self.bur, self.bds, self.bdr,
         self.xs, self.xr, self.cs, self.cr) = sems
        self.me, self.z, self.x, self.c, self.core, self.side = place()

    COUNT = 13

    @staticmethod
    def scratch(chunks):
        dma = pltpu.SemaphoreType.DMA
        return [dma] + [dma((4, chunks))] * 8 + [dma((7, chunks))] * 2 + [dma((14, chunks))] * 2

    def alt(self, k):
        return k >= (self.chunks + 1) // 2

    def order(self, ks=None):
        return range(self.chunks - 1, -1, -1) if ks is None else ks

    def copy(self, block, k, src, send, recv, to):
        src_ref = self.src if src is None else self.view(self.out, src)
        dst_ref = self.view(self.out, block)
        if self.chunks > 1:
            part = pl.ds(k * self.rows, self.rows)
            src_ref, dst_ref = src_ref.at[part], dst_ref.at[part]
        return pltpu.make_async_remote_copy(
            src_ref=src_ref,
            dst_ref=dst_ref,
            send_sem=send, recv_sem=recv,
            device_id={"expert": to}, device_id_type=MESH,
        )

    def up(self, k, s, src=None):
        return self.copy(self.me - 4 * s, k, src, self.us.at[s, k], self.ur.at[s, k], self.me + 4)

    def down(self, k, s, src=None):
        return self.copy(self.me + 4 * s, k, src, self.ds.at[s, k], self.dr.at[s, k], self.me - 4)

    def up_b(self, k, s):
        b = self.side - 4 * s
        return self.copy(b, k, b, self.bus.at[s, k], self.bur.at[s, k], self.me + 4)

    def down_b(self, k, s):
        b = self.side + 4 * s
        return self.copy(b, k, b, self.bds.at[s, k], self.bdr.at[s, k], self.me - 4)

    def across(self, k, slot, block, src=None):
        return self.copy(block, k, src, self.xs.at[slot, k], self.xr.at[slot, k], self.side)

    def over(self, k, slot, block, src=None):
        return self.copy(block, k, src, self.cs.at[slot, k], self.cr.at[slot, k], self.core)

    def arrived(self, b, k, sems, s):
        return self.copy(b, k, b, sems[0].at[s - 1, k], sems[1].at[s - 1, k], self.side)

    def shift(self, base, slot):
        return base - 4 * slot if slot <= 3 else base + 4 * (slot - 3)

    def core_block(self, slot):
        if slot < 7:
            return self.shift(self.core, slot)
        return self.shift(self.core + 2 - 4 * self.x, slot - 7)

    def has(self, slot):
        slot = slot % 7
        if slot == 0:
            return self.z >= 0
        return self.z >= slot if slot <= 3 else self.z + (slot - 3) <= NZ - 1

    def crosses(self, k, slot):
        if slot == 0 or not self.alt(k):
            return self.has(slot)
        return self.z > slot if slot <= 3 else self.z + (slot - 3) < NZ - 1

    def kept(self):
        return pltpu.make_async_copy(self.src, self.view(self.out, self.me), self.own_sem)

    def start(self, ks=None):
        z, me = self.z, self.me
        if ks is None or 0 in ks:
            self.kept().start()
        for k in self.order(ks):
            self.across(k, 0, me).start()

            @pl.when(z < NZ - 1)
            def _():
                self.up(k, 0).start()

            @pl.when(z > 0)
            def _():
                self.down(k, 0).start()

            self.over(k, 0, me).start()

    def line(self, k, s):
        z, me = self.z, self.me

        @pl.when(z >= s)
        def _():
            b = me - 4 * s
            self.arrived(b, k, (self.us, self.ur), s).wait_recv()

            @pl.when(self.crosses(k, s))
            def _():
                self.across(k, s, b, b).start()

            @pl.when(z < NZ - 1)
            def _():
                self.up(k, s, b).start()

            self.over(k, s, b, b).start()

        @pl.when(z + s <= NZ - 1)
        def _():
            b = me + 4 * s
            self.arrived(b, k, (self.ds, self.dr), s).wait_recv()

            @pl.when(self.crosses(k, 3 + s))
            def _():
                self.across(k, 3 + s, b, b).start()

            @pl.when(z > 0)
            def _():
                self.down(k, s, b).start()

            self.over(k, 3 + s, b, b).start()

    def line_b(self, k, s):
        z = self.z

        @pl.when(z == s)
        def _():
            b = self.side - 4 * s
            self.arrived(b, k, (self.bus, self.bur), s).wait_recv()

            @pl.when(z < NZ - 1)
            def _():
                self.up_b(k, s).start()

            self.over(k, 7 + s, b, b).start()

        @pl.when(z + s == NZ - 1)
        def _():
            b = self.side + 4 * s
            self.arrived(b, k, (self.bds, self.bdr), s).wait_recv()

            @pl.when(z > 0)
            def _():
                self.down_b(k, s).start()

            self.over(k, 10 + s, b, b).start()

    def from_side(self, k, slot):
        @pl.when(self.crosses(k, slot))
        def _():
            b = self.shift(self.side, slot)
            self.across(k, slot, b, b).wait_recv()
            if slot == 0 and self.alt(k):
                @pl.when(self.z == 0)
                def _():
                    self.up_b(k, 0).start()

                @pl.when(self.z == NZ - 1)
                def _():
                    self.down_b(k, 0).start()

            self.over(k, 7 + slot, b, b).start()

    def round(self, s, ks=None):
        if s < NZ:
            for k in self.order(ks):
                self.line(k, s)
        for k in self.order(ks):
            for slot in ((0,) if s == 1 else (s - 1, s + 2)):
                self.from_side(k, slot)
        if s > 1:
            for k in self.order(ks):
                if self.alt(k):
                    self.line_b(k, s - 1)

    def landed(self, ks=None):
        for k in self.order(ks):
            for slot in range(14):
                @pl.when(self.has(slot))
                def _():
                    b = self.core_block(slot)
                    self.over(k, slot, b, b).wait_recv()

    def finish(self, landed=True):
        z = self.z
        if landed:
            self.kept().wait()
            self.landed()
        for k in self.order():
            for slot in range(14):
                @pl.when(self.has(slot))
                def _():
                    b = self.core_block(slot)
                    self.over(k, slot, b, b).wait_send()
            for slot in range(7):
                @pl.when(self.crosses(k, slot))
                def _():
                    self.across(k, slot, self.me).wait_send()
            for s in range(NZ - 1):
                @pl.when((z >= s) & (z < NZ - 1))
                def _():
                    self.up(k, s).wait_send()

                @pl.when((z + s <= NZ - 1) & (z > 0))
                def _():
                    self.down(k, s).wait_send()

                if self.alt(k):
                    @pl.when(z == s)
                    def _():
                        self.up_b(k, s).wait_send()

                    @pl.when(z + s == NZ - 1)
                    def _():
                        self.down_b(k, s).wait_send()


def gather_kernel(chunks, dp, span, extra, x_ref, *refs):
    job = None
    ng = Gather.COUNT
    if not extra:
        o_ref, *sems = refs
    else:
        src, o_ref, out, *sems = refs
        job = side_job(dp, span, src, out, sems[ng:])
    g = Gather(x_ref, o_ref, chunks, sems[:ng])
    enter(g.me, g.z, g.core, g.side, 1 if job is None else dp)
    if job is not None:
        job.start()
    g.start()
    for s in range(1, NZ + 1):
        g.round(s)
    g.finish()
    if job is not None:
        job.finish()


COST = pl.CostEstimate(flops=0, bytes_accessed=4_000_000, transcendentals=0)
ANY = pl.BlockSpec(memory_space=pl.ANY)


def gather16(v, cid, chunks=2, dp=1, span=None, side=None):
    rows, width = v.shape
    extra = side is not None
    out = pl.pallas_call(
        functools.partial(gather_kernel, chunks, dp, span, extra),
        out_shape=(jax.ShapeDtypeStruct((NE, rows, width), v.dtype),)
        + ((side_shape(dp, span, side),) if extra else ()),
        in_specs=[ANY] * (2 if extra else 1),
        out_specs=(ANY,) * (2 if extra else 1),
        scratch_shapes=Gather.scratch(chunks) + (side_scratch(dp, span) if extra else []),
        compiler_params=pltpu.CompilerParams(collective_id=cid, has_side_effects=True),
        cost_estimate=COST,
        name="gather16",
    )(*((v, side) if extra else (v,)))
    return out if extra else out[0]


def opening_kernel(dp, chunks, x_ref, small_ref, parts_ref, out_ref,
                   x_all, small_all, parts_head, out_head, small_dp, out_dp, *sems):
    ng = Gather.COUNT
    gx = Gather(x_ref, x_all, chunks, sems[:ng])
    gs = Gather(small_dp, small_all, 1, sems[ng:2 * ng], lambda ref, b: ref.at[:, b])
    loc, ys, yr, ps, pr, os_, or_, pl_sem, ol_sem = sems[2 * ng:]
    me = gx.me
    plane = lax.axis_index("dp")
    enter_all(me, plane, dp)
    pairs = ((small_ref, small_dp), (out_ref, out_dp), (parts_head.at[plane], parts_head))

    def lift(i, r):
        src, dst = pairs[i]
        return pltpu.make_async_remote_copy(
            src_ref=src, dst_ref=dst.at[plane], send_sem=ys.at[i, r], recv_sem=yr.at[i, r],
            device_id={"dp": (plane + r) % dp}, device_id_type=MESH)

    def landed(i, r):
        p = (plane - r + dp) % dp
        dst = pairs[i][1].at[p]
        return pltpu.make_async_remote_copy(
            src_ref=dst, dst_ref=dst, send_sem=ys.at[i, r], recv_sem=yr.at[i, r],
            device_id={"dp": p}, device_id_type=MESH)

    def kept(i):
        src, dst = pairs[i]
        return pltpu.make_async_copy(src, dst.at[plane], loc.at[i])

    def part(r):
        h = (me + r) % NE
        return pltpu.make_async_remote_copy(
            src_ref=parts_ref.at[h], dst_ref=parts_head.at[plane, me],
            send_sem=ps.at[r], recv_sem=pr.at[r],
            device_id={"expert": h}, device_id_type=MESH)

    def part_in(r):
        e = (me - r + NE) % NE
        return pltpu.make_async_remote_copy(
            src_ref=parts_head.at[plane, e], dst_ref=parts_head.at[plane, e],
            send_sem=ps.at[r], recv_sem=pr.at[r],
            device_id={"expert": e}, device_id_type=MESH)

    def part_kept():
        return pltpu.make_async_copy(parts_ref.at[me], parts_head.at[plane, me], pl_sem)

    for i in range(2):
        for r in range(1, dp):
            lift(i, r).start()
        kept(i).start()
    gx.start()
    for r in range(1, NE):
        part(r).start()
    part_kept().start()
    gx.round(1)

    kept(0).wait()
    for r in range(1, dp):
        landed(0, r).wait_recv()
    gs.start()

    for r in range(1, NE):
        part_in(r).wait_recv()
    part_kept().wait()
    for r in range(1, dp):
        lift(2, r).start()
    gx.round(2)

    def row(d):
        b = NE * d + me
        return pltpu.make_async_remote_copy(
            src_ref=out_dp.at[d], dst_ref=out_head.at[b % dp],
            send_sem=os_.at[d], recv_sem=or_.at[b % dp],
            device_id={"expert": b // dp}, device_id_type=MESH)

    def row_kept(d):
        b = NE * d + me
        return pltpu.make_async_copy(out_dp.at[d], out_head.at[b % dp], ol_sem.at[d])

    kept(1).wait()
    for r in range(1, dp):
        landed(1, r).wait_recv()
    for d in range(dp):
        home = (NE * d + me) // dp

        @pl.when(home != me)
        def _():
            row(d).start()

        @pl.when(home == me)
        def _():
            row_kept(d).start()

    gs.round(1)
    gx.round(3)
    gs.round(2)
    gx.round(4)
    gs.round(3)
    gs.round(4)

    def row_in(j):
        return pltpu.make_async_remote_copy(
            src_ref=out_head.at[j], dst_ref=out_head.at[j], send_sem=os_.at[j], recv_sem=or_.at[j],
            device_id={"expert": gx.core}, device_id_type=MESH)

    for r in range(1, NE):
        part(r).wait_send()
    for j in range(dp):
        @pl.when((dp * me + j) % NE != me)
        def _():
            row_in(j).wait_recv()
    for d in range(dp):
        home = (NE * d + me) // dp

        @pl.when(home != me)
        def _():
            row(d).wait_send()

        @pl.when(home == me)
        def _():
            row_kept(d).wait()
    for r in range(1, dp):
        landed(2, r).wait_recv()
    for i in range(3):
        for r in range(1, dp):
            lift(i, r).wait_send()
    gx.finish()
    gs.finish()


def opening(dp, x, small, parts, out, cid, chunks=2):
    dma = pltpu.SemaphoreType.DMA
    rows, ws = small.shape
    bf = x.dtype
    wo = out.shape[1]
    shape = jax.ShapeDtypeStruct
    res = pl.pallas_call(
        functools.partial(opening_kernel, dp, chunks),
        out_shape=(
            shape((NE,) + x.shape, bf), shape((dp, NE, rows, ws), bf), shape((dp, NE) + parts.shape[1:], bf),
            shape((dp, rows, wo), bf),
            shape((dp, rows, ws), bf), shape((dp, rows, wo), bf),
        ),
        in_specs=[ANY] * 4,
        out_specs=[ANY] * 6,
        scratch_shapes=Gather.scratch(chunks) + Gather.scratch(1) + [
            dma((2,)), dma((3, dp)), dma((3, dp)), dma((NE,)), dma((NE,)), dma((dp,)), dma((dp,)), dma, dma((dp,))],
        compiler_params=pltpu.CompilerParams(collective_id=cid, has_side_effects=True),
        cost_estimate=COST,
        name="opening",
    )(x, small, parts, out)
    return res[:4]


def order(z, i):
    a, b = (3, 2, 1, 0)[i], (3, 2, 0, 1)[i]
    return jnp.where(z == 0, a, jnp.where(z == 1, b, jnp.where(z == 2, 3 - b, 3 - a)))


class Scatter:
    COUNT = 14

    def __init__(self, p_ref, o_ref, chunks, scratch):
        self.p, self.o, self.chunks = p_ref, o_ref, chunks
        (self.cbuf, self.own, self.xbuf, self.ubuf, self.dbuf, self.ld, self.cs, self.cr, self.xs, self.xr,
         self.us, self.ur, self.ds, self.dr) = scratch
        self.rows = o_ref.shape[0] // chunks
        self.me, self.z, self.x, self.c, self.core, self.side = place()

    @staticmethod
    def scratch(rows, width, chunks, bf):
        dma = pltpu.SemaphoreType.DMA
        return [pltpu.VMEM((n, rows, width), bf) for n in (8, 8, 4, 4, 4)] + [
            dma((8, chunks)), dma((8, chunks)), dma((8, chunks))] + [dma((4, chunks))] * 6

    def rng(self, k):
        return pl.ds(k * self.rows, self.rows)

    def column(self, i, j):
        return 4 * order(self.z, i) + 2 * jnp.where(j == 0, 1 - self.x, self.x)

    def remote(self, src, dst, send, recv, to):
        return pltpu.make_async_remote_copy(
            src_ref=src, dst_ref=dst, send_sem=send, recv_sem=recv,
            device_id={"expert": to}, device_id_type=MESH)

    def over(self, i, j, k):
        n = 2 * i + j
        return self.remote(
            self.p.at[self.column(i, j) + 1 - self.c, self.rng(k)], self.cbuf.at[n, self.rng(k)],
            self.cs.at[n, k], self.cr.at[n, k], self.core)

    def load(self, i, j, k):
        n = 2 * i + j
        return pltpu.make_async_copy(
            self.p.at[self.column(i, j) + self.c, self.rng(k)], self.own.at[n, self.rng(k)], self.ld.at[n, k])

    def which(self, ks):
        return range(self.chunks) if ks is None else ks

    def across(self, i, k):
        return self.remote(self.own.at[2 * i, self.rng(k)], self.xbuf.at[i, self.rng(k)],
                           self.xs.at[i, k], self.xr.at[i, k], self.side)

    def up(self, t, i, k):
        return self.remote(self.own.at[2 * i + 1, self.rng(k)], self.ubuf.at[t, self.rng(k)],
                           self.us.at[t, k], self.ur.at[t, k], self.me + 4)

    def down(self, t, i, k):
        return self.remote(self.own.at[2 * i + 1, self.rng(k)], self.dbuf.at[t, self.rng(k)],
                           self.ds.at[t, k], self.dr.at[t, k], self.me - 4)

    def start(self, ks=None):
        for i in range(NZ):
            for j in range(2):
                for k in self.which(ks):
                    self.load(i, j, k).start()
                    self.over(i, j, k).start()

    def first(self, i, ks=None):
        f32 = jnp.float32
        for k in self.which(ks):
            self.load(i, 0, k).wait()
            self.over(i, 0, k).wait_recv()
            s = self.rng(k)
            self.own[2 * i, s] = (
                self.own[2 * i, s].astype(f32) + self.cbuf[2 * i, s].astype(f32)).astype(self.own.dtype)
            self.across(i, k).start()

    def second(self, i, ks=None):
        f32 = jnp.float32
        z, own, o = self.z, self.own, self.o
        t = order(z, i)
        for k in self.which(ks):
            self.load(i, 1, k).wait()
            s = self.rng(k)
            self.over(i, 1, k).wait_recv()
            self.across(i, k).wait_recv()

            def base():
                return (own[2 * i + 1, s].astype(f32) + self.cbuf[2 * i + 1, s].astype(f32)
                        + self.xbuf[i, s].astype(f32))

            if i < NZ - 1:
                @pl.when(t > z)
                def _():
                    @pl.when(z > 0)
                    def _():
                        self.up(t, i, k).wait_recv()
                        own[2 * i + 1, s] = (base() + self.ubuf[t, s].astype(f32)).astype(own.dtype)

                    @pl.when(z == 0)
                    def _():
                        own[2 * i + 1, s] = base().astype(own.dtype)

                    self.up(t, i, k).start()

                @pl.when(t < z)
                def _():
                    @pl.when(z < NZ - 1)
                    def _():
                        self.down(t, i, k).wait_recv()
                        own[2 * i + 1, s] = (base() + self.dbuf[t, s].astype(f32)).astype(own.dtype)

                    @pl.when(z == NZ - 1)
                    def _():
                        own[2 * i + 1, s] = base().astype(own.dtype)

                    self.down(t, i, k).start()
            else:
                @pl.when(z > 0)
                def _():
                    self.up(t, i, k).wait_recv()

                @pl.when(z < NZ - 1)
                def _():
                    self.down(t, i, k).wait_recv()

                @pl.when((z > 0) & (z < NZ - 1))
                def _():
                    o[s] = (base() + self.ubuf[t, s].astype(f32) + self.dbuf[t, s].astype(f32)).astype(o.dtype)

                @pl.when(z == 0)
                def _():
                    o[s] = (base() + self.dbuf[t, s].astype(f32)).astype(o.dtype)

                @pl.when(z == NZ - 1)
                def _():
                    o[s] = (base() + self.ubuf[t, s].astype(f32)).astype(o.dtype)

    def run(self, between=lambda: None):
        self.first(0)
        for i in range(NZ):
            if i + 1 < NZ:
                self.first(i + 1)
            between()
            self.second(i)
            between()

    def finish(self):
        z = self.z
        for k in range(self.chunks):
            for i in range(NZ):
                self.across(i, k).wait_send()
                for j in range(2):
                    self.over(i, j, k).wait_send()
                if i < NZ - 1:
                    t = order(z, i)

                    @pl.when(t > z)
                    def _():
                        self.up(t, i, k).wait_send()

                    @pl.when(t < z)
                    def _():
                        self.down(t, i, k).wait_send()


def scatter_kernel(chunks, dp, span, extra, p_ref, *refs):
    job = None
    ns = Scatter.COUNT
    if not extra:
        o_ref, *scratch = refs
    else:
        src, o_ref, out, *scratch = refs
        job = side_job(dp, span, src, out, scratch[ns:])
    s = Scatter(p_ref, o_ref, chunks, scratch[:ns])
    enter(s.me, s.z, s.core, s.side, 1 if job is None else dp)
    if job is not None:
        job.start()
    s.start()
    s.run()
    s.finish()
    if job is not None:
        job.finish()


VMEM = pl.BlockSpec(memory_space=pltpu.VMEM)


def scatter16(p, cid, chunks=2, dp=1, span=None, side=None):
    _, rows, width = p.shape
    extra = side is not None
    out = pl.pallas_call(
        functools.partial(scatter_kernel, chunks, dp, span, extra),
        out_shape=(jax.ShapeDtypeStruct((rows, width), jnp.float32),)
        + ((side_shape(dp, span, side),) if extra else ()),
        in_specs=[ANY] * (2 if extra else 1),
        out_specs=(VMEM,) + ((ANY,) if extra else ()),
        scratch_shapes=Scatter.scratch(rows, width, chunks, p.dtype) + (side_scratch(dp, span) if extra else []),
        compiler_params=pltpu.CompilerParams(
            collective_id=cid, has_side_effects=True, vmem_limit_bytes=60 * 1024 * 1024),
        cost_estimate=COST,
        name="scatter16",
    )(*((p, side) if extra else (p,)))
    return out if extra else out[0]


def return_kernel(dp, chunks, p_ref, parts_ref, rows_ref, o_ref, parts_far, rows_far, *scratch):
    ns = Scatter.COUNT
    s = Scatter(p_ref, o_ref, chunks, scratch[:ns])
    swap = Swap(dp, parts_ref, parts_far, scratch[ns:ns + 2])
    rs, rr = scratch[ns + 2:]
    plane = lax.axis_index("dp")
    keeper = s.me * dp // NE
    enter(s.me, s.z, s.core, s.side, dp)

    def row(r):
        return pltpu.make_async_remote_copy(
            src_ref=rows_ref, dst_ref=rows_far.at[r - 1], send_sem=rs.at[r], recv_sem=rr.at[r],
            device_id={"dp": (plane + r) % dp}, device_id_type=MESH)

    swap.start()
    for r in range(1, dp):
        @pl.when((plane + r) % dp == keeper)
        def _():
            row(r).start()
    s.start()
    s.run()
    s.finish()
    swap.finish()
    for r in range(1, dp):
        @pl.when((plane + r) % dp == keeper)
        def _():
            row(r).wait_send()

        @pl.when(plane == keeper)
        def _():
            row(r).wait_recv()


def returning(dp, p, parts, rows, cid, chunks=2):
    dma = pltpu.SemaphoreType.DMA
    _, n, width = p.shape
    shape = jax.ShapeDtypeStruct
    return pl.pallas_call(
        functools.partial(return_kernel, dp, chunks),
        out_shape=(
            shape((n, width), jnp.float32), shape((dp - 1,) + parts.shape[1:], parts.dtype),
            shape((dp - 1,) + rows.shape, rows.dtype)),
        in_specs=[ANY] * 3,
        out_specs=[VMEM, ANY, ANY],
        scratch_shapes=Scatter.scratch(n, width, chunks, p.dtype) + [dma((dp,))] * 4,
        compiler_params=pltpu.CompilerParams(
            collective_id=cid, has_side_effects=True, vmem_limit_bytes=60 * 1024 * 1024),
        cost_estimate=COST,
        name="returning",
    )(p, parts, rows)


def closing_kernel(dp, p_ref, parts_ref, rows_ref, o_ref, far_ref, query_ref, expand_ref, output_ref,
                   parts_in, row_in, *scratch):
    ns = Scatter.COUNT
    s = Scatter(p_ref, o_ref, 1, scratch[:ns])
    ys, yr, ps, pr, kept_sem, rs, rr = scratch[ns:]
    me = s.me
    plane = lax.axis_index("dp")
    rows = o_ref.shape[0] // dp
    enter_all(me, plane, dp)

    def lift(r):
        to = (plane + r) % dp
        return pltpu.make_async_remote_copy(
            src_ref=o_ref.at[pl.ds(pl.multiple_of(to * rows, 16), rows)], dst_ref=far_ref.at[r - 1],
            send_sem=ys.at[r], recv_sem=yr.at[r],
            device_id={"dp": to}, device_id_type=MESH)

    def part(r):
        e = (me + r) % NE
        return pltpu.make_async_remote_copy(
            src_ref=parts_ref.at[e], dst_ref=parts_in.at[me], send_sem=ps.at[r], recv_sem=pr.at[r],
            device_id={"expert": e}, device_id_type=MESH)

    def part_in(r):
        h = (me - r + NE) % NE
        return pltpu.make_async_remote_copy(
            src_ref=parts_in.at[h], dst_ref=parts_in.at[h], send_sem=ps.at[r], recv_sem=pr.at[r],
            device_id={"expert": h}, device_id_type=MESH)

    def part_kept():
        return pltpu.make_async_copy(parts_ref.at[me], parts_in.at[me], kept_sem.at[0])

    keeper = plane == me * dp // NE
    source = (NE * plane + me) // dp

    def row(j):
        return pltpu.make_async_remote_copy(
            src_ref=rows_ref.at[j], dst_ref=row_in, send_sem=rs.at[j], recv_sem=rr,
            device_id={"expert": (dp * me + j) % NE}, device_id_type=MESH)

    def row_kept(j):
        return pltpu.make_async_copy(rows_ref.at[j], row_in, kept_sem.at[1])

    s.start()
    for i in range(NZ):
        s.first(i)
    for r in range(1, NE):
        part(r).start()
    part_kept().start()
    for j in range(dp):
        home = (dp * me + j) % NE

        @pl.when(keeper & (home != me))
        def _():
            row(j).start()

        @pl.when(keeper & (home == me))
        def _():
            row_kept(j).start()
    for i in range(NZ):
        s.second(i)
    for r in range(1, dp):
        lift(r).start()
    for r in range(1, NE):
        part_in(r).wait_recv()
    part_kept().wait()
    rows_l = expand_ref.shape[0]
    f32 = jnp.float32
    for h in range(0, NE, 2):
        pair = [parts_in[h + i].astype(f32) for i in range(2)]
        query_ref[:, h * 192:(h + 2) * 192] = jnp.concatenate([v[:, :192] for v in pair], axis=1)
        for i, v in enumerate(pair):
            expand_ref[:, (h + i) * 256:(h + i + 1) * 256] = jnp.concatenate(
                [v[c * rows_l:(c + 1) * rows_l, 192:] for c in range(4)], axis=1)

    @pl.when(source != me)
    def _():
        row(0).wait_recv()

    for j in range(dp):
        home = (dp * me + j) % NE

        @pl.when(keeper & (home != me))
        def _():
            row(j).wait_send()

        @pl.when(keeper & (home == me))
        def _():
            row_kept(j).wait()
    output_ref[...] = row_in[...].astype(f32)
    for r in range(1, NE):
        part(r).wait_send()
    s.finish()
    for r in range(1, dp):
        lift(r).wait_recv()
        lift(r).wait_send()


def closing(dp, p, parts, rows, rows_l, cid):
    dma = pltpu.SemaphoreType.DMA
    _, n, width = p.shape
    shape = jax.ShapeDtypeStruct
    rows_w = parts.shape[1]
    near, far, query, expand, output = pl.pallas_call(
        functools.partial(closing_kernel, dp),
        out_shape=(
            shape((n, width), p.dtype), shape((dp - 1, n // dp, width), p.dtype),
            shape((rows_w, NE * 192), jnp.float32), shape((rows_l, NE * 256), jnp.float32),
            shape(rows.shape[1:], jnp.float32)),
        in_specs=[ANY] * 3,
        out_specs=[VMEM] * 5,
        scratch_shapes=[pltpu.VMEM(parts.shape, parts.dtype), pltpu.VMEM(rows.shape[1:], rows.dtype)]
        + Scatter.scratch(n, width, 1, p.dtype)
        + [dma((dp,)), dma((dp,)), dma((NE,)), dma((NE,)), dma((2,)), dma((dp,)), dma],
        compiler_params=pltpu.CompilerParams(
            collective_id=cid, has_side_effects=True, vmem_limit_bytes=60 * 1024 * 1024),
        cost_estimate=COST,
        name="closing",
    )(p, parts, rows)
    own = lax.dynamic_slice_in_dim(near, lax.axis_index("dp") * (n // dp), n // dp).astype(jnp.float32)
    return own + jnp.sum(far.astype(jnp.float32), axis=0), query, expand, output
BF = jnp.bfloat16
F32 = jnp.float32


def mm(a, b):
    return jnp.dot(a, b, preferred_element_type=F32)


def mm_t(a, b):
    return lax.dot_general(a, b, (((1,), (1,)), ((), ())), preferred_element_type=F32)


def silu_pair(gate_in):
    sigmoid = 1.0 / (1.0 + jnp.exp(-gate_in))
    return (gate_in * sigmoid, sigmoid * (1.0 + gate_in * (1.0 - sigmoid)))


TILE = 256
WIDE = 512
SHARE = 176


def down_copies(parts, out, sem, which):
    dp = parts[0].shape[0]
    sizes = [part.shape[1] for part in parts]
    rows, first = sum(sizes), sum(sizes[:which])
    return [
        pltpu.make_async_copy(
            parts[which].at[d], out.at[pl.ds(d * rows + first, sizes[which])], sem.at[len(parts) * d + which])
        for d in range(dp)
    ]


def share_copies(share_ref, fan, down, sem):
    dp, rows, w = share_ref.shape
    n = rows // 3
    copies = []
    for d in range(dp):
        cols = pl.ds(d * w, w)
        for i, (dst, first) in enumerate(((fan, 0), (fan, TILE), (down, 0))):
            copies.append(pltpu.make_async_copy(
                share_ref.at[d, pl.ds(i * n, n)], dst.at[pl.ds(first, n), cols], sem.at[3 * d + i]))
    return copies


def share_blank(fan, down):
    pad = jnp.zeros((TILE - SHARE, fan.shape[1]), BF)
    fan[SHARE:TILE] = pad
    fan[TILE + SHARE:] = pad
    down[SHARE:] = pad


def valid_of(len_ref, first_device, tokens, batches, here):
    n = lax.broadcasted_iota(jnp.int32, (tokens, 1), 0)
    if here & (here - 1) or batches & (batches - 1):
        device, batch, place_in = n // (batches * here), (n // here) % batches, n % here
    else:
        bits, more = here.bit_length() - 1, (batches * here).bit_length() - 1
        device, batch, place_in = n >> more, (n >> bits) & (batches - 1), n & (here - 1)
    position = (first_device + device) * here + place_in
    length = jnp.zeros((tokens, 1), jnp.int32)
    for b in range(batches):
        length = jnp.where(batch == b, len_ref[b], length)
    return (position < length).astype(F32)


def slot_tables(here, slots=128):
    n = np.arange(256)
    same = n[:, None] // here == n[None, :] // here
    before = same & (n[None, :] < n[:, None])
    tables = np.stack([before, before.T, np.eye(256, dtype=bool)]).astype(np.float32)
    base = np.broadcast_to((n // here * 32)[:, None], (256, slots)).astype(np.float32)
    return jnp.asarray(tables, BF), jnp.asarray(base), jnp.asarray(base.T)


def one_hots(taken, tables, base_c, base_r, groups, slots):
    lane = lax.broadcasted_iota(jnp.int32, (256, slots), 1).astype(F32)
    row = lax.broadcasted_iota(jnp.int32, (slots, 256), 0).astype(F32)
    to_slot, to_token = [], []
    for g in range(groups):
        t = jnp.broadcast_to(taken[g * 256:(g + 1) * 256], (256, slots))
        low = t.astype(BF)
        place_c = mm(tables[0], low) + base_c[...]
        place_r = mm_lead(low, tables[1]) + base_r[...]
        taken_r = mm_lead(low, tables[2])
        to_token.append(jnp.where((place_c == lane) & (t > 0.5), 1.0, 0.0).astype(BF))
        to_slot.append(jnp.where((place_r == row) & (taken_r > 0.5), 1.0, 0.0).astype(BF))
    return to_slot, to_token


def mm_lead(a, b):
    return lax.dot_general(a, b, (((0,), (0,)), ((), ())), preferred_element_type=F32)


def lanes(j):
    return pl.ds(pl.multiple_of(j * WIDE, WIDE), WIDE)


def over_columns(total, body):
    def step(j, _):
        body(pl.multiple_of(j * WIDE, WIDE), WIDE)
        return 0

    lax.fori_loop(0, total // WIDE, step, 0)
    if total % WIDE:
        body(total // WIDE * WIDE, total % WIDE)


def forward_kernel(chunks, dp, span, batches, here, len_ref, pick_ref, mix_ref, mask_ref, tab_ref, basec_ref, baser_ref, wg_ref, wu_ref, router_ref,
                   share_ref, wda_ref, wdb_ref, down_ref, dy_ref,
                   out_ref, rows_ref, hid_ref, act_ref, slo_ref, eo_ref, sh_ref, sact_ref, sslo_ref, gate_ref,
                   slot_ref, token_ref, dy_all, wdc_ref,
                   wd_ref, fan_ref, sd_ref, hid_buf, sh_buf, gate_buf, token_buf, wd_sem, sh_sem, *sems):
    step = pl.program_id(0)
    tokens, width = mix_ref.shape
    groups, slots = tokens // 256, 128
    half = groups * slots
    ff = hid_ref.shape[1]
    phase = pl.num_programs(0) // 2
    g = Gather(dy_ref, dy_all, chunks, sems[:Gather.COUNT])
    job = side_job(dp, span, down_ref, wdc_ref, sems[Gather.COUNT:])
    parts = (wda_ref, wdb_ref, wdc_ref)

    @pl.when(step == 0)
    def _():
        enter(g.me, g.z, g.core, g.side, dp)
        job.start()
        g.start()
        copies = share_copies(share_ref, fan_ref, sd_ref, sh_sem)
        for copy in copies + down_copies(parts, wd_ref, wd_sem, 0) + down_copies(parts, wd_ref, wd_sem, 1):
            copy.start()
        share_blank(fan_ref, sd_ref)
        fan_ref[SHARE:SHARE + 16] = router_ref[...]
        for copy in copies:
            copy.wait()

    @pl.when(step < phase)
    def _():
        mix = mix_ref[...]
        fanned = mm_t(mix, fan_ref[:TILE, :])
        s_up = mm_t(mix, fan_ref[TILE:, :])
        s_act, s_slope = silu_pair(fanned)
        s_hidden = (s_act * s_up).astype(BF)
        at = pl.ds(pl.multiple_of(step * tokens, tokens), tokens)
        sh_ref[...] = s_hidden
        sh_buf[at] = s_hidden
        sact_ref[...] = s_act.astype(BF)
        sslo_ref[...] = (s_up * s_slope).astype(BF)
        logits = fanned[:, SHARE:SHARE + 16]
        mask = mask_ref[...].astype(F32)
        taken = jnp.sum(mask * pick_ref[:, :16], axis=1, keepdims=True) * valid_of(len_ref, step * (tokens // (batches * here)), tokens, batches, here)
        held = jnp.where(mask > 0.5, logits, -1e30)
        raised = jnp.exp(held - jnp.max(held, axis=1, keepdims=True)) * mask
        gate = jnp.sum(raised * pick_ref[:, :16], axis=1, keepdims=True) / jnp.sum(raised, axis=1, keepdims=True) * taken
        gate_ref[...] = gate
        gate_buf[at] = gate
        to_slot, to_token = one_hots(taken, tab_ref, basec_ref, baser_ref, groups, slots)
        for n in range(groups):
            slot_ref[n * slots:(n + 1) * slots] = to_slot[n]
            token_ref[n * 256:(n + 1) * 256] = to_token[n]
            token_buf[pl.ds(pl.multiple_of(step * tokens + n * 256, 256), 256)] = to_token[n]

        def dispatch(j, _):
            for n in range(groups):
                rows_ref[n * slots:(n + 1) * slots, lanes(j)] = mm(
                    to_slot[n], mix_ref[n * 256:(n + 1) * 256, lanes(j)]).astype(BF)
            return 0

        lax.fori_loop(0, width // WIDE, dispatch, 0)
        rows_at = pl.ds(pl.multiple_of(step * half, half), half)

        def fan_in(start, size):
            cols = pl.ds(start, size)
            gate_in = mm(rows_ref[...], wg_ref[:, cols])
            up_in = mm(rows_ref[...], wu_ref[:, cols])
            act, slope = silu_pair(gate_in)
            hidden = (act * up_in).astype(BF)
            hid_ref[:, cols] = hidden
            hid_buf[rows_at, cols] = hidden
            act_ref[:, cols] = act.astype(BF)
            slo_ref[:, cols] = (up_in * slope).astype(BF)

        over_columns(ff, fan_in)

    @pl.when(step == phase)
    def _():
        job.finish()
        for copy in down_copies(parts, wd_ref, wd_sem, 2):
            copy.start()
        for which in range(3):
            for copy in down_copies(parts, wd_ref, wd_sem, which):
                copy.wait()

    @pl.when(step >= phase)
    def _():
        tile = step - phase
        at = pl.ds(pl.multiple_of(tile * tokens, tokens), tokens)
        rows_at = pl.ds(pl.multiple_of(tile * half, half), half)
        gate = gate_buf[at]
        s_hidden = sh_buf[at]
        to_token = [token_buf[pl.ds(pl.multiple_of(tile * tokens + n * 256, 256), 256)] for n in range(groups)]

        def fan_out(j, _):
            eo = mm(hid_buf[rows_at], wd_ref[:, lanes(j)]).astype(BF)
            eo_ref[:, lanes(j)] = eo
            shared = mm(s_hidden, sd_ref[:, lanes(j)])
            picked = jnp.concatenate(
                [mm(to_token[n], eo[n * slots:(n + 1) * slots]) for n in range(groups)], axis=0)
            out_ref[:, lanes(j)] = (shared + gate * picked).astype(BF)
            return 0

        lax.fori_loop(0, width // WIDE, fan_out, 0)

    for r, s in ((1, 1), (2, 3), (3, 5), (4, 7)):
        @pl.when(step == s)
        def _():
            g.round(r)

    @pl.when(step == 2 * phase - 1)
    def _():
        g.finish()


def backward_kernel(chunks, pick_ref, dy_ref, wg_ref, wu_ref, share_ref, wda_ref, wdb_ref, wdc_ref,
                    act_ref, slo_ref, eo_ref, sact_ref, sslo_ref, gate_ref, slot_ref, token_ref, part_ref,
                    dh_ref, deo_ref, dg_ref, du_ref, ds_ref, sum_ref,
                    wd_ref, fan_ref, sd_ref, wd_sem, sh_sem, *scratch):
    step = pl.program_id(0)
    tokens, width = dy_ref.shape
    groups, slots = tokens // 256, 128
    ff = dg_ref.shape[1]
    sc = Scatter(part_ref, sum_ref, chunks, scratch)

    @pl.when(step == 0)
    def _():
        enter(sc.me, sc.z, sc.core, sc.side)
        copies = share_copies(share_ref, fan_ref, sd_ref, sh_sem)
        for which in range(3):
            copies += down_copies((wda_ref, wdb_ref, wdc_ref), wd_ref, wd_sem, which)
        for copy in copies:
            copy.start()
        sc.start()
        share_blank(fan_ref, sd_ref)
        for copy in copies:
            copy.wait()

    d_sh = mm_t(dy_ref[...], sd_ref[...])
    d_s = jnp.concatenate([(d_sh * sslo_ref[...].astype(F32)).astype(BF),
                           (d_sh * sact_ref[...].astype(F32)).astype(BF)], axis=1)
    ds_ref[...] = d_s
    gate = gate_ref[...]
    to_slot = [slot_ref[n * slots:(n + 1) * slots] for n in range(groups)]
    to_token = [token_ref[n * 256:(n + 1) * 256] for n in range(groups)]

    @pl.when(step == 0)
    def _():
        sc.first(0)
        sc.first(1)

    def dispatch(j, total):
        dy = dy_ref[:, lanes(j)].astype(F32)
        gated = (gate * dy).astype(BF)
        for n in range(groups):
            deo_ref[n * slots:(n + 1) * slots, lanes(j)] = mm(to_slot[n], gated[n * 256:(n + 1) * 256]).astype(BF)
        picked = jnp.concatenate(
            [mm(to_token[n], eo_ref[n * slots:(n + 1) * slots, lanes(j)]) for n in range(groups)], axis=0)
        return total + jnp.sum(dy * picked, axis=1, keepdims=True)

    d_gates = lax.fori_loop(0, width // WIDE, dispatch, jnp.zeros((tokens, 1), F32))

    def back_out(start, size):
        cols = pl.ds(start, size)
        d_eh = mm_t(deo_ref[...], wd_ref[cols, :])
        dg_ref[:, cols] = (d_eh * slo_ref[:, cols].astype(F32)).astype(BF)
        du_ref[:, cols] = (d_eh * act_ref[:, cols].astype(F32)).astype(BF)

    over_columns(ff, back_out)

    @pl.when(step == 0)
    def _():
        sc.first(2)
        sc.first(3)

    def back_in(j, _):
        d_rows = (mm_t(dg_ref[...], wg_ref[lanes(j), :]) + mm_t(du_ref[...], wu_ref[lanes(j), :])).astype(BF)
        shared = mm(d_s, fan_ref[:, lanes(j)])
        taken_rows = jnp.concatenate(
            [mm(to_token[n], d_rows[n * slots:(n + 1) * slots]) for n in range(groups)], axis=0)
        dh_ref[:, lanes(j)] = (shared + taken_rows).astype(BF)
        return 0

    lax.fori_loop(0, width // WIDE, back_in, 0)
    high = d_gates.astype(BF).astype(F32)
    dh_ref[:, width:] = (high * pick_ref[:, :128] + (d_gates - high) * pick_ref[:, 128:]).astype(BF)

    outer = (sc.z == 0) | (sc.z == NZ - 1)
    for i in range(NZ - 1):
        @pl.when((step == i) & outer)
        def _():
            sc.second(i)

        @pl.when((step == min(i + 1, 2)) & jnp.logical_not(outer))
        def _():
            sc.second(i)

    @pl.when(step == NZ - 1)
    def _():
        sc.second(NZ - 1)
        sc.finish()


def whole(v):
    zeros = (0,) * v.ndim
    return pl.BlockSpec(v.shape, lambda i: zeros, pipeline_mode=pl.Buffered(buffer_count=1))


def tiles(rows, w):
    return pl.BlockSpec((rows, w), lambda i: (i, 0))


SMEM = pl.BlockSpec(memory_space=pltpu.SMEM)


def mixture_forward(dp, batches, here, lengths, pick, mix, mask, wg, wu, router, share, wda, wdb, span, down, dy, cid,
                    chunks=2):
    total, width = mix.shape
    step, half = total // 4, total // 8
    ff = wg.shape[1]
    tables = slot_tables(here)
    shape = jax.ShapeDtypeStruct
    rows = total // 2
    dma = pltpu.SemaphoreType.DMA

    def early(n, w):
        return pl.BlockSpec((n, w), lambda i: (jnp.minimum(i, 3), 0))

    def late(n, w):
        return pl.BlockSpec((n, w), lambda i: (jnp.maximum(i - 4, 0), 0))

    return pl.pallas_call(
        functools.partial(forward_kernel, chunks, dp, span, batches, here),
        grid=(8,),
        out_shape=(
            shape((total, width), BF), shape((rows, width), BF), shape((rows, ff), BF), shape((rows, ff), BF),
            shape((rows, ff), BF), shape((rows, width), BF), shape((total, TILE), BF), shape((total, TILE), BF),
            shape((total, TILE), BF), shape((total, 1), F32), shape((rows, 256), BF), shape((total, 128), BF),
            shape((NE,) + dy.shape, BF),
            shape((dp, span[1], width), BF)),
        in_specs=[SMEM, whole(pick), early(step, width), early(step, mask.shape[1])] + [whole(v) for v in tables] + [whole(wg), whole(wu),
                  whole(router), ANY, ANY, ANY, ANY, ANY],
        out_specs=[late(step, width), early(half, width), early(half, ff), early(half, ff), early(half, ff),
                   late(half, width), early(step, TILE), early(step, TILE), early(step, TILE), early(step, 1),
                   early(half, 256), early(step, 128), ANY, ANY],
        scratch_shapes=[
            pltpu.VMEM((ff, width), BF), pltpu.VMEM((2 * TILE, width), BF), pltpu.VMEM((TILE, width), BF),
            pltpu.VMEM((rows, ff), BF), pltpu.VMEM((total, TILE), BF), pltpu.VMEM((total, 1), F32),
            pltpu.VMEM((total, 128), BF), dma((3 * dp,)), dma((3 * dp,))] + Gather.scratch(chunks) + Spread.scratch(dp),
        compiler_params=pltpu.CompilerParams(
            collective_id=cid, has_side_effects=True, vmem_limit_bytes=60 * 1024 * 1024),
        cost_estimate=COST,
        name="mixture_forward",
    )(lengths, pick, mix, mask, *tables, wg, wu, router, share, wda, wdb, down, dy)


def mixture_backward(pick, dy, wg, wu, share, wda, wdb, wdc, act, slo, eo, sact, sslo, gate, slot, token, part, cid, chunks=2):
    total, width = dy.shape
    step, half = total // NZ, total // NZ // 2
    ff = wg.shape[1]
    shape = jax.ShapeDtypeStruct
    rows = total // 2
    dp = wda.shape[0]
    _, own, _ = part.shape
    dma = pltpu.SemaphoreType.DMA
    return pl.pallas_call(
        functools.partial(backward_kernel, chunks),
        grid=(NZ,),
        out_shape=(
            shape((total, width + 128), BF), shape((rows, width), BF), shape((rows, ff), BF), shape((rows, ff), BF),
            shape((total, 2 * TILE), BF), shape((own, width), F32)),
        in_specs=[whole(pick), tiles(step, width), whole(wg), whole(wu), ANY, ANY, ANY, ANY,
                  tiles(half, ff), tiles(half, ff), tiles(half, width), tiles(step, TILE), tiles(step, TILE),
                  tiles(step, 1), tiles(half, 256), tiles(step, 128), ANY],
        out_specs=[tiles(step, width + 128), tiles(half, width), tiles(half, ff), tiles(half, ff),
                   tiles(step, 2 * TILE), pl.BlockSpec((own, width), lambda i: (0, 0))],
        scratch_shapes=[
            pltpu.VMEM((ff, width), BF), pltpu.VMEM((2 * TILE, width), BF), pltpu.VMEM((TILE, width), BF),
            dma((3 * dp,)), dma((3 * dp,))] + Scatter.scratch(own, width, chunks, BF),
        compiler_params=pltpu.CompilerParams(
            collective_id=cid, has_side_effects=True, vmem_limit_bytes=62 * 1024 * 1024),
        cost_estimate=COST,
        name="mixture_backward",
    )(pick, dy, wg, wu, share, wda, wdb, wdc, act, slo, eo, sact, sslo, gate, slot, token, part)


class ShareWork:
    ROWS = 256

    def __init__(self, ds_ref, sh_ref, mix_ref, dy_ref, out_ref, scratch):
        self.sources = (ds_ref, sh_ref, mix_ref, dy_ref)
        self.out = out_ref
        *self.buffers, self.gfan, self.gsd, self.sem = scratch
        self.steps = mix_ref.shape[0] // self.ROWS
        self.done = 0

    @staticmethod
    def scratch(width):
        r = ShareWork.ROWS
        return [pltpu.VMEM((2, r, w), BF) for w in (2 * TILE, TILE, width, width)] + [
            pltpu.VMEM((2 * TILE, width), F32), pltpu.VMEM((TILE, width), F32), pltpu.SemaphoreType.DMA((2, 4))]

    COUNT = 7

    def copies(self, n):
        return [pltpu.make_async_copy(src.at[pl.ds(n * self.ROWS, self.ROWS)], buf.at[n % 2], self.sem.at[n % 2, i])
                for i, (src, buf) in enumerate(zip(self.sources, self.buffers))]

    def start(self):
        for copy in self.copies(0):
            copy.start()
        self.gfan[...] = jnp.zeros_like(self.gfan)
        self.gsd[...] = jnp.zeros_like(self.gsd)

    def step(self):
        n = self.done
        if n == self.steps:
            return
        self.done += 1
        for copy in self.copies(n):
            copy.wait()
        if n + 1 < self.steps:
            for copy in self.copies(n + 1):
                copy.start()
        ds, sh, mix, dy = self.buffers

        def columns(j, _):
            self.gfan[:, lanes(j)] += mm_lead(ds[n % 2], mix[n % 2, :, lanes(j)])
            self.gsd[:, lanes(j)] += mm_lead(sh[n % 2], dy[n % 2, :, lanes(j)])
            return 0

        lax.fori_loop(0, mix.shape[2] // WIDE, columns, 0)

    def finish(self):
        while self.done < self.steps:
            self.step()
        dp, rows, w = self.out.shape
        n = rows // 3
        for d in range(dp):
            cols = slice(d * w, (d + 1) * w)
            self.out[d, :n] = self.gfan[:n, cols].astype(BF)
            self.out[d, n:2 * n] = self.gfan[TILE:TILE + n, cols].astype(BF)
            self.out[d, 2 * n:] = self.gsd[:n, cols].astype(BF)


class WeightWork:
    COUNT = 6
    ROWS = 256

    def __init__(self, lhs, rhs, outs, scratch):
        self.sources, self.outs = (lhs,) + tuple(rhs), outs
        *self.held, self.buf, self.in_sem, self.out_sem = scratch
        self.steps = lhs.shape[1] // self.ROWS

    @staticmethod
    def scratch(lhs, rhs):
        dma = pltpu.SemaphoreType.DMA
        return [pltpu.VMEM(v.shape, BF) for v in (lhs,) + tuple(rhs)] + [
            pltpu.VMEM((2, WeightWork.ROWS, rhs[0].shape[1]), BF), dma((3,)), dma((2,))]

    def loads(self):
        return [pltpu.make_async_copy(v, held, self.in_sem.at[i])
                for i, (v, held) in enumerate(zip(self.sources, self.held))]

    def start(self):
        for copy in self.loads():
            copy.start()

    def ready(self):
        for copy in self.loads():
            copy.wait()

    def store(self, p, n):
        at = pl.ds(pl.multiple_of(n * self.ROWS, self.ROWS), self.ROWS)
        return pltpu.make_async_copy(self.buf.at[p], self.outs[p].at[at], self.out_sem.at[p])

    def step(self, begin, end):
        def body(n, _):
            left = self.held[0][:, pl.ds(pl.multiple_of(n * self.ROWS, self.ROWS), self.ROWS)]
            for p in range(2):
                @pl.when(n > 0)
                def _():
                    self.store(p, n - 1).wait()

                rhs = self.held[1 + p]
                width = rhs.shape[1]
                for at in range(0, width, WIDE):
                    size = min(WIDE, width - at)
                    self.buf[p, :, at:at + size] = mm_lead(left, rhs[:, at:at + size]).astype(BF)
                self.store(p, n).start()
            return 0

        lax.fori_loop(begin, end, body, 0)

    def finish(self):
        for p in range(2):
            self.store(p, self.steps - 1).wait()


def scatter_share_kernel(chunks, dp, p_ref, ds_ref, sh_ref, mix_ref, dy_ref, rows_ref, dg_ref, du_ref, down_ref,
                         o_ref, g_ref, ggate_ref, gup_ref, far_ref, *scratch):
    ns, nw = Scatter.COUNT, ShareWork.COUNT
    s = Scatter(p_ref, o_ref, chunks, scratch[:ns])
    share = ShareWork(ds_ref, sh_ref, mix_ref, dy_ref, g_ref, scratch[ns:ns + nw])
    work = WeightWork(rows_ref, (dg_ref, du_ref), (ggate_ref, gup_ref), scratch[ns + nw:-2])
    swap = Swap(dp, down_ref, far_ref, scratch[-2:])
    enter(s.me, s.z, s.core, s.side, dp)
    swap.start()
    s.start()
    work.start()
    share.start()
    s.first(0)
    s.first(1)
    work.ready()
    third = work.steps // 3
    work.step(0, third)
    s.second(0)
    s.first(2)
    s.first(3)
    work.step(third, 2 * third)
    s.second(1)
    work.step(2 * third, work.steps)
    s.second(2)
    work.finish()
    while share.done < share.steps:
        share.step()
    s.second(3)
    share.finish()
    s.finish()
    swap.finish()


def scatter_share(p, ds, sh, mix, dy, rows, dg, du, down, share_shape, cid, chunks=2):
    _, n, width = p.shape
    shape = jax.ShapeDtypeStruct
    grad = shape((rows.shape[1], dg.shape[1]), BF)
    return pl.pallas_call(
        functools.partial(scatter_share_kernel, chunks, down.shape[0]),
        out_shape=(shape((n, width), F32), shape(share_shape, BF), grad, grad,
                   shape((down.shape[0] - 1,) + down.shape[1:], BF)),
        in_specs=[ANY] * 9,
        out_specs=(VMEM, VMEM, ANY, ANY, ANY),
        scratch_shapes=Scatter.scratch(n, width, chunks, p.dtype) + ShareWork.scratch(mix.shape[1])
        + WeightWork.scratch(rows, (dg, du)) + Swap.scratch(down.shape[0]),
        compiler_params=pltpu.CompilerParams(
            collective_id=cid, has_side_effects=True, vmem_limit_bytes=60 * 1024 * 1024),
        cost_estimate=COST,
        name="scatter_share",
    )(p, ds, sh, mix, dy, rows, dg, du, down)


def turn(v, cosine, sine):
    half = v.shape[1] // 2
    a, b = v[:, :half], v[:, half:]
    return jnp.concatenate([a * cosine - b * sine, b * cosine + a * sine], axis=1)


def project_kernel(x_ref, gain_ref, lgain_ref, wq_ref, wl_ref, we_ref, cos_ref, sin_ref,
                   h_ref, q_ref, k_ref, v_ref, lat_ref):
    blocks = x_ref.shape[0]
    batches, rows, _ = q_ref.shape
    here = rows // blocks
    x = x_ref[...].reshape(blocks * batches * here, x_ref.shape[2]).astype(F32)
    h = x * lax.rsqrt(jnp.mean(x * x, axis=1, keepdims=True) + 1e-6) * gain_ref[...]
    h = h.astype(BF)
    h_ref[...] = h
    raw = mm(h, wq_ref[...])
    raw_lat = mm(h, wl_ref[...])
    cosine, sine = cos_ref[...], sin_ref[...]
    zeros = jnp.zeros((raw.shape[0], 64), BF)
    q = jnp.concatenate([raw[:, :128].astype(BF), turn(raw[:, 128:192], cosine, sine).astype(BF), zeros], axis=1)
    k_rope = turn(raw_lat[:, 512:576], cosine, sine).astype(BF)
    lat = raw_lat[:, :512]
    lat = (lat * lax.rsqrt(jnp.mean(lat * lat, axis=1, keepdims=True) + 1e-6) * lgain_ref[...]).astype(BF)
    expanded = mm(lat, we_ref[...]).astype(BF)
    k = jnp.concatenate([expanded[:, :128], k_rope, zeros], axis=1)
    for e in range(blocks):
        for m in range(batches):
            src = slice((e * batches + m) * here, (e * batches + m + 1) * here)
            dst = slice(e * here, (e + 1) * here)
            q_ref[m, dst] = q[src]
            k_ref[m, dst] = k[src]
            v_ref[m, dst] = expanded[src, 128:]
            lat_ref[m, dst] = lat[src]


def project(x_all, gain, lgain, wq, wl, we, cosine, sine, batches):
    groups, rows, width = x_all.shape
    here = rows // batches
    per = 4
    seq = groups * here
    shape = jax.ShapeDtypeStruct

    def whole(v):
        return pl.BlockSpec(v.shape, lambda i: (0, 0))

    def by_seq(w):
        return pl.BlockSpec((batches, per * here, w), lambda i: (0, i, 0))

    table = pl.BlockSpec((per * rows, 32), lambda i: (i, 0))
    return pl.pallas_call(
        project_kernel,
        grid=(groups // per,),
        out_shape=(shape((groups * rows, width), BF), shape((batches, seq, 256), BF), shape((batches, seq, 256), BF),
                   shape((batches, seq, 128), BF), shape((batches, seq, 512), BF)),
        in_specs=[pl.BlockSpec((per, rows, width), lambda i: (i, 0, 0)), whole(gain), whole(lgain), whole(wq), whole(wl), whole(we),
                  table, table],
        out_specs=[pl.BlockSpec((per * rows, width), lambda i: (i, 0)), by_seq(256), by_seq(256), by_seq(128), by_seq(512)],
        compiler_params=pltpu.CompilerParams(vmem_limit_bytes=48 * 1024 * 1024),
        cost_estimate=pl.CostEstimate(flops=7_000_000_000, bytes_accessed=20_000_000, transcendentals=0),
        name="project",
    )(x_all, gain, lgain, wq, wl, we, cosine, sine)


ROWS = 256
SCALE = 192.0 ** -0.5


def held_scores(q, k, first, length):
    s = mm_t(q, k) * SCALE
    t = lax.broadcasted_iota(jnp.int32, s.shape, 0) + first
    u = lax.broadcasted_iota(jnp.int32, s.shape, 1)
    return jnp.where((u <= t) & (u < length), s, -1e30)


def attend_kernel(dp, span, len_ref, q_ref, k_ref, v_ref, wo_ref, side_ref, sum_ref, att_ref, lse_ref, side_out,
                  part, *scratch):
    m = pl.program_id(0)
    length = len_ref[m]
    seq = q_ref.shape[1]
    groups, rows, width = part.shape
    here = rows // 2
    per = ROWS // here
    sc = Scatter(part, sum_ref, 2, scratch[:Scatter.COUNT])
    job = side_job(dp, span, side_ref, side_out, scratch[Scatter.COUNT:])

    @pl.when(m == 0)
    def _():
        enter(sc.me, sc.z, sc.core, sc.side, dp)
        job.start()

    mine = pl.ds(pl.multiple_of(m * here, here), here)
    for i in range(seq // ROWS):
        tile = slice(i * ROWS, (i + 1) * ROWS)
        ext = (i + 1) * ROWS
        s = held_scores(q_ref[0, tile], k_ref[0, :ext], i * ROWS, length)
        peak = jnp.max(s, axis=1, keepdims=True)
        raised = jnp.exp(s - peak)
        total = jnp.sum(raised, axis=1, keepdims=True)
        lse_ref[0, tile] = peak + jnp.log(total)
        p = (raised / total).astype(BF)
        att = mm(p, v_ref[0, :ext]).astype(BF)
        att_ref[i * per:(i + 1) * per, 0] = att.reshape(per, here, att.shape[1])
        for j in range(width // 512):
            cols = slice(j * 512, (j + 1) * 512)
            part[i * per:(i + 1) * per, mine, cols] = mm(att, wo_ref[:, cols]).astype(BF).reshape(per, here, 512)

        @pl.when(m == 1)
        def _():
            sc.first(i, [0])

    @pl.when(m == 0)
    def _():
        sc.start([0])

    @pl.when(m == 1)
    def _():
        sc.start([1])
        sc.first(0, [1])
        sc.first(1, [1])
        sc.second(0, [0])
        sc.first(2, [1])
        sc.first(3, [1])
        sc.second(1, [0])
        sc.second(2, [0])
        sc.second(0, [1])
        sc.second(3, [0])
        sc.second(1, [1])
        sc.second(2, [1])
        sc.second(3, [1])
        sc.finish()
        job.finish()


def attend(lengths, q, k, v, wo, groups, dp, span, side, cid):
    batches, seq, _ = q.shape
    here = seq // groups
    width = wo.shape[1]
    shape = jax.ShapeDtypeStruct

    def by_seq(w):
        return pl.BlockSpec((1, seq, w), lambda m: (m, 0, 0))

    return pl.pallas_call(
        functools.partial(attend_kernel, dp, span),
        grid=(batches,),
        out_shape=(shape((batches * here, width), F32), shape((groups, batches, here, 128), BF),
                   shape((batches, seq, 1), F32), side_shape(dp, span, side)),
        in_specs=[pl.BlockSpec(memory_space=pltpu.SMEM), by_seq(256), by_seq(256), by_seq(128),
                  pl.BlockSpec(wo.shape, lambda m: (0, 0)), ANY],
        out_specs=[pl.BlockSpec((batches * here, width), lambda m: (0, 0)),
                   pl.BlockSpec((groups, 1, here, 128), lambda m: (0, m, 0, 0)), by_seq(1), ANY],
        scratch_shapes=[pltpu.VMEM((groups, batches * here, width), BF)]
        + Scatter.scratch(batches * here, width, 2, BF) + side_scratch(dp, span),
        compiler_params=pltpu.CompilerParams(
            collective_id=cid, has_side_effects=True, vmem_limit_bytes=60 * 1024 * 1024),
        cost_estimate=COST,
        name="attend",
    )(lengths, q, k, v, wo, side)


def attend_back_kernel(dp, len_ref, own_ref, side_ref, h_ref, q_ref, k_ref, v_ref, lat_ref, att_ref, lse_ref, wo_ref, wq_ref, we_ref,
                       cos_ref, sin_ref, part_ref, gwq_ref, gwo_out, gwe_out, side_out,
                       dout_ref, dk, dv, datt, gwq, gwo_ref, gwe_ref, *scratch):
    m = pl.program_id(0)
    length = len_ref[m]
    seq = q_ref.shape[1]
    groups, _, width = dout_ref.shape
    here = h_ref.shape[2]
    per = ROWS // here
    g = Gather(own_ref, dout_ref, 2, scratch[:Gather.COUNT])
    job = side_job(dp, None, side_ref, side_out, scratch[Gather.COUNT:])

    @pl.when(m == 0)
    def _():
        enter(g.me, g.z, g.core, g.side, dp)
        job.start()
        g.start([0])
        g.start([1])
        g.round(1, [0])
        g.round(2, [0])
        g.round(1, [1])
        g.round(3, [0])
        g.round(2, [1])
        g.round(4, [0])
        g.kept().wait()
        g.landed([0])
        gwo_ref[...] = jnp.zeros_like(gwo_ref)
        gwe_ref[...] = jnp.zeros_like(gwe_ref)
        gwq[...] = jnp.zeros_like(gwq)

    @pl.when(m == 1)
    def _():
        g.round(4, [1])
        g.landed([1])

    mine = pl.ds(pl.multiple_of(m * here, here), here)
    for j in range(4):
        blocks = slice(j * groups // 4, (j + 1) * groups // 4)
        dout = dout_ref[blocks, mine].reshape(seq // 4, width)
        rows = slice(j * seq // 4, (j + 1) * seq // 4)
        datt[rows] = mm_t(dout, wo_ref[...]).astype(BF)
        gwo_ref[...] += mm_lead(att_ref[blocks].reshape(seq // 4, 128), dout)
    @pl.when(m == 0)
    def _():
        g.round(3, [1])

    dk[...] = jnp.zeros_like(dk)
    dv[...] = jnp.zeros_like(dv)
    for i in range(seq // ROWS):
        tile = slice(i * ROWS, (i + 1) * ROWS)
        ext = (i + 1) * ROWS
        q = q_ref[0, tile]
        p = jnp.exp(held_scores(q, k_ref[0, :ext], i * ROWS, length) - lse_ref[0, tile])
        da = datt[tile]
        dp = mm_t(da, v_ref[0, :ext])
        inner = jnp.sum(dp * p, axis=1, keepdims=True)
        ds = (p * (dp - inner)).astype(BF)
        dq = mm(ds, k_ref[0, :ext]) * SCALE
        dk[:ext] += mm_lead(ds, q)
        dv[:ext] += mm_lead(p.astype(BF), da)
        rope = turn(dq[:, 128:192], cos_ref[tile], -sin_ref[tile])
        dq = jnp.concatenate([dq[:, :128].astype(BF), rope.astype(BF), jnp.zeros((ROWS, 64), BF)], axis=1)
        hidden = h_ref[i * per:(i + 1) * per, 0].reshape(ROWS, width)
        for j in range(width // 512):
            cols = slice(j * 512, (j + 1) * 512)
            gwq[:, cols] += mm_lead(dq, hidden[:, cols])
        for j in range(width // 512):
            cols = slice(j * 512, (j + 1) * 512)
            part_ref[i * per:(i + 1) * per, 0, :, cols] = mm_t(dq, wq_ref[cols]).astype(BF).reshape(per, here, 512)
    for i in range(seq // ROWS):
        tile = slice(i * ROWS, (i + 1) * ROWS)
        d_k = dk[tile] * SCALE
        d_exp = jnp.concatenate([d_k[:, :128].astype(BF), dv[tile].astype(BF)], axis=1)
        gwe_ref[...] += mm_lead(lat_ref[0, tile], d_exp)
        d_lat = mm_t(d_exp, we_ref[...]).astype(BF)
        tail = jnp.concatenate([d_lat, d_k[:, 128:].astype(BF)], axis=1)
        pad = part_ref.shape[3] - width - tail.shape[1]
        if pad > 0:
            tail = jnp.concatenate([tail, jnp.zeros((ROWS, pad), BF)], axis=1)
        part_ref[i * per:(i + 1) * per, 0, :, width:] = tail[:, :part_ref.shape[3] - width].reshape(per, here, -1)

    @pl.when(m == pl.num_programs(0) - 1)
    def _():
        for j in range(width // 256):
            cols = slice(j * 256, (j + 1) * 256)
            gwq_ref[cols] = gwq[:, cols].T.astype(BF)
        gwo_out[...] = gwo_ref[...].astype(BF)
        gwe_out[...] = gwe_ref[...].astype(BF)
        g.finish(False)
        job.finish()


def attend_back(dp, lengths, dout, side, h, q, k, v, lat, att, lse, wo, wq, we, cosine, sine, tail, cid):
    groups, batches, here, width = h.shape
    seq = groups * here
    shape = jax.ShapeDtypeStruct

    def by_seq(w):
        return pl.BlockSpec((1, seq, w), lambda m: (m, 0, 0))

    def by_dev(w):
        return pl.BlockSpec((groups, 1, here, w), lambda m: (0, m, 0, 0))

    def whole(v):
        return pl.BlockSpec(v.shape, lambda m: (0, 0))

    return pl.pallas_call(
        functools.partial(attend_back_kernel, dp),
        grid=(batches,),
        out_shape=(shape((groups, batches, here, width + tail), BF), shape(wq.shape, BF),
                   shape(wo.shape, BF), shape(we.shape, BF), side_shape(dp, None, side)),
        in_specs=[pl.BlockSpec(memory_space=pltpu.SMEM), ANY, ANY, by_dev(width), by_seq(256), by_seq(256), by_seq(128),
                  by_seq(512), by_dev(128), by_seq(1), whole(wo), whole(wq), whole(we), whole(cosine), whole(sine)],
        out_specs=[by_dev(width + tail), whole(wq), whole(wo), whole(we), ANY],
        scratch_shapes=[pltpu.VMEM((groups, batches * here, width), BF), pltpu.VMEM((seq, 256), F32), pltpu.VMEM((seq, 128), F32), pltpu.VMEM((seq, 128), BF),
                        pltpu.VMEM((256, width), F32), pltpu.VMEM(wo.shape, F32), pltpu.VMEM(we.shape, F32)]
        + Gather.scratch(2) + side_scratch(dp, None),
        compiler_params=pltpu.CompilerParams(
            collective_id=cid, has_side_effects=True, vmem_limit_bytes=60 * 1024 * 1024),
        cost_estimate=COST,
        name="attend_back",
    )(lengths, dout, side, h, q, k, v, lat, att, lse, wo, wq, we, cosine, sine)


def turn_kernel(v_ref, o_ref):
    for i in range(v_ref.shape[0] // 128):
        rows = slice(i * 128, (i + 1) * 128)
        o_ref[:, rows] = v_ref[rows].astype(F32).T.astype(o_ref.dtype)


def turned(v, block):
    return pl.pallas_call(
        turn_kernel,
        grid=(1,),
        out_shape=jax.ShapeDtypeStruct((128, v.shape[0]), v.dtype),
        in_specs=[pl.BlockSpec((v.shape[0], 128), lambda i: (0, block))],
        out_specs=pl.BlockSpec((128, v.shape[0]), lambda i: (0, 0)),
        compiler_params=pltpu.CompilerParams(vmem_limit_bytes=16 * 1024 * 1024),
        cost_estimate=COST,
        name="turned",
    )(v)


def split_rows(v):
    high = v.astype(BF)
    return [high, (v - high.astype(F32)).astype(BF)]


def own_back_kernel(dp, back_ref, x_ref, mix_ref, logit_ref, gmix_ref, gain_ref, lgain_ref, small_ref, cos_ref, sin_ref,
                    mid_ref, place_ref, grad_ref, out_ref):
    width = x_ref.shape[1]
    rows_w = out_ref.shape[1] // dp
    lanes_w = out_ref.shape[2]
    x = x_ref[...].astype(F32)
    factor = lax.rsqrt(jnp.mean(x * x, axis=1, keepdims=True) + 1e-6)
    unit = x * factor
    hidden = (unit * gain_ref[...]).astype(BF)
    lat = mm(hidden, small_ref[:, :512])
    factor_l = lax.rsqrt(jnp.mean(lat * lat, axis=1, keepdims=True) + 1e-6)
    unit_l = lat * factor_l
    d_lat = back_ref[:, width:width + 512]
    scaled = d_lat * lgain_ref[...]
    d_in = factor_l * (scaled - unit_l * jnp.mean(scaled * unit_l, axis=1, keepdims=True))
    g_lat = jnp.sum(d_lat * unit_l, axis=0, keepdims=True)
    d_rope = turn(back_ref[:, width + 512:width + 576], cos_ref[...], -sin_ref[...])
    tokens = x.shape[0]
    d_raw = jnp.concatenate(
        [d_in.astype(BF), d_rope.astype(BF), jnp.zeros((tokens, lanes_w - 576), BF)], axis=1)
    d_hidden = back_ref[:, :width] + mm_t(d_raw, small_ref[...])
    scaled = d_hidden * gain_ref[...]
    grad_ref[...] = mid_ref[...] + factor * (scaled - unit * jnp.mean(scaled * unit, axis=1, keepdims=True))
    g_gain = jnp.sum(d_hidden * unit, axis=0, keepdims=True)
    spread = [mm(v, place_ref[...]).astype(BF) for v in split_rows(g_lat)]
    extra = split_rows(g_gain) + split_rows(gmix_ref[...]) + spread + [jnp.zeros((10, width), BF)]
    left = jnp.concatenate([hidden, mix_ref[...]] + extra, axis=0)
    logit = jnp.concatenate(
        [jnp.zeros((tokens, 576), BF), logit_ref[...], jnp.zeros((tokens, lanes_w - 592), BF)], axis=1)
    n = lax.broadcasted_iota(jnp.int32, (16, lanes_w), 0)
    at = 592 + (n >> 1)
    hot = jnp.where((lax.broadcasted_iota(jnp.int32, (16, lanes_w), 1) == at) & (n < 6), 1.0, 0.0).astype(BF)
    right = jnp.concatenate([d_raw, logit, hot], axis=0)
    for j in range(width // 256):
        part = mm_lead(left[:, j * 256:(j + 1) * 256], right).astype(BF)
        for i in range(256 // rows_w):
            owner = j * (256 // rows_w) + i
            d, e = owner // NE, owner % NE
            out_ref[e, d * rows_w:(d + 1) * rows_w] = part[i * rows_w:(i + 1) * rows_w]


def one_step(*arrays):
    return [pl.BlockSpec(v.shape, lambda i, n=v.ndim if hasattr(v, "ndim") else len(v.shape): (0,) * n) for v in arrays]


def own_back(dp, back, x, mix, logit, gmix, gain, lgain, small, cosine, sine, mid, rows_l):
    tokens, width = x.shape
    rows_w = width // (dp * NE)
    count = np.arange(width)
    place = (count // rows_w * rows_l + count % rows_w)[None, :] == np.arange(512)[:, None]
    place = place & (count % rows_w < rows_l)[None, :]
    shape = jax.ShapeDtypeStruct
    args = (back, x, mix, logit, gmix, gain, lgain, small, cosine, sine, mid, jnp.asarray(place.astype(np.float32), BF))
    outs = (shape((tokens, width), F32), shape((NE, dp * rows_w, small.shape[1]), BF))
    return pl.pallas_call(
        functools.partial(own_back_kernel, dp),
        grid=(1,),
        out_shape=outs,
        in_specs=one_step(*args),
        out_specs=tuple(one_step(*outs)),
        compiler_params=pltpu.CompilerParams(vmem_limit_bytes=60 * 1024 * 1024),
        cost_estimate=COST,
        name="own_back",
    )(*args)


def own_middle_kernel(sum_ref, mix_ref, mask_ref, router_ref, middle_ref, gain_ref, dy_ref, valid_ref,
                      grad_ref, low_ref, logit_ref, gmix_ref):
    width = mix_ref.shape[1]
    middle = middle_ref[...]
    factor = lax.rsqrt(jnp.mean(middle * middle, axis=1, keepdims=True) + 1e-6)
    unit = middle * factor
    mask = mask_ref[...].astype(F32)
    held = jnp.where(mask > 0.5, mm_t(mix_ref[...], router_ref[...]), -1e30)
    raised = jnp.exp(held - jnp.max(held, axis=1, keepdims=True)) * mask
    soft = raised / jnp.sum(raised, axis=1, keepdims=True)
    d_gates = (sum_ref[:, width:width + 16] + sum_ref[:, width + 16:width + 32]) * valid_ref[...]
    d_logits = (soft * (d_gates - jnp.sum(d_gates * soft, axis=1, keepdims=True))).astype(BF)
    logit_ref[...] = d_logits
    d_mix = sum_ref[:, :width] + mm(d_logits, router_ref[...])
    gmix_ref[...] = jnp.sum(d_mix * unit, axis=0, keepdims=True)
    scaled = d_mix * gain_ref[...]
    grad = dy_ref[...].astype(F32) + factor * (scaled - unit * jnp.mean(scaled * unit, axis=1, keepdims=True))
    grad_ref[...] = grad
    low_ref[...] = grad.astype(BF)


def own_middle(total, mix, mask, router, middle, gain, dy, valid):
    shape = jax.ShapeDtypeStruct
    args = (total, mix, mask, router, middle, gain, dy, valid)
    outs = (shape(middle.shape, F32), shape(middle.shape, BF), shape(mask.shape, BF), shape(gain.shape, F32))
    return pl.pallas_call(
        own_middle_kernel,
        grid=(1,),
        out_shape=outs,
        in_specs=one_step(*args),
        out_specs=tuple(one_step(*outs)),
        compiler_params=pltpu.CompilerParams(vmem_limit_bytes=60 * 1024 * 1024),
        cost_estimate=COST,
        name="own_middle",
    )(*args)


def widen_kernel(plane_ref, gate_ref, up_ref, down_ref, down_far, share_ref, share_far, gate_out, up_out, down_out, sg_out,
                 su_out, sd_out):
    gate_out[...] = gate_ref[...].astype(F32)
    up_out[...] = up_ref[...].astype(F32)
    down = down_ref[0].astype(F32)
    for r in range(down_far.shape[0]):
        down = down + down_far[r].astype(F32)
    down_out[...] = down

    @pl.when(pl.program_id(0) == 0)
    def _():
        n = sg_out.shape[0]
        for i, out in enumerate((sg_out, su_out, sd_out)):
            rows = slice(i * n, (i + 1) * n)
            v = share_ref[0, rows].astype(F32)
            for r in range(share_far.shape[0]):
                v = v + share_far[r, rows].astype(F32)
            out[...] = v


def widen(plane, gate, up, down, down_far, share, share_far):
    steps = 2 if down.shape[1] % 32 == 0 else 1
    shape = jax.ShapeDtypeStruct

    def cut(rows, w):
        return pl.BlockSpec((rows // steps, w), lambda i, p: (i, 0))

    def full(shape_):
        zeros = (0,) * len(shape_)
        return pl.BlockSpec(shape_, lambda i, p: zeros)

    _, rows, w = down.shape
    third = (share.shape[1] // 3, share.shape[2])
    return pl.pallas_call(
        widen_kernel,
        grid_spec=pltpu.PrefetchScalarGridSpec(
            num_scalar_prefetch=1,
            grid=(steps,),
            in_specs=[cut(*gate.shape), cut(*up.shape),
                      pl.BlockSpec((1, rows // steps, w), lambda i, p: (p[0], i, 0)),
                      pl.BlockSpec((down_far.shape[0], rows // steps, w), lambda i, p: (0, i, 0)),
                      pl.BlockSpec((1,) + share.shape[1:], lambda i, p: (p[0], 0, 0)), full(share_far.shape)],
            out_specs=[cut(*gate.shape), cut(*up.shape), cut(rows, w)] + [full(third)] * 3,
        ),
        out_shape=tuple(shape(v, F32) for v in (gate.shape, up.shape, (rows, w))) + (shape(third, F32),) * 3,
        compiler_params=pltpu.CompilerParams(vmem_limit_bytes=56 * 1024 * 1024),
        cost_estimate=COST,
        name="widen",
    )(plane, gate, up, down, down_far, share, share_far)


H = 16
QK_NOPE = 128
ROPE = 64
V_DIM = 128
KV_RANK = 512
GROUPS = 16
EPSILON = 1e-06
ROTARY_BASE = 10000.0


def product(left_side, right_side):
    return jnp.dot(left_side, right_side, preferred_element_type=F32)


def product_lead(left_side, right_side):
    return lax.dot_general(
        left_side, right_side, (((0,), (0,)), ((), ())), preferred_element_type=F32
    )


def product_trail(left_side, right_side):
    return lax.dot_general(
        left_side, right_side, (((1,), (1,)), ((), ())), preferred_element_type=F32
    )


def rotary_tables(count):
    frequency = ROTARY_BASE ** (-np.arange(ROPE // 2, dtype=np.float32) * np.float32(2.0) / np.float32(ROPE))
    angles = np.arange(count, dtype=np.float32)[:, None] * frequency.astype(np.float32)[None, :]
    return np.cos(angles).astype(np.float32), np.sin(angles).astype(np.float32)


def rotate(values, cosine, sine_table):
    first_half, second_half = jnp.split(values, 2, axis=-1)
    return jnp.concatenate(
        [
            first_half * cosine - second_half * sine_table,
            second_half * cosine + first_half * sine_table,
        ],
        axis=-1,
    )


def norm_forward(values, gains):
    factor = lax.rsqrt(jnp.mean(values * values, axis=-1, keepdims=True) + EPSILON)
    normed = values * factor
    return (normed * gains, normed, factor)


def norm_backward(gradient, normed, factor, gains):
    gain_grad = jnp.sum(gradient * normed, axis=0)
    scaled = gradient * gains
    return (
        factor * (scaled - normed * jnp.mean(scaled * normed, axis=-1, keepdims=True)),
        gain_grad,
    )


def selected_experts(routes):
    chosen = routes[:, :, None] == jnp.arange(GROUPS, dtype=routes.dtype)
    return jnp.any(chosen, axis=1)


def masked_softmax(logits, mask):
    held = jnp.where(mask, logits, -1e30)
    peak = jnp.max(held, axis=-1, keepdims=True)
    raised = jnp.where(mask, jnp.exp(held - peak), 0.0)
    return raised / jnp.sum(raised, axis=-1, keepdims=True)


def per_device(
    layer_input,
    out_cotangent,
    lengths,
    routes,
    attn_gain,
    query_weight,
    latent_weight,
    latent_gain,
    expand_weight,
    output_weight,
    mixer_gain,
    router_weight,
    gate_weight,
    up_weight,
    down_weight,
    shared_gate,
    shared_up,
    shared_down,
):
    dp = lax.axis_size("dp")
    me = lax.axis_index("expert")
    plane = lax.axis_index("dp")
    batches, _, here, width = layer_input.shape
    own = batches * here
    total = own * GROUPS
    seq_total = here * GROUPS
    rows_w = query_weight.shape[0]
    rows_l = expand_weight.shape[0]

    x_own = layer_input.reshape(own, width)
    mask_own = selected_experts(routes.reshape(own, -1))
    mask_columns = mask_own.astype(BF).reshape(rows_w, -1)
    small_width = -(-(595 + mask_columns.shape[1]) // 128) * 128
    latent_column = jnp.zeros((rows_w,), BF).at[:rows_l].set(latent_gain)
    small = jnp.concatenate(
        [
            latent_weight,
            router_weight,
            attn_gain[:, None],
            mixer_gain[:, None],
            latent_column[:, None],
            mask_columns,
            jnp.zeros((rows_w, small_width - 595 - mask_columns.shape[1]), BF),
        ],
        axis=1,
    )
    query_parts = query_weight.reshape(rows_w, H, QK_NOPE + ROPE).transpose(1, 0, 2)
    expand_parts = expand_weight.reshape(rows_l, H, QK_NOPE + V_DIM).transpose(1, 0, 2)
    expand_parts = expand_parts.reshape(H, rows_l, 4, ROPE).swapaxes(1, 2).reshape(H, rows_w, ROPE)
    parts = jnp.concatenate([query_parts, expand_parts], axis=2)
    x_all, small, parts_head, output_head = opening(dp, x_own, small, parts, output_weight, 1)
    x_all = x_all.reshape(total, width)
    mask_all = lax.dynamic_index_in_dim(small, plane, 0, False)[..., 595 : 595 + mask_columns.shape[1]]
    mask_all = mask_all.reshape(total, GROUPS)
    small = small.reshape(width, small_width)
    parts_head = parts_head.reshape(width, TILE)
    latent_full = small[:, :576]
    lines = turned(small, 4)
    router_lines = lines[64:80]
    gain_attn = lines[80].astype(F32)
    gain_mixer = lines[81].astype(F32)
    gain_latent = lines[82].reshape(dp * GROUPS, rows_w)[:, :rows_l].reshape(-1).astype(F32)
    expand_head = parts_head[:, QK_NOPE + ROPE :].reshape(dp * GROUPS, 4, rows_l, ROPE)
    expand_head = expand_head.swapaxes(1, 2).reshape(KV_RANK, QK_NOPE + V_DIM)
    output_head = output_head.reshape(V_DIM, width)

    ff = gate_weight.shape[2]
    share_own = jnp.concatenate([shared_gate.T, shared_up.T, shared_down], axis=0)
    share_width = shared_down.shape[0]
    gate_full = lax.all_gather(gate_weight[0], "dp", axis=0, tiled=True)
    up_full = lax.all_gather(up_weight[0], "dp", axis=0, tiled=True)
    share_full = lax.all_gather(share_own, "dp", axis=0)
    seq_lengths = lengths.reshape(batches)
    own_positions = me * here + jnp.arange(here, dtype=jnp.int32)
    valid_own = (own_positions[None, :] < seq_lengths[:, None]).reshape(own).astype(F32)
    cosine, sine_table = rotary_tables(seq_total)

    grad_own = out_cotangent.reshape(own, width) * valid_own[:, None].astype(BF)

    def by_token(table):
        return jnp.asarray(np.broadcast_to(
            table.reshape(GROUPS, 1, here, -1), (GROUPS, batches, here, table.shape[1])).reshape(total, -1))

    hidden_all, query, key, values, latent = project(
        x_all.reshape(GROUPS, own, width), gain_attn[None], gain_latent[None], parts_head, small, expand_head,
        by_token(cosine), by_token(sine_table), batches)
    down_own = down_weight[0]
    cut = down_own.shape[0] * 3 // 160 * 16
    cuts = (0, cut, 2 * cut + cut // 48 * 16, down_own.shape[0])
    spans = [(first, last - first) for first, last in zip(cuts, cuts[1:])]
    attn_out, attended, log_total, down_a = attend(
        seq_lengths, query, key, values, output_head, GROUPS, dp, spans[0], down_own, 2)

    x_wide = x_own.astype(F32)
    middle = x_wide + attn_out
    normed_mix, unit_mix, factor_mix = norm_forward(middle, gain_mixer)
    hidden_mix = normed_mix.astype(BF)
    mix_all, down_b = gather16(hidden_mix, 3, dp=dp, span=spans[1], side=down_own)
    mix_all = mix_all.reshape(total, width)

    lane = jnp.arange(128)[None, :]
    pick = jnp.concatenate([lane == me, lane == me + GROUPS], axis=1).astype(F32)
    (out_part, rows, hidden, act, slope, result, share_hidden, share_act, share_slope, gates, to_slot, to_token,
     grad_all, down_c) = mixture_forward(
        dp, batches, here, seq_lengths, pick, mix_all, mask_all, gate_full, up_full, router_lines, share_full,
        down_a, down_b, spans[2], down_own, grad_own, 4)
    grad_all = grad_all.reshape(total, width)
    mix_part, grad_result, grad_gate_in, grad_up_in, grad_share_in, mixed = mixture_backward(
        pick, grad_all, gate_full, up_full, share_full, down_a, down_b, down_c, act, slope, result,
        share_act, share_slope, gates, to_slot, to_token, out_part.reshape(GROUPS, own, width), 8)
    grad_down = product_lead(hidden, grad_result).astype(BF)
    grad_down = grad_down.reshape(dp, ff // dp, width)
    mix_sum, grad_share, grad_gate, grad_up, far_down = scatter_share(
        mix_part.reshape(GROUPS, own, width + 128), grad_share_in, share_hidden, mix_all, grad_all,
        rows, grad_gate_in, grad_up_in, grad_down, share_full.shape, 5)
    layer_output = valid_own[:, None] * (middle + mixed)

    out_gate = lax.psum_scatter(grad_gate, "dp", scatter_dimension=0, tiled=True)
    out_up = lax.psum_scatter(grad_up, "dp", scatter_dimension=0, tiled=True)

    grad_middle, grad_middle_low, grad_logits, grad_gain_mixer = own_middle(
        mix_sum, hidden_mix, mask_own.astype(BF), router_lines, middle, gain_mixer[None], grad_own, valid_own[:, None])

    back_part, grad_query_w, grad_output, grad_expand, share_far = attend_back(
        dp, seq_lengths, grad_middle_low, grad_share, hidden_all.reshape(GROUPS, batches, here, width), query, key,
        values, latent, attended, log_total, output_head, parts_head, expand_head, jnp.asarray(cosine),
        jnp.asarray(sine_table), 640, 6)
    grad_expand = grad_expand.reshape(dp * GROUPS, rows_l, 4, ROPE).swapaxes(1, 2).reshape(width, ROPE)
    parts_grad = grad_query_w + jnp.pad(grad_expand, ((0, 0), (QK_NOPE + ROPE, 0)))
    parts_grad = parts_grad.reshape(dp, GROUPS, rows_w, TILE)
    rows_grad = grad_output.reshape(dp, rows_w, width)
    back_sum, parts_far, rows_far = returning(
        dp, back_part.reshape(GROUPS, own, back_part.shape[3]), parts_grad, rows_grad, 7)
    parts_sum = lax.dynamic_index_in_dim(parts_grad, plane, 0, False).astype(F32)
    parts_sum = (parts_sum + jnp.sum(parts_far.astype(F32), axis=0)).astype(BF)
    rows_sum = (rows_grad.astype(F32) + jnp.sum(rows_far.astype(F32), axis=0)).astype(BF)

    def own_table(table):
        own_rows = lax.dynamic_slice_in_dim(jnp.asarray(table), me * here, here)
        return jnp.broadcast_to(own_rows[None], (batches, here, ROPE // 2)).reshape(own, ROPE // 2)

    grad_input, small_grad = own_back(
        dp, back_sum, x_own, hidden_mix, grad_logits, grad_gain_mixer, gain_attn[None], gain_latent[None], small,
        own_table(cosine), own_table(sine_table), grad_middle, rows_l)
    small_sum, out_query, out_expand, out_output = closing(dp, small_grad, parts_sum, rows_sum, rows_l, 9)

    out_gate, out_up, out_down, out_sgate, out_sup, out_sdown = widen(
        plane.reshape(1).astype(jnp.int32), out_gate, out_up, grad_down, far_down, grad_share, share_far)

    def as_input(v):
        return v.reshape(batches, 1, here, width)

    return (
        as_input(layer_output),
        as_input(grad_input),
        small_sum[:, 592],
        out_query,
        small_sum[:, :576],
        small_sum[:rows_l, 594],
        out_expand,
        out_output,
        small_sum[:, 593],
        small_sum[:, 576:592],
        out_gate[None],
        out_up[None],
        out_down[None],
        out_sgate.T,
        out_sup.T,
        out_sdown,
    )


def solution(mesh):
    split = P(("dp", "expert"), None)
    line = P(("dp", "expert"))
    tokens = P(None, "dp", "expert", None)
    expert = P("expert", "dp", None)
    return jax.shard_map(
        per_device,
        mesh=mesh,
        in_specs=(
            tokens, tokens, P(None, "dp"), tokens, line, split, split, line, split, split, line, split,
            expert, expert, expert, P("dp", "expert"), P("dp", "expert"), P("expert", "dp"),
        ),
        out_specs=(
            tokens, tokens, line, split, split, line, split, split, line, split,
            expert, expert, expert, P("dp", "expert"), P("dp", "expert"), P("expert", "dp"),
        ),
        check_vma=False,
    )
```

```python
import functools
import jax
import jax.numpy as jnp
import numpy as np
from jax import lax
from jax.experimental import pallas as pl
from jax.experimental.pallas import tpu as pltpu
from jax.sharding import PartitionSpec as P

MESH = pl.DeviceIdType.MESH
NZ = 4
NE = 16


def place():
    me = lax.axis_index("expert")
    z = me // 4
    x = (me // 2) % 2
    c = me % 2
    return me, z, x, c, me + 1 - 2 * c, me + 2 - 4 * x


def enter(me, z, core, side, dp=1):
    barrier = pltpu.get_barrier_semaphore()
    plane = lax.axis_index("dp")
    for r in range(1, dp):
        pl.semaphore_signal(barrier, inc=1, device_id={"dp": (plane + r) % dp}, device_id_type=MESH)
    for other in (core, side):
        pl.semaphore_signal(barrier, inc=1, device_id={"expert": other}, device_id_type=MESH)

    @pl.when(z < NZ - 1)
    def _():
        pl.semaphore_signal(barrier, inc=1, device_id={"expert": me + 4}, device_id_type=MESH)

    @pl.when(z > 0)
    def _():
        pl.semaphore_signal(barrier, inc=1, device_id={"expert": me - 4}, device_id_type=MESH)

    pl.semaphore_wait(barrier, dp + 1 + (z < NZ - 1).astype(jnp.int32) + (z > 0).astype(jnp.int32))


class Spread:
    def __init__(self, dp, src, out, sems):
        self.dp, self.src, self.out = dp, src, out
        self.own, self.send, self.recv = sems
        self.plane = lax.axis_index("dp")

    @staticmethod
    def scratch(dp):
        dma = pltpu.SemaphoreType.DMA
        return [dma, dma((dp,)), dma((dp,))]

    def copy(self, r):
        return pltpu.make_async_remote_copy(
            src_ref=self.src, dst_ref=self.out.at[self.plane], send_sem=self.send.at[r], recv_sem=self.recv.at[r],
            device_id={"dp": (self.plane + r) % self.dp}, device_id_type=MESH)

    def arrival(self, r):
        p = (self.plane - r + self.dp) % self.dp
        return pltpu.make_async_remote_copy(
            src_ref=self.src, dst_ref=self.out.at[p], send_sem=self.send.at[r], recv_sem=self.recv.at[r],
            device_id={"dp": p}, device_id_type=MESH)

    def start(self):
        for r in range(1, self.dp):
            self.copy(r).start()
        self.kept = pltpu.make_async_copy(self.src, self.out.at[self.plane], self.own)
        self.kept.start()

    def finish(self):
        self.kept.wait()
        for r in range(1, self.dp):
            self.arrival(r).wait_recv()
            self.copy(r).wait_send()


class Swap:
    def __init__(self, dp, src, out, sems):
        self.dp, self.src, self.out = dp, src, out
        self.send, self.recv = sems
        self.plane = lax.axis_index("dp")

    @staticmethod
    def scratch(dp):
        dma = pltpu.SemaphoreType.DMA
        return [dma((dp,)), dma((dp,))]

    def copy(self, r):
        to = (self.plane + r) % self.dp
        return pltpu.make_async_remote_copy(
            src_ref=self.src.at[to], dst_ref=self.out.at[r - 1], send_sem=self.send.at[r], recv_sem=self.recv.at[r],
            device_id={"dp": to}, device_id_type=MESH)

    def start(self):
        for r in range(1, self.dp):
            self.copy(r).start()

    def finish(self):
        for r in range(1, self.dp):
            self.copy(r).wait_recv()
            self.copy(r).wait_send()


def side_job(dp, span, src, out, sems):
    if span is None:
        return Swap(dp, src, out, sems)
    return Spread(dp, src.at[pl.ds(span[0], span[1])], out, sems)


def side_shape(dp, span, side):
    if span is None:
        return jax.ShapeDtypeStruct((dp - 1,) + side.shape[1:], side.dtype)
    return jax.ShapeDtypeStruct((dp, span[1], side.shape[1]), side.dtype)


def side_scratch(dp, span):
    return (Swap if span is None else Spread).scratch(dp)


def enter_all(me, plane, dp):
    barrier = pltpu.get_barrier_semaphore()
    for r in range(1, NE):
        pl.semaphore_signal(
            barrier, inc=1, device_id={"expert": (me + r) % NE}, device_id_type=MESH)
    for r in range(1, dp):
        pl.semaphore_signal(
            barrier, inc=1, device_id={"dp": (plane + r) % dp}, device_id_type=MESH)
    pl.semaphore_wait(barrier, NE - 1 + dp - 1)


class Gather:
    def __init__(self, src, out, chunks, sems, view=lambda ref, b: ref.at[b]):
        self.src, self.out, self.chunks, self.view = src, out, chunks, view
        self.rows = src.shape[0] // chunks
        (self.own_sem, self.us, self.ur, self.ds, self.dr, self.bus, self.bur, self.bds, self.bdr,
         self.xs, self.xr, self.cs, self.cr) = sems
        self.me, self.z, self.x, self.c, self.core, self.side = place()

    COUNT = 13

    @staticmethod
    def scratch(chunks):
        dma = pltpu.SemaphoreType.DMA
        return [dma] + [dma((4, chunks))] * 8 + [dma((7, chunks))] * 2 + [dma((14, chunks))] * 2

    def alt(self, k):
        return k >= (self.chunks + 1) // 2

    def order(self, ks=None):
        return range(self.chunks - 1, -1, -1) if ks is None else ks

    def copy(self, block, k, src, send, recv, to):
        src_ref = self.src if src is None else self.view(self.out, src)
        dst_ref = self.view(self.out, block)
        if self.chunks > 1:
            part = pl.ds(k * self.rows, self.rows)
            src_ref, dst_ref = src_ref.at[part], dst_ref.at[part]
        return pltpu.make_async_remote_copy(
            src_ref=src_ref,
            dst_ref=dst_ref,
            send_sem=send, recv_sem=recv,
            device_id={"expert": to}, device_id_type=MESH,
        )

    def up(self, k, s, src=None):
        return self.copy(self.me - 4 * s, k, src, self.us.at[s, k], self.ur.at[s, k], self.me + 4)

    def down(self, k, s, src=None):
        return self.copy(self.me + 4 * s, k, src, self.ds.at[s, k], self.dr.at[s, k], self.me - 4)

    def up_b(self, k, s):
        b = self.side - 4 * s
        return self.copy(b, k, b, self.bus.at[s, k], self.bur.at[s, k], self.me + 4)

    def down_b(self, k, s):
        b = self.side + 4 * s
        return self.copy(b, k, b, self.bds.at[s, k], self.bdr.at[s, k], self.me - 4)

    def across(self, k, slot, block, src=None):
        return self.copy(block, k, src, self.xs.at[slot, k], self.xr.at[slot, k], self.side)

    def over(self, k, slot, block, src=None):
        return self.copy(block, k, src, self.cs.at[slot, k], self.cr.at[slot, k], self.core)

    def arrived(self, b, k, sems, s):
        return self.copy(b, k, b, sems[0].at[s - 1, k], sems[1].at[s - 1, k], self.side)

    def shift(self, base, slot):
        return base - 4 * slot if slot <= 3 else base + 4 * (slot - 3)

    def core_block(self, slot):
        if slot < 7:
            return self.shift(self.core, slot)
        return self.shift(self.core + 2 - 4 * self.x, slot - 7)

    def has(self, slot):
        slot = slot % 7
        if slot == 0:
            return self.z >= 0
        return self.z >= slot if slot <= 3 else self.z + (slot - 3) <= NZ - 1

    def crosses(self, k, slot):
        if slot == 0 or not self.alt(k):
            return self.has(slot)
        return self.z > slot if slot <= 3 else self.z + (slot - 3) < NZ - 1

    def kept(self):
        return pltpu.make_async_copy(self.src, self.view(self.out, self.me), self.own_sem)

    def start(self, ks=None):
        z, me = self.z, self.me
        if ks is None or 0 in ks:
            self.kept().start()
        for k in self.order(ks):
            self.across(k, 0, me).start()

            @pl.when(z < NZ - 1)
            def _():
                self.up(k, 0).start()

            @pl.when(z > 0)
            def _():
                self.down(k, 0).start()

            self.over(k, 0, me).start()

    def line(self, k, s):
        z, me = self.z, self.me

        @pl.when(z >= s)
        def _():
            b = me - 4 * s
            self.arrived(b, k, (self.us, self.ur), s).wait_recv()

            @pl.when(self.crosses(k, s))
            def _():
                self.across(k, s, b, b).start()

            @pl.when(z < NZ - 1)
            def _():
                self.up(k, s, b).start()

            self.over(k, s, b, b).start()

        @pl.when(z + s <= NZ - 1)
        def _():
            b = me + 4 * s
            self.arrived(b, k, (self.ds, self.dr), s).wait_recv()

            @pl.when(self.crosses(k, 3 + s))
            def _():
                self.across(k, 3 + s, b, b).start()

            @pl.when(z > 0)
            def _():
                self.down(k, s, b).start()

            self.over(k, 3 + s, b, b).start()

    def line_b(self, k, s):
        z = self.z

        @pl.when(z == s)
        def _():
            b = self.side - 4 * s
            self.arrived(b, k, (self.bus, self.bur), s).wait_recv()

            @pl.when(z < NZ - 1)
            def _():
                self.up_b(k, s).start()

            self.over(k, 7 + s, b, b).start()

        @pl.when(z + s == NZ - 1)
        def _():
            b = self.side + 4 * s
            self.arrived(b, k, (self.bds, self.bdr), s).wait_recv()

            @pl.when(z > 0)
            def _():
                self.down_b(k, s).start()

            self.over(k, 10 + s, b, b).start()

    def from_side(self, k, slot):
        @pl.when(self.crosses(k, slot))
        def _():
            b = self.shift(self.side, slot)
            self.across(k, slot, b, b).wait_recv()
            if slot == 0 and self.alt(k):
                @pl.when(self.z == 0)
                def _():
                    self.up_b(k, 0).start()

                @pl.when(self.z == NZ - 1)
                def _():
                    self.down_b(k, 0).start()

            self.over(k, 7 + slot, b, b).start()

    def round(self, s, ks=None):
        if s < NZ:
            for k in self.order(ks):
                self.line(k, s)
        for k in self.order(ks):
            for slot in ((0,) if s == 1 else (s - 1, s + 2)):
                self.from_side(k, slot)
        if s > 1:
            for k in self.order(ks):
                if self.alt(k):
                    self.line_b(k, s - 1)

    def landed(self, ks=None):
        for k in self.order(ks):
            for slot in range(14):
                @pl.when(self.has(slot))
                def _():
                    b = self.core_block(slot)
                    self.over(k, slot, b, b).wait_recv()

    def finish(self, landed=True):
        z = self.z
        if landed:
            self.kept().wait()
            self.landed()
        for k in self.order():
            for slot in range(14):
                @pl.when(self.has(slot))
                def _():
                    b = self.core_block(slot)
                    self.over(k, slot, b, b).wait_send()
            for slot in range(7):
                @pl.when(self.crosses(k, slot))
                def _():
                    self.across(k, slot, self.me).wait_send()
            for s in range(NZ - 1):
                @pl.when((z >= s) & (z < NZ - 1))
                def _():
                    self.up(k, s).wait_send()

                @pl.when((z + s <= NZ - 1) & (z > 0))
                def _():
                    self.down(k, s).wait_send()

                if self.alt(k):
                    @pl.when(z == s)
                    def _():
                        self.up_b(k, s).wait_send()

                    @pl.when(z + s == NZ - 1)
                    def _():
                        self.down_b(k, s).wait_send()


def gather_kernel(chunks, dp, span, extra, x_ref, *refs):
    job = None
    ng = Gather.COUNT
    if not extra:
        o_ref, *sems = refs
    else:
        src, o_ref, out, *sems = refs
        job = side_job(dp, span, src, out, sems[ng:])
    g = Gather(x_ref, o_ref, chunks, sems[:ng])
    enter(g.me, g.z, g.core, g.side, 1 if job is None else dp)
    if job is not None:
        job.start()
    g.start()
    for s in range(1, NZ + 1):
        g.round(s)
    g.finish()
    if job is not None:
        job.finish()


COST = pl.CostEstimate(flops=0, bytes_accessed=4_000_000, transcendentals=0)
ANY = pl.BlockSpec(memory_space=pl.ANY)


def gather16(v, cid, chunks=2, dp=1, span=None, side=None):
    rows, width = v.shape
    extra = side is not None
    out = pl.pallas_call(
        functools.partial(gather_kernel, chunks, dp, span, extra),
        out_shape=(jax.ShapeDtypeStruct((NE, rows, width), v.dtype),)
        + ((side_shape(dp, span, side),) if extra else ()),
        in_specs=[ANY] * (2 if extra else 1),
        out_specs=(ANY,) * (2 if extra else 1),
        scratch_shapes=Gather.scratch(chunks) + (side_scratch(dp, span) if extra else []),
        compiler_params=pltpu.CompilerParams(collective_id=cid, has_side_effects=True),
        cost_estimate=COST,
        name="gather16",
    )(*((v, side) if extra else (v,)))
    return out if extra else out[0]


def opening_kernel(dp, chunks, x_ref, small_ref, parts_ref, out_ref,
                   x_all, small_all, parts_head, out_head, small_dp, out_dp, *sems):
    ng = Gather.COUNT
    gx = Gather(x_ref, x_all, chunks, sems[:ng])
    gs = Gather(small_dp, small_all, 1, sems[ng:2 * ng], lambda ref, b: ref.at[:, b])
    loc, ys, yr, ps, pr, os_, or_, pl_sem, ol_sem = sems[2 * ng:]
    me = gx.me
    plane = lax.axis_index("dp")
    enter_all(me, plane, dp)
    pairs = ((small_ref, small_dp), (out_ref, out_dp), (parts_head.at[plane], parts_head))

    def lift(i, r):
        src, dst = pairs[i]
        return pltpu.make_async_remote_copy(
            src_ref=src, dst_ref=dst.at[plane], send_sem=ys.at[i, r], recv_sem=yr.at[i, r],
            device_id={"dp": (plane + r) % dp}, device_id_type=MESH)

    def landed(i, r):
        p = (plane - r + dp) % dp
        dst = pairs[i][1].at[p]
        return pltpu.make_async_remote_copy(
            src_ref=dst, dst_ref=dst, send_sem=ys.at[i, r], recv_sem=yr.at[i, r],
            device_id={"dp": p}, device_id_type=MESH)

    def kept(i):
        src, dst = pairs[i]
        return pltpu.make_async_copy(src, dst.at[plane], loc.at[i])

    def part(r):
        h = (me + r) % NE
        return pltpu.make_async_remote_copy(
            src_ref=parts_ref.at[h], dst_ref=parts_head.at[plane, me],
            send_sem=ps.at[r], recv_sem=pr.at[r],
            device_id={"expert": h}, device_id_type=MESH)

    def part_in(r):
        e = (me - r + NE) % NE
        return pltpu.make_async_remote_copy(
            src_ref=parts_head.at[plane, e], dst_ref=parts_head.at[plane, e],
            send_sem=ps.at[r], recv_sem=pr.at[r],
            device_id={"expert": e}, device_id_type=MESH)

    def part_kept():
        return pltpu.make_async_copy(parts_ref.at[me], parts_head.at[plane, me], pl_sem)

    for i in range(2):
        for r in range(1, dp):
            lift(i, r).start()
        kept(i).start()
    gx.start()
    for r in range(1, NE):
        part(r).start()
    part_kept().start()
    gx.round(1)

    kept(0).wait()
    for r in range(1, dp):
        landed(0, r).wait_recv()
    gs.start()

    for r in range(1, NE):
        part_in(r).wait_recv()
    part_kept().wait()
    for r in range(1, dp):
        lift(2, r).start()
    gx.round(2)

    def row(d):
        b = NE * d + me
        return pltpu.make_async_remote_copy(
            src_ref=out_dp.at[d], dst_ref=out_head.at[b % dp],
            send_sem=os_.at[d], recv_sem=or_.at[b % dp],
            device_id={"expert": b // dp}, device_id_type=MESH)

    def row_kept(d):
        b = NE * d + me
        return pltpu.make_async_copy(out_dp.at[d], out_head.at[b % dp], ol_sem.at[d])

    kept(1).wait()
    for r in range(1, dp):
        landed(1, r).wait_recv()
    for d in range(dp):
        home = (NE * d + me) // dp

        @pl.when(home != me)
        def _():
            row(d).start()

        @pl.when(home == me)
        def _():
            row_kept(d).start()

    gs.round(1)
    gx.round(3)
    gs.round(2)
    gx.round(4)
    gs.round(3)
    gs.round(4)

    def row_in(j):
        return pltpu.make_async_remote_copy(
            src_ref=out_head.at[j], dst_ref=out_head.at[j], send_sem=os_.at[j], recv_sem=or_.at[j],
            device_id={"expert": gx.core}, device_id_type=MESH)

    for r in range(1, NE):
        part(r).wait_send()
    for j in range(dp):
        @pl.when((dp * me + j) % NE != me)
        def _():
            row_in(j).wait_recv()
    for d in range(dp):
        home = (NE * d + me) // dp

        @pl.when(home != me)
        def _():
            row(d).wait_send()

        @pl.when(home == me)
        def _():
            row_kept(d).wait()
    for r in range(1, dp):
        landed(2, r).wait_recv()
    for i in range(3):
        for r in range(1, dp):
            lift(i, r).wait_send()
    gx.finish()
    gs.finish()


def opening(dp, x, small, parts, out, cid, chunks=2):
    dma = pltpu.SemaphoreType.DMA
    rows, ws = small.shape
    bf = x.dtype
    wo = out.shape[1]
    shape = jax.ShapeDtypeStruct
    res = pl.pallas_call(
        functools.partial(opening_kernel, dp, chunks),
        out_shape=(
            shape((NE,) + x.shape, bf), shape((dp, NE, rows, ws), bf), shape((dp, NE) + parts.shape[1:], bf),
            shape((dp, rows, wo), bf),
            shape((dp, rows, ws), bf), shape((dp, rows, wo), bf),
        ),
        in_specs=[ANY] * 4,
        out_specs=[ANY] * 6,
        scratch_shapes=Gather.scratch(chunks) + Gather.scratch(1) + [
            dma((2,)), dma((3, dp)), dma((3, dp)), dma((NE,)), dma((NE,)), dma((dp,)), dma((dp,)), dma, dma((dp,))],
        compiler_params=pltpu.CompilerParams(collective_id=cid, has_side_effects=True),
        cost_estimate=COST,
        name="opening",
    )(x, small, parts, out)
    return res[:4]


def order(z, i):
    a, b = (3, 2, 1, 0)[i], (3, 2, 0, 1)[i]
    return jnp.where(z == 0, a, jnp.where(z == 1, b, jnp.where(z == 2, 3 - b, 3 - a)))


class Scatter:
    COUNT = 14

    def __init__(self, p_ref, o_ref, chunks, scratch):
        self.p, self.o, self.chunks = p_ref, o_ref, chunks
        (self.cbuf, self.own, self.xbuf, self.ubuf, self.dbuf, self.ld, self.cs, self.cr, self.xs, self.xr,
         self.us, self.ur, self.ds, self.dr) = scratch
        self.rows = o_ref.shape[0] // chunks
        self.me, self.z, self.x, self.c, self.core, self.side = place()

    @staticmethod
    def scratch(rows, width, chunks, bf):
        dma = pltpu.SemaphoreType.DMA
        return [pltpu.VMEM((n, rows, width), bf) for n in (8, 8, 4, 4, 4)] + [
            dma((8, chunks)), dma((8, chunks)), dma((8, chunks))] + [dma((4, chunks))] * 6

    def rng(self, k):
        return pl.ds(k * self.rows, self.rows)

    def column(self, i, j):
        return 4 * order(self.z, i) + 2 * jnp.where(j == 0, 1 - self.x, self.x)

    def remote(self, src, dst, send, recv, to):
        return pltpu.make_async_remote_copy(
            src_ref=src, dst_ref=dst, send_sem=send, recv_sem=recv,
            device_id={"expert": to}, device_id_type=MESH)

    def over(self, i, j, k):
        n = 2 * i + j
        return self.remote(
            self.p.at[self.column(i, j) + 1 - self.c, self.rng(k)], self.cbuf.at[n, self.rng(k)],
            self.cs.at[n, k], self.cr.at[n, k], self.core)

    def load(self, i, j, k):
        n = 2 * i + j
        return pltpu.make_async_copy(
            self.p.at[self.column(i, j) + self.c, self.rng(k)], self.own.at[n, self.rng(k)], self.ld.at[n, k])

    def which(self, ks):
        return range(self.chunks) if ks is None else ks

    def across(self, i, k):
        return self.remote(self.own.at[2 * i, self.rng(k)], self.xbuf.at[i, self.rng(k)],
                           self.xs.at[i, k], self.xr.at[i, k], self.side)

    def up(self, t, i, k):
        return self.remote(self.own.at[2 * i + 1, self.rng(k)], self.ubuf.at[t, self.rng(k)],
                           self.us.at[t, k], self.ur.at[t, k], self.me + 4)

    def down(self, t, i, k):
        return self.remote(self.own.at[2 * i + 1, self.rng(k)], self.dbuf.at[t, self.rng(k)],
                           self.ds.at[t, k], self.dr.at[t, k], self.me - 4)

    def start(self, ks=None):
        for i in range(NZ):
            for j in range(2):
                for k in self.which(ks):
                    self.load(i, j, k).start()
                    self.over(i, j, k).start()

    def first(self, i, ks=None):
        f32 = jnp.float32
        for k in self.which(ks):
            self.load(i, 0, k).wait()
            self.over(i, 0, k).wait_recv()
            s = self.rng(k)
            self.own[2 * i, s] = (
                self.own[2 * i, s].astype(f32) + self.cbuf[2 * i, s].astype(f32)).astype(self.own.dtype)
            self.across(i, k).start()

    def second(self, i, ks=None):
        f32 = jnp.float32
        z, own, o = self.z, self.own, self.o
        t = order(z, i)
        for k in self.which(ks):
            self.load(i, 1, k).wait()
            s = self.rng(k)
            self.over(i, 1, k).wait_recv()
            self.across(i, k).wait_recv()

            def base():
                return (own[2 * i + 1, s].astype(f32) + self.cbuf[2 * i + 1, s].astype(f32)
                        + self.xbuf[i, s].astype(f32))

            if i < NZ - 1:
                @pl.when(t > z)
                def _():
                    @pl.when(z > 0)
                    def _():
                        self.up(t, i, k).wait_recv()
                        own[2 * i + 1, s] = (base() + self.ubuf[t, s].astype(f32)).astype(own.dtype)

                    @pl.when(z == 0)
                    def _():
                        own[2 * i + 1, s] = base().astype(own.dtype)

                    self.up(t, i, k).start()

                @pl.when(t < z)
                def _():
                    @pl.when(z < NZ - 1)
                    def _():
                        self.down(t, i, k).wait_recv()
                        own[2 * i + 1, s] = (base() + self.dbuf[t, s].astype(f32)).astype(own.dtype)

                    @pl.when(z == NZ - 1)
                    def _():
                        own[2 * i + 1, s] = base().astype(own.dtype)

                    self.down(t, i, k).start()
            else:
                @pl.when(z > 0)
                def _():
                    self.up(t, i, k).wait_recv()

                @pl.when(z < NZ - 1)
                def _():
                    self.down(t, i, k).wait_recv()

                @pl.when((z > 0) & (z < NZ - 1))
                def _():
                    o[s] = (base() + self.ubuf[t, s].astype(f32) + self.dbuf[t, s].astype(f32)).astype(o.dtype)

                @pl.when(z == 0)
                def _():
                    o[s] = (base() + self.dbuf[t, s].astype(f32)).astype(o.dtype)

                @pl.when(z == NZ - 1)
                def _():
                    o[s] = (base() + self.ubuf[t, s].astype(f32)).astype(o.dtype)

    def run(self, between=lambda: None):
        self.first(0)
        for i in range(NZ):
            if i + 1 < NZ:
                self.first(i + 1)
            between()
            self.second(i)
            between()

    def finish(self):
        z = self.z
        for k in range(self.chunks):
            for i in range(NZ):
                self.across(i, k).wait_send()
                for j in range(2):
                    self.over(i, j, k).wait_send()
                if i < NZ - 1:
                    t = order(z, i)

                    @pl.when(t > z)
                    def _():
                        self.up(t, i, k).wait_send()

                    @pl.when(t < z)
                    def _():
                        self.down(t, i, k).wait_send()


def scatter_kernel(chunks, dp, span, extra, p_ref, *refs):
    job = None
    ns = Scatter.COUNT
    if not extra:
        o_ref, *scratch = refs
    else:
        src, o_ref, out, *scratch = refs
        job = side_job(dp, span, src, out, scratch[ns:])
    s = Scatter(p_ref, o_ref, chunks, scratch[:ns])
    enter(s.me, s.z, s.core, s.side, 1 if job is None else dp)
    if job is not None:
        job.start()
    s.start()
    s.run()
    s.finish()
    if job is not None:
        job.finish()


VMEM = pl.BlockSpec(memory_space=pltpu.VMEM)


def scatter16(p, cid, chunks=2, dp=1, span=None, side=None):
    _, rows, width = p.shape
    extra = side is not None
    out = pl.pallas_call(
        functools.partial(scatter_kernel, chunks, dp, span, extra),
        out_shape=(jax.ShapeDtypeStruct((rows, width), jnp.float32),)
        + ((side_shape(dp, span, side),) if extra else ()),
        in_specs=[ANY] * (2 if extra else 1),
        out_specs=(VMEM,) + ((ANY,) if extra else ()),
        scratch_shapes=Scatter.scratch(rows, width, chunks, p.dtype) + (side_scratch(dp, span) if extra else []),
        compiler_params=pltpu.CompilerParams(
            collective_id=cid, has_side_effects=True, vmem_limit_bytes=60 * 1024 * 1024),
        cost_estimate=COST,
        name="scatter16",
    )(*((p, side) if extra else (p,)))
    return out if extra else out[0]


def return_kernel(dp, chunks, p_ref, parts_ref, rows_ref, o_ref, parts_far, rows_far, *scratch):
    ns = Scatter.COUNT
    s = Scatter(p_ref, o_ref, chunks, scratch[:ns])
    swap = Swap(dp, parts_ref, parts_far, scratch[ns:ns + 2])
    rs, rr = scratch[ns + 2:]
    plane = lax.axis_index("dp")
    keeper = s.me * dp // NE
    enter(s.me, s.z, s.core, s.side, dp)

    def row(r):
        return pltpu.make_async_remote_copy(
            src_ref=rows_ref, dst_ref=rows_far.at[r - 1], send_sem=rs.at[r], recv_sem=rr.at[r],
            device_id={"dp": (plane + r) % dp}, device_id_type=MESH)

    s.start()
    swap.start()
    for r in range(1, dp):
        @pl.when((plane + r) % dp == keeper)
        def _():
            row(r).start()
    s.run()
    s.finish()
    swap.finish()
    for r in range(1, dp):
        @pl.when((plane + r) % dp == keeper)
        def _():
            row(r).wait_send()

        @pl.when(plane == keeper)
        def _():
            row(r).wait_recv()


def returning(dp, p, parts, rows, cid, chunks=2):
    dma = pltpu.SemaphoreType.DMA
    _, n, width = p.shape
    shape = jax.ShapeDtypeStruct
    return pl.pallas_call(
        functools.partial(return_kernel, dp, chunks),
        out_shape=(
            shape((n, width), jnp.float32), shape((dp - 1,) + parts.shape[1:], parts.dtype),
            shape((dp - 1,) + rows.shape, rows.dtype)),
        in_specs=[ANY] * 3,
        out_specs=[VMEM, ANY, ANY],
        scratch_shapes=Scatter.scratch(n, width, chunks, p.dtype) + [dma((dp,))] * 4,
        compiler_params=pltpu.CompilerParams(
            collective_id=cid, has_side_effects=True, vmem_limit_bytes=60 * 1024 * 1024),
        cost_estimate=COST,
        name="returning",
    )(p, parts, rows)


def closing_kernel(dp, p_ref, parts_ref, rows_ref, o_ref, far_ref, query_ref, expand_ref, output_ref,
                   parts_in, row_in, *scratch):
    ns = Scatter.COUNT
    s = Scatter(p_ref, o_ref, 1, scratch[:ns])
    ys, yr, ps, pr, kept_sem, rs, rr = scratch[ns:]
    me = s.me
    plane = lax.axis_index("dp")
    rows = o_ref.shape[0] // dp
    enter_all(me, plane, dp)

    def lift(r):
        to = (plane + r) % dp
        return pltpu.make_async_remote_copy(
            src_ref=o_ref.at[pl.ds(pl.multiple_of(to * rows, 16), rows)], dst_ref=far_ref.at[r - 1],
            send_sem=ys.at[r], recv_sem=yr.at[r],
            device_id={"dp": to}, device_id_type=MESH)

    def part(r):
        e = (me + r) % NE
        return pltpu.make_async_remote_copy(
            src_ref=parts_ref.at[e], dst_ref=parts_in.at[me], send_sem=ps.at[r], recv_sem=pr.at[r],
            device_id={"expert": e}, device_id_type=MESH)

    def part_in(r):
        h = (me - r + NE) % NE
        return pltpu.make_async_remote_copy(
            src_ref=parts_in.at[h], dst_ref=parts_in.at[h], send_sem=ps.at[r], recv_sem=pr.at[r],
            device_id={"expert": h}, device_id_type=MESH)

    def part_kept():
        return pltpu.make_async_copy(parts_ref.at[me], parts_in.at[me], kept_sem.at[0])

    keeper = plane == me * dp // NE
    source = (NE * plane + me) // dp

    def row(j):
        return pltpu.make_async_remote_copy(
            src_ref=rows_ref.at[j], dst_ref=row_in, send_sem=rs.at[j], recv_sem=rr,
            device_id={"expert": (dp * me + j) % NE}, device_id_type=MESH)

    def row_kept(j):
        return pltpu.make_async_copy(rows_ref.at[j], row_in, kept_sem.at[1])

    s.start()
    for i in range(NZ):
        s.first(i)
    for r in range(1, NE):
        part(r).start()
    part_kept().start()
    for j in range(dp):
        home = (dp * me + j) % NE

        @pl.when(keeper & (home != me))
        def _():
            row(j).start()

        @pl.when(keeper & (home == me))
        def _():
            row_kept(j).start()
    for i in range(NZ):
        s.second(i)
    for r in range(1, dp):
        lift(r).start()
    for r in range(1, NE):
        part_in(r).wait_recv()
    part_kept().wait()
    rows_l = expand_ref.shape[0]
    f32 = jnp.float32
    for h in range(0, NE, 2):
        pair = [parts_in[h + i].astype(f32) for i in range(2)]
        query_ref[:, h * 192:(h + 2) * 192] = jnp.concatenate([v[:, :192] for v in pair], axis=1)
        for i, v in enumerate(pair):
            expand_ref[:, (h + i) * 256:(h + i + 1) * 256] = jnp.concatenate(
                [v[c * rows_l:(c + 1) * rows_l, 192:] for c in range(4)], axis=1)

    @pl.when(source != me)
    def _():
        row(0).wait_recv()

    for j in range(dp):
        home = (dp * me + j) % NE

        @pl.when(keeper & (home != me))
        def _():
            row(j).wait_send()

        @pl.when(keeper & (home == me))
        def _():
            row_kept(j).wait()
    output_ref[...] = row_in[...].astype(f32)
    for r in range(1, NE):
        part(r).wait_send()
    s.finish()
    for r in range(1, dp):
        lift(r).wait_recv()
        lift(r).wait_send()


def closing(dp, p, parts, rows, rows_l, cid):
    dma = pltpu.SemaphoreType.DMA
    _, n, width = p.shape
    shape = jax.ShapeDtypeStruct
    rows_w = parts.shape[1]
    near, far, query, expand, output = pl.pallas_call(
        functools.partial(closing_kernel, dp),
        out_shape=(
            shape((n, width), p.dtype), shape((dp - 1, n // dp, width), p.dtype),
            shape((rows_w, NE * 192), jnp.float32), shape((rows_l, NE * 256), jnp.float32),
            shape(rows.shape[1:], jnp.float32)),
        in_specs=[ANY] * 3,
        out_specs=[VMEM] * 5,
        scratch_shapes=[pltpu.VMEM(parts.shape, parts.dtype), pltpu.VMEM(rows.shape[1:], rows.dtype)]
        + Scatter.scratch(n, width, 1, p.dtype)
        + [dma((dp,)), dma((dp,)), dma((NE,)), dma((NE,)), dma((2,)), dma((dp,)), dma],
        compiler_params=pltpu.CompilerParams(
            collective_id=cid, has_side_effects=True, vmem_limit_bytes=60 * 1024 * 1024),
        cost_estimate=COST,
        name="closing",
    )(p, parts, rows)
    own = lax.dynamic_slice_in_dim(near, lax.axis_index("dp") * (n // dp), n // dp).astype(jnp.float32)
    return own + jnp.sum(far.astype(jnp.float32), axis=0), query, expand, output
BF = jnp.bfloat16
F32 = jnp.float32


def mm(a, b):
    return jnp.dot(a, b, preferred_element_type=F32)


def mm_t(a, b):
    return lax.dot_general(a, b, (((1,), (1,)), ((), ())), preferred_element_type=F32)


def silu_pair(gate_in):
    sigmoid = 1.0 / (1.0 + jnp.exp(-gate_in))
    return (gate_in * sigmoid, sigmoid * (1.0 + gate_in * (1.0 - sigmoid)))


TILE = 256
WIDE = 512
SHARE = 176


def down_copies(parts, out, sem, which):
    dp = parts[0].shape[0]
    sizes = [part.shape[1] for part in parts]
    rows, first = sum(sizes), sum(sizes[:which])
    return [
        pltpu.make_async_copy(
            parts[which].at[d], out.at[pl.ds(d * rows + first, sizes[which])], sem.at[len(parts) * d + which])
        for d in range(dp)
    ]


def share_copies(share_ref, fan, down, sem):
    dp, rows, w = share_ref.shape
    n = rows // 3
    copies = []
    for d in range(dp):
        cols = pl.ds(d * w, w)
        for i, (dst, first) in enumerate(((fan, 0), (fan, TILE), (down, 0))):
            copies.append(pltpu.make_async_copy(
                share_ref.at[d, pl.ds(i * n, n)], dst.at[pl.ds(first, n), cols], sem.at[3 * d + i]))
    return copies


def share_blank(fan, down):
    pad = jnp.zeros((TILE - SHARE, fan.shape[1]), BF)
    fan[SHARE:TILE] = pad
    fan[TILE + SHARE:] = pad
    down[SHARE:] = pad


def valid_of(len_ref, first_device, tokens, batches, here):
    n = lax.broadcasted_iota(jnp.int32, (tokens, 1), 0)
    if here & (here - 1) or batches & (batches - 1):
        device, batch, place_in = n // (batches * here), (n // here) % batches, n % here
    else:
        bits, more = here.bit_length() - 1, (batches * here).bit_length() - 1
        device, batch, place_in = n >> more, (n >> bits) & (batches - 1), n & (here - 1)
    position = (first_device + device) * here + place_in
    length = jnp.zeros((tokens, 1), jnp.int32)
    for b in range(batches):
        length = jnp.where(batch == b, len_ref[b], length)
    return (position < length).astype(F32)


def slot_tables(here, slots=128):
    n = np.arange(256)
    same = n[:, None] // here == n[None, :] // here
    before = same & (n[None, :] < n[:, None])
    tables = np.stack([before, before.T, np.eye(256, dtype=bool)]).astype(np.float32)
    base = np.broadcast_to((n // here * 32)[:, None], (256, slots)).astype(np.float32)
    return jnp.asarray(tables, BF), jnp.asarray(base), jnp.asarray(base.T)


def one_hots(taken, tables, base_c, base_r, groups, slots):
    lane = lax.broadcasted_iota(jnp.int32, (256, slots), 1).astype(F32)
    row = lax.broadcasted_iota(jnp.int32, (slots, 256), 0).astype(F32)
    to_slot, to_token = [], []
    for g in range(groups):
        t = jnp.broadcast_to(taken[g * 256:(g + 1) * 256], (256, slots))
        low = t.astype(BF)
        place_c = mm(tables[0], low) + base_c[...]
        place_r = mm_lead(low, tables[1]) + base_r[...]
        taken_r = mm_lead(low, tables[2])
        to_token.append(jnp.where((place_c == lane) & (t > 0.5), 1.0, 0.0).astype(BF))
        to_slot.append(jnp.where((place_r == row) & (taken_r > 0.5), 1.0, 0.0).astype(BF))
    return to_slot, to_token


def mm_lead(a, b):
    return lax.dot_general(a, b, (((0,), (0,)), ((), ())), preferred_element_type=F32)


def lanes(j):
    return pl.ds(pl.multiple_of(j * WIDE, WIDE), WIDE)


def over_columns(total, body):
    def step(j, _):
        body(pl.multiple_of(j * WIDE, WIDE), WIDE)
        return 0

    lax.fori_loop(0, total // WIDE, step, 0)
    if total % WIDE:
        body(total // WIDE * WIDE, total % WIDE)


def forward_kernel(chunks, dp, span, batches, here, len_ref, pick_ref, mix_ref, mask_ref, tab_ref, basec_ref, baser_ref, wg_ref, wu_ref, router_ref,
                   share_ref, wda_ref, wdb_ref, down_ref, dy_ref,
                   out_ref, rows_ref, hid_ref, act_ref, slo_ref, eo_ref, sh_ref, sact_ref, sslo_ref, gate_ref,
                   slot_ref, token_ref, dy_all, wdc_ref,
                   wd_ref, fan_ref, sd_ref, hid_buf, sh_buf, gate_buf, token_buf, wd_sem, sh_sem, *sems):
    step = pl.program_id(0)
    tokens, width = mix_ref.shape
    groups, slots = tokens // 256, 128
    half = groups * slots
    ff = hid_ref.shape[1]
    phase = pl.num_programs(0) // 2
    g = Gather(dy_ref, dy_all, chunks, sems[:Gather.COUNT])
    job = side_job(dp, span, down_ref, wdc_ref, sems[Gather.COUNT:])
    parts = (wda_ref, wdb_ref, wdc_ref)

    @pl.when(step == 0)
    def _():
        enter(g.me, g.z, g.core, g.side, dp)
        job.start()
        g.start()
        copies = share_copies(share_ref, fan_ref, sd_ref, sh_sem)
        for copy in copies + down_copies(parts, wd_ref, wd_sem, 0) + down_copies(parts, wd_ref, wd_sem, 1):
            copy.start()
        share_blank(fan_ref, sd_ref)
        fan_ref[SHARE:SHARE + 16] = router_ref[...]
        for copy in copies:
            copy.wait()

    @pl.when(step < phase)
    def _():
        mix = mix_ref[...]
        fanned = mm_t(mix, fan_ref[:TILE, :])
        s_up = mm_t(mix, fan_ref[TILE:, :])
        s_act, s_slope = silu_pair(fanned)
        s_hidden = (s_act * s_up).astype(BF)
        at = pl.ds(pl.multiple_of(step * tokens, tokens), tokens)
        sh_ref[...] = s_hidden
        sh_buf[at] = s_hidden
        sact_ref[...] = s_act.astype(BF)
        sslo_ref[...] = (s_up * s_slope).astype(BF)
        logits = fanned[:, SHARE:SHARE + 16]
        mask = mask_ref[...].astype(F32)
        taken = jnp.sum(mask * pick_ref[:, :16], axis=1, keepdims=True) * valid_of(len_ref, step * (tokens // (batches * here)), tokens, batches, here)
        held = jnp.where(mask > 0.5, logits, -1e30)
        raised = jnp.exp(held - jnp.max(held, axis=1, keepdims=True)) * mask
        gate = jnp.sum(raised * pick_ref[:, :16], axis=1, keepdims=True) / jnp.sum(raised, axis=1, keepdims=True) * taken
        gate_ref[...] = gate
        gate_buf[at] = gate
        to_slot, to_token = one_hots(taken, tab_ref, basec_ref, baser_ref, groups, slots)
        for n in range(groups):
            slot_ref[n * slots:(n + 1) * slots] = to_slot[n]
            token_ref[n * 256:(n + 1) * 256] = to_token[n]
            token_buf[pl.ds(pl.multiple_of(step * tokens + n * 256, 256), 256)] = to_token[n]

        def dispatch(j, _):
            for n in range(groups):
                rows_ref[n * slots:(n + 1) * slots, lanes(j)] = mm(
                    to_slot[n], mix_ref[n * 256:(n + 1) * 256, lanes(j)]).astype(BF)
            return 0

        lax.fori_loop(0, width // WIDE, dispatch, 0)
        rows_at = pl.ds(pl.multiple_of(step * half, half), half)

        def fan_in(start, size):
            cols = pl.ds(start, size)
            gate_in = mm(rows_ref[...], wg_ref[:, cols])
            up_in = mm(rows_ref[...], wu_ref[:, cols])
            act, slope = silu_pair(gate_in)
            hidden = (act * up_in).astype(BF)
            hid_ref[:, cols] = hidden
            hid_buf[rows_at, cols] = hidden
            act_ref[:, cols] = act.astype(BF)
            slo_ref[:, cols] = (up_in * slope).astype(BF)

        over_columns(ff, fan_in)

    @pl.when(step == phase)
    def _():
        job.finish()
        for copy in down_copies(parts, wd_ref, wd_sem, 2):
            copy.start()
        for which in range(3):
            for copy in down_copies(parts, wd_ref, wd_sem, which):
                copy.wait()

    @pl.when(step >= phase)
    def _():
        tile = step - phase
        at = pl.ds(pl.multiple_of(tile * tokens, tokens), tokens)
        rows_at = pl.ds(pl.multiple_of(tile * half, half), half)
        gate = gate_buf[at]
        s_hidden = sh_buf[at]
        to_token = [token_buf[pl.ds(pl.multiple_of(tile * tokens + n * 256, 256), 256)] for n in range(groups)]

        def fan_out(j, _):
            eo = mm(hid_buf[rows_at], wd_ref[:, lanes(j)]).astype(BF)
            eo_ref[:, lanes(j)] = eo
            shared = mm(s_hidden, sd_ref[:, lanes(j)])
            picked = jnp.concatenate(
                [mm(to_token[n], eo[n * slots:(n + 1) * slots]) for n in range(groups)], axis=0)
            out_ref[:, lanes(j)] = (shared + gate * picked).astype(BF)
            return 0

        lax.fori_loop(0, width // WIDE, fan_out, 0)

    for r, s in ((1, 1), (2, 3), (3, 5), (4, 7)):
        @pl.when(step == s)
        def _():
            g.round(r)

    @pl.when(step == 2 * phase - 1)
    def _():
        g.finish()


def backward_kernel(chunks, pick_ref, dy_ref, wg_ref, wu_ref, share_ref, wda_ref, wdb_ref, wdc_ref,
                    act_ref, slo_ref, eo_ref, sact_ref, sslo_ref, gate_ref, slot_ref, token_ref, part_ref,
                    dh_ref, deo_ref, dg_ref, du_ref, ds_ref, sum_ref,
                    wd_ref, fan_ref, sd_ref, wd_sem, sh_sem, *scratch):
    step = pl.program_id(0)
    tokens, width = dy_ref.shape
    groups, slots = tokens // 256, 128
    ff = dg_ref.shape[1]
    sc = Scatter(part_ref, sum_ref, chunks, scratch)

    @pl.when(step == 0)
    def _():
        enter(sc.me, sc.z, sc.core, sc.side)
        copies = share_copies(share_ref, fan_ref, sd_ref, sh_sem)
        for which in range(3):
            copies += down_copies((wda_ref, wdb_ref, wdc_ref), wd_ref, wd_sem, which)
        for copy in copies:
            copy.start()
        sc.start()
        share_blank(fan_ref, sd_ref)
        for copy in copies:
            copy.wait()

    d_sh = mm_t(dy_ref[...], sd_ref[...])
    d_s = jnp.concatenate([(d_sh * sslo_ref[...].astype(F32)).astype(BF),
                           (d_sh * sact_ref[...].astype(F32)).astype(BF)], axis=1)
    ds_ref[...] = d_s
    gate = gate_ref[...]
    to_slot = [slot_ref[n * slots:(n + 1) * slots] for n in range(groups)]
    to_token = [token_ref[n * 256:(n + 1) * 256] for n in range(groups)]

    @pl.when(step == 0)
    def _():
        sc.first(0)
        sc.first(1)

    def dispatch(j, total):
        dy = dy_ref[:, lanes(j)].astype(F32)
        gated = (gate * dy).astype(BF)
        for n in range(groups):
            deo_ref[n * slots:(n + 1) * slots, lanes(j)] = mm(to_slot[n], gated[n * 256:(n + 1) * 256]).astype(BF)
        picked = jnp.concatenate(
            [mm(to_token[n], eo_ref[n * slots:(n + 1) * slots, lanes(j)]) for n in range(groups)], axis=0)
        return total + jnp.sum(dy * picked, axis=1, keepdims=True)

    d_gates = lax.fori_loop(0, width // WIDE, dispatch, jnp.zeros((tokens, 1), F32))

    def back_out(start, size):
        cols = pl.ds(start, size)
        d_eh = mm_t(deo_ref[...], wd_ref[cols, :])
        dg_ref[:, cols] = (d_eh * slo_ref[:, cols].astype(F32)).astype(BF)
        du_ref[:, cols] = (d_eh * act_ref[:, cols].astype(F32)).astype(BF)

    over_columns(ff, back_out)

    @pl.when(step == 0)
    def _():
        sc.first(2)
        sc.first(3)

    def back_in(j, _):
        d_rows = (mm_t(dg_ref[...], wg_ref[lanes(j), :]) + mm_t(du_ref[...], wu_ref[lanes(j), :])).astype(BF)
        shared = mm(d_s, fan_ref[:, lanes(j)])
        taken_rows = jnp.concatenate(
            [mm(to_token[n], d_rows[n * slots:(n + 1) * slots]) for n in range(groups)], axis=0)
        dh_ref[:, lanes(j)] = (shared + taken_rows).astype(BF)
        return 0

    lax.fori_loop(0, width // WIDE, back_in, 0)
    high = d_gates.astype(BF).astype(F32)
    dh_ref[:, width:] = (high * pick_ref[:, :128] + (d_gates - high) * pick_ref[:, 128:]).astype(BF)

    outer = (sc.z == 0) | (sc.z == NZ - 1)
    for i in range(NZ - 1):
        @pl.when((step == i) & outer)
        def _():
            sc.second(i)

        @pl.when((step == min(i + 1, 2)) & jnp.logical_not(outer))
        def _():
            sc.second(i)

    @pl.when(step == NZ - 1)
    def _():
        sc.second(NZ - 1)
        sc.finish()


def whole(v):
    zeros = (0,) * v.ndim
    return pl.BlockSpec(v.shape, lambda i: zeros, pipeline_mode=pl.Buffered(buffer_count=1))


def tiles(rows, w):
    return pl.BlockSpec((rows, w), lambda i: (i, 0))


SMEM = pl.BlockSpec(memory_space=pltpu.SMEM)


def mixture_forward(dp, batches, here, lengths, pick, mix, mask, wg, wu, router, share, wda, wdb, span, down, dy, cid,
                    chunks=2):
    total, width = mix.shape
    step, half = total // 4, total // 8
    ff = wg.shape[1]
    tables = slot_tables(here)
    shape = jax.ShapeDtypeStruct
    rows = total // 2
    dma = pltpu.SemaphoreType.DMA

    def early(n, w):
        return pl.BlockSpec((n, w), lambda i: (jnp.minimum(i, 3), 0))

    def late(n, w):
        return pl.BlockSpec((n, w), lambda i: (jnp.maximum(i - 4, 0), 0))

    return pl.pallas_call(
        functools.partial(forward_kernel, chunks, dp, span, batches, here),
        grid=(8,),
        out_shape=(
            shape((total, width), BF), shape((rows, width), BF), shape((rows, ff), BF), shape((rows, ff), BF),
            shape((rows, ff), BF), shape((rows, width), BF), shape((total, TILE), BF), shape((total, TILE), BF),
            shape((total, TILE), BF), shape((total, 1), F32), shape((rows, 256), BF), shape((total, 128), BF),
            shape((NE,) + dy.shape, BF),
            shape((dp, span[1], width), BF)),
        in_specs=[SMEM, whole(pick), early(step, width), early(step, mask.shape[1])] + [whole(v) for v in tables] + [whole(wg), whole(wu),
                  whole(router), ANY, ANY, ANY, ANY, ANY],
        out_specs=[late(step, width), early(half, width), early(half, ff), early(half, ff), early(half, ff),
                   late(half, width), early(step, TILE), early(step, TILE), early(step, TILE), early(step, 1),
                   early(half, 256), early(step, 128), ANY, ANY],
        scratch_shapes=[
            pltpu.VMEM((ff, width), BF), pltpu.VMEM((2 * TILE, width), BF), pltpu.VMEM((TILE, width), BF),
            pltpu.VMEM((rows, ff), BF), pltpu.VMEM((total, TILE), BF), pltpu.VMEM((total, 1), F32),
            pltpu.VMEM((total, 128), BF), dma((3 * dp,)), dma((3 * dp,))] + Gather.scratch(chunks) + Spread.scratch(dp),
        compiler_params=pltpu.CompilerParams(
            collective_id=cid, has_side_effects=True, vmem_limit_bytes=60 * 1024 * 1024),
        cost_estimate=COST,
        name="mixture_forward",
    )(lengths, pick, mix, mask, *tables, wg, wu, router, share, wda, wdb, down, dy)


def mixture_backward(pick, dy, wg, wu, share, wda, wdb, wdc, act, slo, eo, sact, sslo, gate, slot, token, part, cid, chunks=2):
    total, width = dy.shape
    step, half = total // NZ, total // NZ // 2
    ff = wg.shape[1]
    shape = jax.ShapeDtypeStruct
    rows = total // 2
    dp = wda.shape[0]
    _, own, _ = part.shape
    dma = pltpu.SemaphoreType.DMA
    return pl.pallas_call(
        functools.partial(backward_kernel, chunks),
        grid=(NZ,),
        out_shape=(
            shape((total, width + 128), BF), shape((rows, width), BF), shape((rows, ff), BF), shape((rows, ff), BF),
            shape((total, 2 * TILE), BF), shape((own, width), F32)),
        in_specs=[whole(pick), tiles(step, width), whole(wg), whole(wu), ANY, ANY, ANY, ANY,
                  tiles(half, ff), tiles(half, ff), tiles(half, width), tiles(step, TILE), tiles(step, TILE),
                  tiles(step, 1), tiles(half, 256), tiles(step, 128), ANY],
        out_specs=[tiles(step, width + 128), tiles(half, width), tiles(half, ff), tiles(half, ff),
                   tiles(step, 2 * TILE), pl.BlockSpec((own, width), lambda i: (0, 0))],
        scratch_shapes=[
            pltpu.VMEM((ff, width), BF), pltpu.VMEM((2 * TILE, width), BF), pltpu.VMEM((TILE, width), BF),
            dma((3 * dp,)), dma((3 * dp,))] + Scatter.scratch(own, width, chunks, BF),
        compiler_params=pltpu.CompilerParams(
            collective_id=cid, has_side_effects=True, vmem_limit_bytes=62 * 1024 * 1024),
        cost_estimate=COST,
        name="mixture_backward",
    )(pick, dy, wg, wu, share, wda, wdb, wdc, act, slo, eo, sact, sslo, gate, slot, token, part)


class ShareWork:
    ROWS = 256

    def __init__(self, ds_ref, sh_ref, mix_ref, dy_ref, out_ref, scratch):
        self.sources = (ds_ref, sh_ref, mix_ref, dy_ref)
        self.out = out_ref
        *self.buffers, self.gfan, self.gsd, self.sem = scratch
        self.steps = mix_ref.shape[0] // self.ROWS
        self.done = 0

    @staticmethod
    def scratch(width):
        r = ShareWork.ROWS
        return [pltpu.VMEM((2, r, w), BF) for w in (2 * TILE, TILE, width, width)] + [
            pltpu.VMEM((2 * TILE, width), F32), pltpu.VMEM((TILE, width), F32), pltpu.SemaphoreType.DMA((2, 4))]

    COUNT = 7

    def copies(self, n):
        return [pltpu.make_async_copy(src.at[pl.ds(n * self.ROWS, self.ROWS)], buf.at[n % 2], self.sem.at[n % 2, i])
                for i, (src, buf) in enumerate(zip(self.sources, self.buffers))]

    def start(self):
        for copy in self.copies(0):
            copy.start()
        self.gfan[...] = jnp.zeros_like(self.gfan)
        self.gsd[...] = jnp.zeros_like(self.gsd)

    def step(self):
        n = self.done
        if n == self.steps:
            return
        self.done += 1
        for copy in self.copies(n):
            copy.wait()
        if n + 1 < self.steps:
            for copy in self.copies(n + 1):
                copy.start()
        ds, sh, mix, dy = self.buffers

        def columns(j, _):
            self.gfan[:, lanes(j)] += mm_lead(ds[n % 2], mix[n % 2, :, lanes(j)])
            self.gsd[:, lanes(j)] += mm_lead(sh[n % 2], dy[n % 2, :, lanes(j)])
            return 0

        lax.fori_loop(0, mix.shape[2] // WIDE, columns, 0)

    def finish(self):
        while self.done < self.steps:
            self.step()
        dp, rows, w = self.out.shape
        n = rows // 3
        for d in range(dp):
            cols = slice(d * w, (d + 1) * w)
            self.out[d, :n] = self.gfan[:n, cols].astype(BF)
            self.out[d, n:2 * n] = self.gfan[TILE:TILE + n, cols].astype(BF)
            self.out[d, 2 * n:] = self.gsd[:n, cols].astype(BF)


class WeightWork:
    COUNT = 6
    ROWS = 256

    def __init__(self, lhs, rhs, outs, scratch):
        self.sources, self.outs = (lhs,) + tuple(rhs), outs
        *self.held, self.buf, self.in_sem, self.out_sem = scratch
        self.steps = lhs.shape[1] // self.ROWS

    @staticmethod
    def scratch(lhs, rhs):
        dma = pltpu.SemaphoreType.DMA
        return [pltpu.VMEM(v.shape, BF) for v in (lhs,) + tuple(rhs)] + [
            pltpu.VMEM((2, WeightWork.ROWS, rhs[0].shape[1]), BF), dma((3,)), dma((2,))]

    def loads(self):
        return [pltpu.make_async_copy(v, held, self.in_sem.at[i])
                for i, (v, held) in enumerate(zip(self.sources, self.held))]

    def start(self):
        for copy in self.loads():
            copy.start()

    def ready(self):
        for copy in self.loads():
            copy.wait()

    def store(self, p, n):
        at = pl.ds(pl.multiple_of(n * self.ROWS, self.ROWS), self.ROWS)
        return pltpu.make_async_copy(self.buf.at[p], self.outs[p].at[at], self.out_sem.at[p])

    def step(self, begin, end):
        def body(n, _):
            left = self.held[0][:, pl.ds(pl.multiple_of(n * self.ROWS, self.ROWS), self.ROWS)]
            for p in range(2):
                @pl.when(n > 0)
                def _():
                    self.store(p, n - 1).wait()

                rhs = self.held[1 + p]
                width = rhs.shape[1]
                for at in range(0, width, WIDE):
                    size = min(WIDE, width - at)
                    self.buf[p, :, at:at + size] = mm_lead(left, rhs[:, at:at + size]).astype(BF)
                self.store(p, n).start()
            return 0

        lax.fori_loop(begin, end, body, 0)

    def finish(self):
        for p in range(2):
            self.store(p, self.steps - 1).wait()


def scatter_share_kernel(chunks, dp, p_ref, ds_ref, sh_ref, mix_ref, dy_ref, rows_ref, dg_ref, du_ref, down_ref,
                         o_ref, g_ref, ggate_ref, gup_ref, far_ref, *scratch):
    ns, nw = Scatter.COUNT, ShareWork.COUNT
    s = Scatter(p_ref, o_ref, chunks, scratch[:ns])
    share = ShareWork(ds_ref, sh_ref, mix_ref, dy_ref, g_ref, scratch[ns:ns + nw])
    work = WeightWork(rows_ref, (dg_ref, du_ref), (ggate_ref, gup_ref), scratch[ns + nw:-2])
    swap = Swap(dp, down_ref, far_ref, scratch[-2:])
    enter(s.me, s.z, s.core, s.side, dp)
    swap.start()
    s.start()
    work.start()
    share.start()
    s.first(0)
    s.first(1)
    work.ready()
    third = work.steps // 3
    work.step(0, third)
    s.second(0)
    s.first(2)
    s.first(3)
    work.step(third, 2 * third)
    s.second(1)
    work.step(2 * third, work.steps)
    s.second(2)
    work.finish()
    while share.done < share.steps:
        share.step()
    s.second(3)
    share.finish()
    s.finish()
    swap.finish()


def scatter_share(p, ds, sh, mix, dy, rows, dg, du, down, share_shape, cid, chunks=2):
    _, n, width = p.shape
    shape = jax.ShapeDtypeStruct
    grad = shape((rows.shape[1], dg.shape[1]), BF)
    return pl.pallas_call(
        functools.partial(scatter_share_kernel, chunks, down.shape[0]),
        out_shape=(shape((n, width), F32), shape(share_shape, BF), grad, grad,
                   shape((down.shape[0] - 1,) + down.shape[1:], BF)),
        in_specs=[ANY] * 9,
        out_specs=(VMEM, VMEM, ANY, ANY, ANY),
        scratch_shapes=Scatter.scratch(n, width, chunks, p.dtype) + ShareWork.scratch(mix.shape[1])
        + WeightWork.scratch(rows, (dg, du)) + Swap.scratch(down.shape[0]),
        compiler_params=pltpu.CompilerParams(
            collective_id=cid, has_side_effects=True, vmem_limit_bytes=60 * 1024 * 1024),
        cost_estimate=COST,
        name="scatter_share",
    )(p, ds, sh, mix, dy, rows, dg, du, down)


def turn(v, cosine, sine):
    half = v.shape[1] // 2
    a, b = v[:, :half], v[:, half:]
    return jnp.concatenate([a * cosine - b * sine, b * cosine + a * sine], axis=1)


def project_kernel(x_ref, gain_ref, lgain_ref, wq_ref, wl_ref, we_ref, cos_ref, sin_ref,
                   h_ref, q_ref, k_ref, v_ref, lat_ref):
    blocks = x_ref.shape[0]
    batches, rows, _ = q_ref.shape
    here = rows // blocks
    x = x_ref[...].reshape(blocks * batches * here, x_ref.shape[2]).astype(F32)
    h = x * lax.rsqrt(jnp.mean(x * x, axis=1, keepdims=True) + 1e-6) * gain_ref[...]
    h = h.astype(BF)
    h_ref[...] = h
    raw = mm(h, wq_ref[...])
    raw_lat = mm(h, wl_ref[...])
    cosine, sine = cos_ref[...], sin_ref[...]
    zeros = jnp.zeros((raw.shape[0], 64), BF)
    q = jnp.concatenate([raw[:, :128].astype(BF), turn(raw[:, 128:192], cosine, sine).astype(BF), zeros], axis=1)
    k_rope = turn(raw_lat[:, 512:576], cosine, sine).astype(BF)
    lat = raw_lat[:, :512]
    lat = (lat * lax.rsqrt(jnp.mean(lat * lat, axis=1, keepdims=True) + 1e-6) * lgain_ref[...]).astype(BF)
    expanded = mm(lat, we_ref[...]).astype(BF)
    k = jnp.concatenate([expanded[:, :128], k_rope, zeros], axis=1)
    for e in range(blocks):
        for m in range(batches):
            src = slice((e * batches + m) * here, (e * batches + m + 1) * here)
            dst = slice(e * here, (e + 1) * here)
            q_ref[m, dst] = q[src]
            k_ref[m, dst] = k[src]
            v_ref[m, dst] = expanded[src, 128:]
            lat_ref[m, dst] = lat[src]


def project(x_all, gain, lgain, wq, wl, we, cosine, sine, batches):
    groups, rows, width = x_all.shape
    here = rows // batches
    per = 4
    seq = groups * here
    shape = jax.ShapeDtypeStruct

    def whole(v):
        return pl.BlockSpec(v.shape, lambda i: (0, 0))

    def by_seq(w):
        return pl.BlockSpec((batches, per * here, w), lambda i: (0, i, 0))

    table = pl.BlockSpec((per * rows, 32), lambda i: (i, 0))
    return pl.pallas_call(
        project_kernel,
        grid=(groups // per,),
        out_shape=(shape((groups * rows, width), BF), shape((batches, seq, 256), BF), shape((batches, seq, 256), BF),
                   shape((batches, seq, 128), BF), shape((batches, seq, 512), BF)),
        in_specs=[pl.BlockSpec((per, rows, width), lambda i: (i, 0, 0)), whole(gain), whole(lgain), whole(wq), whole(wl), whole(we),
                  table, table],
        out_specs=[pl.BlockSpec((per * rows, width), lambda i: (i, 0)), by_seq(256), by_seq(256), by_seq(128), by_seq(512)],
        compiler_params=pltpu.CompilerParams(vmem_limit_bytes=48 * 1024 * 1024),
        cost_estimate=pl.CostEstimate(flops=7_000_000_000, bytes_accessed=20_000_000, transcendentals=0),
        name="project",
    )(x_all, gain, lgain, wq, wl, we, cosine, sine)


ROWS = 256
SCALE = 192.0 ** -0.5


def held_scores(q, k, first, length):
    s = mm_t(q, k) * SCALE
    t = lax.broadcasted_iota(jnp.int32, s.shape, 0) + first
    u = lax.broadcasted_iota(jnp.int32, s.shape, 1)
    return jnp.where((u <= t) & (u < length), s, -1e30)


def attend_kernel(dp, span, len_ref, q_ref, k_ref, v_ref, wo_ref, side_ref, sum_ref, att_ref, lse_ref, side_out,
                  part, *scratch):
    m = pl.program_id(0)
    length = len_ref[m]
    seq = q_ref.shape[1]
    groups, rows, width = part.shape
    here = rows // 2
    per = ROWS // here
    sc = Scatter(part, sum_ref, 2, scratch[:Scatter.COUNT])
    job = side_job(dp, span, side_ref, side_out, scratch[Scatter.COUNT:])

    @pl.when(m == 0)
    def _():
        enter(sc.me, sc.z, sc.core, sc.side, dp)
        job.start()

    mine = pl.ds(pl.multiple_of(m * here, here), here)
    for i in range(seq // ROWS):
        tile = slice(i * ROWS, (i + 1) * ROWS)
        ext = (i + 1) * ROWS
        s = held_scores(q_ref[0, tile], k_ref[0, :ext], i * ROWS, length)
        peak = jnp.max(s, axis=1, keepdims=True)
        raised = jnp.exp(s - peak)
        total = jnp.sum(raised, axis=1, keepdims=True)
        lse_ref[0, tile] = peak + jnp.log(total)
        p = (raised / total).astype(BF)
        att = mm(p, v_ref[0, :ext]).astype(BF)
        att_ref[i * per:(i + 1) * per, 0] = att.reshape(per, here, att.shape[1])
        for j in range(width // 512):
            cols = slice(j * 512, (j + 1) * 512)
            part[i * per:(i + 1) * per, mine, cols] = mm(att, wo_ref[:, cols]).astype(BF).reshape(per, here, 512)

        @pl.when(m == 1)
        def _():
            sc.first(i, [0])

    @pl.when(m == 0)
    def _():
        sc.start([0])

    @pl.when(m == 1)
    def _():
        sc.start([1])
        sc.first(0, [1])
        sc.first(1, [1])
        sc.second(0, [0])
        sc.first(2, [1])
        sc.first(3, [1])
        sc.second(1, [0])
        sc.second(2, [0])
        sc.second(0, [1])
        sc.second(3, [0])
        sc.second(1, [1])
        sc.second(2, [1])
        sc.second(3, [1])
        sc.finish()
        job.finish()


def attend(lengths, q, k, v, wo, groups, dp, span, side, cid):
    batches, seq, _ = q.shape
    here = seq // groups
    width = wo.shape[1]
    shape = jax.ShapeDtypeStruct

    def by_seq(w):
        return pl.BlockSpec((1, seq, w), lambda m: (m, 0, 0))

    return pl.pallas_call(
        functools.partial(attend_kernel, dp, span),
        grid=(batches,),
        out_shape=(shape((batches * here, width), F32), shape((groups, batches, here, 128), BF),
                   shape((batches, seq, 1), F32), side_shape(dp, span, side)),
        in_specs=[pl.BlockSpec(memory_space=pltpu.SMEM), by_seq(256), by_seq(256), by_seq(128),
                  pl.BlockSpec(wo.shape, lambda m: (0, 0)), ANY],
        out_specs=[pl.BlockSpec((batches * here, width), lambda m: (0, 0)),
                   pl.BlockSpec((groups, 1, here, 128), lambda m: (0, m, 0, 0)), by_seq(1), ANY],
        scratch_shapes=[pltpu.VMEM((groups, batches * here, width), BF)]
        + Scatter.scratch(batches * here, width, 2, BF) + side_scratch(dp, span),
        compiler_params=pltpu.CompilerParams(
            collective_id=cid, has_side_effects=True, vmem_limit_bytes=60 * 1024 * 1024),
        cost_estimate=COST,
        name="attend",
    )(lengths, q, k, v, wo, side)


def attend_back_kernel(dp, len_ref, own_ref, side_ref, h_ref, q_ref, k_ref, v_ref, lat_ref, att_ref, lse_ref, wo_ref, wq_ref, we_ref,
                       cos_ref, sin_ref, part_ref, gwq_ref, gwo_out, gwe_out, side_out,
                       dout_ref, dk, dv, datt, gwq, gwo_ref, gwe_ref, *scratch):
    m = pl.program_id(0)
    length = len_ref[m]
    seq = q_ref.shape[1]
    groups, _, width = dout_ref.shape
    here = h_ref.shape[2]
    per = ROWS // here
    g = Gather(own_ref, dout_ref, 2, scratch[:Gather.COUNT])
    job = side_job(dp, None, side_ref, side_out, scratch[Gather.COUNT:])

    @pl.when(m == 0)
    def _():
        enter(g.me, g.z, g.core, g.side, dp)
        job.start()
        g.start([0])
        g.start([1])
        g.round(1, [0])
        g.round(2, [0])
        g.round(1, [1])
        g.round(3, [0])
        g.round(2, [1])
        g.round(4, [0])
        g.kept().wait()
        g.landed([0])
        gwo_ref[...] = jnp.zeros_like(gwo_ref)
        gwe_ref[...] = jnp.zeros_like(gwe_ref)
        gwq[...] = jnp.zeros_like(gwq)

    @pl.when(m == 1)
    def _():
        g.round(4, [1])
        g.landed([1])

    mine = pl.ds(pl.multiple_of(m * here, here), here)
    for j in range(4):
        blocks = slice(j * groups // 4, (j + 1) * groups // 4)
        dout = dout_ref[blocks, mine].reshape(seq // 4, width)
        rows = slice(j * seq // 4, (j + 1) * seq // 4)
        datt[rows] = mm_t(dout, wo_ref[...]).astype(BF)
        gwo_ref[...] += mm_lead(att_ref[blocks].reshape(seq // 4, 128), dout)
    @pl.when(m == 0)
    def _():
        g.round(3, [1])

    dk[...] = jnp.zeros_like(dk)
    dv[...] = jnp.zeros_like(dv)
    for i in range(seq // ROWS):
        tile = slice(i * ROWS, (i + 1) * ROWS)
        ext = (i + 1) * ROWS
        q = q_ref[0, tile]
        p = jnp.exp(held_scores(q, k_ref[0, :ext], i * ROWS, length) - lse_ref[0, tile])
        da = datt[tile]
        dp = mm_t(da, v_ref[0, :ext])
        inner = jnp.sum(dp * p, axis=1, keepdims=True)
        ds = (p * (dp - inner)).astype(BF)
        dq = mm(ds, k_ref[0, :ext]) * SCALE
        dk[:ext] += mm_lead(ds, q)
        dv[:ext] += mm_lead(p.astype(BF), da)
        rope = turn(dq[:, 128:192], cos_ref[tile], -sin_ref[tile])
        dq = jnp.concatenate([dq[:, :128].astype(BF), rope.astype(BF), jnp.zeros((ROWS, 64), BF)], axis=1)
        hidden = h_ref[i * per:(i + 1) * per, 0].reshape(ROWS, width)
        for j in range(width // 512):
            cols = slice(j * 512, (j + 1) * 512)
            gwq[:, cols] += mm_lead(dq, hidden[:, cols])
        for j in range(width // 512):
            cols = slice(j * 512, (j + 1) * 512)
            part_ref[i * per:(i + 1) * per, 0, :, cols] = mm_t(dq, wq_ref[cols]).astype(BF).reshape(per, here, 512)
    for i in range(seq // ROWS):
        tile = slice(i * ROWS, (i + 1) * ROWS)
        d_k = dk[tile] * SCALE
        d_exp = jnp.concatenate([d_k[:, :128].astype(BF), dv[tile].astype(BF)], axis=1)
        gwe_ref[...] += mm_lead(lat_ref[0, tile], d_exp)
        d_lat = mm_t(d_exp, we_ref[...]).astype(BF)
        tail = jnp.concatenate([d_lat, d_k[:, 128:].astype(BF)], axis=1)
        pad = part_ref.shape[3] - width - tail.shape[1]
        if pad > 0:
            tail = jnp.concatenate([tail, jnp.zeros((ROWS, pad), BF)], axis=1)
        part_ref[i * per:(i + 1) * per, 0, :, width:] = tail[:, :part_ref.shape[3] - width].reshape(per, here, -1)

    @pl.when(m == pl.num_programs(0) - 1)
    def _():
        for j in range(width // 256):
            cols = slice(j * 256, (j + 1) * 256)
            gwq_ref[cols] = gwq[:, cols].T.astype(BF)
        gwo_out[...] = gwo_ref[...].astype(BF)
        gwe_out[...] = gwe_ref[...].astype(BF)
        g.finish(False)
        job.finish()


def attend_back(dp, lengths, dout, side, h, q, k, v, lat, att, lse, wo, wq, we, cosine, sine, tail, cid):
    groups, batches, here, width = h.shape
    seq = groups * here
    shape = jax.ShapeDtypeStruct

    def by_seq(w):
        return pl.BlockSpec((1, seq, w), lambda m: (m, 0, 0))

    def by_dev(w):
        return pl.BlockSpec((groups, 1, here, w), lambda m: (0, m, 0, 0))

    def whole(v):
        return pl.BlockSpec(v.shape, lambda m: (0, 0))

    return pl.pallas_call(
        functools.partial(attend_back_kernel, dp),
        grid=(batches,),
        out_shape=(shape((groups, batches, here, width + tail), BF), shape(wq.shape, BF),
                   shape(wo.shape, BF), shape(we.shape, BF), side_shape(dp, None, side)),
        in_specs=[pl.BlockSpec(memory_space=pltpu.SMEM), ANY, ANY, by_dev(width), by_seq(256), by_seq(256), by_seq(128),
                  by_seq(512), by_dev(128), by_seq(1), whole(wo), whole(wq), whole(we), whole(cosine), whole(sine)],
        out_specs=[by_dev(width + tail), whole(wq), whole(wo), whole(we), ANY],
        scratch_shapes=[pltpu.VMEM((groups, batches * here, width), BF), pltpu.VMEM((seq, 256), F32), pltpu.VMEM((seq, 128), F32), pltpu.VMEM((seq, 128), BF),
                        pltpu.VMEM((256, width), F32), pltpu.VMEM(wo.shape, F32), pltpu.VMEM(we.shape, F32)]
        + Gather.scratch(2) + side_scratch(dp, None),
        compiler_params=pltpu.CompilerParams(
            collective_id=cid, has_side_effects=True, vmem_limit_bytes=60 * 1024 * 1024),
        cost_estimate=COST,
        name="attend_back",
    )(lengths, dout, side, h, q, k, v, lat, att, lse, wo, wq, we, cosine, sine)


def turn_kernel(v_ref, o_ref):
    for i in range(v_ref.shape[0] // 128):
        rows = slice(i * 128, (i + 1) * 128)
        o_ref[:, rows] = v_ref[rows].astype(F32).T.astype(o_ref.dtype)


def turned(v, block):
    return pl.pallas_call(
        turn_kernel,
        grid=(1,),
        out_shape=jax.ShapeDtypeStruct((128, v.shape[0]), v.dtype),
        in_specs=[pl.BlockSpec((v.shape[0], 128), lambda i: (0, block))],
        out_specs=pl.BlockSpec((128, v.shape[0]), lambda i: (0, 0)),
        compiler_params=pltpu.CompilerParams(vmem_limit_bytes=16 * 1024 * 1024),
        cost_estimate=COST,
        name="turned",
    )(v)


def split_rows(v):
    high = v.astype(BF)
    return [high, (v - high.astype(F32)).astype(BF)]


def own_back_kernel(dp, back_ref, x_ref, mix_ref, logit_ref, gmix_ref, gain_ref, lgain_ref, small_ref, cos_ref, sin_ref,
                    mid_ref, place_ref, grad_ref, out_ref):
    width = x_ref.shape[1]
    rows_w = out_ref.shape[1] // dp
    lanes_w = out_ref.shape[2]
    x = x_ref[...].astype(F32)
    factor = lax.rsqrt(jnp.mean(x * x, axis=1, keepdims=True) + 1e-6)
    unit = x * factor
    hidden = (unit * gain_ref[...]).astype(BF)
    lat = mm(hidden, small_ref[:, :512])
    factor_l = lax.rsqrt(jnp.mean(lat * lat, axis=1, keepdims=True) + 1e-6)
    unit_l = lat * factor_l
    d_lat = back_ref[:, width:width + 512]
    scaled = d_lat * lgain_ref[...]
    d_in = factor_l * (scaled - unit_l * jnp.mean(scaled * unit_l, axis=1, keepdims=True))
    g_lat = jnp.sum(d_lat * unit_l, axis=0, keepdims=True)
    d_rope = turn(back_ref[:, width + 512:width + 576], cos_ref[...], -sin_ref[...])
    tokens = x.shape[0]
    d_raw = jnp.concatenate(
        [d_in.astype(BF), d_rope.astype(BF), jnp.zeros((tokens, lanes_w - 576), BF)], axis=1)
    d_hidden = back_ref[:, :width] + mm_t(d_raw, small_ref[...])
    scaled = d_hidden * gain_ref[...]
    grad_ref[...] = mid_ref[...] + factor * (scaled - unit * jnp.mean(scaled * unit, axis=1, keepdims=True))
    g_gain = jnp.sum(d_hidden * unit, axis=0, keepdims=True)
    spread = [mm(v, place_ref[...]).astype(BF) for v in split_rows(g_lat)]
    extra = split_rows(g_gain) + split_rows(gmix_ref[...]) + spread + [jnp.zeros((10, width), BF)]
    left = jnp.concatenate([hidden, mix_ref[...]] + extra, axis=0)
    logit = jnp.concatenate(
        [jnp.zeros((tokens, 576), BF), logit_ref[...], jnp.zeros((tokens, lanes_w - 592), BF)], axis=1)
    n = lax.broadcasted_iota(jnp.int32, (16, lanes_w), 0)
    at = 592 + (n >> 1)
    hot = jnp.where((lax.broadcasted_iota(jnp.int32, (16, lanes_w), 1) == at) & (n < 6), 1.0, 0.0).astype(BF)
    right = jnp.concatenate([d_raw, logit, hot], axis=0)
    for j in range(width // 256):
        part = mm_lead(left[:, j * 256:(j + 1) * 256], right).astype(BF)
        for i in range(256 // rows_w):
            owner = j * (256 // rows_w) + i
            d, e = owner // NE, owner % NE
            out_ref[e, d * rows_w:(d + 1) * rows_w] = part[i * rows_w:(i + 1) * rows_w]


def one_step(*arrays):
    return [pl.BlockSpec(v.shape, lambda i, n=v.ndim if hasattr(v, "ndim") else len(v.shape): (0,) * n) for v in arrays]


def own_back(dp, back, x, mix, logit, gmix, gain, lgain, small, cosine, sine, mid, rows_l):
    tokens, width = x.shape
    rows_w = width // (dp * NE)
    count = np.arange(width)
    place = (count // rows_w * rows_l + count % rows_w)[None, :] == np.arange(512)[:, None]
    place = place & (count % rows_w < rows_l)[None, :]
    shape = jax.ShapeDtypeStruct
    args = (back, x, mix, logit, gmix, gain, lgain, small, cosine, sine, mid, jnp.asarray(place.astype(np.float32), BF))
    outs = (shape((tokens, width), F32), shape((NE, dp * rows_w, small.shape[1]), BF))
    return pl.pallas_call(
        functools.partial(own_back_kernel, dp),
        grid=(1,),
        out_shape=outs,
        in_specs=one_step(*args),
        out_specs=tuple(one_step(*outs)),
        compiler_params=pltpu.CompilerParams(vmem_limit_bytes=60 * 1024 * 1024),
        cost_estimate=COST,
        name="own_back",
    )(*args)


def own_middle_kernel(sum_ref, mix_ref, mask_ref, router_ref, middle_ref, gain_ref, dy_ref, valid_ref,
                      grad_ref, low_ref, logit_ref, gmix_ref):
    width = mix_ref.shape[1]
    middle = middle_ref[...]
    factor = lax.rsqrt(jnp.mean(middle * middle, axis=1, keepdims=True) + 1e-6)
    unit = middle * factor
    mask = mask_ref[...].astype(F32)
    held = jnp.where(mask > 0.5, mm_t(mix_ref[...], router_ref[...]), -1e30)
    raised = jnp.exp(held - jnp.max(held, axis=1, keepdims=True)) * mask
    soft = raised / jnp.sum(raised, axis=1, keepdims=True)
    d_gates = (sum_ref[:, width:width + 16] + sum_ref[:, width + 16:width + 32]) * valid_ref[...]
    d_logits = (soft * (d_gates - jnp.sum(d_gates * soft, axis=1, keepdims=True))).astype(BF)
    logit_ref[...] = d_logits
    d_mix = sum_ref[:, :width] + mm(d_logits, router_ref[...])
    gmix_ref[...] = jnp.sum(d_mix * unit, axis=0, keepdims=True)
    scaled = d_mix * gain_ref[...]
    grad = dy_ref[...].astype(F32) + factor * (scaled - unit * jnp.mean(scaled * unit, axis=1, keepdims=True))
    grad_ref[...] = grad
    low_ref[...] = grad.astype(BF)


def own_middle(total, mix, mask, router, middle, gain, dy, valid):
    shape = jax.ShapeDtypeStruct
    args = (total, mix, mask, router, middle, gain, dy, valid)
    outs = (shape(middle.shape, F32), shape(middle.shape, BF), shape(mask.shape, BF), shape(gain.shape, F32))
    return pl.pallas_call(
        own_middle_kernel,
        grid=(1,),
        out_shape=outs,
        in_specs=one_step(*args),
        out_specs=tuple(one_step(*outs)),
        compiler_params=pltpu.CompilerParams(vmem_limit_bytes=60 * 1024 * 1024),
        cost_estimate=COST,
        name="own_middle",
    )(*args)


def widen_kernel(plane_ref, gate_ref, up_ref, down_ref, down_far, share_ref, share_far, gate_out, up_out, down_out, sg_out,
                 su_out, sd_out):
    gate_out[...] = gate_ref[...].astype(F32)
    up_out[...] = up_ref[...].astype(F32)
    down = down_ref[0].astype(F32)
    for r in range(down_far.shape[0]):
        down = down + down_far[r].astype(F32)
    down_out[...] = down

    @pl.when(pl.program_id(0) == 0)
    def _():
        n = sg_out.shape[0]
        for i, out in enumerate((sg_out, su_out, sd_out)):
            rows = slice(i * n, (i + 1) * n)
            v = share_ref[0, rows].astype(F32)
            for r in range(share_far.shape[0]):
                v = v + share_far[r, rows].astype(F32)
            out[...] = v


def widen(plane, gate, up, down, down_far, share, share_far):
    steps = 2 if down.shape[1] % 32 == 0 else 1
    shape = jax.ShapeDtypeStruct

    def cut(rows, w):
        return pl.BlockSpec((rows // steps, w), lambda i, p: (i, 0))

    def full(shape_):
        zeros = (0,) * len(shape_)
        return pl.BlockSpec(shape_, lambda i, p: zeros)

    _, rows, w = down.shape
    third = (share.shape[1] // 3, share.shape[2])
    return pl.pallas_call(
        widen_kernel,
        grid_spec=pltpu.PrefetchScalarGridSpec(
            num_scalar_prefetch=1,
            grid=(steps,),
            in_specs=[cut(*gate.shape), cut(*up.shape),
                      pl.BlockSpec((1, rows // steps, w), lambda i, p: (p[0], i, 0)),
                      pl.BlockSpec((down_far.shape[0], rows // steps, w), lambda i, p: (0, i, 0)),
                      pl.BlockSpec((1,) + share.shape[1:], lambda i, p: (p[0], 0, 0)), full(share_far.shape)],
            out_specs=[cut(*gate.shape), cut(*up.shape), cut(rows, w)] + [full(third)] * 3,
        ),
        out_shape=tuple(shape(v, F32) for v in (gate.shape, up.shape, (rows, w))) + (shape(third, F32),) * 3,
        compiler_params=pltpu.CompilerParams(vmem_limit_bytes=56 * 1024 * 1024),
        cost_estimate=COST,
        name="widen",
    )(plane, gate, up, down, down_far, share, share_far)


H = 16
QK_NOPE = 128
ROPE = 64
V_DIM = 128
KV_RANK = 512
GROUPS = 16
EPSILON = 1e-06
ROTARY_BASE = 10000.0


def product(left_side, right_side):
    return jnp.dot(left_side, right_side, preferred_element_type=F32)


def product_lead(left_side, right_side):
    return lax.dot_general(
        left_side, right_side, (((0,), (0,)), ((), ())), preferred_element_type=F32
    )


def product_trail(left_side, right_side):
    return lax.dot_general(
        left_side, right_side, (((1,), (1,)), ((), ())), preferred_element_type=F32
    )


def rotary_tables(count):
    frequency = ROTARY_BASE ** (-np.arange(ROPE // 2, dtype=np.float32) * np.float32(2.0) / np.float32(ROPE))
    angles = np.arange(count, dtype=np.float32)[:, None] * frequency.astype(np.float32)[None, :]
    return np.cos(angles).astype(np.float32), np.sin(angles).astype(np.float32)


def rotate(values, cosine, sine_table):
    first_half, second_half = jnp.split(values, 2, axis=-1)
    return jnp.concatenate(
        [
            first_half * cosine - second_half * sine_table,
            second_half * cosine + first_half * sine_table,
        ],
        axis=-1,
    )


def norm_forward(values, gains):
    factor = lax.rsqrt(jnp.mean(values * values, axis=-1, keepdims=True) + EPSILON)
    normed = values * factor
    return (normed * gains, normed, factor)


def norm_backward(gradient, normed, factor, gains):
    gain_grad = jnp.sum(gradient * normed, axis=0)
    scaled = gradient * gains
    return (
        factor * (scaled - normed * jnp.mean(scaled * normed, axis=-1, keepdims=True)),
        gain_grad,
    )


def selected_experts(routes):
    chosen = routes[:, :, None] == jnp.arange(GROUPS, dtype=routes.dtype)
    return jnp.any(chosen, axis=1)


def masked_softmax(logits, mask):
    held = jnp.where(mask, logits, -1e30)
    peak = jnp.max(held, axis=-1, keepdims=True)
    raised = jnp.where(mask, jnp.exp(held - peak), 0.0)
    return raised / jnp.sum(raised, axis=-1, keepdims=True)


def per_device(
    layer_input,
    out_cotangent,
    lengths,
    routes,
    attn_gain,
    query_weight,
    latent_weight,
    latent_gain,
    expand_weight,
    output_weight,
    mixer_gain,
    router_weight,
    gate_weight,
    up_weight,
    down_weight,
    shared_gate,
    shared_up,
    shared_down,
):
    dp = lax.axis_size("dp")
    me = lax.axis_index("expert")
    plane = lax.axis_index("dp")
    batches, _, here, width = layer_input.shape
    own = batches * here
    total = own * GROUPS
    seq_total = here * GROUPS
    rows_w = query_weight.shape[0]
    rows_l = expand_weight.shape[0]

    x_own = layer_input.reshape(own, width)
    mask_own = selected_experts(routes.reshape(own, -1))
    mask_columns = mask_own.astype(BF).reshape(rows_w, -1)
    small_width = -(-(595 + mask_columns.shape[1]) // 128) * 128
    latent_column = jnp.zeros((rows_w,), BF).at[:rows_l].set(latent_gain)
    small = jnp.concatenate(
        [
            latent_weight,
            router_weight,
            attn_gain[:, None],
            mixer_gain[:, None],
            latent_column[:, None],
            mask_columns,
            jnp.zeros((rows_w, small_width - 595 - mask_columns.shape[1]), BF),
        ],
        axis=1,
    )
    query_parts = query_weight.reshape(rows_w, H, QK_NOPE + ROPE).transpose(1, 0, 2)
    expand_parts = expand_weight.reshape(rows_l, H, QK_NOPE + V_DIM).transpose(1, 0, 2)
    expand_parts = expand_parts.reshape(H, rows_l, 4, ROPE).swapaxes(1, 2).reshape(H, rows_w, ROPE)
    parts = jnp.concatenate([query_parts, expand_parts], axis=2)
    x_all, small, parts_head, output_head = opening(dp, x_own, small, parts, output_weight, 1)
    x_all = x_all.reshape(total, width)
    mask_all = lax.dynamic_index_in_dim(small, plane, 0, False)[..., 595 : 595 + mask_columns.shape[1]]
    mask_all = mask_all.reshape(total, GROUPS)
    small = small.reshape(width, small_width)
    parts_head = parts_head.reshape(width, TILE)
    latent_full = small[:, :576]
    lines = turned(small, 4)
    router_lines = lines[64:80]
    gain_attn = lines[80].astype(F32)
    gain_mixer = lines[81].astype(F32)
    gain_latent = lines[82].reshape(dp * GROUPS, rows_w)[:, :rows_l].reshape(-1).astype(F32)
    expand_head = parts_head[:, QK_NOPE + ROPE :].reshape(dp * GROUPS, 4, rows_l, ROPE)
    expand_head = expand_head.swapaxes(1, 2).reshape(KV_RANK, QK_NOPE + V_DIM)
    output_head = output_head.reshape(V_DIM, width)

    ff = gate_weight.shape[2]
    share_own = jnp.concatenate([shared_gate.T, shared_up.T, shared_down], axis=0)
    share_width = shared_down.shape[0]
    gate_full = lax.all_gather(gate_weight[0], "dp", axis=0, tiled=True)
    up_full = lax.all_gather(up_weight[0], "dp", axis=0, tiled=True)
    share_full = lax.all_gather(share_own, "dp", axis=0)
    seq_lengths = lengths.reshape(batches)
    own_positions = me * here + jnp.arange(here, dtype=jnp.int32)
    valid_own = (own_positions[None, :] < seq_lengths[:, None]).reshape(own).astype(F32)
    cosine, sine_table = rotary_tables(seq_total)

    grad_own = out_cotangent.reshape(own, width) * valid_own[:, None].astype(BF)

    def by_token(table):
        return jnp.asarray(np.broadcast_to(
            table.reshape(GROUPS, 1, here, -1), (GROUPS, batches, here, table.shape[1])).reshape(total, -1))

    hidden_all, query, key, values, latent = project(
        x_all.reshape(GROUPS, own, width), gain_attn[None], gain_latent[None], parts_head, small, expand_head,
        by_token(cosine), by_token(sine_table), batches)
    down_own = down_weight[0]
    cut = down_own.shape[0] * 3 // 160 * 16
    cuts = (0, cut, 2 * cut + cut // 48 * 16, down_own.shape[0])
    spans = [(first, last - first) for first, last in zip(cuts, cuts[1:])]
    attn_out, attended, log_total, down_a = attend(
        seq_lengths, query, key, values, output_head, GROUPS, dp, spans[0], down_own, 2)

    x_wide = x_own.astype(F32)
    middle = x_wide + attn_out
    normed_mix, unit_mix, factor_mix = norm_forward(middle, gain_mixer)
    hidden_mix = normed_mix.astype(BF)
    mix_all, down_b = gather16(hidden_mix, 3, dp=dp, span=spans[1], side=down_own)
    mix_all = mix_all.reshape(total, width)

    lane = jnp.arange(128)[None, :]
    pick = jnp.concatenate([lane == me, lane == me + GROUPS], axis=1).astype(F32)
    (out_part, rows, hidden, act, slope, result, share_hidden, share_act, share_slope, gates, to_slot, to_token,
     grad_all, down_c) = mixture_forward(
        dp, batches, here, seq_lengths, pick, mix_all, mask_all, gate_full, up_full, router_lines, share_full,
        down_a, down_b, spans[2], down_own, grad_own, 4)
    grad_all = grad_all.reshape(total, width)
    mix_part, grad_result, grad_gate_in, grad_up_in, grad_share_in, mixed = mixture_backward(
        pick, grad_all, gate_full, up_full, share_full, down_a, down_b, down_c, act, slope, result,
        share_act, share_slope, gates, to_slot, to_token, out_part.reshape(GROUPS, own, width), 8)
    grad_down = product_lead(hidden, grad_result).astype(BF)
    grad_down = grad_down.reshape(dp, ff // dp, width)
    mix_sum, grad_share, grad_gate, grad_up, far_down = scatter_share(
        mix_part.reshape(GROUPS, own, width + 128), grad_share_in, share_hidden, mix_all, grad_all,
        rows, grad_gate_in, grad_up_in, grad_down, share_full.shape, 5)
    layer_output = valid_own[:, None] * (middle + mixed)

    out_gate = lax.psum_scatter(grad_gate, "dp", scatter_dimension=0, tiled=True)
    out_up = lax.psum_scatter(grad_up, "dp", scatter_dimension=0, tiled=True)

    grad_middle, grad_middle_low, grad_logits, grad_gain_mixer = own_middle(
        mix_sum, hidden_mix, mask_own.astype(BF), router_lines, middle, gain_mixer[None], grad_own, valid_own[:, None])

    back_part, grad_query_w, grad_output, grad_expand, share_far = attend_back(
        dp, seq_lengths, grad_middle_low, grad_share, hidden_all.reshape(GROUPS, batches, here, width), query, key,
        values, latent, attended, log_total, output_head, parts_head, expand_head, jnp.asarray(cosine),
        jnp.asarray(sine_table), 640, 6)
    grad_expand = grad_expand.reshape(dp * GROUPS, rows_l, 4, ROPE).swapaxes(1, 2).reshape(width, ROPE)
    parts_grad = grad_query_w + jnp.pad(grad_expand, ((0, 0), (QK_NOPE + ROPE, 0)))
    parts_grad = parts_grad.reshape(dp, GROUPS, rows_w, TILE)
    rows_grad = grad_output.reshape(dp, rows_w, width)
    back_sum, parts_far, rows_far = returning(
        dp, back_part.reshape(GROUPS, own, back_part.shape[3]), parts_grad, rows_grad, 7)
    parts_sum = lax.dynamic_index_in_dim(parts_grad, plane, 0, False).astype(F32)
    parts_sum = (parts_sum + jnp.sum(parts_far.astype(F32), axis=0)).astype(BF)
    rows_sum = (rows_grad.astype(F32) + jnp.sum(rows_far.astype(F32), axis=0)).astype(BF)

    def own_table(table):
        own_rows = lax.dynamic_slice_in_dim(jnp.asarray(table), me * here, here)
        return jnp.broadcast_to(own_rows[None], (batches, here, ROPE // 2)).reshape(own, ROPE // 2)

    grad_input, small_grad = own_back(
        dp, back_sum, x_own, hidden_mix, grad_logits, grad_gain_mixer, gain_attn[None], gain_latent[None], small,
        own_table(cosine), own_table(sine_table), grad_middle, rows_l)
    small_sum, out_query, out_expand, out_output = closing(dp, small_grad, parts_sum, rows_sum, rows_l, 9)

    out_gate, out_up, out_down, out_sgate, out_sup, out_sdown = widen(
        plane.reshape(1).astype(jnp.int32), out_gate, out_up, grad_down, far_down, grad_share, share_far)

    def as_input(v):
        return v.reshape(batches, 1, here, width)

    return (
        as_input(layer_output),
        as_input(grad_input),
        small_sum[:, 592],
        out_query,
        small_sum[:, :576],
        small_sum[:rows_l, 594],
        out_expand,
        out_output,
        small_sum[:, 593],
        small_sum[:, 576:592],
        out_gate[None],
        out_up[None],
        out_down[None],
        out_sgate.T,
        out_sup.T,
        out_sdown,
    )


def solution(mesh):
    split = P(("dp", "expert"), None)
    line = P(("dp", "expert"))
    tokens = P(None, "dp", "expert", None)
    expert = P("expert", "dp", None)
    return jax.shard_map(
        per_device,
        mesh=mesh,
        in_specs=(
            tokens, tokens, P(None, "dp"), tokens, line, split, split, line, split, split, line, split,
            expert, expert, expert, P("dp", "expert"), P("dp", "expert"), P("expert", "dp"),
        ),
        out_specs=(
            tokens, tokens, line, split, split, line, split, split, line, split,
            expert, expert, expert, P("dp", "expert"), P("dp", "expert"), P("expert", "dp"),
        ),
        check_vma=False,
    )
```
